32 devices in a mesh: groups: 2 (over y), dp: 8 (over z, x), tensor: 2 (over core).
Axes of the slice: x: 2, y: 2, z: 4, core: 2. Of those that a mesh axis runs over, the one named last changes fastest.
Arguments:
- prefix_kv: bfloat16 [128, 256, 512], P(('groups', 'dp'), None, 'tensor'), parts along dimension 0, may hold values from -4.5 to 4.5
- move_ids: int32 [8192], P(('groups', 'dp')), parts along dimension 0, may hold values from 0 to 1023
- move_board: int32 [8192, 1], P(('groups', 'dp')), parts along dimension 0, may hold values from 0 to 63; in each aligned block of 512 rows (0 to 511, 512 to 1023, ...) at most 16 rows name the same one
- move_table: bfloat16 [1024, 4096], replicated, may hold values from -4.5 to 4.5
- norm_gain: bfloat16 [4096], replicated, may hold values from 0.25 to 1.75
- w_query: bfloat16 [4096, 2048], P('dp', 'tensor'), may hold values from -0.0625 to 0.0625
- w_keyval: bfloat16 [4096, 512], P('dp', 'tensor'), may hold values from -0.09375 to 0.09375
- w_score: bfloat16 [2048], P('tensor'), may hold values from -3 to 3
Outputs:
- move_logprob: float32 [8192], P(('groups', 'dp')), parts along dimension 0
The draws below stay inside these ranges and needn't reach their ends.
There are 2 independent parts, one for each index of `groups`. The reference program is written for one: setup_inputs(seed, part) draws one part's arguments, and reference() takes and returns one part's arrays. A program takes and returns all parts, laid end to end along the dimension named above; an argument that names none is the same for every part. Nothing has to cross between parts.
Inputs may be any that keep to these rules, and one draw needn't show every extreme that they name: `move_board`: within the rows of one device, at most 16 rows name one board, a bound that some block reaches; every board is named by some row.
All inputs are finite; a program needn't handle non-finite values.
Results may differ from the reference program's by a relative error of at most 0.003.
Values may be sent and summed in bfloat16 or wider, within the bound.
No kernel may reach another device: no remote copies, remote signals or barrier semaphores. Data moves between devices by JAX's collectives and lax.ppermute only.
A program may use at most 128 MiB of HBM per device.

```python
import math
import jax
import jax.numpy as jnp
import numpy as np
from jax import lax

D = 4096
QH = 16
KVH = 2
HD = 128
PREFIX = 256
MOVES = 1024
ROW_DEV = 512
BOARDS = 64
ROWS = 4096
CAPB = 16


def draw_prefix_kv(key, part):
    key = jax.random.fold_in(key, 11)
    noise_key = jax.random.fold_in(key, 0)
    shape = (BOARDS, PREFIX, KVH, 2, HD)
    values = jnp.clip(jax.random.normal(noise_key, shape, jnp.float32), -4.5, 4.5)
    return values.reshape(BOARDS, PREFIX, 2 * KVH * HD).astype(jnp.bfloat16)


def draw_move_table(key, part):
    key = jax.random.fold_in(key, 12)
    rough_key = jax.random.fold_in(key, 0)
    table = jnp.clip(jax.random.normal(rough_key, (MOVES, D), jnp.float32), -4.5, 4.5)
    return table.astype(jnp.bfloat16)


def draw_w_query(key, part):
    key = jax.random.fold_in(key, 13)
    scale = 1.0 / math.sqrt(D)
    weights = jnp.clip(jax.random.normal(key, (D, QH * HD), jnp.float32), -4.0, 4.0) * scale
    return weights.astype(jnp.bfloat16)


def draw_w_score(key, part):
    key = jax.random.fold_in(key, 14)
    weights = jnp.clip(0.5 * jax.random.normal(key, (QH * HD,), jnp.float32), -3.0, 3.0)
    return weights.astype(jnp.bfloat16)


def touch_ends(result, key, low, top_value):
    place = [jax.random.randint(jax.random.fold_in(key, axis), (), 0, length) for axis, length in enumerate(result.shape)]
    longest = result.shape.index(max(result.shape))
    neighbour = place[:longest] + [(place[longest] + 1) % result.shape[longest]] + place[longest + 1:]
    return result.at[tuple(place)].set(low).at[tuple(neighbour)].set(top_value)


def block_scale(key, dims, cuts, smallest, top_value):
    def one(axis_at, parts):
        heights = jax.random.uniform(jax.random.fold_in(jax.random.fold_in(key, 6), axis_at), (parts,), jnp.float32, smallest / len(cuts), top_value / len(cuts))
        return jnp.repeat(jnp.exp(heights), dims[axis_at] // parts).reshape((-1,) + (1,) * (len(dims) - axis_at - 1))

    level = one(*cuts[0])
    for cut in cuts[1:]:
        level = level * one(*cut)
    return level


def assign_block(rng, own, number, rows, amount, top, bound, slope):
    order = jax.random.permutation(rng, amount)
    packed, usual = portions_of(amount, rows * top, bound, slope, True), portions_of(amount, rows * top, bound, slope, False)
    places = jnp.arange(amount)

    def named(lengths, rotation):
        used = int((lengths > 0).sum())
        fixed = max(1, used // 4)
        moved = fixed + (places - fixed + rotation * (used - fixed)) % max(1, amount - fixed)
        return jnp.zeros((amount,), jnp.int32).at[order[jnp.where(places < fixed, places, moved)]].set(jnp.asarray(lengths, jnp.int32))

    lengths = jnp.where(number % 4 == 0, named(packed, number // 4), named(usual, number - number // 4 - 1))
    mixed = jax.random.permutation(jax.random.fold_in(own, 3), amount)
    giver, receiver = mixed[0:amount // 2 * 2:2], mixed[1:amount // 2 * 2:2]
    margin = jnp.minimum(lengths[giver] - 1, bound - lengths[receiver]) // 2
    margin = jnp.where((giver == order[0]) | (receiver == order[0]) | (lengths[receiver] == 0), 0, jnp.maximum(margin, 0))
    moved = jax.random.randint(jax.random.fold_in(own, 4), (amount // 2,), 0, 1 << 20) % (margin + 1)
    lengths = lengths.at[giver].add(-moved).at[receiver].add(moved)
    items = jnp.searchsorted(jnp.cumsum(lengths), jnp.arange(rows * top), side="right").astype(jnp.int32)
    grid = items.reshape(top, rows).T
    grid = grid[jax.random.permutation(jax.random.fold_in(own, 1), rows)]
    rotation = jax.random.randint(jax.random.fold_in(own, 2), (rows, 1), 0, top)
    return jnp.take_along_axis(grid, (jnp.arange(top)[None, :] + rotation) % top, axis=1)


def portions_of(amount, total, most, lean, full):
    weights = [(1 << 20) // math.isqrt(grade ** lean) + 1 for grade in range(1, amount + 1)]
    largest = most if full else min(most, max(-(-total // amount), total * weights[0] // sum(weights)))
    least = 1 if total - largest >= amount - 1 else 0
    holding, surplus = [largest] + [least] * (amount - 1), total - largest - least * (amount - 1)
    while surplus > 0:
        movable = [i for i in range(1, amount) if holding[i] < largest] or [i for i in range(1, amount) if holding[i] < most]
        whole, budget = sum([weights[i] for i in movable]), surplus
        for i in movable:
            extra = min(most - holding[i], max(1, budget * weights[i] // whole), surplus)
            holding[i] = holding[i] + extra
            surplus = surplus - extra
    return np.array(holding)


def gaussian(stream_key, shape, deviation, most, pieces=(), held_as=jnp.bfloat16):
    gain = block_scale(stream_key, shape, pieces, -0.22, 0.18) if pieces else 1.0
    result = jax.random.normal(stream_key, shape, jnp.float32) * deviation * gain
    return jnp.minimum(jnp.maximum(result, -most), most).astype(held_as)


def setup_inputs(seed: int = 0, part: int = 0) -> dict:
    key_list = jax.random.split(jax.random.key(seed), 9)
    part_keys = jax.random.split(jax.random.fold_in(key_list[8], part), 9)
    prefix_kv = draw_prefix_kv(jax.random.fold_in(jax.random.fold_in(key_list[8], part), 71), part)
    move_ids = touch_ends(jax.random.randint(part_keys[1], (ROWS,), 0, MOVES), jax.random.fold_in(part_keys[1], 1), 0, MOVES - 1).astype(jnp.int32)
    move_board_keys = jax.random.split(jax.random.fold_in(part_keys[2], 1), ROWS // ROW_DEV)
    move_board_turns = jax.random.permutation(jax.random.fold_in(part_keys[2], 3), ROWS // ROW_DEV)
    move_board = jax.vmap(lambda own, number: assign_block(jax.random.fold_in(part_keys[2], 2), own, number, ROW_DEV, BOARDS, 1, CAPB, 1))(move_board_keys, move_board_turns).reshape((ROWS, 1))
    move_table = draw_move_table(jax.random.fold_in(key_list[8], 71), part)
    norm_gain = jnp.clip(1.0 + 0.15 * jax.random.normal(key_list[4], (D,), jnp.float32), 0.25, 1.75).astype(jnp.bfloat16)
    w_query = draw_w_query(jax.random.fold_in(key_list[8], 71), part)
    w_keyval = gaussian(key_list[6], (D, 2 * KVH * HD), D ** -0.5, 0.09375, ((0, 8), (1, 2)))
    w_score = draw_w_score(jax.random.fold_in(key_list[8], 71), part)
    return dict(prefix_kv=prefix_kv, move_ids=move_ids, move_board=move_board, move_table=move_table, norm_gain=norm_gain, w_query=w_query, w_keyval=w_keyval, w_score=w_score)


EPS = 1e-06
THETA = 5000000.0

def rotate(block, position):
    full_width = block.shape[-1]
    half_width = full_width // 2
    frequency = THETA ** (-2.0 * jnp.arange(half_width, dtype=jnp.float32) / full_width)
    angles = position * frequency
    cosine = jnp.cos(angles)
    sin_part = jnp.sin(angles)
    first_half = block[..., :half_width]
    second = block[..., half_width:]
    return jnp.concatenate([first_half * cosine - second * sin_part, second * cosine + first_half * sin_part], axis=-1)

def normalize(embedded, norm_gain):
    raw_values = embedded.astype(jnp.float32)
    inverse = lax.rsqrt(lax.optimization_barrier(jnp.mean(raw_values * raw_values, axis=-1, keepdims=True)) + EPS)
    return (raw_values * inverse * norm_gain.astype(jnp.float32)).astype(jnp.bfloat16)

def reference(prefix_kv, move_ids, move_board, move_table, norm_gain, w_query, w_keyval, w_score):
    row_count = move_ids.shape[0]
    board_of = move_board[:, 0]
    normed = normalize(jnp.take(move_table, move_ids, axis=0), norm_gain)
    query_rows = jnp.dot(normed, w_query, preferred_element_type=jnp.float32).reshape(row_count, QH, HD)
    query_rows = rotate(query_rows, PREFIX).astype(jnp.bfloat16)
    keyval = jnp.dot(normed, w_keyval, preferred_element_type=jnp.float32).reshape(row_count, KVH, 2, HD)
    own_key = rotate(keyval[:, :, 0], PREFIX).astype(jnp.bfloat16)
    own_value = keyval[:, :, 1].astype(jnp.bfloat16)
    inv_root = 1.0 / math.sqrt(HD)
    block_rows = math.gcd(row_count, 128)
    block_count = row_count // block_rows

    def attend(block):
        query_b, key_b, value_b, board_b = block
        prefix_split = jnp.take(prefix_kv, board_b, axis=0).reshape(block_rows, PREFIX, KVH, 2, HD).astype(jnp.float32)
        grouped = query_b.astype(jnp.float32).reshape(block_rows, KVH, QH // KVH, HD)
        logit_prefix = jnp.einsum('rkgd,rpkd->rkgp', grouped, prefix_split[:, :, :, 0]) * inv_root
        logit_own = jnp.einsum('rkgd,rkd->rkg', grouped, key_b.astype(jnp.float32)) * inv_root
        peak = jnp.maximum(lax.optimization_barrier(jnp.max(logit_prefix, axis=-1)), logit_own)
        exp_prefix = jnp.exp(logit_prefix - peak[..., None])
        exp_own = jnp.exp(logit_own - peak)
        denom = lax.optimization_barrier(jnp.sum(exp_prefix, axis=-1)) + exp_own
        weight_prefix = (exp_prefix / denom[..., None]).astype(jnp.bfloat16)
        weight_own = (exp_own / denom).astype(jnp.bfloat16)
        context = jnp.einsum('rkgp,rpkd->rkgd', weight_prefix.astype(jnp.float32), prefix_split[:, :, :, 1])
        context = context + weight_own.astype(jnp.float32)[..., None] * value_b.astype(jnp.float32)[:, :, None, :]
        return context.astype(jnp.bfloat16).reshape(block_rows, QH * HD)
    context_all = lax.map(attend, (query_rows.reshape(block_count, block_rows, QH, HD), own_key.reshape(block_count, block_rows, KVH, HD), own_value.reshape(block_count, block_rows, KVH, HD), board_of.reshape(block_count, block_rows)))
    context_all = context_all.reshape(row_count, QH * HD)
    scores_all = jnp.dot(context_all, w_score, preferred_element_type=jnp.float32)
    member = board_of[None, :] == jnp.arange(BOARDS, dtype=jnp.int32)[:, None]
    peak_board = lax.optimization_barrier(jnp.max(jnp.where(member, scores_all[None, :], -1e+30), axis=1))
    row_peak = jnp.take(peak_board, board_of)
    shifted = jnp.exp(scores_all - row_peak)
    denom_board = lax.optimization_barrier(jnp.sum(jnp.where(member, shifted[None, :], 0.0), axis=1))
    return scores_all - row_peak - jnp.log(jnp.take(denom_board, board_of))
```

```python
import functools
import math

import jax
import jax.numpy as jnp
import numpy as np
from jax import lax
from jax.experimental import pallas as pl
from jax.experimental.pallas import tpu as pltpu
from jax.sharding import Mesh
from jax.sharding import PartitionSpec as P

HD = 128
HALF = HD // 2
EPS = 1e-06
THETA = 5000000.0
DEAD = -1e30

F32 = jnp.float32
BF16 = jnp.bfloat16

NN = (((1,), (0,)), ((), ()))
NT = (((1,), (1,)), ((), ()))
TN = (((0,), (0,)), ((), ()))


def matmul(a, b, dims=NN):
    return lax.dot_general(a, b, dims, preferred_element_type=F32)


def limits(mib):
    return pltpu.CompilerParams(vmem_limit_bytes=mib * 1024 * 1024)


class Plan:
    def __init__(self, groups, line, pair, heads, capacity):
        self.groups, self.line, self.pair = groups, line, pair
        self.peers = line * pair
        self.slab = groups * pair
        self.heads = heads
        self.mine = heads // self.slab
        self.pairs = HALF // line
        self.q_rows = self.mine * 2 * self.pairs
        self.k_rows = HD // (groups * self.peers)
        self.fold_rows = 2 * self.mine
        used = self.q_rows + self.k_rows + self.fold_rows
        self.rows = -(-used // 16) * 16
        self.capacity = capacity
        self.slots = self.peers * capacity


def pack_weights(plan, at_ref, wq_ref, wkv_ref, ws_ref, out_ref, pick):
    group = at_ref[0]
    rows, half_cols = plan.rows, wq_ref.shape[1]
    r = lax.broadcasted_iota(jnp.int32, (rows, 1), 0)
    part = r // (plan.mine * plan.pairs)
    head = (r // plan.pairs) % plan.mine
    entry = r % plan.pairs
    is_q = r < plan.q_rows
    k_at = r - plan.q_rows
    is_k = (k_at >= 0) & (k_at < plan.k_rows)
    f_at = k_at - plan.k_rows
    is_f = (f_at >= 0) & (f_at < plan.fold_rows)
    f_head = f_at // 2
    q_lane = lax.broadcasted_iota(jnp.int32, (rows, half_cols), 1)
    k_lane = lax.broadcasted_iota(jnp.int32, (rows, HD), 1)

    ws = ws_ref[...].astype(F32)

    def fill(peer, carry):
        line, pair = peer // plan.pair, peer % plan.pair
        column = (pair * plan.mine + head) * HD + part * HALF + line * plan.pairs + entry
        column = jnp.where(is_q, column, -1)
        at = pl.ds(pl.multiple_of(peer * rows, 16), rows)
        pick[at, :half_cols] = jnp.where(q_lane == column, 1.0, 0.0).astype(BF16)
        k_column = jnp.where(is_k, (group * plan.peers + peer) * plan.k_rows + k_at, -1)
        pick[at, half_cols : half_cols + HD] = jnp.where(k_lane == k_column, 1.0, 0.0).astype(BF16)
        fold = jnp.zeros((rows, HD), F32)
        my_head = jnp.where(is_f, (group * plan.pair + pair) * plan.mine + f_head, -1)
        for h in range(plan.heads):
            fold = jnp.where(my_head == h, ws[h : h + 1], fold)
        pick[at, half_cols + HD :] = fold.astype(BF16)
        return carry

    lax.fori_loop(0, plan.peers, fill, 0, unroll=plan.peers <= 8)
    total = matmul(pick[:, :half_cols], wq_ref[...], NT) + matmul(pick[:, half_cols:], wkv_ref[...], NT)
    rounded = total.astype(BF16)
    rest = (total - rounded.astype(F32)).astype(BF16)
    is_rest = is_f & (f_at % 2 == 1)
    for peer in range(plan.peers):
        at = slice(peer * rows, (peer + 1) * rows)
        out_ref[peer] = jnp.where(is_rest, rest[at].astype(F32), rounded[at].astype(F32)).astype(BF16)


def normalize(table_ref, gain_ref, out_ref):
    raw = table_ref[...].astype(F32)
    inverse = lax.rsqrt(jnp.mean(raw * raw, axis=-1, keepdims=True) + EPS)
    out_ref[...] = (raw * inverse * gain_ref[...].astype(F32)).astype(BF16)


def project(plan, w_ref, normed_ref, turn_ref, q_ref, k_ref, vo_ref):
    if len(w_ref.shape) == 3:
        depth = w_ref.shape[2]
        total = sum(
            matmul(w_ref[s], normed_ref[:, s * depth : (s + 1) * depth], NT) for s in range(w_ref.shape[0])
        )
    else:
        total = matmul(w_ref[...], normed_ref[...], NT)
    half = plan.q_rows // 2
    first, second = total[:half], total[half : 2 * half]
    cosine, sine = turn_ref[:, 0:1], turn_ref[:, 1:2]
    q = jnp.concatenate([first * cosine - second * sine, second * cosine + first * sine], axis=0).astype(BF16)
    for copy in range(q_ref.shape[0]):
        q_ref[copy] = q
    k = total[plan.q_rows : plan.q_rows + plan.k_rows].astype(BF16)
    for copy in range(k_ref.shape[0]):
        k_ref[copy] = k
    base = plan.q_rows + plan.k_rows
    for h in range(plan.mine):
        vo_ref[h : h + 1, :] = total[base + 2 * h : base + 2 * h + 1] + total[base + 2 * h + 1 : base + 2 * h + 2]


def pack_prefix(prefix_ref, ws_ref, out_ref):
    prefix_len = prefix_ref.shape[1]
    heads = ws_ref.shape[0]
    for board in range(prefix_ref.shape[0]):
        out_ref[board, :prefix_len] = prefix_ref[board, :, :HD]
        fold = matmul(ws_ref[...], prefix_ref[board, :, HD:], NT)
        rounded = fold.astype(BF16)
        rest = fold - rounded.astype(F32)
        both = jnp.concatenate([rounded.astype(F32), rest], axis=0).astype(BF16)
        for piece in range(prefix_len // HD):
            at = prefix_len + piece * 2 * heads
            out_ref[board, at : at + 2 * heads] = both[:, piece * HD : (piece + 1) * HD]


def list_moves(plan, at_ref, board_col_ref, board_row_ref, ids_ref, out_ref, slot_ref):
    count = board_col_ref.shape[0]
    same = board_col_ref[...] == board_row_ref[...]
    other = lax.broadcasted_iota(jnp.int32, (count, count), 0)
    own = lax.broadcasted_iota(jnp.int32, (count, count), 1)
    rank = jnp.sum(jnp.where(same & (other < own), 1.0, 0.0), axis=0, keepdims=True)
    slot = rank.astype(jnp.int32) + at_ref[0] * plan.capacity
    slot_ref[...] = slot
    slots_in = lax.broadcasted_iota(jnp.int32, (plan.slots, count), 0) == slot
    boards = plan.line * out_ref.shape[3]
    member = lax.broadcasted_iota(jnp.int32, (boards, count), 0) == board_row_ref[...]
    move = ids_ref[...] + 1
    high, low = (move // 64).astype(F32), (move % 64).astype(F32)
    slots_in = jnp.where(slots_in, 1.0, 0.0).astype(BF16)
    listed = 64.0 * matmul(jnp.where(member, high, 0.0).astype(BF16), slots_in, NT)
    listed = listed + matmul(jnp.where(member, low, 0.0).astype(BF16), slots_in, NT)
    share = boards // plan.line
    for line in range(plan.line):
        for g in range(plan.groups):
            for p in range(plan.pair):
                out_ref[g, line, p] = listed[line * share : (line + 1) * share]


def attend(plan, at_ref, q_ref, order_ref, k_ref, turn_ref, vo_ref, own_ref, *rest):
    peers = rest[: plan.slab - 1]
    moves_ref, out_ref, table, extra, scores = rest[plan.slab - 1 :]
    payloads = (own_ref, *peers)
    here = at_ref[0]
    mine, heads, slots = plan.mine, plan.heads, plan.slots
    moves = q_ref.shape[1]
    boards = own_ref.shape[0]
    prefix_len = own_ref.shape[1] - 2 * heads * (256 // HD)
    query_rows = mine * HD

    table[:query_rows] = matmul(order_ref[...], q_ref[...]).astype(BF16)
    key = k_ref[...].astype(F32)
    first, second = key[:HALF], key[HALF:]
    cosine, sine = turn_ref[:, 0:1], turn_ref[:, 1:2]
    key_first, key_second = first * cosine - second * sine, second * cosine + first * sine
    extra[...] = jnp.zeros_like(extra)
    for h in range(mine):
        q_first = table[h * HD : h * HD + HALF].astype(F32)
        q_second = table[h * HD + HALF : (h + 1) * HD].astype(F32)
        own_logit = jnp.sum(q_first * key_first + q_second * key_second, axis=0, keepdims=True)
        for place, value in ((0, own_logit), (2 * mine, vo_ref[h : h + 1, :])):
            rounded = value.astype(BF16).astype(F32)
            extra[place + h : place + h + 1] = rounded
            extra[place + mine + h : place + mine + h + 1] = value - rounded
    table[query_rows:] = extra[...].astype(BF16)

    scale = math.log2(math.e) / math.sqrt(HD)
    move_at = lax.broadcasted_iota(jnp.int32, (moves, slots), 0) + 1
    lanes = mine * slots
    fold_at = lax.broadcasted_iota(jnp.int32, (2 * heads, lanes), 0)
    fold_head = here * mine + lax.broadcasted_iota(jnp.int32, (2 * heads, lanes), 1) // slots
    fold_mine = (fold_at == fold_head) | (fold_at == fold_head + heads)

    def per_head(x, base):
        pieces = [x[base + h : base + h + 1] + x[base + mine + h : base + mine + h + 1] for h in range(mine)]
        return jnp.concatenate(pieces, axis=1)

    def step(board, carry):
        listed = []
        for j in range(plan.slab):
            owner = here ^ j
            listed.append(moves_ref[owner, pl.ds(board, 1), :])
        chosen = [jnp.where(move_at == row, 1.0, 0.0).astype(BF16) for row in listed]
        taken = matmul(table[...], jnp.concatenate(chosen, axis=1))
        for j in range(plan.slab):
            owner = here ^ j
            x = taken[:, j * slots : (j + 1) * slots]
            q = jnp.concatenate([x[h * HD : (h + 1) * HD].astype(BF16) for h in range(mine)], axis=1)
            logits = matmul(payloads[j][board, :prefix_len], q)
            own_logit = per_head(x, query_rows)
            own_value = per_head(x, query_rows + 2 * mine)
            peak = jnp.maximum(jnp.max(logits, axis=0, keepdims=True), own_logit)
            weight = jnp.exp2((logits - peak) * scale)
            own_weight = jnp.exp2((own_logit - peak) * scale)
            denom = jnp.sum(weight, axis=0, keepdims=True) + own_weight
            fold = jnp.concatenate(
                [
                    payloads[j][board, prefix_len + p * 2 * heads : prefix_len + (p + 1) * 2 * heads]
                    for p in range(prefix_len // HD)
                ],
                axis=1,
            )
            value = matmul(fold, weight.astype(BF16))
            value = jnp.sum(jnp.where(fold_mine, value, 0.0), axis=0, keepdims=True)
            value = (value + own_value * own_weight) / denom
            score = sum(value[:, h * slots : (h + 1) * slots] for h in range(mine))
            scores[owner, pl.ds(board, 1), :] = jnp.where(listed[j] > 0, score, DEAD)
        return carry

    lax.fori_loop(0, boards, step, 0)
    for g in range(plan.groups):
        mine_all = jnp.concatenate([scores[g * plan.pair + p] for p in range(plan.pair)], axis=0)
        for copy in range(out_ref.shape[1]):
            out_ref[g, copy] = mine_all


def finish(plan, parts_ref, board_ref, slot_ref, out_ref):
    line = parts_ref.shape[1]
    columns = []
    for at in range(line):
        total = None
        for g in range(parts_ref.shape[0]):
            for p in range(parts_ref.shape[2]):
                term = parts_ref[g, at, p]
                total = term if total is None else total + term
        columns.append(total)
    scores = jnp.concatenate(columns, axis=0)
    live = scores > 0.5 * DEAD
    peak = jnp.max(scores, axis=1, keepdims=True)
    denom = jnp.sum(jnp.where(live, jnp.exp(scores - peak), 0.0), axis=1, keepdims=True)
    logprob = jnp.where(live, scores - peak - jnp.log(denom), 0.0)
    count = board_ref.shape[1]
    member = lax.broadcasted_iota(jnp.int32, (scores.shape[0], count), 0) == board_ref[...]
    member = jnp.where(member, 1.0, 0.0).astype(BF16)
    found = jnp.zeros((plan.slots, count), F32)
    for _ in range(3):
        rounded = logprob.astype(BF16)
        found = found + matmul(rounded, member, TN)
        logprob = logprob - rounded.astype(F32)
    at = lax.broadcasted_iota(jnp.int32, (plan.slots, count), 0) == slot_ref[...]
    out_ref[...] = jnp.sum(jnp.where(at, found, 0.0), axis=0, keepdims=True)


def scalar_call(kernel, at, args, outs, scratch, mib, cost=None, specs=None):
    whole = lambda x: pl.BlockSpec(x.shape, lambda i, at, n=len(x.shape): (0,) * n)
    specs = specs or {}
    return pl.pallas_call(
        kernel,
        out_shape=outs,
        grid_spec=pltpu.PrefetchScalarGridSpec(
            num_scalar_prefetch=1,
            grid=(1,),
            in_specs=[specs.get(i, whole(x)) for i, x in enumerate(args)],
            out_specs=jax.tree.map(whole, outs),
            scratch_shapes=scratch,
        ),
        compiler_params=limits(mib),
        cost_estimate=cost,
    )(at, *args)


def shape(dims, dtype):
    return jax.ShapeDtypeStruct(tuple(dims), dtype)


def turn_table(position):
    frequency = THETA ** (-2.0 * np.arange(HALF, dtype=np.float32) / HD)
    angles = np.float32(position) * frequency.astype(np.float32)
    return np.stack([np.cos(angles), np.sin(angles)], axis=1).astype(np.float32)


def entry_order(plan):
    order = np.zeros((plan.mine * HD, plan.mine * HD), np.float32)
    for head in range(plan.mine):
        for part in range(2):
            for entry in range(HALF):
                line, at = divmod(entry, plan.pairs)
                source = line * plan.q_rows + (part * plan.mine + head) * plan.pairs + at
                order[head * HD + part * HALF + entry, source] = 1.0
    return order


def per_device(prefix_kv, move_ids, move_board, move_table, norm_gain, w_query, w_keyval, w_score):
    row_count = move_ids.shape[0]
    boards_here, prefix_len, _ = prefix_kv.shape
    moves, width = move_table.shape
    groups, line, pair = lax.axis_size("groups"), lax.axis_size("line"), lax.axis_size("pair")
    board_total = boards_here * line * pair
    capacity = max(2, (2 * row_count + board_total - 1) // board_total)
    heads = w_query.shape[1] // HD
    plan = Plan(groups, line, pair, heads, capacity)
    depth = w_query.shape[0]
    group_at = lax.axis_index("groups").astype(jnp.int32)
    line_at = lax.axis_index("line").astype(jnp.int32)
    pair_at = lax.axis_index("pair").astype(jnp.int32)
    slab_at = group_at * pair + pair_at
    as_index = lambda x: x.reshape(1)
    ws = w_score.reshape(heads, HD)

    half_cols = w_query.shape[1] // groups
    packed = scalar_call(
        functools.partial(pack_weights, plan),
        as_index(group_at),
        (w_query, w_keyval, ws),
        shape((plan.peers, plan.rows, depth), BF16),
        [pltpu.VMEM((plan.peers * plan.rows, half_cols + 2 * HD), BF16)],
        32,
        specs={0: pl.BlockSpec((depth, half_cols), lambda i, at: (0, at[0]))},
    )
    weights = lax.all_to_all(packed, ("line", "pair"), split_axis=0, concat_axis=0, tiled=True)

    board_row = move_board.reshape(1, row_count)
    share = pair * boards_here
    listed, slot_row = scalar_call(
        functools.partial(list_moves, plan),
        as_index(line_at * pair + pair_at),
        (move_board, board_row, move_ids.reshape(1, row_count)),
        (shape((groups, line, pair, share, plan.slots), F32), shape((1, row_count), jnp.int32)),
        [],
        32,
    )
    everywhere = ("groups", "line", "pair")
    listed = lax.all_to_all(
        listed.reshape(groups * plan.peers, share, plan.slots), everywhere, split_axis=0, concat_axis=0, tiled=True
    )
    listed = jnp.sum(listed.reshape(groups, plan.peers, share, plan.slots), axis=1)
    listed = listed.astype(jnp.int32).reshape(plan.slab, boards_here, plan.slots)

    pieces = prefix_len // HD
    payload = pl.pallas_call(
        pack_prefix,
        out_shape=shape((boards_here, prefix_len + pieces * 2 * heads, HD), BF16),
        compiler_params=limits(32),
    )(prefix_kv, ws)
    payloads = [payload]
    for step in range(1, plan.slab):
        swap = [(at, at ^ step) for at in range(plan.slab)]
        payloads.append(lax.ppermute(payload, ("groups", "pair"), swap))

    block = min(moves, 128)
    normed = pl.pallas_call(
        normalize,
        out_shape=shape((moves, width), BF16),
        grid=(moves // block,),
        in_specs=[pl.BlockSpec((block, width), lambda i: (i, 0)), pl.BlockSpec((1, width), lambda i: (0, 0))],
        out_specs=pl.BlockSpec((block, width), lambda i: (i, 0)),
        compiler_params=limits(32),
    )(move_table, norm_gain.reshape(1, width))
    turns = jnp.asarray(turn_table(prefix_len))
    my_turns = jnp.tile(lax.dynamic_slice_in_dim(turns, line_at * plan.pairs, plan.pairs, axis=0), (plan.mine, 1))
    if depth % HD:
        weights = weights.transpose(1, 0, 2).reshape(plan.rows, width)
    block = min(moves, 256)
    queries, keys, own_values = pl.pallas_call(
        functools.partial(project, plan),
        out_shape=(
            shape((line, plan.q_rows, moves), BF16),
            shape((groups * plan.peers, plan.k_rows, moves), BF16),
            shape((plan.mine, moves), F32),
        ),
        grid=(moves // block,),
        in_specs=[
            pl.BlockSpec(weights.shape, lambda i, n=weights.ndim: (0,) * n),
            pl.BlockSpec((block, width), lambda i: (i, 0)),
            pl.BlockSpec(my_turns.shape, lambda i: (0, 0)),
        ],
        out_specs=(
            pl.BlockSpec((line, plan.q_rows, block), lambda i: (0, 0, i)),
            pl.BlockSpec((groups * plan.peers, plan.k_rows, block), lambda i: (0, 0, i)),
            pl.BlockSpec((plan.mine, block), lambda i: (0, i)),
        ),
        compiler_params=limits(40),
    )(weights, normed, my_turns)
    queries = lax.all_to_all(queries, "line", split_axis=0, concat_axis=0, tiled=True)
    keys = lax.all_to_all(keys, everywhere, split_axis=0, concat_axis=0, tiled=True)

    query_rows = plan.mine * HD
    back = plan.peers * lax.axis_size("tensor")
    parts = scalar_call(
        functools.partial(attend, plan),
        as_index(slab_at),
        (
            queries.reshape(query_rows, moves),
            jnp.asarray(entry_order(plan), BF16),
            keys.reshape(HD, moves),
            turns,
            own_values,
            *payloads,
            listed,
        ),
        shape((groups, back, share, plan.slots), F32),
        [
            pltpu.VMEM((query_rows + 16, moves), BF16),
            pltpu.VMEM((16, moves), F32),
            pltpu.VMEM((plan.slab, boards_here, plan.slots), F32),
        ],
        48,
    )
    parts = lax.all_to_all(
        parts.reshape(groups * back, share, plan.slots),
        ("groups", "line", "pair", "tensor"),
        split_axis=0,
        concat_axis=0,
        tiled=True,
    )
    parts = parts.reshape(groups, line, back // line, share, plan.slots)
    logprob = pl.pallas_call(
        functools.partial(finish, plan), out_shape=shape((1, row_count), F32), compiler_params=limits(32)
    )(parts, board_row, slot_row)
    return logprob.reshape(row_count)


def solution(mesh):
    order = ("groups", "dp", "tensor")
    assert mesh.axis_names == order
    pair = 2
    groups, peers, tensor = (mesh.shape[name] for name in order)
    fine = Mesh(mesh.devices.reshape(groups, peers // pair, pair, tensor), ("groups", "line", "pair", "tensor"))
    rows = ("groups", "line", "pair")
    placed = (
        P(rows, None, "tensor"),
        P(rows),
        P(rows, None),
        P(),
        P(),
        P(("line", "pair"), "tensor"),
        P(("line", "pair"), "tensor"),
        P("tensor"),
    )
    return jax.shard_map(per_device, mesh=fine, in_specs=placed, out_specs=P(rows), check_vma=False)
```

```python
import functools
import math

import jax
import jax.numpy as jnp
import numpy as np
from jax import lax
from jax.experimental import pallas as pl
from jax.experimental.pallas import tpu as pltpu
from jax.sharding import Mesh
from jax.sharding import PartitionSpec as P

HD = 128
HALF = HD // 2
EPS = 1e-06
THETA = 5000000.0
DEAD = -1e30

F32 = jnp.float32
BF16 = jnp.bfloat16

NN = (((1,), (0,)), ((), ()))
NT = (((1,), (1,)), ((), ()))
TN = (((0,), (0,)), ((), ()))


def matmul(a, b, dims=NN):
    return lax.dot_general(a, b, dims, preferred_element_type=F32)


def limits(mib):
    return pltpu.CompilerParams(vmem_limit_bytes=mib * 1024 * 1024)


class Plan:
    def __init__(self, groups, line, pair, heads, capacity):
        self.groups, self.line, self.pair = groups, line, pair
        self.peers = line * pair
        self.slab = groups * pair
        self.heads = heads
        self.mine = heads // self.slab
        self.pairs = HALF // line
        self.q_rows = self.mine * 2 * self.pairs
        self.k_rows = HD // (groups * self.peers)
        self.fold_rows = 2 * self.mine
        used = self.q_rows + self.k_rows + self.fold_rows
        self.rows = -(-used // 16) * 16
        self.capacity = capacity
        self.slots = self.peers * capacity


def pack_weights(plan, at_ref, wq_ref, wkv_ref, ws_ref, out_ref, pick):
    group = at_ref[0]
    rows, half_cols = plan.rows, wq_ref.shape[1]
    r = lax.broadcasted_iota(jnp.int32, (rows, 1), 0)
    part = r // (plan.mine * plan.pairs)
    head = (r // plan.pairs) % plan.mine
    entry = r % plan.pairs
    is_q = r < plan.q_rows
    k_at = r - plan.q_rows
    is_k = (k_at >= 0) & (k_at < plan.k_rows)
    f_at = k_at - plan.k_rows
    is_f = (f_at >= 0) & (f_at < plan.fold_rows)
    f_head = f_at // 2
    q_lane = lax.broadcasted_iota(jnp.int32, (rows, half_cols), 1)
    k_lane = lax.broadcasted_iota(jnp.int32, (rows, HD), 1)

    ws = ws_ref[...].astype(F32)

    def fill(peer, carry):
        line, pair = peer // plan.pair, peer % plan.pair
        column = (pair * plan.mine + head) * HD + part * HALF + line * plan.pairs + entry
        column = jnp.where(is_q, column, -1)
        at = pl.ds(pl.multiple_of(peer * rows, 16), rows)
        pick[at, :half_cols] = jnp.where(q_lane == column, 1.0, 0.0).astype(BF16)
        k_column = jnp.where(is_k, (group * plan.peers + peer) * plan.k_rows + k_at, -1)
        pick[at, half_cols : half_cols + HD] = jnp.where(k_lane == k_column, 1.0, 0.0).astype(BF16)
        fold = jnp.zeros((rows, HD), F32)
        my_head = jnp.where(is_f, (group * plan.pair + pair) * plan.mine + f_head, -1)
        for h in range(plan.heads):
            fold = jnp.where(my_head == h, ws[h : h + 1], fold)
        pick[at, half_cols + HD :] = fold.astype(BF16)
        return carry

    lax.fori_loop(0, plan.peers, fill, 0, unroll=plan.peers <= 8)
    total = matmul(pick[:, :half_cols], wq_ref[...], NT) + matmul(pick[:, half_cols:], wkv_ref[...], NT)
    rounded = total.astype(BF16)
    rest = (total - rounded.astype(F32)).astype(BF16)
    is_rest = is_f & (f_at % 2 == 1)
    for peer in range(plan.peers):
        at = slice(peer * rows, (peer + 1) * rows)
        out_ref[peer] = jnp.where(is_rest, rest[at].astype(F32), rounded[at].astype(F32)).astype(BF16)


def normalize(table_ref, gain_ref, out_ref):
    raw = table_ref[...].astype(F32)
    inverse = lax.rsqrt(jnp.mean(raw * raw, axis=-1, keepdims=True) + EPS)
    out_ref[...] = (raw * inverse * gain_ref[...].astype(F32)).astype(BF16)


def project(plan, w_ref, normed_ref, turn_ref, q_ref, k_ref, vo_ref):
    if len(w_ref.shape) == 3:
        depth = w_ref.shape[2]
        total = sum(
            matmul(w_ref[s], normed_ref[:, s * depth : (s + 1) * depth], NT) for s in range(w_ref.shape[0])
        )
    else:
        total = matmul(w_ref[...], normed_ref[...], NT)
    half = plan.q_rows // 2
    first, second = total[:half], total[half : 2 * half]
    cosine, sine = turn_ref[:, 0:1], turn_ref[:, 1:2]
    q = jnp.concatenate([first * cosine - second * sine, second * cosine + first * sine], axis=0).astype(BF16)
    for copy in range(q_ref.shape[0]):
        q_ref[copy] = q
    k = total[plan.q_rows : plan.q_rows + plan.k_rows].astype(BF16)
    k_ref[...] = k
    base = plan.q_rows + plan.k_rows
    for h in range(plan.mine):
        vo_ref[h : h + 1, :] = total[base + 2 * h : base + 2 * h + 1] + total[base + 2 * h + 1 : base + 2 * h + 2]


def pack_prefix(prefix_ref, ws_ref, out_ref):
    prefix_len = prefix_ref.shape[1]
    heads = ws_ref.shape[0]
    for board in range(prefix_ref.shape[0]):
        out_ref[board, :prefix_len] = prefix_ref[board, :, :HD]
        fold = matmul(ws_ref[...], prefix_ref[board, :, HD:], NT)
        rounded = fold.astype(BF16)
        rest = fold - rounded.astype(F32)
        both = jnp.concatenate([rounded.astype(F32), rest], axis=0).astype(BF16)
        for piece in range(prefix_len // HD):
            at = prefix_len + piece * 2 * heads
            out_ref[board, at : at + 2 * heads] = both[:, piece * HD : (piece + 1) * HD]


def list_moves(plan, at_ref, board_col_ref, board_row_ref, ids_ref, out_ref, slot_ref):
    count = board_col_ref.shape[0]
    same = board_col_ref[...] == board_row_ref[...]
    other = lax.broadcasted_iota(jnp.int32, (count, count), 0)
    own = lax.broadcasted_iota(jnp.int32, (count, count), 1)
    rank = jnp.sum(jnp.where(same & (other < own), 1.0, 0.0), axis=0, keepdims=True)
    slot = rank.astype(jnp.int32) + at_ref[0] * plan.capacity
    slot_ref[...] = slot
    slots_in = lax.broadcasted_iota(jnp.int32, (plan.slots, count), 0) == slot
    boards = out_ref.shape[0]
    member = lax.broadcasted_iota(jnp.int32, (boards, count), 0) == board_row_ref[...]
    move = ids_ref[...] + 1
    high, low = (move // 64).astype(F32), (move % 64).astype(F32)
    slots_in = jnp.where(slots_in, 1.0, 0.0).astype(BF16)
    listed = 64.0 * matmul(jnp.where(member, high, 0.0).astype(BF16), slots_in, NT)
    listed = listed + matmul(jnp.where(member, low, 0.0).astype(BF16), slots_in, NT)
    out_ref[...] = listed


def attend(plan, at_ref, q_ref, order_ref, k_ref, turn_ref, vo_ref, prefix_ref, moves_ref, out_ref, table, extra, scores):
    here = at_ref[0]
    mine, heads, slots = plan.mine, plan.heads, plan.slots
    moves = q_ref.shape[1]
    boards = prefix_ref.shape[1]
    prefix_len = prefix_ref.shape[2] * HD // (HD + 2 * heads)
    query_rows = mine * HD

    table[:query_rows] = matmul(order_ref[...], q_ref[...]).astype(BF16)
    key = k_ref[...].astype(F32)
    first, second = key[:HALF], key[HALF:]
    cosine, sine = turn_ref[:, 0:1], turn_ref[:, 1:2]
    key_first, key_second = first * cosine - second * sine, second * cosine + first * sine
    extra[...] = jnp.zeros_like(extra)
    for h in range(mine):
        q_first = table[h * HD : h * HD + HALF].astype(F32)
        q_second = table[h * HD + HALF : (h + 1) * HD].astype(F32)
        own_logit = jnp.sum(q_first * key_first + q_second * key_second, axis=0, keepdims=True)
        for place, value in ((0, own_logit), (2 * mine, vo_ref[h : h + 1, :])):
            rounded = value.astype(BF16).astype(F32)
            extra[place + h : place + h + 1] = rounded
            extra[place + mine + h : place + mine + h + 1] = value - rounded
    table[query_rows:] = extra[...].astype(BF16)

    scale = math.log2(math.e) / math.sqrt(HD)
    move_at = lax.broadcasted_iota(jnp.int32, (moves, slots), 0) + 1
    lanes = mine * slots
    fold_at = lax.broadcasted_iota(jnp.int32, (2 * heads, lanes), 0)
    fold_head = here * mine + lax.broadcasted_iota(jnp.int32, (2 * heads, lanes), 1) // slots
    fold_mine = (fold_at == fold_head) | (fold_at == fold_head + heads)

    def per_head(x, base):
        pieces = [x[base + h : base + h + 1] + x[base + mine + h : base + mine + h + 1] for h in range(mine)]
        return jnp.concatenate(pieces, axis=1)

    def step(board, carry):
        listed = []
        for j in range(plan.slab):
            listed.append(moves_ref[j, pl.ds(board, 1), :])
        chosen = [jnp.where(move_at == row, 1.0, 0.0).astype(BF16) for row in listed]
        taken = matmul(table[...], jnp.concatenate(chosen, axis=1))
        for j in range(plan.slab):
            x = taken[:, j * slots : (j + 1) * slots]
            q = jnp.concatenate([x[h * HD : (h + 1) * HD].astype(BF16) for h in range(mine)], axis=1)
            logits = matmul(prefix_ref[j, board, :prefix_len], q)
            own_logit = per_head(x, query_rows)
            own_value = per_head(x, query_rows + 2 * mine)
            peak = jnp.maximum(jnp.max(logits, axis=0, keepdims=True), own_logit)
            weight = jnp.exp2((logits - peak) * scale)
            own_weight = jnp.exp2((own_logit - peak) * scale)
            denom = jnp.sum(weight, axis=0, keepdims=True) + own_weight
            fold = jnp.concatenate(
                [
                    prefix_ref[j, board, prefix_len + p * 2 * heads : prefix_len + (p + 1) * 2 * heads]
                    for p in range(prefix_len // HD)
                ],
                axis=1,
            )
            value = matmul(fold, weight.astype(BF16))
            value = jnp.sum(jnp.where(fold_mine, value, 0.0), axis=0, keepdims=True)
            value = (value + own_value * own_weight) / denom
            score = sum(value[:, h * slots : (h + 1) * slots] for h in range(mine))
            scores[j, pl.ds(board, 1), :] = jnp.where(listed[j] > 0, score, DEAD)
        return carry

    lax.fori_loop(0, boards, step, 0)
    for g in range(plan.groups):
        mine_all = jnp.concatenate([scores[g * plan.pair + p] for p in range(plan.pair)], axis=0)
        for copy in range(out_ref.shape[1]):
            out_ref[g, copy] = mine_all


def finish(plan, parts_ref, board_ref, slot_ref, out_ref):
    line = parts_ref.shape[1]
    columns = []
    for at in range(line):
        total = None
        for g in range(parts_ref.shape[0]):
            for p in range(parts_ref.shape[2]):
                term = parts_ref[g, at, p]
                total = term if total is None else total + term
        columns.append(total)
    scores = jnp.concatenate(columns, axis=0)
    live = scores > 0.5 * DEAD
    peak = jnp.max(scores, axis=1, keepdims=True)
    denom = jnp.sum(jnp.where(live, jnp.exp(scores - peak), 0.0), axis=1, keepdims=True)
    logprob = jnp.where(live, scores - peak - jnp.log(denom), 0.0)
    count = board_ref.shape[1]
    member = lax.broadcasted_iota(jnp.int32, (scores.shape[0], count), 0) == board_ref[...]
    member = jnp.where(member, 1.0, 0.0).astype(BF16)
    found = jnp.zeros((plan.slots, count), F32)
    for _ in range(3):
        rounded = logprob.astype(BF16)
        found = found + matmul(rounded, member, TN)
        logprob = logprob - rounded.astype(F32)
    at = lax.broadcasted_iota(jnp.int32, (plan.slots, count), 0) == slot_ref[...]
    out_ref[...] = jnp.sum(jnp.where(at, found, 0.0), axis=0, keepdims=True)


def scalar_call(kernel, at, args, outs, scratch, mib, cost=None, specs=None):
    whole = lambda x: pl.BlockSpec(x.shape, lambda i, at, n=len(x.shape): (0,) * n)
    specs = specs or {}
    return pl.pallas_call(
        kernel,
        out_shape=outs,
        grid_spec=pltpu.PrefetchScalarGridSpec(
            num_scalar_prefetch=1,
            grid=(1,),
            in_specs=[specs.get(i, whole(x)) for i, x in enumerate(args)],
            out_specs=jax.tree.map(whole, outs),
            scratch_shapes=scratch,
        ),
        compiler_params=limits(mib),
        cost_estimate=cost,
    )(at, *args)


def shape(dims, dtype):
    return jax.ShapeDtypeStruct(tuple(dims), dtype)


def turn_table(position):
    frequency = THETA ** (-2.0 * np.arange(HALF, dtype=np.float32) / HD)
    angles = np.float32(position) * frequency.astype(np.float32)
    return np.stack([np.cos(angles), np.sin(angles)], axis=1).astype(np.float32)


def entry_order(plan):
    order = np.zeros((plan.mine * HD, plan.mine * HD), np.float32)
    for head in range(plan.mine):
        for part in range(2):
            for entry in range(HALF):
                line, at = divmod(entry, plan.pairs)
                source = line * plan.q_rows + (part * plan.mine + head) * plan.pairs + at
                order[head * HD + part * HALF + entry, source] = 1.0
    return order


def per_device(prefix_kv, move_ids, move_board, move_table, norm_gain, w_query, w_keyval, w_score):
    row_count = move_ids.shape[0]
    boards_here, prefix_len, _ = prefix_kv.shape
    moves, width = move_table.shape
    groups, line, pair = lax.axis_size("groups"), lax.axis_size("line"), lax.axis_size("pair")
    board_total = boards_here * line * pair
    capacity = max(2, (2 * row_count + board_total - 1) // board_total)
    heads = w_query.shape[1] // HD
    plan = Plan(groups, line, pair, heads, capacity)
    depth = w_query.shape[0]
    group_at = lax.axis_index("groups").astype(jnp.int32)
    line_at = lax.axis_index("line").astype(jnp.int32)
    pair_at = lax.axis_index("pair").astype(jnp.int32)
    slab_at = group_at * pair + pair_at
    as_index = lambda x: x.reshape(1)
    ws = w_score.reshape(heads, HD)

    half_cols = w_query.shape[1] // groups
    packed = scalar_call(
        functools.partial(pack_weights, plan),
        as_index(group_at),
        (w_query, w_keyval, ws),
        shape((plan.peers, plan.rows, depth), BF16),
        [pltpu.VMEM((plan.peers * plan.rows, half_cols + 2 * HD), BF16)],
        32,
        specs={0: pl.BlockSpec((depth, half_cols), lambda i, at: (0, at[0]))},
    )
    weights = lax.all_to_all(packed, ("line", "pair"), split_axis=0, concat_axis=0, tiled=True)

    board_row = move_board.reshape(1, row_count)
    share = pair * boards_here
    listed, slot_row = scalar_call(
        functools.partial(list_moves, plan),
        as_index(line_at * pair + pair_at),
        (move_board, board_row, move_ids.reshape(1, row_count)),
        (shape((board_total, plan.slots), F32), shape((1, row_count), jnp.int32)),
        [],
        32,
        pl.CostEstimate(flops=10**8, bytes_accessed=10**5, transcendentals=0),
    )
    everywhere = ("groups", "line", "pair")
    listed = lax.all_gather(listed, everywhere)
    listed = listed.reshape(groups, plan.peers, line, share, plan.slots)
    listed = lax.dynamic_index_in_dim(listed, line_at, axis=2, keepdims=False)
    listed = jnp.sum(listed, axis=1).astype(jnp.int32).reshape(plan.slab, boards_here, plan.slots)

    pieces = prefix_len // HD
    payload = pl.pallas_call(
        pack_prefix,
        out_shape=shape((boards_here, prefix_len + pieces * 2 * heads, HD), BF16),
        compiler_params=limits(32),
        cost_estimate=pl.CostEstimate(flops=10**8, bytes_accessed=2 * 10**6, transcendentals=0),
    )(prefix_kv, ws)
    payloads = lax.all_gather(payload, ("groups", "pair"))

    block = min(moves, 128)
    normed = pl.pallas_call(
        normalize,
        out_shape=shape((moves, width), BF16),
        grid=(moves // block,),
        in_specs=[pl.BlockSpec((block, width), lambda i: (i, 0)), pl.BlockSpec((1, width), lambda i: (0, 0))],
        out_specs=pl.BlockSpec((block, width), lambda i: (i, 0)),
        compiler_params=limits(32),
        cost_estimate=pl.CostEstimate(
            flops=8 * moves * width, bytes_accessed=4 * moves * width, transcendentals=moves
        ),
    )(move_table, norm_gain.reshape(1, width))
    turns = jnp.asarray(turn_table(prefix_len))
    my_turns = jnp.tile(lax.dynamic_slice_in_dim(turns, line_at * plan.pairs, plan.pairs, axis=0), (plan.mine, 1))
    if depth % HD:
        weights = weights.transpose(1, 0, 2).reshape(plan.rows, width)
    block = min(moves, 256)
    queries, keys, own_values = pl.pallas_call(
        functools.partial(project, plan),
        out_shape=(
            shape((line, plan.q_rows, moves), BF16),
            shape((plan.k_rows, moves), BF16),
            shape((plan.mine, moves), F32),
        ),
        grid=(moves // block,),
        in_specs=[
            pl.BlockSpec(weights.shape, lambda i, n=weights.ndim: (0,) * n),
            pl.BlockSpec((block, width), lambda i: (i, 0)),
            pl.BlockSpec(my_turns.shape, lambda i: (0, 0)),
        ],
        out_specs=(
            pl.BlockSpec((line, plan.q_rows, block), lambda i: (0, 0, i)),
            pl.BlockSpec((plan.k_rows, block), lambda i: (0, i)),
            pl.BlockSpec((plan.mine, block), lambda i: (0, i)),
        ),
        compiler_params=limits(40),
        cost_estimate=pl.CostEstimate(
            flops=2 * moves * width * 256, bytes_accessed=2 * moves * width, transcendentals=0
        ),
    )(weights, normed, my_turns)
    queries = lax.all_to_all(queries, "line", split_axis=0, concat_axis=0, tiled=True)
    keys = lax.all_gather(keys, everywhere)

    query_rows = plan.mine * HD
    back = plan.peers * lax.axis_size("tensor")
    parts = scalar_call(
        functools.partial(attend, plan),
        as_index(slab_at),
        (
            queries.reshape(query_rows, moves),
            jnp.asarray(entry_order(plan), BF16),
            keys.reshape(HD, moves),
            turns,
            own_values,
            payloads,
            listed,
        ),
        shape((groups, back, share, plan.slots), F32),
        [
            pltpu.VMEM((query_rows + 16, moves), BF16),
            pltpu.VMEM((16, moves), F32),
            pltpu.VMEM((plan.slab, boards_here, plan.slots), F32),
        ],
        48,
    )
    parts = lax.all_to_all(
        parts.reshape(groups * back, share, plan.slots),
        ("groups", "line", "pair", "tensor"),
        split_axis=0,
        concat_axis=0,
        tiled=True,
    )
    parts = parts.reshape(groups, line, back // line, share, plan.slots)
    logprob = pl.pallas_call(
        functools.partial(finish, plan), out_shape=shape((1, row_count), F32), compiler_params=limits(32)
    )(parts, board_row, slot_row)
    return logprob.reshape(row_count)


def solution(mesh):
    order = ("groups", "dp", "tensor")
    assert mesh.axis_names == order
    pair = 2
    groups, peers, tensor = (mesh.shape[name] for name in order)
    fine = Mesh(mesh.devices.reshape(groups, peers // pair, pair, tensor), ("groups", "line", "pair", "tensor"))
    rows = ("groups", "line", "pair")
    placed = (
        P(rows, None, "tensor"),
        P(rows),
        P(rows, None),
        P(),
        P(),
        P(("line", "pair"), "tensor"),
        P(("line", "pair"), "tensor"),
        P("tensor"),
    )
    return jax.shard_map(per_device, mesh=fine, in_specs=placed, out_specs=P(rows), check_vma=False)
```

```python
import functools
import math

import jax
import jax.numpy as jnp
import numpy as np
from jax import lax
from jax.experimental import pallas as pl
from jax.experimental.pallas import tpu as pltpu
from jax.sharding import Mesh
from jax.sharding import PartitionSpec as P

HD = 128
HALF = HD // 2
EPS = 1e-06
THETA = 5000000.0
DEAD = -1e30
VMEM_MIB = 52

F32 = jnp.float32
BF16 = jnp.bfloat16

NN = (((1,), (0,)), ((), ()))
NT = (((1,), (1,)), ((), ()))
TN = (((0,), (0,)), ((), ()))


def matmul(a, b, dims=NN):
    return lax.dot_general(a, b, dims, preferred_element_type=F32)


def limits(mib):
    return pltpu.CompilerParams(vmem_limit_bytes=mib * 1024 * 1024)


class Plan:
    def __init__(self, groups, line, pair, heads, capacity):
        self.groups, self.line, self.pair = groups, line, pair
        self.peers = line * pair
        self.slab = groups * pair
        self.heads = heads
        self.mine = heads // self.slab
        self.pairs = HALF // line
        self.q_rows = self.mine * 2 * self.pairs
        self.k_rows = HD // (groups * self.peers)
        self.fold_rows = 2 * self.mine
        used = self.q_rows + self.k_rows + self.fold_rows
        self.rows = -(-used // 16) * 16
        self.capacity = capacity
        self.slots = self.peers * capacity


def pack_weights(plan, at_ref, wq_ref, wkv_ref, ws_ref, out_ref, pick):
    group = at_ref[0]
    rows, half_cols = plan.rows, wq_ref.shape[1]
    r = lax.broadcasted_iota(jnp.int32, (rows, 1), 0)
    part = r // (plan.mine * plan.pairs)
    head = (r // plan.pairs) % plan.mine
    entry = r % plan.pairs
    is_q = r < plan.q_rows
    k_at = r - plan.q_rows
    is_k = (k_at >= 0) & (k_at < plan.k_rows)
    f_at = k_at - plan.k_rows
    is_f = (f_at >= 0) & (f_at < plan.fold_rows)
    f_head = f_at // 2
    q_lane = lax.broadcasted_iota(jnp.int32, (rows, half_cols), 1)
    k_lane = lax.broadcasted_iota(jnp.int32, (rows, HD), 1)

    ws = ws_ref[...].astype(F32)

    def fill(peer, carry):
        line, pair = peer // plan.pair, peer % plan.pair
        column = (pair * plan.mine + head) * HD + part * HALF + line * plan.pairs + entry
        column = jnp.where(is_q, column, -1)
        at = pl.ds(pl.multiple_of(peer * rows, 16), rows)
        pick[at, :half_cols] = jnp.where(q_lane == column, 1.0, 0.0).astype(BF16)
        chip = line * plan.slab + group * plan.pair + pair
        k_column = jnp.where(is_k, chip * plan.k_rows + k_at, -1)
        pick[at, half_cols : half_cols + HD] = jnp.where(k_lane == k_column, 1.0, 0.0).astype(BF16)
        fold = jnp.zeros((rows, HD), F32)
        my_head = jnp.where(is_f, (group * plan.pair + pair) * plan.mine + f_head, -1)
        for h in range(plan.heads):
            fold = jnp.where(my_head == h, ws[h : h + 1], fold)
        pick[at, half_cols + HD :] = fold.astype(BF16)
        return carry

    lax.fori_loop(0, plan.peers, fill, 0, unroll=plan.peers <= 8)
    total = matmul(pick[:, :half_cols], wq_ref[...], NT) + matmul(pick[:, half_cols:], wkv_ref[...], NT)
    rounded = total.astype(BF16)
    rest = (total - rounded.astype(F32)).astype(BF16)
    is_rest = is_f & (f_at % 2 == 1)
    for peer in range(plan.peers):
        at = slice(peer * rows, (peer + 1) * rows)
        out_ref[peer] = jnp.where(is_rest, rest[at].astype(F32), rounded[at].astype(F32)).astype(BF16)


def normalize(table_ref, gain_ref, after_ref, out_ref):
    raw = table_ref[...].astype(F32)
    inverse = lax.rsqrt(jnp.mean(raw * raw, axis=-1, keepdims=True) + EPS)
    out_ref[...] = (raw * inverse * gain_ref[...].astype(F32)).astype(BF16)


def project(plan, w_ref, normed_ref, turn_ref, *rest):
    q_ref, k_ref, vo_ref = rest[-3:]
    if len(w_ref.shape) == 3:
        depth = w_ref.shape[2]
        total = sum(
            matmul(w_ref[s], normed_ref[:, s * depth : (s + 1) * depth], NT) for s in range(w_ref.shape[0])
        )
    else:
        total = matmul(w_ref[...], normed_ref[...], NT)
    half = plan.q_rows // 2
    first, second = total[:half], total[half : 2 * half]
    cosine, sine = turn_ref[:, 0:1], turn_ref[:, 1:2]
    q = jnp.concatenate([first * cosine - second * sine, second * cosine + first * sine], axis=0).astype(BF16)
    for copy in range(q_ref.shape[0]):
        q_ref[copy] = q
    k = total[plan.q_rows : plan.q_rows + plan.k_rows].astype(BF16)
    k_ref[...] = k
    base = plan.q_rows + plan.k_rows
    for h in range(plan.mine):
        vo_ref[h : h + 1, :] = total[base + 2 * h : base + 2 * h + 1] + total[base + 2 * h + 1 : base + 2 * h + 2]


def pack_prefix(prefix_ref, ws_ref, after_ref, out_ref):
    boards = prefix_ref.shape[0]
    heads = ws_ref.shape[0]
    span = HD // boards
    ws = jnp.concatenate([ws_ref[...].astype(F32)] * (HD // heads), axis=0)
    row = lax.broadcasted_iota(jnp.int32, (HD, 1), 0)
    fold = None
    for board in range(boards):
        out_ref[board] = prefix_ref[board, :, :HD]
        keep = (row // span == board) & (row % span < 2 * heads)
        term = matmul(prefix_ref[board, :, HD:], jnp.where(keep, ws, 0.0).astype(BF16), NT)
        fold = term if fold is None else fold + term
    rounded = fold.astype(BF16).astype(F32)
    lane = lax.broadcasted_iota(jnp.int32, fold.shape, 1)
    out_ref[boards] = jnp.where(lane % span < heads, rounded, fold - rounded).astype(BF16)


def list_moves(plan, at_ref, board_col_ref, board_row_ref, ids_ref, after_ref, out_ref, slot_ref):
    count = board_col_ref.shape[0]
    same = board_col_ref[...] == board_row_ref[...]
    other = lax.broadcasted_iota(jnp.int32, (count, count), 0)
    own = lax.broadcasted_iota(jnp.int32, (count, count), 1)
    rank = jnp.sum(jnp.where(same & (other < own), 1.0, 0.0), axis=0, keepdims=True)
    slot = rank.astype(jnp.int32) + at_ref[0] * plan.capacity
    slot_ref[...] = slot
    slots_in = lax.broadcasted_iota(jnp.int32, (plan.slots, count), 0) == slot
    boards = out_ref.shape[0] * out_ref.shape[1]
    member = lax.broadcasted_iota(jnp.int32, (boards, count), 0) == board_row_ref[...]
    move = ids_ref[...] + 1
    high, low = (move // 64).astype(F32), (move % 64).astype(F32)
    slots_in = jnp.where(slots_in, 1.0, 0.0).astype(BF16)
    listed = 64.0 * matmul(jnp.where(member, high, 0.0).astype(BF16), slots_in, NT)
    listed = listed + matmul(jnp.where(member, low, 0.0).astype(BF16), slots_in, NT)
    out_ref[...] = listed.reshape(out_ref.shape)


def attend(plan, at_ref, q_ref, order_ref, k_ref, turn_ref, vo_ref, *rest):
    prefix_refs = rest[: plan.slab]
    moves_ref, out_ref, table, extra, scores = rest[plan.slab :]
    here, chip = at_ref[0], at_ref[1]
    mine, heads, slots = plan.mine, plan.heads, plan.slots
    moves = q_ref.shape[1]
    boards = prefix_refs[0].shape[0] - 1
    query_rows = mine * HD

    table[:query_rows] = matmul(order_ref[...], q_ref[...]).astype(BF16)
    row = lax.broadcasted_iota(jnp.int32, (HD, HD), 0)
    source = ((row // plan.k_rows) ^ chip) * plan.k_rows + row % plan.k_rows
    pick = jnp.where(lax.broadcasted_iota(jnp.int32, (HD, HD), 1) == source, 1.0, 0.0).astype(BF16)
    key = matmul(pick, k_ref[...])
    first, second = key[:HALF], key[HALF:]
    cosine, sine = turn_ref[:, 0:1], turn_ref[:, 1:2]
    key_first, key_second = first * cosine - second * sine, second * cosine + first * sine
    extra[...] = jnp.zeros_like(extra)
    for h in range(mine):
        q_first = table[h * HD : h * HD + HALF].astype(F32)
        q_second = table[h * HD + HALF : (h + 1) * HD].astype(F32)
        own_logit = jnp.sum(q_first * key_first + q_second * key_second, axis=0, keepdims=True)
        for place, value in ((0, own_logit), (2 * mine, vo_ref[h : h + 1, :])):
            rounded = value.astype(BF16).astype(F32)
            extra[place + h : place + h + 1] = rounded
            extra[place + mine + h : place + mine + h + 1] = value - rounded
    table[query_rows:] = extra[...].astype(BF16)

    scale = math.log2(math.e) / math.sqrt(HD)
    move_at = lax.broadcasted_iota(jnp.int32, (moves, slots), 0) + 1
    lanes = mine * slots
    span = HD // boards
    fold_row = lax.broadcasted_iota(jnp.int32, (HD, lanes), 0)
    fold_head = here * mine + lax.broadcasted_iota(jnp.int32, (HD, lanes), 1) // slots

    def per_head(x, base):
        pieces = [x[base + h : base + h + 1] + x[base + mine + h : base + mine + h + 1] for h in range(mine)]
        return jnp.concatenate(pieces, axis=1)

    def step(board, carry):
        listed = [moves_ref[here ^ j, pl.ds(board, 1), :] for j in range(plan.slab)]
        chosen = [jnp.where(move_at == row, 1.0, 0.0).astype(BF16) for row in listed]
        taken = matmul(table[...], jnp.concatenate(chosen, axis=1))
        at = fold_row - board * span
        fold_pick = jnp.where((at == fold_head) | (at == fold_head + heads), 1.0, 0.0).astype(BF16)
        for j in range(plan.slab):
            x = taken[:, j * slots : (j + 1) * slots]
            q = jnp.concatenate([x[h * HD : (h + 1) * HD].astype(BF16) for h in range(mine)], axis=1)
            logits = matmul(prefix_refs[j][board], q)
            fold = matmul(prefix_refs[j][boards], fold_pick)
            own_logit = per_head(x, query_rows)
            own_value = per_head(x, query_rows + 2 * mine)
            peak = jnp.maximum(jnp.max(logits, axis=0, keepdims=True), own_logit)
            weight = jnp.exp2((logits - peak) * scale)
            own_weight = jnp.exp2((own_logit - peak) * scale)
            denom = jnp.sum(weight, axis=0, keepdims=True) + own_weight
            value = (jnp.sum(weight * fold, axis=0, keepdims=True) + own_value * own_weight) / denom
            score = sum(value[:, h * slots : (h + 1) * slots] for h in range(mine))
            scores[here ^ j, pl.ds(board, 1), :] = jnp.where(listed[j] > 0, score, DEAD)
        return carry

    lax.fori_loop(0, boards, step, 0)
    for g in range(plan.groups):
        both = jnp.concatenate([scores[g * plan.pair + p] for p in range(plan.pair)], axis=0)
        for copy in range(out_ref.shape[1]):
            out_ref[g, copy] = both


def finish(plan, parts_ref, board_ref, slot_ref, out_ref):
    line = parts_ref.shape[1]
    columns = []
    for at in range(line):
        total = None
        for g in range(parts_ref.shape[0]):
            for p in range(parts_ref.shape[2]):
                term = parts_ref[g, at, p]
                total = term if total is None else total + term
        columns.append(total)
    scores = jnp.concatenate(columns, axis=0)
    live = scores > 0.5 * DEAD
    peak = jnp.max(scores, axis=1, keepdims=True)
    denom = jnp.sum(jnp.where(live, jnp.exp(scores - peak), 0.0), axis=1, keepdims=True)
    logprob = jnp.where(live, scores - peak - jnp.log(denom), 0.0)
    count = board_ref.shape[1]
    member = lax.broadcasted_iota(jnp.int32, (scores.shape[0], count), 0) == board_ref[...]
    member = jnp.where(member, 1.0, 0.0).astype(BF16)
    found = jnp.zeros((plan.slots, count), F32)
    for _ in range(3):
        rounded = logprob.astype(BF16)
        found = found + matmul(rounded, member, TN)
        logprob = logprob - rounded.astype(F32)
    at = lax.broadcasted_iota(jnp.int32, (plan.slots, count), 0) == slot_ref[...]
    out_ref[...] = jnp.sum(jnp.where(at, found, 0.0), axis=0, keepdims=True)


def untouched():
    return pl.BlockSpec(memory_space=pl.ANY)


def scalar_call(kernel, at, args, outs, scratch, cost=None, specs=None):
    whole = lambda x: pl.BlockSpec(x.shape, lambda i, at, n=len(x.shape): (0,) * n)
    specs = specs or {}
    return pl.pallas_call(
        kernel,
        out_shape=outs,
        grid_spec=pltpu.PrefetchScalarGridSpec(
            num_scalar_prefetch=1,
            grid=(1,),
            in_specs=[specs.get(i, whole(x)) for i, x in enumerate(args)],
            out_specs=jax.tree.map(whole, outs),
            scratch_shapes=scratch,
        ),
        compiler_params=limits(VMEM_MIB),
        cost_estimate=cost,
    )(at, *args)


def cost(flops, nbytes):
    return pl.CostEstimate(flops=int(flops), bytes_accessed=int(nbytes), transcendentals=0)


def swap(x, names, size, step):
    return lax.ppermute(x, names, [(at, at ^ step) for at in range(size)])


def gather_near(x, names, size):
    return jnp.concatenate([x] + [swap(x, names, size, step) for step in range(1, size)], axis=0)


def shape(dims, dtype):
    return jax.ShapeDtypeStruct(tuple(dims), dtype)


def turn_table(position):
    frequency = THETA ** (-2.0 * np.arange(HALF, dtype=np.float32) / HD)
    angles = np.float32(position) * frequency.astype(np.float32)
    return np.stack([np.cos(angles), np.sin(angles)], axis=1).astype(np.float32)


def entry_order(plan):
    order = np.zeros((plan.mine * HD, plan.mine * HD), np.float32)
    for head in range(plan.mine):
        for part in range(2):
            for entry in range(HALF):
                line, at = divmod(entry, plan.pairs)
                source = line * plan.q_rows + (part * plan.mine + head) * plan.pairs + at
                order[head * HD + part * HALF + entry, source] = 1.0
    return order


def per_device(prefix_kv, move_ids, move_board, move_table, norm_gain, w_query, w_keyval, w_score):
    row_count = move_ids.shape[0]
    boards_here, prefix_len, _ = prefix_kv.shape
    moves, width = move_table.shape
    groups, line, pair = lax.axis_size("groups"), lax.axis_size("line"), lax.axis_size("pair")
    board_total = boards_here * line * pair
    capacity = max(2, (2 * row_count + board_total - 1) // board_total)
    heads = w_query.shape[1] // HD
    plan = Plan(groups, line, pair, heads, capacity)
    depth = w_query.shape[0]
    group_at = lax.axis_index("groups").astype(jnp.int32)
    line_at = lax.axis_index("line").astype(jnp.int32)
    pair_at = lax.axis_index("pair").astype(jnp.int32)
    slab_at = group_at * pair + pair_at
    ws = w_score.reshape(heads, HD)
    slab_axes = ("groups", "pair")

    half_cols = w_query.shape[1] // groups
    packed = scalar_call(
        functools.partial(pack_weights, plan),
        group_at.reshape(1),
        (w_query, w_keyval, ws),
        shape((plan.peers, plan.rows, depth), BF16),
        [pltpu.VMEM((plan.peers * plan.rows, half_cols + 2 * HD), BF16)],
        cost(2 * plan.peers * plan.rows * half_cols * depth, 4 * w_query.size),
        {0: pl.BlockSpec((depth, half_cols), lambda i, at: (0, at[0]))},
    )
    weights = lax.all_to_all(packed, ("line", "pair"), split_axis=0, concat_axis=0, tiled=True)

    payload = pl.pallas_call(
        pack_prefix,
        out_shape=shape((boards_here + 1, prefix_len, HD), BF16),
        in_specs=[pl.BlockSpec(memory_space=pltpu.VMEM), pl.BlockSpec(memory_space=pltpu.VMEM), untouched()],
        compiler_params=limits(VMEM_MIB),
        cost_estimate=cost(2 * prefix_len * HD * HD * boards_here, 2 * prefix_kv.size),
    )(prefix_kv, ws, packed)
    beside = swap(payload, slab_axes, plan.slab, 1)
    across = swap(payload, slab_axes, plan.slab, 2)

    board_row = move_board.reshape(1, row_count)
    share = pair * boards_here
    listed, slot_row = scalar_call(
        functools.partial(list_moves, plan),
        (line_at * pair + pair_at).reshape(1),
        (move_board, board_row, move_ids.reshape(1, row_count), packed),
        (shape((line, share, plan.slots), F32), shape((1, row_count), jnp.int32)),
        [],
        cost(8 * row_count * row_count, 4 * board_total * plan.slots),
        {3: untouched()},
    )
    remaining = line
    while remaining > 1:
        remaining //= 2
        upper = (line_at // remaining) % 2
        kept = lax.dynamic_slice_in_dim(listed, upper * remaining, remaining, axis=0)
        given = lax.dynamic_slice_in_dim(listed, (1 - upper) * remaining, remaining, axis=0)
        listed = kept + swap(given, "line", line, remaining)
    listed = listed[0]
    turned = [listed] + [swap(listed, slab_axes, plan.slab, step) for step in range(1, plan.slab)]
    same = sum(turned[:pair])
    other = sum(turned[pair:])
    listed = jnp.where(group_at == 0, jnp.stack([same, other]), jnp.stack([other, same]))
    listed = listed.astype(jnp.int32).reshape(plan.slab, boards_here, plan.slots)

    block = min(moves, 128)
    normed = pl.pallas_call(
        normalize,
        out_shape=shape((moves, width), BF16),
        grid=(moves // block,),
        in_specs=[
            pl.BlockSpec((block, width), lambda i: (i, 0)),
            pl.BlockSpec((1, width), lambda i: (0, 0)),
            untouched(),
        ],
        out_specs=pl.BlockSpec((block, width), lambda i: (i, 0)),
        compiler_params=limits(VMEM_MIB),
        cost_estimate=cost(8 * moves * width, 4 * moves * width),
    )(move_table, norm_gain.reshape(1, width), packed)
    turns = jnp.asarray(turn_table(prefix_len))
    my_turns = jnp.tile(lax.dynamic_slice_in_dim(turns, line_at * plan.pairs, plan.pairs, axis=0), (plan.mine, 1))
    if depth % HD:
        weights = weights.transpose(1, 0, 2).reshape(plan.rows, width)
    block = min(moves, 256)
    queries, keys, own_values = pl.pallas_call(
        functools.partial(project, plan),
        out_shape=(
            shape((line, plan.q_rows, moves), BF16),
            shape((plan.k_rows, moves), BF16),
            shape((plan.mine, moves), F32),
        ),
        grid=(moves // block,),
        in_specs=[
            pl.BlockSpec(weights.shape, lambda i, n=weights.ndim: (0,) * n),
            pl.BlockSpec((block, width), lambda i: (i, 0)),
            pl.BlockSpec(my_turns.shape, lambda i: (0, 0)),
            untouched(),
            untouched(),
            untouched(),
        ],
        out_specs=(
            pl.BlockSpec((line, plan.q_rows, block), lambda i: (0, 0, i)),
            pl.BlockSpec((plan.k_rows, block), lambda i: (0, i)),
            pl.BlockSpec((plan.mine, block), lambda i: (0, i)),
        ),
        compiler_params=limits(VMEM_MIB),
        cost_estimate=cost(2 * moves * width * 256, 2 * moves * width),
    )(weights, normed, my_turns, beside, across, listed)
    queries = lax.all_to_all(queries, "line", split_axis=0, concat_axis=0, tiled=True)
    diagonal = swap(beside, slab_axes, plan.slab, 2)
    keys = gather_near(keys, slab_axes, plan.slab)
    bit = 1
    while bit < line:
        size = min(4, line // bit)
        keys = jnp.concatenate([keys] + [swap(keys, "line", line, at * bit) for at in range(1, size)], axis=0)
        bit *= size

    query_rows = plan.mine * HD
    back = plan.peers * lax.axis_size("tensor")
    parts = scalar_call(
        functools.partial(attend, plan),
        jnp.stack([slab_at, line_at * plan.slab + slab_at]),
        (
            queries.reshape(query_rows, moves),
            jnp.asarray(entry_order(plan), BF16),
            keys,
            turns,
            own_values,
            payload,
            beside,
            across,
            diagonal,
            listed,
        ),
        shape((groups, back, share, plan.slots), F32),
        [
            pltpu.VMEM((query_rows + 16, moves), BF16),
            pltpu.VMEM((16, moves), F32),
            pltpu.VMEM((plan.slab, boards_here, plan.slots), F32),
        ],
        cost(2 * 272 * moves * 4096, 4 * 10**6),
    )
    parts = lax.all_to_all(
        parts.reshape(groups * back, share, plan.slots),
        ("groups", "line", "pair", "tensor"),
        split_axis=0,
        concat_axis=0,
        tiled=True,
    )
    parts = parts.reshape(groups, line, back // line, share, plan.slots)
    logprob = pl.pallas_call(
        functools.partial(finish, plan), out_shape=shape((1, row_count), F32), compiler_params=limits(VMEM_MIB)
    )(parts, board_row, slot_row)
    return logprob.reshape(row_count)


def solution(mesh):
    order = ("groups", "dp", "tensor")
    assert mesh.axis_names == order
    pair = 2
    groups, peers, tensor = (mesh.shape[name] for name in order)
    fine = Mesh(mesh.devices.reshape(groups, peers // pair, pair, tensor), ("groups", "line", "pair", "tensor"))
    rows = ("groups", "line", "pair")
    placed = (
        P(rows, None, "tensor"),
        P(rows),
        P(rows, None),
        P(),
        P(),
        P(("line", "pair"), "tensor"),
        P(("line", "pair"), "tensor"),
        P("tensor"),
    )
    return jax.shard_map(per_device, mesh=fine, in_specs=placed, out_specs=P(rows), check_vma=False)
```

```python
import functools
import math

import jax
import jax.numpy as jnp
import numpy as np
from jax import lax
from jax.experimental import pallas as pl
from jax.experimental.pallas import tpu as pltpu
from jax.sharding import Mesh
from jax.sharding import PartitionSpec as P

HD = 128
HALF = HD // 2
EPS = 1e-06
THETA = 5000000.0
DEAD = -1e30
VMEM_MIB = 52

F32 = jnp.float32
BF16 = jnp.bfloat16

NN = (((1,), (0,)), ((), ()))
NT = (((1,), (1,)), ((), ()))
TN = (((0,), (0,)), ((), ()))


def matmul(a, b, dims=NN):
    return lax.dot_general(a, b, dims, preferred_element_type=F32)


def limits(mib):
    return pltpu.CompilerParams(vmem_limit_bytes=mib * 1024 * 1024)


class Plan:
    def __init__(self, groups, line, pair, heads, capacity, share):
        self.groups, self.line, self.pair = groups, line, pair
        self.peers = line * pair
        self.slab = groups * pair
        self.heads = heads
        self.mine = heads // self.slab
        self.pairs = HALF // line
        self.q_rows = self.mine * 2 * self.pairs
        self.k_rows = 2 * self.pairs
        self.fold_at = self.q_rows + self.k_rows
        self.list_at = self.fold_at + self.mine
        self.rows = -(-(self.list_at + 1) // 8) * 8
        self.line_rows = -(-(self.q_rows + 2 * self.mine) // 8) * 8
        self.capacity = capacity
        self.share = share
        self.slots = self.peers * capacity


def pack_weights(plan, at_ref, wq_hbm, wkv_hbm, ws_ref, board_ref, ids_ref, out_ref, wq, wkv, pick, sems):
    group = at_ref[0]
    rows, half_cols = plan.rows, wq.shape[1]
    columns_here = pl.ds(pl.multiple_of(group * half_cols, HD), half_cols)
    copies = (
        pltpu.make_async_copy(wq_hbm.at[:, columns_here], wq, sems.at[0]),
        pltpu.make_async_copy(wkv_hbm, wkv, sems.at[1]),
    )
    for copy in copies:
        copy.start()
    r = lax.broadcasted_iota(jnp.int32, (rows, 1), 0)
    part = r // (plan.mine * plan.pairs)
    head = (r // plan.pairs) % plan.mine
    entry = r % plan.pairs
    is_q = r < plan.q_rows
    k_at = r - plan.q_rows
    is_k = (k_at >= 0) & (k_at < plan.k_rows)
    f_at = r - plan.fold_at
    is_f = (f_at >= 0) & (f_at < plan.mine)
    q_lane = lax.broadcasted_iota(jnp.int32, (rows, half_cols), 1)
    k_lane = lax.broadcasted_iota(jnp.int32, (rows, HD), 1)
    ws = ws_ref[...].astype(F32)

    def fill(peer, carry):
        line, pair = peer // plan.pair, peer % plan.pair
        column = (pair * plan.mine + head) * HD + part * HALF + line * plan.pairs + entry
        column = jnp.where(is_q, column, -1)
        at = pl.ds(pl.multiple_of(peer * rows, 8), rows)
        pick[at, :half_cols] = jnp.where(q_lane == column, 1.0, 0.0)
        k_column = (k_at // plan.pairs) * HALF + line * plan.pairs + k_at % plan.pairs
        k_column = jnp.where(is_k, k_column, -1)
        pick[at, half_cols : half_cols + HD] = jnp.where(k_lane == k_column, 1.0, 0.0)
        fold = jnp.zeros((rows, HD), F32)
        my_head = jnp.where(is_f, (group * plan.pair + pair) * plan.mine + f_at, -1)
        for h in range(plan.heads):
            fold = jnp.where(my_head == h, ws[h : h + 1], fold)
        pick[at, half_cols + HD :] = fold
        return carry

    lax.fori_loop(0, plan.peers, fill, 0, unroll=plan.peers <= 8)

    count, depth = board_ref.shape[1], wq.shape[0]
    board_row = board_ref[...]
    board_col = jnp.broadcast_to(board_row.astype(F32), (8, count)).T[:, 0:1].astype(jnp.int32)
    own = lax.broadcasted_iota(jnp.int32, (count, count), 0)
    other = lax.broadcasted_iota(jnp.int32, (count, count), 1)
    ahead = jnp.where((board_col == board_row) & (other < own), 1.0, 0.0)
    rank = jnp.sum(ahead, axis=1, keepdims=True).astype(jnp.int32)
    key = board_col * plan.capacity + rank
    move = ids_ref[...] + 1
    parts = jnp.concatenate([(move // 64).astype(F32), (move % 64).astype(F32)], axis=0).astype(BF16)
    span = plan.share * plan.capacity
    lane = lax.broadcasted_iota(jnp.int32, (count, depth), 1)
    lane_row = lax.broadcasted_iota(jnp.int32, (1, depth), 1)
    lists = []
    for line in range(plan.line):
        place = jnp.where(lane < span, lane, lane - span) + line * span
        found = matmul(parts, jnp.where(key == place, 1.0, 0.0).astype(BF16))
        lists.append(jnp.where(lane_row < span, found[0:1], found[1:2]))

    for copy in copies:
        copy.wait()
    left = pick[...].astype(BF16)
    total = matmul(left[:, :half_cols], wq[...], NT) + matmul(left[:, half_cols:], wkv[...], NT)
    for peer in range(plan.peers):
        mine = total[peer * rows : (peer + 1) * rows]
        out_ref[peer] = jnp.where(r == plan.list_at, lists[peer // plan.pair], mine).astype(BF16)


def normalize(table_hbm, gain_ref, after_ref, out_ref, buffers, sems):
    held, block, width = buffers.shape
    steps = table_hbm.shape[0] // block

    def copy(step):
        at = step % held
        return pltpu.make_async_copy(table_hbm.at[pl.ds(step * block, block)], buffers.at[at], sems.at[at])

    for step in range(min(held - 1, steps)):
        copy(step).start()
    gain = gain_ref[...].astype(F32)
    for step in range(steps):
        if step + held - 1 < steps:
            copy(step + held - 1).start()
        copy(step).wait()

        def one(tile, carry):
            raw = buffers[step % held, pl.ds(pl.multiple_of(tile * 16, 16), 16)].astype(F32)
            inverse = lax.rsqrt(jnp.mean(raw * raw, axis=-1, keepdims=True) + EPS)
            at = pl.ds(pl.multiple_of(step * block + tile * 16, 16), 16)
            out_ref[at, :] = (raw * inverse * gain).astype(BF16)
            return carry

        lax.fori_loop(0, block // 16, one, 0)


def project(plan, w_ref, normed_ref, turn_ref, *rest):
    q_ref, vo_ref = rest[-2:]
    moves = normed_ref.shape[0]
    block = min(moves, 256)
    half, k_half = plan.q_rows // 2, plan.k_rows // 2
    cosine, sine = turn_ref[:, 0:1], turn_ref[:, 1:2]
    for start in range(0, moves, block):
        at = slice(start, start + block)
        if len(w_ref.shape) == 3:
            depth = w_ref.shape[2]
            total = None
            for s in range(w_ref.shape[0]):
                term = matmul(w_ref[s], normed_ref[at, s * depth : (s + 1) * depth], NT)
                total = term if total is None else total + term
        else:
            total = matmul(w_ref[...], normed_ref[at, :], NT)
        first, second = total[:half], total[half : 2 * half]
        q_first = (first * cosine - second * sine).astype(BF16)
        q_second = (second * cosine + first * sine).astype(BF16)
        first, second = total[plan.q_rows : plan.q_rows + k_half], total[plan.q_rows + k_half : plan.fold_at]
        cos_k, sin_k = cosine[:k_half], sine[:k_half]
        k_first = (first * cos_k - second * sin_k).astype(BF16).astype(F32)
        k_second = (second * cos_k + first * sin_k).astype(BF16).astype(F32)
        f_first, f_second = q_first.astype(F32), q_second.astype(F32)
        logits, tails = [], []
        for h in range(plan.mine):
            own = slice(h * k_half, (h + 1) * k_half)
            logit = jnp.sum(f_first[own] * k_first + f_second[own] * k_second, axis=0, keepdims=True)
            logits.append(logit.astype(BF16).astype(F32))
            tails.append(logit - logits[-1])
        pad = plan.line_rows - plan.q_rows - 2 * plan.mine
        pieces = [f_first, f_second, *logits, *tails]
        if pad:
            pieces.append(jnp.zeros((pad, block), F32))
        out = jnp.concatenate(pieces, axis=0).astype(BF16)
        for copy in range(q_ref.shape[0]):
            q_ref[copy, :, at] = out
        vo_ref[:, at] = total[plan.fold_at : plan.list_at]


def pack_prefix(prefix_ref, ws_ref, after_ref, out_ref):
    boards = prefix_ref.shape[0]
    heads = ws_ref.shape[0]
    span = HD // boards
    ws = jnp.concatenate([ws_ref[...].astype(F32)] * (HD // heads), axis=0)
    row = lax.broadcasted_iota(jnp.int32, (HD, 1), 0)
    fold = None
    for board in range(boards):
        out_ref[board] = prefix_ref[board, :, :HD]
        keep = (row // span == board) & (row % span < 2 * heads)
        term = matmul(prefix_ref[board, :, HD:], jnp.where(keep, ws, 0.0).astype(BF16), NT)
        fold = term if fold is None else fold + term
    rounded = fold.astype(BF16).astype(F32)
    lane = lax.broadcasted_iota(jnp.int32, fold.shape, 1)
    out_ref[boards] = jnp.where(lane % span < heads, rounded, fold - rounded).astype(BF16)


def find_slots(plan, at_ref, board_ref, after_ref, slot_ref):
    count = board_ref.shape[1]
    board_row = board_ref[...]
    board_col = jnp.broadcast_to(board_row.astype(F32), (8, count)).T[:, 0:1].astype(jnp.int32)
    other = lax.broadcasted_iota(jnp.int32, (count, count), 0)
    own = lax.broadcasted_iota(jnp.int32, (count, count), 1)
    rank = jnp.sum(jnp.where((board_col == board_row) & (other < own), 1.0, 0.0), axis=0, keepdims=True)
    slot_ref[...] = rank.astype(jnp.int32) + at_ref[0] * plan.capacity


def read_lists(plan, w_ref, out_ref):
    share, capacity, peers = plan.share, plan.capacity, plan.peers
    span = share * capacity
    rows = jnp.concatenate([w_ref[s].astype(F32)[plan.list_at : plan.list_at + 1] for s in range(peers)], axis=0)
    lane = lax.broadcasted_iota(jnp.int32, (share * peers, 2 * span), 1)
    row = lax.broadcasted_iota(jnp.int32, (share * peers, 2 * span), 0)
    lane = jnp.where(lane < span, lane, lane - span)
    spread = jnp.concatenate([rows] * share, axis=0)
    spread = jnp.where(lane // capacity == row // peers, spread, 0.0).astype(BF16)
    c = lax.broadcasted_iota(jnp.int32, (2 * span, plan.slots), 0)
    slot = lax.broadcasted_iota(jnp.int32, (2 * span, plan.slots), 1)
    scale = jnp.where(c < span, 64.0, 1.0)
    place = jnp.where(c % capacity == slot % capacity, scale, 0.0).astype(BF16)
    listed = matmul(spread, place)
    row = lax.broadcasted_iota(jnp.int32, listed.shape, 0)
    slot = lax.broadcasted_iota(jnp.int32, listed.shape, 1)
    listed = jnp.where(slot // capacity == row % peers, listed, 0.0)
    out_ref[...] = jnp.sum(listed.reshape(share, peers, plan.slots), axis=1)


def attend(plan, at_ref, q_ref, order_ref, vo_ref, *rest):
    prefix_refs = rest[: plan.slab]
    moves_ref, out_ref, table, extra, scores = rest[plan.slab :]
    here = at_ref[0]
    mine, heads, slots = plan.mine, plan.heads, plan.slots
    moves = q_ref.shape[1]
    boards = prefix_refs[0].shape[0] - 1
    query_rows = mine * HD

    mixed = matmul(order_ref[...], q_ref[...])
    table[:query_rows] = mixed[:query_rows].astype(BF16)
    extra[...] = jnp.zeros_like(extra)
    for place, value in ((0, mixed[query_rows : query_rows + mine]), (2 * mine, vo_ref[...])):
        rounded = value.astype(BF16).astype(F32)
        extra[place : place + mine] = rounded
        extra[place + mine : place + 2 * mine] = value - rounded
    table[query_rows:] = extra[...].astype(BF16)

    scale = math.log2(math.e) / math.sqrt(HD)
    move_at = lax.broadcasted_iota(jnp.int32, (moves, slots), 0) + 1
    lanes = mine * slots
    span = HD // boards
    fold_row = lax.broadcasted_iota(jnp.int32, (HD, lanes), 0)
    fold_head = here * mine + lax.broadcasted_iota(jnp.int32, (HD, lanes), 1) // slots

    def per_head(x, base):
        pieces = [x[base + h : base + h + 1] + x[base + mine + h : base + mine + h + 1] for h in range(mine)]
        return jnp.concatenate(pieces, axis=1)

    def step(board, carry):
        listed = [moves_ref[j // plan.pair, pl.ds(((here ^ j) % plan.pair) * boards + board, 1), :] for j in range(plan.slab)]
        chosen = [jnp.where(move_at == row, 1.0, 0.0).astype(BF16) for row in listed]
        taken = matmul(table[...], jnp.concatenate(chosen, axis=1))
        at = fold_row - board * span
        fold_pick = jnp.where((at == fold_head) | (at == fold_head + heads), 1.0, 0.0).astype(BF16)
        for j in range(plan.slab):
            x = taken[:, j * slots : (j + 1) * slots]
            q = jnp.concatenate([x[h * HD : (h + 1) * HD].astype(BF16) for h in range(mine)], axis=1)
            logits = matmul(prefix_refs[j][board], q)
            fold = matmul(prefix_refs[j][boards], fold_pick)
            own_logit = per_head(x, query_rows)
            own_value = per_head(x, query_rows + 2 * mine)
            peak = jnp.maximum(jnp.max(logits, axis=0, keepdims=True), own_logit)
            weight = jnp.exp2((logits - peak) * scale)
            own_weight = jnp.exp2((own_logit - peak) * scale)
            denom = jnp.sum(weight, axis=0, keepdims=True) + own_weight
            value = (jnp.sum(weight * fold, axis=0, keepdims=True) + own_value * own_weight) / denom
            score = sum(value[:, h * slots : (h + 1) * slots] for h in range(mine))
            scores[here ^ j, pl.ds(board, 1), :] = jnp.where(listed[j] > 0, score, DEAD)
        return carry

    lax.fori_loop(0, boards, step, 0)
    for g in range(plan.groups):
        both = jnp.concatenate([scores[g * plan.pair + p] for p in range(plan.pair)], axis=0)
        for copy in range(out_ref.shape[1]):
            out_ref[g, copy] = both


def finish(plan, parts_ref, board_ref, slot_ref, out_ref):
    line = parts_ref.shape[1]
    columns = []
    for at in range(line):
        total = None
        for g in range(parts_ref.shape[0]):
            for p in range(parts_ref.shape[2]):
                term = parts_ref[g, at, p]
                total = term if total is None else total + term
        columns.append(total)
    scores = jnp.concatenate(columns, axis=0)
    live = scores > 0.5 * DEAD
    peak = jnp.max(scores, axis=1, keepdims=True)
    denom = jnp.sum(jnp.where(live, jnp.exp(scores - peak), 0.0), axis=1, keepdims=True)
    logprob = jnp.where(live, scores - peak - jnp.log(denom), 0.0)
    count = board_ref.shape[1]
    member = lax.broadcasted_iota(jnp.int32, (scores.shape[0], count), 0) == board_ref[...]
    member = jnp.where(member, 1.0, 0.0).astype(BF16)
    found = jnp.zeros((plan.slots, count), F32)
    for _ in range(3):
        rounded = logprob.astype(BF16)
        found = found + matmul(rounded, member, TN)
        logprob = logprob - rounded.astype(F32)
    at = lax.broadcasted_iota(jnp.int32, (plan.slots, count), 0) == slot_ref[...]
    out_ref[...] = jnp.sum(jnp.where(at, found, 0.0), axis=0, keepdims=True)


def untouched():
    return pl.BlockSpec(memory_space=pl.ANY)


def scalar_call(kernel, at, args, outs, scratch, cost=None, specs=None):
    whole = lambda x: pl.BlockSpec(x.shape, lambda i, at, n=len(x.shape): (0,) * n)
    specs = specs or {}
    return pl.pallas_call(
        kernel,
        out_shape=outs,
        grid_spec=pltpu.PrefetchScalarGridSpec(
            num_scalar_prefetch=1,
            grid=(1,),
            in_specs=[specs.get(i, whole(x)) for i, x in enumerate(args)],
            out_specs=jax.tree.map(whole, outs),
            scratch_shapes=scratch,
        ),
        compiler_params=limits(VMEM_MIB),
        cost_estimate=cost,
    )(at, *args)


def cost(flops, nbytes):
    return pl.CostEstimate(flops=int(flops), bytes_accessed=int(nbytes), transcendentals=0)


def swap(x, names, size, step):
    return lax.ppermute(x, names, [(at, at ^ step) for at in range(size)])


def shape(dims, dtype):
    return jax.ShapeDtypeStruct(tuple(dims), dtype)


def turn_table(position):
    frequency = THETA ** (-2.0 * np.arange(HALF, dtype=np.float32) / HD)
    angles = np.float32(position) * frequency.astype(np.float32)
    return np.stack([np.cos(angles), np.sin(angles)], axis=1).astype(np.float32)


def entry_order(plan):
    order = np.zeros((plan.mine * HD + 16, plan.line * plan.line_rows), np.float32)
    for head in range(plan.mine):
        for part in range(2):
            for entry in range(HALF):
                line, at = divmod(entry, plan.pairs)
                source = line * plan.line_rows + (part * plan.mine + head) * plan.pairs + at
                order[head * HD + part * HALF + entry, source] = 1.0
        for line in range(plan.line):
            for piece in range(2):
                order[plan.mine * HD + head, line * plan.line_rows + plan.q_rows + piece * plan.mine + head] = 1.0
    return order


def per_device(prefix_kv, move_ids, move_board, move_table, norm_gain, w_query, w_keyval, w_score):
    row_count = move_ids.shape[0]
    boards_here, prefix_len, _ = prefix_kv.shape
    moves, width = move_table.shape
    groups, line, pair = lax.axis_size("groups"), lax.axis_size("line"), lax.axis_size("pair")
    board_total = boards_here * line * pair
    capacity = max(2, (2 * row_count + board_total - 1) // board_total)
    heads = w_query.shape[1] // HD
    plan = Plan(groups, line, pair, heads, capacity, pair * boards_here)
    depth = w_query.shape[0]
    group_at = lax.axis_index("groups").astype(jnp.int32)
    line_at = lax.axis_index("line").astype(jnp.int32)
    pair_at = lax.axis_index("pair").astype(jnp.int32)
    slab_at = group_at * pair + pair_at
    ws = w_score.reshape(heads, HD)
    slab_axes = ("groups", "pair")
    board_row = move_board.reshape(1, row_count)

    half_cols = w_query.shape[1] // groups
    packed = scalar_call(
        functools.partial(pack_weights, plan),
        group_at.reshape(1),
        (w_query, w_keyval, ws, board_row, move_ids.reshape(1, row_count)),
        shape((plan.peers, plan.rows, depth), BF16),
        [
            pltpu.VMEM((depth, half_cols), BF16),
            pltpu.VMEM((depth, 2 * HD), BF16),
            pltpu.VMEM((plan.peers * plan.rows, half_cols + 2 * HD), F32),
            pltpu.SemaphoreType.DMA((2,)),
        ],
        cost(2 * plan.peers * plan.rows * half_cols * depth, 4 * w_query.size),
        {0: untouched(), 1: untouched()},
    )
    weights = lax.all_to_all(packed, ("line", "pair"), split_axis=0, concat_axis=0, tiled=True)

    payload = pl.pallas_call(
        pack_prefix,
        out_shape=shape((boards_here + 1, prefix_len, HD), BF16),
        in_specs=[pl.BlockSpec(memory_space=pltpu.VMEM), pl.BlockSpec(memory_space=pltpu.VMEM), untouched()],
        compiler_params=limits(32),
        cost_estimate=cost(2 * prefix_len * HD * HD * boards_here, 2 * prefix_kv.size),
    )(prefix_kv, ws, packed)
    beside = swap(payload, slab_axes, plan.slab, 1)
    across = swap(payload, slab_axes, plan.slab, 2)
    slot_row = scalar_call(
        functools.partial(find_slots, plan),
        (line_at * pair + pair_at).reshape(1),
        (board_row, packed),
        shape((1, row_count), jnp.int32),
        [],
        cost(4 * row_count * row_count, 4 * row_count),
        {1: untouched()},
    )

    block = min(moves, 128)
    normed = pl.pallas_call(
        normalize,
        out_shape=shape((moves, width), BF16),
        in_specs=[untouched(), pl.BlockSpec(memory_space=pltpu.VMEM), untouched()],
        out_specs=pl.BlockSpec(memory_space=pltpu.VMEM),
        scratch_shapes=[pltpu.VMEM((3, block, width), BF16), pltpu.SemaphoreType.DMA((3,))],
        compiler_params=limits(32),
        cost_estimate=cost(8 * moves * width, 2 * moves * width),
    )(move_table, norm_gain.reshape(1, width), packed)
    turns = jnp.asarray(turn_table(prefix_len))
    my_turns = jnp.tile(lax.dynamic_slice_in_dim(turns, line_at * plan.pairs, plan.pairs, axis=0), (plan.mine, 1))
    flat = weights.transpose(1, 0, 2).reshape(plan.rows, width) if depth % HD else weights
    queries, own_values = pl.pallas_call(
        functools.partial(project, plan),
        out_shape=(shape((line, plan.line_rows, moves), BF16), shape((plan.mine, moves), F32)),
        in_specs=[pl.BlockSpec(memory_space=pltpu.VMEM)] * 3 + [untouched()] * 3,
        compiler_params=limits(32),
        cost_estimate=cost(2 * moves * width * 256, 2 * moves * width),
    )(flat, normed, my_turns, beside, across, slot_row)
    queries = lax.all_to_all(queries, "line", split_axis=0, concat_axis=0, tiled=True)
    diagonal = swap(beside, slab_axes, plan.slab, 2)
    listed = pl.pallas_call(
        functools.partial(read_lists, plan),
        out_shape=shape((plan.share, plan.slots), F32),
        compiler_params=limits(32),
        cost_estimate=cost(10**7, 10**6),
    )(weights)
    listed = jnp.stack([listed, swap(listed, slab_axes, plan.slab, pair)]).astype(jnp.int32)

    query_rows = plan.mine * HD
    back = plan.peers * lax.axis_size("tensor")
    parts = scalar_call(
        functools.partial(attend, plan),
        slab_at.reshape(1),
        (
            queries.reshape(line * plan.line_rows, moves),
            jnp.asarray(entry_order(plan), BF16),
            own_values,
            payload,
            beside,
            across,
            diagonal,
            listed,
        ),
        shape((groups, back, plan.share, plan.slots), F32),
        [
            pltpu.VMEM((query_rows + 16, moves), BF16),
            pltpu.VMEM((16, moves), F32),
            pltpu.VMEM((plan.slab, boards_here, plan.slots), F32),
        ],
        cost(2 * 272 * moves * 4096, 4 * 10**6),
    )
    parts = lax.all_to_all(
        parts.reshape(groups * back, plan.share, plan.slots),
        ("groups", "line", "pair", "tensor"),
        split_axis=0,
        concat_axis=0,
        tiled=True,
    )
    parts = parts.reshape(groups, line, back // line, plan.share, plan.slots)
    logprob = pl.pallas_call(
        functools.partial(finish, plan), out_shape=shape((1, row_count), F32), compiler_params=limits(VMEM_MIB)
    )(parts, board_row, slot_row)
    return logprob.reshape(row_count)


def solution(mesh):
    order = ("groups", "dp", "tensor")
    assert mesh.axis_names == order
    pair = 2
    groups, peers, tensor = (mesh.shape[name] for name in order)
    fine = Mesh(mesh.devices.reshape(groups, peers // pair, pair, tensor), ("groups", "line", "pair", "tensor"))
    rows = ("groups", "line", "pair")
    placed = (
        P(rows, None, "tensor"),
        P(rows),
        P(rows, None),
        P(),
        P(),
        P(("line", "pair"), "tensor"),
        P(("line", "pair"), "tensor"),
        P("tensor"),
    )
    return jax.shard_map(per_device, mesh=fine, in_specs=placed, out_specs=P(rows), check_vma=False)
```

```python
import functools
import math

import jax
import jax.numpy as jnp
import numpy as np
from jax import lax
from jax.experimental import pallas as pl
from jax.experimental.pallas import tpu as pltpu
from jax.sharding import Mesh
from jax.sharding import PartitionSpec as P

HD = 128
HALF = HD // 2
EPS = 1e-06
THETA = 5000000.0
DEAD = -1e30
VMEM_MIB = 52

F32 = jnp.float32
BF16 = jnp.bfloat16

NN = (((1,), (0,)), ((), ()))
NT = (((1,), (1,)), ((), ()))
TN = (((0,), (0,)), ((), ()))


def matmul(a, b, dims=NN):
    return lax.dot_general(a, b, dims, preferred_element_type=F32)


def limits(mib):
    return pltpu.CompilerParams(vmem_limit_bytes=mib * 1024 * 1024)


class Plan:
    def __init__(self, groups, line, pair, heads, capacity, share):
        self.groups, self.line, self.pair = groups, line, pair
        self.peers = line * pair
        self.slab = groups * pair
        self.heads = heads
        self.mine = heads // self.slab
        self.pairs = HALF // line
        self.q_rows = self.mine * 2 * self.pairs
        self.k_rows = 2 * self.pairs
        self.fold_at = self.q_rows + self.k_rows
        self.list_at = self.fold_at + self.mine
        self.rows = -(-(self.list_at + 1) // 8) * 8
        self.line_rows = -(-(self.q_rows + 2 * self.mine) // 8) * 8
        self.capacity = capacity
        self.share = share
        self.slots = self.peers * capacity


def pack_weights(plan, at_ref, wq_hbm, wkv_hbm, ws_hbm, board_hbm, ids_hbm, out_ref, *scratch):
    wq, wkv, ws_ref, board_ref, ids_ref, pick, sems = scratch
    group = at_ref[0]
    rows, half_cols = plan.rows, wq.shape[1]
    columns_here = pl.ds(pl.multiple_of(group * half_cols, HD), half_cols)
    copies = (
        pltpu.make_async_copy(ws_hbm, ws_ref, sems.at[0]),
        pltpu.make_async_copy(board_hbm, board_ref, sems.at[1]),
        pltpu.make_async_copy(ids_hbm, ids_ref, sems.at[2]),
        pltpu.make_async_copy(wq_hbm.at[:, columns_here], wq, sems.at[3]),
        pltpu.make_async_copy(wkv_hbm, wkv, sems.at[4]),
    )
    for copy in copies:
        copy.start()
    for copy in copies[:3]:
        copy.wait()
    r = lax.broadcasted_iota(jnp.int32, (rows, 1), 0)
    part = r // (plan.mine * plan.pairs)
    head = (r // plan.pairs) % plan.mine
    entry = r % plan.pairs
    is_q = r < plan.q_rows
    k_at = r - plan.q_rows
    is_k = (k_at >= 0) & (k_at < plan.k_rows)
    f_at = r - plan.fold_at
    is_f = (f_at >= 0) & (f_at < plan.mine)
    q_lane = lax.broadcasted_iota(jnp.int32, (rows, half_cols), 1)
    k_lane = lax.broadcasted_iota(jnp.int32, (rows, HD), 1)
    ws = ws_ref[...].astype(F32)

    def fill(peer, carry):
        line, pair = peer // plan.pair, peer % plan.pair
        column = (pair * plan.mine + head) * HD + part * HALF + line * plan.pairs + entry
        column = jnp.where(is_q, column, -1)
        at = pl.ds(pl.multiple_of(peer * rows, 8), rows)
        pick[at, :half_cols] = jnp.where(q_lane == column, 1.0, 0.0)
        k_column = (k_at // plan.pairs) * HALF + line * plan.pairs + k_at % plan.pairs
        k_column = jnp.where(is_k, k_column, -1)
        pick[at, half_cols : half_cols + HD] = jnp.where(k_lane == k_column, 1.0, 0.0)
        fold = jnp.zeros((rows, HD), F32)
        my_head = jnp.where(is_f, (group * plan.pair + pair) * plan.mine + f_at, -1)
        for h in range(plan.heads):
            fold = jnp.where(my_head == h, ws[h : h + 1], fold)
        pick[at, half_cols + HD :] = fold
        return carry

    lax.fori_loop(0, plan.peers, fill, 0, unroll=plan.peers <= 8)

    count, depth = board_ref.shape[1], wq.shape[0]
    board_row = board_ref[...]
    board_col = jnp.broadcast_to(board_row.astype(F32), (8, count)).T[:, 0:1].astype(jnp.int32)
    own = lax.broadcasted_iota(jnp.int32, (count, count), 0)
    other = lax.broadcasted_iota(jnp.int32, (count, count), 1)
    ahead = jnp.where((board_col == board_row) & (other < own), 1.0, 0.0)
    rank = jnp.sum(ahead, axis=1, keepdims=True).astype(jnp.int32)
    key = board_col * plan.capacity + rank
    move = ids_ref[...] + 1
    parts = jnp.concatenate([(move // 64).astype(F32), (move % 64).astype(F32)], axis=0).astype(BF16)
    span = plan.share * plan.capacity
    lane = lax.broadcasted_iota(jnp.int32, (count, depth), 1)
    lane_row = lax.broadcasted_iota(jnp.int32, (1, depth), 1)
    lists = []
    for line in range(plan.line):
        place = jnp.where(lane < span, lane, lane - span) + line * span
        found = matmul(parts, jnp.where(key == place, 1.0, 0.0).astype(BF16))
        lists.append(jnp.where(lane_row < span, found[0:1], found[1:2]))

    for copy in copies[3:]:
        copy.wait()
    left = pick[...].astype(BF16)
    total = matmul(left[:, :half_cols], wq[...], NT) + matmul(left[:, half_cols:], wkv[...], NT)
    for peer in range(plan.peers):
        mine = total[peer * rows : (peer + 1) * rows]
        out_ref[peer] = jnp.where(r == plan.list_at, lists[peer // plan.pair], mine).astype(BF16)


def normalize(table_ref, gain_ref, after_ref, out_ref):
    raw = table_ref[...].astype(F32)
    inverse = lax.rsqrt(jnp.mean(raw * raw, axis=-1, keepdims=True) + EPS)
    out_ref[...] = (raw * inverse * gain_ref[...].astype(F32)).astype(BF16)


def project(plan, w_ref, normed_hbm, turn_ref, *rest):
    q_ref, vo_ref, buffers, total_ref, sems = rest[-5:]
    moves = normed_hbm.shape[0]
    held, _, depth = buffers.shape
    steps = normed_hbm.shape[1] // depth

    def copy(step):
        at = step % held
        return pltpu.make_async_copy(normed_hbm.at[:, step * depth : (step + 1) * depth], buffers.at[at], sems.at[at])

    for step in range(min(held, steps)):
        copy(step).start()
    for step in range(steps):
        copy(step).wait()
        w = w_ref[step] if len(w_ref.shape) == 3 else w_ref[:, step * depth : (step + 1) * depth]
        term = matmul(w, buffers[step % held], NT)
        total_ref[...] = term if step == 0 else total_ref[...] + term
        if step + held < steps:
            copy(step + held).start()

    half, k_half = plan.q_rows // 2, plan.k_rows // 2
    cosine, sine = turn_ref[:, 0:1], turn_ref[:, 1:2]
    cos_k, sin_k = cosine[:k_half], sine[:k_half]
    block = min(moves, 256)
    for start in range(0, moves, block):
        at = slice(start, start + block)
        total = total_ref[:, at]
        first, second = total[:half], total[half : 2 * half]
        f_first = (first * cosine - second * sine).astype(BF16).astype(F32)
        f_second = (second * cosine + first * sine).astype(BF16).astype(F32)
        first, second = total[plan.q_rows : plan.q_rows + k_half], total[plan.q_rows + k_half : plan.fold_at]
        k_first = (first * cos_k - second * sin_k).astype(BF16).astype(F32)
        k_second = (second * cos_k + first * sin_k).astype(BF16).astype(F32)
        logits, tails = [], []
        for h in range(plan.mine):
            own = slice(h * k_half, (h + 1) * k_half)
            logit = jnp.sum(f_first[own] * k_first + f_second[own] * k_second, axis=0, keepdims=True)
            logits.append(logit.astype(BF16).astype(F32))
            tails.append(logit - logits[-1])
        pad = plan.line_rows - plan.q_rows - 2 * plan.mine
        pieces = [f_first, f_second, *logits, *tails]
        if pad:
            pieces.append(jnp.zeros((pad, block), F32))
        out = jnp.concatenate(pieces, axis=0).astype(BF16)
        for copy_at in range(q_ref.shape[0]):
            q_ref[copy_at, :, at] = out
        vo_ref[:, at] = total[plan.fold_at : plan.list_at]


def pack_prefix(prefix_ref, ws_ref, after_ref, out_ref):
    boards = prefix_ref.shape[0]
    heads = ws_ref.shape[0]
    span = HD // boards
    ws = jnp.concatenate([ws_ref[...].astype(F32)] * (HD // heads), axis=0)
    row = lax.broadcasted_iota(jnp.int32, (HD, 1), 0)
    fold = None
    for board in range(boards):
        out_ref[board] = prefix_ref[board, :, :HD]
        keep = (row // span == board) & (row % span < 2 * heads)
        term = matmul(prefix_ref[board, :, HD:], jnp.where(keep, ws, 0.0).astype(BF16), NT)
        fold = term if fold is None else fold + term
    rounded = fold.astype(BF16).astype(F32)
    lane = lax.broadcasted_iota(jnp.int32, fold.shape, 1)
    out_ref[boards] = jnp.where(lane % span < heads, rounded, fold - rounded).astype(BF16)


def find_slots(plan, at_ref, board_ref, after_ref, slot_ref):
    count = board_ref.shape[1]
    board_row = board_ref[...]
    board_col = jnp.broadcast_to(board_row.astype(F32), (8, count)).T[:, 0:1].astype(jnp.int32)
    other = lax.broadcasted_iota(jnp.int32, (count, count), 0)
    own = lax.broadcasted_iota(jnp.int32, (count, count), 1)
    rank = jnp.sum(jnp.where((board_col == board_row) & (other < own), 1.0, 0.0), axis=0, keepdims=True)
    slot_ref[...] = rank.astype(jnp.int32) + at_ref[0] * plan.capacity


def read_lists(plan, w_ref, out_ref):
    share, capacity, peers = plan.share, plan.capacity, plan.peers
    span = share * capacity
    rows = jnp.concatenate([w_ref[s].astype(F32)[plan.list_at : plan.list_at + 1] for s in range(peers)], axis=0)
    lane = lax.broadcasted_iota(jnp.int32, (share * peers, 2 * span), 1)
    row = lax.broadcasted_iota(jnp.int32, (share * peers, 2 * span), 0)
    lane = jnp.where(lane < span, lane, lane - span)
    spread = jnp.concatenate([rows] * share, axis=0)
    spread = jnp.where(lane // capacity == row // peers, spread, 0.0).astype(BF16)
    c = lax.broadcasted_iota(jnp.int32, (2 * span, plan.slots), 0)
    slot = lax.broadcasted_iota(jnp.int32, (2 * span, plan.slots), 1)
    scale = jnp.where(c < span, 64.0, 1.0)
    place = jnp.where(c % capacity == slot % capacity, scale, 0.0).astype(BF16)
    listed = matmul(spread, place)
    row = lax.broadcasted_iota(jnp.int32, listed.shape, 0)
    slot = lax.broadcasted_iota(jnp.int32, listed.shape, 1)
    listed = jnp.where(slot // capacity == row % peers, listed, 0.0)
    out_ref[...] = jnp.sum(listed.reshape(share, peers, plan.slots), axis=1)


def attend(plan, at_ref, q_ref, order_ref, vo_ref, *rest):
    prefix_refs = rest[: plan.slab]
    moves_ref, out_ref, table, extra, scores, taken_even, taken_odd = rest[plan.slab :]
    here = at_ref[0]
    mine, heads, slots = plan.mine, plan.heads, plan.slots
    moves = q_ref.shape[1]
    boards = prefix_refs[0].shape[0] - 1
    query_rows = mine * HD

    mixed = matmul(order_ref[...], q_ref[...])
    table[:query_rows] = mixed[:query_rows].astype(BF16)
    extra[...] = jnp.zeros_like(extra)
    for place, value in ((0, mixed[query_rows : query_rows + mine]), (2 * mine, vo_ref[...])):
        rounded = value.astype(BF16).astype(F32)
        extra[place : place + mine] = rounded
        extra[place + mine : place + 2 * mine] = value - rounded
    table[query_rows:] = extra[...].astype(BF16)

    scale = math.log2(math.e) / math.sqrt(HD)
    move_at = lax.broadcasted_iota(jnp.int32, (moves, slots), 0) + 1
    lanes = mine * slots
    span = HD // boards
    fold_row = lax.broadcasted_iota(jnp.int32, (HD, lanes), 0)
    fold_head = here * mine + lax.broadcasted_iota(jnp.int32, (HD, lanes), 1) // slots

    def per_head(x, base):
        pieces = [x[base + h : base + h + 1] + x[base + mine + h : base + mine + h + 1] for h in range(mine)]
        return jnp.concatenate(pieces, axis=1)

    def moves_of(j, board):
        place = ((here ^ j) % plan.pair) * boards + board
        return moves_ref[j // plan.pair, pl.ds(place, 1), :]

    def gather(board, taken):
        chosen = [
            jnp.where(move_at == moves_of(j, board), 1.0, 0.0).astype(BF16) for j in range(plan.slab)
        ]
        taken[...] = matmul(table[...], jnp.concatenate(chosen, axis=1))

    def score_board(board, taken):
        at = fold_row - board * span
        fold_pick = jnp.where((at == fold_head) | (at == fold_head + heads), 1.0, 0.0).astype(BF16)
        for j in range(plan.slab):
            x = taken[:, j * slots : (j + 1) * slots]
            q = jnp.concatenate([x[h * HD : (h + 1) * HD].astype(BF16) for h in range(mine)], axis=1)
            logits = matmul(prefix_refs[j][board], q)
            fold = matmul(prefix_refs[j][boards], fold_pick)
            own_logit = per_head(x, query_rows)
            own_value = per_head(x, query_rows + 2 * mine)
            peak = jnp.maximum(jnp.max(logits, axis=0, keepdims=True), own_logit)
            weight = jnp.exp2((logits - peak) * scale)
            own_weight = jnp.exp2((own_logit - peak) * scale)
            denom = jnp.sum(weight, axis=0, keepdims=True) + own_weight
            value = (jnp.sum(weight * fold, axis=0, keepdims=True) + own_value * own_weight) / denom
            score = sum(value[:, h * slots : (h + 1) * slots] for h in range(mine))
            scores[here ^ j, pl.ds(board, 1), :] = jnp.where(moves_of(j, board) > 0, score, DEAD)

    gather(0, taken_even)

    def step(at, carry):
        board = 2 * at
        gather(jnp.minimum(board + 1, boards - 1), taken_odd)
        score_board(board, taken_even)
        gather(jnp.minimum(board + 2, boards - 1), taken_even)
        score_board(jnp.minimum(board + 1, boards - 1), taken_odd)
        return carry

    lax.fori_loop(0, -(-boards // 2), step, 0)
    for g in range(plan.groups):
        both = jnp.concatenate([scores[g * plan.pair + p] for p in range(plan.pair)], axis=0)
        for copy in range(out_ref.shape[1]):
            out_ref[g, copy] = both


def finish(plan, parts_ref, board_ref, slot_ref, out_ref):
    line = parts_ref.shape[1]
    columns = []
    for at in range(line):
        total = None
        for g in range(parts_ref.shape[0]):
            for p in range(parts_ref.shape[2]):
                term = parts_ref[g, at, p]
                total = term if total is None else total + term
        columns.append(total)
    scores = jnp.concatenate(columns, axis=0)
    live = scores > 0.5 * DEAD
    peak = jnp.max(scores, axis=1, keepdims=True)
    denom = jnp.sum(jnp.where(live, jnp.exp(scores - peak), 0.0), axis=1, keepdims=True)
    logprob = jnp.where(live, scores - peak - jnp.log(denom), 0.0)
    count = board_ref.shape[1]
    member = lax.broadcasted_iota(jnp.int32, (scores.shape[0], count), 0) == board_ref[...]
    member = jnp.where(member, 1.0, 0.0).astype(BF16)
    found = jnp.zeros((plan.slots, count), F32)
    for _ in range(3):
        rounded = logprob.astype(BF16)
        found = found + matmul(rounded, member, TN)
        logprob = logprob - rounded.astype(F32)
    at = lax.broadcasted_iota(jnp.int32, (plan.slots, count), 0) == slot_ref[...]
    out_ref[...] = jnp.sum(jnp.where(at, found, 0.0), axis=0, keepdims=True)


def untouched():
    return pl.BlockSpec(memory_space=pl.ANY)


def scalar_call(kernel, at, args, outs, scratch, cost=None, specs=None, mib=VMEM_MIB):
    whole = lambda x: pl.BlockSpec(x.shape, lambda i, at, n=len(x.shape): (0,) * n)
    specs = specs or {}
    return pl.pallas_call(
        kernel,
        out_shape=outs,
        grid_spec=pltpu.PrefetchScalarGridSpec(
            num_scalar_prefetch=1,
            grid=(1,),
            in_specs=[specs.get(i, whole(x)) for i, x in enumerate(args)],
            out_specs=jax.tree.map(whole, outs),
            scratch_shapes=scratch,
        ),
        compiler_params=limits(mib),
        cost_estimate=cost,
    )(at, *args)


def cost(flops, nbytes):
    return pl.CostEstimate(flops=int(flops), bytes_accessed=int(nbytes), transcendentals=0)


def swap(x, names, size, step):
    return lax.ppermute(x, names, [(at, at ^ step) for at in range(size)])


def shape(dims, dtype):
    return jax.ShapeDtypeStruct(tuple(dims), dtype)


def turn_table(position):
    frequency = THETA ** (-2.0 * np.arange(HALF, dtype=np.float32) / HD)
    angles = np.float32(position) * frequency.astype(np.float32)
    return np.stack([np.cos(angles), np.sin(angles)], axis=1).astype(np.float32)


def entry_order(plan):
    order = np.zeros((plan.mine * HD + 16, plan.line * plan.line_rows), np.float32)
    for head in range(plan.mine):
        for part in range(2):
            for entry in range(HALF):
                line, at = divmod(entry, plan.pairs)
                source = line * plan.line_rows + (part * plan.mine + head) * plan.pairs + at
                order[head * HD + part * HALF + entry, source] = 1.0
        for line in range(plan.line):
            for piece in range(2):
                order[plan.mine * HD + head, line * plan.line_rows + plan.q_rows + piece * plan.mine + head] = 1.0
    return order


def per_device(prefix_kv, move_ids, move_board, move_table, norm_gain, w_query, w_keyval, w_score):
    row_count = move_ids.shape[0]
    boards_here, prefix_len, _ = prefix_kv.shape
    moves, width = move_table.shape
    groups, line, pair = lax.axis_size("groups"), lax.axis_size("line"), lax.axis_size("pair")
    board_total = boards_here * line * pair
    capacity = max(2, (2 * row_count + board_total - 1) // board_total)
    heads = w_query.shape[1] // HD
    plan = Plan(groups, line, pair, heads, capacity, pair * boards_here)
    depth = w_query.shape[0]
    group_at = lax.axis_index("groups").astype(jnp.int32)
    line_at = lax.axis_index("line").astype(jnp.int32)
    pair_at = lax.axis_index("pair").astype(jnp.int32)
    slab_at = group_at * pair + pair_at
    ws = w_score.reshape(heads, HD)
    slab_axes = ("groups", "pair")
    board_row = move_board.reshape(1, row_count)

    half_cols = w_query.shape[1] // groups
    packed = scalar_call(
        functools.partial(pack_weights, plan),
        group_at.reshape(1),
        (w_query, w_keyval, ws, board_row, move_ids.reshape(1, row_count)),
        shape((plan.peers, plan.rows, depth), BF16),
        [
            pltpu.VMEM((depth, half_cols), BF16),
            pltpu.VMEM((depth, 2 * HD), BF16),
            pltpu.VMEM((heads, HD), BF16),
            pltpu.VMEM((1, row_count), jnp.int32),
            pltpu.VMEM((1, row_count), jnp.int32),
            pltpu.VMEM((plan.peers * plan.rows, half_cols + 2 * HD), F32),
            pltpu.SemaphoreType.DMA((5,)),
        ],
        cost(2 * plan.peers * plan.rows * half_cols * depth, 4 * w_query.size),
        {at: untouched() for at in range(5)},
        62,
    )
    weights = lax.all_to_all(packed, ("line", "pair"), split_axis=0, concat_axis=0, tiled=True)

    payload = pl.pallas_call(
        pack_prefix,
        out_shape=shape((boards_here + 1, prefix_len, HD), BF16),
        in_specs=[pl.BlockSpec(memory_space=pltpu.VMEM), pl.BlockSpec(memory_space=pltpu.VMEM), untouched()],
        compiler_params=limits(32),
        cost_estimate=cost(2 * prefix_len * HD * HD * boards_here, 2 * prefix_kv.size),
    )(prefix_kv, ws, packed)
    beside = swap(payload, slab_axes, plan.slab, 1)
    across = swap(payload, slab_axes, plan.slab, 2)
    slot_row = scalar_call(
        functools.partial(find_slots, plan),
        (line_at * pair + pair_at).reshape(1),
        (board_row, packed),
        shape((1, row_count), jnp.int32),
        [],
        cost(4 * row_count * row_count, 4 * row_count),
        {1: untouched()},
    )

    block = min(moves, 128)
    normed = pl.pallas_call(
        normalize,
        out_shape=shape((moves, width), BF16),
        grid=(moves // block,),
        in_specs=[
            pl.BlockSpec((block, width), lambda i: (i, 0)),
            pl.BlockSpec((1, width), lambda i: (0, 0)),
            untouched(),
        ],
        out_specs=pl.BlockSpec((block, width), lambda i: (i, 0)),
        compiler_params=limits(57),
        cost_estimate=cost(8 * moves * width, 4 * moves * width),
    )(move_table, norm_gain.reshape(1, width), packed)
    turns = jnp.asarray(turn_table(prefix_len))
    my_turns = jnp.tile(lax.dynamic_slice_in_dim(turns, line_at * plan.pairs, plan.pairs, axis=0), (plan.mine, 1))
    flat = weights.transpose(1, 0, 2).reshape(plan.rows, width) if depth % HD else weights
    chunk = width // 8 if depth % HD else depth
    queries, own_values = pl.pallas_call(
        functools.partial(project, plan),
        out_shape=(shape((line, plan.line_rows, moves), BF16), shape((plan.mine, moves), F32)),
        in_specs=[
            pl.BlockSpec(memory_space=pltpu.VMEM),
            untouched(),
            pl.BlockSpec(memory_space=pltpu.VMEM),
            untouched(),
            untouched(),
            untouched(),
        ],
        scratch_shapes=[
            pltpu.VMEM((4, moves, chunk), BF16),
            pltpu.VMEM((plan.rows, moves), F32),
            pltpu.SemaphoreType.DMA((4,)),
        ],
        compiler_params=limits(57),
        cost_estimate=cost(2 * moves * width * 256, 2 * moves * width),
    )(flat, normed, my_turns, beside, across, slot_row)
    queries = lax.all_to_all(queries, "line", split_axis=0, concat_axis=0, tiled=True)
    diagonal = swap(beside, slab_axes, plan.slab, 2)
    listed = pl.pallas_call(
        functools.partial(read_lists, plan),
        out_shape=shape((plan.share, plan.slots), F32),
        compiler_params=limits(32),
        cost_estimate=cost(10**7, 10**6),
    )(weights)
    listed = jnp.stack([listed, swap(listed, slab_axes, plan.slab, pair)]).astype(jnp.int32)

    query_rows = plan.mine * HD
    back = plan.peers * lax.axis_size("tensor")
    parts = scalar_call(
        functools.partial(attend, plan),
        slab_at.reshape(1),
        (
            queries.reshape(line * plan.line_rows, moves),
            jnp.asarray(entry_order(plan), BF16),
            own_values,
            payload,
            beside,
            across,
            diagonal,
            listed,
        ),
        shape((groups, back, plan.share, plan.slots), F32),
        [
            pltpu.VMEM((query_rows + 16, moves), BF16),
            pltpu.VMEM((16, moves), F32),
            pltpu.VMEM((plan.slab, boards_here, plan.slots), F32),
            pltpu.VMEM((query_rows + 16, plan.slab * plan.slots), F32),
            pltpu.VMEM((query_rows + 16, plan.slab * plan.slots), F32),
        ],
        cost(2 * 272 * moves * 4096, 4 * 10**6),
    )
    parts = lax.all_to_all(
        parts.reshape(groups * back, plan.share, plan.slots),
        ("groups", "line", "pair", "tensor"),
        split_axis=0,
        concat_axis=0,
        tiled=True,
    )
    parts = parts.reshape(groups, line, back // line, plan.share, plan.slots)
    logprob = pl.pallas_call(
        functools.partial(finish, plan), out_shape=shape((1, row_count), F32), compiler_params=limits(VMEM_MIB)
    )(parts, board_row, slot_row)
    return logprob.reshape(row_count)


def solution(mesh):
    order = ("groups", "dp", "tensor")
    assert mesh.axis_names == order
    pair = 2
    groups, peers, tensor = (mesh.shape[name] for name in order)
    fine = Mesh(mesh.devices.reshape(groups, peers // pair, pair, tensor), ("groups", "line", "pair", "tensor"))
    rows = ("groups", "line", "pair")
    placed = (
        P(rows, None, "tensor"),
        P(rows),
        P(rows, None),
        P(),
        P(),
        P(("line", "pair"), "tensor"),
        P(("line", "pair"), "tensor"),
        P("tensor"),
    )
    return jax.shard_map(per_device, mesh=fine, in_specs=placed, out_specs=P(rows), check_vma=False)
```

```python
import functools
import math

import jax
import jax.numpy as jnp
import numpy as np
from jax import lax
from jax.experimental import pallas as pl
from jax.experimental.pallas import tpu as pltpu
from jax.sharding import Mesh
from jax.sharding import PartitionSpec as P

HD = 128
HALF = HD // 2
EPS = 1e-06
THETA = 5000000.0
DEAD = -1e30
VMEM_MIB = 52

F32 = jnp.float32
BF16 = jnp.bfloat16

NN = (((1,), (0,)), ((), ()))
NT = (((1,), (1,)), ((), ()))
TN = (((0,), (0,)), ((), ()))


def matmul(a, b, dims=NN):
    return lax.dot_general(a, b, dims, preferred_element_type=F32)


def limits(mib):
    return pltpu.CompilerParams(vmem_limit_bytes=mib * 1024 * 1024)


class Plan:
    def __init__(self, groups, line, pair, heads, capacity, share):
        self.groups, self.line, self.pair = groups, line, pair
        self.peers = line * pair
        self.slab = groups * pair
        self.heads = heads
        self.mine = heads // self.slab
        self.pairs = HALF // line
        self.q_rows = self.mine * 2 * self.pairs
        self.k_rows = 2 * self.pairs
        self.fold_at = self.q_rows + self.k_rows
        self.list_at = self.fold_at + self.mine
        self.rows = -(-(self.list_at + 1) // 8) * 8
        self.line_rows = -(-(self.q_rows + 2 * self.mine) // 8) * 8
        self.capacity = capacity
        self.share = share
        self.slots = self.peers * capacity


def pack_weights(plan, at_ref, wq_hbm, wkv_hbm, ws_hbm, board_hbm, ids_hbm, gain_hbm, out_ref, *scratch):
    wq, wkv, ws_ref, board_ref, ids_ref, gain_ref, pick, sems = scratch
    group, peer_at = at_ref[0], at_ref[1]
    rows, half_cols = plan.rows, wq.shape[1]
    columns_here = pl.ds(pl.multiple_of(group * half_cols, HD), half_cols)
    copies = (
        pltpu.make_async_copy(ws_hbm, ws_ref, sems.at[0]),
        pltpu.make_async_copy(board_hbm, board_ref, sems.at[1]),
        pltpu.make_async_copy(ids_hbm, ids_ref, sems.at[2]),
        pltpu.make_async_copy(gain_hbm, gain_ref, sems.at[3]),
        pltpu.make_async_copy(wq_hbm.at[:, columns_here], wq, sems.at[4]),
        pltpu.make_async_copy(wkv_hbm, wkv, sems.at[5]),
    )
    for copy in copies:
        copy.start()
    for copy in copies[:4]:
        copy.wait()
    r = lax.broadcasted_iota(jnp.int32, (rows, 1), 0)
    part = r // (plan.mine * plan.pairs)
    head = (r // plan.pairs) % plan.mine
    entry = r % plan.pairs
    is_q = r < plan.q_rows
    k_at = r - plan.q_rows
    is_k = (k_at >= 0) & (k_at < plan.k_rows)
    f_at = r - plan.fold_at
    is_f = (f_at >= 0) & (f_at < plan.mine)
    q_lane = lax.broadcasted_iota(jnp.int32, (rows, half_cols), 1)
    k_lane = lax.broadcasted_iota(jnp.int32, (rows, HD), 1)
    ws = ws_ref[...].astype(F32)

    def fill(peer, carry):
        line, pair = peer // plan.pair, peer % plan.pair
        column = (pair * plan.mine + head) * HD + part * HALF + line * plan.pairs + entry
        column = jnp.where(is_q, column, -1)
        at = pl.ds(pl.multiple_of(peer * rows, 8), rows)
        pick[at, :half_cols] = jnp.where(q_lane == column, 1.0, 0.0)
        k_column = (k_at // plan.pairs) * HALF + line * plan.pairs + k_at % plan.pairs
        k_column = jnp.where(is_k, k_column, -1)
        pick[at, half_cols : half_cols + HD] = jnp.where(k_lane == k_column, 1.0, 0.0)
        fold = jnp.zeros((rows, HD), F32)
        my_head = jnp.where(is_f, (group * plan.pair + pair) * plan.mine + f_at, -1)
        for h in range(plan.heads):
            fold = jnp.where(my_head == h, ws[h : h + 1], fold)
        pick[at, half_cols + HD :] = fold
        return carry

    lax.fori_loop(0, plan.peers, fill, 0, unroll=plan.peers <= 8)

    count, depth = board_ref.shape[1], wq.shape[0]
    board_row = board_ref[...]
    board_col = jnp.broadcast_to(board_row.astype(F32), (8, count)).T[:, 0:1].astype(jnp.int32)
    own = lax.broadcasted_iota(jnp.int32, (count, count), 0)
    other = lax.broadcasted_iota(jnp.int32, (count, count), 1)
    ahead = jnp.where((board_col == board_row) & (other < own), 1.0, 0.0)
    rank = jnp.sum(ahead, axis=1, keepdims=True).astype(jnp.int32)
    key = board_col * plan.capacity + rank
    move = ids_ref[...] + 1
    parts = jnp.concatenate([(move // 64).astype(F32), (move % 64).astype(F32)], axis=0).astype(BF16)
    span = plan.share * plan.capacity
    lane = lax.broadcasted_iota(jnp.int32, (count, depth), 1)
    lane_row = lax.broadcasted_iota(jnp.int32, (1, depth), 1)
    lists = []
    for line in range(plan.line):
        place = jnp.where(lane < span, lane, lane - span) + line * span
        found = matmul(parts, jnp.where(key == place, 1.0, 0.0).astype(BF16))
        lists.append(jnp.where(lane_row < span, found[0:1], found[1:2]))

    count, depth = wq.shape
    gain = gain_ref[...].astype(F32)
    gain_row = lax.broadcasted_iota(jnp.int32, gain.shape, 0)
    first = peer_at * (count // gain.shape[1]) if gain.shape[0] > 1 else 0
    pieces = max(1, count // gain.shape[1])
    gain = [jnp.sum(jnp.where(gain_row == first + p, gain, 0.0), axis=0, keepdims=True) for p in range(pieces)]
    gain = jnp.concatenate(gain, axis=1)

    for copy in copies[4:]:
        copy.wait()
    left = pick[...].astype(BF16)
    total = matmul(left[:, :half_cols], wq[...], NT) + matmul(left[:, half_cols:], wkv[...], NT)
    for peer in range(plan.peers):
        mine = total[peer * rows : (peer + 1) * rows] * gain
        out_ref[peer] = jnp.where(r == plan.list_at, lists[peer // plan.pair], mine).astype(BF16)


def inverse_norms(table_ref, after_ref, out_ref):
    raw = table_ref[...].astype(F32)
    count = raw.shape[0]
    inverse = lax.rsqrt(jnp.mean(raw * raw, axis=-1, keepdims=True) + EPS)
    out_ref[...] = jnp.broadcast_to(inverse, (count, count)).T[0:1]


def project(plan, at_ref, w_ref, table_hbm, inverse_ref, turn_ref, *rest):
    q_ref, vo_ref, table, sems = rest[-4:]
    moves, width = table_hbm.shape
    block = moves // sems.shape[0]

    def copy(step):
        at = pl.ds(step * block, block)
        return pltpu.make_async_copy(table_hbm.at[at], table.at[at], sems.at[step])

    for step in range(sems.shape[0]):
        copy(step).start()

    half, k_half = plan.q_rows // 2, plan.k_rows // 2
    turns = turn_ref[at_ref[0]]
    cosine, sine = turns[:, 0:1], turns[:, 1:2]
    cos_k, sin_k = cosine[:k_half], sine[:k_half]
    for step in range(sems.shape[0]):
        copy(step).wait()
        at = slice(step * block, (step + 1) * block)
        if len(w_ref.shape) == 3:
            depth = w_ref.shape[2]
            total = None
            for s in range(w_ref.shape[0]):
                term = matmul(w_ref[s], table[at, s * depth : (s + 1) * depth], NT)
                total = term if total is None else total + term
        else:
            total = matmul(w_ref[...], table[at, :], NT)
        total = total * inverse_ref[:, at]
        first, second = total[:half], total[half : 2 * half]
        f_first = (first * cosine - second * sine).astype(BF16).astype(F32)
        f_second = (second * cosine + first * sine).astype(BF16).astype(F32)
        first, second = total[plan.q_rows : plan.q_rows + k_half], total[plan.q_rows + k_half : plan.fold_at]
        k_first = (first * cos_k - second * sin_k).astype(BF16).astype(F32)
        k_second = (second * cos_k + first * sin_k).astype(BF16).astype(F32)
        logits, tails = [], []
        for h in range(plan.mine):
            own = slice(h * k_half, (h + 1) * k_half)
            logit = jnp.sum(f_first[own] * k_first + f_second[own] * k_second, axis=0, keepdims=True)
            logits.append(logit.astype(BF16).astype(F32))
            tails.append(logit - logits[-1])
        pad = plan.line_rows - plan.q_rows - 2 * plan.mine
        pieces = [f_first, f_second, *logits, *tails]
        if pad:
            pieces.append(jnp.zeros((pad, block), F32))
        out = jnp.concatenate(pieces, axis=0).astype(BF16)
        for copy_at in range(q_ref.shape[0]):
            q_ref[copy_at, :, at] = out
        vo_ref[:, at] = total[plan.fold_at : plan.list_at]


def pack_prefix(plan, at_ref, prefix_hbm, ws_hbm, board_hbm, after_ref, out_ref, slot_ref, *scratch):
    values, ws_ref, board_ref, sems = scratch
    boards = values.shape[0]
    heads = plan.heads
    copies = (
        pltpu.make_async_copy(board_hbm, board_ref, sems.at[0]),
        pltpu.make_async_copy(ws_hbm, ws_ref, sems.at[1]),
        pltpu.make_async_copy(prefix_hbm.at[:, :, pl.ds(HD, HD)], values, sems.at[2]),
        pltpu.make_async_copy(prefix_hbm.at[:, :, pl.ds(0, HD)], out_ref.at[pl.ds(0, boards)], sems.at[3]),
    )
    for copy in copies:
        copy.start()
    copies[0].wait()
    count = board_ref.shape[1]
    board_row = board_ref[...]
    board_col = jnp.broadcast_to(board_row.astype(F32), (8, count)).T[:, 0:1].astype(jnp.int32)
    other = lax.broadcasted_iota(jnp.int32, (count, count), 0)
    own = lax.broadcasted_iota(jnp.int32, (count, count), 1)
    rank = jnp.sum(jnp.where((board_col == board_row) & (other < own), 1.0, 0.0), axis=0, keepdims=True)
    slot_ref[...] = rank.astype(jnp.int32) + at_ref[0] * plan.capacity

    copies[1].wait()
    span = HD // boards
    ws = jnp.concatenate([ws_ref[...].astype(F32)] * (HD // heads), axis=0)
    row = lax.broadcasted_iota(jnp.int32, (HD, 1), 0)
    copies[2].wait()
    fold = None
    for board in range(boards):
        keep = (row // span == board) & (row % span < 2 * heads)
        term = matmul(values[board], jnp.where(keep, ws, 0.0).astype(BF16), NT)
        fold = term if fold is None else fold + term
    rounded = fold.astype(BF16).astype(F32)
    lane = lax.broadcasted_iota(jnp.int32, fold.shape, 1)
    out_ref[boards] = jnp.where(lane % span < heads, rounded, fold - rounded).astype(BF16)
    copies[3].wait()


def read_lists(plan, w_ref, out_ref):
    share, capacity, peers = plan.share, plan.capacity, plan.peers
    span = share * capacity
    rows = jnp.concatenate([w_ref[s].astype(F32)[plan.list_at : plan.list_at + 1] for s in range(peers)], axis=0)
    lane = lax.broadcasted_iota(jnp.int32, (share * peers, 2 * span), 1)
    row = lax.broadcasted_iota(jnp.int32, (share * peers, 2 * span), 0)
    lane = jnp.where(lane < span, lane, lane - span)
    spread = jnp.concatenate([rows] * share, axis=0)
    spread = jnp.where(lane // capacity == row // peers, spread, 0.0).astype(BF16)
    c = lax.broadcasted_iota(jnp.int32, (2 * span, plan.slots), 0)
    slot = lax.broadcasted_iota(jnp.int32, (2 * span, plan.slots), 1)
    scale = jnp.where(c < span, 64.0, 1.0)
    place = jnp.where(c % capacity == slot % capacity, scale, 0.0).astype(BF16)
    listed = matmul(spread, place)
    row = lax.broadcasted_iota(jnp.int32, listed.shape, 0)
    slot = lax.broadcasted_iota(jnp.int32, listed.shape, 1)
    listed = jnp.where(slot // capacity == row % peers, listed, 0.0)
    out_ref[...] = jnp.sum(listed.reshape(share, peers, plan.slots), axis=1)


def attend(plan, at_ref, q_ref, order_ref, vo_ref, *rest):
    prefix_refs = rest[: plan.slab]
    moves_ref, out_ref, table, extra, scores, taken_even, taken_odd = rest[plan.slab :]
    here = at_ref[0]
    mine, heads, slots = plan.mine, plan.heads, plan.slots
    moves = q_ref.shape[1]
    boards = prefix_refs[0].shape[0] - 1
    query_rows = mine * HD

    mixed = matmul(order_ref[...], q_ref[...])
    table[:query_rows] = mixed[:query_rows].astype(BF16)
    extra[...] = jnp.zeros_like(extra)
    for place, value in ((0, mixed[query_rows : query_rows + mine]), (2 * mine, vo_ref[...])):
        rounded = value.astype(BF16).astype(F32)
        extra[place : place + mine] = rounded
        extra[place + mine : place + 2 * mine] = value - rounded
    table[query_rows:] = extra[...].astype(BF16)

    scale = math.log2(math.e) / math.sqrt(HD)
    move_at = lax.broadcasted_iota(jnp.int32, (moves, slots), 0) + 1
    lanes = mine * slots
    span = HD // boards
    fold_row = lax.broadcasted_iota(jnp.int32, (HD, lanes), 0)
    fold_head = here * mine + lax.broadcasted_iota(jnp.int32, (HD, lanes), 1) // slots

    def per_head(x, base):
        pieces = [x[base + h : base + h + 1] + x[base + mine + h : base + mine + h + 1] for h in range(mine)]
        return jnp.concatenate(pieces, axis=1)

    def moves_of(j, board):
        place = ((here ^ j) % plan.pair) * boards + board
        return moves_ref[j // plan.pair, pl.ds(place, 1), :]

    def gather(board, taken):
        chosen = [
            jnp.where(move_at == moves_of(j, board), 1.0, 0.0).astype(BF16) for j in range(plan.slab)
        ]
        taken[...] = matmul(table[...], jnp.concatenate(chosen, axis=1))

    def score_board(board, taken):
        at = fold_row - board * span
        fold_pick = jnp.where((at == fold_head) | (at == fold_head + heads), 1.0, 0.0).astype(BF16)
        for j in range(plan.slab):
            x = taken[:, j * slots : (j + 1) * slots]
            q = jnp.concatenate([x[h * HD : (h + 1) * HD].astype(BF16) for h in range(mine)], axis=1)
            logits = matmul(prefix_refs[j][board], q)
            fold = matmul(prefix_refs[j][boards], fold_pick)
            own_logit = per_head(x, query_rows)
            own_value = per_head(x, query_rows + 2 * mine)
            peak = jnp.maximum(jnp.max(logits, axis=0, keepdims=True), own_logit)
            weight = jnp.exp2((logits - peak) * scale)
            own_weight = jnp.exp2((own_logit - peak) * scale)
            denom = jnp.sum(weight, axis=0, keepdims=True) + own_weight
            value = (jnp.sum(weight * fold, axis=0, keepdims=True) + own_value * own_weight) / denom
            score = sum(value[:, h * slots : (h + 1) * slots] for h in range(mine))
            scores[here ^ j, pl.ds(board, 1), :] = jnp.where(moves_of(j, board) > 0, score, DEAD)

    gather(0, taken_even)

    def step(at, carry):
        board = 2 * at
        gather(jnp.minimum(board + 1, boards - 1), taken_odd)
        score_board(board, taken_even)
        gather(jnp.minimum(board + 2, boards - 1), taken_even)
        score_board(jnp.minimum(board + 1, boards - 1), taken_odd)
        return carry

    lax.fori_loop(0, -(-boards // 2), step, 0)
    for g in range(plan.groups):
        both = jnp.concatenate([scores[g * plan.pair + p] for p in range(plan.pair)], axis=0)
        for copy in range(out_ref.shape[1]):
            out_ref[g, copy] = both


def finish(plan, parts_ref, board_ref, slot_ref, out_ref):
    line = parts_ref.shape[1]
    columns = []
    for at in range(line):
        total = None
        for g in range(parts_ref.shape[0]):
            for p in range(parts_ref.shape[2]):
                term = parts_ref[g, at, p]
                total = term if total is None else total + term
        columns.append(total)
    scores = jnp.concatenate(columns, axis=0)
    live = scores > 0.5 * DEAD
    peak = jnp.max(scores, axis=1, keepdims=True)
    denom = jnp.sum(jnp.where(live, jnp.exp(scores - peak), 0.0), axis=1, keepdims=True)
    logprob = jnp.where(live, scores - peak - jnp.log(denom), 0.0)
    count = board_ref.shape[1]
    member = lax.broadcasted_iota(jnp.int32, (scores.shape[0], count), 0) == board_ref[...]
    member = jnp.where(member, 1.0, 0.0).astype(BF16)
    found = jnp.zeros((plan.slots, count), F32)
    for _ in range(3):
        rounded = logprob.astype(BF16)
        found = found + matmul(rounded, member, TN)
        logprob = logprob - rounded.astype(F32)
    at = lax.broadcasted_iota(jnp.int32, (plan.slots, count), 0) == slot_ref[...]
    out_ref[...] = jnp.sum(jnp.where(at, found, 0.0), axis=0, keepdims=True)


def untouched():
    return pl.BlockSpec(memory_space=pl.ANY)


def scalar_call(kernel, at, args, outs, scratch, cost=None, specs=None, mib=VMEM_MIB):
    whole = lambda x: pl.BlockSpec(x.shape, lambda i, at, n=len(x.shape): (0,) * n)
    specs = specs or {}
    return pl.pallas_call(
        kernel,
        out_shape=outs,
        grid_spec=pltpu.PrefetchScalarGridSpec(
            num_scalar_prefetch=1,
            grid=(1,),
            in_specs=[specs.get(i, whole(x)) for i, x in enumerate(args)],
            out_specs=jax.tree.map(whole, outs),
            scratch_shapes=scratch,
        ),
        compiler_params=limits(mib),
        cost_estimate=cost,
    )(at, *args)


def cost(flops, nbytes):
    return pl.CostEstimate(flops=int(flops), bytes_accessed=int(nbytes), transcendentals=0)


def swap(x, names, size, step):
    return lax.ppermute(x, names, [(at, at ^ step) for at in range(size)])


def shape(dims, dtype):
    return jax.ShapeDtypeStruct(tuple(dims), dtype)


def turn_table(position):
    frequency = THETA ** (-2.0 * np.arange(HALF, dtype=np.float32) / HD)
    angles = np.float32(position) * frequency.astype(np.float32)
    return np.stack([np.cos(angles), np.sin(angles)], axis=1).astype(np.float32)


def entry_order(plan):
    order = np.zeros((plan.mine * HD + 16, plan.line * plan.line_rows), np.float32)
    for head in range(plan.mine):
        for part in range(2):
            for entry in range(HALF):
                line, at = divmod(entry, plan.pairs)
                source = line * plan.line_rows + (part * plan.mine + head) * plan.pairs + at
                order[head * HD + part * HALF + entry, source] = 1.0
        for line in range(plan.line):
            for piece in range(2):
                order[plan.mine * HD + head, line * plan.line_rows + plan.q_rows + piece * plan.mine + head] = 1.0
    return order


def per_device(prefix_kv, move_ids, move_board, move_table, norm_gain, w_query, w_keyval, w_score):
    row_count = move_ids.shape[0]
    boards_here, prefix_len, _ = prefix_kv.shape
    moves, width = move_table.shape
    groups, line, pair = lax.axis_size("groups"), lax.axis_size("line"), lax.axis_size("pair")
    board_total = boards_here * line * pair
    capacity = max(2, (2 * row_count + board_total - 1) // board_total)
    heads = w_query.shape[1] // HD
    plan = Plan(groups, line, pair, heads, capacity, pair * boards_here)
    depth = w_query.shape[0]
    group_at = lax.axis_index("groups").astype(jnp.int32)
    line_at = lax.axis_index("line").astype(jnp.int32)
    pair_at = lax.axis_index("pair").astype(jnp.int32)
    slab_at = group_at * pair + pair_at
    ws = w_score.reshape(heads, HD)
    slab_axes = ("groups", "pair")
    board_row = move_board.reshape(1, row_count)

    if depth % HD:
        gain = lax.dynamic_slice_in_dim(norm_gain, (line_at * pair + pair_at) * depth, depth).reshape(1, depth)
    else:
        gain = norm_gain.reshape(width // HD, HD)

    half_cols = w_query.shape[1] // groups
    packed = scalar_call(
        functools.partial(pack_weights, plan),
        jnp.stack([group_at, line_at * pair + pair_at]),
        (w_query, w_keyval, ws, board_row, move_ids.reshape(1, row_count), gain),
        shape((plan.peers, plan.rows, depth), BF16),
        [
            pltpu.VMEM((depth, half_cols), BF16),
            pltpu.VMEM((depth, 2 * HD), BF16),
            pltpu.VMEM((heads, HD), BF16),
            pltpu.VMEM((1, row_count), jnp.int32),
            pltpu.VMEM((1, row_count), jnp.int32),
            pltpu.VMEM(gain.shape, BF16),
            pltpu.VMEM((plan.peers * plan.rows, half_cols + 2 * HD), F32),
            pltpu.SemaphoreType.DMA((6,)),
        ],
        cost(2 * plan.peers * plan.rows * half_cols * depth, 4 * w_query.size),
        {at: untouched() for at in range(6)},
        62,
    )
    weights = lax.all_to_all(packed, ("line", "pair"), split_axis=0, concat_axis=0, tiled=True)

    payload, slot_row = scalar_call(
        functools.partial(pack_prefix, plan),
        (line_at * pair + pair_at).reshape(1),
        (prefix_kv, ws, board_row, packed),
        (shape((boards_here + 1, prefix_len, HD), BF16), shape((1, row_count), jnp.int32)),
        [
            pltpu.VMEM((boards_here, prefix_len, HD), BF16),
            pltpu.VMEM((heads, HD), BF16),
            pltpu.VMEM((1, row_count), jnp.int32),
            pltpu.SemaphoreType.DMA((4,)),
        ],
        cost(2 * prefix_len * HD * HD * boards_here, 2 * prefix_kv.size),
        {at: untouched() for at in range(4)},
        62,
    )
    beside = swap(payload, slab_axes, plan.slab, 1)
    across = swap(payload, slab_axes, plan.slab, 2)

    block = min(moves, 128)
    inverse = pl.pallas_call(
        inverse_norms,
        out_shape=shape((1, moves), F32),
        grid=(moves // block,),
        in_specs=[pl.BlockSpec((block, width), lambda i: (i, 0)), untouched()],
        out_specs=pl.BlockSpec((1, block), lambda i: (0, i)),
        compiler_params=limits(58),
        cost_estimate=cost(8 * moves * width, 2 * moves * width),
    )(move_table, packed)
    turns = turn_table(prefix_len).reshape(line, 1, plan.pairs, 2)
    turns = jnp.asarray(np.tile(turns, (1, plan.mine, 1, 1)).reshape(line, plan.mine * plan.pairs, 2))
    flat = weights.transpose(1, 0, 2).reshape(plan.rows, width) if depth % HD else weights
    queries, own_values = scalar_call(
        functools.partial(project, plan),
        line_at.reshape(1),
        (flat, move_table, inverse, turns, beside, across),
        (shape((line, plan.line_rows, moves), BF16), shape((plan.mine, moves), F32)),
        [pltpu.VMEM((moves, width), BF16), pltpu.SemaphoreType.DMA((4,))],
        cost(2 * moves * width * 256, 2 * moves * width),
        {1: untouched(), 4: untouched(), 5: untouched()},
        58,
    )
    queries = lax.all_to_all(queries, "line", split_axis=0, concat_axis=0, tiled=True)
    listed = pl.pallas_call(
        functools.partial(read_lists, plan),
        out_shape=shape((plan.share, plan.slots), F32),
        compiler_params=limits(32),
        cost_estimate=cost(10**7, 10**6),
    )(weights)
    listed = jnp.stack([listed, swap(listed, slab_axes, plan.slab, pair)]).astype(jnp.int32)
    diagonal = swap(beside, slab_axes, plan.slab, 2)

    query_rows = plan.mine * HD
    back = plan.peers * lax.axis_size("tensor")
    parts = scalar_call(
        functools.partial(attend, plan),
        slab_at.reshape(1),
        (
            queries.reshape(line * plan.line_rows, moves),
            jnp.asarray(entry_order(plan), BF16),
            own_values,
            payload,
            beside,
            across,
            diagonal,
            listed,
        ),
        shape((groups, back, plan.share, plan.slots), F32),
        [
            pltpu.VMEM((query_rows + 16, moves), BF16),
            pltpu.VMEM((16, moves), F32),
            pltpu.VMEM((plan.slab, boards_here, plan.slots), F32),
            pltpu.VMEM((query_rows + 16, plan.slab * plan.slots), F32),
            pltpu.VMEM((query_rows + 16, plan.slab * plan.slots), F32),
        ],
        cost(2 * 272 * moves * 4096, 4 * 10**6),
    )
    parts = lax.all_to_all(
        parts.reshape(groups * back, plan.share, plan.slots),
        ("groups", "line", "pair", "tensor"),
        split_axis=0,
        concat_axis=0,
        tiled=True,
    )
    parts = parts.reshape(groups, line, back // line, plan.share, plan.slots)
    logprob = pl.pallas_call(
        functools.partial(finish, plan), out_shape=shape((1, row_count), F32), compiler_params=limits(VMEM_MIB)
    )(parts, board_row, slot_row)
    return logprob.reshape(row_count)


def solution(mesh):
    order = ("groups", "dp", "tensor")
    assert mesh.axis_names == order
    pair = 2
    groups, peers, tensor = (mesh.shape[name] for name in order)
    fine = Mesh(mesh.devices.reshape(groups, peers // pair, pair, tensor), ("groups", "line", "pair", "tensor"))
    rows = ("groups", "line", "pair")
    placed = (
        P(rows, None, "tensor"),
        P(rows),
        P(rows, None),
        P(),
        P(),
        P(("line", "pair"), "tensor"),
        P(("line", "pair"), "tensor"),
        P("tensor"),
    )
    return jax.shard_map(per_device, mesh=fine, in_specs=placed, out_specs=P(rows), check_vma=False)
```

```python
import functools
import math

import jax
import jax.numpy as jnp
import numpy as np
from jax import lax
from jax.experimental import pallas as pl
from jax.experimental.pallas import tpu as pltpu
from jax.sharding import Mesh
from jax.sharding import PartitionSpec as P

HD = 128
HALF = HD // 2
EPS = 1e-06
THETA = 5000000.0
DEAD = -1e30
VMEM_MIB = 52

F32 = jnp.float32
BF16 = jnp.bfloat16

NN = (((1,), (0,)), ((), ()))
NT = (((1,), (1,)), ((), ()))
TN = (((0,), (0,)), ((), ()))


def matmul(a, b, dims=NN):
    return lax.dot_general(a, b, dims, preferred_element_type=F32)


def limits(mib):
    return pltpu.CompilerParams(vmem_limit_bytes=mib * 1024 * 1024)


class Plan:
    def __init__(self, groups, line, pair, heads, capacity, share):
        self.groups, self.line, self.pair = groups, line, pair
        self.peers = line * pair
        self.slab = groups * pair
        self.heads = heads
        self.mine = heads // self.slab
        self.pairs = HALF // line
        self.q_rows = self.mine * 2 * self.pairs
        self.k_rows = 2 * self.pairs
        self.fold_at = self.q_rows + self.k_rows
        self.list_at = self.fold_at + self.mine
        self.rows = -(-(self.list_at + 1) // 8) * 8
        self.line_rows = -(-(self.q_rows + 2 * self.mine) // 8) * 8
        self.capacity = capacity
        self.share = share
        self.slots = self.peers * capacity


def pack_weights(plan, at_ref, wq_hbm, wkv_hbm, ws_hbm, board_hbm, ids_hbm, out_ref, *scratch):
    wq, wkv, ws_ref, board_ref, ids_ref, pick, sems = scratch
    group = at_ref[0]
    rows, half_cols = plan.rows, wq.shape[1]
    columns_here = pl.ds(pl.multiple_of(group * half_cols, HD), half_cols)
    copies = (
        pltpu.make_async_copy(ws_hbm, ws_ref, sems.at[0]),
        pltpu.make_async_copy(board_hbm, board_ref, sems.at[1]),
        pltpu.make_async_copy(ids_hbm, ids_ref, sems.at[2]),
        pltpu.make_async_copy(wq_hbm.at[:, columns_here], wq, sems.at[3]),
        pltpu.make_async_copy(wkv_hbm, wkv, sems.at[4]),
    )
    for copy in copies:
        copy.start()
    for copy in copies[:3]:
        copy.wait()
    r = lax.broadcasted_iota(jnp.int32, (rows, 1), 0)
    part = r // (plan.mine * plan.pairs)
    head = (r // plan.pairs) % plan.mine
    entry = r % plan.pairs
    is_q = r < plan.q_rows
    k_at = r - plan.q_rows
    is_k = (k_at >= 0) & (k_at < plan.k_rows)
    f_at = r - plan.fold_at
    is_f = (f_at >= 0) & (f_at < plan.mine)
    q_lane = lax.broadcasted_iota(jnp.int32, (rows, half_cols), 1)
    k_lane = lax.broadcasted_iota(jnp.int32, (rows, HD), 1)
    ws = ws_ref[...].astype(F32)

    def fill(peer, carry):
        line, pair = peer // plan.pair, peer % plan.pair
        column = (pair * plan.mine + head) * HD + part * HALF + line * plan.pairs + entry
        column = jnp.where(is_q, column, -1)
        at = pl.ds(pl.multiple_of(peer * rows, 8), rows)
        pick[at, :half_cols] = jnp.where(q_lane == column, 1.0, 0.0)
        k_column = (k_at // plan.pairs) * HALF + line * plan.pairs + k_at % plan.pairs
        k_column = jnp.where(is_k, k_column, -1)
        pick[at, half_cols : half_cols + HD] = jnp.where(k_lane == k_column, 1.0, 0.0)
        fold = jnp.zeros((rows, HD), F32)
        my_head = jnp.where(is_f, (group * plan.pair + pair) * plan.mine + f_at, -1)
        for h in range(plan.heads):
            fold = jnp.where(my_head == h, ws[h : h + 1], fold)
        pick[at, half_cols + HD :] = fold
        return carry

    lax.fori_loop(0, plan.peers, fill, 0, unroll=plan.peers <= 8)

    count, depth = board_ref.shape[1], wq.shape[0]
    board_row = board_ref[...]
    board_col = jnp.broadcast_to(board_row.astype(F32), (8, count)).T[:, 0:1].astype(jnp.int32)
    own = lax.broadcasted_iota(jnp.int32, (count, count), 0)
    other = lax.broadcasted_iota(jnp.int32, (count, count), 1)
    ahead = jnp.where((board_col == board_row) & (other < own), 1.0, 0.0)
    rank = jnp.sum(ahead, axis=1, keepdims=True).astype(jnp.int32)
    key = board_col * plan.capacity + rank
    move = ids_ref[...] + 1
    parts = jnp.concatenate([(move // 64).astype(F32), (move % 64).astype(F32)], axis=0).astype(BF16)
    span = plan.share * plan.capacity
    lane = lax.broadcasted_iota(jnp.int32, (count, depth), 1)
    lane_row = lax.broadcasted_iota(jnp.int32, (1, depth), 1)
    lists = []
    for line in range(plan.line):
        place = jnp.where(lane < span, lane, lane - span) + line * span
        found = matmul(parts, jnp.where(key == place, 1.0, 0.0).astype(BF16))
        lists.append(jnp.where(lane_row < span, found[0:1], found[1:2]))

    for copy in copies[3:]:
        copy.wait()
    left = pick[...].astype(BF16)
    total = matmul(left[:, :half_cols], wq[...], NT) + matmul(left[:, half_cols:], wkv[...], NT)
    for peer in range(plan.peers):
        mine = total[peer * rows : (peer + 1) * rows]
        out_ref[peer] = jnp.where(r == plan.list_at, lists[peer // plan.pair], mine).astype(BF16)


def normalize(table_ref, gain_ref, after_ref, out_ref, gain):
    @pl.when(pl.program_id(0) == 0)
    def _():
        rows = gain_ref[...].astype(F32)
        gain[...] = jnp.concatenate([rows[r : r + 1] for r in range(rows.shape[0])], axis=1)

    half = table_ref.shape[0] // 2
    for at in (slice(0, half), slice(half, 2 * half)):
        raw = table_ref[at].astype(F32)
        inverse = lax.rsqrt(jnp.mean(raw * raw, axis=-1, keepdims=True) + EPS)
        out_ref[at] = (raw * inverse * gain[...]).astype(BF16)


def project(plan, at_ref, w_ref, normed_hbm, turn_ref, *rest):
    q_ref, vo_ref, buffers, sems = rest[-4:]
    moves, width = normed_hbm.shape
    held, block, _ = buffers.shape
    steps = moves // block

    def copy(step):
        at = step % held
        return pltpu.make_async_copy(normed_hbm.at[pl.ds(step * block, block)], buffers.at[at], sems.at[at])

    for step in range(min(held, steps)):
        copy(step).start()

    half, k_half = plan.q_rows // 2, plan.k_rows // 2
    turns = turn_ref[at_ref[0]]
    cosine, sine = turns[:, 0:1], turns[:, 1:2]
    cos_k, sin_k = cosine[:k_half], sine[:k_half]
    for step in range(steps):
        copy(step).wait()
        at = slice(step * block, (step + 1) * block)
        held_at = step % held
        if len(w_ref.shape) == 3:
            depth = w_ref.shape[2]
            total = None
            for s in range(w_ref.shape[0]):
                term = matmul(buffers[held_at, :, s * depth : (s + 1) * depth], w_ref[s], NT)
                total = term if total is None else total + term
        else:
            total = matmul(buffers[held_at], w_ref[...], NT)
        if step + held < steps:
            copy(step + held).start()
        pad = -total.shape[1] % HD
        if pad:
            total = jnp.concatenate([total, jnp.zeros((block, pad), F32)], axis=1)
        total = total.T
        first, second = total[:half], total[half : 2 * half]
        f_first = (first * cosine - second * sine).astype(BF16).astype(F32)
        f_second = (second * cosine + first * sine).astype(BF16).astype(F32)
        first, second = total[plan.q_rows : plan.q_rows + k_half], total[plan.q_rows + k_half : plan.fold_at]
        k_first = (first * cos_k - second * sin_k).astype(BF16).astype(F32)
        k_second = (second * cos_k + first * sin_k).astype(BF16).astype(F32)
        logits, tails = [], []
        for h in range(plan.mine):
            own = slice(h * k_half, (h + 1) * k_half)
            logit = jnp.sum(f_first[own] * k_first + f_second[own] * k_second, axis=0, keepdims=True)
            logits.append(logit.astype(BF16).astype(F32))
            tails.append(logit - logits[-1])
        pad = plan.line_rows - plan.q_rows - 2 * plan.mine
        pieces = [f_first, f_second, *logits, *tails]
        if pad:
            pieces.append(jnp.zeros((pad, block), F32))
        out = jnp.concatenate(pieces, axis=0).astype(BF16)
        for copy_at in range(q_ref.shape[0]):
            q_ref[copy_at, :, at] = out
        vo_ref[:, at] = total[plan.fold_at : plan.list_at]


def tie(x_ref, beside_ref, across_ref, out_ref):
    pass


def pack_prefix(plan, at_ref, prefix_hbm, ws_hbm, board_hbm, after_ref, out_ref, slot_ref, *scratch):
    values, ws_ref, board_ref, sems = scratch
    boards = values.shape[0]
    heads = plan.heads
    copies = (
        pltpu.make_async_copy(board_hbm, board_ref, sems.at[0]),
        pltpu.make_async_copy(ws_hbm, ws_ref, sems.at[1]),
        pltpu.make_async_copy(prefix_hbm.at[:, :, pl.ds(HD, HD)], values, sems.at[2]),
        pltpu.make_async_copy(prefix_hbm.at[:, :, pl.ds(0, HD)], out_ref.at[pl.ds(0, boards)], sems.at[3]),
    )
    for copy in copies:
        copy.start()
    copies[0].wait()
    count = board_ref.shape[1]
    board_row = board_ref[...]
    board_col = jnp.broadcast_to(board_row.astype(F32), (8, count)).T[:, 0:1].astype(jnp.int32)
    other = lax.broadcasted_iota(jnp.int32, (count, count), 0)
    own = lax.broadcasted_iota(jnp.int32, (count, count), 1)
    rank = jnp.sum(jnp.where((board_col == board_row) & (other < own), 1.0, 0.0), axis=0, keepdims=True)
    slot_ref[...] = rank.astype(jnp.int32) + at_ref[0] * plan.capacity

    copies[1].wait()
    span = HD // boards
    ws = jnp.concatenate([ws_ref[...].astype(F32)] * (HD // heads), axis=0)
    row = lax.broadcasted_iota(jnp.int32, (HD, 1), 0)
    copies[2].wait()
    fold = None
    for board in range(boards):
        keep = (row // span == board) & (row % span < 2 * heads)
        term = matmul(values[board], jnp.where(keep, ws, 0.0).astype(BF16), NT)
        fold = term if fold is None else fold + term
    rounded = fold.astype(BF16).astype(F32)
    lane = lax.broadcasted_iota(jnp.int32, fold.shape, 1)
    out_ref[boards] = jnp.where(lane % span < heads, rounded, fold - rounded).astype(BF16)
    copies[3].wait()


def read_lists(plan, w_ref, out_ref):
    share, capacity, peers = plan.share, plan.capacity, plan.peers
    span = share * capacity
    rows = jnp.concatenate([w_ref[s].astype(F32)[plan.list_at : plan.list_at + 1] for s in range(peers)], axis=0)
    lane = lax.broadcasted_iota(jnp.int32, (share * peers, 2 * span), 1)
    row = lax.broadcasted_iota(jnp.int32, (share * peers, 2 * span), 0)
    lane = jnp.where(lane < span, lane, lane - span)
    spread = jnp.concatenate([rows] * share, axis=0)
    spread = jnp.where(lane // capacity == row // peers, spread, 0.0).astype(BF16)
    c = lax.broadcasted_iota(jnp.int32, (2 * span, plan.slots), 0)
    slot = lax.broadcasted_iota(jnp.int32, (2 * span, plan.slots), 1)
    scale = jnp.where(c < span, 64.0, 1.0)
    place = jnp.where(c % capacity == slot % capacity, scale, 0.0).astype(BF16)
    listed = matmul(spread, place)
    row = lax.broadcasted_iota(jnp.int32, listed.shape, 0)
    slot = lax.broadcasted_iota(jnp.int32, listed.shape, 1)
    listed = jnp.where(slot // capacity == row % peers, listed, 0.0)
    out_ref[...] = jnp.sum(listed.reshape(share, peers, plan.slots), axis=1)


def attend(plan, at_ref, q_ref, order_ref, vo_ref, *rest):
    prefix_refs = rest[: plan.slab]
    moves_ref, out_ref, table, extra, scores, taken_even, taken_odd = rest[plan.slab :]
    here = at_ref[0]
    mine, heads, slots = plan.mine, plan.heads, plan.slots
    moves = q_ref.shape[1]
    boards = prefix_refs[0].shape[0] - 1
    query_rows = mine * HD

    mixed = matmul(order_ref[...], q_ref[...])
    table[:query_rows] = mixed[:query_rows].astype(BF16)
    extra[...] = jnp.zeros_like(extra)
    for place, value in ((0, mixed[query_rows : query_rows + mine]), (2 * mine, vo_ref[...])):
        rounded = value.astype(BF16).astype(F32)
        extra[place : place + mine] = rounded
        extra[place + mine : place + 2 * mine] = value - rounded
    table[query_rows:] = extra[...].astype(BF16)

    scale = math.log2(math.e) / math.sqrt(HD)
    move_at = lax.broadcasted_iota(jnp.int32, (moves, slots), 0) + 1
    lanes = mine * slots
    span = HD // boards
    fold_row = lax.broadcasted_iota(jnp.int32, (HD, lanes), 0)
    fold_head = here * mine + lax.broadcasted_iota(jnp.int32, (HD, lanes), 1) // slots

    def per_head(x, base):
        pieces = [x[base + h : base + h + 1] + x[base + mine + h : base + mine + h + 1] for h in range(mine)]
        return jnp.concatenate(pieces, axis=1)

    def moves_of(j, board):
        place = ((here ^ j) % plan.pair) * boards + board
        return moves_ref[j // plan.pair, pl.ds(place, 1), :]

    def gather(board, taken):
        chosen = [
            jnp.where(move_at == moves_of(j, board), 1.0, 0.0).astype(BF16) for j in range(plan.slab)
        ]
        taken[...] = matmul(table[...], jnp.concatenate(chosen, axis=1))

    def score_board(board, taken):
        at = fold_row - board * span
        fold_pick = jnp.where((at == fold_head) | (at == fold_head + heads), 1.0, 0.0).astype(BF16)
        for j in range(plan.slab):
            x = taken[:, j * slots : (j + 1) * slots]
            q = jnp.concatenate([x[h * HD : (h + 1) * HD].astype(BF16) for h in range(mine)], axis=1)
            logits = matmul(prefix_refs[j][board], q)
            fold = matmul(prefix_refs[j][boards], fold_pick)
            own_logit = per_head(x, query_rows)
            own_value = per_head(x, query_rows + 2 * mine)
            peak = jnp.maximum(jnp.max(logits, axis=0, keepdims=True), own_logit)
            weight = jnp.exp2((logits - peak) * scale)
            own_weight = jnp.exp2((own_logit - peak) * scale)
            denom = jnp.sum(weight, axis=0, keepdims=True) + own_weight
            value = (jnp.sum(weight * fold, axis=0, keepdims=True) + own_value * own_weight) / denom
            score = sum(value[:, h * slots : (h + 1) * slots] for h in range(mine))
            scores[here ^ j, pl.ds(board, 1), :] = jnp.where(moves_of(j, board) > 0, score, DEAD)

    gather(0, taken_even)

    def step(at, carry):
        board = 2 * at
        gather(jnp.minimum(board + 1, boards - 1), taken_odd)
        score_board(board, taken_even)
        gather(jnp.minimum(board + 2, boards - 1), taken_even)
        score_board(jnp.minimum(board + 1, boards - 1), taken_odd)
        return carry

    lax.fori_loop(0, -(-boards // 2), step, 0)
    for g in range(plan.groups):
        out_ref[g] = jnp.concatenate([scores[g * plan.pair + p] for p in range(plan.pair)], axis=0)


def finish(plan, parts_ref, board_ref, slot_ref, out_ref):
    columns = []
    for at in range(plan.line):
        columns.append(sum(parts_ref[at * plan.pair + p] for p in range(plan.pair)))
    scores = jnp.concatenate(columns, axis=0)
    live = scores > 0.5 * DEAD
    peak = jnp.max(scores, axis=1, keepdims=True)
    denom = jnp.sum(jnp.where(live, jnp.exp(scores - peak), 0.0), axis=1, keepdims=True)
    logprob = jnp.where(live, scores - peak - jnp.log(denom), 0.0)
    count = board_ref.shape[1]
    member = lax.broadcasted_iota(jnp.int32, (scores.shape[0], count), 0) == board_ref[...]
    member = jnp.where(member, 1.0, 0.0).astype(BF16)
    found = jnp.zeros((plan.slots, count), F32)
    for _ in range(3):
        rounded = logprob.astype(BF16)
        found = found + matmul(rounded, member, TN)
        logprob = logprob - rounded.astype(F32)
    at = lax.broadcasted_iota(jnp.int32, (plan.slots, count), 0) == slot_ref[...]
    out_ref[...] = jnp.sum(jnp.where(at, found, 0.0), axis=0, keepdims=True)


def untouched():
    return pl.BlockSpec(memory_space=pl.ANY)


def scalar_call(kernel, at, args, outs, scratch, cost=None, specs=None, mib=VMEM_MIB):
    whole = lambda x: pl.BlockSpec(x.shape, lambda i, at, n=len(x.shape): (0,) * n)
    specs = specs or {}
    return pl.pallas_call(
        kernel,
        out_shape=outs,
        grid_spec=pltpu.PrefetchScalarGridSpec(
            num_scalar_prefetch=1,
            grid=(1,),
            in_specs=[specs.get(i, whole(x)) for i, x in enumerate(args)],
            out_specs=jax.tree.map(whole, outs),
            scratch_shapes=scratch,
        ),
        compiler_params=limits(mib),
        cost_estimate=cost,
    )(at, *args)


def cost(flops, nbytes):
    return pl.CostEstimate(flops=int(flops), bytes_accessed=int(nbytes), transcendentals=0)


def swap(x, names, size, step):
    return lax.ppermute(x, names, [(at, at ^ step) for at in range(size)])


def shape(dims, dtype):
    return jax.ShapeDtypeStruct(tuple(dims), dtype)


def turn_table(position):
    frequency = THETA ** (-2.0 * np.arange(HALF, dtype=np.float32) / HD)
    angles = np.float32(position) * frequency.astype(np.float32)
    return np.stack([np.cos(angles), np.sin(angles)], axis=1).astype(np.float32)


def entry_order(plan):
    order = np.zeros((plan.mine * HD + 16, plan.line * plan.line_rows), np.float32)
    for head in range(plan.mine):
        for part in range(2):
            for entry in range(HALF):
                line, at = divmod(entry, plan.pairs)
                source = line * plan.line_rows + (part * plan.mine + head) * plan.pairs + at
                order[head * HD + part * HALF + entry, source] = 1.0
        for line in range(plan.line):
            for piece in range(2):
                order[plan.mine * HD + head, line * plan.line_rows + plan.q_rows + piece * plan.mine + head] = 1.0
    return order


def per_device(prefix_kv, move_ids, move_board, move_table, norm_gain, w_query, w_keyval, w_score):
    row_count = move_ids.shape[0]
    boards_here, prefix_len, _ = prefix_kv.shape
    moves, width = move_table.shape
    groups, line, pair = lax.axis_size("groups"), lax.axis_size("line"), lax.axis_size("pair")
    board_total = boards_here * line * pair
    capacity = max(2, (2 * row_count + board_total - 1) // board_total)
    heads = w_query.shape[1] // HD
    plan = Plan(groups, line, pair, heads, capacity, pair * boards_here)
    depth = w_query.shape[0]
    group_at = lax.axis_index("groups").astype(jnp.int32)
    line_at = lax.axis_index("line").astype(jnp.int32)
    pair_at = lax.axis_index("pair").astype(jnp.int32)
    slab_at = group_at * pair + pair_at
    ws = w_score.reshape(heads, HD)
    slab_axes = ("groups", "pair")
    board_row = move_board.reshape(1, row_count)

    half_cols = w_query.shape[1] // groups
    packed = scalar_call(
        functools.partial(pack_weights, plan),
        group_at.reshape(1),
        (w_query, w_keyval, ws, board_row, move_ids.reshape(1, row_count)),
        shape((plan.peers, plan.rows, depth), BF16),
        [
            pltpu.VMEM((depth, half_cols), BF16),
            pltpu.VMEM((depth, 2 * HD), BF16),
            pltpu.VMEM((heads, HD), BF16),
            pltpu.VMEM((1, row_count), jnp.int32),
            pltpu.VMEM((1, row_count), jnp.int32),
            pltpu.VMEM((plan.peers * plan.rows, half_cols + 2 * HD), F32),
            pltpu.SemaphoreType.DMA((5,)),
        ],
        cost(2 * plan.peers * plan.rows * half_cols * depth, 4 * w_query.size),
        {at: untouched() for at in range(5)},
        62,
    )
    weights = lax.all_to_all(packed, ("line", "pair"), split_axis=0, concat_axis=0, tiled=True)

    payload, slot_row = scalar_call(
        functools.partial(pack_prefix, plan),
        (line_at * pair + pair_at).reshape(1),
        (prefix_kv, ws, board_row, packed),
        (shape((boards_here + 1, prefix_len, HD), BF16), shape((1, row_count), jnp.int32)),
        [
            pltpu.VMEM((boards_here, prefix_len, HD), BF16),
            pltpu.VMEM((heads, HD), BF16),
            pltpu.VMEM((1, row_count), jnp.int32),
            pltpu.SemaphoreType.DMA((4,)),
        ],
        cost(2 * prefix_len * HD * HD * boards_here, 2 * prefix_kv.size),
        {at: untouched() for at in range(4)},
        62,
    )
    beside = swap(payload, slab_axes, plan.slab, 1)
    across = swap(payload, slab_axes, plan.slab, 2)

    block = min(moves, 256)
    normed = pl.pallas_call(
        normalize,
        out_shape=shape((moves, width), BF16),
        grid=(moves // block,),
        in_specs=[
            pl.BlockSpec((block, width), lambda i: (i, 0)),
            pl.BlockSpec((width // HD, HD), lambda i: (0, 0)),
            untouched(),
        ],
        out_specs=pl.BlockSpec((block, width), lambda i: (i, 0)),
        scratch_shapes=[pltpu.VMEM((1, width), F32)],
        compiler_params=limits(58),
        cost_estimate=cost(moves * width, moves * width // 4),
    )(move_table, norm_gain.reshape(width // HD, HD), packed)
    turns = turn_table(prefix_len).reshape(line, 1, plan.pairs, 2)
    turns = jnp.asarray(np.tile(turns, (1, plan.mine, 1, 1)).reshape(line, plan.mine * plan.pairs, 2))
    flat = weights.transpose(1, 0, 2).reshape(plan.rows, width) if depth % HD else weights
    queries, own_values = scalar_call(
        functools.partial(project, plan),
        line_at.reshape(1),
        (flat, normed, turns),
        (shape((line, plan.line_rows, moves), BF16), shape((plan.mine, moves), F32)),
        [pltpu.VMEM((2, block, width), BF16), pltpu.SemaphoreType.DMA((2,))],
        cost(moves * width, moves * width // 4),
        {1: untouched()},
        58,
    )
    queries = pl.pallas_call(
        tie,
        out_shape=shape(queries.shape, BF16),
        in_specs=[untouched()] * 3,
        out_specs=untouched(),
        input_output_aliases={0: 0},
        cost_estimate=cost(0, 0),
    )(queries, beside, across)
    queries = lax.all_to_all(queries, "line", split_axis=0, concat_axis=0, tiled=True)
    listed = pl.pallas_call(
        functools.partial(read_lists, plan),
        out_shape=shape((plan.share, plan.slots), F32),
        compiler_params=limits(32),
        cost_estimate=cost(10**7, 10**6),
    )(weights)
    listed = jnp.stack([listed, swap(listed, slab_axes, plan.slab, pair)]).astype(jnp.int32)
    diagonal = swap(beside, slab_axes, plan.slab, 2)

    query_rows = plan.mine * HD
    parts = scalar_call(
        functools.partial(attend, plan),
        slab_at.reshape(1),
        (
            queries.reshape(line * plan.line_rows, moves),
            jnp.asarray(entry_order(plan), BF16),
            own_values,
            payload,
            beside,
            across,
            diagonal,
            listed,
        ),
        shape((groups, plan.share, plan.slots), F32),
        [
            pltpu.VMEM((query_rows + 16, moves), BF16),
            pltpu.VMEM((16, moves), F32),
            pltpu.VMEM((plan.slab, boards_here, plan.slots), F32),
            pltpu.VMEM((query_rows + 16, plan.slab * plan.slots), F32),
            pltpu.VMEM((query_rows + 16, plan.slab * plan.slots), F32),
        ],
        cost(2 * 272 * moves * 4096, 4 * 10**6),
    )
    parts = lax.psum(parts, ("groups", "tensor"))
    parts = lax.dynamic_index_in_dim(parts, group_at, axis=0)
    parts = jnp.broadcast_to(parts, (plan.peers, plan.share, plan.slots))
    parts = lax.all_to_all(parts, ("line", "pair"), split_axis=0, concat_axis=0, tiled=True)
    logprob = pl.pallas_call(
        functools.partial(finish, plan), out_shape=shape((1, row_count), F32), compiler_params=limits(VMEM_MIB)
    )(parts, board_row, slot_row)
    return logprob.reshape(row_count)


def solution(mesh):
    order = ("groups", "dp", "tensor")
    assert mesh.axis_names == order
    pair = 2
    groups, peers, tensor = (mesh.shape[name] for name in order)
    fine = Mesh(mesh.devices.reshape(groups, peers // pair, pair, tensor), ("groups", "line", "pair", "tensor"))
    rows = ("groups", "line", "pair")
    placed = (
        P(rows, None, "tensor"),
        P(rows),
        P(rows, None),
        P(),
        P(),
        P(("line", "pair"), "tensor"),
        P(("line", "pair"), "tensor"),
        P("tensor"),
    )
    return jax.shard_map(per_device, mesh=fine, in_specs=placed, out_specs=P(rows), check_vma=False)
```

```python
import functools
import math

import jax
import jax.numpy as jnp
import numpy as np
from jax import lax
from jax.experimental import pallas as pl
from jax.experimental.pallas import tpu as pltpu
from jax.sharding import Mesh
from jax.sharding import PartitionSpec as P

HD = 128
HALF = HD // 2
EPS = 1e-06
THETA = 5000000.0
DEAD = -1e30
VMEM_MIB = 52

F32 = jnp.float32
BF16 = jnp.bfloat16

NN = (((1,), (0,)), ((), ()))
NT = (((1,), (1,)), ((), ()))
TN = (((0,), (0,)), ((), ()))


def matmul(a, b, dims=NN):
    return lax.dot_general(a, b, dims, preferred_element_type=F32)


def limits(mib):
    return pltpu.CompilerParams(vmem_limit_bytes=mib * 1024 * 1024)


class Plan:
    def __init__(self, groups, line, pair, heads, capacity, share):
        self.groups, self.line, self.pair = groups, line, pair
        self.peers = line * pair
        self.slab = groups * pair
        self.heads = heads
        self.mine = heads // self.slab
        self.pairs = HALF // line
        self.q_rows = self.mine * 2 * self.pairs
        self.k_rows = 2 * self.pairs
        self.fold_at = self.q_rows + self.k_rows
        self.list_at = self.fold_at + self.mine
        self.rows = -(-(self.list_at + 1) // 8) * 8
        self.line_rows = -(-(self.q_rows + 2 * self.mine) // 8) * 8
        self.capacity = capacity
        self.share = share
        self.slots = self.peers * capacity


def pack_weights(plan, at_ref, wq_hbm, wkv_hbm, ws_hbm, board_hbm, ids_hbm, out_ref, *scratch):
    wq, wkv, ws_ref, board_ref, ids_ref, pick, sems = scratch
    group = at_ref[0]
    rows, half_cols = plan.rows, wq.shape[1]
    columns_here = pl.ds(pl.multiple_of(group * half_cols, HD), half_cols)
    copies = (
        pltpu.make_async_copy(ws_hbm, ws_ref, sems.at[0]),
        pltpu.make_async_copy(board_hbm, board_ref, sems.at[1]),
        pltpu.make_async_copy(ids_hbm, ids_ref, sems.at[2]),
        pltpu.make_async_copy(wq_hbm.at[:, columns_here], wq, sems.at[3]),
        pltpu.make_async_copy(wkv_hbm, wkv, sems.at[4]),
    )
    for copy in copies:
        copy.start()
    for copy in copies[:3]:
        copy.wait()
    r = lax.broadcasted_iota(jnp.int32, (rows, 1), 0)
    part = r // (plan.mine * plan.pairs)
    head = (r // plan.pairs) % plan.mine
    entry = r % plan.pairs
    is_q = r < plan.q_rows
    k_at = r - plan.q_rows
    is_k = (k_at >= 0) & (k_at < plan.k_rows)
    f_at = r - plan.fold_at
    is_f = (f_at >= 0) & (f_at < plan.mine)
    q_lane = lax.broadcasted_iota(jnp.int32, (rows, half_cols), 1)
    k_lane = lax.broadcasted_iota(jnp.int32, (rows, HD), 1)
    ws = ws_ref[...].astype(F32)

    def fill(peer, carry):
        line, pair = peer // plan.pair, peer % plan.pair
        column = (pair * plan.mine + head) * HD + part * HALF + line * plan.pairs + entry
        column = jnp.where(is_q, column, -1)
        at = pl.ds(pl.multiple_of(peer * rows, 8), rows)
        pick[at, :half_cols] = jnp.where(q_lane == column, 1.0, 0.0)
        k_column = (k_at // plan.pairs) * HALF + line * plan.pairs + k_at % plan.pairs
        k_column = jnp.where(is_k, k_column, -1)
        pick[at, half_cols : half_cols + HD] = jnp.where(k_lane == k_column, 1.0, 0.0)
        fold = jnp.zeros((rows, HD), F32)
        my_head = jnp.where(is_f, (group * plan.pair + pair) * plan.mine + f_at, -1)
        for h in range(plan.heads):
            fold = jnp.where(my_head == h, ws[h : h + 1], fold)
        pick[at, half_cols + HD :] = fold
        return carry

    lax.fori_loop(0, plan.peers, fill, 0, unroll=plan.peers <= 8)

    count, depth = board_ref.shape[1], wq.shape[0]
    board_row = board_ref[...]
    board_col = jnp.broadcast_to(board_row.astype(F32), (8, count)).T[:, 0:1].astype(jnp.int32)
    own = lax.broadcasted_iota(jnp.int32, (count, count), 0)
    other = lax.broadcasted_iota(jnp.int32, (count, count), 1)
    ahead = jnp.where((board_col == board_row) & (other < own), 1.0, 0.0)
    rank = jnp.sum(ahead, axis=1, keepdims=True).astype(jnp.int32)
    key = board_col * plan.capacity + rank
    move = ids_ref[...] + 1
    parts = jnp.concatenate([(move // 64).astype(F32), (move % 64).astype(F32)], axis=0).astype(BF16)
    span = plan.share * plan.capacity
    lane = lax.broadcasted_iota(jnp.int32, (count, depth), 1)
    lane_row = lax.broadcasted_iota(jnp.int32, (1, depth), 1)
    lists = []
    for line in range(plan.line):
        place = jnp.where(lane < span, lane, lane - span) + line * span
        found = matmul(parts, jnp.where(key == place, 1.0, 0.0).astype(BF16))
        lists.append(jnp.where(lane_row < span, found[0:1], found[1:2]))

    for copy in copies[3:]:
        copy.wait()
    left = pick[...].astype(BF16)
    total = matmul(left[:, :half_cols], wq[...], NT) + matmul(left[:, half_cols:], wkv[...], NT)
    for peer in range(plan.peers):
        mine = total[peer * rows : (peer + 1) * rows]
        out_ref[peer] = jnp.where(r == plan.list_at, lists[peer // plan.pair], mine).astype(BF16)


def normalize(table_ref, gain_ref, after_ref, late_ref, out_ref, late_out_ref, gain):
    @pl.when(pl.program_id(0) == 0)
    def _():
        rows = gain_ref[...].astype(F32)
        gain[...] = jnp.concatenate([rows[r : r + 1] for r in range(rows.shape[0])], axis=1)

    half = table_ref.shape[0] // 2
    for at in (slice(0, half), slice(half, 2 * half)):
        raw = table_ref[at].astype(F32)
        inverse = lax.rsqrt(jnp.mean(raw * raw, axis=-1, keepdims=True) + EPS)
        out_ref[at] = (raw * inverse * gain[...]).astype(BF16)


def project(plan, at_ref, w_ref, normed_hbm, turn_ref, *rest):
    q_ref, vo_ref, table, sems = rest[-4:]
    moves = normed_hbm.shape[0]
    steps = sems.shape[0]
    block = moves // steps
    piece = math.gcd(block, 32)

    def copy(start, rows, step):
        at = pl.ds(start, rows)
        return pltpu.make_async_copy(normed_hbm.at[at], table.at[at], sems.at[step])

    for start in range(0, moves, piece):
        copy(start, piece, start // block).start()

    half, k_half = plan.q_rows // 2, plan.k_rows // 2
    turns = turn_ref[at_ref[0]]
    cosine, sine = turns[:, 0:1], turns[:, 1:2]
    cos_k, sin_k = cosine[:k_half], sine[:k_half]
    for step in range(steps):
        copy(step * block, block, step).wait()
        at = slice(step * block, (step + 1) * block)
        if len(w_ref.shape) == 3:
            depth = w_ref.shape[2]
            total = None
            for s in range(w_ref.shape[0]):
                term = matmul(table[at, s * depth : (s + 1) * depth], w_ref[s], NT)
                total = term if total is None else total + term
        else:
            total = matmul(table[at, :], w_ref[...], NT)
        pad = -total.shape[1] % HD
        if pad:
            total = jnp.concatenate([total, jnp.zeros((block, pad), F32)], axis=1)
        total = total.T
        first, second = total[:half], total[half : 2 * half]
        f_first = (first * cosine - second * sine).astype(BF16).astype(F32)
        f_second = (second * cosine + first * sine).astype(BF16).astype(F32)
        first, second = total[plan.q_rows : plan.q_rows + k_half], total[plan.q_rows + k_half : plan.fold_at]
        k_first = (first * cos_k - second * sin_k).astype(BF16).astype(F32)
        k_second = (second * cos_k + first * sin_k).astype(BF16).astype(F32)
        logits, tails = [], []
        for h in range(plan.mine):
            own = slice(h * k_half, (h + 1) * k_half)
            logit = jnp.sum(f_first[own] * k_first + f_second[own] * k_second, axis=0, keepdims=True)
            logits.append(logit.astype(BF16).astype(F32))
            tails.append(logit - logits[-1])
        pad = plan.line_rows - plan.q_rows - 2 * plan.mine
        pieces = [f_first, f_second, *logits, *tails]
        if pad:
            pieces.append(jnp.zeros((pad, block), F32))
        out = jnp.concatenate(pieces, axis=0).astype(BF16)
        for copy_at in range(q_ref.shape[0]):
            q_ref[copy_at, :, at] = out
        vo_ref[:, at] = total[plan.fold_at : plan.list_at]


def tied(x, *others):
    return pl.pallas_call(
        lambda *refs: None,
        out_shape=shape(x.shape, x.dtype),
        in_specs=[untouched()] * (1 + len(others)),
        out_specs=untouched(),
        input_output_aliases={0: 0},
        compiler_params=limits(62),
        cost_estimate=cost(0, 0),
    )(x, *others)


def pack_prefix(plan, at_ref, prefix_hbm, ws_hbm, board_hbm, after_ref, out_ref, late_ref, slot_ref, *scratch):
    values, ws_ref, board_ref, sems = scratch
    boards = values.shape[0]
    heads = plan.heads
    copies = (
        pltpu.make_async_copy(board_hbm, board_ref, sems.at[0]),
        pltpu.make_async_copy(ws_hbm, ws_ref, sems.at[1]),
        pltpu.make_async_copy(prefix_hbm.at[:, :, pl.ds(HD, HD)], values, sems.at[2]),
        pltpu.make_async_copy(prefix_hbm.at[:, :, pl.ds(0, HD)], out_ref.at[pl.ds(0, boards)], sems.at[3]),
    )
    for copy in copies:
        copy.start()
    copies[0].wait()
    count = board_ref.shape[1]
    board_row = board_ref[...]
    board_col = jnp.broadcast_to(board_row.astype(F32), (8, count)).T[:, 0:1].astype(jnp.int32)
    other = lax.broadcasted_iota(jnp.int32, (count, count), 0)
    own = lax.broadcasted_iota(jnp.int32, (count, count), 1)
    rank = jnp.sum(jnp.where((board_col == board_row) & (other < own), 1.0, 0.0), axis=0, keepdims=True)
    slot_ref[...] = rank.astype(jnp.int32) + at_ref[0] * plan.capacity

    copies[1].wait()
    span = HD // boards
    ws = jnp.concatenate([ws_ref[...].astype(F32)] * (HD // heads), axis=0)
    row = lax.broadcasted_iota(jnp.int32, (HD, 1), 0)
    copies[2].wait()
    fold = None
    for board in range(boards):
        keep = (row // span == board) & (row % span < 2 * heads)
        term = matmul(values[board], jnp.where(keep, ws, 0.0).astype(BF16), NT)
        fold = term if fold is None else fold + term
    rounded = fold.astype(BF16).astype(F32)
    lane = lax.broadcasted_iota(jnp.int32, fold.shape, 1)
    out_ref[boards] = jnp.where(lane % span < heads, rounded, fold - rounded).astype(BF16)
    copies[3].wait()
    late_ref[...] = out_ref[...]


def read_lists(plan, w_ref, out_ref):
    share, capacity, peers = plan.share, plan.capacity, plan.peers
    span = share * capacity
    rows = jnp.concatenate([w_ref[s].astype(F32)[plan.list_at : plan.list_at + 1] for s in range(peers)], axis=0)
    lane = lax.broadcasted_iota(jnp.int32, (share * peers, 2 * span), 1)
    row = lax.broadcasted_iota(jnp.int32, (share * peers, 2 * span), 0)
    lane = jnp.where(lane < span, lane, lane - span)
    spread = jnp.concatenate([rows] * share, axis=0)
    spread = jnp.where(lane // capacity == row // peers, spread, 0.0).astype(BF16)
    c = lax.broadcasted_iota(jnp.int32, (2 * span, plan.slots), 0)
    slot = lax.broadcasted_iota(jnp.int32, (2 * span, plan.slots), 1)
    scale = jnp.where(c < span, 64.0, 1.0)
    place = jnp.where(c % capacity == slot % capacity, scale, 0.0).astype(BF16)
    listed = matmul(spread, place)
    row = lax.broadcasted_iota(jnp.int32, listed.shape, 0)
    slot = lax.broadcasted_iota(jnp.int32, listed.shape, 1)
    listed = jnp.where(slot // capacity == row % peers, listed, 0.0)
    out_ref[...] = jnp.sum(listed.reshape(share, peers, plan.slots), axis=1)


def attend(plan, at_ref, q_ref, order_ref, vo_ref, *rest):
    prefix_refs = rest[: plan.slab]
    moves_ref, out_ref, table, extra, scores, taken_even, taken_odd = rest[plan.slab :]
    here = at_ref[0]
    mine, heads, slots = plan.mine, plan.heads, plan.slots
    moves = q_ref.shape[1]
    boards = prefix_refs[0].shape[0] - 1
    query_rows = mine * HD

    mixed = matmul(order_ref[...], q_ref[...])
    table[:query_rows] = mixed[:query_rows].astype(BF16)
    extra[...] = jnp.zeros_like(extra)
    for place, value in ((0, mixed[query_rows : query_rows + mine]), (2 * mine, vo_ref[...])):
        rounded = value.astype(BF16).astype(F32)
        extra[place : place + mine] = rounded
        extra[place + mine : place + 2 * mine] = value - rounded
    table[query_rows:] = extra[...].astype(BF16)

    scale = math.log2(math.e) / math.sqrt(HD)
    move_at = lax.broadcasted_iota(jnp.int32, (moves, slots), 0) + 1
    lanes = mine * slots
    span = HD // boards
    fold_row = lax.broadcasted_iota(jnp.int32, (HD, lanes), 0)
    fold_head = here * mine + lax.broadcasted_iota(jnp.int32, (HD, lanes), 1) // slots

    def per_head(x, base):
        pieces = [x[base + h : base + h + 1] + x[base + mine + h : base + mine + h + 1] for h in range(mine)]
        return jnp.concatenate(pieces, axis=1)

    def moves_of(j, board):
        place = ((here ^ j) % plan.pair) * boards + board
        return moves_ref[j // plan.pair, pl.ds(place, 1), :]

    def gather(board, taken):
        chosen = [
            jnp.where(move_at == moves_of(j, board), 1.0, 0.0).astype(BF16) for j in range(plan.slab)
        ]
        taken[...] = matmul(table[...], jnp.concatenate(chosen, axis=1))

    def score_board(board, taken):
        at = fold_row - board * span
        fold_pick = jnp.where((at == fold_head) | (at == fold_head + heads), 1.0, 0.0).astype(BF16)
        for j in range(plan.slab):
            x = taken[:, j * slots : (j + 1) * slots]
            q = jnp.concatenate([x[h * HD : (h + 1) * HD].astype(BF16) for h in range(mine)], axis=1)
            logits = matmul(prefix_refs[j][board], q)
            fold = matmul(prefix_refs[j][boards], fold_pick)
            own_logit = per_head(x, query_rows)
            own_value = per_head(x, query_rows + 2 * mine)
            peak = jnp.maximum(jnp.max(logits, axis=0, keepdims=True), own_logit)
            weight = jnp.exp2((logits - peak) * scale)
            own_weight = jnp.exp2((own_logit - peak) * scale)
            denom = jnp.sum(weight, axis=0, keepdims=True) + own_weight
            value = (jnp.sum(weight * fold, axis=0, keepdims=True) + own_value * own_weight) / denom
            score = sum(value[:, h * slots : (h + 1) * slots] for h in range(mine))
            scores[here ^ j, pl.ds(board, 1), :] = jnp.where(moves_of(j, board) > 0, score, DEAD)

    gather(0, taken_even)

    def step(at, carry):
        board = 2 * at
        gather(jnp.minimum(board + 1, boards - 1), taken_odd)
        score_board(board, taken_even)
        gather(jnp.minimum(board + 2, boards - 1), taken_even)
        score_board(jnp.minimum(board + 1, boards - 1), taken_odd)
        return carry

    lax.fori_loop(0, -(-boards // 2), step, 0)
    for g in range(plan.groups):
        both = jnp.concatenate([scores[g * plan.pair + p] for p in range(plan.pair)], axis=0)
        for copy in range(out_ref.shape[1]):
            out_ref[g, copy] = both


def finish(plan, parts_ref, board_ref, slot_ref, out_ref):
    line = parts_ref.shape[1]
    columns = []
    for at in range(line):
        total = None
        for g in range(parts_ref.shape[0]):
            for p in range(parts_ref.shape[2]):
                term = parts_ref[g, at, p]
                total = term if total is None else total + term
        columns.append(total)
    scores = jnp.concatenate(columns, axis=0)
    live = scores > 0.5 * DEAD
    peak = jnp.max(scores, axis=1, keepdims=True)
    denom = jnp.sum(jnp.where(live, jnp.exp(scores - peak), 0.0), axis=1, keepdims=True)
    logprob = jnp.where(live, scores - peak - jnp.log(denom), 0.0)
    count = board_ref.shape[1]
    member = lax.broadcasted_iota(jnp.int32, (scores.shape[0], count), 0) == board_ref[...]
    member = jnp.where(member, 1.0, 0.0).astype(BF16)
    found = jnp.zeros((plan.slots, count), F32)
    for _ in range(3):
        rounded = logprob.astype(BF16)
        found = found + matmul(rounded, member, TN)
        logprob = logprob - rounded.astype(F32)
    at = lax.broadcasted_iota(jnp.int32, (plan.slots, count), 0) == slot_ref[...]
    out_ref[...] = jnp.sum(jnp.where(at, found, 0.0), axis=0, keepdims=True)


def untouched():
    return pl.BlockSpec(memory_space=pl.ANY)


def scalar_call(kernel, at, args, outs, scratch, cost=None, specs=None, mib=VMEM_MIB):
    whole = lambda x: pl.BlockSpec(x.shape, lambda i, at, n=len(x.shape): (0,) * n)
    specs = specs or {}
    return pl.pallas_call(
        kernel,
        out_shape=outs,
        grid_spec=pltpu.PrefetchScalarGridSpec(
            num_scalar_prefetch=1,
            grid=(1,),
            in_specs=[specs.get(i, whole(x)) for i, x in enumerate(args)],
            out_specs=jax.tree.map(whole, outs),
            scratch_shapes=scratch,
        ),
        compiler_params=limits(mib),
        cost_estimate=cost,
    )(at, *args)


def cost(flops, nbytes):
    return pl.CostEstimate(flops=int(flops), bytes_accessed=int(nbytes), transcendentals=0)


def swap(x, names, size, step):
    return lax.ppermute(x, names, [(at, at ^ step) for at in range(size)])


def shape(dims, dtype):
    return jax.ShapeDtypeStruct(tuple(dims), dtype)


def turn_table(position):
    frequency = THETA ** (-2.0 * np.arange(HALF, dtype=np.float32) / HD)
    angles = np.float32(position) * frequency.astype(np.float32)
    return np.stack([np.cos(angles), np.sin(angles)], axis=1).astype(np.float32)


def entry_order(plan):
    order = np.zeros((plan.mine * HD + 16, plan.line * plan.line_rows), np.float32)
    for head in range(plan.mine):
        for part in range(2):
            for entry in range(HALF):
                line, at = divmod(entry, plan.pairs)
                source = line * plan.line_rows + (part * plan.mine + head) * plan.pairs + at
                order[head * HD + part * HALF + entry, source] = 1.0
        for line in range(plan.line):
            for piece in range(2):
                order[plan.mine * HD + head, line * plan.line_rows + plan.q_rows + piece * plan.mine + head] = 1.0
    return order


def per_device(prefix_kv, move_ids, move_board, move_table, norm_gain, w_query, w_keyval, w_score):
    row_count = move_ids.shape[0]
    boards_here, prefix_len, _ = prefix_kv.shape
    moves, width = move_table.shape
    groups, line, pair = lax.axis_size("groups"), lax.axis_size("line"), lax.axis_size("pair")
    board_total = boards_here * line * pair
    capacity = max(2, (2 * row_count + board_total - 1) // board_total)
    heads = w_query.shape[1] // HD
    plan = Plan(groups, line, pair, heads, capacity, pair * boards_here)
    depth = w_query.shape[0]
    group_at = lax.axis_index("groups").astype(jnp.int32)
    line_at = lax.axis_index("line").astype(jnp.int32)
    pair_at = lax.axis_index("pair").astype(jnp.int32)
    slab_at = group_at * pair + pair_at
    ws = w_score.reshape(heads, HD)
    slab_axes = ("groups", "pair")
    board_row = move_board.reshape(1, row_count)

    half_cols = w_query.shape[1] // groups
    packed = scalar_call(
        functools.partial(pack_weights, plan),
        group_at.reshape(1),
        (w_query, w_keyval, ws, board_row, move_ids.reshape(1, row_count)),
        shape((plan.peers, plan.rows, depth), BF16),
        [
            pltpu.VMEM((depth, half_cols), BF16),
            pltpu.VMEM((depth, 2 * HD), BF16),
            pltpu.VMEM((heads, HD), BF16),
            pltpu.VMEM((1, row_count), jnp.int32),
            pltpu.VMEM((1, row_count), jnp.int32),
            pltpu.VMEM((plan.peers * plan.rows, half_cols + 2 * HD), F32),
            pltpu.SemaphoreType.DMA((5,)),
        ],
        cost(2 * plan.peers * plan.rows * half_cols * depth, 4 * w_query.size),
        {at: untouched() for at in range(5)},
        62,
    )
    weights = lax.all_to_all(packed, ("line", "pair"), split_axis=0, concat_axis=0, tiled=True)

    payload, late, slot_row = scalar_call(
        functools.partial(pack_prefix, plan),
        (line_at * pair + pair_at).reshape(1),
        (prefix_kv, ws, board_row, packed),
        (*[shape((boards_here + 1, prefix_len, HD), BF16)] * 2, shape((1, row_count), jnp.int32)),
        [
            pltpu.VMEM((boards_here, prefix_len, HD), BF16),
            pltpu.VMEM((heads, HD), BF16),
            pltpu.VMEM((1, row_count), jnp.int32),
            pltpu.SemaphoreType.DMA((4,)),
        ],
        cost(2 * prefix_len * HD * HD * boards_here, 2 * prefix_kv.size),
        {at: untouched() for at in range(4)},
        62,
    )
    across = swap(payload, slab_axes, plan.slab, 2)

    block = min(moves, 256)
    normed, late = pl.pallas_call(
        normalize,
        out_shape=(shape((moves, width), BF16), shape(late.shape, BF16)),
        grid=(moves // block,),
        in_specs=[
            pl.BlockSpec((block, width), lambda i: (i, 0)),
            pl.BlockSpec((width // HD, HD), lambda i: (0, 0)),
            untouched(),
            untouched(),
        ],
        out_specs=(pl.BlockSpec((block, width), lambda i: (i, 0)), untouched()),
        scratch_shapes=[pltpu.VMEM((1, width), F32)],
        input_output_aliases={3: 1},
        compiler_params=limits(58),
        cost_estimate=cost(moves * width, moves * width // 4),
    )(move_table, norm_gain.reshape(width // HD, HD), packed, late)
    beside = swap(late, slab_axes, plan.slab, 1)
    turns = turn_table(prefix_len).reshape(line, 1, plan.pairs, 2)
    turns = jnp.asarray(np.tile(turns, (1, plan.mine, 1, 1)).reshape(line, plan.mine * plan.pairs, 2))
    flat = weights.transpose(1, 0, 2).reshape(plan.rows, width) if depth % HD else weights
    queries, own_values = scalar_call(
        functools.partial(project, plan),
        line_at.reshape(1),
        (flat, normed, turns),
        (shape((line, plan.line_rows, moves), BF16), shape((plan.mine, moves), F32)),
        [pltpu.VMEM((moves, width), BF16), pltpu.SemaphoreType.DMA((moves // block,))],
        cost(moves * width, moves * width // 4),
        {1: untouched()},
        57,
    )
    queries = tied(queries, beside, across)
    queries = lax.all_to_all(queries, "line", split_axis=0, concat_axis=0, tiled=True)
    listed = pl.pallas_call(
        functools.partial(read_lists, plan),
        out_shape=shape((plan.share, plan.slots), F32),
        compiler_params=limits(32),
        cost_estimate=cost(10**7, 10**6),
    )(weights)
    listed = jnp.stack([listed, swap(listed, slab_axes, plan.slab, pair)]).astype(jnp.int32)
    diagonal = swap(beside, slab_axes, plan.slab, 2)

    query_rows = plan.mine * HD
    back = plan.peers * lax.axis_size("tensor")
    parts = pl.pallas_call(
        functools.partial(attend, plan),
        out_shape=shape((groups, back, plan.share, plan.slots), F32),
        in_specs=[pl.BlockSpec(memory_space=pltpu.SMEM)] + [pl.BlockSpec(memory_space=pltpu.VMEM)] * 8,
        out_specs=pl.BlockSpec(memory_space=pltpu.VMEM),
        scratch_shapes=[
            pltpu.VMEM((query_rows + 16, moves), BF16),
            pltpu.VMEM((16, moves), F32),
            pltpu.VMEM((plan.slab, boards_here, plan.slots), F32),
            pltpu.VMEM((query_rows + 16, plan.slab * plan.slots), F32),
            pltpu.VMEM((query_rows + 16, plan.slab * plan.slots), F32),
        ],
        compiler_params=limits(24),
        cost_estimate=cost(2 * 272 * moves * 4096, 4 * 10**6),
    )(
        slab_at.reshape(1),
        queries.reshape(line * plan.line_rows, moves),
        jnp.asarray(entry_order(plan), BF16),
        own_values,
        payload,
        beside,
        across,
        diagonal,
        listed,
    )
    parts = lax.all_to_all(
        parts.reshape(groups * back, plan.share, plan.slots),
        ("groups", "line", "pair", "tensor"),
        split_axis=0,
        concat_axis=0,
        tiled=True,
    )
    parts = parts.reshape(groups, line, back // line, plan.share, plan.slots)
    logprob = pl.pallas_call(
        functools.partial(finish, plan), out_shape=shape((1, row_count), F32), compiler_params=limits(VMEM_MIB)
    )(parts, board_row, slot_row)
    return logprob.reshape(row_count)


def solution(mesh):
    order = ("groups", "dp", "tensor")
    assert mesh.axis_names == order
    pair = 2
    groups, peers, tensor = (mesh.shape[name] for name in order)
    fine = Mesh(mesh.devices.reshape(groups, peers // pair, pair, tensor), ("groups", "line", "pair", "tensor"))
    rows = ("groups", "line", "pair")
    placed = (
        P(rows, None, "tensor"),
        P(rows),
        P(rows, None),
        P(),
        P(),
        P(("line", "pair"), "tensor"),
        P(("line", "pair"), "tensor"),
        P("tensor"),
    )
    return jax.shard_map(per_device, mesh=fine, in_specs=placed, out_specs=P(rows), check_vma=False)
```

```python
import functools
import math

import jax
import jax.numpy as jnp
import numpy as np
from jax import lax
from jax.experimental import pallas as pl
from jax.experimental.pallas import tpu as pltpu
from jax.sharding import Mesh
from jax.sharding import PartitionSpec as P

HD = 128
HALF = HD // 2
EPS = 1e-06
THETA = 5000000.0
DEAD = -1e30
VMEM_MIB = 52
GROUP, LINE, PEER, SLAB = range(4)

F32 = jnp.float32
BF16 = jnp.bfloat16

NN = (((1,), (0,)), ((), ()))
NT = (((1,), (1,)), ((), ()))
TN = (((0,), (0,)), ((), ()))


def matmul(a, b, dims=NN):
    return lax.dot_general(a, b, dims, preferred_element_type=F32)


def limits(mib):
    return pltpu.CompilerParams(vmem_limit_bytes=mib * 1024 * 1024)


class Plan:
    def __init__(self, groups, line, pair, heads, capacity, share):
        self.groups, self.line, self.pair = groups, line, pair
        self.peers = line * pair
        self.slab = groups * pair
        self.heads = heads
        self.mine = heads // self.slab
        self.pairs = HALF // line
        self.q_rows = self.mine * 2 * self.pairs
        self.k_rows = 2 * self.pairs
        self.fold_at = self.q_rows + self.k_rows
        self.list_at = self.fold_at + self.mine
        self.rows = -(-(self.list_at + 1) // 8) * 8
        self.line_rows = -(-(self.q_rows + 2 * self.mine) // 8) * 8
        self.capacity = capacity
        self.share = share
        self.slots = self.peers * capacity
        self.direct = line <= 4


def pack_weights(plan, place_ref, wq_hbm, wkv_hbm, ws_hbm, board_hbm, ids_hbm, *rest):
    out_ref, wq, wkv, ws_ref, board_ref, ids_ref, pick, sems = rest
    group = place_ref[GROUP]
    rows, half_cols = plan.rows, wq.shape[1]
    columns_here = pl.ds(pl.multiple_of(group * half_cols, HD), half_cols)
    copies = (
        pltpu.make_async_copy(ws_hbm, ws_ref, sems.at[0]),
        pltpu.make_async_copy(board_hbm, board_ref, sems.at[1]),
        pltpu.make_async_copy(ids_hbm, ids_ref, sems.at[2]),
        pltpu.make_async_copy(wq_hbm.at[:, columns_here], wq, sems.at[3]),
        pltpu.make_async_copy(wkv_hbm, wkv, sems.at[4]),
    )
    for copy in copies:
        copy.start()
    for copy in copies[:3]:
        copy.wait()
    r = lax.broadcasted_iota(jnp.int32, (rows, 1), 0)
    part = r // (plan.mine * plan.pairs)
    head = (r // plan.pairs) % plan.mine
    entry = r % plan.pairs
    is_q = r < plan.q_rows
    k_at = r - plan.q_rows
    is_k = (k_at >= 0) & (k_at < plan.k_rows)
    f_at = r - plan.fold_at
    is_f = (f_at >= 0) & (f_at < plan.mine)
    q_lane = lax.broadcasted_iota(jnp.int32, (rows, half_cols), 1)
    k_lane = lax.broadcasted_iota(jnp.int32, (rows, HD), 1)
    ws = ws_ref[...].astype(F32)

    def fill(peer, carry):
        line, pair = peer // plan.pair, peer % plan.pair
        column = (pair * plan.mine + head) * HD + part * HALF + line * plan.pairs + entry
        column = jnp.where(is_q, column, -1)
        at = pl.ds(pl.multiple_of(peer * rows, 8), rows)
        pick[at, :half_cols] = jnp.where(q_lane == column, 1.0, 0.0)
        k_column = (k_at // plan.pairs) * HALF + line * plan.pairs + k_at % plan.pairs
        k_column = jnp.where(is_k, k_column, -1)
        pick[at, half_cols : half_cols + HD] = jnp.where(k_lane == k_column, 1.0, 0.0)
        fold = jnp.zeros((rows, HD), F32)
        my_head = jnp.where(is_f, (group * plan.pair + pair) * plan.mine + f_at, -1)
        for h in range(plan.heads):
            fold = jnp.where(my_head == h, ws[h : h + 1], fold)
        pick[at, half_cols + HD :] = fold
        return carry

    lax.fori_loop(0, plan.peers, fill, 0, unroll=plan.peers <= 8)

    count, depth = board_ref.shape[1], wq.shape[0]
    board_row = board_ref[...]
    board_col = jnp.broadcast_to(board_row.astype(F32), (8, count)).T[:, 0:1].astype(jnp.int32)
    own = lax.broadcasted_iota(jnp.int32, (count, count), 0)
    other = lax.broadcasted_iota(jnp.int32, (count, count), 1)
    ahead = jnp.where((board_col == board_row) & (other < own), 1.0, 0.0)
    rank = jnp.sum(ahead, axis=1, keepdims=True).astype(jnp.int32)
    key = board_col * plan.capacity + rank
    move = ids_ref[...] + 1
    parts = jnp.concatenate([(move // 64).astype(F32), (move % 64).astype(F32)], axis=0).astype(BF16)
    span = plan.share * plan.capacity
    lane = lax.broadcasted_iota(jnp.int32, (count, depth), 1)
    lane_row = lax.broadcasted_iota(jnp.int32, (1, depth), 1)
    lists = []
    for line in range(plan.line):
        place = jnp.where(lane < span, lane, lane - span) + line * span
        found = matmul(parts, jnp.where(key == place, 1.0, 0.0).astype(BF16))
        lists.append(jnp.where(lane_row < span, found[0:1], found[1:2]))

    for copy in copies[3:]:
        copy.wait()
    left = pick[...].astype(BF16)
    total = matmul(left[:, :half_cols], wq[...], NT) + matmul(left[:, half_cols:], wkv[...], NT)
    for peer in range(plan.peers):
        mine = total[peer * rows : (peer + 1) * rows]
        out_ref[peer] = jnp.where(r == plan.list_at, lists[peer // plan.pair], mine).astype(BF16)


def normalize(table_ref, gain_ref, after_ref, out_ref, gain):
    @pl.when(pl.program_id(0) == 0)
    def _():
        rows = gain_ref[...].astype(F32)
        gain[...] = jnp.concatenate([rows[r : r + 1] for r in range(rows.shape[0])], axis=1)

    half = table_ref.shape[0] // 2
    for at in (slice(0, half), slice(half, 2 * half)):
        raw = table_ref[at].astype(F32)
        inverse = lax.rsqrt(jnp.mean(raw * raw, axis=-1, keepdims=True) + EPS)
        out_ref[at] = (raw * inverse * gain[...]).astype(BF16)


def project(plan, place_ref, w_ref, normed_hbm, turn_hbm, q_ref, vo_ref, table, turns, sems, turn_sem):
    moves = normed_hbm.shape[0]
    steps = sems.shape[0]
    block = moves // steps
    piece = math.gcd(block, 32)

    def copy(start, rows, step):
        at = pl.ds(start, rows)
        return pltpu.make_async_copy(normed_hbm.at[at], table.at[at], sems.at[step])

    turn_copy = pltpu.make_async_copy(turn_hbm.at[place_ref[LINE]], turns, turn_sem)
    turn_copy.start()
    for start in range(0, moves, piece):
        copy(start, piece, start // block).start()
    turn_copy.wait()

    half, k_half = plan.q_rows // 2, plan.k_rows // 2
    cosine, sine = turns[:, 0:1], turns[:, 1:2]
    cos_k, sin_k = cosine[:k_half], sine[:k_half]
    for step in range(steps):
        copy(step * block, block, step).wait()
        at = slice(step * block, (step + 1) * block)
        if len(w_ref.shape) == 3:
            depth = w_ref.shape[2]
            total = None
            for s in range(w_ref.shape[0]):
                term = matmul(w_ref[s], table[at, s * depth : (s + 1) * depth], NT)
                total = term if total is None else total + term
        else:
            total = matmul(w_ref[...], table[at, :], NT)
        first, second = total[:half], total[half : 2 * half]
        f_first = (first * cosine - second * sine).astype(BF16).astype(F32)
        f_second = (second * cosine + first * sine).astype(BF16).astype(F32)
        first, second = total[plan.q_rows : plan.q_rows + k_half], total[plan.q_rows + k_half : plan.fold_at]
        k_first = (first * cos_k - second * sin_k).astype(BF16).astype(F32)
        k_second = (second * cos_k + first * sin_k).astype(BF16).astype(F32)
        logits, tails = [], []
        for h in range(plan.mine):
            own = slice(h * k_half, (h + 1) * k_half)
            logit = jnp.sum(f_first[own] * k_first + f_second[own] * k_second, axis=0, keepdims=True)
            logits.append(logit.astype(BF16).astype(F32))
            tails.append(logit - logits[-1])
        pad = plan.line_rows - plan.q_rows - 2 * plan.mine
        pieces = [f_first, f_second, *logits, *tails]
        if pad:
            pieces.append(jnp.zeros((pad, block), F32))
        out = jnp.concatenate(pieces, axis=0).astype(BF16)
        if plan.direct:
            q_ref[:, at] = out
        else:
            for line in range(plan.line):
                q_ref[line, :, at] = out
        vo_ref[:, at] = total[plan.fold_at : plan.list_at]


def tied(x, *others):
    return pl.pallas_call(
        lambda *refs: None,
        out_shape=shape(x.shape, x.dtype),
        in_specs=[untouched()] * (1 + len(others)),
        out_specs=untouched(),
        input_output_aliases={0: 0},
        compiler_params=limits(1),
        cost_estimate=cost(0, 0),
    )(x, *others)


def pack_prefix(plan, place_ref, prefix_hbm, ws_hbm, board_hbm, after_ref, out_ref, slot_ref, *scratch):
    values, ws_ref, board_ref, sems = scratch
    boards = values.shape[0]
    heads = plan.heads
    copies = (
        pltpu.make_async_copy(board_hbm, board_ref, sems.at[0]),
        pltpu.make_async_copy(ws_hbm, ws_ref, sems.at[1]),
        pltpu.make_async_copy(prefix_hbm.at[:, :, pl.ds(HD, HD)], values, sems.at[2]),
        pltpu.make_async_copy(prefix_hbm.at[:, :, pl.ds(0, HD)], out_ref.at[pl.ds(0, boards)], sems.at[3]),
    )
    for copy in copies:
        copy.start()
    copies[0].wait()
    count = board_ref.shape[1]
    board_row = board_ref[...]
    board_col = jnp.broadcast_to(board_row.astype(F32), (8, count)).T[:, 0:1].astype(jnp.int32)
    other = lax.broadcasted_iota(jnp.int32, (count, count), 0)
    own = lax.broadcasted_iota(jnp.int32, (count, count), 1)
    rank = jnp.sum(jnp.where((board_col == board_row) & (other < own), 1.0, 0.0), axis=0, keepdims=True)
    slot_ref[...] = rank.astype(jnp.int32) + place_ref[PEER] * plan.capacity

    copies[1].wait()
    span = HD // boards
    ws = jnp.concatenate([ws_ref[...].astype(F32)] * (HD // heads), axis=0)
    row = lax.broadcasted_iota(jnp.int32, (HD, 1), 0)
    copies[2].wait()
    fold = None
    for board in range(boards):
        keep = (row // span == board) & (row % span < 2 * heads)
        term = matmul(values[board], jnp.where(keep, ws, 0.0).astype(BF16), NT)
        fold = term if fold is None else fold + term
    rounded = fold.astype(BF16).astype(F32)
    lane = lax.broadcasted_iota(jnp.int32, fold.shape, 1)
    out_ref[boards] = jnp.where(lane % span < heads, rounded, fold - rounded).astype(BF16)
    copies[3].wait()


def read_lists(plan, place_ref, *refs):
    w_ref, out_ref = refs
    share, capacity, peers = plan.share, plan.capacity, plan.peers
    span = share * capacity
    rows = jnp.concatenate([w_ref[s].astype(F32)[plan.list_at : plan.list_at + 1] for s in range(peers)], axis=0)
    lane = lax.broadcasted_iota(jnp.int32, (share * peers, 2 * span), 1)
    row = lax.broadcasted_iota(jnp.int32, (share * peers, 2 * span), 0)
    lane = jnp.where(lane < span, lane, lane - span)
    spread = jnp.concatenate([rows] * share, axis=0)
    spread = jnp.where(lane // capacity == row // peers, spread, 0.0).astype(BF16)
    c = lax.broadcasted_iota(jnp.int32, (2 * span, plan.slots), 0)
    slot = lax.broadcasted_iota(jnp.int32, (2 * span, plan.slots), 1)
    scale = jnp.where(c < span, 64.0, 1.0)
    place = jnp.where(c % capacity == slot % capacity, scale, 0.0).astype(BF16)
    listed = matmul(spread, place)
    row = lax.broadcasted_iota(jnp.int32, listed.shape, 0)
    slot = lax.broadcasted_iota(jnp.int32, listed.shape, 1)
    listed = jnp.where(slot // capacity == row % peers, listed, 0.0)
    out_ref[...] = jnp.sum(listed.reshape(share, peers, plan.slots), axis=1)


def attend(plan, place_ref, vo_ref, own_ref, other_ref, *rest):
    prefix_refs, rest = rest[: plan.slab], rest[plan.slab :]
    *q_refs, out_ref, table, extra, scores, taken_even, taken_odd = rest
    here = place_ref[SLAB]
    mine, heads, slots = plan.mine, plan.heads, plan.slots
    moves = vo_ref.shape[1]
    boards = prefix_refs[0].shape[0] - 1
    query_rows = mine * HD

    mixed = None
    for step, q_ref in enumerate(q_refs):
        r = lax.broadcasted_iota(jnp.int32, (query_rows + 8, q_ref.shape[0]), 0)
        c = lax.broadcasted_iota(jnp.int32, (query_rows + 8, q_ref.shape[0]), 1)
        line, at = (place_ref[LINE] ^ step, c) if plan.direct else (c // plan.line_rows, c % plan.line_rows)
        part, head, entry = at // (mine * plan.pairs), (at // plan.pairs) % mine, at % plan.pairs
        goes = jnp.where(at < plan.q_rows, head * HD + part * HALF + line * plan.pairs + entry, -1)
        tail = at - plan.q_rows
        goes = jnp.where((tail >= 0) & (tail < 2 * mine), query_rows + tail % mine, goes)
        term = matmul(jnp.where(r == goes, 1.0, 0.0).astype(BF16), q_ref[...])
        mixed = term if mixed is None else mixed + term
    table[:query_rows] = mixed[:query_rows].astype(BF16)
    extra[...] = jnp.zeros_like(extra)
    for place, value in ((0, mixed[query_rows : query_rows + mine]), (2 * mine, vo_ref[...])):
        rounded = value.astype(BF16).astype(F32)
        extra[place : place + mine] = rounded
        extra[place + mine : place + 2 * mine] = value - rounded
    table[query_rows:] = extra[...].astype(BF16)

    scale = math.log2(math.e) / math.sqrt(HD)
    move_at = lax.broadcasted_iota(jnp.int32, (moves, slots), 0) + 1
    lanes = mine * slots
    span = HD // boards
    fold_row = lax.broadcasted_iota(jnp.int32, (HD, lanes), 0)
    fold_head = here * mine + lax.broadcasted_iota(jnp.int32, (HD, lanes), 1) // slots

    def per_head(x, base):
        pieces = [x[base + h : base + h + 1] + x[base + mine + h : base + mine + h + 1] for h in range(mine)]
        return jnp.concatenate(pieces, axis=1)

    def moves_of(j, board):
        place = ((here ^ j) % plan.pair) * boards + board
        return (own_ref, other_ref)[j // plan.pair][pl.ds(place, 1), :].astype(jnp.int32)

    def gather(board, taken):
        chosen = [
            jnp.where(move_at == moves_of(j, board), 1.0, 0.0).astype(BF16) for j in range(plan.slab)
        ]
        taken[...] = matmul(table[...], jnp.concatenate(chosen, axis=1))

    def score_board(board, taken):
        at = fold_row - board * span
        fold_pick = jnp.where((at == fold_head) | (at == fold_head + heads), 1.0, 0.0).astype(BF16)
        for j in range(plan.slab):
            x = taken[:, j * slots : (j + 1) * slots]
            q = jnp.concatenate([x[h * HD : (h + 1) * HD].astype(BF16) for h in range(mine)], axis=1)
            logits = matmul(prefix_refs[j][board], q)
            fold = matmul(prefix_refs[j][boards], fold_pick)
            own_logit = per_head(x, query_rows)
            own_value = per_head(x, query_rows + 2 * mine)
            peak = jnp.maximum(jnp.max(logits, axis=0, keepdims=True), own_logit)
            weight = jnp.exp2((logits - peak) * scale)
            own_weight = jnp.exp2((own_logit - peak) * scale)
            denom = jnp.sum(weight, axis=0, keepdims=True) + own_weight
            value = (jnp.sum(weight * fold, axis=0, keepdims=True) + own_value * own_weight) / denom
            score = sum(value[:, h * slots : (h + 1) * slots] for h in range(mine))
            scores[here ^ j, pl.ds(board, 1), :] = jnp.where(moves_of(j, board) > 0, score, DEAD)

    gather(0, taken_even)

    def step(at, carry):
        board = 2 * at
        gather(jnp.minimum(board + 1, boards - 1), taken_odd)
        score_board(board, taken_even)
        gather(jnp.minimum(board + 2, boards - 1), taken_even)
        score_board(jnp.minimum(board + 1, boards - 1), taken_odd)
        return carry

    lax.fori_loop(0, -(-boards // 2), step, 0)
    for g in range(plan.groups):
        both = jnp.concatenate([scores[g * plan.pair + p] for p in range(plan.pair)], axis=0)
        for copy in range(out_ref.shape[1]):
            out_ref[g, copy] = both


def finish(plan, parts_ref, board_ref, slot_ref, out_ref):
    line = parts_ref.shape[1]
    columns = []
    for at in range(line):
        total = None
        for g in range(parts_ref.shape[0]):
            for p in range(parts_ref.shape[2]):
                term = parts_ref[g, at, p]
                total = term if total is None else total + term
        columns.append(total)
    scores = jnp.concatenate(columns, axis=0)
    live = scores > 0.5 * DEAD
    peak = jnp.max(scores, axis=1, keepdims=True)
    denom = jnp.sum(jnp.where(live, jnp.exp(scores - peak), 0.0), axis=1, keepdims=True)
    logprob = jnp.where(live, scores - peak - jnp.log(denom), 0.0)
    count = board_ref.shape[1]
    member = lax.broadcasted_iota(jnp.int32, (scores.shape[0], count), 0) == board_ref[...]
    member = jnp.where(member, 1.0, 0.0).astype(BF16)
    found = jnp.zeros((plan.slots, count), F32)
    for _ in range(3):
        rounded = logprob.astype(BF16)
        found = found + matmul(rounded, member, TN)
        logprob = logprob - rounded.astype(F32)
    at = lax.broadcasted_iota(jnp.int32, (plan.slots, count), 0) == slot_ref[...]
    out_ref[...] = jnp.sum(jnp.where(at, found, 0.0), axis=0, keepdims=True)


def untouched():
    return pl.BlockSpec(memory_space=pl.ANY)


def local_call(kernel, place, args, outs, scratch=(), mib=40, copied=(), flops=0, nbytes=0):
    vmem = pl.BlockSpec(memory_space=pltpu.VMEM)
    return pl.pallas_call(
        kernel,
        out_shape=outs,
        in_specs=[pl.BlockSpec(memory_space=pltpu.SMEM)]
        + [untouched() if at in copied else vmem for at in range(len(args))],
        out_specs=jax.tree.map(lambda x: vmem, outs),
        scratch_shapes=scratch,
        compiler_params=limits(mib),
        cost_estimate=cost(flops, nbytes),
    )(place, *args)


def cost(flops, nbytes):
    return pl.CostEstimate(flops=int(flops), bytes_accessed=int(nbytes), transcendentals=0)


def swap(x, names, size, step):
    return lax.ppermute(x, names, [(at, at ^ step) for at in range(size)])


def shape(dims, dtype):
    return jax.ShapeDtypeStruct(tuple(dims), dtype)


def turn_table(position):
    frequency = THETA ** (-2.0 * np.arange(HALF, dtype=np.float32) / HD)
    angles = np.float32(position) * frequency.astype(np.float32)
    return np.stack([np.cos(angles), np.sin(angles)], axis=1).astype(np.float32)


def per_device(prefix_kv, move_ids, move_board, move_table, norm_gain, w_query, w_keyval, w_score):
    row_count = move_ids.shape[0]
    boards_here, prefix_len, _ = prefix_kv.shape
    moves, width = move_table.shape
    groups, line, pair = lax.axis_size("groups"), lax.axis_size("line"), lax.axis_size("pair")
    board_total = boards_here * line * pair
    capacity = max(2, (2 * row_count + board_total - 1) // board_total)
    heads = w_query.shape[1] // HD
    plan = Plan(groups, line, pair, heads, capacity, pair * boards_here)
    depth = w_query.shape[0]
    group_at = lax.axis_index("groups").astype(jnp.int32)
    line_at = lax.axis_index("line").astype(jnp.int32)
    pair_at = lax.axis_index("pair").astype(jnp.int32)
    place = jnp.stack([group_at, line_at, line_at * pair + pair_at, group_at * pair + pair_at])
    ws = w_score.reshape(heads, HD)
    slab_axes = ("groups", "pair")
    board_row = move_board.reshape(1, row_count)

    half_cols = w_query.shape[1] // groups
    packed = local_call(
        functools.partial(pack_weights, plan),
        place,
        (w_query, w_keyval, ws, board_row, move_ids.reshape(1, row_count)),
        shape((plan.peers, plan.rows, depth), BF16),
        [
            pltpu.VMEM((depth, half_cols), BF16),
            pltpu.VMEM((depth, 2 * HD), BF16),
            pltpu.VMEM((heads, HD), BF16),
            pltpu.VMEM((1, row_count), jnp.int32),
            pltpu.VMEM((1, row_count), jnp.int32),
            pltpu.VMEM((plan.peers * plan.rows, half_cols + 2 * HD), F32),
            pltpu.SemaphoreType.DMA((5,)),
        ],
        62,
        range(5),
    )
    weights = lax.all_to_all(packed, ("line", "pair"), split_axis=0, concat_axis=0, tiled=True)

    keys = shape((boards_here + 1, prefix_len, HD), BF16)
    payload, slot_row = local_call(
        functools.partial(pack_prefix, plan),
        place,
        (prefix_kv, ws, board_row, packed),
        (keys, shape((1, row_count), jnp.int32)),
        [
            pltpu.VMEM((boards_here, prefix_len, HD), BF16),
            pltpu.VMEM((heads, HD), BF16),
            pltpu.VMEM((1, row_count), jnp.int32),
            pltpu.SemaphoreType.DMA((4,)),
        ],
        56,
        range(4),
    )
    beside = swap(payload, slab_axes, plan.slab, 1)
    across = swap(payload, slab_axes, plan.slab, 2)

    block = min(moves, 256)
    normed = pl.pallas_call(
        normalize,
        out_shape=shape((moves, width), BF16),
        grid=(moves // block,),
        in_specs=[
            pl.BlockSpec((block, width), lambda i: (i, 0)),
            pl.BlockSpec((width // HD, HD), lambda i: (0, 0)),
            untouched(),
        ],
        out_specs=pl.BlockSpec((block, width), lambda i: (i, 0)),
        scratch_shapes=[pltpu.VMEM((1, width), F32)],
        compiler_params=limits(58),
        cost_estimate=cost(moves * width, moves * width // 4),
    )(move_table, norm_gain.reshape(width // HD, HD), packed)
    turns = turn_table(prefix_len).reshape(line, 1, plan.pairs, 2)
    turns = np.tile(turns, (1, plan.mine, 1, 1)).reshape(line, plan.mine * plan.pairs, 2)
    flat = weights.transpose(1, 0, 2).reshape(plan.rows, width) if depth % HD else weights
    sent = (plan.line_rows, moves)
    queries, own_values = local_call(
        functools.partial(project, plan),
        place,
        (flat, normed, jnp.asarray(turns)),
        (shape(sent if plan.direct else (line, *sent), BF16), shape((plan.mine, moves), F32)),
        [
            pltpu.VMEM((moves, width), BF16),
            pltpu.VMEM(turns.shape[1:], F32),
            pltpu.SemaphoreType.DMA((4,)),
            pltpu.SemaphoreType.DMA,
        ],
        53,
        (1, 2),
        2 * moves * width * 256,
        2 * moves * width,
    )
    queries = tied(queries, beside, across)
    if plan.direct:
        queries = [queries] + [swap(queries, "line", line, step) for step in range(1, line)]
    else:
        queries = lax.all_to_all(queries, "line", split_axis=0, concat_axis=0, tiled=True)
        queries = [queries.reshape(line * plan.line_rows, moves)]
    listed = local_call(
        functools.partial(read_lists, plan), place, (weights,), shape((plan.share, plan.slots), F32)
    )
    other = swap(listed, slab_axes, plan.slab, pair)
    diagonal = swap(beside, slab_axes, plan.slab, 2)

    query_rows = plan.mine * HD
    back = plan.peers * lax.axis_size("tensor")
    parts = local_call(
        functools.partial(attend, plan),
        place,
        (own_values, listed, other, payload, beside, across, diagonal, *queries),
        shape((groups, back, plan.share, plan.slots), F32),
        [
            pltpu.VMEM((query_rows + 16, moves), BF16),
            pltpu.VMEM((16, moves), F32),
            pltpu.VMEM((plan.slab, boards_here, plan.slots), F32),
            pltpu.VMEM((query_rows + 16, plan.slab * plan.slots), F32),
            pltpu.VMEM((query_rows + 16, plan.slab * plan.slots), F32),
        ],
        24,
    )
    parts = lax.all_to_all(
        parts.reshape(groups * back, plan.share, plan.slots),
        ("groups", "line", "pair", "tensor"),
        split_axis=0,
        concat_axis=0,
        tiled=True,
    )
    parts = parts.reshape(groups, line, back // line, plan.share, plan.slots)
    logprob = pl.pallas_call(
        functools.partial(finish, plan), out_shape=shape((1, row_count), F32), compiler_params=limits(VMEM_MIB)
    )(parts, board_row, slot_row)
    return logprob.reshape(row_count)


def solution(mesh):
    order = ("groups", "dp", "tensor")
    assert mesh.axis_names == order
    pair = 2
    groups, peers, tensor = (mesh.shape[name] for name in order)
    fine = Mesh(mesh.devices.reshape(groups, peers // pair, pair, tensor), ("groups", "line", "pair", "tensor"))
    rows = ("groups", "line", "pair")
    placed = (
        P(rows, None, "tensor"),
        P(rows),
        P(rows, None),
        P(),
        P(),
        P(("line", "pair"), "tensor"),
        P(("line", "pair"), "tensor"),
        P("tensor"),
    )
    return jax.shard_map(per_device, mesh=fine, in_specs=placed, out_specs=P(rows), check_vma=False)
```

```python
import functools
import math

import jax
import jax.numpy as jnp
import numpy as np
from jax import lax
from jax.experimental import pallas as pl
from jax.experimental.pallas import tpu as pltpu
from jax.sharding import Mesh
from jax.sharding import PartitionSpec as P

HD = 128
HALF = HD // 2
EPS = 1e-06
THETA = 5000000.0
DEAD = -1e30
VMEM_MIB = 52
GROUP, LINE, PEER, SLAB = range(4)

F32 = jnp.float32
BF16 = jnp.bfloat16

NN = (((1,), (0,)), ((), ()))
NT = (((1,), (1,)), ((), ()))
TN = (((0,), (0,)), ((), ()))


def matmul(a, b, dims=NN):
    return lax.dot_general(a, b, dims, preferred_element_type=F32)


def limits(mib):
    return pltpu.CompilerParams(vmem_limit_bytes=mib * 1024 * 1024)


class Plan:
    def __init__(self, groups, line, pair, heads, capacity, share):
        self.groups, self.line, self.pair = groups, line, pair
        self.peers = line * pair
        self.slab = groups * pair
        self.heads = heads
        self.mine = heads // self.slab
        self.pairs = HALF // line
        self.q_rows = self.mine * 2 * self.pairs
        self.k_rows = 2 * self.pairs
        self.fold_at = self.q_rows + self.k_rows
        self.list_at = self.fold_at + self.mine
        self.rows = -(-(self.list_at + 1) // 8) * 8
        self.line_rows = -(-(self.q_rows + 2 * self.mine) // 8) * 8
        self.capacity = capacity
        self.share = share
        self.slots = self.peers * capacity
        self.direct = line <= 4


def pack_weights(plan, place_ref, wq_hbm, wkv_hbm, ws_hbm, board_hbm, ids_hbm, *rest):
    out_ref, wq, wkv, ws_ref, board_ref, ids_ref, pick, sems = rest
    group = place_ref[0]
    rows, half_cols = plan.rows, wq.shape[1]
    columns_here = pl.ds(pl.multiple_of(group * half_cols, HD), half_cols)
    copies = (
        pltpu.make_async_copy(ws_hbm, ws_ref, sems.at[0]),
        pltpu.make_async_copy(board_hbm, board_ref, sems.at[1]),
        pltpu.make_async_copy(ids_hbm, ids_ref, sems.at[2]),
        pltpu.make_async_copy(wq_hbm.at[:, columns_here], wq, sems.at[3]),
        pltpu.make_async_copy(wkv_hbm, wkv, sems.at[4]),
    )
    for copy in copies:
        copy.start()
    for copy in copies[:3]:
        copy.wait()
    r = lax.broadcasted_iota(jnp.int32, (rows, 1), 0)
    part = r // (plan.mine * plan.pairs)
    head = (r // plan.pairs) % plan.mine
    entry = r % plan.pairs
    is_q = r < plan.q_rows
    k_at = r - plan.q_rows
    is_k = (k_at >= 0) & (k_at < plan.k_rows)
    f_at = r - plan.fold_at
    is_f = (f_at >= 0) & (f_at < plan.mine)
    q_lane = lax.broadcasted_iota(jnp.int32, (rows, half_cols), 1)
    k_lane = lax.broadcasted_iota(jnp.int32, (rows, HD), 1)
    ws = ws_ref[...].astype(F32)

    def fill(peer, carry):
        line, pair = peer // plan.pair, peer % plan.pair
        column = (pair * plan.mine + head) * HD + part * HALF + line * plan.pairs + entry
        column = jnp.where(is_q, column, -1)
        at = pl.ds(pl.multiple_of(peer * rows, 8), rows)
        pick[at, :half_cols] = jnp.where(q_lane == column, 1.0, 0.0)
        k_column = (k_at // plan.pairs) * HALF + line * plan.pairs + k_at % plan.pairs
        k_column = jnp.where(is_k, k_column, -1)
        pick[at, half_cols : half_cols + HD] = jnp.where(k_lane == k_column, 1.0, 0.0)
        fold = jnp.zeros((rows, HD), F32)
        my_head = jnp.where(is_f, (group * plan.pair + pair) * plan.mine + f_at, -1)
        for h in range(plan.heads):
            fold = jnp.where(my_head == h, ws[h : h + 1], fold)
        pick[at, half_cols + HD :] = fold
        return carry

    lax.fori_loop(0, plan.peers, fill, 0, unroll=plan.peers <= 8)

    count, depth = board_ref.shape[1], wq.shape[0]
    board_row = board_ref[...]
    board_col = jnp.broadcast_to(board_row.astype(F32), (8, count)).T[:, 0:1].astype(jnp.int32)
    own = lax.broadcasted_iota(jnp.int32, (count, count), 0)
    other = lax.broadcasted_iota(jnp.int32, (count, count), 1)
    ahead = jnp.where((board_col == board_row) & (other < own), 1.0, 0.0)
    rank = jnp.sum(ahead, axis=1, keepdims=True).astype(jnp.int32)
    key = board_col * plan.capacity + rank
    move = ids_ref[...] + 1
    parts = jnp.concatenate([(move // 64).astype(F32), (move % 64).astype(F32)], axis=0).astype(BF16)
    span = plan.share * plan.capacity
    lane = lax.broadcasted_iota(jnp.int32, (count, depth), 1)
    lane_row = lax.broadcasted_iota(jnp.int32, (1, depth), 1)
    lists = []
    for line in range(plan.line):
        place = jnp.where(lane < span, lane, lane - span) + line * span
        found = matmul(parts, jnp.where(key == place, 1.0, 0.0).astype(BF16))
        lists.append(jnp.where(lane_row < span, found[0:1], found[1:2]))

    for copy in copies[3:]:
        copy.wait()
    left = pick[...].astype(BF16)
    total = matmul(left[:, :half_cols], wq[...], NT) + matmul(left[:, half_cols:], wkv[...], NT)
    for peer in range(plan.peers):
        mine = total[peer * rows : (peer + 1) * rows]
        out_ref[peer] = jnp.where(r == plan.list_at, lists[peer // plan.pair], mine).astype(BF16)


def normalize(table_ref, gain_ref, after_ref, *refs):
    *outs, gain, held, sems = refs
    here = pl.program_id(0)

    @pl.when(here == 0)
    def _():
        rows = gain_ref[...].astype(F32)
        gain[...] = jnp.concatenate([rows[r : r + 1] for r in range(rows.shape[0])], axis=1)

    def copy(step):
        return pltpu.make_async_copy(held.at[step % 2], outs[step], sems.at[step % 2])

    def one(step):
        if step >= 2:
            copy(step - 2).wait()
        half = table_ref.shape[0] // 2
        for at in (slice(0, half), slice(half, 2 * half)):
            raw = table_ref[at].astype(F32)
            inverse = lax.rsqrt(jnp.mean(raw * raw, axis=-1, keepdims=True) + EPS)
            held[step % 2, at] = (raw * inverse * gain[...]).astype(BF16)
        copy(step).start()
        if step == len(outs) - 1:
            for last in range(max(0, step - 1), step + 1):
                copy(last).wait()

    for step in range(len(outs)):
        pl.when(here == step)(functools.partial(one, step))


def project(plan, at, place_ref, w_ref, normed_ref, turn_hbm, *refs):
    q_ref, vo_ref, turns, turn_sem = refs[-4:]
    copy = pltpu.make_async_copy(turn_hbm.at[place_ref[LINE]], turns, turn_sem)
    copy.start()
    if len(w_ref.shape) == 3:
        depth = w_ref.shape[2]
        total = None
        for s in range(w_ref.shape[0]):
            term = matmul(w_ref[s], normed_ref[:, s * depth : (s + 1) * depth], NT)
            total = term if total is None else total + term
    else:
        total = matmul(w_ref[...], normed_ref[...], NT)
    copy.wait()
    half, k_half = plan.q_rows // 2, plan.k_rows // 2
    cosine, sine = turns[:, 0:1], turns[:, 1:2]
    cos_k, sin_k = cosine[:k_half], sine[:k_half]
    first, second = total[:half], total[half : 2 * half]
    f_first = (first * cosine - second * sine).astype(BF16).astype(F32)
    f_second = (second * cosine + first * sine).astype(BF16).astype(F32)
    first, second = total[plan.q_rows : plan.q_rows + k_half], total[plan.q_rows + k_half : plan.fold_at]
    k_first = (first * cos_k - second * sin_k).astype(BF16).astype(F32)
    k_second = (second * cos_k + first * sin_k).astype(BF16).astype(F32)
    logits, tails = [], []
    for h in range(plan.mine):
        own = slice(h * k_half, (h + 1) * k_half)
        logit = jnp.sum(f_first[own] * k_first + f_second[own] * k_second, axis=0, keepdims=True)
        logits.append(logit.astype(BF16).astype(F32))
        tails.append(logit - logits[-1])
    pad = plan.line_rows - plan.q_rows - 2 * plan.mine
    pieces = [f_first, f_second, *logits, *tails]
    if pad:
        pieces.append(jnp.zeros((pad, total.shape[1]), F32))
    out = jnp.concatenate(pieces, axis=0).astype(BF16)
    if plan.direct:
        q_ref[:, at] = out
    else:
        for line in range(plan.line):
            q_ref[line, :, at] = out
    vo_ref[:, at] = total[plan.fold_at : plan.list_at]


def tied(x, *others):
    return pl.pallas_call(
        lambda *refs: None,
        out_shape=shape(x.shape, x.dtype),
        in_specs=[untouched()] * (1 + len(others)),
        out_specs=untouched(),
        input_output_aliases={0: 0},
        compiler_params=limits(1),
        cost_estimate=cost(0, 0),
    )(x, *others)


def pack_prefix(plan, place_ref, prefix_hbm, ws_hbm, board_hbm, after_ref, out_ref, slot_ref, *scratch):
    values, ws_ref, board_ref, sems = scratch
    boards = values.shape[0]
    heads = plan.heads
    copies = (
        pltpu.make_async_copy(board_hbm, board_ref, sems.at[0]),
        pltpu.make_async_copy(ws_hbm, ws_ref, sems.at[1]),
        pltpu.make_async_copy(prefix_hbm.at[:, :, pl.ds(HD, HD)], values, sems.at[2]),
        pltpu.make_async_copy(prefix_hbm.at[:, :, pl.ds(0, HD)], out_ref.at[pl.ds(0, boards)], sems.at[3]),
    )
    for copy in copies:
        copy.start()
    copies[0].wait()
    count = board_ref.shape[1]
    board_row = board_ref[...]
    board_col = jnp.broadcast_to(board_row.astype(F32), (8, count)).T[:, 0:1].astype(jnp.int32)
    other = lax.broadcasted_iota(jnp.int32, (count, count), 0)
    own = lax.broadcasted_iota(jnp.int32, (count, count), 1)
    rank = jnp.sum(jnp.where((board_col == board_row) & (other < own), 1.0, 0.0), axis=0, keepdims=True)
    slot_ref[...] = rank.astype(jnp.int32) + place_ref[PEER] * plan.capacity

    copies[1].wait()
    span = HD // boards
    ws = jnp.concatenate([ws_ref[...].astype(F32)] * (HD // heads), axis=0)
    row = lax.broadcasted_iota(jnp.int32, (HD, 1), 0)
    copies[2].wait()
    fold = None
    for board in range(boards):
        keep = (row // span == board) & (row % span < 2 * heads)
        term = matmul(values[board], jnp.where(keep, ws, 0.0).astype(BF16), NT)
        fold = term if fold is None else fold + term
    rounded = fold.astype(BF16).astype(F32)
    lane = lax.broadcasted_iota(jnp.int32, fold.shape, 1)
    out_ref[boards] = jnp.where(lane % span < heads, rounded, fold - rounded).astype(BF16)
    copies[3].wait()


def read_lists(plan, place_ref, *refs):
    w_ref, out_ref = refs
    share, capacity, peers = plan.share, plan.capacity, plan.peers
    span = share * capacity
    rows = jnp.concatenate([w_ref[s].astype(F32)[plan.list_at : plan.list_at + 1] for s in range(peers)], axis=0)
    lane = lax.broadcasted_iota(jnp.int32, (share * peers, 2 * span), 1)
    row = lax.broadcasted_iota(jnp.int32, (share * peers, 2 * span), 0)
    lane = jnp.where(lane < span, lane, lane - span)
    spread = jnp.concatenate([rows] * share, axis=0)
    spread = jnp.where(lane // capacity == row // peers, spread, 0.0).astype(BF16)
    c = lax.broadcasted_iota(jnp.int32, (2 * span, plan.slots), 0)
    slot = lax.broadcasted_iota(jnp.int32, (2 * span, plan.slots), 1)
    scale = jnp.where(c < span, 64.0, 1.0)
    place = jnp.where(c % capacity == slot % capacity, scale, 0.0).astype(BF16)
    listed = matmul(spread, place)
    row = lax.broadcasted_iota(jnp.int32, listed.shape, 0)
    slot = lax.broadcasted_iota(jnp.int32, listed.shape, 1)
    listed = jnp.where(slot // capacity == row % peers, listed, 0.0)
    out_ref[...] = jnp.sum(listed.reshape(share, peers, plan.slots), axis=1)


def attend(plan, place_ref, vo_ref, own_ref, other_ref, *rest):
    prefix_refs, rest = rest[: plan.slab], rest[plan.slab :]
    *q_refs, out_ref, table, extra, scores, taken_even, taken_odd = rest
    here = place_ref[SLAB]
    mine, heads, slots = plan.mine, plan.heads, plan.slots
    moves = vo_ref.shape[1]
    boards = prefix_refs[0].shape[0] - 1
    query_rows = mine * HD

    mixed = None
    for step, q_ref in enumerate(q_refs):
        r = lax.broadcasted_iota(jnp.int32, (query_rows + 8, q_ref.shape[0]), 0)
        c = lax.broadcasted_iota(jnp.int32, (query_rows + 8, q_ref.shape[0]), 1)
        line, at = (place_ref[LINE] ^ step, c) if plan.direct else (c // plan.line_rows, c % plan.line_rows)
        part, head, entry = at // (mine * plan.pairs), (at // plan.pairs) % mine, at % plan.pairs
        goes = jnp.where(at < plan.q_rows, head * HD + part * HALF + line * plan.pairs + entry, -1)
        tail = at - plan.q_rows
        goes = jnp.where((tail >= 0) & (tail < 2 * mine), query_rows + tail % mine, goes)
        term = matmul(jnp.where(r == goes, 1.0, 0.0).astype(BF16), q_ref[...])
        mixed = term if mixed is None else mixed + term
    table[:query_rows] = mixed[:query_rows].astype(BF16)
    extra[...] = jnp.zeros_like(extra)
    for place, value in ((0, mixed[query_rows : query_rows + mine]), (2 * mine, vo_ref[...])):
        rounded = value.astype(BF16).astype(F32)
        extra[place : place + mine] = rounded
        extra[place + mine : place + 2 * mine] = value - rounded
    table[query_rows:] = extra[...].astype(BF16)

    scale = math.log2(math.e) / math.sqrt(HD)
    move_at = lax.broadcasted_iota(jnp.int32, (moves, slots), 0) + 1
    lanes = mine * slots
    span = HD // boards
    fold_row = lax.broadcasted_iota(jnp.int32, (HD, lanes), 0)
    fold_head = here * mine + lax.broadcasted_iota(jnp.int32, (HD, lanes), 1) // slots

    def per_head(x, base):
        pieces = [x[base + h : base + h + 1] + x[base + mine + h : base + mine + h + 1] for h in range(mine)]
        return jnp.concatenate(pieces, axis=1)

    def moves_of(j, board):
        place = ((here ^ j) % plan.pair) * boards + board
        return (own_ref, other_ref)[j // plan.pair][pl.ds(place, 1), :].astype(jnp.int32)

    def gather(board, taken):
        chosen = [
            jnp.where(move_at == moves_of(j, board), 1.0, 0.0).astype(BF16) for j in range(plan.slab)
        ]
        taken[...] = matmul(table[...], jnp.concatenate(chosen, axis=1))

    def score_board(board, taken):
        at = fold_row - board * span
        fold_pick = jnp.where((at == fold_head) | (at == fold_head + heads), 1.0, 0.0).astype(BF16)
        for j in range(plan.slab):
            x = taken[:, j * slots : (j + 1) * slots]
            q = jnp.concatenate([x[h * HD : (h + 1) * HD].astype(BF16) for h in range(mine)], axis=1)
            logits = matmul(prefix_refs[j][board], q)
            fold = matmul(prefix_refs[j][boards], fold_pick)
            own_logit = per_head(x, query_rows)
            own_value = per_head(x, query_rows + 2 * mine)
            peak = jnp.maximum(jnp.max(logits, axis=0, keepdims=True), own_logit)
            weight = jnp.exp2((logits - peak) * scale)
            own_weight = jnp.exp2((own_logit - peak) * scale)
            denom = jnp.sum(weight, axis=0, keepdims=True) + own_weight
            value = (jnp.sum(weight * fold, axis=0, keepdims=True) + own_value * own_weight) / denom
            score = sum(value[:, h * slots : (h + 1) * slots] for h in range(mine))
            scores[here ^ j, pl.ds(board, 1), :] = jnp.where(moves_of(j, board) > 0, score, DEAD)

    gather(0, taken_even)

    def step(at, carry):
        board = 2 * at
        gather(jnp.minimum(board + 1, boards - 1), taken_odd)
        score_board(board, taken_even)
        gather(jnp.minimum(board + 2, boards - 1), taken_even)
        score_board(jnp.minimum(board + 1, boards - 1), taken_odd)
        return carry

    lax.fori_loop(0, -(-boards // 2), step, 0)
    for g in range(plan.groups):
        both = jnp.concatenate([scores[g * plan.pair + p] for p in range(plan.pair)], axis=0)
        for copy in range(out_ref.shape[1]):
            out_ref[g, copy] = both


def finish(plan, parts_ref, board_ref, slot_ref, out_ref):
    line = parts_ref.shape[1]
    columns = []
    for at in range(line):
        total = None
        for g in range(parts_ref.shape[0]):
            for p in range(parts_ref.shape[2]):
                term = parts_ref[g, at, p]
                total = term if total is None else total + term
        columns.append(total)
    scores = jnp.concatenate(columns, axis=0)
    live = scores > 0.5 * DEAD
    peak = jnp.max(scores, axis=1, keepdims=True)
    denom = jnp.sum(jnp.where(live, jnp.exp(scores - peak), 0.0), axis=1, keepdims=True)
    logprob = jnp.where(live, scores - peak - jnp.log(denom), 0.0)
    count = board_ref.shape[1]
    member = lax.broadcasted_iota(jnp.int32, (scores.shape[0], count), 0) == board_ref[...]
    member = jnp.where(member, 1.0, 0.0).astype(BF16)
    found = jnp.zeros((plan.slots, count), F32)
    for _ in range(3):
        rounded = logprob.astype(BF16)
        found = found + matmul(rounded, member, TN)
        logprob = logprob - rounded.astype(F32)
    at = lax.broadcasted_iota(jnp.int32, (plan.slots, count), 0) == slot_ref[...]
    out_ref[...] = jnp.sum(jnp.where(at, found, 0.0), axis=0, keepdims=True)


def untouched():
    return pl.BlockSpec(memory_space=pl.ANY)


def local_call(kernel, place, args, outs, scratch=(), mib=40, copied=(), flops=0, nbytes=0, aliases=None):
    vmem = pl.BlockSpec(memory_space=pltpu.VMEM)
    return pl.pallas_call(
        kernel,
        out_shape=outs,
        in_specs=[pl.BlockSpec(memory_space=pltpu.SMEM)]
        + [untouched() if at in copied else vmem for at in range(len(args))],
        out_specs=jax.tree.map(lambda x: vmem, outs),
        scratch_shapes=scratch,
        input_output_aliases=aliases or {},
        compiler_params=limits(mib),
        cost_estimate=cost(flops, nbytes),
    )(place, *args)


def cost(flops, nbytes):
    return pl.CostEstimate(flops=int(flops), bytes_accessed=int(nbytes), transcendentals=0)


def swap(x, names, size, step):
    return lax.ppermute(x, names, [(at, at ^ step) for at in range(size)])


def shape(dims, dtype):
    return jax.ShapeDtypeStruct(tuple(dims), dtype)


def turn_table(position):
    frequency = THETA ** (-2.0 * np.arange(HALF, dtype=np.float32) / HD)
    angles = np.float32(position) * frequency.astype(np.float32)
    return np.stack([np.cos(angles), np.sin(angles)], axis=1).astype(np.float32)


def per_device(prefix_kv, move_ids, move_board, move_table, norm_gain, w_query, w_keyval, w_score):
    row_count = move_ids.shape[0]
    boards_here, prefix_len, _ = prefix_kv.shape
    moves, width = move_table.shape
    groups, line, pair = lax.axis_size("groups"), lax.axis_size("line"), lax.axis_size("pair")
    board_total = boards_here * line * pair
    capacity = max(2, (2 * row_count + board_total - 1) // board_total)
    heads = w_query.shape[1] // HD
    plan = Plan(groups, line, pair, heads, capacity, pair * boards_here)
    depth = w_query.shape[0]
    group_at = lax.axis_index("groups").astype(jnp.int32)
    line_at = lax.axis_index("line").astype(jnp.int32)
    pair_at = lax.axis_index("pair").astype(jnp.int32)
    place = jnp.stack([group_at, line_at, line_at * pair + pair_at, group_at * pair + pair_at])
    ws = w_score.reshape(heads, HD)
    slab_axes = ("groups", "pair")
    board_row = move_board.reshape(1, row_count)

    half_cols = w_query.shape[1] // groups
    packed = local_call(
        functools.partial(pack_weights, plan),
        group_at.reshape(1),
        (w_query, w_keyval, ws, board_row, move_ids.reshape(1, row_count)),
        shape((plan.peers, plan.rows, depth), BF16),
        [
            pltpu.VMEM((depth, half_cols), BF16),
            pltpu.VMEM((depth, 2 * HD), BF16),
            pltpu.VMEM((heads, HD), BF16),
            pltpu.VMEM((1, row_count), jnp.int32),
            pltpu.VMEM((1, row_count), jnp.int32),
            pltpu.VMEM((plan.peers * plan.rows, half_cols + 2 * HD), F32),
            pltpu.SemaphoreType.DMA((5,)),
        ],
        62,
        range(5),
    )
    weights = lax.all_to_all(packed, ("line", "pair"), split_axis=0, concat_axis=0, tiled=True)

    keys = shape((boards_here + 1, prefix_len, HD), BF16)
    payload, slot_row = local_call(
        functools.partial(pack_prefix, plan),
        place,
        (prefix_kv, ws, board_row, packed),
        (keys, shape((1, row_count), jnp.int32)),
        [
            pltpu.VMEM((boards_here, prefix_len, HD), BF16),
            pltpu.VMEM((heads, HD), BF16),
            pltpu.VMEM((1, row_count), jnp.int32),
            pltpu.SemaphoreType.DMA((4,)),
        ],
        56,
        range(4),
    )
    beside = swap(payload, slab_axes, plan.slab, 1)
    across = swap(payload, slab_axes, plan.slab, 2)

    block = min(moves, 256)
    steps = moves // block
    normed = pl.pallas_call(
        normalize,
        out_shape=[shape((block, width), BF16)] * steps,
        grid=(steps,),
        in_specs=[
            pl.BlockSpec((block, width), lambda i: (i, 0)),
            pl.BlockSpec((width // HD, HD), lambda i: (0, 0)),
            untouched(),
        ],
        out_specs=[untouched()] * steps,
        scratch_shapes=[
            pltpu.VMEM((1, width), F32),
            pltpu.VMEM((2, block, width), BF16),
            pltpu.SemaphoreType.DMA((2,)),
        ],
        compiler_params=limits(58),
        cost_estimate=cost(moves * width, moves * width // 4),
    )(move_table, norm_gain.reshape(width // HD, HD), packed)
    turns = turn_table(prefix_len).reshape(line, 1, plan.pairs, 2)
    turns = np.tile(turns, (1, plan.mine, 1, 1)).reshape(line, plan.mine * plan.pairs, 2)
    flat = weights.transpose(1, 0, 2).reshape(plan.rows, width) if depth % HD else weights
    sent = (plan.line_rows, moves)
    outs = (shape(sent if plan.direct else (line, *sent), BF16), shape((plan.mine, moves), F32))
    filled = ()
    for step in range(steps):
        filled = local_call(
            functools.partial(project, plan, slice(step * block, (step + 1) * block)),
            place,
            (flat, normed[step], jnp.asarray(turns), *filled),
            outs,
            [pltpu.VMEM(turns.shape[1:], F32), pltpu.SemaphoreType.DMA],
            16,
            (2,),
            2 * block * width * 1024,
            block * width,
            {4: 0, 5: 1} if filled else None,
        )
    queries, own_values = filled
    queries = tied(queries, beside, across)
    beside = tied(beside, own_values)
    if plan.direct:
        queries = [queries] + [swap(queries, "line", line, step) for step in range(1, line)]
    else:
        queries = lax.all_to_all(queries, "line", split_axis=0, concat_axis=0, tiled=True)
        queries = [queries.reshape(line * plan.line_rows, moves)]
    listed = local_call(
        functools.partial(read_lists, plan), place, (weights,), shape((plan.share, plan.slots), F32)
    )
    other = swap(listed, slab_axes, plan.slab, pair)
    diagonal = swap(beside, slab_axes, plan.slab, 2)

    query_rows = plan.mine * HD
    back = plan.peers * lax.axis_size("tensor")
    parts = local_call(
        functools.partial(attend, plan),
        place,
        (own_values, listed, other, payload, beside, across, diagonal, *queries),
        shape((groups, back, plan.share, plan.slots), F32),
        [
            pltpu.VMEM((query_rows + 16, moves), BF16),
            pltpu.VMEM((16, moves), F32),
            pltpu.VMEM((plan.slab, boards_here, plan.slots), F32),
            pltpu.VMEM((query_rows + 16, plan.slab * plan.slots), F32),
            pltpu.VMEM((query_rows + 16, plan.slab * plan.slots), F32),
        ],
        24,
    )
    parts = lax.all_to_all(
        parts.reshape(groups * back, plan.share, plan.slots),
        ("groups", "line", "pair", "tensor"),
        split_axis=0,
        concat_axis=0,
        tiled=True,
    )
    parts = parts.reshape(groups, line, back // line, plan.share, plan.slots)
    logprob = pl.pallas_call(
        functools.partial(finish, plan), out_shape=shape((1, row_count), F32), compiler_params=limits(VMEM_MIB)
    )(parts, board_row, slot_row)
    return logprob.reshape(row_count)


def solution(mesh):
    order = ("groups", "dp", "tensor")
    assert mesh.axis_names == order
    pair = 2
    groups, peers, tensor = (mesh.shape[name] for name in order)
    fine = Mesh(mesh.devices.reshape(groups, peers // pair, pair, tensor), ("groups", "line", "pair", "tensor"))
    rows = ("groups", "line", "pair")
    placed = (
        P(rows, None, "tensor"),
        P(rows),
        P(rows, None),
        P(),
        P(),
        P(("line", "pair"), "tensor"),
        P(("line", "pair"), "tensor"),
        P("tensor"),
    )
    return jax.shard_map(per_device, mesh=fine, in_specs=placed, out_specs=P(rows), check_vma=False)
```

```python
import functools
import math

import jax
import jax.numpy as jnp
import numpy as np
from jax import lax
from jax.experimental import pallas as pl
from jax.experimental.pallas import tpu as pltpu
from jax.sharding import Mesh
from jax.sharding import PartitionSpec as P

HD = 128
HALF = HD // 2
EPS = 1e-06
THETA = 5000000.0
DEAD = -1e30
VMEM_MIB = 52
GROUP, LINE, PEER, SLAB = range(4)

F32 = jnp.float32
BF16 = jnp.bfloat16

NN = (((1,), (0,)), ((), ()))
NT = (((1,), (1,)), ((), ()))
TN = (((0,), (0,)), ((), ()))


def matmul(a, b, dims=NN):
    return lax.dot_general(a, b, dims, preferred_element_type=F32)


def limits(mib):
    return pltpu.CompilerParams(vmem_limit_bytes=mib * 1024 * 1024)


class Plan:
    def __init__(self, groups, line, pair, heads, capacity, share):
        self.groups, self.line, self.pair = groups, line, pair
        self.peers = line * pair
        self.slab = groups * pair
        self.heads = heads
        self.mine = heads // self.slab
        self.pairs = HALF // line
        self.q_rows = self.mine * 2 * self.pairs
        self.k_rows = 2 * self.pairs
        self.fold_at = self.q_rows + self.k_rows
        self.list_at = self.fold_at + self.mine
        self.rows = -(-(self.list_at + 1) // 8) * 8
        self.line_rows = -(-(self.q_rows + 2 * self.mine) // 8) * 8
        self.capacity = capacity
        self.share = share
        self.slots = self.peers * capacity
        self.direct = line <= 4


def pack_weights(plan, place_ref, wq_hbm, wkv_hbm, ws_hbm, board_hbm, ids_hbm, *rest):
    out_ref, wq, wkv, ws_ref, board_ref, ids_ref, pick, sems = rest
    group = place_ref[0]
    rows, half_cols = plan.rows, wq.shape[1]
    columns_here = pl.ds(pl.multiple_of(group * half_cols, HD), half_cols)
    copies = (
        pltpu.make_async_copy(ws_hbm, ws_ref, sems.at[0]),
        pltpu.make_async_copy(board_hbm, board_ref, sems.at[1]),
        pltpu.make_async_copy(ids_hbm, ids_ref, sems.at[2]),
        pltpu.make_async_copy(wq_hbm.at[:, columns_here], wq, sems.at[3]),
        pltpu.make_async_copy(wkv_hbm, wkv, sems.at[4]),
    )
    for copy in copies:
        copy.start()
    for copy in copies[:3]:
        copy.wait()
    r = lax.broadcasted_iota(jnp.int32, (rows, 1), 0)
    part = r // (plan.mine * plan.pairs)
    head = (r // plan.pairs) % plan.mine
    entry = r % plan.pairs
    is_q = r < plan.q_rows
    k_at = r - plan.q_rows
    is_k = (k_at >= 0) & (k_at < plan.k_rows)
    f_at = r - plan.fold_at
    is_f = (f_at >= 0) & (f_at < plan.mine)
    q_lane = lax.broadcasted_iota(jnp.int32, (rows, half_cols), 1)
    k_lane = lax.broadcasted_iota(jnp.int32, (rows, HD), 1)
    ws = ws_ref[...].astype(F32)

    def fill(peer, carry):
        line, pair = peer // plan.pair, peer % plan.pair
        column = (pair * plan.mine + head) * HD + part * HALF + line * plan.pairs + entry
        column = jnp.where(is_q, column, -1)
        at = pl.ds(pl.multiple_of(peer * rows, 8), rows)
        pick[at, :half_cols] = jnp.where(q_lane == column, 1.0, 0.0)
        k_column = (k_at // plan.pairs) * HALF + line * plan.pairs + k_at % plan.pairs
        k_column = jnp.where(is_k, k_column, -1)
        pick[at, half_cols : half_cols + HD] = jnp.where(k_lane == k_column, 1.0, 0.0)
        fold = jnp.zeros((rows, HD), F32)
        my_head = jnp.where(is_f, (group * plan.pair + pair) * plan.mine + f_at, -1)
        for h in range(plan.heads):
            fold = jnp.where(my_head == h, ws[h : h + 1], fold)
        pick[at, half_cols + HD :] = fold
        return carry

    lax.fori_loop(0, plan.peers, fill, 0, unroll=plan.peers <= 8)

    count, depth = board_ref.shape[1], wq.shape[0]
    board_row = board_ref[...]
    board_col = jnp.broadcast_to(board_row.astype(F32), (8, count)).T[:, 0:1].astype(jnp.int32)
    own = lax.broadcasted_iota(jnp.int32, (count, count), 0)
    other = lax.broadcasted_iota(jnp.int32, (count, count), 1)
    ahead = jnp.where((board_col == board_row) & (other < own), 1.0, 0.0)
    rank = jnp.sum(ahead, axis=1, keepdims=True).astype(jnp.int32)
    move = ids_ref[...] + 1
    boards, span = plan.line * plan.share, plan.share * plan.capacity
    member = lax.broadcasted_iota(jnp.int32, (boards, count), 0) == board_row
    parts = [jnp.where(member, part.astype(F32), 0.0) for part in (move // 64, move % 64)]
    lane = lax.broadcasted_iota(jnp.int32, (count, depth), 1)
    ranked = jnp.where(rank == (lane % span) % plan.capacity, 1.0, 0.0).astype(BF16)
    found = matmul(jnp.concatenate(parts, axis=0).astype(BF16), ranked)
    lane = lax.broadcasted_iota(jnp.int32, (2 * boards, depth), 1)
    row = lax.broadcasted_iota(jnp.int32, (2 * boards, depth), 0)
    keep = (row // boards == lane // span) & (row % plan.share == (lane % span) // plan.capacity)
    found = jnp.where(keep, found, 0.0)
    lists = []
    for line in range(plan.line):
        at = line * plan.share
        both = found[at : at + plan.share] + found[boards + at : boards + at + plan.share]
        lists.append(jnp.sum(both, axis=0, keepdims=True))

    for copy in copies[3:]:
        copy.wait()
    left = pick[...].astype(BF16)
    total = matmul(left[:, :half_cols], wq[...], NT) + matmul(left[:, half_cols:], wkv[...], NT)
    for peer in range(plan.peers):
        mine = total[peer * rows : (peer + 1) * rows]
        out_ref[peer] = jnp.where(r == plan.list_at, lists[peer // plan.pair], mine).astype(BF16)


def normalize(table_ref, gain_ref, after_ref, *refs):
    *outs, gain, held, sems = refs
    here = pl.program_id(0)

    @pl.when(here == 0)
    def _():
        rows = gain_ref[...].astype(F32)
        gain[...] = jnp.concatenate([rows[r : r + 1] for r in range(rows.shape[0])], axis=1)

    def copy(step):
        return pltpu.make_async_copy(held.at[step % 2], outs[step], sems.at[step % 2])

    def one(step):
        if step >= 2:
            copy(step - 2).wait()
        half = table_ref.shape[0] // 2
        for at in (slice(0, half), slice(half, 2 * half)):
            raw = table_ref[at].astype(F32)
            inverse = lax.rsqrt(jnp.mean(raw * raw, axis=-1, keepdims=True) + EPS)
            held[step % 2, at] = (raw * inverse * gain[...]).astype(BF16)
        copy(step).start()
        if step == len(outs) - 1:
            for last in range(max(0, step - 1), step + 1):
                copy(last).wait()

    for step in range(len(outs)):
        pl.when(here == step)(functools.partial(one, step))


def project(plan, at, mark, place_ref, w_ref, normed_ref, turn_ref, *refs):
    if mark:
        *refs, mark_ref = refs
        mark_ref[...] = jnp.zeros_like(mark_ref)
    q_ref, vo_ref = refs[-2:]
    if len(w_ref.shape) == 3:
        depth = w_ref.shape[2]
        total = None
        for s in range(w_ref.shape[0]):
            term = matmul(w_ref[s], normed_ref[:, s * depth : (s + 1) * depth], NT)
            total = term if total is None else total + term
    else:
        total = matmul(w_ref[...], normed_ref[...], NT)
    turns = turn_ref[place_ref[LINE]]
    half, k_half = plan.q_rows // 2, plan.k_rows // 2
    cosine, sine = turns[:, 0:1], turns[:, 1:2]
    cos_k, sin_k = cosine[:k_half], sine[:k_half]
    first, second = total[:half], total[half : 2 * half]
    f_first = (first * cosine - second * sine).astype(BF16).astype(F32)
    f_second = (second * cosine + first * sine).astype(BF16).astype(F32)
    first, second = total[plan.q_rows : plan.q_rows + k_half], total[plan.q_rows + k_half : plan.fold_at]
    k_first = (first * cos_k - second * sin_k).astype(BF16).astype(F32)
    k_second = (second * cos_k + first * sin_k).astype(BF16).astype(F32)
    logits, tails = [], []
    for h in range(plan.mine):
        own = slice(h * k_half, (h + 1) * k_half)
        logit = jnp.sum(f_first[own] * k_first + f_second[own] * k_second, axis=0, keepdims=True)
        logits.append(logit.astype(BF16).astype(F32))
        tails.append(logit - logits[-1])
    pad = plan.line_rows - plan.q_rows - 2 * plan.mine
    pieces = [f_first, f_second, *logits, *tails]
    if pad:
        pieces.append(jnp.zeros((pad, total.shape[1]), F32))
    out = jnp.concatenate(pieces, axis=0).astype(BF16)
    if plan.direct:
        q_ref[:, at] = out
    else:
        for line in range(plan.line):
            q_ref[line, :, at] = out
    vo_ref[:, at] = total[plan.fold_at : plan.list_at]


def tied(x, *others):
    return pl.pallas_call(
        lambda *refs: None,
        out_shape=shape(x.shape, x.dtype),
        in_specs=[untouched()] * (1 + len(others)),
        out_specs=untouched(),
        input_output_aliases={0: 0},
        compiler_params=limits(1),
        cost_estimate=cost(0, 0),
    )(x, *others)


def pack_prefix(plan, place_ref, prefix_hbm, ws_hbm, board_hbm, after_ref, out_ref, slot_ref, *scratch):
    values, ws_ref, board_ref, sems = scratch
    boards = values.shape[0]
    heads = plan.heads
    copies = (
        pltpu.make_async_copy(board_hbm, board_ref, sems.at[0]),
        pltpu.make_async_copy(ws_hbm, ws_ref, sems.at[1]),
        pltpu.make_async_copy(prefix_hbm.at[:, :, pl.ds(HD, HD)], values, sems.at[2]),
        pltpu.make_async_copy(prefix_hbm.at[:, :, pl.ds(0, HD)], out_ref.at[pl.ds(0, boards)], sems.at[3]),
    )
    for copy in copies:
        copy.start()
    copies[0].wait()
    count = board_ref.shape[1]
    board_row = board_ref[...]
    board_col = jnp.broadcast_to(board_row.astype(F32), (8, count)).T[:, 0:1].astype(jnp.int32)
    other = lax.broadcasted_iota(jnp.int32, (count, count), 0)
    own = lax.broadcasted_iota(jnp.int32, (count, count), 1)
    rank = jnp.sum(jnp.where((board_col == board_row) & (other < own), 1.0, 0.0), axis=0, keepdims=True)
    slot_ref[...] = rank.astype(jnp.int32) + place_ref[PEER] * plan.capacity

    copies[1].wait()
    span = HD // boards
    ws = jnp.concatenate([ws_ref[...].astype(F32)] * (HD // heads), axis=0)
    row = lax.broadcasted_iota(jnp.int32, (HD, 1), 0)
    copies[2].wait()
    fold = None
    for board in range(boards):
        keep = (row // span == board) & (row % span < 2 * heads)
        term = matmul(values[board], jnp.where(keep, ws, 0.0).astype(BF16), NT)
        fold = term if fold is None else fold + term
    rounded = fold.astype(BF16).astype(F32)
    lane = lax.broadcasted_iota(jnp.int32, fold.shape, 1)
    out_ref[boards] = jnp.where(lane % span < heads, rounded, fold - rounded).astype(BF16)
    copies[3].wait()


def read_lists(plan, place_ref, *refs):
    w_ref, _, out_ref = refs
    share, capacity, peers = plan.share, plan.capacity, plan.peers
    span = share * capacity
    rows = jnp.concatenate([w_ref[s].astype(F32)[plan.list_at : plan.list_at + 1] for s in range(peers)], axis=0)
    lane = lax.broadcasted_iota(jnp.int32, (share * peers, 2 * span), 1)
    row = lax.broadcasted_iota(jnp.int32, (share * peers, 2 * span), 0)
    lane = jnp.where(lane < span, lane, lane - span)
    spread = jnp.concatenate([rows] * share, axis=0)
    spread = jnp.where(lane // capacity == row // peers, spread, 0.0).astype(BF16)
    c = lax.broadcasted_iota(jnp.int32, (2 * span, plan.slots), 0)
    slot = lax.broadcasted_iota(jnp.int32, (2 * span, plan.slots), 1)
    scale = jnp.where(c < span, 64.0, 1.0)
    place = jnp.where(c % capacity == slot % capacity, scale, 0.0).astype(BF16)
    listed = matmul(spread, place)
    row = lax.broadcasted_iota(jnp.int32, listed.shape, 0)
    slot = lax.broadcasted_iota(jnp.int32, listed.shape, 1)
    listed = jnp.where(slot // capacity == row % peers, listed, 0.0)
    out_ref[...] = jnp.sum(listed.reshape(share, peers, plan.slots), axis=1)


def fold_columns(plan, here, block, board, boards, heads):
    lanes = plan.mine * plan.slots
    row = lax.broadcasted_iota(jnp.int32, (HD, lanes), 0) - board * (HD // boards)
    head = here * plan.mine + lax.broadcasted_iota(jnp.int32, (HD, lanes), 1) // plan.slots
    pick = jnp.where((row == head) | (row == head + heads), 1.0, 0.0).astype(BF16)
    return matmul(block, pick)


def prepare(plan, place_ref, own_ref, other_ref, *rest):
    *prefix_refs, chosen_ref, fold_ref = rest
    here = place_ref[SLAB]
    boards, moves = chosen_ref.shape[0], chosen_ref.shape[1]
    move_at = lax.broadcasted_iota(jnp.int32, (moves, plan.slots), 0) + 1

    def step(board, carry):
        for j in range(plan.slab):
            place = ((here ^ j) % plan.pair) * boards + board
            row = (own_ref, other_ref)[j // plan.pair][pl.ds(place, 1), :].astype(jnp.int32)
            at = slice(j * plan.slots, (j + 1) * plan.slots)
            chosen_ref[board, :, at] = jnp.where(move_at == row, 1.0, 0.0).astype(BF16)
        for j, prefix_ref in enumerate(prefix_refs):
            fold_ref[j, board] = fold_columns(plan, here, prefix_ref[boards], board, boards, plan.heads)
        return carry

    lax.fori_loop(0, boards, step, 0)


def attend(plan, place_ref, vo_ref, own_ref, other_ref, chosen_ref, fold_ref, *rest):
    prefix_refs, rest = rest[: plan.slab], rest[plan.slab :]
    *q_refs, out_ref, table, extra, scores, taken_even, taken_odd = rest
    here = place_ref[SLAB]
    mine, heads, slots = plan.mine, plan.heads, plan.slots
    moves = vo_ref.shape[1]
    boards = prefix_refs[0].shape[0] - 1
    query_rows = mine * HD

    mixed = None
    for step, q_ref in enumerate(q_refs):
        r = lax.broadcasted_iota(jnp.int32, (query_rows + 8, q_ref.shape[0]), 0)
        c = lax.broadcasted_iota(jnp.int32, (query_rows + 8, q_ref.shape[0]), 1)
        line, at = (place_ref[LINE] ^ step, c) if plan.direct else (c // plan.line_rows, c % plan.line_rows)
        part, head, entry = at // (mine * plan.pairs), (at // plan.pairs) % mine, at % plan.pairs
        goes = jnp.where(at < plan.q_rows, head * HD + part * HALF + line * plan.pairs + entry, -1)
        tail = at - plan.q_rows
        goes = jnp.where((tail >= 0) & (tail < 2 * mine), query_rows + tail % mine, goes)
        term = matmul(jnp.where(r == goes, 1.0, 0.0).astype(BF16), q_ref[...])
        mixed = term if mixed is None else mixed + term
    table[:query_rows] = mixed[:query_rows].astype(BF16)
    extra[...] = jnp.zeros_like(extra)
    for place, value in ((0, mixed[query_rows : query_rows + mine]), (2 * mine, vo_ref[...])):
        rounded = value.astype(BF16).astype(F32)
        extra[place : place + mine] = rounded
        extra[place + mine : place + 2 * mine] = value - rounded
    table[query_rows:] = extra[...].astype(BF16)

    scale = math.log2(math.e) / math.sqrt(HD)
    def per_head(x, base):
        pieces = [x[base + h : base + h + 1] + x[base + mine + h : base + mine + h + 1] for h in range(mine)]
        return jnp.concatenate(pieces, axis=1)

    def moves_of(j, board):
        place = ((here ^ j) % plan.pair) * boards + board
        return (own_ref, other_ref)[j // plan.pair][pl.ds(place, 1), :].astype(jnp.int32)

    def gather(board, taken):
        taken[...] = matmul(table[...], chosen_ref[board])

    def score_board(board, taken):
        for j in range(plan.slab):
            x = taken[:, j * slots : (j + 1) * slots]
            q = jnp.concatenate([x[h * HD : (h + 1) * HD].astype(BF16) for h in range(mine)], axis=1)
            logits = matmul(prefix_refs[j][board], q)
            if j < plan.slab - 1:
                fold = fold_ref[j, board]
            else:
                fold = fold_columns(plan, here, prefix_refs[j][boards], board, boards, heads)
            own_logit = per_head(x, query_rows)
            own_value = per_head(x, query_rows + 2 * mine)
            peak = jnp.maximum(jnp.max(logits, axis=0, keepdims=True), own_logit)
            weight = jnp.exp2((logits - peak) * scale)
            own_weight = jnp.exp2((own_logit - peak) * scale)
            denom = jnp.sum(weight, axis=0, keepdims=True) + own_weight
            value = (jnp.sum(weight * fold, axis=0, keepdims=True) + own_value * own_weight) / denom
            score = sum(value[:, h * slots : (h + 1) * slots] for h in range(mine))
            scores[here ^ j, pl.ds(board, 1), :] = jnp.where(moves_of(j, board) > 0, score, DEAD)

    gather(0, taken_even)

    def step(at, carry):
        board = 2 * at
        gather(jnp.minimum(board + 1, boards - 1), taken_odd)
        score_board(board, taken_even)
        gather(jnp.minimum(board + 2, boards - 1), taken_even)
        score_board(jnp.minimum(board + 1, boards - 1), taken_odd)
        return carry

    lax.fori_loop(0, -(-boards // 2), step, 0)
    for g in range(plan.groups):
        both = jnp.concatenate([scores[g * plan.pair + p] for p in range(plan.pair)], axis=0)
        for copy in range(out_ref.shape[1]):
            out_ref[g, copy] = both


def finish(plan, parts_ref, board_ref, slot_ref, out_ref):
    line = parts_ref.shape[1]
    columns = []
    for at in range(line):
        total = None
        for g in range(parts_ref.shape[0]):
            for p in range(parts_ref.shape[2]):
                term = parts_ref[g, at, p]
                total = term if total is None else total + term
        columns.append(total)
    scores = jnp.concatenate(columns, axis=0)
    live = scores > 0.5 * DEAD
    peak = jnp.max(scores, axis=1, keepdims=True)
    denom = jnp.sum(jnp.where(live, jnp.exp(scores - peak), 0.0), axis=1, keepdims=True)
    logprob = jnp.where(live, scores - peak - jnp.log(denom), 0.0)
    count = board_ref.shape[1]
    member = lax.broadcasted_iota(jnp.int32, (scores.shape[0], count), 0) == board_ref[...]
    member = jnp.where(member, 1.0, 0.0).astype(BF16)
    found = jnp.zeros((plan.slots, count), F32)
    for _ in range(3):
        rounded = logprob.astype(BF16)
        found = found + matmul(rounded, member, TN)
        logprob = logprob - rounded.astype(F32)
    at = lax.broadcasted_iota(jnp.int32, (plan.slots, count), 0) == slot_ref[...]
    out_ref[...] = jnp.sum(jnp.where(at, found, 0.0), axis=0, keepdims=True)


def untouched():
    return pl.BlockSpec(memory_space=pl.ANY)


def local_call(kernel, place, args, outs, scratch=(), mib=40, copied=(), flops=0, nbytes=0, aliases=None):
    vmem = pl.BlockSpec(memory_space=pltpu.VMEM)
    return pl.pallas_call(
        kernel,
        out_shape=outs,
        in_specs=[pl.BlockSpec(memory_space=pltpu.SMEM)]
        + [untouched() if at in copied else vmem for at in range(len(args))],
        out_specs=jax.tree.map(lambda x: vmem, outs),
        scratch_shapes=scratch,
        input_output_aliases=aliases or {},
        compiler_params=limits(mib),
        cost_estimate=cost(flops, nbytes),
    )(place, *args)


def cost(flops, nbytes):
    return pl.CostEstimate(flops=int(flops), bytes_accessed=int(nbytes), transcendentals=0)


def swap(x, names, size, step):
    return lax.ppermute(x, names, [(at, at ^ step) for at in range(size)])


def shape(dims, dtype):
    return jax.ShapeDtypeStruct(tuple(dims), dtype)


def turn_table(position):
    frequency = THETA ** (-2.0 * np.arange(HALF, dtype=np.float32) / HD)
    angles = np.float32(position) * frequency.astype(np.float32)
    return np.stack([np.cos(angles), np.sin(angles)], axis=1).astype(np.float32)


def per_device(prefix_kv, move_ids, move_board, move_table, norm_gain, w_query, w_keyval, w_score):
    row_count = move_ids.shape[0]
    boards_here, prefix_len, _ = prefix_kv.shape
    moves, width = move_table.shape
    groups, line, pair = lax.axis_size("groups"), lax.axis_size("line"), lax.axis_size("pair")
    board_total = boards_here * line * pair
    capacity = max(2, (2 * row_count + board_total - 1) // board_total)
    heads = w_query.shape[1] // HD
    plan = Plan(groups, line, pair, heads, capacity, pair * boards_here)
    depth = w_query.shape[0]
    group_at = lax.axis_index("groups").astype(jnp.int32)
    line_at = lax.axis_index("line").astype(jnp.int32)
    pair_at = lax.axis_index("pair").astype(jnp.int32)
    place = jnp.stack([group_at, line_at, line_at * pair + pair_at, group_at * pair + pair_at])
    ws = w_score.reshape(heads, HD)
    slab_axes = ("groups", "pair")
    board_row = move_board.reshape(1, row_count)

    half_cols = w_query.shape[1] // groups
    packed = local_call(
        functools.partial(pack_weights, plan),
        group_at.reshape(1),
        (w_query, w_keyval, ws, board_row, move_ids.reshape(1, row_count)),
        shape((plan.peers, plan.rows, depth), BF16),
        [
            pltpu.VMEM((depth, half_cols), BF16),
            pltpu.VMEM((depth, 2 * HD), BF16),
            pltpu.VMEM((heads, HD), BF16),
            pltpu.VMEM((1, row_count), jnp.int32),
            pltpu.VMEM((1, row_count), jnp.int32),
            pltpu.VMEM((plan.peers * plan.rows, half_cols + 2 * HD), F32),
            pltpu.SemaphoreType.DMA((5,)),
        ],
        62,
        range(5),
    )
    weights = lax.all_to_all(packed, ("line", "pair"), split_axis=0, concat_axis=0, tiled=True)

    keys = shape((boards_here + 1, prefix_len, HD), BF16)
    payload, slot_row = local_call(
        functools.partial(pack_prefix, plan),
        place,
        (prefix_kv, ws, board_row, packed),
        (keys, shape((1, row_count), jnp.int32)),
        [
            pltpu.VMEM((boards_here, prefix_len, HD), BF16),
            pltpu.VMEM((heads, HD), BF16),
            pltpu.VMEM((1, row_count), jnp.int32),
            pltpu.SemaphoreType.DMA((4,)),
        ],
        56,
        range(4),
    )
    beside = swap(payload, slab_axes, plan.slab, 1)
    across = swap(payload, slab_axes, plan.slab, 2)

    block = min(moves, 256)
    steps = moves // block
    normed = pl.pallas_call(
        normalize,
        out_shape=[shape((block, width), BF16)] * steps,
        grid=(steps,),
        in_specs=[
            pl.BlockSpec((block, width), lambda i: (i, 0)),
            pl.BlockSpec((width // HD, HD), lambda i: (0, 0)),
            untouched(),
        ],
        out_specs=[untouched()] * steps,
        scratch_shapes=[
            pltpu.VMEM((1, width), F32),
            pltpu.VMEM((2, block, width), BF16),
            pltpu.SemaphoreType.DMA((2,)),
        ],
        compiler_params=limits(58),
        cost_estimate=cost(moves * width, moves * width // 4),
    )(move_table, norm_gain.reshape(width // HD, HD), packed)
    turns = turn_table(prefix_len).reshape(line, 1, plan.pairs, 2)
    turns = np.tile(turns, (1, plan.mine, 1, 1)).reshape(line, plan.mine * plan.pairs, 2)
    flat = weights.transpose(1, 0, 2).reshape(plan.rows, width) if depth % HD else weights
    sent = (plan.line_rows, moves)
    outs = (shape(sent if plan.direct else (line, *sent), BF16), shape((plan.mine, moves), F32))
    filled, ready = (), None
    for step in range(steps):
        made = local_call(
            functools.partial(project, plan, slice(step * block, (step + 1) * block), step == 0),
            place,
            (flat, normed[step], jnp.asarray(turns), *filled),
            [*outs, shape((8, HD), F32)] if step == 0 else list(outs),
            (),
            16,
            (),
            2 * block * width * 1024,
            block * width,
            {4: 0, 5: 1} if filled else None,
        )
        filled = made[:2]
        ready = made[2] if step == 0 else ready
    queries, own_values = filled
    listed = local_call(
        functools.partial(read_lists, plan),
        place,
        (weights, ready),
        shape((plan.share, plan.slots), F32),
        copied=(1,),
    )
    other = swap(listed, slab_axes, plan.slab, pair)
    beside = tied(beside, other)
    queries = tied(queries, beside, across)
    if plan.direct:
        queries = [queries] + [swap(queries, "line", line, step) for step in range(1, line)]
    else:
        queries = lax.all_to_all(queries, "line", split_axis=0, concat_axis=0, tiled=True)
        queries = [queries.reshape(line * plan.line_rows, moves)]
    diagonal = swap(beside, slab_axes, plan.slab, 2)

    query_rows = plan.mine * HD
    back = plan.peers * lax.axis_size("tensor")
    chosen, folds = local_call(
        functools.partial(prepare, plan),
        place,
        (listed, other, payload, beside, across),
        (
            shape((boards_here, moves, plan.slab * plan.slots), BF16),
            shape((plan.slab - 1, boards_here, prefix_len, plan.mine * plan.slots), F32),
        ),
        mib=20,
        flops=10**9,
        nbytes=10**6,
    )
    parts = local_call(
        functools.partial(attend, plan),
        place,
        (own_values, listed, other, chosen, folds, payload, beside, across, diagonal, *queries),
        shape((groups, back, plan.share, plan.slots), F32),
        [
            pltpu.VMEM((query_rows + 16, moves), BF16),
            pltpu.VMEM((16, moves), F32),
            pltpu.VMEM((plan.slab, boards_here, plan.slots), F32),
            pltpu.VMEM((query_rows + 16, plan.slab * plan.slots), F32),
            pltpu.VMEM((query_rows + 16, plan.slab * plan.slots), F32),
        ],
        24,
    )
    parts = lax.all_to_all(
        parts.reshape(groups * back, plan.share, plan.slots),
        ("groups", "line", "pair", "tensor"),
        split_axis=0,
        concat_axis=0,
        tiled=True,
    )
    parts = parts.reshape(groups, line, back // line, plan.share, plan.slots)
    logprob = pl.pallas_call(
        functools.partial(finish, plan), out_shape=shape((1, row_count), F32), compiler_params=limits(VMEM_MIB)
    )(parts, board_row, slot_row)
    return logprob.reshape(row_count)


def solution(mesh):
    order = ("groups", "dp", "tensor")
    assert mesh.axis_names == order
    pair = 2
    groups, peers, tensor = (mesh.shape[name] for name in order)
    fine = Mesh(mesh.devices.reshape(groups, peers // pair, pair, tensor), ("groups", "line", "pair", "tensor"))
    rows = ("groups", "line", "pair")
    placed = (
        P(rows, None, "tensor"),
        P(rows),
        P(rows, None),
        P(),
        P(),
        P(("line", "pair"), "tensor"),
        P(("line", "pair"), "tensor"),
        P("tensor"),
    )
    return jax.shard_map(per_device, mesh=fine, in_specs=placed, out_specs=P(rows), check_vma=False)
```

```python
import functools
import math

import jax
import jax.numpy as jnp
import numpy as np
from jax import lax
from jax.experimental import pallas as pl
from jax.experimental.pallas import tpu as pltpu
from jax.sharding import Mesh
from jax.sharding import PartitionSpec as P

HD = 128
HALF = HD // 2
EPS = 1e-06
THETA = 5000000.0
DEAD = -1e30
VMEM_MIB = 52
GROUP, LINE, PEER, SLAB = range(4)

F32 = jnp.float32
BF16 = jnp.bfloat16

NN = (((1,), (0,)), ((), ()))
NT = (((1,), (1,)), ((), ()))
TN = (((0,), (0,)), ((), ()))


def matmul(a, b, dims=NN):
    return lax.dot_general(a, b, dims, preferred_element_type=F32)


def limits(mib):
    return pltpu.CompilerParams(vmem_limit_bytes=mib * 1024 * 1024)


class Plan:
    def __init__(self, groups, line, pair, heads, capacity, share):
        self.groups, self.line, self.pair = groups, line, pair
        self.peers = line * pair
        self.slab = groups * pair
        self.heads = heads
        self.mine = heads // self.slab
        self.pairs = HALF // line
        self.q_rows = self.mine * 2 * self.pairs
        self.k_rows = 2 * self.pairs
        self.fold_at = self.q_rows + self.k_rows
        self.list_at = self.fold_at + self.mine
        self.rows = -(-(self.list_at + 1) // 8) * 8
        self.line_rows = -(-(self.q_rows + 2 * self.mine) // 8) * 8
        self.capacity = capacity
        self.share = share
        self.slots = self.peers * capacity
        self.direct = line <= 4


def pack_weights(plan, place_ref, wq_hbm, wkv_hbm, ws_hbm, board_hbm, ids_hbm, *rest):
    out_ref, wq, wkv, ws_ref, board_ref, ids_ref, pick, sems = rest
    group = place_ref[0]
    rows, half_cols = plan.rows, wq.shape[1]
    columns_here = pl.ds(pl.multiple_of(group * half_cols, HD), half_cols)
    copies = (
        pltpu.make_async_copy(ws_hbm, ws_ref, sems.at[0]),
        pltpu.make_async_copy(board_hbm, board_ref, sems.at[1]),
        pltpu.make_async_copy(ids_hbm, ids_ref, sems.at[2]),
        pltpu.make_async_copy(wq_hbm.at[:, columns_here], wq, sems.at[3]),
        pltpu.make_async_copy(wkv_hbm, wkv, sems.at[4]),
    )
    for copy in copies:
        copy.start()
    for copy in copies[:3]:
        copy.wait()
    r = lax.broadcasted_iota(jnp.int32, (rows, 1), 0)
    part = r // (plan.mine * plan.pairs)
    head = (r // plan.pairs) % plan.mine
    entry = r % plan.pairs
    is_q = r < plan.q_rows
    k_at = r - plan.q_rows
    is_k = (k_at >= 0) & (k_at < plan.k_rows)
    f_at = r - plan.fold_at
    is_f = (f_at >= 0) & (f_at < plan.mine)
    q_lane = lax.broadcasted_iota(jnp.int32, (rows, half_cols), 1)
    k_lane = lax.broadcasted_iota(jnp.int32, (rows, HD), 1)
    ws = ws_ref[...].astype(F32)

    def fill(peer, carry):
        line, pair = peer // plan.pair, peer % plan.pair
        column = (pair * plan.mine + head) * HD + part * HALF + line * plan.pairs + entry
        column = jnp.where(is_q, column, -1)
        at = pl.ds(pl.multiple_of(peer * rows, 8), rows)
        pick[at, :half_cols] = jnp.where(q_lane == column, 1.0, 0.0)
        k_column = (k_at // plan.pairs) * HALF + line * plan.pairs + k_at % plan.pairs
        k_column = jnp.where(is_k, k_column, -1)
        pick[at, half_cols : half_cols + HD] = jnp.where(k_lane == k_column, 1.0, 0.0)
        fold = jnp.zeros((rows, HD), F32)
        my_head = jnp.where(is_f, (group * plan.pair + pair) * plan.mine + f_at, -1)
        for h in range(plan.heads):
            fold = jnp.where(my_head == h, ws[h : h + 1], fold)
        pick[at, half_cols + HD :] = fold
        return carry

    lax.fori_loop(0, plan.peers, fill, 0, unroll=plan.peers <= 8)

    count, depth = board_ref.shape[1], wq.shape[0]
    board_row = board_ref[...]
    board_col = jnp.broadcast_to(board_row.astype(F32), (8, count)).T[:, 0:1].astype(jnp.int32)
    own = lax.broadcasted_iota(jnp.int32, (count, count), 0)
    other = lax.broadcasted_iota(jnp.int32, (count, count), 1)
    ahead = jnp.where((board_col == board_row) & (other < own), 1.0, 0.0)
    rank = jnp.sum(ahead, axis=1, keepdims=True).astype(jnp.int32)
    move = ids_ref[...] + 1
    boards, span = plan.line * plan.share, plan.share * plan.capacity
    member = lax.broadcasted_iota(jnp.int32, (boards, count), 0) == board_row
    parts = [jnp.where(member, part.astype(F32), 0.0) for part in (move // 64, move % 64)]
    lane = lax.broadcasted_iota(jnp.int32, (count, depth), 1)
    ranked = jnp.where(rank == (lane % span) % plan.capacity, 1.0, 0.0).astype(BF16)
    found = matmul(jnp.concatenate(parts, axis=0).astype(BF16), ranked)
    lane = lax.broadcasted_iota(jnp.int32, (2 * boards, depth), 1)
    row = lax.broadcasted_iota(jnp.int32, (2 * boards, depth), 0)
    keep = (row // boards == lane // span) & (row % plan.share == (lane % span) // plan.capacity)
    found = jnp.where(keep, found, 0.0)
    lists = []
    for line in range(plan.line):
        at = line * plan.share
        both = found[at : at + plan.share] + found[boards + at : boards + at + plan.share]
        lists.append(jnp.sum(both, axis=0, keepdims=True))

    for copy in copies[3:]:
        copy.wait()
    left = pick[...].astype(BF16)
    total = matmul(left[:, :half_cols], wq[...], NT) + matmul(left[:, half_cols:], wkv[...], NT)
    for peer in range(plan.peers):
        mine = total[peer * rows : (peer + 1) * rows]
        out_ref[peer] = jnp.where(r == plan.list_at, lists[peer // plan.pair], mine).astype(BF16)


def normalize(table_ref, gain_ref, after_ref, *refs):
    *outs, gain, held, sems = refs
    here = pl.program_id(0)

    @pl.when(here == 0)
    def _():
        rows = gain_ref[...].astype(F32)
        gain[...] = jnp.concatenate([rows[r : r + 1] for r in range(rows.shape[0])], axis=1)

    def copy(step):
        return pltpu.make_async_copy(held.at[step % 2], outs[step], sems.at[step % 2])

    def one(step):
        if step >= 2:
            copy(step - 2).wait()
        half = table_ref.shape[0] // 2
        for at in (slice(0, half), slice(half, 2 * half)):
            raw = table_ref[at].astype(F32)
            inverse = lax.rsqrt(jnp.mean(raw * raw, axis=-1, keepdims=True) + EPS)
            held[step % 2, at] = (raw * inverse * gain[...]).astype(BF16)
        copy(step).start()
        if step == len(outs) - 1:
            for last in range(max(0, step - 1), step + 1):
                copy(last).wait()

    for step in range(len(outs)):
        pl.when(here == step)(functools.partial(one, step))


def read_lists(plan, w_ref, out_ref):
    share, capacity, peers = plan.share, plan.capacity, plan.peers
    span = share * capacity
    if len(w_ref.shape) == 3:
        rows = [w_ref[s].astype(F32)[plan.list_at : plan.list_at + 1] for s in range(peers)]
    else:
        row = w_ref[...].astype(F32)[plan.list_at : plan.list_at + 1]
        rows = [row[:, s * 2 * span : (s + 1) * 2 * span] for s in range(peers)]
    rows = jnp.concatenate(rows, axis=0)
    lane = lax.broadcasted_iota(jnp.int32, (share * peers, 2 * span), 1)
    row = lax.broadcasted_iota(jnp.int32, (share * peers, 2 * span), 0)
    lane = jnp.where(lane < span, lane, lane - span)
    spread = jnp.concatenate([rows] * share, axis=0)
    spread = jnp.where(lane // capacity == row // peers, spread, 0.0).astype(BF16)
    c = lax.broadcasted_iota(jnp.int32, (2 * span, plan.slots), 0)
    slot = lax.broadcasted_iota(jnp.int32, (2 * span, plan.slots), 1)
    scale = jnp.where(c < span, 64.0, 1.0)
    place = jnp.where(c % capacity == slot % capacity, scale, 0.0).astype(BF16)
    listed = matmul(spread, place)
    row = lax.broadcasted_iota(jnp.int32, listed.shape, 0)
    slot = lax.broadcasted_iota(jnp.int32, listed.shape, 1)
    listed = jnp.where(slot // capacity == row % peers, listed, 0.0)
    out_ref[...] = jnp.sum(listed.reshape(share, peers, plan.slots), axis=1)


def project(plan, at, lists, place_ref, w_ref, normed_ref, turn_ref, *refs):
    if lists:
        *refs, list_ref = refs
        read_lists(plan, w_ref, list_ref)
    q_ref, vo_ref = refs[-2:]
    if len(w_ref.shape) == 3:
        depth = w_ref.shape[2]
        total = None
        for s in range(w_ref.shape[0]):
            term = matmul(w_ref[s], normed_ref[:, s * depth : (s + 1) * depth], NT)
            total = term if total is None else total + term
    else:
        total = matmul(w_ref[...], normed_ref[...], NT)
    turns = turn_ref[place_ref[LINE]]
    half, k_half = plan.q_rows // 2, plan.k_rows // 2
    cosine, sine = turns[:, 0:1], turns[:, 1:2]
    cos_k, sin_k = cosine[:k_half], sine[:k_half]
    first, second = total[:half], total[half : 2 * half]
    f_first = (first * cosine - second * sine).astype(BF16).astype(F32)
    f_second = (second * cosine + first * sine).astype(BF16).astype(F32)
    first, second = total[plan.q_rows : plan.q_rows + k_half], total[plan.q_rows + k_half : plan.fold_at]
    k_first = (first * cos_k - second * sin_k).astype(BF16).astype(F32)
    k_second = (second * cos_k + first * sin_k).astype(BF16).astype(F32)
    logits, tails = [], []
    for h in range(plan.mine):
        own = slice(h * k_half, (h + 1) * k_half)
        logit = jnp.sum(f_first[own] * k_first + f_second[own] * k_second, axis=0, keepdims=True)
        logits.append(logit.astype(BF16).astype(F32))
        tails.append(logit - logits[-1])
    pad = plan.line_rows - plan.q_rows - 2 * plan.mine
    pieces = [f_first, f_second, *logits, *tails]
    if pad:
        pieces.append(jnp.zeros((pad, total.shape[1]), F32))
    out = jnp.concatenate(pieces, axis=0).astype(BF16)
    if plan.direct:
        q_ref[:, at] = out
    else:
        for line in range(plan.line):
            q_ref[line, :, at] = out
    vo_ref[:, at] = total[plan.fold_at : plan.list_at]


def tied(x, *others):
    return pl.pallas_call(
        lambda *refs: None,
        out_shape=shape(x.shape, x.dtype),
        in_specs=[untouched()] * (1 + len(others)),
        out_specs=untouched(),
        input_output_aliases={0: 0},
        compiler_params=limits(1),
        cost_estimate=cost(0, 0),
    )(x, *others)


def pack_prefix(plan, place_ref, prefix_hbm, ws_hbm, board_hbm, after_ref, out_ref, slot_ref, *scratch):
    values, ws_ref, board_ref, sems = scratch
    boards = values.shape[0]
    heads = plan.heads
    copies = (
        pltpu.make_async_copy(board_hbm, board_ref, sems.at[0]),
        pltpu.make_async_copy(ws_hbm, ws_ref, sems.at[1]),
        pltpu.make_async_copy(prefix_hbm.at[:, :, pl.ds(HD, HD)], values, sems.at[2]),
        pltpu.make_async_copy(prefix_hbm.at[:, :, pl.ds(0, HD)], out_ref.at[pl.ds(0, boards)], sems.at[3]),
    )
    for copy in copies:
        copy.start()
    copies[0].wait()
    count = board_ref.shape[1]
    board_row = board_ref[...]
    board_col = jnp.broadcast_to(board_row.astype(F32), (8, count)).T[:, 0:1].astype(jnp.int32)
    other = lax.broadcasted_iota(jnp.int32, (count, count), 0)
    own = lax.broadcasted_iota(jnp.int32, (count, count), 1)
    rank = jnp.sum(jnp.where((board_col == board_row) & (other < own), 1.0, 0.0), axis=0, keepdims=True)
    slot_ref[...] = rank.astype(jnp.int32) + place_ref[PEER] * plan.capacity

    copies[1].wait()
    span = HD // boards
    ws = jnp.concatenate([ws_ref[...].astype(F32)] * (HD // heads), axis=0)
    row = lax.broadcasted_iota(jnp.int32, (HD, 1), 0)
    copies[2].wait()
    fold = None
    for board in range(boards):
        keep = (row // span == board) & (row % span < 2 * heads)
        term = matmul(values[board], jnp.where(keep, ws, 0.0).astype(BF16), NT)
        fold = term if fold is None else fold + term
    rounded = fold.astype(BF16).astype(F32)
    lane = lax.broadcasted_iota(jnp.int32, fold.shape, 1)
    out_ref[boards] = jnp.where(lane % span < heads, rounded, fold - rounded).astype(BF16)
    copies[3].wait()


def fold_columns(plan, here, block, board, boards, heads):
    lanes = plan.mine * plan.slots
    row = lax.broadcasted_iota(jnp.int32, (HD, lanes), 0) - board * (HD // boards)
    head = here * plan.mine + lax.broadcasted_iota(jnp.int32, (HD, lanes), 1) // plan.slots
    pick = jnp.where((row == head) | (row == head + heads), 1.0, 0.0).astype(BF16)
    return matmul(block, pick)


def prepare(plan, place_ref, own_ref, other_ref, *rest):
    *prefix_refs, chosen_ref, fold_ref = rest
    here = place_ref[SLAB]
    boards, moves = chosen_ref.shape[0], chosen_ref.shape[1]
    move_at = lax.broadcasted_iota(jnp.int32, (moves, plan.slots), 0) + 1

    def step(board, carry):
        for j in range(plan.slab):
            place = ((here ^ j) % plan.pair) * boards + board
            row = (own_ref, other_ref)[j // plan.pair][pl.ds(place, 1), :].astype(jnp.int32)
            at = slice(j * plan.slots, (j + 1) * plan.slots)
            chosen_ref[board, :, at] = jnp.where(move_at == row, 1.0, 0.0).astype(BF16)
        for j, prefix_ref in enumerate(prefix_refs):
            fold_ref[j, board] = fold_columns(plan, here, prefix_ref[boards], board, boards, plan.heads)
        return carry

    lax.fori_loop(0, boards, step, 0)


def attend(plan, place_ref, vo_ref, own_ref, other_ref, chosen_ref, fold_ref, *rest):
    prefix_refs, rest = rest[: plan.slab], rest[plan.slab :]
    *q_refs, out_ref, table, extra, scores, taken_even, taken_odd = rest
    here = place_ref[SLAB]
    mine, heads, slots = plan.mine, plan.heads, plan.slots
    moves = vo_ref.shape[1]
    boards = prefix_refs[0].shape[0] - 1
    query_rows = mine * HD

    mixed = None
    for step, q_ref in enumerate(q_refs):
        r = lax.broadcasted_iota(jnp.int32, (query_rows + 8, q_ref.shape[0]), 0)
        c = lax.broadcasted_iota(jnp.int32, (query_rows + 8, q_ref.shape[0]), 1)
        line, at = (place_ref[LINE] ^ step, c) if plan.direct else (c // plan.line_rows, c % plan.line_rows)
        part, head, entry = at // (mine * plan.pairs), (at // plan.pairs) % mine, at % plan.pairs
        goes = jnp.where(at < plan.q_rows, head * HD + part * HALF + line * plan.pairs + entry, -1)
        tail = at - plan.q_rows
        goes = jnp.where((tail >= 0) & (tail < 2 * mine), query_rows + tail % mine, goes)
        term = matmul(jnp.where(r == goes, 1.0, 0.0).astype(BF16), q_ref[...])
        mixed = term if mixed is None else mixed + term
    table[:query_rows] = mixed[:query_rows].astype(BF16)
    extra[...] = jnp.zeros_like(extra)
    for place, value in ((0, mixed[query_rows : query_rows + mine]), (2 * mine, vo_ref[...])):
        rounded = value.astype(BF16).astype(F32)
        extra[place : place + mine] = rounded
        extra[place + mine : place + 2 * mine] = value - rounded
    table[query_rows:] = extra[...].astype(BF16)

    scale = math.log2(math.e) / math.sqrt(HD)
    def per_head(x, base):
        pieces = [x[base + h : base + h + 1] + x[base + mine + h : base + mine + h + 1] for h in range(mine)]
        return jnp.concatenate(pieces, axis=1)

    def moves_of(j, board):
        place = ((here ^ j) % plan.pair) * boards + board
        return (own_ref, other_ref)[j // plan.pair][pl.ds(place, 1), :].astype(jnp.int32)

    def gather(board, taken):
        taken[...] = matmul(table[...], chosen_ref[board])

    def score_board(board, taken):
        for j in range(plan.slab):
            x = taken[:, j * slots : (j + 1) * slots]
            q = jnp.concatenate([x[h * HD : (h + 1) * HD].astype(BF16) for h in range(mine)], axis=1)
            logits = matmul(prefix_refs[j][board], q)
            if j < plan.slab - 1:
                fold = fold_ref[j, board]
            else:
                fold = fold_columns(plan, here, prefix_refs[j][boards], board, boards, heads)
            own_logit = per_head(x, query_rows)
            own_value = per_head(x, query_rows + 2 * mine)
            peak = jnp.maximum(jnp.max(logits, axis=0, keepdims=True), own_logit)
            weight = jnp.exp2((logits - peak) * scale)
            own_weight = jnp.exp2((own_logit - peak) * scale)
            denom = jnp.sum(weight, axis=0, keepdims=True) + own_weight
            value = (jnp.sum(weight * fold, axis=0, keepdims=True) + own_value * own_weight) / denom
            score = sum(value[:, h * slots : (h + 1) * slots] for h in range(mine))
            scores[here ^ j, pl.ds(board, 1), :] = jnp.where(moves_of(j, board) > 0, score, DEAD)

    gather(0, taken_even)

    def step(at, carry):
        board = 2 * at
        gather(jnp.minimum(board + 1, boards - 1), taken_odd)
        score_board(board, taken_even)
        gather(jnp.minimum(board + 2, boards - 1), taken_even)
        score_board(jnp.minimum(board + 1, boards - 1), taken_odd)
        return carry

    lax.fori_loop(0, -(-boards // 2), step, 0)
    for g in range(plan.groups):
        both = jnp.concatenate([scores[g * plan.pair + p] for p in range(plan.pair)], axis=0)
        for copy in range(out_ref.shape[1]):
            out_ref[g, copy] = both


def finish(plan, parts_ref, board_ref, slot_ref, out_ref):
    line = parts_ref.shape[1]
    columns = []
    for at in range(line):
        total = None
        for g in range(parts_ref.shape[0]):
            for p in range(parts_ref.shape[2]):
                term = parts_ref[g, at, p]
                total = term if total is None else total + term
        columns.append(total)
    scores = jnp.concatenate(columns, axis=0)
    live = scores > 0.5 * DEAD
    peak = jnp.max(scores, axis=1, keepdims=True)
    denom = jnp.sum(jnp.where(live, jnp.exp(scores - peak), 0.0), axis=1, keepdims=True)
    logprob = jnp.where(live, scores - peak - jnp.log(denom), 0.0)
    count = board_ref.shape[1]
    member = lax.broadcasted_iota(jnp.int32, (scores.shape[0], count), 0) == board_ref[...]
    member = jnp.where(member, 1.0, 0.0).astype(BF16)
    found = jnp.zeros((plan.slots, count), F32)
    for _ in range(3):
        rounded = logprob.astype(BF16)
        found = found + matmul(rounded, member, TN)
        logprob = logprob - rounded.astype(F32)
    at = lax.broadcasted_iota(jnp.int32, (plan.slots, count), 0) == slot_ref[...]
    out_ref[...] = jnp.sum(jnp.where(at, found, 0.0), axis=0, keepdims=True)


def untouched():
    return pl.BlockSpec(memory_space=pl.ANY)


def local_call(kernel, place, args, outs, scratch=(), mib=40, copied=(), flops=0, nbytes=0, aliases=None):
    vmem = pl.BlockSpec(memory_space=pltpu.VMEM)
    return pl.pallas_call(
        kernel,
        out_shape=outs,
        in_specs=[pl.BlockSpec(memory_space=pltpu.SMEM)]
        + [untouched() if at in copied else vmem for at in range(len(args))],
        out_specs=jax.tree.map(lambda x: vmem, outs),
        scratch_shapes=scratch,
        input_output_aliases=aliases or {},
        compiler_params=limits(mib),
        cost_estimate=cost(flops, nbytes),
    )(place, *args)


def cost(flops, nbytes):
    return pl.CostEstimate(flops=int(flops), bytes_accessed=int(nbytes), transcendentals=0)


def swap(x, names, size, step):
    return lax.ppermute(x, names, [(at, at ^ step) for at in range(size)])


def shape(dims, dtype):
    return jax.ShapeDtypeStruct(tuple(dims), dtype)


def turn_table(position):
    frequency = THETA ** (-2.0 * np.arange(HALF, dtype=np.float32) / HD)
    angles = np.float32(position) * frequency.astype(np.float32)
    return np.stack([np.cos(angles), np.sin(angles)], axis=1).astype(np.float32)


def per_device(prefix_kv, move_ids, move_board, move_table, norm_gain, w_query, w_keyval, w_score):
    row_count = move_ids.shape[0]
    boards_here, prefix_len, _ = prefix_kv.shape
    moves, width = move_table.shape
    groups, line, pair = lax.axis_size("groups"), lax.axis_size("line"), lax.axis_size("pair")
    board_total = boards_here * line * pair
    capacity = max(2, (2 * row_count + board_total - 1) // board_total)
    heads = w_query.shape[1] // HD
    plan = Plan(groups, line, pair, heads, capacity, pair * boards_here)
    depth = w_query.shape[0]
    group_at = lax.axis_index("groups").astype(jnp.int32)
    line_at = lax.axis_index("line").astype(jnp.int32)
    pair_at = lax.axis_index("pair").astype(jnp.int32)
    place = jnp.stack([group_at, line_at, line_at * pair + pair_at, group_at * pair + pair_at])
    ws = w_score.reshape(heads, HD)
    slab_axes = ("groups", "pair")
    board_row = move_board.reshape(1, row_count)

    half_cols = w_query.shape[1] // groups
    packed = local_call(
        functools.partial(pack_weights, plan),
        group_at.reshape(1),
        (w_query, w_keyval, ws, board_row, move_ids.reshape(1, row_count)),
        shape((plan.peers, plan.rows, depth), BF16),
        [
            pltpu.VMEM((depth, half_cols), BF16),
            pltpu.VMEM((depth, 2 * HD), BF16),
            pltpu.VMEM((heads, HD), BF16),
            pltpu.VMEM((1, row_count), jnp.int32),
            pltpu.VMEM((1, row_count), jnp.int32),
            pltpu.VMEM((plan.peers * plan.rows, half_cols + 2 * HD), F32),
            pltpu.SemaphoreType.DMA((5,)),
        ],
        62,
        range(5),
    )
    weights = lax.all_to_all(packed, ("line", "pair"), split_axis=0, concat_axis=0, tiled=True)

    keys = shape((boards_here + 1, prefix_len, HD), BF16)
    payload, slot_row = local_call(
        functools.partial(pack_prefix, plan),
        place,
        (prefix_kv, ws, board_row, packed),
        (keys, shape((1, row_count), jnp.int32)),
        [
            pltpu.VMEM((boards_here, prefix_len, HD), BF16),
            pltpu.VMEM((heads, HD), BF16),
            pltpu.VMEM((1, row_count), jnp.int32),
            pltpu.SemaphoreType.DMA((4,)),
        ],
        56,
        range(4),
    )
    beside = swap(payload, slab_axes, plan.slab, 1)
    across = swap(payload, slab_axes, plan.slab, 2)

    block = min(moves, 256)
    steps = moves // block
    normed = pl.pallas_call(
        normalize,
        out_shape=[shape((block, width), BF16)] * steps,
        grid=(steps,),
        in_specs=[
            pl.BlockSpec((block, width), lambda i: (i, 0)),
            pl.BlockSpec((width // HD, HD), lambda i: (0, 0)),
            untouched(),
        ],
        out_specs=[untouched()] * steps,
        scratch_shapes=[
            pltpu.VMEM((1, width), F32),
            pltpu.VMEM((2, block, width), BF16),
            pltpu.SemaphoreType.DMA((2,)),
        ],
        compiler_params=limits(58),
        cost_estimate=cost(moves * width, moves * width // 4),
    )(move_table, norm_gain.reshape(width // HD, HD), packed)
    turns = turn_table(prefix_len).reshape(line, 1, plan.pairs, 2)
    turns = np.tile(turns, (1, plan.mine, 1, 1)).reshape(line, plan.mine * plan.pairs, 2)
    flat = weights.transpose(1, 0, 2).reshape(plan.rows, width) if depth % HD else weights
    sent = (plan.line_rows, moves)
    outs = (shape(sent if plan.direct else (line, *sent), BF16), shape((plan.mine, moves), F32))
    waits = {0: across, steps - 1: beside}
    filled, listed = (), None
    for step in range(steps):
        args = (flat, normed[step], jnp.asarray(turns), *filled)
        more = (waits[step],) if step in waits else ()
        lists = [shape((plan.share, plan.slots), F32)] if step == 0 else []
        made = local_call(
            functools.partial(project, plan, slice(step * block, (step + 1) * block), step == 0),
            place,
            (*args, *more),
            [*outs, *lists],
            (),
            16,
            range(len(args), len(args) + len(more)),
            2 * block * width * 1024,
            block * width,
            {4: 0, 5: 1} if filled else None,
        )
        filled = made[:2]
        listed = made[2] if step == 0 else listed
    queries, own_values = filled
    other = swap(listed, slab_axes, plan.slab, pair)
    across = tied(across, listed)
    diagonal = swap(across, slab_axes, plan.slab, 1)
    if plan.direct:
        queries = [queries] + [swap(queries, "line", line, step) for step in range(1, line)]
    else:
        queries = lax.all_to_all(queries, "line", split_axis=0, concat_axis=0, tiled=True)
        queries = [queries.reshape(line * plan.line_rows, moves)]

    query_rows = plan.mine * HD
    back = plan.peers * lax.axis_size("tensor")
    chosen, folds = local_call(
        functools.partial(prepare, plan),
        place,
        (listed, other, payload, beside, across),
        (
            shape((boards_here, moves, plan.slab * plan.slots), BF16),
            shape((plan.slab - 1, boards_here, prefix_len, plan.mine * plan.slots), F32),
        ),
        mib=20,
        flops=10**9,
        nbytes=10**6,
    )
    parts = local_call(
        functools.partial(attend, plan),
        place,
        (own_values, listed, other, chosen, folds, payload, beside, across, diagonal, *queries),
        shape((groups, back, plan.share, plan.slots), F32),
        [
            pltpu.VMEM((query_rows + 16, moves), BF16),
            pltpu.VMEM((16, moves), F32),
            pltpu.VMEM((plan.slab, boards_here, plan.slots), F32),
            pltpu.VMEM((query_rows + 16, plan.slab * plan.slots), F32),
            pltpu.VMEM((query_rows + 16, plan.slab * plan.slots), F32),
        ],
        24,
    )
    parts = lax.all_to_all(
        parts.reshape(groups * back, plan.share, plan.slots),
        ("groups", "line", "pair", "tensor"),
        split_axis=0,
        concat_axis=0,
        tiled=True,
    )
    parts = parts.reshape(groups, line, back // line, plan.share, plan.slots)
    logprob = pl.pallas_call(
        functools.partial(finish, plan), out_shape=shape((1, row_count), F32), compiler_params=limits(VMEM_MIB)
    )(parts, board_row, slot_row)
    return logprob.reshape(row_count)


def solution(mesh):
    order = ("groups", "dp", "tensor")
    assert mesh.axis_names == order
    pair = 2
    groups, peers, tensor = (mesh.shape[name] for name in order)
    fine = Mesh(mesh.devices.reshape(groups, peers // pair, pair, tensor), ("groups", "line", "pair", "tensor"))
    rows = ("groups", "line", "pair")
    placed = (
        P(rows, None, "tensor"),
        P(rows),
        P(rows, None),
        P(),
        P(),
        P(("line", "pair"), "tensor"),
        P(("line", "pair"), "tensor"),
        P("tensor"),
    )
    return jax.shard_map(per_device, mesh=fine, in_specs=placed, out_specs=P(rows), check_vma=False)
```

```python
import functools
import math

import jax
import jax.numpy as jnp
import numpy as np
from jax import lax
from jax.experimental import pallas as pl
from jax.experimental.pallas import tpu as pltpu
from jax.sharding import Mesh
from jax.sharding import PartitionSpec as P

HD = 128
HALF = HD // 2
EPS = 1e-06
THETA = 5000000.0
DEAD = -1e30
VMEM_MIB = 52
GROUP, LINE, PEER, SLAB = range(4)

F32 = jnp.float32
BF16 = jnp.bfloat16

NN = (((1,), (0,)), ((), ()))
NT = (((1,), (1,)), ((), ()))
TN = (((0,), (0,)), ((), ()))


def matmul(a, b, dims=NN):
    return lax.dot_general(a, b, dims, preferred_element_type=F32)


def limits(mib):
    return pltpu.CompilerParams(vmem_limit_bytes=mib * 1024 * 1024)


class Plan:
    def __init__(self, groups, line, pair, heads, capacity, share):
        self.groups, self.line, self.pair = groups, line, pair
        self.peers = line * pair
        self.slab = groups * pair
        self.heads = heads
        self.mine = heads // self.slab
        self.pairs = HALF // line
        self.q_rows = self.mine * 2 * self.pairs
        self.k_rows = 2 * self.pairs
        self.fold_at = self.q_rows + self.k_rows
        self.list_at = self.fold_at + self.mine
        self.rows = -(-(self.list_at + 1) // 8) * 8
        self.line_rows = -(-(self.q_rows + 2 * self.mine) // 8) * 8
        self.capacity = capacity
        self.share = share
        self.slots = self.peers * capacity
        self.direct = line <= 4


def pack_weights(plan, place_ref, wq_hbm, wkv_hbm, ws_hbm, board_hbm, ids_hbm, *rest):
    out_ref, wq, wkv, ws_ref, board_ref, ids_ref, pick, sems = rest
    group = place_ref[0]
    half_cols = wq.shape[1]
    columns_here = pl.ds(pl.multiple_of(group * half_cols, HD), half_cols)
    copies = (
        pltpu.make_async_copy(ws_hbm, ws_ref, sems.at[0]),
        pltpu.make_async_copy(board_hbm, board_ref, sems.at[1]),
        pltpu.make_async_copy(ids_hbm, ids_ref, sems.at[2]),
        pltpu.make_async_copy(wq_hbm.at[:, columns_here], wq, sems.at[3]),
        pltpu.make_async_copy(wkv_hbm, wkv, sems.at[4]),
    )
    for copy in copies:
        copy.start()
    for copy in copies[:3]:
        copy.wait()
    count, depth = board_ref.shape[1], wq.shape[0]
    board_row = board_ref[...]
    board_col = jnp.broadcast_to(board_row.astype(F32), (8, count)).T[:, 0:1].astype(jnp.int32)
    own = lax.broadcasted_iota(jnp.int32, (count, count), 0)
    other = lax.broadcasted_iota(jnp.int32, (count, count), 1)
    ahead = jnp.where((board_col == board_row) & (other < own), 1.0, 0.0)
    rank = jnp.sum(ahead, axis=1, keepdims=True).astype(jnp.int32)
    move = ids_ref[...] + 1
    boards, span = plan.line * plan.share, plan.share * plan.capacity
    member = lax.broadcasted_iota(jnp.int32, (boards, count), 0) == board_row
    parts = [jnp.where(member, part.astype(F32), 0.0) for part in (move // 64, move % 64)]
    lane = lax.broadcasted_iota(jnp.int32, (count, depth), 1)
    ranked = jnp.where(rank == (lane % span) % plan.capacity, 1.0, 0.0).astype(BF16)
    found = matmul(jnp.concatenate(parts, axis=0).astype(BF16), ranked)
    lane = lax.broadcasted_iota(jnp.int32, (2 * boards, depth), 1)
    row = lax.broadcasted_iota(jnp.int32, (2 * boards, depth), 0)
    keep = (row // boards == lane // span) & (row % plan.share == (lane % span) // plan.capacity)
    found = jnp.where(keep, found, 0.0)
    lists = []
    for line in range(plan.line):
        at = line * plan.share
        both = found[at : at + plan.share] + found[boards + at : boards + at + plan.share]
        lists.append(jnp.sum(both, axis=0, keepdims=True))

    if plan.pairs % 16 == 0:
        turn_weights(plan, group, lists, copies[3:], wq, wkv, ws_ref, out_ref)
    else:
        pick_weights(plan, group, lists, copies[3:], wq, wkv, ws_ref, out_ref, pick)


def turn_weights(plan, group, lists, copies, wq, wkv, ws_ref, out_ref):
    for copy in copies:
        copy.wait()
    q = wq[...].T
    k = wkv[:, :HD].T
    folds = matmul(ws_ref[...], wkv[:, HD:], NT)
    row = lax.broadcasted_iota(jnp.int32, folds.shape, 0)
    pairs = plan.pairs
    zeros = jnp.zeros((plan.rows - plan.list_at - 1, folds.shape[1]), F32)
    for pair in range(plan.pair):
        first = (group * plan.pair + pair) * plan.mine
        mine = [jnp.sum(jnp.where(row == first + h, folds, 0.0), axis=0, keepdims=True) for h in range(plan.mine)]
        for line in range(plan.line):
            peer = line * plan.pair + pair
            for part in range(2):
                entry = part * HALF + line * pairs
                for h in range(plan.mine):
                    at = (part * plan.mine + h) * pairs
                    source = (pair * plan.mine + h) * HD + entry
                    out_ref[peer, at : at + pairs] = q[source : source + pairs]
                at = plan.q_rows + part * pairs
                out_ref[peer, at : at + pairs] = k[entry : entry + pairs]
            last = jnp.concatenate([*mine, lists[line], zeros], axis=0)
            out_ref[peer, plan.fold_at :] = last.astype(BF16)


def pick_weights(plan, group, lists, copies, wq, wkv, ws_ref, out_ref, pick):
    rows, half_cols = plan.rows, wq.shape[1]
    r = lax.broadcasted_iota(jnp.int32, (rows, 1), 0)
    part = r // (plan.mine * plan.pairs)
    head = (r // plan.pairs) % plan.mine
    entry = r % plan.pairs
    is_q = r < plan.q_rows
    k_at = r - plan.q_rows
    is_k = (k_at >= 0) & (k_at < plan.k_rows)
    f_at = r - plan.fold_at
    is_f = (f_at >= 0) & (f_at < plan.mine)
    q_lane = lax.broadcasted_iota(jnp.int32, (rows, half_cols), 1)
    k_lane = lax.broadcasted_iota(jnp.int32, (rows, HD), 1)
    ws = ws_ref[...].astype(F32)

    def fill(peer, carry):
        line, pair = peer // plan.pair, peer % plan.pair
        column = (pair * plan.mine + head) * HD + part * HALF + line * plan.pairs + entry
        column = jnp.where(is_q, column, -1)
        at = pl.ds(pl.multiple_of(peer * rows, 8), rows)
        pick[at, :half_cols] = jnp.where(q_lane == column, 1.0, 0.0)
        k_column = (k_at // plan.pairs) * HALF + line * plan.pairs + k_at % plan.pairs
        k_column = jnp.where(is_k, k_column, -1)
        pick[at, half_cols : half_cols + HD] = jnp.where(k_lane == k_column, 1.0, 0.0)
        fold = jnp.zeros((rows, HD), F32)
        my_head = jnp.where(is_f, (group * plan.pair + pair) * plan.mine + f_at, -1)
        for h in range(plan.heads):
            fold = jnp.where(my_head == h, ws[h : h + 1], fold)
        pick[at, half_cols + HD :] = fold
        return carry

    lax.fori_loop(0, plan.peers, fill, 0, unroll=plan.peers <= 8)

    for copy in copies:
        copy.wait()
    left = pick[...].astype(BF16)
    total = matmul(left[:, :half_cols], wq[...], NT) + matmul(left[:, half_cols:], wkv[...], NT)
    for peer in range(plan.peers):
        mine = total[peer * rows : (peer + 1) * rows]
        out_ref[peer] = jnp.where(r == plan.list_at, lists[peer // plan.pair], mine).astype(BF16)


def normalize(table_ref, gain_ref, after_ref, *refs):
    *outs, mark_ref, gain, held, sems = refs
    here = pl.program_id(0)
    block = table_ref.shape[0]
    starts = np.cumsum([0] + [out.shape[0] for out in outs])

    @pl.when(here == 0)
    def _():
        rows = gain_ref[...].astype(F32)
        gain[...] = jnp.concatenate([rows[r : r + 1] for r in range(rows.shape[0])], axis=1)
        mark_ref[...] = jnp.zeros_like(mark_ref)

    def copies(step):
        found = []
        for out, start in zip(outs, starts.tolist()):
            low = max(step * block, start)
            size = min((step + 1) * block, start + out.shape[0]) - low
            if size > 0:
                slot, place = step % 2, len(found)
                source = held.at[slot, pl.ds(low - step * block, size)]
                found.append(pltpu.make_async_copy(source, out.at[pl.ds(low - start, size)], sems.at[slot, place]))
        return found

    steps = int(starts[-1]) // block

    def one(step):
        if step >= 2:
            for copy in copies(step - 2):
                copy.wait()
        half = block // 2
        for at in (slice(0, half), slice(half, 2 * half)):
            raw = table_ref[at].astype(F32)
            inverse = lax.rsqrt(jnp.mean(raw * raw, axis=-1, keepdims=True) + EPS)
            held[step % 2, at] = (raw * inverse * gain[...]).astype(BF16)
        for copy in copies(step):
            copy.start()
        if step == steps - 1:
            for last in range(max(0, step - 1), step + 1):
                for copy in copies(last):
                    copy.wait()

    for step in range(steps):
        pl.when(here == step)(functools.partial(one, step))


def read_lists(plan, w_ref, out_ref):
    share, capacity, peers = plan.share, plan.capacity, plan.peers
    span = share * capacity
    if len(w_ref.shape) == 3:
        rows = [w_ref[s].astype(F32)[plan.list_at : plan.list_at + 1] for s in range(peers)]
    else:
        row = w_ref[...].astype(F32)[plan.list_at : plan.list_at + 1]
        rows = [row[:, s * 2 * span : (s + 1) * 2 * span] for s in range(peers)]
    rows = jnp.concatenate(rows, axis=0)
    lane = lax.broadcasted_iota(jnp.int32, (share * peers, 2 * span), 1)
    row = lax.broadcasted_iota(jnp.int32, (share * peers, 2 * span), 0)
    lane = jnp.where(lane < span, lane, lane - span)
    spread = jnp.concatenate([rows] * share, axis=0)
    spread = jnp.where(lane // capacity == row // peers, spread, 0.0).astype(BF16)
    c = lax.broadcasted_iota(jnp.int32, (2 * span, plan.slots), 0)
    slot = lax.broadcasted_iota(jnp.int32, (2 * span, plan.slots), 1)
    scale = jnp.where(c < span, 64.0, 1.0)
    place = jnp.where(c % capacity == slot % capacity, scale, 0.0).astype(BF16)
    listed = matmul(spread, place)
    row = lax.broadcasted_iota(jnp.int32, listed.shape, 0)
    slot = lax.broadcasted_iota(jnp.int32, listed.shape, 1)
    listed = jnp.where(slot // capacity == row % peers, listed, 0.0)
    out_ref[...] = jnp.sum(listed.reshape(share, peers, plan.slots), axis=1)


def project(plan, at, lists, place_ref, w_ref, normed_ref, turn_ref, *refs):
    if lists:
        *refs, list_ref = refs
        read_lists(plan, w_ref, list_ref)
    q_ref, vo_ref = refs[-2:]
    if len(w_ref.shape) == 3:
        depth = w_ref.shape[2]
        total = None
        for s in range(w_ref.shape[0]):
            term = matmul(w_ref[s], normed_ref[:, s * depth : (s + 1) * depth], NT)
            total = term if total is None else total + term
    else:
        total = matmul(w_ref[...], normed_ref[...], NT)
    turns = turn_ref[place_ref[LINE]]
    half, k_half = plan.q_rows // 2, plan.k_rows // 2
    cosine, sine = turns[:, 0:1], turns[:, 1:2]
    cos_k, sin_k = cosine[:k_half], sine[:k_half]
    first, second = total[:half], total[half : 2 * half]
    f_first = (first * cosine - second * sine).astype(BF16).astype(F32)
    f_second = (second * cosine + first * sine).astype(BF16).astype(F32)
    first, second = total[plan.q_rows : plan.q_rows + k_half], total[plan.q_rows + k_half : plan.fold_at]
    k_first = (first * cos_k - second * sin_k).astype(BF16).astype(F32)
    k_second = (second * cos_k + first * sin_k).astype(BF16).astype(F32)
    logits, tails = [], []
    for h in range(plan.mine):
        own = slice(h * k_half, (h + 1) * k_half)
        logit = jnp.sum(f_first[own] * k_first + f_second[own] * k_second, axis=0, keepdims=True)
        logits.append(logit.astype(BF16).astype(F32))
        tails.append(logit - logits[-1])
    pad = plan.line_rows - plan.q_rows - 2 * plan.mine
    pieces = [f_first, f_second, *logits, *tails]
    if pad:
        pieces.append(jnp.zeros((pad, total.shape[1]), F32))
    out = jnp.concatenate(pieces, axis=0).astype(BF16)
    if plan.direct:
        q_ref[:, at] = out
    else:
        for line in range(plan.line):
            q_ref[line, :, at] = out
    vo_ref[:, at] = total[plan.fold_at : plan.list_at]


def tied(x, *others):
    return pl.pallas_call(
        lambda *refs: None,
        out_shape=shape(x.shape, x.dtype),
        in_specs=[untouched()] * (1 + len(others)),
        out_specs=untouched(),
        input_output_aliases={0: 0},
        compiler_params=limits(1),
        cost_estimate=cost(0, 0),
    )(x, *others)


def pack_prefix(plan, place_ref, prefix_hbm, ws_hbm, board_hbm, after_ref, out_ref, slot_ref, *scratch):
    values, ws_ref, board_ref, sems = scratch
    boards = values.shape[0]
    heads = plan.heads
    copies = (
        pltpu.make_async_copy(board_hbm, board_ref, sems.at[0]),
        pltpu.make_async_copy(ws_hbm, ws_ref, sems.at[1]),
        pltpu.make_async_copy(prefix_hbm.at[:, :, pl.ds(HD, HD)], values, sems.at[2]),
        pltpu.make_async_copy(prefix_hbm.at[:, :, pl.ds(0, HD)], out_ref.at[pl.ds(0, boards)], sems.at[3]),
    )
    for copy in copies:
        copy.start()
    copies[0].wait()
    count = board_ref.shape[1]
    board_row = board_ref[...]
    board_col = jnp.broadcast_to(board_row.astype(F32), (8, count)).T[:, 0:1].astype(jnp.int32)
    other = lax.broadcasted_iota(jnp.int32, (count, count), 0)
    own = lax.broadcasted_iota(jnp.int32, (count, count), 1)
    rank = jnp.sum(jnp.where((board_col == board_row) & (other < own), 1.0, 0.0), axis=0, keepdims=True)
    slot_ref[...] = rank.astype(jnp.int32) + place_ref[PEER] * plan.capacity

    copies[1].wait()
    span = HD // boards
    ws = jnp.concatenate([ws_ref[...].astype(F32)] * (HD // heads), axis=0)
    row = lax.broadcasted_iota(jnp.int32, (HD, 1), 0)
    copies[2].wait()
    fold = None
    for board in range(boards):
        keep = (row // span == board) & (row % span < 2 * heads)
        term = matmul(values[board], jnp.where(keep, ws, 0.0).astype(BF16), NT)
        fold = term if fold is None else fold + term
    rounded = fold.astype(BF16).astype(F32)
    lane = lax.broadcasted_iota(jnp.int32, fold.shape, 1)
    out_ref[boards] = jnp.where(lane % span < heads, rounded, fold - rounded).astype(BF16)
    copies[3].wait()


def fold_columns(plan, here, block, board, boards, heads):
    lanes = plan.mine * plan.slots
    row = lax.broadcasted_iota(jnp.int32, (HD, lanes), 0) - board * (HD // boards)
    head = here * plan.mine + lax.broadcasted_iota(jnp.int32, (HD, lanes), 1) // plan.slots
    pick = jnp.where((row == head) | (row == head + heads), 1.0, 0.0).astype(BF16)
    return matmul(block, pick)


def prepare(plan, place_ref, own_ref, other_ref, *rest):
    *prefix_refs, chosen_ref, fold_ref = rest
    here = place_ref[SLAB]
    boards, moves = chosen_ref.shape[0], chosen_ref.shape[1]
    move_at = lax.broadcasted_iota(jnp.int32, (moves, plan.slots), 0) + 1

    def step(board, carry):
        for j in range(plan.slab):
            place = ((here ^ j) % plan.pair) * boards + board
            row = (own_ref, other_ref)[j // plan.pair][pl.ds(place, 1), :].astype(jnp.int32)
            at = slice(j * plan.slots, (j + 1) * plan.slots)
            chosen_ref[board, :, at] = jnp.where(move_at == row, 1.0, 0.0).astype(BF16)
        for j, prefix_ref in enumerate(prefix_refs):
            fold_ref[j, board] = fold_columns(plan, here, prefix_ref[boards], board, boards, plan.heads)
        return carry

    lax.fori_loop(0, boards, step, 0)


def attend(plan, place_ref, vo_ref, own_ref, other_ref, chosen_ref, fold_ref, *rest):
    prefix_refs, rest = rest[: plan.slab], rest[plan.slab :]
    *q_refs, out_ref, table, extra, scores, taken_even, taken_odd = rest
    here = place_ref[SLAB]
    mine, heads, slots = plan.mine, plan.heads, plan.slots
    moves = vo_ref.shape[1]
    boards = prefix_refs[0].shape[0] - 1
    query_rows = mine * HD

    mixed = None
    for step, q_ref in enumerate(q_refs):
        r = lax.broadcasted_iota(jnp.int32, (query_rows + 8, q_ref.shape[0]), 0)
        c = lax.broadcasted_iota(jnp.int32, (query_rows + 8, q_ref.shape[0]), 1)
        line, at = (place_ref[LINE] ^ step, c) if plan.direct else (c // plan.line_rows, c % plan.line_rows)
        part, head, entry = at // (mine * plan.pairs), (at // plan.pairs) % mine, at % plan.pairs
        goes = jnp.where(at < plan.q_rows, head * HD + part * HALF + line * plan.pairs + entry, -1)
        tail = at - plan.q_rows
        goes = jnp.where((tail >= 0) & (tail < 2 * mine), query_rows + tail % mine, goes)
        term = matmul(jnp.where(r == goes, 1.0, 0.0).astype(BF16), q_ref[...])
        mixed = term if mixed is None else mixed + term
    table[:query_rows] = mixed[:query_rows].astype(BF16)
    extra[...] = jnp.zeros_like(extra)
    for place, value in ((0, mixed[query_rows : query_rows + mine]), (2 * mine, vo_ref[...])):
        rounded = value.astype(BF16).astype(F32)
        extra[place : place + mine] = rounded
        extra[place + mine : place + 2 * mine] = value - rounded
    table[query_rows:] = extra[...].astype(BF16)

    scale = math.log2(math.e) / math.sqrt(HD)
    def per_head(x, base):
        pieces = [x[base + h : base + h + 1] + x[base + mine + h : base + mine + h + 1] for h in range(mine)]
        return jnp.concatenate(pieces, axis=1)

    def moves_of(j, board):
        place = ((here ^ j) % plan.pair) * boards + board
        return (own_ref, other_ref)[j // plan.pair][pl.ds(place, 1), :].astype(jnp.int32)

    def gather(board, taken):
        taken[...] = matmul(table[...], chosen_ref[board])

    def score_board(board, taken):
        for j in range(plan.slab):
            x = taken[:, j * slots : (j + 1) * slots]
            q = jnp.concatenate([x[h * HD : (h + 1) * HD].astype(BF16) for h in range(mine)], axis=1)
            logits = matmul(prefix_refs[j][board], q)
            if j < plan.slab - 1:
                fold = fold_ref[j, board]
            else:
                fold = fold_columns(plan, here, prefix_refs[j][boards], board, boards, heads)
            own_logit = per_head(x, query_rows)
            own_value = per_head(x, query_rows + 2 * mine)
            peak = jnp.maximum(jnp.max(logits, axis=0, keepdims=True), own_logit)
            weight = jnp.exp2((logits - peak) * scale)
            own_weight = jnp.exp2((own_logit - peak) * scale)
            denom = jnp.sum(weight, axis=0, keepdims=True) + own_weight
            value = (jnp.sum(weight * fold, axis=0, keepdims=True) + own_value * own_weight) / denom
            score = sum(value[:, h * slots : (h + 1) * slots] for h in range(mine))
            scores[here ^ j, pl.ds(board, 1), :] = jnp.where(moves_of(j, board) > 0, score, DEAD)

    gather(0, taken_even)

    def step(at, carry):
        board = 2 * at
        gather(jnp.minimum(board + 1, boards - 1), taken_odd)
        score_board(board, taken_even)
        gather(jnp.minimum(board + 2, boards - 1), taken_even)
        score_board(jnp.minimum(board + 1, boards - 1), taken_odd)
        return carry

    lax.fori_loop(0, -(-boards // 2), step, 0)
    for g in range(plan.groups):
        both = jnp.concatenate([scores[g * plan.pair + p] for p in range(plan.pair)], axis=0)
        for copy in range(out_ref.shape[1]):
            out_ref[g, copy] = both


def finish(plan, parts_ref, board_ref, slot_ref, out_ref):
    line = parts_ref.shape[1]
    columns = []
    for at in range(line):
        total = None
        for g in range(parts_ref.shape[0]):
            for p in range(parts_ref.shape[2]):
                term = parts_ref[g, at, p]
                total = term if total is None else total + term
        columns.append(total)
    scores = jnp.concatenate(columns, axis=0)
    live = scores > 0.5 * DEAD
    peak = jnp.max(scores, axis=1, keepdims=True)
    denom = jnp.sum(jnp.where(live, jnp.exp(scores - peak), 0.0), axis=1, keepdims=True)
    logprob = jnp.where(live, scores - peak - jnp.log(denom), 0.0)
    count = board_ref.shape[1]
    member = lax.broadcasted_iota(jnp.int32, (scores.shape[0], count), 0) == board_ref[...]
    member = jnp.where(member, 1.0, 0.0).astype(BF16)
    found = jnp.zeros((plan.slots, count), F32)
    for _ in range(3):
        rounded = logprob.astype(BF16)
        found = found + matmul(rounded, member, TN)
        logprob = logprob - rounded.astype(F32)
    at = lax.broadcasted_iota(jnp.int32, (plan.slots, count), 0) == slot_ref[...]
    out_ref[...] = jnp.sum(jnp.where(at, found, 0.0), axis=0, keepdims=True)


def untouched():
    return pl.BlockSpec(memory_space=pl.ANY)


def local_call(kernel, place, args, outs, scratch=(), mib=40, copied=(), flops=0, nbytes=0, aliases=None):
    vmem = pl.BlockSpec(memory_space=pltpu.VMEM)
    return pl.pallas_call(
        kernel,
        out_shape=outs,
        in_specs=[pl.BlockSpec(memory_space=pltpu.SMEM)]
        + [untouched() if at in copied else vmem for at in range(len(args))],
        out_specs=jax.tree.map(lambda x: vmem, outs),
        scratch_shapes=scratch,
        input_output_aliases=aliases or {},
        compiler_params=limits(mib),
        cost_estimate=cost(flops, nbytes),
    )(place, *args)


def cost(flops, nbytes):
    return pl.CostEstimate(flops=int(flops), bytes_accessed=int(nbytes), transcendentals=0)


def swap(x, names, size, step):
    return lax.ppermute(x, names, [(at, at ^ step) for at in range(size)])


def shape(dims, dtype):
    return jax.ShapeDtypeStruct(tuple(dims), dtype)


def turn_table(position):
    frequency = THETA ** (-2.0 * np.arange(HALF, dtype=np.float32) / HD)
    angles = np.float32(position) * frequency.astype(np.float32)
    return np.stack([np.cos(angles), np.sin(angles)], axis=1).astype(np.float32)


def per_device(prefix_kv, move_ids, move_board, move_table, norm_gain, w_query, w_keyval, w_score):
    row_count = move_ids.shape[0]
    boards_here, prefix_len, _ = prefix_kv.shape
    moves, width = move_table.shape
    groups, line, pair = lax.axis_size("groups"), lax.axis_size("line"), lax.axis_size("pair")
    board_total = boards_here * line * pair
    capacity = max(2, (2 * row_count + board_total - 1) // board_total)
    heads = w_query.shape[1] // HD
    plan = Plan(groups, line, pair, heads, capacity, pair * boards_here)
    depth = w_query.shape[0]
    group_at = lax.axis_index("groups").astype(jnp.int32)
    line_at = lax.axis_index("line").astype(jnp.int32)
    pair_at = lax.axis_index("pair").astype(jnp.int32)
    place = jnp.stack([group_at, line_at, line_at * pair + pair_at, group_at * pair + pair_at])
    ws = w_score.reshape(heads, HD)
    slab_axes = ("groups", "pair")
    board_row = move_board.reshape(1, row_count)

    half_cols = w_query.shape[1] // groups
    packed = local_call(
        functools.partial(pack_weights, plan),
        group_at.reshape(1),
        (w_query, w_keyval, ws, board_row, move_ids.reshape(1, row_count)),
        shape((plan.peers, plan.rows, depth), BF16),
        [
            pltpu.VMEM((depth, half_cols), BF16),
            pltpu.VMEM((depth, 2 * HD), BF16),
            pltpu.VMEM((heads, HD), BF16),
            pltpu.VMEM((1, row_count), jnp.int32),
            pltpu.VMEM((1, row_count), jnp.int32),
            pltpu.VMEM((plan.peers * plan.rows, half_cols + 2 * HD), F32),
            pltpu.SemaphoreType.DMA((5,)),
        ],
        62,
        range(5),
    )
    weights = lax.all_to_all(packed, ("line", "pair"), split_axis=0, concat_axis=0, tiled=True)

    keys = shape((boards_here + 1, prefix_len, HD), BF16)
    payload, slot_row = local_call(
        functools.partial(pack_prefix, plan),
        place,
        (prefix_kv, ws, board_row, packed),
        (keys, shape((1, row_count), jnp.int32)),
        [
            pltpu.VMEM((boards_here, prefix_len, HD), BF16),
            pltpu.VMEM((heads, HD), BF16),
            pltpu.VMEM((1, row_count), jnp.int32),
            pltpu.SemaphoreType.DMA((4,)),
        ],
        56,
        range(4),
    )
    beside = swap(payload, slab_axes, plan.slab, 1)
    across = swap(payload, slab_axes, plan.slab, 2)

    block = min(moves, 256)
    blocks = (moves // 4, moves * 3 // 8, moves * 3 // 8)
    *normed, mark = pl.pallas_call(
        normalize,
        out_shape=[*[shape((size, width), BF16) for size in blocks], shape((8, HD), F32)],
        grid=(moves // block,),
        in_specs=[
            pl.BlockSpec((block, width), lambda i: (i, 0)),
            pl.BlockSpec((width // HD, HD), lambda i: (0, 0)),
            untouched(),
        ],
        out_specs=[*[untouched()] * len(blocks), pl.BlockSpec((8, HD), lambda i: (0, 0))],
        scratch_shapes=[
            pltpu.VMEM((1, width), F32),
            pltpu.VMEM((2, block, width), BF16),
            pltpu.SemaphoreType.DMA((2, 2)),
        ],
        compiler_params=limits(58),
        cost_estimate=cost(moves * width, moves * width // 4),
    )(move_table, norm_gain.reshape(width // HD, HD), packed)
    turns = turn_table(prefix_len).reshape(line, 1, plan.pairs, 2)
    turns = np.tile(turns, (1, plan.mine, 1, 1)).reshape(line, plan.mine * plan.pairs, 2)
    flat = weights.transpose(1, 0, 2).reshape(plan.rows, width) if depth % HD else weights
    sent = (plan.line_rows, moves)
    outs = (shape(sent if plan.direct else (line, *sent), BF16), shape((plan.mine, moves), F32))
    across = tied(across, mark)
    diagonal = swap(across, slab_axes, plan.slab, 1)
    waits = {0: across, len(blocks) - 1: beside}
    filled, listed, start = (), None, 0
    for step, block in enumerate(blocks):
        args = (flat, normed[step], jnp.asarray(turns), *filled)
        more = (waits[step],) if step in waits else ()
        lists = [shape((plan.share, plan.slots), F32)] if step == 0 else []
        made = local_call(
            functools.partial(project, plan, slice(start, start + block), step == 0),
            place,
            (*args, *more),
            [*outs, *lists],
            (),
            16,
            range(len(args), len(args) + len(more)),
            2 * block * width * 1024,
            block * width,
            {4: 0, 5: 1} if filled else None,
        )
        filled, start = made[:2], start + block
        listed = made[2] if step == 0 else listed
    queries, own_values = filled
    other = swap(listed, slab_axes, plan.slab, pair)
    if plan.direct:
        queries = [queries] + [swap(queries, "line", line, step) for step in range(1, line)]
    else:
        queries = lax.all_to_all(queries, "line", split_axis=0, concat_axis=0, tiled=True)
        queries = [queries.reshape(line * plan.line_rows, moves)]

    query_rows = plan.mine * HD
    back = plan.peers * lax.axis_size("tensor")
    chosen, folds = local_call(
        functools.partial(prepare, plan),
        place,
        (listed, other, payload, beside, across),
        (
            shape((boards_here, moves, plan.slab * plan.slots), BF16),
            shape((plan.slab - 1, boards_here, prefix_len, plan.mine * plan.slots), F32),
        ),
        mib=20,
        flops=10**9,
        nbytes=10**6,
    )
    parts = local_call(
        functools.partial(attend, plan),
        place,
        (own_values, listed, other, chosen, folds, payload, beside, across, diagonal, *queries),
        shape((groups, back, plan.share, plan.slots), F32),
        [
            pltpu.VMEM((query_rows + 16, moves), BF16),
            pltpu.VMEM((16, moves), F32),
            pltpu.VMEM((plan.slab, boards_here, plan.slots), F32),
            pltpu.VMEM((query_rows + 16, plan.slab * plan.slots), F32),
            pltpu.VMEM((query_rows + 16, plan.slab * plan.slots), F32),
        ],
        24,
    )
    parts = lax.all_to_all(
        parts.reshape(groups * back, plan.share, plan.slots),
        ("groups", "line", "pair", "tensor"),
        split_axis=0,
        concat_axis=0,
        tiled=True,
    )
    parts = parts.reshape(groups, line, back // line, plan.share, plan.slots)
    logprob = pl.pallas_call(
        functools.partial(finish, plan), out_shape=shape((1, row_count), F32), compiler_params=limits(VMEM_MIB)
    )(parts, board_row, slot_row)
    return logprob.reshape(row_count)


def solution(mesh):
    order = ("groups", "dp", "tensor")
    assert mesh.axis_names == order
    pair = 2
    groups, peers, tensor = (mesh.shape[name] for name in order)
    fine = Mesh(mesh.devices.reshape(groups, peers // pair, pair, tensor), ("groups", "line", "pair", "tensor"))
    rows = ("groups", "line", "pair")
    placed = (
        P(rows, None, "tensor"),
        P(rows),
        P(rows, None),
        P(),
        P(),
        P(("line", "pair"), "tensor"),
        P(("line", "pair"), "tensor"),
        P("tensor"),
    )
    return jax.shard_map(per_device, mesh=fine, in_specs=placed, out_specs=P(rows), check_vma=False)
```

```python
import functools
import math

import jax
import jax.numpy as jnp
import numpy as np
from jax import lax
from jax.experimental import pallas as pl
from jax.experimental.pallas import tpu as pltpu
from jax.sharding import Mesh
from jax.sharding import PartitionSpec as P

HD = 128
HALF = HD // 2
EPS = 1e-06
THETA = 5000000.0
DEAD = -1e30
VMEM_MIB = 52
GROUP, LINE, PEER, SLAB = range(4)

F32 = jnp.float32
BF16 = jnp.bfloat16

NN = (((1,), (0,)), ((), ()))
NT = (((1,), (1,)), ((), ()))
TN = (((0,), (0,)), ((), ()))


def matmul(a, b, dims=NN):
    return lax.dot_general(a, b, dims, preferred_element_type=F32)


def limits(mib):
    return pltpu.CompilerParams(vmem_limit_bytes=mib * 1024 * 1024)


class Plan:
    def __init__(self, groups, line, pair, heads, capacity, share):
        self.groups, self.line, self.pair = groups, line, pair
        self.peers = line * pair
        self.slab = groups * pair
        self.heads = heads
        self.mine = heads // self.slab
        self.pairs = HALF // line
        self.q_rows = self.mine * 2 * self.pairs
        self.k_rows = 2 * self.pairs
        self.fold_at = self.q_rows + self.k_rows
        self.list_at = self.fold_at + self.mine
        self.rows = -(-(self.list_at + 1) // 8) * 8
        self.line_rows = -(-(self.q_rows + 2 * self.mine) // 8) * 8
        self.capacity = capacity
        self.share = share
        self.slots = self.peers * capacity
        self.direct = line <= 4


def pack_weights(plan, place_ref, wq_hbm, wkv_hbm, ws_hbm, board_hbm, ids_hbm, *rest):
    out_ref, wq, wkv, ws_ref, board_ref, ids_ref, pick, sems = rest
    group = place_ref[0]
    half_cols = wq.shape[1]
    columns_here = pl.ds(pl.multiple_of(group * half_cols, HD), half_cols)
    copies = (
        pltpu.make_async_copy(ws_hbm, ws_ref, sems.at[0]),
        pltpu.make_async_copy(board_hbm, board_ref, sems.at[1]),
        pltpu.make_async_copy(ids_hbm, ids_ref, sems.at[2]),
        pltpu.make_async_copy(wq_hbm.at[:, columns_here], wq, sems.at[3]),
        pltpu.make_async_copy(wkv_hbm, wkv, sems.at[4]),
    )
    for copy in copies:
        copy.start()
    for copy in copies[:3]:
        copy.wait()
    count, depth = board_ref.shape[1], wq.shape[0]
    board_row = board_ref[...]
    board_col = jnp.broadcast_to(board_row.astype(F32), (8, count)).T[:, 0:1].astype(jnp.int32)
    own = lax.broadcasted_iota(jnp.int32, (count, count), 0)
    other = lax.broadcasted_iota(jnp.int32, (count, count), 1)
    ahead = jnp.where((board_col == board_row) & (other < own), 1.0, 0.0)
    rank = jnp.sum(ahead, axis=1, keepdims=True).astype(jnp.int32)
    move = ids_ref[...] + 1
    boards, span = plan.line * plan.share, plan.share * plan.capacity
    member = lax.broadcasted_iota(jnp.int32, (boards, count), 0) == board_row
    parts = [jnp.where(member, part.astype(F32), 0.0) for part in (move // 64, move % 64)]
    lane = lax.broadcasted_iota(jnp.int32, (count, depth), 1)
    ranked = jnp.where(rank == (lane % span) % plan.capacity, 1.0, 0.0).astype(BF16)
    found = matmul(jnp.concatenate(parts, axis=0).astype(BF16), ranked)
    lane = lax.broadcasted_iota(jnp.int32, (2 * boards, depth), 1)
    row = lax.broadcasted_iota(jnp.int32, (2 * boards, depth), 0)
    keep = (row // boards == lane // span) & (row % plan.share == (lane % span) // plan.capacity)
    found = jnp.where(keep, found, 0.0)
    lists = []
    for line in range(plan.line):
        at = line * plan.share
        both = found[at : at + plan.share] + found[boards + at : boards + at + plan.share]
        lists.append(jnp.sum(both, axis=0, keepdims=True))

    if plan.pairs % 16 == 0:
        turn_weights(plan, group, lists, copies[3:], wq, wkv, ws_ref, out_ref)
    else:
        pick_weights(plan, group, lists, copies[3:], wq, wkv, ws_ref, out_ref, pick)


def turn_weights(plan, group, lists, copies, wq, wkv, ws_ref, out_ref):
    for copy in copies:
        copy.wait()
    q = wq[...].T
    k = wkv[:, :HD].T
    folds = matmul(ws_ref[...], wkv[:, HD:], NT)
    row = lax.broadcasted_iota(jnp.int32, folds.shape, 0)
    pairs = plan.pairs
    zeros = jnp.zeros((plan.rows - plan.list_at - 1, folds.shape[1]), F32)
    for pair in range(plan.pair):
        first = (group * plan.pair + pair) * plan.mine
        mine = [jnp.sum(jnp.where(row == first + h, folds, 0.0), axis=0, keepdims=True) for h in range(plan.mine)]
        for line in range(plan.line):
            peer = line * plan.pair + pair
            for part in range(2):
                entry = part * HALF + line * pairs
                for h in range(plan.mine):
                    at = (part * plan.mine + h) * pairs
                    source = (pair * plan.mine + h) * HD + entry
                    out_ref[peer, at : at + pairs] = q[source : source + pairs]
                at = plan.q_rows + part * pairs
                out_ref[peer, at : at + pairs] = k[entry : entry + pairs]
            last = jnp.concatenate([*mine, lists[line], zeros], axis=0)
            out_ref[peer, plan.fold_at :] = last.astype(BF16)


def pick_weights(plan, group, lists, copies, wq, wkv, ws_ref, out_ref, pick):
    rows, half_cols = plan.rows, wq.shape[1]
    r = lax.broadcasted_iota(jnp.int32, (rows, 1), 0)
    part = r // (plan.mine * plan.pairs)
    head = (r // plan.pairs) % plan.mine
    entry = r % plan.pairs
    is_q = r < plan.q_rows
    k_at = r - plan.q_rows
    is_k = (k_at >= 0) & (k_at < plan.k_rows)
    f_at = r - plan.fold_at
    is_f = (f_at >= 0) & (f_at < plan.mine)
    q_lane = lax.broadcasted_iota(jnp.int32, (rows, half_cols), 1)
    k_lane = lax.broadcasted_iota(jnp.int32, (rows, HD), 1)
    ws = ws_ref[...].astype(F32)

    def fill(peer, carry):
        line, pair = peer // plan.pair, peer % plan.pair
        column = (pair * plan.mine + head) * HD + part * HALF + line * plan.pairs + entry
        column = jnp.where(is_q, column, -1)
        at = pl.ds(pl.multiple_of(peer * rows, 8), rows)
        pick[at, :half_cols] = jnp.where(q_lane == column, 1.0, 0.0)
        k_column = (k_at // plan.pairs) * HALF + line * plan.pairs + k_at % plan.pairs
        k_column = jnp.where(is_k, k_column, -1)
        pick[at, half_cols : half_cols + HD] = jnp.where(k_lane == k_column, 1.0, 0.0)
        fold = jnp.zeros((rows, HD), F32)
        my_head = jnp.where(is_f, (group * plan.pair + pair) * plan.mine + f_at, -1)
        for h in range(plan.heads):
            fold = jnp.where(my_head == h, ws[h : h + 1], fold)
        pick[at, half_cols + HD :] = fold
        return carry

    lax.fori_loop(0, plan.peers, fill, 0, unroll=plan.peers <= 8)

    for copy in copies:
        copy.wait()
    left = pick[...].astype(BF16)
    total = matmul(left[:, :half_cols], wq[...], NT) + matmul(left[:, half_cols:], wkv[...], NT)
    for peer in range(plan.peers):
        mine = total[peer * rows : (peer + 1) * rows]
        out_ref[peer] = jnp.where(r == plan.list_at, lists[peer // plan.pair], mine).astype(BF16)


def normalize(table_hbm, gain_ref, after_ref, out_ref, mark_ref, gain, buffers, sems):
    mark_ref[...] = jnp.zeros_like(mark_ref)
    held, block, _ = buffers.shape
    steps = table_hbm.shape[0] // block

    def copy(step):
        source = table_hbm.at[pl.ds(step * block, block)]
        return pltpu.make_async_copy(source, buffers.at[step % held], sems.at[step % held])

    for step in range(min(held, steps)):
        copy(step).start()
    rows = gain_ref[...].astype(F32)
    gain[...] = jnp.concatenate([rows[r : r + 1] for r in range(rows.shape[0])], axis=1)
    for step in range(steps):
        copy(step).wait()
        raw = buffers[step % held].astype(F32)
        inverse = lax.rsqrt(jnp.mean(raw * raw, axis=-1, keepdims=True) + EPS)
        out_ref[step * block : (step + 1) * block] = (raw * inverse * gain[...]).astype(BF16)
        if step + held < steps:
            copy(step + held).start()


def read_lists(plan, w_ref, out_ref):
    share, capacity, peers = plan.share, plan.capacity, plan.peers
    span = share * capacity
    if len(w_ref.shape) == 3:
        rows = [w_ref[s].astype(F32)[plan.list_at : plan.list_at + 1] for s in range(peers)]
    else:
        row = w_ref[...].astype(F32)[plan.list_at : plan.list_at + 1]
        rows = [row[:, s * 2 * span : (s + 1) * 2 * span] for s in range(peers)]
    rows = jnp.concatenate(rows, axis=0)
    lane = lax.broadcasted_iota(jnp.int32, (share * peers, 2 * span), 1)
    row = lax.broadcasted_iota(jnp.int32, (share * peers, 2 * span), 0)
    lane = jnp.where(lane < span, lane, lane - span)
    spread = jnp.concatenate([rows] * share, axis=0)
    spread = jnp.where(lane // capacity == row // peers, spread, 0.0).astype(BF16)
    c = lax.broadcasted_iota(jnp.int32, (2 * span, plan.slots), 0)
    slot = lax.broadcasted_iota(jnp.int32, (2 * span, plan.slots), 1)
    scale = jnp.where(c < span, 64.0, 1.0)
    place = jnp.where(c % capacity == slot % capacity, scale, 0.0).astype(BF16)
    listed = matmul(spread, place)
    row = lax.broadcasted_iota(jnp.int32, listed.shape, 0)
    slot = lax.broadcasted_iota(jnp.int32, listed.shape, 1)
    listed = jnp.where(slot // capacity == row % peers, listed, 0.0)
    out_ref[...] = jnp.sum(listed.reshape(share, peers, plan.slots), axis=1)


def project(plan, place_ref, w_ref, normed_ref, turn_ref, after_ref, q_ref, vo_ref, list_ref):
    read_lists(plan, w_ref, list_ref)
    turns = turn_ref[place_ref[LINE]]
    half, k_half = plan.q_rows // 2, plan.k_rows // 2
    cosine, sine = turns[:, 0:1], turns[:, 1:2]
    cos_k, sin_k = cosine[:k_half], sine[:k_half]
    moves = normed_ref.shape[0]
    block = min(moves, 512)
    for start in range(0, moves, block):
        at = slice(start, start + block)
        if len(w_ref.shape) == 3:
            depth = w_ref.shape[2]
            total = None
            for s in range(w_ref.shape[0]):
                term = matmul(w_ref[s], normed_ref[at, s * depth : (s + 1) * depth], NT)
                total = term if total is None else total + term
        else:
            total = matmul(w_ref[...], normed_ref[at, :], NT)
        first, second = total[:half], total[half : 2 * half]
        f_first = (first * cosine - second * sine).astype(BF16).astype(F32)
        f_second = (second * cosine + first * sine).astype(BF16).astype(F32)
        first, second = total[plan.q_rows : plan.q_rows + k_half], total[plan.q_rows + k_half : plan.fold_at]
        k_first = (first * cos_k - second * sin_k).astype(BF16).astype(F32)
        k_second = (second * cos_k + first * sin_k).astype(BF16).astype(F32)
        logits, tails = [], []
        for h in range(plan.mine):
            own = slice(h * k_half, (h + 1) * k_half)
            logit = jnp.sum(f_first[own] * k_first + f_second[own] * k_second, axis=0, keepdims=True)
            logits.append(logit.astype(BF16).astype(F32))
            tails.append(logit - logits[-1])
        pad = plan.line_rows - plan.q_rows - 2 * plan.mine
        pieces = [f_first, f_second, *logits, *tails]
        if pad:
            pieces.append(jnp.zeros((pad, block), F32))
        out = jnp.concatenate(pieces, axis=0).astype(BF16)
        if plan.direct:
            q_ref[:, at] = out
        else:
            for line in range(plan.line):
                q_ref[line, :, at] = out
        vo_ref[:, at] = total[plan.fold_at : plan.list_at]


def tied(x, *others):
    return pl.pallas_call(
        lambda *refs: None,
        out_shape=shape(x.shape, x.dtype),
        in_specs=[untouched()] * (1 + len(others)),
        out_specs=untouched(),
        input_output_aliases={0: 0},
        compiler_params=limits(1),
        cost_estimate=cost(0, 0),
    )(x, *others)


def pack_prefix(plan, place_ref, prefix_hbm, ws_hbm, board_hbm, after_ref, out_ref, slot_ref, *scratch):
    values, ws_ref, board_ref, sems = scratch
    boards = values.shape[0]
    heads = plan.heads
    copies = (
        pltpu.make_async_copy(board_hbm, board_ref, sems.at[0]),
        pltpu.make_async_copy(ws_hbm, ws_ref, sems.at[1]),
        pltpu.make_async_copy(prefix_hbm.at[:, :, pl.ds(HD, HD)], values, sems.at[2]),
        pltpu.make_async_copy(prefix_hbm.at[:, :, pl.ds(0, HD)], out_ref.at[pl.ds(0, boards)], sems.at[3]),
    )
    for copy in copies:
        copy.start()
    copies[0].wait()
    count = board_ref.shape[1]
    board_row = board_ref[...]
    board_col = jnp.broadcast_to(board_row.astype(F32), (8, count)).T[:, 0:1].astype(jnp.int32)
    other = lax.broadcasted_iota(jnp.int32, (count, count), 0)
    own = lax.broadcasted_iota(jnp.int32, (count, count), 1)
    rank = jnp.sum(jnp.where((board_col == board_row) & (other < own), 1.0, 0.0), axis=0, keepdims=True)
    slot_ref[...] = rank.astype(jnp.int32) + place_ref[PEER] * plan.capacity

    copies[1].wait()
    span = HD // boards
    ws = jnp.concatenate([ws_ref[...].astype(F32)] * (HD // heads), axis=0)
    row = lax.broadcasted_iota(jnp.int32, (HD, 1), 0)
    copies[2].wait()
    fold = None
    for board in range(boards):
        keep = (row // span == board) & (row % span < 2 * heads)
        term = matmul(values[board], jnp.where(keep, ws, 0.0).astype(BF16), NT)
        fold = term if fold is None else fold + term
    rounded = fold.astype(BF16).astype(F32)
    lane = lax.broadcasted_iota(jnp.int32, fold.shape, 1)
    out_ref[boards] = jnp.where(lane % span < heads, rounded, fold - rounded).astype(BF16)
    copies[3].wait()


def fold_columns(plan, here, block, board, boards, heads):
    lanes = plan.mine * plan.slots
    row = lax.broadcasted_iota(jnp.int32, (HD, lanes), 0) - board * (HD // boards)
    head = here * plan.mine + lax.broadcasted_iota(jnp.int32, (HD, lanes), 1) // plan.slots
    pick = jnp.where((row == head) | (row == head + heads), 1.0, 0.0).astype(BF16)
    return matmul(block, pick)


def prepare(plan, place_ref, own_ref, other_ref, *rest):
    *prefix_refs, chosen_ref, fold_ref = rest
    here = place_ref[SLAB]
    boards, moves = chosen_ref.shape[0], chosen_ref.shape[1]
    move_at = lax.broadcasted_iota(jnp.int32, (moves, plan.slots), 0) + 1

    def step(board, carry):
        for j in range(plan.slab):
            place = ((here ^ j) % plan.pair) * boards + board
            row = (own_ref, other_ref)[j // plan.pair][pl.ds(place, 1), :].astype(jnp.int32)
            at = slice(j * plan.slots, (j + 1) * plan.slots)
            chosen_ref[board, :, at] = jnp.where(move_at == row, 1.0, 0.0).astype(BF16)
        for j, prefix_ref in enumerate(prefix_refs):
            fold_ref[j, board] = fold_columns(plan, here, prefix_ref[boards], board, boards, plan.heads)
        return carry

    lax.fori_loop(0, boards, step, 0)


def attend(plan, place_ref, vo_ref, own_ref, other_ref, chosen_ref, fold_ref, *rest):
    prefix_refs, rest = rest[: plan.slab], rest[plan.slab :]
    *q_refs, out_ref, table, extra, scores, taken_even, taken_odd = rest
    here = place_ref[SLAB]
    mine, heads, slots = plan.mine, plan.heads, plan.slots
    moves = vo_ref.shape[1]
    boards = prefix_refs[0].shape[0] - 1
    query_rows = mine * HD

    mixed = None
    for step, q_ref in enumerate(q_refs):
        r = lax.broadcasted_iota(jnp.int32, (query_rows + 8, q_ref.shape[0]), 0)
        c = lax.broadcasted_iota(jnp.int32, (query_rows + 8, q_ref.shape[0]), 1)
        line, at = (place_ref[LINE] ^ step, c) if plan.direct else (c // plan.line_rows, c % plan.line_rows)
        part, head, entry = at // (mine * plan.pairs), (at // plan.pairs) % mine, at % plan.pairs
        goes = jnp.where(at < plan.q_rows, head * HD + part * HALF + line * plan.pairs + entry, -1)
        tail = at - plan.q_rows
        goes = jnp.where((tail >= 0) & (tail < 2 * mine), query_rows + tail % mine, goes)
        term = matmul(jnp.where(r == goes, 1.0, 0.0).astype(BF16), q_ref[...])
        mixed = term if mixed is None else mixed + term
    table[:query_rows] = mixed[:query_rows].astype(BF16)
    extra[...] = jnp.zeros_like(extra)
    for place, value in ((0, mixed[query_rows : query_rows + mine]), (2 * mine, vo_ref[...])):
        rounded = value.astype(BF16).astype(F32)
        extra[place : place + mine] = rounded
        extra[place + mine : place + 2 * mine] = value - rounded
    table[query_rows:] = extra[...].astype(BF16)

    scale = math.log2(math.e) / math.sqrt(HD)
    def per_head(x, base):
        pieces = [x[base + h : base + h + 1] + x[base + mine + h : base + mine + h + 1] for h in range(mine)]
        return jnp.concatenate(pieces, axis=1)

    def moves_of(j, board):
        place = ((here ^ j) % plan.pair) * boards + board
        return (own_ref, other_ref)[j // plan.pair][pl.ds(place, 1), :].astype(jnp.int32)

    def gather(board, taken):
        taken[...] = matmul(table[...], chosen_ref[board])

    def score_board(board, taken):
        for j in range(plan.slab):
            x = taken[:, j * slots : (j + 1) * slots]
            q = jnp.concatenate([x[h * HD : (h + 1) * HD].astype(BF16) for h in range(mine)], axis=1)
            logits = matmul(prefix_refs[j][board], q)
            if j < plan.slab - 1:
                fold = fold_ref[j, board]
            else:
                fold = fold_columns(plan, here, prefix_refs[j][boards], board, boards, heads)
            own_logit = per_head(x, query_rows)
            own_value = per_head(x, query_rows + 2 * mine)
            peak = jnp.maximum(jnp.max(logits, axis=0, keepdims=True), own_logit)
            weight = jnp.exp2((logits - peak) * scale)
            own_weight = jnp.exp2((own_logit - peak) * scale)
            denom = jnp.sum(weight, axis=0, keepdims=True) + own_weight
            value = (jnp.sum(weight * fold, axis=0, keepdims=True) + own_value * own_weight) / denom
            score = sum(value[:, h * slots : (h + 1) * slots] for h in range(mine))
            scores[here ^ j, pl.ds(board, 1), :] = jnp.where(moves_of(j, board) > 0, score, DEAD)

    gather(0, taken_even)

    def step(at, carry):
        board = 2 * at
        gather(jnp.minimum(board + 1, boards - 1), taken_odd)
        score_board(board, taken_even)
        gather(jnp.minimum(board + 2, boards - 1), taken_even)
        score_board(jnp.minimum(board + 1, boards - 1), taken_odd)
        return carry

    lax.fori_loop(0, -(-boards // 2), step, 0)
    for g in range(plan.groups):
        both = jnp.concatenate([scores[g * plan.pair + p] for p in range(plan.pair)], axis=0)
        for copy in range(out_ref.shape[1]):
            out_ref[g, copy] = both


def finish(plan, parts_ref, board_ref, slot_ref, out_ref):
    line = parts_ref.shape[1]
    columns = []
    for at in range(line):
        total = None
        for g in range(parts_ref.shape[0]):
            for p in range(parts_ref.shape[2]):
                term = parts_ref[g, at, p]
                total = term if total is None else total + term
        columns.append(total)
    scores = jnp.concatenate(columns, axis=0)
    live = scores > 0.5 * DEAD
    peak = jnp.max(scores, axis=1, keepdims=True)
    denom = jnp.sum(jnp.where(live, jnp.exp(scores - peak), 0.0), axis=1, keepdims=True)
    logprob = jnp.where(live, scores - peak - jnp.log(denom), 0.0)
    count = board_ref.shape[1]
    member = lax.broadcasted_iota(jnp.int32, (scores.shape[0], count), 0) == board_ref[...]
    member = jnp.where(member, 1.0, 0.0).astype(BF16)
    found = jnp.zeros((plan.slots, count), F32)
    for _ in range(3):
        rounded = logprob.astype(BF16)
        found = found + matmul(rounded, member, TN)
        logprob = logprob - rounded.astype(F32)
    at = lax.broadcasted_iota(jnp.int32, (plan.slots, count), 0) == slot_ref[...]
    out_ref[...] = jnp.sum(jnp.where(at, found, 0.0), axis=0, keepdims=True)


def untouched():
    return pl.BlockSpec(memory_space=pl.ANY)


def local_call(kernel, place, args, outs, scratch=(), mib=40, copied=(), flops=0, nbytes=0, aliases=None):
    vmem = pl.BlockSpec(memory_space=pltpu.VMEM)
    return pl.pallas_call(
        kernel,
        out_shape=outs,
        in_specs=[pl.BlockSpec(memory_space=pltpu.SMEM)]
        + [untouched() if at in copied else vmem for at in range(len(args))],
        out_specs=jax.tree.map(lambda x: vmem, outs),
        scratch_shapes=scratch,
        input_output_aliases=aliases or {},
        compiler_params=limits(mib),
        cost_estimate=cost(flops, nbytes),
    )(place, *args)


def cost(flops, nbytes):
    return pl.CostEstimate(flops=int(flops), bytes_accessed=int(nbytes), transcendentals=0)


def swap(x, names, size, step):
    return lax.ppermute(x, names, [(at, at ^ step) for at in range(size)])


def shape(dims, dtype):
    return jax.ShapeDtypeStruct(tuple(dims), dtype)


def turn_table(position):
    frequency = THETA ** (-2.0 * np.arange(HALF, dtype=np.float32) / HD)
    angles = np.float32(position) * frequency.astype(np.float32)
    return np.stack([np.cos(angles), np.sin(angles)], axis=1).astype(np.float32)


def per_device(prefix_kv, move_ids, move_board, move_table, norm_gain, w_query, w_keyval, w_score):
    row_count = move_ids.shape[0]
    boards_here, prefix_len, _ = prefix_kv.shape
    moves, width = move_table.shape
    groups, line, pair = lax.axis_size("groups"), lax.axis_size("line"), lax.axis_size("pair")
    board_total = boards_here * line * pair
    capacity = max(2, (2 * row_count + board_total - 1) // board_total)
    heads = w_query.shape[1] // HD
    plan = Plan(groups, line, pair, heads, capacity, pair * boards_here)
    depth = w_query.shape[0]
    group_at = lax.axis_index("groups").astype(jnp.int32)
    line_at = lax.axis_index("line").astype(jnp.int32)
    pair_at = lax.axis_index("pair").astype(jnp.int32)
    place = jnp.stack([group_at, line_at, line_at * pair + pair_at, group_at * pair + pair_at])
    ws = w_score.reshape(heads, HD)
    slab_axes = ("groups", "pair")
    board_row = move_board.reshape(1, row_count)

    half_cols = w_query.shape[1] // groups
    packed = local_call(
        functools.partial(pack_weights, plan),
        group_at.reshape(1),
        (w_query, w_keyval, ws, board_row, move_ids.reshape(1, row_count)),
        shape((plan.peers, plan.rows, depth), BF16),
        [
            pltpu.VMEM((depth, half_cols), BF16),
            pltpu.VMEM((depth, 2 * HD), BF16),
            pltpu.VMEM((heads, HD), BF16),
            pltpu.VMEM((1, row_count), jnp.int32),
            pltpu.VMEM((1, row_count), jnp.int32),
            pltpu.VMEM((plan.peers * plan.rows, half_cols + 2 * HD), F32),
            pltpu.SemaphoreType.DMA((5,)),
        ],
        62,
        range(5),
    )
    weights = lax.all_to_all(packed, ("line", "pair"), split_axis=0, concat_axis=0, tiled=True)

    keys = shape((boards_here + 1, prefix_len, HD), BF16)
    payload, slot_row = local_call(
        functools.partial(pack_prefix, plan),
        place,
        (prefix_kv, ws, board_row, packed),
        (keys, shape((1, row_count), jnp.int32)),
        [
            pltpu.VMEM((boards_here, prefix_len, HD), BF16),
            pltpu.VMEM((heads, HD), BF16),
            pltpu.VMEM((1, row_count), jnp.int32),
            pltpu.SemaphoreType.DMA((4,)),
        ],
        56,
        range(4),
    )
    beside = swap(payload, slab_axes, plan.slab, 1)
    across = swap(payload, slab_axes, plan.slab, 2)

    block = min(moves, 128)
    vmem = pl.BlockSpec(memory_space=pltpu.VMEM)
    normed, mark = pl.pallas_call(
        normalize,
        out_shape=(pltpu.VMEM((moves, width), BF16), shape((8, HD), F32)),
        in_specs=[untouched(), vmem, untouched()],
        out_specs=(vmem, vmem),
        scratch_shapes=[
            pltpu.VMEM((1, width), F32),
            pltpu.VMEM((3, block, width), BF16),
            pltpu.SemaphoreType.DMA((3,)),
        ],
        compiler_params=limits(48),
        cost_estimate=cost(moves * width, moves * width // 4),
    )(move_table, norm_gain.reshape(width // HD, HD), packed)
    turns = turn_table(prefix_len).reshape(line, 1, plan.pairs, 2)
    turns = np.tile(turns, (1, plan.mine, 1, 1)).reshape(line, plan.mine * plan.pairs, 2)
    flat = weights.transpose(1, 0, 2).reshape(plan.rows, width) if depth % HD else weights
    sent = (plan.line_rows, moves)
    outs = (shape(sent if plan.direct else (line, *sent), BF16), shape((plan.mine, moves), F32))
    across = tied(across, mark)
    diagonal = swap(across, slab_axes, plan.slab, 1)
    queries, own_values, listed = local_call(
        functools.partial(project, plan),
        place,
        (flat, normed, jnp.asarray(turns), across),
        (*outs, shape((plan.share, plan.slots), F32)),
        (),
        20,
        (3,),
        2 * moves * width * 256,
        2 * moves * width,
    )
    queries = tied(queries, beside)
    other = swap(listed, slab_axes, plan.slab, pair)
    if plan.direct:
        queries = [queries] + [swap(queries, "line", line, step) for step in range(1, line)]
    else:
        queries = lax.all_to_all(queries, "line", split_axis=0, concat_axis=0, tiled=True)
        queries = [queries.reshape(line * plan.line_rows, moves)]

    query_rows = plan.mine * HD
    back = plan.peers * lax.axis_size("tensor")
    chosen, folds = local_call(
        functools.partial(prepare, plan),
        place,
        (listed, other, payload, beside, across),
        (
            shape((boards_here, moves, plan.slab * plan.slots), BF16),
            shape((plan.slab - 1, boards_here, prefix_len, plan.mine * plan.slots), F32),
        ),
        mib=20,
        flops=10**9,
        nbytes=10**6,
    )
    parts = local_call(
        functools.partial(attend, plan),
        place,
        (own_values, listed, other, chosen, folds, payload, beside, across, diagonal, *queries),
        shape((groups, back, plan.share, plan.slots), F32),
        [
            pltpu.VMEM((query_rows + 16, moves), BF16),
            pltpu.VMEM((16, moves), F32),
            pltpu.VMEM((plan.slab, boards_here, plan.slots), F32),
            pltpu.VMEM((query_rows + 16, plan.slab * plan.slots), F32),
            pltpu.VMEM((query_rows + 16, plan.slab * plan.slots), F32),
        ],
        24,
    )
    parts = lax.all_to_all(
        parts.reshape(groups * back, plan.share, plan.slots),
        ("groups", "line", "pair", "tensor"),
        split_axis=0,
        concat_axis=0,
        tiled=True,
    )
    parts = parts.reshape(groups, line, back // line, plan.share, plan.slots)
    logprob = pl.pallas_call(
        functools.partial(finish, plan), out_shape=shape((1, row_count), F32), compiler_params=limits(VMEM_MIB)
    )(parts, board_row, slot_row)
    return logprob.reshape(row_count)


def solution(mesh):
    order = ("groups", "dp", "tensor")
    assert mesh.axis_names == order
    pair = 2
    groups, peers, tensor = (mesh.shape[name] for name in order)
    fine = Mesh(mesh.devices.reshape(groups, peers // pair, pair, tensor), ("groups", "line", "pair", "tensor"))
    rows = ("groups", "line", "pair")
    placed = (
        P(rows, None, "tensor"),
        P(rows),
        P(rows, None),
        P(),
        P(),
        P(("line", "pair"), "tensor"),
        P(("line", "pair"), "tensor"),
        P("tensor"),
    )
    return jax.shard_map(per_device, mesh=fine, in_specs=placed, out_specs=P(rows), check_vma=False)
```

```python
import functools
import math

import jax
import jax.numpy as jnp
import numpy as np
from jax import lax
from jax.experimental import pallas as pl
from jax.experimental.pallas import tpu as pltpu
from jax.sharding import Mesh
from jax.sharding import PartitionSpec as P

HD = 128
HALF = HD // 2
EPS = 1e-06
THETA = 5000000.0
DEAD = -1e30
VMEM_MIB = 52
GROUP, LINE, PEER, SLAB = range(4)

F32 = jnp.float32
BF16 = jnp.bfloat16

NN = (((1,), (0,)), ((), ()))
NT = (((1,), (1,)), ((), ()))
TN = (((0,), (0,)), ((), ()))


def matmul(a, b, dims=NN):
    return lax.dot_general(a, b, dims, preferred_element_type=F32)


def limits(mib):
    return pltpu.CompilerParams(vmem_limit_bytes=mib * 1024 * 1024)


class Plan:
    def __init__(self, groups, line, pair, heads, capacity, share):
        self.groups, self.line, self.pair = groups, line, pair
        self.peers = line * pair
        self.slab = groups * pair
        self.heads = heads
        self.mine = heads // self.slab
        self.pairs = HALF // line
        self.q_rows = self.mine * 2 * self.pairs
        self.k_rows = 2 * self.pairs
        self.fold_at = self.q_rows + self.k_rows
        self.list_at = self.fold_at + self.mine
        self.rows = -(-(self.list_at + 1) // 8) * 8
        self.line_rows = -(-(self.q_rows + 2 * self.mine) // 8) * 8
        self.capacity = capacity
        self.share = share
        self.slots = self.peers * capacity
        self.direct = line <= 4


def pack_weights(plan, place_ref, wq_hbm, wkv_hbm, ws_hbm, board_hbm, ids_hbm, *rest):
    out_ref, wq, wkv, ws_ref, board_ref, ids_ref, pick, sems = rest
    group = place_ref[0]
    half_cols = wq.shape[1]
    columns_here = pl.ds(pl.multiple_of(group * half_cols, HD), half_cols)
    copies = (
        pltpu.make_async_copy(ws_hbm, ws_ref, sems.at[0]),
        pltpu.make_async_copy(board_hbm, board_ref, sems.at[1]),
        pltpu.make_async_copy(ids_hbm, ids_ref, sems.at[2]),
        pltpu.make_async_copy(wq_hbm.at[:, columns_here], wq, sems.at[3]),
        pltpu.make_async_copy(wkv_hbm, wkv, sems.at[4]),
    )
    for copy in copies:
        copy.start()
    for copy in copies[:3]:
        copy.wait()
    count, depth = board_ref.shape[1], wq.shape[0]
    board_row = board_ref[...]
    board_col = jnp.broadcast_to(board_row.astype(F32), (8, count)).T[:, 0:1].astype(jnp.int32)
    own = lax.broadcasted_iota(jnp.int32, (count, count), 0)
    other = lax.broadcasted_iota(jnp.int32, (count, count), 1)
    ahead = jnp.where((board_col == board_row) & (other < own), 1.0, 0.0)
    rank = jnp.sum(ahead, axis=1, keepdims=True).astype(jnp.int32)
    move = ids_ref[...] + 1
    boards, span = plan.line * plan.share, plan.share * plan.capacity
    member = lax.broadcasted_iota(jnp.int32, (boards, count), 0) == board_row
    parts = [jnp.where(member, part.astype(F32), 0.0) for part in (move // 64, move % 64)]
    lane = lax.broadcasted_iota(jnp.int32, (count, depth), 1)
    ranked = jnp.where(rank == (lane % span) % plan.capacity, 1.0, 0.0).astype(BF16)
    found = matmul(jnp.concatenate(parts, axis=0).astype(BF16), ranked)
    lane = lax.broadcasted_iota(jnp.int32, (2 * boards, depth), 1)
    row = lax.broadcasted_iota(jnp.int32, (2 * boards, depth), 0)
    keep = (row // boards == lane // span) & (row % plan.share == (lane % span) // plan.capacity)
    found = jnp.where(keep, found, 0.0)
    lists = []
    for line in range(plan.line):
        at = line * plan.share
        both = found[at : at + plan.share] + found[boards + at : boards + at + plan.share]
        lists.append(jnp.sum(both, axis=0, keepdims=True))

    if plan.pairs % 16 == 0:
        turn_weights(plan, group, lists, copies[3:], wq, wkv, ws_ref, out_ref)
    else:
        pick_weights(plan, group, lists, copies[3:], wq, wkv, ws_ref, out_ref, pick)


def turn_weights(plan, group, lists, copies, wq, wkv, ws_ref, out_ref):
    for copy in copies:
        copy.wait()
    q = wq[...].T
    k = wkv[:, :HD].T
    folds = matmul(ws_ref[...], wkv[:, HD:], NT)
    row = lax.broadcasted_iota(jnp.int32, folds.shape, 0)
    pairs = plan.pairs
    zeros = jnp.zeros((plan.rows - plan.list_at - 1, folds.shape[1]), F32)
    for pair in range(plan.pair):
        first = (group * plan.pair + pair) * plan.mine
        mine = [jnp.sum(jnp.where(row == first + h, folds, 0.0), axis=0, keepdims=True) for h in range(plan.mine)]
        for line in range(plan.line):
            peer = line * plan.pair + pair
            for part in range(2):
                entry = part * HALF + line * pairs
                for h in range(plan.mine):
                    at = (part * plan.mine + h) * pairs
                    source = (pair * plan.mine + h) * HD + entry
                    out_ref[peer, at : at + pairs] = q[source : source + pairs]
                at = plan.q_rows + part * pairs
                out_ref[peer, at : at + pairs] = k[entry : entry + pairs]
            last = jnp.concatenate([*mine, lists[line], zeros], axis=0)
            out_ref[peer, plan.fold_at :] = last.astype(BF16)


def pick_weights(plan, group, lists, copies, wq, wkv, ws_ref, out_ref, pick):
    rows, half_cols = plan.rows, wq.shape[1]
    r = lax.broadcasted_iota(jnp.int32, (rows, 1), 0)
    part = r // (plan.mine * plan.pairs)
    head = (r // plan.pairs) % plan.mine
    entry = r % plan.pairs
    is_q = r < plan.q_rows
    k_at = r - plan.q_rows
    is_k = (k_at >= 0) & (k_at < plan.k_rows)
    f_at = r - plan.fold_at
    is_f = (f_at >= 0) & (f_at < plan.mine)
    q_lane = lax.broadcasted_iota(jnp.int32, (rows, half_cols), 1)
    k_lane = lax.broadcasted_iota(jnp.int32, (rows, HD), 1)
    ws = ws_ref[...].astype(F32)

    def fill(peer, carry):
        line, pair = peer // plan.pair, peer % plan.pair
        column = (pair * plan.mine + head) * HD + part * HALF + line * plan.pairs + entry
        column = jnp.where(is_q, column, -1)
        at = pl.ds(pl.multiple_of(peer * rows, 8), rows)
        pick[at, :half_cols] = jnp.where(q_lane == column, 1.0, 0.0)
        k_column = (k_at // plan.pairs) * HALF + line * plan.pairs + k_at % plan.pairs
        k_column = jnp.where(is_k, k_column, -1)
        pick[at, half_cols : half_cols + HD] = jnp.where(k_lane == k_column, 1.0, 0.0)
        fold = jnp.zeros((rows, HD), F32)
        my_head = jnp.where(is_f, (group * plan.pair + pair) * plan.mine + f_at, -1)
        for h in range(plan.heads):
            fold = jnp.where(my_head == h, ws[h : h + 1], fold)
        pick[at, half_cols + HD :] = fold
        return carry

    lax.fori_loop(0, plan.peers, fill, 0, unroll=plan.peers <= 8)

    for copy in copies:
        copy.wait()
    left = pick[...].astype(BF16)
    total = matmul(left[:, :half_cols], wq[...], NT) + matmul(left[:, half_cols:], wkv[...], NT)
    for peer in range(plan.peers):
        mine = total[peer * rows : (peer + 1) * rows]
        out_ref[peer] = jnp.where(r == plan.list_at, lists[peer // plan.pair], mine).astype(BF16)


def normalize(table_hbm, gain_ref, after_ref, *refs):
    *outs, mark_ref, gain, buffers, made, sems, out_sems = refs
    mark_ref[...] = jnp.zeros_like(mark_ref)
    held, block, _ = buffers.shape
    steps = table_hbm.shape[0] // block
    each = outs[0].shape[0] // block

    def copy(step):
        source = table_hbm.at[pl.ds(step * block, block)]
        return pltpu.make_async_copy(source, buffers.at[step % held], sems.at[step % held])

    def store(step):
        target = outs[step // each].at[pl.ds(step % each * block, block)]
        return pltpu.make_async_copy(made.at[step % held], target, out_sems.at[step % held])

    for step in range(min(held, steps)):
        copy(step).start()
    rows = gain_ref[...].astype(F32)
    gain[...] = jnp.concatenate([rows[r : r + 1] for r in range(rows.shape[0])], axis=1)
    for step in range(steps):
        copy(step).wait()
        if step >= held:
            store(step - held).wait()
        raw = buffers[step % held].astype(F32)
        inverse = lax.rsqrt(jnp.mean(raw * raw, axis=-1, keepdims=True) + EPS)
        made[step % held] = (raw * inverse * gain[...]).astype(BF16)
        store(step).start()
        if step + held < steps:
            copy(step + held).start()
    for step in range(max(0, steps - held), steps):
        store(step).wait()


def read_lists(plan, w_ref, out_ref):
    share, capacity, peers = plan.share, plan.capacity, plan.peers
    span = share * capacity
    if len(w_ref.shape) == 3:
        rows = [w_ref[s].astype(F32)[plan.list_at : plan.list_at + 1] for s in range(peers)]
    else:
        row = w_ref[...].astype(F32)[plan.list_at : plan.list_at + 1]
        rows = [row[:, s * 2 * span : (s + 1) * 2 * span] for s in range(peers)]
    rows = jnp.concatenate(rows, axis=0)
    lane = lax.broadcasted_iota(jnp.int32, (share * peers, 2 * span), 1)
    row = lax.broadcasted_iota(jnp.int32, (share * peers, 2 * span), 0)
    lane = jnp.where(lane < span, lane, lane - span)
    spread = jnp.concatenate([rows] * share, axis=0)
    spread = jnp.where(lane // capacity == row // peers, spread, 0.0).astype(BF16)
    c = lax.broadcasted_iota(jnp.int32, (2 * span, plan.slots), 0)
    slot = lax.broadcasted_iota(jnp.int32, (2 * span, plan.slots), 1)
    scale = jnp.where(c < span, 64.0, 1.0)
    place = jnp.where(c % capacity == slot % capacity, scale, 0.0).astype(BF16)
    listed = matmul(spread, place)
    row = lax.broadcasted_iota(jnp.int32, listed.shape, 0)
    slot = lax.broadcasted_iota(jnp.int32, listed.shape, 1)
    listed = jnp.where(slot // capacity == row % peers, listed, 0.0)
    out_ref[...] = jnp.sum(listed.reshape(share, peers, plan.slots), axis=1)


def project(plan, place, lists, place_ref, w_ref, normed_ref, turn_ref, after_ref, *refs):
    if lists:
        *refs, list_ref = refs
        read_lists(plan, w_ref, list_ref)
    q_ref, vo_ref = refs[-2:]
    turns = turn_ref[place_ref[LINE]]
    half, k_half = plan.q_rows // 2, plan.k_rows // 2
    cosine, sine = turns[:, 0:1], turns[:, 1:2]
    cos_k, sin_k = cosine[:k_half], sine[:k_half]
    moves = normed_ref.shape[0]
    block = min(moves, 256)
    for start in range(0, moves, block):
        at, to = slice(start, start + block), slice(place + start, place + start + block)
        if len(w_ref.shape) == 3:
            depth = w_ref.shape[2]
            total = None
            for s in range(w_ref.shape[0]):
                term = matmul(w_ref[s], normed_ref[at, s * depth : (s + 1) * depth], NT)
                total = term if total is None else total + term
        else:
            total = matmul(w_ref[...], normed_ref[at, :], NT)
        first, second = total[:half], total[half : 2 * half]
        f_first = (first * cosine - second * sine).astype(BF16).astype(F32)
        f_second = (second * cosine + first * sine).astype(BF16).astype(F32)
        first, second = total[plan.q_rows : plan.q_rows + k_half], total[plan.q_rows + k_half : plan.fold_at]
        k_first = (first * cos_k - second * sin_k).astype(BF16).astype(F32)
        k_second = (second * cos_k + first * sin_k).astype(BF16).astype(F32)
        logits, tails = [], []
        for h in range(plan.mine):
            own = slice(h * k_half, (h + 1) * k_half)
            logit = jnp.sum(f_first[own] * k_first + f_second[own] * k_second, axis=0, keepdims=True)
            logits.append(logit.astype(BF16).astype(F32))
            tails.append(logit - logits[-1])
        pad = plan.line_rows - plan.q_rows - 2 * plan.mine
        pieces = [f_first, f_second, *logits, *tails]
        if pad:
            pieces.append(jnp.zeros((pad, block), F32))
        out = jnp.concatenate(pieces, axis=0).astype(BF16)
        if plan.direct:
            q_ref[:, to] = out
        else:
            for line in range(plan.line):
                q_ref[line, :, to] = out
        vo_ref[:, to] = total[plan.fold_at : plan.list_at]


def tied(x, *others):
    return pl.pallas_call(
        lambda *refs: None,
        out_shape=shape(x.shape, x.dtype),
        in_specs=[untouched()] * (1 + len(others)),
        out_specs=untouched(),
        input_output_aliases={0: 0},
        compiler_params=limits(1),
        cost_estimate=cost(0, 0),
    )(x, *others)


def pack_prefix(plan, place_ref, prefix_hbm, ws_hbm, board_hbm, after_ref, out_ref, slot_ref, *scratch):
    values, ws_ref, board_ref, sems = scratch
    boards = values.shape[0]
    heads = plan.heads
    copies = (
        pltpu.make_async_copy(board_hbm, board_ref, sems.at[0]),
        pltpu.make_async_copy(ws_hbm, ws_ref, sems.at[1]),
        pltpu.make_async_copy(prefix_hbm.at[:, :, pl.ds(HD, HD)], values, sems.at[2]),
        pltpu.make_async_copy(prefix_hbm.at[:, :, pl.ds(0, HD)], out_ref.at[pl.ds(0, boards)], sems.at[3]),
    )
    for copy in copies:
        copy.start()
    copies[0].wait()
    count = board_ref.shape[1]
    board_row = board_ref[...]
    board_col = jnp.broadcast_to(board_row.astype(F32), (8, count)).T[:, 0:1].astype(jnp.int32)
    other = lax.broadcasted_iota(jnp.int32, (count, count), 0)
    own = lax.broadcasted_iota(jnp.int32, (count, count), 1)
    rank = jnp.sum(jnp.where((board_col == board_row) & (other < own), 1.0, 0.0), axis=0, keepdims=True)
    slot_ref[...] = rank.astype(jnp.int32) + place_ref[PEER] * plan.capacity

    copies[1].wait()
    span = HD // boards
    ws = jnp.concatenate([ws_ref[...].astype(F32)] * (HD // heads), axis=0)
    row = lax.broadcasted_iota(jnp.int32, (HD, 1), 0)
    copies[2].wait()
    fold = None
    for board in range(boards):
        keep = (row // span == board) & (row % span < 2 * heads)
        term = matmul(values[board], jnp.where(keep, ws, 0.0).astype(BF16), NT)
        fold = term if fold is None else fold + term
    rounded = fold.astype(BF16).astype(F32)
    lane = lax.broadcasted_iota(jnp.int32, fold.shape, 1)
    out_ref[boards] = jnp.where(lane % span < heads, rounded, fold - rounded).astype(BF16)
    copies[3].wait()


def fold_columns(plan, here, block, board, boards, heads):
    lanes = plan.mine * plan.slots
    row = lax.broadcasted_iota(jnp.int32, (HD, lanes), 0) - board * (HD // boards)
    head = here * plan.mine + lax.broadcasted_iota(jnp.int32, (HD, lanes), 1) // plan.slots
    pick = jnp.where((row == head) | (row == head + heads), 1.0, 0.0).astype(BF16)
    return matmul(block, pick)


def prepare(plan, place_ref, own_ref, other_ref, *rest):
    *prefix_refs, chosen_ref, fold_ref = rest
    here = place_ref[SLAB]
    boards, moves = chosen_ref.shape[0], chosen_ref.shape[1]
    move_at = lax.broadcasted_iota(jnp.int32, (moves, plan.slots), 0) + 1

    def step(board, carry):
        for j in range(plan.slab):
            place = ((here ^ j) % plan.pair) * boards + board
            row = (own_ref, other_ref)[j // plan.pair][pl.ds(place, 1), :].astype(jnp.int32)
            at = slice(j * plan.slots, (j + 1) * plan.slots)
            chosen_ref[board, :, at] = jnp.where(move_at == row, 1.0, 0.0).astype(BF16)
        for j, prefix_ref in enumerate(prefix_refs):
            fold_ref[j, board] = fold_columns(plan, here, prefix_ref[boards], board, boards, plan.heads)
        return carry

    lax.fori_loop(0, boards, step, 0)


def attend(plan, place_ref, vo_ref, own_ref, other_ref, chosen_ref, fold_ref, *rest):
    prefix_refs, rest = rest[: plan.slab], rest[plan.slab :]
    *q_refs, out_ref, table, extra, scores, taken_even, taken_odd = rest
    here = place_ref[SLAB]
    mine, heads, slots = plan.mine, plan.heads, plan.slots
    moves = vo_ref.shape[1]
    boards = prefix_refs[0].shape[0] - 1
    query_rows = mine * HD

    mixed = None
    for step, q_ref in enumerate(q_refs):
        r = lax.broadcasted_iota(jnp.int32, (query_rows + 8, q_ref.shape[0]), 0)
        c = lax.broadcasted_iota(jnp.int32, (query_rows + 8, q_ref.shape[0]), 1)
        line, at = (place_ref[LINE] ^ step, c) if plan.direct else (c // plan.line_rows, c % plan.line_rows)
        part, head, entry = at // (mine * plan.pairs), (at // plan.pairs) % mine, at % plan.pairs
        goes = jnp.where(at < plan.q_rows, head * HD + part * HALF + line * plan.pairs + entry, -1)
        tail = at - plan.q_rows
        goes = jnp.where((tail >= 0) & (tail < 2 * mine), query_rows + tail % mine, goes)
        term = matmul(jnp.where(r == goes, 1.0, 0.0).astype(BF16), q_ref[...])
        mixed = term if mixed is None else mixed + term
    table[:query_rows] = mixed[:query_rows].astype(BF16)
    extra[...] = jnp.zeros_like(extra)
    for place, value in ((0, mixed[query_rows : query_rows + mine]), (2 * mine, vo_ref[...])):
        rounded = value.astype(BF16).astype(F32)
        extra[place : place + mine] = rounded
        extra[place + mine : place + 2 * mine] = value - rounded
    table[query_rows:] = extra[...].astype(BF16)

    scale = math.log2(math.e) / math.sqrt(HD)
    def per_head(x, base):
        pieces = [x[base + h : base + h + 1] + x[base + mine + h : base + mine + h + 1] for h in range(mine)]
        return jnp.concatenate(pieces, axis=1)

    def moves_of(j, board):
        place = ((here ^ j) % plan.pair) * boards + board
        return (own_ref, other_ref)[j // plan.pair][pl.ds(place, 1), :].astype(jnp.int32)

    def gather(board, taken):
        taken[...] = matmul(table[...], chosen_ref[board])

    def score_board(board, taken):
        for j in range(plan.slab):
            x = taken[:, j * slots : (j + 1) * slots]
            q = jnp.concatenate([x[h * HD : (h + 1) * HD].astype(BF16) for h in range(mine)], axis=1)
            logits = matmul(prefix_refs[j][board], q)
            if j < plan.slab - 1:
                fold = fold_ref[j, board]
            else:
                fold = fold_columns(plan, here, prefix_refs[j][boards], board, boards, heads)
            own_logit = per_head(x, query_rows)
            own_value = per_head(x, query_rows + 2 * mine)
            peak = jnp.maximum(jnp.max(logits, axis=0, keepdims=True), own_logit)
            weight = jnp.exp2((logits - peak) * scale)
            own_weight = jnp.exp2((own_logit - peak) * scale)
            denom = jnp.sum(weight, axis=0, keepdims=True) + own_weight
            value = (jnp.sum(weight * fold, axis=0, keepdims=True) + own_value * own_weight) / denom
            score = sum(value[:, h * slots : (h + 1) * slots] for h in range(mine))
            scores[here ^ j, pl.ds(board, 1), :] = jnp.where(moves_of(j, board) > 0, score, DEAD)

    gather(0, taken_even)

    def step(at, carry):
        board = 2 * at
        gather(jnp.minimum(board + 1, boards - 1), taken_odd)
        score_board(board, taken_even)
        gather(jnp.minimum(board + 2, boards - 1), taken_even)
        score_board(jnp.minimum(board + 1, boards - 1), taken_odd)
        return carry

    lax.fori_loop(0, -(-boards // 2), step, 0)
    live = scores[...] > 0.5 * DEAD
    count = jnp.sum(jnp.where(live, 1.0, 0.0), axis=2, keepdims=True)
    mean = jnp.sum(jnp.where(live, scores[...], 0.0), axis=2, keepdims=True) / jnp.maximum(count, 1.0)
    centered = jnp.where(live, scores[...] - mean, DEAD)
    for g in range(plan.groups):
        both = jnp.concatenate([centered[g * plan.pair + p] for p in range(plan.pair)], axis=0).astype(BF16)
        for copy in range(out_ref.shape[1]):
            out_ref[g, copy] = both


def finish(plan, parts_ref, board_ref, slot_ref, out_ref):
    line = parts_ref.shape[1]
    columns = []
    for at in range(line):
        total = None
        for g in range(parts_ref.shape[0]):
            for p in range(parts_ref.shape[2]):
                term = parts_ref[g, at, p].astype(F32)
                total = term if total is None else total + term
        columns.append(total)
    scores = jnp.concatenate(columns, axis=0)
    live = scores > 0.5 * DEAD
    peak = jnp.max(scores, axis=1, keepdims=True)
    denom = jnp.sum(jnp.where(live, jnp.exp(scores - peak), 0.0), axis=1, keepdims=True)
    logprob = jnp.where(live, scores - peak - jnp.log(denom), 0.0)
    count = board_ref.shape[1]
    member = lax.broadcasted_iota(jnp.int32, (scores.shape[0], count), 0) == board_ref[...]
    member = jnp.where(member, 1.0, 0.0).astype(BF16)
    found = jnp.zeros((plan.slots, count), F32)
    for _ in range(3):
        rounded = logprob.astype(BF16)
        found = found + matmul(rounded, member, TN)
        logprob = logprob - rounded.astype(F32)
    at = lax.broadcasted_iota(jnp.int32, (plan.slots, count), 0) == slot_ref[...]
    out_ref[...] = jnp.sum(jnp.where(at, found, 0.0), axis=0, keepdims=True)


def untouched():
    return pl.BlockSpec(memory_space=pl.ANY)


def local_call(kernel, place, args, outs, scratch=(), mib=40, copied=(), flops=0, nbytes=0, aliases=None):
    vmem = pl.BlockSpec(memory_space=pltpu.VMEM)
    return pl.pallas_call(
        kernel,
        out_shape=outs,
        in_specs=[pl.BlockSpec(memory_space=pltpu.SMEM)]
        + [untouched() if at in copied else vmem for at in range(len(args))],
        out_specs=jax.tree.map(lambda x: vmem, outs),
        scratch_shapes=scratch,
        input_output_aliases=aliases or {},
        compiler_params=limits(mib),
        cost_estimate=cost(flops, nbytes),
    )(place, *args)


def cost(flops, nbytes):
    return pl.CostEstimate(flops=int(flops), bytes_accessed=int(nbytes), transcendentals=0)


def swap(x, names, size, step):
    return lax.ppermute(x, names, [(at, at ^ step) for at in range(size)])


def shape(dims, dtype):
    return jax.ShapeDtypeStruct(tuple(dims), dtype)


def turn_table(position):
    frequency = THETA ** (-2.0 * np.arange(HALF, dtype=np.float32) / HD)
    angles = np.float32(position) * frequency.astype(np.float32)
    return np.stack([np.cos(angles), np.sin(angles)], axis=1).astype(np.float32)


def per_device(prefix_kv, move_ids, move_board, move_table, norm_gain, w_query, w_keyval, w_score):
    row_count = move_ids.shape[0]
    boards_here, prefix_len, _ = prefix_kv.shape
    moves, width = move_table.shape
    groups, line, pair = lax.axis_size("groups"), lax.axis_size("line"), lax.axis_size("pair")
    board_total = boards_here * line * pair
    capacity = max(2, (2 * row_count + board_total - 1) // board_total)
    heads = w_query.shape[1] // HD
    plan = Plan(groups, line, pair, heads, capacity, pair * boards_here)
    depth = w_query.shape[0]
    group_at = lax.axis_index("groups").astype(jnp.int32)
    line_at = lax.axis_index("line").astype(jnp.int32)
    pair_at = lax.axis_index("pair").astype(jnp.int32)
    place = jnp.stack([group_at, line_at, line_at * pair + pair_at, group_at * pair + pair_at])
    ws = w_score.reshape(heads, HD)
    slab_axes = ("groups", "pair")
    board_row = move_board.reshape(1, row_count)

    half_cols = w_query.shape[1] // groups
    packed = local_call(
        functools.partial(pack_weights, plan),
        group_at.reshape(1),
        (w_query, w_keyval, ws, board_row, move_ids.reshape(1, row_count)),
        shape((plan.peers, plan.rows, depth), BF16),
        [
            pltpu.VMEM((depth, half_cols), BF16),
            pltpu.VMEM((depth, 2 * HD), BF16),
            pltpu.VMEM((heads, HD), BF16),
            pltpu.VMEM((1, row_count), jnp.int32),
            pltpu.VMEM((1, row_count), jnp.int32),
            pltpu.VMEM((plan.peers * plan.rows, half_cols + 2 * HD), F32),
            pltpu.SemaphoreType.DMA((5,)),
        ],
        62,
        range(5),
    )
    weights = lax.all_to_all(packed, ("line", "pair"), split_axis=0, concat_axis=0, tiled=True)

    keys = shape((boards_here + 1, prefix_len, HD), BF16)
    payload, slot_row = local_call(
        functools.partial(pack_prefix, plan),
        place,
        (prefix_kv, ws, board_row, packed),
        (keys, shape((1, row_count), jnp.int32)),
        [
            pltpu.VMEM((boards_here, prefix_len, HD), BF16),
            pltpu.VMEM((heads, HD), BF16),
            pltpu.VMEM((1, row_count), jnp.int32),
            pltpu.SemaphoreType.DMA((4,)),
        ],
        56,
        range(4),
    )
    beside = swap(payload, slab_axes, plan.slab, 1)
    across = swap(payload, slab_axes, plan.slab, 2)

    block = min(moves, 128)
    vmem = pl.BlockSpec(memory_space=pltpu.VMEM)
    *normed, mark = pl.pallas_call(
        normalize,
        out_shape=[*[shape((moves // 2, width), BF16)] * 2, shape((8, HD), F32)],
        in_specs=[untouched(), vmem, untouched()],
        out_specs=[untouched(), untouched(), vmem],
        scratch_shapes=[
            pltpu.VMEM((1, width), F32),
            pltpu.VMEM((3, block, width), BF16),
            pltpu.VMEM((3, block, width), BF16),
            pltpu.SemaphoreType.DMA((3,)),
            pltpu.SemaphoreType.DMA((3,)),
        ],
        compiler_params=limits(58),
        cost_estimate=cost(moves * width, moves * width // 4),
    )(move_table, norm_gain.reshape(width // HD, HD), packed)
    turns = turn_table(prefix_len).reshape(line, 1, plan.pairs, 2)
    turns = np.tile(turns, (1, plan.mine, 1, 1)).reshape(line, plan.mine * plan.pairs, 2)
    flat = weights.transpose(1, 0, 2).reshape(plan.rows, width) if depth % HD else weights
    sent = (plan.line_rows, moves)
    outs = (shape(sent if plan.direct else (line, *sent), BF16), shape((plan.mine, moves), F32))
    across = tied(across, mark)
    diagonal = swap(across, slab_axes, plan.slab, 1)
    filled, listed = (), None
    for step, after in enumerate((across, beside)):
        made = local_call(
            functools.partial(project, plan, step * moves // 2, step == 0),
            place,
            (flat, normed[step], jnp.asarray(turns), after, *filled),
            [*outs, *([shape((plan.share, plan.slots), F32)] if step == 0 else [])],
            (),
            20,
            (3,),
            moves * width * 1024,
            moves * width,
            {5: 0, 6: 1} if filled else None,
        )
        filled, listed = made[:2], made[2] if step == 0 else listed
    queries, own_values = filled
    other = swap(listed, slab_axes, plan.slab, pair)
    if plan.direct:
        queries = [queries] + [swap(queries, "line", line, step) for step in range(1, line)]
    else:
        queries = lax.all_to_all(queries, "line", split_axis=0, concat_axis=0, tiled=True)
        queries = [queries.reshape(line * plan.line_rows, moves)]

    query_rows = plan.mine * HD
    back = plan.peers * lax.axis_size("tensor")
    chosen, folds = local_call(
        functools.partial(prepare, plan),
        place,
        (listed, other, payload, beside, across),
        (
            shape((boards_here, moves, plan.slab * plan.slots), BF16),
            shape((plan.slab - 1, boards_here, prefix_len, plan.mine * plan.slots), F32),
        ),
        mib=20,
        flops=10**9,
        nbytes=10**6,
    )
    parts = local_call(
        functools.partial(attend, plan),
        place,
        (own_values, listed, other, chosen, folds, payload, beside, across, diagonal, *queries),
        shape((groups, back, plan.share, plan.slots), BF16),
        [
            pltpu.VMEM((query_rows + 16, moves), BF16),
            pltpu.VMEM((16, moves), F32),
            pltpu.VMEM((plan.slab, boards_here, plan.slots), F32),
            pltpu.VMEM((query_rows + 16, plan.slab * plan.slots), F32),
            pltpu.VMEM((query_rows + 16, plan.slab * plan.slots), F32),
        ],
        24,
    )
    parts = lax.all_to_all(
        parts.reshape(groups * back, plan.share, plan.slots),
        ("groups", "line", "pair", "tensor"),
        split_axis=0,
        concat_axis=0,
        tiled=True,
    )
    parts = parts.reshape(groups, line, back // line, plan.share, plan.slots)
    logprob = pl.pallas_call(
        functools.partial(finish, plan), out_shape=shape((1, row_count), F32), compiler_params=limits(VMEM_MIB)
    )(parts, board_row, slot_row)
    return logprob.reshape(row_count)


def solution(mesh):
    order = ("groups", "dp", "tensor")
    assert mesh.axis_names == order
    pair = 2
    groups, peers, tensor = (mesh.shape[name] for name in order)
    fine = Mesh(mesh.devices.reshape(groups, peers // pair, pair, tensor), ("groups", "line", "pair", "tensor"))
    rows = ("groups", "line", "pair")
    placed = (
        P(rows, None, "tensor"),
        P(rows),
        P(rows, None),
        P(),
        P(),
        P(("line", "pair"), "tensor"),
        P(("line", "pair"), "tensor"),
        P("tensor"),
    )
    return jax.shard_map(per_device, mesh=fine, in_specs=placed, out_specs=P(rows), check_vma=False)
```

```python
import functools
import math

import jax
import jax.numpy as jnp
import numpy as np
from jax import lax
from jax.experimental import pallas as pl
from jax.experimental.pallas import tpu as pltpu
from jax.sharding import Mesh
from jax.sharding import PartitionSpec as P

HD = 128
HALF = HD // 2
EPS = 1e-06
THETA = 5000000.0
DEAD = -1e30
VMEM_MIB = 52
GROUP, LINE, PEER, SLAB = range(4)

F32 = jnp.float32
BF16 = jnp.bfloat16

NN = (((1,), (0,)), ((), ()))
NT = (((1,), (1,)), ((), ()))
TN = (((0,), (0,)), ((), ()))


def matmul(a, b, dims=NN):
    return lax.dot_general(a, b, dims, preferred_element_type=F32)


def limits(mib):
    return pltpu.CompilerParams(vmem_limit_bytes=mib * 1024 * 1024)


class Plan:
    def __init__(self, groups, line, pair, heads, capacity, share):
        self.groups, self.line, self.pair = groups, line, pair
        self.peers = line * pair
        self.slab = groups * pair
        self.heads = heads
        self.mine = heads // self.slab
        self.pairs = HALF // line
        self.q_rows = self.mine * 2 * self.pairs
        self.k_rows = 2 * self.pairs
        self.fold_at = self.q_rows + self.k_rows
        self.list_at = self.fold_at + self.mine
        self.rows = -(-(self.list_at + 1) // 8) * 8
        self.line_rows = -(-(self.q_rows + 2 * self.mine) // 8) * 8
        self.capacity = capacity
        self.share = share
        self.slots = self.peers * capacity
        self.direct = line <= 4


def pack_weights(plan, place_ref, wq_hbm, wkv_hbm, ws_hbm, board_hbm, ids_hbm, *rest):
    out_ref, wq, wkv, ws_ref, board_ref, ids_ref, pick, sems = rest
    group = place_ref[0]
    half_cols = wq.shape[1]
    columns_here = pl.ds(pl.multiple_of(group * half_cols, HD), half_cols)
    copies = (
        pltpu.make_async_copy(ws_hbm, ws_ref, sems.at[0]),
        pltpu.make_async_copy(board_hbm, board_ref, sems.at[1]),
        pltpu.make_async_copy(ids_hbm, ids_ref, sems.at[2]),
        pltpu.make_async_copy(wq_hbm.at[:, columns_here], wq, sems.at[3]),
        pltpu.make_async_copy(wkv_hbm, wkv, sems.at[4]),
    )
    for copy in copies:
        copy.start()
    for copy in copies[:3]:
        copy.wait()
    count, depth = board_ref.shape[1], wq.shape[0]
    board_row = board_ref[...]
    board_col = jnp.broadcast_to(board_row.astype(F32), (8, count)).T[:, 0:1].astype(jnp.int32)
    own = lax.broadcasted_iota(jnp.int32, (count, count), 0)
    other = lax.broadcasted_iota(jnp.int32, (count, count), 1)
    ahead = jnp.where((board_col == board_row) & (other < own), 1.0, 0.0)
    rank = jnp.sum(ahead, axis=1, keepdims=True).astype(jnp.int32)
    move = ids_ref[...] + 1
    boards, span = plan.line * plan.share, plan.share * plan.capacity
    member = lax.broadcasted_iota(jnp.int32, (boards, count), 0) == board_row
    parts = [jnp.where(member, part.astype(F32), 0.0) for part in (move // 64, move % 64)]
    lane = lax.broadcasted_iota(jnp.int32, (count, depth), 1)
    ranked = jnp.where(rank == (lane % span) % plan.capacity, 1.0, 0.0).astype(BF16)
    found = matmul(jnp.concatenate(parts, axis=0).astype(BF16), ranked)
    lane = lax.broadcasted_iota(jnp.int32, (2 * boards, depth), 1)
    row = lax.broadcasted_iota(jnp.int32, (2 * boards, depth), 0)
    keep = (row // boards == lane // span) & (row % plan.share == (lane % span) // plan.capacity)
    found = jnp.where(keep, found, 0.0)
    lists = []
    for line in range(plan.line):
        at = line * plan.share
        both = found[at : at + plan.share] + found[boards + at : boards + at + plan.share]
        lists.append(jnp.sum(both, axis=0, keepdims=True))

    if plan.pairs % 16 == 0:
        turn_weights(plan, group, lists, copies[3:], wq, wkv, ws_ref, out_ref)
    else:
        pick_weights(plan, group, lists, copies[3:], wq, wkv, ws_ref, out_ref, pick)


def turn_weights(plan, group, lists, copies, wq, wkv, ws_ref, out_ref):
    for copy in copies:
        copy.wait()
    q = wq[...].T
    k = wkv[:, :HD].T
    folds = matmul(ws_ref[...], wkv[:, HD:], NT)
    row = lax.broadcasted_iota(jnp.int32, folds.shape, 0)
    pairs = plan.pairs
    zeros = jnp.zeros((plan.rows - plan.list_at - 1, folds.shape[1]), F32)
    for pair in range(plan.pair):
        first = (group * plan.pair + pair) * plan.mine
        mine = [jnp.sum(jnp.where(row == first + h, folds, 0.0), axis=0, keepdims=True) for h in range(plan.mine)]
        for line in range(plan.line):
            peer = line * plan.pair + pair
            for part in range(2):
                entry = part * HALF + line * pairs
                for h in range(plan.mine):
                    at = (part * plan.mine + h) * pairs
                    source = (pair * plan.mine + h) * HD + entry
                    out_ref[peer, at : at + pairs] = q[source : source + pairs]
                at = plan.q_rows + part * pairs
                out_ref[peer, at : at + pairs] = k[entry : entry + pairs]
            last = jnp.concatenate([*mine, lists[line], zeros], axis=0)
            out_ref[peer, plan.fold_at :] = last.astype(BF16)


def pick_weights(plan, group, lists, copies, wq, wkv, ws_ref, out_ref, pick):
    rows, half_cols = plan.rows, wq.shape[1]
    r = lax.broadcasted_iota(jnp.int32, (rows, 1), 0)
    part = r // (plan.mine * plan.pairs)
    head = (r // plan.pairs) % plan.mine
    entry = r % plan.pairs
    is_q = r < plan.q_rows
    k_at = r - plan.q_rows
    is_k = (k_at >= 0) & (k_at < plan.k_rows)
    f_at = r - plan.fold_at
    is_f = (f_at >= 0) & (f_at < plan.mine)
    q_lane = lax.broadcasted_iota(jnp.int32, (rows, half_cols), 1)
    k_lane = lax.broadcasted_iota(jnp.int32, (rows, HD), 1)
    ws = ws_ref[...].astype(F32)

    def fill(peer, carry):
        line, pair = peer // plan.pair, peer % plan.pair
        column = (pair * plan.mine + head) * HD + part * HALF + line * plan.pairs + entry
        column = jnp.where(is_q, column, -1)
        at = pl.ds(pl.multiple_of(peer * rows, 8), rows)
        pick[at, :half_cols] = jnp.where(q_lane == column, 1.0, 0.0)
        k_column = (k_at // plan.pairs) * HALF + line * plan.pairs + k_at % plan.pairs
        k_column = jnp.where(is_k, k_column, -1)
        pick[at, half_cols : half_cols + HD] = jnp.where(k_lane == k_column, 1.0, 0.0)
        fold = jnp.zeros((rows, HD), F32)
        my_head = jnp.where(is_f, (group * plan.pair + pair) * plan.mine + f_at, -1)
        for h in range(plan.heads):
            fold = jnp.where(my_head == h, ws[h : h + 1], fold)
        pick[at, half_cols + HD :] = fold
        return carry

    lax.fori_loop(0, plan.peers, fill, 0, unroll=plan.peers <= 8)

    for copy in copies:
        copy.wait()
    left = pick[...].astype(BF16)
    total = matmul(left[:, :half_cols], wq[...], NT) + matmul(left[:, half_cols:], wkv[...], NT)
    for peer in range(plan.peers):
        mine = total[peer * rows : (peer + 1) * rows]
        out_ref[peer] = jnp.where(r == plan.list_at, lists[peer // plan.pair], mine).astype(BF16)


def normalize(table_hbm, gain_ref, after_ref, *refs):
    *outs, mark_ref, gain, buffers, made, sems, out_sems = refs
    held, block, _ = buffers.shape
    steps = table_hbm.shape[0] // block
    each = outs[0].shape[0] // block

    def copy(step):
        source = table_hbm.at[pl.ds(step * block, block)]
        return pltpu.make_async_copy(source, buffers.at[step % held], sems.at[step % held])

    def store(step):
        target = outs[step // each].at[pl.ds(step % each * block, block)]
        return pltpu.make_async_copy(made.at[step % held], target, out_sems.at[step % held])

    for step in range(min(held, steps)):
        copy(step).start()
    rows = gain_ref[...].astype(F32)
    gain[...] = jnp.concatenate([rows[r : r + 1] for r in range(rows.shape[0])], axis=1)
    for step in range(steps):
        copy(step).wait()
        if step >= held:
            store(step - held).wait()
        raw = buffers[step % held].astype(F32)
        inverse = lax.rsqrt(jnp.mean(raw * raw, axis=-1, keepdims=True) + EPS)
        made[step % held] = (raw * inverse * gain[...]).astype(BF16)
        store(step).start()
        if step + held < steps:
            copy(step + held).start()
    for step in range(max(0, steps - held), steps):
        store(step).wait()
    mark = pltpu.make_async_copy(made.at[0, pl.ds(0, mark_ref.shape[0])], mark_ref, out_sems.at[0])
    mark.start()
    mark.wait()


def read_lists(plan, w_ref, out_ref):
    share, capacity, peers = plan.share, plan.capacity, plan.peers
    span = share * capacity
    if len(w_ref.shape) == 3:
        rows = [w_ref[s].astype(F32)[plan.list_at : plan.list_at + 1] for s in range(peers)]
    else:
        row = w_ref[...].astype(F32)[plan.list_at : plan.list_at + 1]
        rows = [row[:, s * 2 * span : (s + 1) * 2 * span] for s in range(peers)]
    rows = jnp.concatenate(rows, axis=0)
    lane = lax.broadcasted_iota(jnp.int32, (share * peers, 2 * span), 1)
    row = lax.broadcasted_iota(jnp.int32, (share * peers, 2 * span), 0)
    lane = jnp.where(lane < span, lane, lane - span)
    spread = jnp.concatenate([rows] * share, axis=0)
    spread = jnp.where(lane // capacity == row // peers, spread, 0.0).astype(BF16)
    c = lax.broadcasted_iota(jnp.int32, (2 * span, plan.slots), 0)
    slot = lax.broadcasted_iota(jnp.int32, (2 * span, plan.slots), 1)
    scale = jnp.where(c < span, 64.0, 1.0)
    place = jnp.where(c % capacity == slot % capacity, scale, 0.0).astype(BF16)
    listed = matmul(spread, place)
    row = lax.broadcasted_iota(jnp.int32, listed.shape, 0)
    slot = lax.broadcasted_iota(jnp.int32, listed.shape, 1)
    listed = jnp.where(slot // capacity == row % peers, listed, 0.0)
    out_ref[...] = jnp.sum(listed.reshape(share, peers, plan.slots), axis=1)


def project(plan, place, lists, place_ref, w_ref, normed_ref, turn_ref, after_ref, *refs):
    if lists:
        *refs, list_ref = refs
        read_lists(plan, w_ref, list_ref)
    q_ref, vo_ref = refs[-2:]
    turns = turn_ref[place_ref[LINE]]
    half, k_half = plan.q_rows // 2, plan.k_rows // 2
    cosine, sine = turns[:, 0:1], turns[:, 1:2]
    cos_k, sin_k = cosine[:k_half], sine[:k_half]
    moves = normed_ref.shape[0]
    block = min(moves, 256)
    for start in range(0, moves, block):
        at, to = slice(start, start + block), slice(place + start, place + start + block)
        if len(w_ref.shape) == 3:
            depth = w_ref.shape[2]
            total = None
            for s in range(w_ref.shape[0]):
                term = matmul(w_ref[s], normed_ref[at, s * depth : (s + 1) * depth], NT)
                total = term if total is None else total + term
        else:
            total = matmul(w_ref[...], normed_ref[at, :], NT)
        first, second = total[:half], total[half : 2 * half]
        f_first = (first * cosine - second * sine).astype(BF16).astype(F32)
        f_second = (second * cosine + first * sine).astype(BF16).astype(F32)
        first, second = total[plan.q_rows : plan.q_rows + k_half], total[plan.q_rows + k_half : plan.fold_at]
        k_first = (first * cos_k - second * sin_k).astype(BF16).astype(F32)
        k_second = (second * cos_k + first * sin_k).astype(BF16).astype(F32)
        logits, tails = [], []
        for h in range(plan.mine):
            own = slice(h * k_half, (h + 1) * k_half)
            logit = jnp.sum(f_first[own] * k_first + f_second[own] * k_second, axis=0, keepdims=True)
            logits.append(logit.astype(BF16).astype(F32))
            tails.append(logit - logits[-1])
        pad = plan.line_rows - plan.q_rows - 2 * plan.mine
        pieces = [f_first, f_second, *logits, *tails]
        if pad:
            pieces.append(jnp.zeros((pad, block), F32))
        out = jnp.concatenate(pieces, axis=0).astype(BF16)
        if plan.direct:
            q_ref[:, to] = out
        else:
            for line in range(plan.line):
                q_ref[line, :, to] = out
        vo_ref[:, to] = total[plan.fold_at : plan.list_at]


def tied(x, *others):
    return pl.pallas_call(
        lambda *refs: None,
        out_shape=shape(x.shape, x.dtype),
        in_specs=[untouched()] + [pl.BlockSpec(memory_space=pltpu.HBM)] * len(others),
        out_specs=untouched(),
        input_output_aliases={0: 0},
        compiler_params=limits(1),
        cost_estimate=cost(0, 0),
    )(x, *others)


def pack_prefix(plan, prefix_hbm, ws_hbm, after_ref, out_ref, *scratch):
    values, ws_ref, sems = scratch
    boards = values.shape[0]
    heads = plan.heads
    copies = (
        pltpu.make_async_copy(ws_hbm, ws_ref, sems.at[0]),
        pltpu.make_async_copy(prefix_hbm.at[:, :, pl.ds(HD, HD)], values, sems.at[1]),
        pltpu.make_async_copy(prefix_hbm.at[:, :, pl.ds(0, HD)], out_ref.at[pl.ds(0, boards)], sems.at[2]),
    )
    for copy in copies:
        copy.start()
    copies[0].wait()
    span = HD // boards
    ws = jnp.concatenate([ws_ref[...].astype(F32)] * (HD // heads), axis=0)
    row = lax.broadcasted_iota(jnp.int32, (HD, 1), 0)
    copies[1].wait()
    fold = None
    for board in range(boards):
        keep = (row // span == board) & (row % span < 2 * heads)
        term = matmul(values[board], jnp.where(keep, ws, 0.0).astype(BF16), NT)
        fold = term if fold is None else fold + term
    rounded = fold.astype(BF16).astype(F32)
    lane = lax.broadcasted_iota(jnp.int32, fold.shape, 1)
    out_ref[boards] = jnp.where(lane % span < heads, rounded, fold - rounded).astype(BF16)
    copies[2].wait()


def fold_columns(plan, here, block, board, boards, heads):
    lanes = plan.mine * plan.slots
    row = lax.broadcasted_iota(jnp.int32, (HD, lanes), 0) - board * (HD // boards)
    head = here * plan.mine + lax.broadcasted_iota(jnp.int32, (HD, lanes), 1) // plan.slots
    pick = jnp.where((row == head) | (row == head + heads), 1.0, 0.0).astype(BF16)
    return matmul(block, pick)


def prepare(plan, place_ref, board_ref, own_ref, other_ref, *rest):
    *prefix_refs, chosen_ref, fold_ref, slot_ref = rest
    count = board_ref.shape[1]
    board_row = board_ref[...]
    board_col = jnp.broadcast_to(board_row.astype(F32), (8, count)).T[:, 0:1].astype(jnp.int32)
    ahead = lax.broadcasted_iota(jnp.int32, (count, count), 0) < lax.broadcasted_iota(jnp.int32, (count, count), 1)
    rank = jnp.sum(jnp.where((board_col == board_row) & ahead, 1.0, 0.0), axis=0, keepdims=True)
    slot_ref[...] = rank.astype(jnp.int32) + place_ref[PEER] * plan.capacity
    here = place_ref[SLAB]
    boards, moves = chosen_ref.shape[0], chosen_ref.shape[1]
    move_at = lax.broadcasted_iota(jnp.int32, (moves, plan.slots), 0) + 1

    def step(board, carry):
        for j in range(plan.slab):
            place = ((here ^ j) % plan.pair) * boards + board
            row = (own_ref, other_ref)[j // plan.pair][pl.ds(place, 1), :].astype(jnp.int32)
            at = slice(j * plan.slots, (j + 1) * plan.slots)
            chosen_ref[board, :, at] = jnp.where(move_at == row, 1.0, 0.0).astype(BF16)
        for j, prefix_ref in enumerate(prefix_refs):
            fold_ref[j, board] = fold_columns(plan, here, prefix_ref[boards], board, boards, plan.heads)
        return carry

    lax.fori_loop(0, boards, step, 0)


def attend(plan, place_ref, vo_ref, own_ref, other_ref, chosen_ref, fold_ref, *rest):
    prefix_refs, rest = rest[: plan.slab], rest[plan.slab :]
    *q_refs, out_ref, table, extra, scores, taken_even, taken_odd = rest
    here = place_ref[SLAB]
    mine, heads, slots = plan.mine, plan.heads, plan.slots
    moves = vo_ref.shape[1]
    boards = prefix_refs[0].shape[0] - 1
    query_rows = mine * HD

    mixed = None
    for step, q_ref in enumerate(q_refs):
        r = lax.broadcasted_iota(jnp.int32, (query_rows + 8, q_ref.shape[0]), 0)
        c = lax.broadcasted_iota(jnp.int32, (query_rows + 8, q_ref.shape[0]), 1)
        line, at = (place_ref[LINE] ^ step, c) if plan.direct else (c // plan.line_rows, c % plan.line_rows)
        part, head, entry = at // (mine * plan.pairs), (at // plan.pairs) % mine, at % plan.pairs
        goes = jnp.where(at < plan.q_rows, head * HD + part * HALF + line * plan.pairs + entry, -1)
        tail = at - plan.q_rows
        goes = jnp.where((tail >= 0) & (tail < 2 * mine), query_rows + tail % mine, goes)
        term = matmul(jnp.where(r == goes, 1.0, 0.0).astype(BF16), q_ref[...])
        mixed = term if mixed is None else mixed + term
    table[:query_rows] = mixed[:query_rows].astype(BF16)
    extra[...] = jnp.zeros_like(extra)
    for place, value in ((0, mixed[query_rows : query_rows + mine]), (2 * mine, vo_ref[...])):
        rounded = value.astype(BF16).astype(F32)
        extra[place : place + mine] = rounded
        extra[place + mine : place + 2 * mine] = value - rounded
    table[query_rows:] = extra[...].astype(BF16)

    scale = math.log2(math.e) / math.sqrt(HD)
    def per_head(x, base):
        pieces = [x[base + h : base + h + 1] + x[base + mine + h : base + mine + h + 1] for h in range(mine)]
        return jnp.concatenate(pieces, axis=1)

    def moves_of(j, board):
        place = ((here ^ j) % plan.pair) * boards + board
        return (own_ref, other_ref)[j // plan.pair][pl.ds(place, 1), :].astype(jnp.int32)

    def gather(board, taken):
        taken[...] = matmul(table[...], chosen_ref[board])

    def score_board(board, taken):
        for j in range(plan.slab):
            x = taken[:, j * slots : (j + 1) * slots]
            q = jnp.concatenate([x[h * HD : (h + 1) * HD].astype(BF16) for h in range(mine)], axis=1)
            logits = matmul(prefix_refs[j][board], q)
            if j < plan.slab - 1:
                fold = fold_ref[j, board]
            else:
                fold = fold_columns(plan, here, prefix_refs[j][boards], board, boards, heads)
            own_logit = per_head(x, query_rows)
            own_value = per_head(x, query_rows + 2 * mine)
            peak = jnp.maximum(jnp.max(logits, axis=0, keepdims=True), own_logit)
            weight = jnp.exp2((logits - peak) * scale)
            own_weight = jnp.exp2((own_logit - peak) * scale)
            denom = jnp.sum(weight, axis=0, keepdims=True) + own_weight
            value = (jnp.sum(weight * fold, axis=0, keepdims=True) + own_value * own_weight) / denom
            score = sum(value[:, h * slots : (h + 1) * slots] for h in range(mine))
            scores[here ^ j, pl.ds(board, 1), :] = jnp.where(moves_of(j, board) > 0, score, DEAD)

    gather(0, taken_even)

    def step(at, carry):
        board = 2 * at
        gather(jnp.minimum(board + 1, boards - 1), taken_odd)
        score_board(board, taken_even)
        gather(jnp.minimum(board + 2, boards - 1), taken_even)
        score_board(jnp.minimum(board + 1, boards - 1), taken_odd)
        return carry

    lax.fori_loop(0, -(-boards // 2), step, 0)
    live = scores[...] > 0.5 * DEAD
    count = jnp.sum(jnp.where(live, 1.0, 0.0), axis=2, keepdims=True)
    mean = jnp.sum(jnp.where(live, scores[...], 0.0), axis=2, keepdims=True) / jnp.maximum(count, 1.0)
    centered = jnp.where(live, scores[...] - mean, DEAD)
    for g in range(plan.groups):
        both = jnp.concatenate([centered[g * plan.pair + p] for p in range(plan.pair)], axis=0).astype(BF16)
        for copy in range(out_ref.shape[1]):
            out_ref[g, copy] = both


def finish(plan, parts_ref, board_ref, slot_ref, out_ref):
    line = parts_ref.shape[1]
    columns = []
    for at in range(line):
        total = None
        for g in range(parts_ref.shape[0]):
            for p in range(parts_ref.shape[2]):
                term = parts_ref[g, at, p].astype(F32)
                total = term if total is None else total + term
        columns.append(total)
    scores = jnp.concatenate(columns, axis=0)
    live = scores > 0.5 * DEAD
    peak = jnp.max(scores, axis=1, keepdims=True)
    denom = jnp.sum(jnp.where(live, jnp.exp(scores - peak), 0.0), axis=1, keepdims=True)
    logprob = jnp.where(live, scores - peak - jnp.log(denom), 0.0)
    count = board_ref.shape[1]
    member = lax.broadcasted_iota(jnp.int32, (scores.shape[0], count), 0) == board_ref[...]
    member = jnp.where(member, 1.0, 0.0).astype(BF16)
    found = jnp.zeros((plan.slots, count), F32)
    for _ in range(3):
        rounded = logprob.astype(BF16)
        found = found + matmul(rounded, member, TN)
        logprob = logprob - rounded.astype(F32)
    at = lax.broadcasted_iota(jnp.int32, (plan.slots, count), 0) == slot_ref[...]
    out_ref[...] = jnp.sum(jnp.where(at, found, 0.0), axis=0, keepdims=True)


def untouched():
    return pl.BlockSpec(memory_space=pl.ANY)


def local_call(kernel, place, args, outs, scratch=(), mib=40, copied=(), flops=0, nbytes=0, aliases=None):
    vmem = pl.BlockSpec(memory_space=pltpu.VMEM)
    return pl.pallas_call(
        kernel,
        out_shape=outs,
        in_specs=[pl.BlockSpec(memory_space=pltpu.SMEM)]
        + [untouched() if at in copied else vmem for at in range(len(args))],
        out_specs=jax.tree.map(lambda x: vmem, outs),
        scratch_shapes=scratch,
        input_output_aliases=aliases or {},
        compiler_params=limits(mib),
        cost_estimate=cost(flops, nbytes),
    )(place, *args)


def cost(flops, nbytes):
    return pl.CostEstimate(flops=int(flops), bytes_accessed=int(nbytes), transcendentals=0)


def swap(x, names, size, step):
    return lax.ppermute(x, names, [(at, at ^ step) for at in range(size)])


def shape(dims, dtype):
    return jax.ShapeDtypeStruct(tuple(dims), dtype)


def turn_table(position):
    frequency = THETA ** (-2.0 * np.arange(HALF, dtype=np.float32) / HD)
    angles = np.float32(position) * frequency.astype(np.float32)
    return np.stack([np.cos(angles), np.sin(angles)], axis=1).astype(np.float32)


def per_device(prefix_kv, move_ids, move_board, move_table, norm_gain, w_query, w_keyval, w_score):
    row_count = move_ids.shape[0]
    boards_here, prefix_len, _ = prefix_kv.shape
    moves, width = move_table.shape
    groups, line, pair = lax.axis_size("groups"), lax.axis_size("line"), lax.axis_size("pair")
    board_total = boards_here * line * pair
    capacity = max(2, (2 * row_count + board_total - 1) // board_total)
    heads = w_query.shape[1] // HD
    plan = Plan(groups, line, pair, heads, capacity, pair * boards_here)
    depth = w_query.shape[0]
    group_at = lax.axis_index("groups").astype(jnp.int32)
    line_at = lax.axis_index("line").astype(jnp.int32)
    pair_at = lax.axis_index("pair").astype(jnp.int32)
    place = jnp.stack([group_at, line_at, line_at * pair + pair_at, group_at * pair + pair_at])
    ws = w_score.reshape(heads, HD)
    slab_axes = ("groups", "pair")
    board_row = move_board.reshape(1, row_count)

    half_cols = w_query.shape[1] // groups
    packed = local_call(
        functools.partial(pack_weights, plan),
        group_at.reshape(1),
        (w_query, w_keyval, ws, board_row, move_ids.reshape(1, row_count)),
        shape((plan.peers, plan.rows, depth), BF16),
        [
            pltpu.VMEM((depth, half_cols), BF16),
            pltpu.VMEM((depth, 2 * HD), BF16),
            pltpu.VMEM((heads, HD), BF16),
            pltpu.VMEM((1, row_count), jnp.int32),
            pltpu.VMEM((1, row_count), jnp.int32),
            pltpu.VMEM((plan.peers * plan.rows, half_cols + 2 * HD), F32),
            pltpu.SemaphoreType.DMA((5,)),
        ],
        62,
        range(5),
    )
    weights = lax.all_to_all(packed, ("line", "pair"), split_axis=0, concat_axis=0, tiled=True)

    payload = pl.pallas_call(
        functools.partial(pack_prefix, plan),
        out_shape=shape((boards_here + 1, prefix_len, HD), BF16),
        in_specs=[untouched()] * 3,
        out_specs=pl.BlockSpec(memory_space=pltpu.VMEM),
        scratch_shapes=[
            pltpu.VMEM((boards_here, prefix_len, HD), BF16),
            pltpu.VMEM((heads, HD), BF16),
            pltpu.SemaphoreType.DMA((3,)),
        ],
        compiler_params=limits(56),
        cost_estimate=cost(0, 0),
    )(prefix_kv, ws, packed)
    beside = swap(payload, slab_axes, plan.slab, 1)
    across = swap(payload, slab_axes, plan.slab, 2)

    block = min(moves, 128)
    vmem = pl.BlockSpec(memory_space=pltpu.VMEM)
    *normed, mark = pl.pallas_call(
        normalize,
        out_shape=[*[shape((moves // 2, width), BF16)] * 2, pltpu.HBM((8, width), BF16)],
        in_specs=[untouched(), vmem, untouched()],
        out_specs=[untouched()] * 3,
        scratch_shapes=[
            pltpu.VMEM((1, width), F32),
            pltpu.VMEM((3, block, width), BF16),
            pltpu.VMEM((3, block, width), BF16),
            pltpu.SemaphoreType.DMA((3,)),
            pltpu.SemaphoreType.DMA((3,)),
        ],
        compiler_params=limits(58),
        cost_estimate=cost(moves * width, moves * width // 4),
    )(move_table, norm_gain.reshape(width // HD, HD), packed)
    turns = turn_table(prefix_len).reshape(line, 1, plan.pairs, 2)
    turns = np.tile(turns, (1, plan.mine, 1, 1)).reshape(line, plan.mine * plan.pairs, 2)
    flat = weights.transpose(1, 0, 2).reshape(plan.rows, width) if depth % HD else weights
    sent = (plan.line_rows, moves)
    outs = (shape(sent if plan.direct else (line, *sent), BF16), shape((plan.mine, moves), F32))
    across = tied(across, mark)
    diagonal = swap(across, slab_axes, plan.slab, 1)
    filled, listed = (), None
    for step, after in enumerate((across, beside)):
        made = local_call(
            functools.partial(project, plan, step * moves // 2, step == 0),
            place,
            (flat, normed[step], jnp.asarray(turns), after, *filled),
            [*outs, *([shape((plan.share, plan.slots), F32)] if step == 0 else [])],
            (),
            20,
            (3,),
            moves * width * 1024,
            moves * width,
            {5: 0, 6: 1} if filled else None,
        )
        filled, listed = made[:2], made[2] if step == 0 else listed
    queries, own_values = filled
    other = swap(listed, slab_axes, plan.slab, pair)
    if plan.direct:
        queries = [queries] + [swap(queries, "line", line, step) for step in range(1, line)]
    else:
        queries = lax.all_to_all(queries, "line", split_axis=0, concat_axis=0, tiled=True)
        queries = [queries.reshape(line * plan.line_rows, moves)]

    query_rows = plan.mine * HD
    back = plan.peers * lax.axis_size("tensor")
    chosen, folds, slot_row = local_call(
        functools.partial(prepare, plan),
        place,
        (board_row, listed, other, payload, beside, across),
        (
            shape((boards_here, moves, plan.slab * plan.slots), BF16),
            shape((plan.slab - 1, boards_here, prefix_len, plan.mine * plan.slots), F32),
            shape((1, row_count), jnp.int32),
        ),
        mib=20,
        flops=10**9,
        nbytes=10**6,
    )
    parts = local_call(
        functools.partial(attend, plan),
        place,
        (own_values, listed, other, chosen, folds, payload, beside, across, diagonal, *queries),
        shape((groups, back, plan.share, plan.slots), BF16),
        [
            pltpu.VMEM((query_rows + 16, moves), BF16),
            pltpu.VMEM((16, moves), F32),
            pltpu.VMEM((plan.slab, boards_here, plan.slots), F32),
            pltpu.VMEM((query_rows + 16, plan.slab * plan.slots), F32),
            pltpu.VMEM((query_rows + 16, plan.slab * plan.slots), F32),
        ],
        24,
    )
    parts = lax.all_to_all(
        parts.reshape(groups * back, plan.share, plan.slots),
        ("groups", "line", "pair", "tensor"),
        split_axis=0,
        concat_axis=0,
        tiled=True,
    )
    parts = parts.reshape(groups, line, back // line, plan.share, plan.slots)
    logprob = pl.pallas_call(
        functools.partial(finish, plan), out_shape=shape((1, row_count), F32), compiler_params=limits(VMEM_MIB)
    )(parts, board_row, slot_row)
    return logprob.reshape(row_count)


def solution(mesh):
    order = ("groups", "dp", "tensor")
    assert mesh.axis_names == order
    pair = 2
    groups, peers, tensor = (mesh.shape[name] for name in order)
    fine = Mesh(mesh.devices.reshape(groups, peers // pair, pair, tensor), ("groups", "line", "pair", "tensor"))
    rows = ("groups", "line", "pair")
    placed = (
        P(rows, None, "tensor"),
        P(rows),
        P(rows, None),
        P(),
        P(),
        P(("line", "pair"), "tensor"),
        P(("line", "pair"), "tensor"),
        P("tensor"),
    )
    return jax.shard_map(per_device, mesh=fine, in_specs=placed, out_specs=P(rows), check_vma=False)
```

```python
import functools
import math

import jax
import jax.numpy as jnp
import numpy as np
from jax import lax
from jax.experimental import pallas as pl
from jax.experimental.pallas import tpu as pltpu
from jax.sharding import Mesh
from jax.sharding import PartitionSpec as P

HD = 128
HALF = HD // 2
EPS = 1e-06
THETA = 5000000.0
DEAD = -1e30
VMEM_MIB = 52
GROUP, LINE, PEER, SLAB = range(4)

F32 = jnp.float32
BF16 = jnp.bfloat16

NN = (((1,), (0,)), ((), ()))
NT = (((1,), (1,)), ((), ()))
TN = (((0,), (0,)), ((), ()))


def matmul(a, b, dims=NN):
    return lax.dot_general(a, b, dims, preferred_element_type=F32)


def limits(mib):
    return pltpu.CompilerParams(vmem_limit_bytes=mib * 1024 * 1024)


class Plan:
    def __init__(self, groups, line, pair, heads, capacity, share):
        self.groups, self.line, self.pair = groups, line, pair
        self.peers = line * pair
        self.slab = groups * pair
        self.heads = heads
        self.mine = heads // self.slab
        self.pairs = HALF // line
        self.q_rows = self.mine * 2 * self.pairs
        self.k_rows = 2 * self.pairs
        self.fold_at = self.q_rows + self.k_rows
        self.list_at = self.fold_at + self.mine
        self.rows = -(-(self.list_at + 1) // 8) * 8
        self.line_rows = -(-(self.q_rows + 2 * self.mine) // 8) * 8
        self.capacity = capacity
        self.share = share
        self.slots = self.peers * capacity
        self.direct = line <= 4


def pack_weights(plan, place_ref, wq_hbm, wkv_hbm, ws_hbm, board_hbm, ids_hbm, *rest):
    out_hbm, wq, wkv, ws_ref, board_ref, ids_ref, pick, made, sems, out_sems = rest
    group = place_ref[0]
    half_cols = wq.shape[1]
    columns_here = pl.ds(pl.multiple_of(group * half_cols, HD), half_cols)
    copies = (
        pltpu.make_async_copy(ws_hbm, ws_ref, sems.at[0]),
        pltpu.make_async_copy(board_hbm, board_ref, sems.at[1]),
        pltpu.make_async_copy(ids_hbm, ids_ref, sems.at[2]),
        pltpu.make_async_copy(wq_hbm.at[:, columns_here], wq, sems.at[3]),
        pltpu.make_async_copy(wkv_hbm, wkv, sems.at[4]),
    )
    for copy in copies:
        copy.start()
    for copy in copies[:3]:
        copy.wait()
    count, depth = board_ref.shape[1], wq.shape[0]
    board_row = board_ref[...]
    board_col = jnp.broadcast_to(board_row.astype(F32), (8, count)).T[:, 0:1].astype(jnp.int32)
    own = lax.broadcasted_iota(jnp.int32, (count, count), 0)
    other = lax.broadcasted_iota(jnp.int32, (count, count), 1)
    ahead = jnp.where((board_col == board_row) & (other < own), 1.0, 0.0)
    rank = jnp.sum(ahead, axis=1, keepdims=True).astype(jnp.int32)
    move = ids_ref[...] + 1
    boards, span = plan.line * plan.share, plan.share * plan.capacity
    member = lax.broadcasted_iota(jnp.int32, (boards, count), 0) == board_row
    parts = [jnp.where(member, part.astype(F32), 0.0) for part in (move // 64, move % 64)]
    lane = lax.broadcasted_iota(jnp.int32, (count, depth), 1)
    ranked = jnp.where(rank == (lane % span) % plan.capacity, 1.0, 0.0).astype(BF16)
    found = matmul(jnp.concatenate(parts, axis=0).astype(BF16), ranked)
    lane = lax.broadcasted_iota(jnp.int32, (2 * boards, depth), 1)
    row = lax.broadcasted_iota(jnp.int32, (2 * boards, depth), 0)
    keep = (row // boards == lane // span) & (row % plan.share == (lane % span) // plan.capacity)
    found = jnp.where(keep, found, 0.0)
    lists = []
    for line in range(plan.line):
        at = line * plan.share
        both = found[at : at + plan.share] + found[boards + at : boards + at + plan.share]
        lists.append(jnp.sum(both, axis=0, keepdims=True))

    def send(peer):
        return pltpu.make_async_copy(made.at[peer], out_hbm.at[peer], out_sems.at[peer])

    if plan.pairs % 16 == 0:
        turn_weights(plan, group, lists, copies[3:], wq, wkv, ws_ref, made, send)
    else:
        pick_weights(plan, group, lists, copies[3:], wq, wkv, ws_ref, made, send, pick)


def turn_weights(plan, group, lists, copies, wq, wkv, ws_ref, out_ref, send):
    for copy in copies:
        copy.wait()
    q = wq[...].T
    k = wkv[:, :HD].T
    folds = matmul(ws_ref[...], wkv[:, HD:], NT)
    row = lax.broadcasted_iota(jnp.int32, folds.shape, 0)
    pairs = plan.pairs
    zeros = jnp.zeros((plan.rows - plan.list_at - 1, folds.shape[1]), F32)
    for pair in range(plan.pair):
        first = (group * plan.pair + pair) * plan.mine
        mine = [jnp.sum(jnp.where(row == first + h, folds, 0.0), axis=0, keepdims=True) for h in range(plan.mine)]
        for line in range(plan.line):
            peer = line * plan.pair + pair
            for part in range(2):
                entry = part * HALF + line * pairs
                for h in range(plan.mine):
                    at = (part * plan.mine + h) * pairs
                    source = (pair * plan.mine + h) * HD + entry
                    out_ref[peer, at : at + pairs] = q[source : source + pairs]
                at = plan.q_rows + part * pairs
                out_ref[peer, at : at + pairs] = k[entry : entry + pairs]
            last = jnp.concatenate([*mine, lists[line], zeros], axis=0)
            out_ref[peer, plan.fold_at :] = last.astype(BF16)
            send(peer).start()
    for peer in range(plan.peers):
        send(peer).wait()


def pick_weights(plan, group, lists, copies, wq, wkv, ws_ref, out_ref, send, pick):
    rows, half_cols = plan.rows, wq.shape[1]
    r = lax.broadcasted_iota(jnp.int32, (rows, 1), 0)
    part = r // (plan.mine * plan.pairs)
    head = (r // plan.pairs) % plan.mine
    entry = r % plan.pairs
    is_q = r < plan.q_rows
    k_at = r - plan.q_rows
    is_k = (k_at >= 0) & (k_at < plan.k_rows)
    f_at = r - plan.fold_at
    is_f = (f_at >= 0) & (f_at < plan.mine)
    q_lane = lax.broadcasted_iota(jnp.int32, (rows, half_cols), 1)
    k_lane = lax.broadcasted_iota(jnp.int32, (rows, HD), 1)
    ws = ws_ref[...].astype(F32)

    def fill(peer, carry):
        line, pair = peer // plan.pair, peer % plan.pair
        column = (pair * plan.mine + head) * HD + part * HALF + line * plan.pairs + entry
        column = jnp.where(is_q, column, -1)
        at = pl.ds(pl.multiple_of(peer * rows, 8), rows)
        pick[at, :half_cols] = jnp.where(q_lane == column, 1.0, 0.0)
        k_column = (k_at // plan.pairs) * HALF + line * plan.pairs + k_at % plan.pairs
        k_column = jnp.where(is_k, k_column, -1)
        pick[at, half_cols : half_cols + HD] = jnp.where(k_lane == k_column, 1.0, 0.0)
        fold = jnp.zeros((rows, HD), F32)
        my_head = jnp.where(is_f, (group * plan.pair + pair) * plan.mine + f_at, -1)
        for h in range(plan.heads):
            fold = jnp.where(my_head == h, ws[h : h + 1], fold)
        pick[at, half_cols + HD :] = fold
        return carry

    lax.fori_loop(0, plan.peers, fill, 0, unroll=plan.peers <= 8)

    for copy in copies:
        copy.wait()
    left = pick[...].astype(BF16)
    total = matmul(left[:, :half_cols], wq[...], NT) + matmul(left[:, half_cols:], wkv[...], NT)
    for peer in range(plan.peers):
        mine = total[peer * rows : (peer + 1) * rows]
        out_ref[peer] = jnp.where(r == plan.list_at, lists[peer // plan.pair], mine).astype(BF16)
        send(peer).start()
    for peer in range(plan.peers):
        send(peer).wait()


def normalize(table_hbm, gain_ref, after_ref, *refs):
    *outs, mark_ref, gain, buffers, made, sems, out_sems = refs
    held, block, _ = buffers.shape
    steps = table_hbm.shape[0] // block
    each = outs[0].shape[0] // block

    def copy(step):
        source = table_hbm.at[pl.ds(step * block, block)]
        return pltpu.make_async_copy(source, buffers.at[step % held], sems.at[step % held])

    def store(step):
        target = outs[step // each].at[pl.ds(step % each * block, block)]
        return pltpu.make_async_copy(made.at[step % held], target, out_sems.at[step % held])

    for step in range(min(held, steps)):
        copy(step).start()
    rows = gain_ref[...].astype(F32)
    gain[...] = jnp.concatenate([rows[r : r + 1] for r in range(rows.shape[0])], axis=1)
    for step in range(steps):
        copy(step).wait()
        if step >= held:
            store(step - held).wait()
        raw = buffers[step % held].astype(F32)
        inverse = lax.rsqrt(jnp.mean(raw * raw, axis=-1, keepdims=True) + EPS)
        made[step % held] = (raw * inverse * gain[...]).astype(BF16)
        store(step).start()
        if step + held < steps:
            copy(step + held).start()
    for step in range(max(0, steps - held), steps):
        store(step).wait()
    mark = pltpu.make_async_copy(made.at[0, pl.ds(0, mark_ref.shape[0])], mark_ref, out_sems.at[0])
    mark.start()
    mark.wait()


def read_lists(plan, w_ref, out_ref):
    share, capacity, peers = plan.share, plan.capacity, plan.peers
    span = share * capacity
    if len(w_ref.shape) == 3:
        rows = [w_ref[s].astype(F32)[plan.list_at : plan.list_at + 1] for s in range(peers)]
    else:
        row = w_ref[...].astype(F32)[plan.list_at : plan.list_at + 1]
        rows = [row[:, s * 2 * span : (s + 1) * 2 * span] for s in range(peers)]
    rows = jnp.concatenate(rows, axis=0)
    lane = lax.broadcasted_iota(jnp.int32, (share * peers, 2 * span), 1)
    row = lax.broadcasted_iota(jnp.int32, (share * peers, 2 * span), 0)
    lane = jnp.where(lane < span, lane, lane - span)
    spread = jnp.concatenate([rows] * share, axis=0)
    spread = jnp.where(lane // capacity == row // peers, spread, 0.0).astype(BF16)
    c = lax.broadcasted_iota(jnp.int32, (2 * span, plan.slots), 0)
    slot = lax.broadcasted_iota(jnp.int32, (2 * span, plan.slots), 1)
    scale = jnp.where(c < span, 64.0, 1.0)
    place = jnp.where(c % capacity == slot % capacity, scale, 0.0).astype(BF16)
    listed = matmul(spread, place)
    row = lax.broadcasted_iota(jnp.int32, listed.shape, 0)
    slot = lax.broadcasted_iota(jnp.int32, listed.shape, 1)
    listed = jnp.where(slot // capacity == row % peers, listed, 0.0)
    out_ref[...] = jnp.sum(listed.reshape(share, peers, plan.slots), axis=1)


def project(plan, place, lists, place_ref, w_ref, normed_ref, turn_ref, after_ref, *refs):
    if lists:
        *refs, list_ref = refs
        read_lists(plan, w_ref, list_ref)
    q_ref, vo_ref = refs[-2:]
    turns = turn_ref[place_ref[LINE]]
    half, k_half = plan.q_rows // 2, plan.k_rows // 2
    cosine, sine = turns[:, 0:1], turns[:, 1:2]
    cos_k, sin_k = cosine[:k_half], sine[:k_half]
    moves = normed_ref.shape[0]
    block = min(moves, 256)
    for start in range(0, moves, block):
        at, to = slice(start, start + block), slice(place + start, place + start + block)
        if len(w_ref.shape) == 3:
            depth = w_ref.shape[2]
            total = None
            for s in range(w_ref.shape[0]):
                term = matmul(w_ref[s], normed_ref[at, s * depth : (s + 1) * depth], NT)
                total = term if total is None else total + term
        else:
            total = matmul(w_ref[...], normed_ref[at, :], NT)
        first, second = total[:half], total[half : 2 * half]
        f_first = (first * cosine - second * sine).astype(BF16).astype(F32)
        f_second = (second * cosine + first * sine).astype(BF16).astype(F32)
        first, second = total[plan.q_rows : plan.q_rows + k_half], total[plan.q_rows + k_half : plan.fold_at]
        k_first = (first * cos_k - second * sin_k).astype(BF16).astype(F32)
        k_second = (second * cos_k + first * sin_k).astype(BF16).astype(F32)
        logits, tails = [], []
        for h in range(plan.mine):
            own = slice(h * k_half, (h + 1) * k_half)
            logit = jnp.sum(f_first[own] * k_first + f_second[own] * k_second, axis=0, keepdims=True)
            logits.append(logit.astype(BF16).astype(F32))
            tails.append(logit - logits[-1])
        pad = plan.line_rows - plan.q_rows - 2 * plan.mine
        pieces = [f_first, f_second, *logits, *tails]
        if pad:
            pieces.append(jnp.zeros((pad, block), F32))
        out = jnp.concatenate(pieces, axis=0).astype(BF16)
        if plan.direct:
            q_ref[:, to] = out
        else:
            for line in range(plan.line):
                q_ref[line, :, to] = out
        vo_ref[:, to] = total[plan.fold_at : plan.list_at]


def tied(x, *others):
    return pl.pallas_call(
        lambda *refs: None,
        out_shape=shape(x.shape, x.dtype),
        in_specs=[untouched()] + [pl.BlockSpec(memory_space=pltpu.HBM)] * len(others),
        out_specs=untouched(),
        input_output_aliases={0: 0},
        compiler_params=limits(1),
        cost_estimate=cost(0, 0),
    )(x, *others)


def pack_prefix(plan, prefix_hbm, ws_hbm, after_ref, out_ref, *scratch):
    values, ws_ref, sems = scratch
    boards = values.shape[0]
    heads = plan.heads
    copies = (
        pltpu.make_async_copy(ws_hbm, ws_ref, sems.at[0]),
        pltpu.make_async_copy(prefix_hbm.at[:, :, pl.ds(HD, HD)], values, sems.at[1]),
        pltpu.make_async_copy(prefix_hbm.at[:, :, pl.ds(0, HD)], out_ref.at[pl.ds(0, boards)], sems.at[2]),
    )
    for copy in copies:
        copy.start()
    copies[0].wait()
    span = HD // boards
    ws = jnp.concatenate([ws_ref[...].astype(F32)] * (HD // heads), axis=0)
    row = lax.broadcasted_iota(jnp.int32, (HD, 1), 0)
    copies[1].wait()
    fold = None
    for board in range(boards):
        keep = (row // span == board) & (row % span < 2 * heads)
        term = matmul(values[board], jnp.where(keep, ws, 0.0).astype(BF16), NT)
        fold = term if fold is None else fold + term
    rounded = fold.astype(BF16).astype(F32)
    lane = lax.broadcasted_iota(jnp.int32, fold.shape, 1)
    out_ref[boards] = jnp.where(lane % span < heads, rounded, fold - rounded).astype(BF16)
    copies[2].wait()


def fold_columns(plan, here, block, board, boards, heads):
    lanes = plan.mine * plan.slots
    row = lax.broadcasted_iota(jnp.int32, (HD, lanes), 0) - board * (HD // boards)
    head = here * plan.mine + lax.broadcasted_iota(jnp.int32, (HD, lanes), 1) // plan.slots
    pick = jnp.where((row == head) | (row == head + heads), 1.0, 0.0).astype(BF16)
    return matmul(block, pick)


def prepare(plan, place_ref, board_ref, own_ref, other_ref, *rest):
    *prefix_refs, chosen_ref, fold_ref, slot_ref, order_ref = rest
    count = board_ref.shape[1]
    board_row = board_ref[...]
    board_col = jnp.broadcast_to(board_row.astype(F32), (8, count)).T[:, 0:1].astype(jnp.int32)
    ahead = lax.broadcasted_iota(jnp.int32, (count, count), 0) < lax.broadcasted_iota(jnp.int32, (count, count), 1)
    rank = jnp.sum(jnp.where((board_col == board_row) & ahead, 1.0, 0.0), axis=0, keepdims=True)
    slot_ref[...] = rank.astype(jnp.int32) + place_ref[PEER] * plan.capacity
    mine, query_rows = plan.mine, plan.mine * HD
    for step in range(order_ref.shape[0]):
        r = lax.broadcasted_iota(jnp.int32, order_ref.shape[1:], 0)
        c = lax.broadcasted_iota(jnp.int32, order_ref.shape[1:], 1)
        line, at = (place_ref[LINE] ^ step, c) if plan.direct else (c // plan.line_rows, c % plan.line_rows)
        part, head, entry = at // (mine * plan.pairs), (at // plan.pairs) % mine, at % plan.pairs
        goes = jnp.where(at < plan.q_rows, head * HD + part * HALF + line * plan.pairs + entry, -1)
        tail = at - plan.q_rows
        goes = jnp.where((tail >= 0) & (tail < 2 * mine), query_rows + tail % mine, goes)
        order_ref[step] = jnp.where(r == goes, 1.0, 0.0).astype(BF16)
    here = place_ref[SLAB]
    boards, moves = chosen_ref.shape[0], chosen_ref.shape[1]
    move_at = lax.broadcasted_iota(jnp.int32, (moves, plan.slots), 0) + 1

    def step(board, carry):
        for j in range(plan.slab):
            place = ((here ^ j) % plan.pair) * boards + board
            row = (own_ref, other_ref)[j // plan.pair][pl.ds(place, 1), :].astype(jnp.int32)
            at = slice(j * plan.slots, (j + 1) * plan.slots)
            chosen_ref[board, :, at] = jnp.where(move_at == row, 1.0, 0.0).astype(BF16)
        for j, prefix_ref in enumerate(prefix_refs):
            fold_ref[j, board] = fold_columns(plan, here, prefix_ref[boards], board, boards, plan.heads)
        return carry

    lax.fori_loop(0, boards, step, 0)


def attend(plan, place_ref, vo_ref, own_ref, other_ref, chosen_ref, fold_ref, order_ref, *rest):
    prefix_refs, rest = rest[: plan.slab], rest[plan.slab :]
    *q_refs, out_ref, table, extra, scores, taken_even, taken_odd = rest
    here = place_ref[SLAB]
    mine, heads, slots = plan.mine, plan.heads, plan.slots
    moves = vo_ref.shape[1]
    boards = prefix_refs[0].shape[0] - 1
    query_rows = mine * HD

    mixed = sum(matmul(order_ref[step], q_ref[...]) for step, q_ref in enumerate(q_refs))
    table[:query_rows] = mixed[:query_rows].astype(BF16)
    extra[...] = jnp.zeros_like(extra)
    for place, value in ((0, mixed[query_rows : query_rows + mine]), (2 * mine, vo_ref[...])):
        rounded = value.astype(BF16).astype(F32)
        extra[place : place + mine] = rounded
        extra[place + mine : place + 2 * mine] = value - rounded
    table[query_rows:] = extra[...].astype(BF16)

    scale = math.log2(math.e) / math.sqrt(HD)
    def per_head(x, base):
        pieces = [x[base + h : base + h + 1] + x[base + mine + h : base + mine + h + 1] for h in range(mine)]
        return jnp.concatenate(pieces, axis=1)

    def moves_of(j, board):
        place = ((here ^ j) % plan.pair) * boards + board
        return (own_ref, other_ref)[j // plan.pair][pl.ds(place, 1), :].astype(jnp.int32)

    def gather(board, taken):
        taken[...] = matmul(table[...], chosen_ref[board])

    def score_board(board, taken):
        for j in range(plan.slab):
            x = taken[:, j * slots : (j + 1) * slots]
            q = jnp.concatenate([x[h * HD : (h + 1) * HD].astype(BF16) for h in range(mine)], axis=1)
            logits = matmul(prefix_refs[j][board], q)
            fold = fold_ref[j, board]
            own_logit = per_head(x, query_rows)
            own_value = per_head(x, query_rows + 2 * mine)
            peak = jnp.maximum(jnp.max(logits, axis=0, keepdims=True), own_logit)
            weight = jnp.exp2((logits - peak) * scale)
            own_weight = jnp.exp2((own_logit - peak) * scale)
            denom = jnp.sum(weight, axis=0, keepdims=True) + own_weight
            value = (jnp.sum(weight * fold, axis=0, keepdims=True) + own_value * own_weight) / denom
            score = sum(value[:, h * slots : (h + 1) * slots] for h in range(mine))
            scores[here ^ j, pl.ds(board, 1), :] = jnp.where(moves_of(j, board) > 0, score, DEAD)

    gather(0, taken_even)

    def step(at, carry):
        board = 2 * at
        gather(jnp.minimum(board + 1, boards - 1), taken_odd)
        score_board(board, taken_even)
        gather(jnp.minimum(board + 2, boards - 1), taken_even)
        score_board(jnp.minimum(board + 1, boards - 1), taken_odd)
        return carry

    lax.fori_loop(0, -(-boards // 2), step, 0)
    live = scores[...] > 0.5 * DEAD
    count = jnp.sum(jnp.where(live, 1.0, 0.0), axis=2, keepdims=True)
    mean = jnp.sum(jnp.where(live, scores[...], 0.0), axis=2, keepdims=True) / jnp.maximum(count, 1.0)
    centered = jnp.where(live, scores[...] - mean, DEAD)
    for g in range(plan.groups):
        both = jnp.concatenate([centered[g * plan.pair + p] for p in range(plan.pair)], axis=0).astype(BF16)
        for copy in range(out_ref.shape[1]):
            out_ref[g, copy] = both


def finish(plan, parts_ref, board_ref, slot_ref, out_ref):
    line = parts_ref.shape[1]
    columns = []
    for at in range(line):
        total = None
        for g in range(parts_ref.shape[0]):
            for p in range(parts_ref.shape[2]):
                term = parts_ref[g, at, p].astype(F32)
                total = term if total is None else total + term
        columns.append(total)
    scores = jnp.concatenate(columns, axis=0)
    live = scores > 0.5 * DEAD
    peak = jnp.max(scores, axis=1, keepdims=True)
    denom = jnp.sum(jnp.where(live, jnp.exp(scores - peak), 0.0), axis=1, keepdims=True)
    logprob = jnp.where(live, scores - peak - jnp.log(denom), 0.0)
    count = board_ref.shape[1]
    member = lax.broadcasted_iota(jnp.int32, (scores.shape[0], count), 0) == board_ref[...]
    member = jnp.where(member, 1.0, 0.0).astype(BF16)
    found = jnp.zeros((plan.slots, count), F32)
    for _ in range(3):
        rounded = logprob.astype(BF16)
        found = found + matmul(rounded, member, TN)
        logprob = logprob - rounded.astype(F32)
    at = lax.broadcasted_iota(jnp.int32, (plan.slots, count), 0) == slot_ref[...]
    out_ref[...] = jnp.sum(jnp.where(at, found, 0.0), axis=0, keepdims=True)


def untouched():
    return pl.BlockSpec(memory_space=pl.ANY)


def local_call(kernel, place, args, outs, scratch=(), mib=40, copied=(), flops=0, nbytes=0, aliases=None):
    vmem = pl.BlockSpec(memory_space=pltpu.VMEM)
    return pl.pallas_call(
        kernel,
        out_shape=outs,
        in_specs=[pl.BlockSpec(memory_space=pltpu.SMEM)]
        + [untouched() if at in copied else vmem for at in range(len(args))],
        out_specs=jax.tree.map(lambda x: vmem, outs),
        scratch_shapes=scratch,
        input_output_aliases=aliases or {},
        compiler_params=limits(mib),
        cost_estimate=cost(flops, nbytes),
    )(place, *args)


def cost(flops, nbytes):
    return pl.CostEstimate(flops=int(flops), bytes_accessed=int(nbytes), transcendentals=0)


def swap(x, names, size, step):
    return lax.ppermute(x, names, [(at, at ^ step) for at in range(size)])


def shape(dims, dtype):
    return jax.ShapeDtypeStruct(tuple(dims), dtype)


def turn_table(position):
    frequency = THETA ** (-2.0 * np.arange(HALF, dtype=np.float32) / HD)
    angles = np.float32(position) * frequency.astype(np.float32)
    return np.stack([np.cos(angles), np.sin(angles)], axis=1).astype(np.float32)


def per_device(prefix_kv, move_ids, move_board, move_table, norm_gain, w_query, w_keyval, w_score):
    row_count = move_ids.shape[0]
    boards_here, prefix_len, _ = prefix_kv.shape
    moves, width = move_table.shape
    groups, line, pair = lax.axis_size("groups"), lax.axis_size("line"), lax.axis_size("pair")
    board_total = boards_here * line * pair
    capacity = max(2, (2 * row_count + board_total - 1) // board_total)
    heads = w_query.shape[1] // HD
    plan = Plan(groups, line, pair, heads, capacity, pair * boards_here)
    depth = w_query.shape[0]
    group_at = lax.axis_index("groups").astype(jnp.int32)
    line_at = lax.axis_index("line").astype(jnp.int32)
    pair_at = lax.axis_index("pair").astype(jnp.int32)
    place = jnp.stack([group_at, line_at, line_at * pair + pair_at, group_at * pair + pair_at])
    ws = w_score.reshape(heads, HD)
    slab_axes = ("groups", "pair")
    board_row = move_board.reshape(1, row_count)

    half_cols = w_query.shape[1] // groups
    packed = pl.pallas_call(
        functools.partial(pack_weights, plan),
        out_shape=shape((plan.peers, plan.rows, depth), BF16),
        in_specs=[pl.BlockSpec(memory_space=pltpu.SMEM)] + [untouched()] * 5,
        out_specs=untouched(),
        scratch_shapes=[
            pltpu.VMEM((depth, half_cols), BF16),
            pltpu.VMEM((depth, 2 * HD), BF16),
            pltpu.VMEM((heads, HD), BF16),
            pltpu.VMEM((1, row_count), jnp.int32),
            pltpu.VMEM((1, row_count), jnp.int32),
            pltpu.VMEM((plan.peers * plan.rows, half_cols + 2 * HD), F32),
            pltpu.VMEM((plan.peers, plan.rows, depth), BF16),
            pltpu.SemaphoreType.DMA((5,)),
            pltpu.SemaphoreType.DMA((plan.peers,)),
        ],
        compiler_params=limits(62),
        cost_estimate=cost(0, 0),
    )(group_at.reshape(1), w_query, w_keyval, ws, board_row, move_ids.reshape(1, row_count))
    weights = lax.all_to_all(packed, ("line", "pair"), split_axis=0, concat_axis=0, tiled=True)

    payload = pl.pallas_call(
        functools.partial(pack_prefix, plan),
        out_shape=shape((boards_here + 1, prefix_len, HD), BF16),
        in_specs=[untouched()] * 3,
        out_specs=pl.BlockSpec(memory_space=pltpu.VMEM),
        scratch_shapes=[
            pltpu.VMEM((boards_here, prefix_len, HD), BF16),
            pltpu.VMEM((heads, HD), BF16),
            pltpu.SemaphoreType.DMA((3,)),
        ],
        compiler_params=limits(56),
        cost_estimate=cost(0, 0),
    )(prefix_kv, ws, packed)
    beside = swap(payload, slab_axes, plan.slab, 1)
    across = swap(payload, slab_axes, plan.slab, 2)

    block = min(moves, 128)
    vmem = pl.BlockSpec(memory_space=pltpu.VMEM)
    *normed, mark = pl.pallas_call(
        normalize,
        out_shape=[*[shape((moves // 2, width), BF16)] * 2, pltpu.HBM((8, width), BF16)],
        in_specs=[untouched(), vmem, untouched()],
        out_specs=[untouched()] * 3,
        scratch_shapes=[
            pltpu.VMEM((1, width), F32),
            pltpu.VMEM((3, block, width), BF16),
            pltpu.VMEM((3, block, width), BF16),
            pltpu.SemaphoreType.DMA((3,)),
            pltpu.SemaphoreType.DMA((3,)),
        ],
        compiler_params=limits(58),
        cost_estimate=cost(moves * width, moves * width // 4),
    )(move_table, norm_gain.reshape(width // HD, HD), packed)
    turns = turn_table(prefix_len).reshape(line, 1, plan.pairs, 2)
    turns = np.tile(turns, (1, plan.mine, 1, 1)).reshape(line, plan.mine * plan.pairs, 2)
    flat = weights.transpose(1, 0, 2).reshape(plan.rows, width) if depth % HD else weights
    sent = (plan.line_rows, moves)
    outs = (shape(sent if plan.direct else (line, *sent), BF16), shape((plan.mine, moves), F32))
    across = tied(across, mark)
    diagonal = swap(across, slab_axes, plan.slab, 1)
    filled, listed = (), None
    for step, after in enumerate((across, beside)):
        made = local_call(
            functools.partial(project, plan, step * moves // 2, step == 0),
            place,
            (flat, normed[step], jnp.asarray(turns), after, *filled),
            [*outs, *([shape((plan.share, plan.slots), F32)] if step == 0 else [])],
            (),
            20,
            (3,),
            moves * width * 1024,
            moves * width,
            {5: 0, 6: 1} if filled else None,
        )
        filled, listed = made[:2], made[2] if step == 0 else listed
    queries, own_values = filled
    other = swap(listed, slab_axes, plan.slab, pair)
    if plan.direct:
        queries = [queries] + [swap(queries, "line", line, step) for step in range(1, line)]
    else:
        queries = lax.all_to_all(queries, "line", split_axis=0, concat_axis=0, tiled=True)
        queries = [queries.reshape(line * plan.line_rows, moves)]

    query_rows = plan.mine * HD
    back = plan.peers * lax.axis_size("tensor")
    chosen, folds, slot_row, order = local_call(
        functools.partial(prepare, plan),
        place,
        (board_row, listed, other, payload, beside, across, diagonal),
        (
            shape((boards_here, moves, plan.slab * plan.slots), BF16),
            shape((plan.slab, boards_here, prefix_len, plan.mine * plan.slots), F32),
            shape((1, row_count), jnp.int32),
            shape((len(queries), plan.mine * HD + 8, queries[0].shape[0]), BF16),
        ),
        mib=20,
        flops=10**9,
        nbytes=10**6,
    )
    parts = local_call(
        functools.partial(attend, plan),
        place,
        (own_values, listed, other, chosen, folds, order, payload, beside, across, diagonal, *queries),
        shape((groups, back, plan.share, plan.slots), BF16),
        [
            pltpu.VMEM((query_rows + 16, moves), BF16),
            pltpu.VMEM((16, moves), F32),
            pltpu.VMEM((plan.slab, boards_here, plan.slots), F32),
            pltpu.VMEM((query_rows + 16, plan.slab * plan.slots), F32),
            pltpu.VMEM((query_rows + 16, plan.slab * plan.slots), F32),
        ],
        24,
    )
    parts = lax.all_to_all(
        parts.reshape(groups * back, plan.share, plan.slots),
        ("groups", "line", "pair", "tensor"),
        split_axis=0,
        concat_axis=0,
        tiled=True,
    )
    parts = parts.reshape(groups, line, back // line, plan.share, plan.slots)
    logprob = pl.pallas_call(
        functools.partial(finish, plan), out_shape=shape((1, row_count), F32), compiler_params=limits(VMEM_MIB)
    )(parts, board_row, slot_row)
    return logprob.reshape(row_count)


def solution(mesh):
    order = ("groups", "dp", "tensor")
    assert mesh.axis_names == order
    pair = 2
    groups, peers, tensor = (mesh.shape[name] for name in order)
    fine = Mesh(mesh.devices.reshape(groups, peers // pair, pair, tensor), ("groups", "line", "pair", "tensor"))
    rows = ("groups", "line", "pair")
    placed = (
        P(rows, None, "tensor"),
        P(rows),
        P(rows, None),
        P(),
        P(),
        P(("line", "pair"), "tensor"),
        P(("line", "pair"), "tensor"),
        P("tensor"),
    )
    return jax.shard_map(per_device, mesh=fine, in_specs=placed, out_specs=P(rows), check_vma=False)
```

```python
import functools
import math

import jax
import jax.numpy as jnp
import numpy as np
from jax import lax
from jax.experimental import pallas as pl
from jax.experimental.pallas import tpu as pltpu
from jax.sharding import Mesh
from jax.sharding import PartitionSpec as P

HD = 128
HALF = HD // 2
EPS = 1e-06
THETA = 5000000.0
DEAD = -1e30
VMEM_MIB = 52
GROUP, LINE, PEER, SLAB = range(4)

F32 = jnp.float32
BF16 = jnp.bfloat16

NN = (((1,), (0,)), ((), ()))
NT = (((1,), (1,)), ((), ()))
TN = (((0,), (0,)), ((), ()))


def matmul(a, b, dims=NN):
    return lax.dot_general(a, b, dims, preferred_element_type=F32)


def limits(mib):
    return pltpu.CompilerParams(vmem_limit_bytes=mib * 1024 * 1024)


class Plan:
    def __init__(self, groups, line, pair, heads, capacity, share):
        self.groups, self.line, self.pair = groups, line, pair
        self.peers = line * pair
        self.slab = groups * pair
        self.heads = heads
        self.mine = heads // self.slab
        self.pairs = HALF // line
        self.q_rows = self.mine * 2 * self.pairs
        self.k_rows = 2 * self.pairs
        self.fold_at = self.q_rows + self.k_rows
        self.list_at = self.fold_at + self.mine
        self.rows = -(-(self.list_at + 1) // 8) * 8
        self.line_rows = -(-(self.q_rows + 2 * self.mine) // 8) * 8
        self.capacity = capacity
        self.share = share
        self.slots = self.peers * capacity
        self.direct = line <= 4


def pack_weights(plan, place_ref, wq_hbm, wkv_hbm, ws_hbm, board_hbm, ids_hbm, *rest):
    out_ref, wq, wkv, ws_ref, board_ref, ids_ref, pick, sems = rest
    group = place_ref[0]
    half_cols = wq.shape[1]
    columns_here = pl.ds(pl.multiple_of(group * half_cols, HD), half_cols)
    copies = (
        pltpu.make_async_copy(ws_hbm, ws_ref, sems.at[0]),
        pltpu.make_async_copy(board_hbm, board_ref, sems.at[1]),
        pltpu.make_async_copy(ids_hbm, ids_ref, sems.at[2]),
        pltpu.make_async_copy(wq_hbm.at[:, columns_here], wq, sems.at[3]),
        pltpu.make_async_copy(wkv_hbm, wkv, sems.at[4]),
    )
    for copy in copies:
        copy.start()
    for copy in copies[:3]:
        copy.wait()
    count, depth = board_ref.shape[1], wq.shape[0]
    board_row = board_ref[...]
    board_col = jnp.broadcast_to(board_row.astype(F32), (8, count)).T[:, 0:1].astype(jnp.int32)
    own = lax.broadcasted_iota(jnp.int32, (count, count), 0)
    other = lax.broadcasted_iota(jnp.int32, (count, count), 1)
    ahead = jnp.where((board_col == board_row) & (other < own), 1.0, 0.0)
    rank = jnp.sum(ahead, axis=1, keepdims=True).astype(jnp.int32)
    move = ids_ref[...] + 1
    boards, span = plan.line * plan.share, plan.share * plan.capacity
    member = lax.broadcasted_iota(jnp.int32, (boards, count), 0) == board_row
    parts = [jnp.where(member, part.astype(F32), 0.0) for part in (move // 64, move % 64)]
    lane = lax.broadcasted_iota(jnp.int32, (count, depth), 1)
    ranked = jnp.where(rank == (lane % span) % plan.capacity, 1.0, 0.0).astype(BF16)
    found = matmul(jnp.concatenate(parts, axis=0).astype(BF16), ranked)
    lane = lax.broadcasted_iota(jnp.int32, (2 * boards, depth), 1)
    row = lax.broadcasted_iota(jnp.int32, (2 * boards, depth), 0)
    keep = (row // boards == lane // span) & (row % plan.share == (lane % span) // plan.capacity)
    found = jnp.where(keep, found, 0.0)
    lists = []
    for line in range(plan.line):
        at = line * plan.share
        both = found[at : at + plan.share] + found[boards + at : boards + at + plan.share]
        lists.append(jnp.sum(both, axis=0, keepdims=True))

    if plan.pairs % 16 == 0:
        turn_weights(plan, group, lists, copies[3:], wq, wkv, ws_ref, out_ref)
    else:
        pick_weights(plan, group, lists, copies[3:], wq, wkv, ws_ref, out_ref, pick)


def turn_weights(plan, group, lists, copies, wq, wkv, ws_ref, out_ref):
    for copy in copies:
        copy.wait()
    q = wq[...].T
    k = wkv[:, :HD].T
    folds = matmul(ws_ref[...], wkv[:, HD:], NT)
    row = lax.broadcasted_iota(jnp.int32, folds.shape, 0)
    pairs = plan.pairs
    zeros = jnp.zeros((plan.rows - plan.list_at - 1, folds.shape[1]), F32)
    for pair in range(plan.pair):
        first = (group * plan.pair + pair) * plan.mine
        mine = [jnp.sum(jnp.where(row == first + h, folds, 0.0), axis=0, keepdims=True) for h in range(plan.mine)]
        for line in range(plan.line):
            peer = line * plan.pair + pair
            for part in range(2):
                entry = part * HALF + line * pairs
                for h in range(plan.mine):
                    at = (part * plan.mine + h) * pairs
                    source = (pair * plan.mine + h) * HD + entry
                    out_ref[peer, at : at + pairs] = q[source : source + pairs]
                at = plan.q_rows + part * pairs
                out_ref[peer, at : at + pairs] = k[entry : entry + pairs]
            last = jnp.concatenate([*mine, lists[line], zeros], axis=0)
            out_ref[peer, plan.fold_at :] = last.astype(BF16)


def pick_weights(plan, group, lists, copies, wq, wkv, ws_ref, out_ref, pick):
    rows, half_cols = plan.rows, wq.shape[1]
    r = lax.broadcasted_iota(jnp.int32, (rows, 1), 0)
    part = r // (plan.mine * plan.pairs)
    head = (r // plan.pairs) % plan.mine
    entry = r % plan.pairs
    is_q = r < plan.q_rows
    k_at = r - plan.q_rows
    is_k = (k_at >= 0) & (k_at < plan.k_rows)
    f_at = r - plan.fold_at
    is_f = (f_at >= 0) & (f_at < plan.mine)
    q_lane = lax.broadcasted_iota(jnp.int32, (rows, half_cols), 1)
    k_lane = lax.broadcasted_iota(jnp.int32, (rows, HD), 1)
    ws = ws_ref[...].astype(F32)

    def fill(peer, carry):
        line, pair = peer // plan.pair, peer % plan.pair
        column = (pair * plan.mine + head) * HD + part * HALF + line * plan.pairs + entry
        column = jnp.where(is_q, column, -1)
        at = pl.ds(pl.multiple_of(peer * rows, 8), rows)
        pick[at, :half_cols] = jnp.where(q_lane == column, 1.0, 0.0)
        k_column = (k_at // plan.pairs) * HALF + line * plan.pairs + k_at % plan.pairs
        k_column = jnp.where(is_k, k_column, -1)
        pick[at, half_cols : half_cols + HD] = jnp.where(k_lane == k_column, 1.0, 0.0)
        fold = jnp.zeros((rows, HD), F32)
        my_head = jnp.where(is_f, (group * plan.pair + pair) * plan.mine + f_at, -1)
        for h in range(plan.heads):
            fold = jnp.where(my_head == h, ws[h : h + 1], fold)
        pick[at, half_cols + HD :] = fold
        return carry

    lax.fori_loop(0, plan.peers, fill, 0, unroll=plan.peers <= 8)

    for copy in copies:
        copy.wait()
    left = pick[...].astype(BF16)
    total = matmul(left[:, :half_cols], wq[...], NT) + matmul(left[:, half_cols:], wkv[...], NT)
    for peer in range(plan.peers):
        mine = total[peer * rows : (peer + 1) * rows]
        out_ref[peer] = jnp.where(r == plan.list_at, lists[peer // plan.pair], mine).astype(BF16)


def normalize(table_hbm, gain_ref, after_ref, *refs):
    *outs, mark_ref, gain, buffers, made, sems, out_sems = refs
    held, block, _ = buffers.shape
    steps = table_hbm.shape[0] // block
    each = outs[0].shape[0] // block

    def copy(step):
        source = table_hbm.at[pl.ds(step * block, block)]
        return pltpu.make_async_copy(source, buffers.at[step % held], sems.at[step % held])

    def store(step):
        target = outs[step // each].at[pl.ds(step % each * block, block)]
        return pltpu.make_async_copy(made.at[step % held], target, out_sems.at[step % held])

    for step in range(min(held, steps)):
        copy(step).start()
    rows = gain_ref[...].astype(F32)
    gain[...] = jnp.concatenate([rows[r : r + 1] for r in range(rows.shape[0])], axis=1)
    for step in range(steps):
        copy(step).wait()
        if step >= held:
            store(step - held).wait()
        raw = buffers[step % held].astype(F32)
        inverse = lax.rsqrt(jnp.mean(raw * raw, axis=-1, keepdims=True) + EPS)
        made[step % held] = (raw * inverse * gain[...]).astype(BF16)
        store(step).start()
        if step + held < steps:
            copy(step + held).start()
    for step in range(max(0, steps - held), steps):
        store(step).wait()
    mark = pltpu.make_async_copy(made.at[0, pl.ds(0, mark_ref.shape[0])], mark_ref, out_sems.at[0])
    mark.start()
    mark.wait()


def read_lists(plan, w_ref, out_ref):
    share, capacity, peers = plan.share, plan.capacity, plan.peers
    span = share * capacity
    if len(w_ref.shape) == 3:
        rows = [w_ref[s].astype(F32)[plan.list_at : plan.list_at + 1] for s in range(peers)]
    else:
        row = w_ref[...].astype(F32)[plan.list_at : plan.list_at + 1]
        rows = [row[:, s * 2 * span : (s + 1) * 2 * span] for s in range(peers)]
    rows = jnp.concatenate(rows, axis=0)
    lane = lax.broadcasted_iota(jnp.int32, (share * peers, 2 * span), 1)
    row = lax.broadcasted_iota(jnp.int32, (share * peers, 2 * span), 0)
    lane = jnp.where(lane < span, lane, lane - span)
    spread = jnp.concatenate([rows] * share, axis=0)
    spread = jnp.where(lane // capacity == row // peers, spread, 0.0).astype(BF16)
    c = lax.broadcasted_iota(jnp.int32, (2 * span, plan.slots), 0)
    slot = lax.broadcasted_iota(jnp.int32, (2 * span, plan.slots), 1)
    scale = jnp.where(c < span, 64.0, 1.0)
    place = jnp.where(c % capacity == slot % capacity, scale, 0.0).astype(BF16)
    listed = matmul(spread, place)
    row = lax.broadcasted_iota(jnp.int32, listed.shape, 0)
    slot = lax.broadcasted_iota(jnp.int32, listed.shape, 1)
    listed = jnp.where(slot // capacity == row % peers, listed, 0.0)
    out_ref[...] = jnp.sum(listed.reshape(share, peers, plan.slots), axis=1)


def project(plan, place, lists, place_ref, w_ref, normed_ref, turn_ref, after_ref, *refs):
    if lists:
        *refs, list_ref = refs
        read_lists(plan, w_ref, list_ref)
    q_ref, vo_ref = refs[-2:]
    turns = turn_ref[place_ref[LINE]]
    half, k_half = plan.q_rows // 2, plan.k_rows // 2
    cosine, sine = turns[:, 0:1], turns[:, 1:2]
    cos_k, sin_k = cosine[:k_half], sine[:k_half]
    moves = normed_ref.shape[0]
    block = min(moves, 256)
    for start in range(0, moves, block):
        at, to = slice(start, start + block), slice(place + start, place + start + block)
        if len(w_ref.shape) == 3:
            depth = w_ref.shape[2]
            total = None
            for s in range(w_ref.shape[0]):
                term = matmul(w_ref[s], normed_ref[at, s * depth : (s + 1) * depth], NT)
                total = term if total is None else total + term
        else:
            total = matmul(w_ref[...], normed_ref[at, :], NT)
        first, second = total[:half], total[half : 2 * half]
        f_first = (first * cosine - second * sine).astype(BF16).astype(F32)
        f_second = (second * cosine + first * sine).astype(BF16).astype(F32)
        first, second = total[plan.q_rows : plan.q_rows + k_half], total[plan.q_rows + k_half : plan.fold_at]
        k_first = (first * cos_k - second * sin_k).astype(BF16).astype(F32)
        k_second = (second * cos_k + first * sin_k).astype(BF16).astype(F32)
        logits, tails = [], []
        for h in range(plan.mine):
            own = slice(h * k_half, (h + 1) * k_half)
            logit = jnp.sum(f_first[own] * k_first + f_second[own] * k_second, axis=0, keepdims=True)
            logits.append(logit.astype(BF16).astype(F32))
            tails.append(logit - logits[-1])
        pad = plan.line_rows - plan.q_rows - 2 * plan.mine
        pieces = [f_first, f_second, *logits, *tails]
        if pad:
            pieces.append(jnp.zeros((pad, block), F32))
        out = jnp.concatenate(pieces, axis=0).astype(BF16)
        if plan.direct:
            q_ref[:, to] = out
        else:
            for line in range(plan.line):
                q_ref[line, :, to] = out
        vo_ref[:, to] = total[plan.fold_at : plan.list_at]


def tied(x, *others):
    return pl.pallas_call(
        lambda *refs: None,
        out_shape=shape(x.shape, x.dtype),
        in_specs=[untouched()] + [pl.BlockSpec(memory_space=pltpu.HBM)] * len(others),
        out_specs=untouched(),
        input_output_aliases={0: 0},
        compiler_params=limits(1),
        cost_estimate=cost(0, 0),
    )(x, *others)


def pack_prefix(plan, prefix_hbm, ws_hbm, after_ref, out_ref, *scratch):
    values, ws_ref, sems = scratch
    boards = values.shape[0]
    heads = plan.heads
    copies = (
        pltpu.make_async_copy(ws_hbm, ws_ref, sems.at[0]),
        pltpu.make_async_copy(prefix_hbm.at[:, :, pl.ds(HD, HD)], values, sems.at[1]),
        pltpu.make_async_copy(prefix_hbm.at[:, :, pl.ds(0, HD)], out_ref.at[pl.ds(0, boards)], sems.at[2]),
    )
    for copy in copies:
        copy.start()
    copies[0].wait()
    span = HD // boards
    ws = jnp.concatenate([ws_ref[...].astype(F32)] * (HD // heads), axis=0)
    row = lax.broadcasted_iota(jnp.int32, (HD, 1), 0)
    copies[1].wait()
    fold = None
    for board in range(boards):
        keep = (row // span == board) & (row % span < 2 * heads)
        term = matmul(values[board], jnp.where(keep, ws, 0.0).astype(BF16), NT)
        fold = term if fold is None else fold + term
    rounded = fold.astype(BF16).astype(F32)
    lane = lax.broadcasted_iota(jnp.int32, fold.shape, 1)
    out_ref[boards] = jnp.where(lane % span < heads, rounded, fold - rounded).astype(BF16)
    copies[2].wait()


def fold_columns(plan, here, block, board, boards, heads):
    lanes = plan.mine * plan.slots
    row = lax.broadcasted_iota(jnp.int32, (HD, lanes), 0) - board * (HD // boards)
    head = here * plan.mine + lax.broadcasted_iota(jnp.int32, (HD, lanes), 1) // plan.slots
    pick = jnp.where((row == head) | (row == head + heads), 1.0, 0.0).astype(BF16)
    return matmul(block, pick)


def prepare(plan, place_ref, board_ref, own_ref, other_ref, *rest):
    *prefix_refs, chosen_ref, fold_ref, slot_ref = rest
    count = board_ref.shape[1]
    board_row = board_ref[...]
    board_col = jnp.broadcast_to(board_row.astype(F32), (8, count)).T[:, 0:1].astype(jnp.int32)
    ahead = lax.broadcasted_iota(jnp.int32, (count, count), 0) < lax.broadcasted_iota(jnp.int32, (count, count), 1)
    rank = jnp.sum(jnp.where((board_col == board_row) & ahead, 1.0, 0.0), axis=0, keepdims=True)
    slot_ref[...] = rank.astype(jnp.int32) + place_ref[PEER] * plan.capacity
    here = place_ref[SLAB]
    boards, moves = chosen_ref.shape[0], chosen_ref.shape[1]
    move_at = lax.broadcasted_iota(jnp.int32, (moves, plan.slots), 0) + 1

    def step(board, carry):
        for j in range(plan.slab):
            place = ((here ^ j) % plan.pair) * boards + board
            row = (own_ref, other_ref)[j // plan.pair][pl.ds(place, 1), :].astype(jnp.int32)
            at = slice(j * plan.slots, (j + 1) * plan.slots)
            chosen_ref[board, :, at] = jnp.where(move_at == row, 1.0, 0.0).astype(BF16)
        for j, prefix_ref in enumerate(prefix_refs):
            fold_ref[j, board] = fold_columns(plan, here, prefix_ref[boards], board, boards, plan.heads)
        return carry

    lax.fori_loop(0, boards, step, 0)


def attend(plan, place_ref, vo_ref, own_ref, other_ref, chosen_ref, fold_ref, *rest):
    prefix_refs, rest = rest[: plan.slab], rest[plan.slab :]
    *q_refs, out_ref, table, extra, scores, taken_even, own_even, taken_odd, own_odd = rest
    even, odd = (taken_even, own_even), (taken_odd, own_odd)
    prefix_len = prefix_refs[0].shape[1]
    here = place_ref[SLAB]
    mine, heads, slots = plan.mine, plan.heads, plan.slots
    moves = vo_ref.shape[1]
    boards = prefix_refs[0].shape[0] - 1
    query_rows = mine * HD

    mixed = None
    for step, q_ref in enumerate(q_refs):
        r = lax.broadcasted_iota(jnp.int32, (query_rows + 8, q_ref.shape[0]), 0)
        c = lax.broadcasted_iota(jnp.int32, (query_rows + 8, q_ref.shape[0]), 1)
        line, at = (place_ref[LINE] ^ step, c) if plan.direct else (c // plan.line_rows, c % plan.line_rows)
        part, head, entry = at // (mine * plan.pairs), (at // plan.pairs) % mine, at % plan.pairs
        goes = jnp.where(at < plan.q_rows, head * HD + part * HALF + line * plan.pairs + entry, -1)
        tail = at - plan.q_rows
        goes = jnp.where((tail >= 0) & (tail < 2 * mine), query_rows + tail % mine, goes)
        term = matmul(jnp.where(r == goes, 1.0, 0.0).astype(BF16), q_ref[...])
        mixed = term if mixed is None else mixed + term
    table[:query_rows] = mixed[:query_rows].astype(BF16)
    extra[...] = jnp.zeros_like(extra)
    for place, value in ((0, mixed[query_rows : query_rows + mine]), (2 * mine, vo_ref[...])):
        rounded = value.astype(BF16).astype(F32)
        extra[place : place + mine] = rounded
        extra[place + mine : place + 2 * mine] = value - rounded
    table[query_rows:] = extra[...].astype(BF16)

    scale = math.log2(math.e) / math.sqrt(HD)
    def per_head(x, base):
        pieces = [x[base + h : base + h + 1] + x[base + mine + h : base + mine + h + 1] for h in range(mine)]
        return jnp.concatenate(pieces, axis=1)

    def moves_of(j, board):
        place = ((here ^ j) % plan.pair) * boards + board
        return (own_ref, other_ref)[j // plan.pair][pl.ds(place, 1), :].astype(jnp.int32)

    def gather(board, taken, own):
        found = matmul(table[...], chosen_ref[board])
        taken[...] = found[:query_rows].astype(BF16)
        own[...] = found[query_rows:]

    def over(values):
        return jnp.sum(values, axis=0, keepdims=True)

    half = prefix_len // 2

    def score_board(board, taken, own):
        for j in range(plan.slab):
            at = slice(j * slots, (j + 1) * slots)
            q = jnp.concatenate([taken[h * HD : (h + 1) * HD, at] for h in range(mine)], axis=1)
            own_logit = per_head(own[:, at], 0)
            own_value = per_head(own[:, at], 2 * mine)
            parts = []
            for keys in (slice(0, half), slice(half, 2 * half)):
                logits = matmul(prefix_refs[j][board, keys], q)
                if j < plan.slab - 1:
                    fold = fold_ref[j, board, keys]
                else:
                    fold = fold_columns(plan, here, prefix_refs[j][boards, keys], board, boards, heads)
                top = jnp.max(logits, axis=0, keepdims=True)
                weight = jnp.exp2((logits - top) * scale)
                parts.append((top, over(weight), over(weight * fold)))
            parts.append((own_logit, 1.0, own_value))
            peak = parts[0][0]
            for top, _, _ in parts[1:]:
                peak = jnp.maximum(peak, top)
            shares = [jnp.exp2((top - peak) * scale) for top, _, _ in parts]
            denom = sum(share * total for share, (_, total, _) in zip(shares, parts))
            value = sum(share * total for share, (_, _, total) in zip(shares, parts)) / denom
            score = sum(value[:, h * slots : (h + 1) * slots] for h in range(mine))
            scores[here ^ j, pl.ds(board, 1), :] = jnp.where(moves_of(j, board) > 0, score, DEAD)

    gather(0, *even)

    def step(at, carry):
        board = 2 * at
        gather(jnp.minimum(board + 1, boards - 1), *odd)
        score_board(board, *even)
        gather(jnp.minimum(board + 2, boards - 1), *even)
        score_board(jnp.minimum(board + 1, boards - 1), *odd)
        return carry

    lax.fori_loop(0, -(-boards // 2), step, 0)
    live = scores[...] > 0.5 * DEAD
    count = jnp.sum(jnp.where(live, 1.0, 0.0), axis=2, keepdims=True)
    mean = jnp.sum(jnp.where(live, scores[...], 0.0), axis=2, keepdims=True) / jnp.maximum(count, 1.0)
    centered = jnp.where(live, scores[...] - mean, DEAD)
    for g in range(plan.groups):
        both = jnp.concatenate([centered[g * plan.pair + p] for p in range(plan.pair)], axis=0).astype(BF16)
        for copy in range(out_ref.shape[1]):
            out_ref[g, copy] = both


def finish(plan, parts_ref, board_ref, slot_ref, out_ref):
    line = parts_ref.shape[1]
    columns = []
    for at in range(line):
        total = None
        for g in range(parts_ref.shape[0]):
            for p in range(parts_ref.shape[2]):
                term = parts_ref[g, at, p].astype(F32)
                total = term if total is None else total + term
        columns.append(total)
    scores = jnp.concatenate(columns, axis=0)
    live = scores > 0.5 * DEAD
    peak = jnp.max(scores, axis=1, keepdims=True)
    denom = jnp.sum(jnp.where(live, jnp.exp(scores - peak), 0.0), axis=1, keepdims=True)
    logprob = jnp.where(live, scores - peak - jnp.log(denom), 0.0)
    count = board_ref.shape[1]
    member = lax.broadcasted_iota(jnp.int32, (scores.shape[0], count), 0) == board_ref[...]
    member = jnp.where(member, 1.0, 0.0).astype(BF16)
    found = jnp.zeros((plan.slots, count), F32)
    for _ in range(3):
        rounded = logprob.astype(BF16)
        found = found + matmul(rounded, member, TN)
        logprob = logprob - rounded.astype(F32)
    at = lax.broadcasted_iota(jnp.int32, (plan.slots, count), 0) == slot_ref[...]
    out_ref[...] = jnp.sum(jnp.where(at, found, 0.0), axis=0, keepdims=True)


def untouched():
    return pl.BlockSpec(memory_space=pl.ANY)


def local_call(kernel, place, args, outs, scratch=(), mib=40, copied=(), flops=0, nbytes=0, aliases=None):
    vmem = pl.BlockSpec(memory_space=pltpu.VMEM)
    return pl.pallas_call(
        kernel,
        out_shape=outs,
        in_specs=[pl.BlockSpec(memory_space=pltpu.SMEM)]
        + [untouched() if at in copied else vmem for at in range(len(args))],
        out_specs=jax.tree.map(lambda x: vmem, outs),
        scratch_shapes=scratch,
        input_output_aliases=aliases or {},
        compiler_params=limits(mib),
        cost_estimate=cost(flops, nbytes),
    )(place, *args)


def cost(flops, nbytes):
    return pl.CostEstimate(flops=int(flops), bytes_accessed=int(nbytes), transcendentals=0)


def swap(x, names, size, step):
    return lax.ppermute(x, names, [(at, at ^ step) for at in range(size)])


def shape(dims, dtype):
    return jax.ShapeDtypeStruct(tuple(dims), dtype)


def turn_table(position):
    frequency = THETA ** (-2.0 * np.arange(HALF, dtype=np.float32) / HD)
    angles = np.float32(position) * frequency.astype(np.float32)
    return np.stack([np.cos(angles), np.sin(angles)], axis=1).astype(np.float32)


def per_device(prefix_kv, move_ids, move_board, move_table, norm_gain, w_query, w_keyval, w_score):
    row_count = move_ids.shape[0]
    boards_here, prefix_len, _ = prefix_kv.shape
    moves, width = move_table.shape
    groups, line, pair = lax.axis_size("groups"), lax.axis_size("line"), lax.axis_size("pair")
    board_total = boards_here * line * pair
    capacity = max(2, (2 * row_count + board_total - 1) // board_total)
    heads = w_query.shape[1] // HD
    plan = Plan(groups, line, pair, heads, capacity, pair * boards_here)
    depth = w_query.shape[0]
    group_at = lax.axis_index("groups").astype(jnp.int32)
    line_at = lax.axis_index("line").astype(jnp.int32)
    pair_at = lax.axis_index("pair").astype(jnp.int32)
    place = jnp.stack([group_at, line_at, line_at * pair + pair_at, group_at * pair + pair_at])
    ws = w_score.reshape(heads, HD)
    slab_axes = ("groups", "pair")
    board_row = move_board.reshape(1, row_count)

    half_cols = w_query.shape[1] // groups
    packed = local_call(
        functools.partial(pack_weights, plan),
        group_at.reshape(1),
        (w_query, w_keyval, ws, board_row, move_ids.reshape(1, row_count)),
        shape((plan.peers, plan.rows, depth), BF16),
        [
            pltpu.VMEM((depth, half_cols), BF16),
            pltpu.VMEM((depth, 2 * HD), BF16),
            pltpu.VMEM((heads, HD), BF16),
            pltpu.VMEM((1, row_count), jnp.int32),
            pltpu.VMEM((1, row_count), jnp.int32),
            pltpu.VMEM((plan.peers * plan.rows, half_cols + 2 * HD), F32),
            pltpu.SemaphoreType.DMA((5,)),
        ],
        62,
        range(5),
    )
    weights = lax.all_to_all(packed, ("line", "pair"), split_axis=0, concat_axis=0, tiled=True)

    payload = pl.pallas_call(
        functools.partial(pack_prefix, plan),
        out_shape=shape((boards_here + 1, prefix_len, HD), BF16),
        in_specs=[untouched()] * 3,
        out_specs=pl.BlockSpec(memory_space=pltpu.VMEM),
        scratch_shapes=[
            pltpu.VMEM((boards_here, prefix_len, HD), BF16),
            pltpu.VMEM((heads, HD), BF16),
            pltpu.SemaphoreType.DMA((3,)),
        ],
        compiler_params=limits(56),
        cost_estimate=cost(0, 0),
    )(prefix_kv, ws, packed)
    beside = swap(payload, slab_axes, plan.slab, 1)
    across = swap(payload, slab_axes, plan.slab, 2)

    block = min(moves, 128)
    vmem = pl.BlockSpec(memory_space=pltpu.VMEM)
    *normed, mark = pl.pallas_call(
        normalize,
        out_shape=[*[shape((moves // 2, width), BF16)] * 2, pltpu.HBM((8, width), BF16)],
        in_specs=[untouched(), vmem, untouched()],
        out_specs=[untouched()] * 3,
        scratch_shapes=[
            pltpu.VMEM((1, width), F32),
            pltpu.VMEM((3, block, width), BF16),
            pltpu.VMEM((3, block, width), BF16),
            pltpu.SemaphoreType.DMA((3,)),
            pltpu.SemaphoreType.DMA((3,)),
        ],
        compiler_params=limits(58),
        cost_estimate=cost(moves * width, moves * width // 4),
    )(move_table, norm_gain.reshape(width // HD, HD), packed)
    turns = turn_table(prefix_len).reshape(line, 1, plan.pairs, 2)
    turns = np.tile(turns, (1, plan.mine, 1, 1)).reshape(line, plan.mine * plan.pairs, 2)
    flat = weights.transpose(1, 0, 2).reshape(plan.rows, width) if depth % HD else weights
    sent = (plan.line_rows, moves)
    outs = (shape(sent if plan.direct else (line, *sent), BF16), shape((plan.mine, moves), F32))
    across = tied(across, mark)
    diagonal = swap(across, slab_axes, plan.slab, 1)
    filled, listed = (), None
    for step, after in enumerate((across, beside)):
        made = local_call(
            functools.partial(project, plan, step * moves // 2, step == 0),
            place,
            (flat, normed[step], jnp.asarray(turns), after, *filled),
            [*outs, *([shape((plan.share, plan.slots), F32)] if step == 0 else [])],
            (),
            20,
            (3,),
            moves * width * 1024,
            moves * width,
            {5: 0, 6: 1} if filled else None,
        )
        filled, listed = made[:2], made[2] if step == 0 else listed
    queries, own_values = filled
    other = swap(listed, slab_axes, plan.slab, pair)
    if plan.direct:
        queries = [queries] + [swap(queries, "line", line, step) for step in range(1, line)]
    else:
        queries = lax.all_to_all(queries, "line", split_axis=0, concat_axis=0, tiled=True)
        queries = [queries.reshape(line * plan.line_rows, moves)]

    query_rows = plan.mine * HD
    back = plan.peers * lax.axis_size("tensor")
    chosen, folds, slot_row = local_call(
        functools.partial(prepare, plan),
        place,
        (board_row, listed, other, payload, beside, across),
        (
            shape((boards_here, moves, plan.slab * plan.slots), BF16),
            shape((plan.slab - 1, boards_here, prefix_len, plan.mine * plan.slots), F32),
            shape((1, row_count), jnp.int32),
        ),
        mib=20,
        flops=10**9,
        nbytes=10**6,
    )
    parts = local_call(
        functools.partial(attend, plan),
        place,
        (own_values, listed, other, chosen, folds, payload, beside, across, diagonal, *queries),
        shape((groups, back, plan.share, plan.slots), BF16),
        [
            pltpu.VMEM((query_rows + 16, moves), BF16),
            pltpu.VMEM((16, moves), F32),
            pltpu.VMEM((plan.slab, boards_here, plan.slots), F32),
            *[pltpu.VMEM((query_rows, plan.slab * plan.slots), BF16), pltpu.VMEM((16, plan.slab * plan.slots), F32)] * 2,
        ],
        24,
    )
    parts = lax.all_to_all(
        parts.reshape(groups * back, plan.share, plan.slots),
        ("groups", "line", "pair", "tensor"),
        split_axis=0,
        concat_axis=0,
        tiled=True,
    )
    parts = parts.reshape(groups, line, back // line, plan.share, plan.slots)
    logprob = pl.pallas_call(
        functools.partial(finish, plan), out_shape=shape((1, row_count), F32), compiler_params=limits(VMEM_MIB)
    )(parts, board_row, slot_row)
    return logprob.reshape(row_count)


def solution(mesh):
    order = ("groups", "dp", "tensor")
    assert mesh.axis_names == order
    pair = 2
    groups, peers, tensor = (mesh.shape[name] for name in order)
    fine = Mesh(mesh.devices.reshape(groups, peers // pair, pair, tensor), ("groups", "line", "pair", "tensor"))
    rows = ("groups", "line", "pair")
    placed = (
        P(rows, None, "tensor"),
        P(rows),
        P(rows, None),
        P(),
        P(),
        P(("line", "pair"), "tensor"),
        P(("line", "pair"), "tensor"),
        P("tensor"),
    )
    return jax.shard_map(per_device, mesh=fine, in_specs=placed, out_specs=P(rows), check_vma=False)
```

```python
import functools
import math

import jax
import jax.numpy as jnp
import numpy as np
from jax import lax
from jax.experimental import pallas as pl
from jax.experimental.pallas import tpu as pltpu
from jax.sharding import Mesh
from jax.sharding import PartitionSpec as P

HD = 128
HALF = HD // 2
EPS = 1e-06
THETA = 5000000.0
DEAD = -1e30
VMEM_MIB = 52
GROUP, LINE, PEER, SLAB = range(4)

F32 = jnp.float32
BF16 = jnp.bfloat16

NN = (((1,), (0,)), ((), ()))
NT = (((1,), (1,)), ((), ()))
TN = (((0,), (0,)), ((), ()))


def matmul(a, b, dims=NN):
    return lax.dot_general(a, b, dims, preferred_element_type=F32)


def limits(mib):
    return pltpu.CompilerParams(vmem_limit_bytes=mib * 1024 * 1024)


class Plan:
    def __init__(self, groups, line, pair, heads, capacity, share):
        self.groups, self.line, self.pair = groups, line, pair
        self.peers = line * pair
        self.slab = groups * pair
        self.heads = heads
        self.mine = heads // self.slab
        self.pairs = HALF // line
        self.q_rows = self.mine * 2 * self.pairs
        self.k_rows = 2 * self.pairs
        self.fold_at = self.q_rows + self.k_rows
        self.list_at = self.fold_at + self.mine
        self.rows = -(-(self.list_at + 1) // 8) * 8
        self.line_rows = -(-(self.q_rows + 2 * self.mine) // 8) * 8
        self.capacity = capacity
        self.share = share
        self.slots = self.peers * capacity
        self.direct = line <= 4


def pack_weights(plan, place_ref, wq_hbm, wkv_hbm, ws_hbm, board_hbm, ids_hbm, *rest):
    out_ref, wq, wkv, ws_ref, board_ref, ids_ref, pick, sems = rest
    group = place_ref[0]
    half_cols = wq.shape[1]
    columns_here = pl.ds(pl.multiple_of(group * half_cols, HD), half_cols)
    copies = (
        pltpu.make_async_copy(ws_hbm, ws_ref, sems.at[0]),
        pltpu.make_async_copy(board_hbm, board_ref, sems.at[1]),
        pltpu.make_async_copy(ids_hbm, ids_ref, sems.at[2]),
        pltpu.make_async_copy(wq_hbm.at[:, columns_here], wq, sems.at[3]),
        pltpu.make_async_copy(wkv_hbm, wkv, sems.at[4]),
    )
    for copy in copies:
        copy.start()
    for copy in copies[:3]:
        copy.wait()
    count, depth = board_ref.shape[1], wq.shape[0]
    board_row = board_ref[...]
    board_col = jnp.broadcast_to(board_row.astype(F32), (8, count)).T[:, 0:1].astype(jnp.int32)
    own = lax.broadcasted_iota(jnp.int32, (count, count), 0)
    other = lax.broadcasted_iota(jnp.int32, (count, count), 1)
    ahead = jnp.where((board_col == board_row) & (other < own), 1.0, 0.0)
    rank = jnp.sum(ahead, axis=1, keepdims=True).astype(jnp.int32)
    move = ids_ref[...] + 1
    boards, span = plan.line * plan.share, plan.share * plan.capacity
    member = lax.broadcasted_iota(jnp.int32, (boards, count), 0) == board_row
    parts = [jnp.where(member, part.astype(F32), 0.0) for part in (move // 64, move % 64)]
    lane = lax.broadcasted_iota(jnp.int32, (count, depth), 1)
    ranked = jnp.where(rank == (lane % span) % plan.capacity, 1.0, 0.0).astype(BF16)
    found = matmul(jnp.concatenate(parts, axis=0).astype(BF16), ranked)
    lane = lax.broadcasted_iota(jnp.int32, (2 * boards, depth), 1)
    row = lax.broadcasted_iota(jnp.int32, (2 * boards, depth), 0)
    keep = (row // boards == lane // span) & (row % plan.share == (lane % span) // plan.capacity)
    found = jnp.where(keep, found, 0.0)
    lists = []
    for line in range(plan.line):
        at = line * plan.share
        both = found[at : at + plan.share] + found[boards + at : boards + at + plan.share]
        lists.append(jnp.sum(both, axis=0, keepdims=True))

    if plan.pairs % 16 == 0:
        turn_weights(plan, group, lists, copies[3:], wq, wkv, ws_ref, out_ref)
    else:
        pick_weights(plan, group, lists, copies[3:], wq, wkv, ws_ref, out_ref, pick)


def turn_weights(plan, group, lists, copies, wq, wkv, ws_ref, out_ref):
    for copy in copies:
        copy.wait()
    q = wq[...].T
    k = wkv[:, :HD].T
    folds = matmul(ws_ref[...], wkv[:, HD:], NT)
    row = lax.broadcasted_iota(jnp.int32, folds.shape, 0)
    pairs = plan.pairs
    zeros = jnp.zeros((plan.rows - plan.list_at - 1, folds.shape[1]), F32)
    for pair in range(plan.pair):
        first = (group * plan.pair + pair) * plan.mine
        mine = [jnp.sum(jnp.where(row == first + h, folds, 0.0), axis=0, keepdims=True) for h in range(plan.mine)]
        for line in range(plan.line):
            peer = line * plan.pair + pair
            for part in range(2):
                entry = part * HALF + line * pairs
                for h in range(plan.mine):
                    at = (part * plan.mine + h) * pairs
                    source = (pair * plan.mine + h) * HD + entry
                    out_ref[peer, at : at + pairs] = q[source : source + pairs]
                at = plan.q_rows + part * pairs
                out_ref[peer, at : at + pairs] = k[entry : entry + pairs]
            last = jnp.concatenate([*mine, lists[line], zeros], axis=0)
            out_ref[peer, plan.fold_at :] = last.astype(BF16)


def pick_weights(plan, group, lists, copies, wq, wkv, ws_ref, out_ref, pick):
    rows, half_cols = plan.rows, wq.shape[1]
    r = lax.broadcasted_iota(jnp.int32, (rows, 1), 0)
    part = r // (plan.mine * plan.pairs)
    head = (r // plan.pairs) % plan.mine
    entry = r % plan.pairs
    is_q = r < plan.q_rows
    k_at = r - plan.q_rows
    is_k = (k_at >= 0) & (k_at < plan.k_rows)
    f_at = r - plan.fold_at
    is_f = (f_at >= 0) & (f_at < plan.mine)
    q_lane = lax.broadcasted_iota(jnp.int32, (rows, half_cols), 1)
    k_lane = lax.broadcasted_iota(jnp.int32, (rows, HD), 1)
    ws = ws_ref[...].astype(F32)

    def fill(peer, carry):
        line, pair = peer // plan.pair, peer % plan.pair
        column = (pair * plan.mine + head) * HD + part * HALF + line * plan.pairs + entry
        column = jnp.where(is_q, column, -1)
        at = pl.ds(pl.multiple_of(peer * rows, 8), rows)
        pick[at, :half_cols] = jnp.where(q_lane == column, 1.0, 0.0)
        k_column = (k_at // plan.pairs) * HALF + line * plan.pairs + k_at % plan.pairs
        k_column = jnp.where(is_k, k_column, -1)
        pick[at, half_cols : half_cols + HD] = jnp.where(k_lane == k_column, 1.0, 0.0)
        fold = jnp.zeros((rows, HD), F32)
        my_head = jnp.where(is_f, (group * plan.pair + pair) * plan.mine + f_at, -1)
        for h in range(plan.heads):
            fold = jnp.where(my_head == h, ws[h : h + 1], fold)
        pick[at, half_cols + HD :] = fold
        return carry

    lax.fori_loop(0, plan.peers, fill, 0, unroll=plan.peers <= 8)

    for copy in copies:
        copy.wait()
    left = pick[...].astype(BF16)
    total = matmul(left[:, :half_cols], wq[...], NT) + matmul(left[:, half_cols:], wkv[...], NT)
    for peer in range(plan.peers):
        mine = total[peer * rows : (peer + 1) * rows]
        out_ref[peer] = jnp.where(r == plan.list_at, lists[peer // plan.pair], mine).astype(BF16)


def normalize(table_hbm, gain_ref, after_ref, *refs):
    *outs, mark_ref, gain, buffers, made, sems, out_sems = refs
    held, block, _ = buffers.shape
    steps = table_hbm.shape[0] // block
    sizes = (table_hbm.shape[0] - outs[1].shape[0], outs[1].shape[0])
    places = [(out, at) for out, size in zip(outs, sizes) for at in range(0, size, block)]

    def copy(step):
        source = table_hbm.at[pl.ds(step * block, block)]
        return pltpu.make_async_copy(source, buffers.at[step % held], sems.at[step % held])

    def store(step):
        out, at = places[step]
        return pltpu.make_async_copy(made.at[step % held], out.at[pl.ds(at, block)], out_sems.at[step % held])

    for step in range(min(held, steps)):
        copy(step).start()
    rows = gain_ref[...].astype(F32)
    gain[...] = jnp.concatenate([rows[r : r + 1] for r in range(rows.shape[0])], axis=1)
    for step in range(steps):
        copy(step).wait()
        if step >= held:
            store(step - held).wait()
        raw = buffers[step % held].astype(F32)
        inverse = lax.rsqrt(jnp.mean(raw * raw, axis=-1, keepdims=True) + EPS)
        made[step % held] = (raw * inverse * gain[...]).astype(BF16)
        store(step).start()
        if step + held < steps:
            copy(step + held).start()
    for step in range(max(0, steps - held), steps):
        store(step).wait()
    mark = pltpu.make_async_copy(made.at[0, pl.ds(0, mark_ref.shape[0])], mark_ref, out_sems.at[0])
    mark.start()
    mark.wait()


def read_lists(plan, w_ref, out_ref):
    share, capacity, peers = plan.share, plan.capacity, plan.peers
    span = share * capacity
    if len(w_ref.shape) == 3:
        rows = [w_ref[s].astype(F32)[plan.list_at : plan.list_at + 1] for s in range(peers)]
    else:
        row = w_ref[...].astype(F32)[plan.list_at : plan.list_at + 1]
        rows = [row[:, s * 2 * span : (s + 1) * 2 * span] for s in range(peers)]
    rows = jnp.concatenate(rows, axis=0)
    lane = lax.broadcasted_iota(jnp.int32, (share * peers, 2 * span), 1)
    row = lax.broadcasted_iota(jnp.int32, (share * peers, 2 * span), 0)
    lane = jnp.where(lane < span, lane, lane - span)
    spread = jnp.concatenate([rows] * share, axis=0)
    spread = jnp.where(lane // capacity == row // peers, spread, 0.0).astype(BF16)
    c = lax.broadcasted_iota(jnp.int32, (2 * span, plan.slots), 0)
    slot = lax.broadcasted_iota(jnp.int32, (2 * span, plan.slots), 1)
    scale = jnp.where(c < span, 64.0, 1.0)
    place = jnp.where(c % capacity == slot % capacity, scale, 0.0).astype(BF16)
    listed = matmul(spread, place)
    row = lax.broadcasted_iota(jnp.int32, listed.shape, 0)
    slot = lax.broadcasted_iota(jnp.int32, listed.shape, 1)
    listed = jnp.where(slot // capacity == row % peers, listed, 0.0)
    out_ref[...] = jnp.sum(listed.reshape(share, peers, plan.slots), axis=1)


def project(plan, place, lists, place_ref, w_ref, normed_ref, turn_ref, after_ref, *refs):
    if lists:
        q_ref, vo_ref, list_ref, table, sems = refs
        count, _, depth = table.shape

        def copy(part):
            source = normed_ref.at[pl.ds(0, table.shape[1]), part * depth : (part + 1) * depth]
            return pltpu.make_async_copy(source, table.at[part], sems.at[part])

        for part in range(count):
            copy(part).start()
        read_lists(plan, w_ref, list_ref)
    else:
        q_ref, vo_ref = refs[-2:]
    turns = turn_ref[place_ref[LINE]]
    half, k_half = plan.q_rows // 2, plan.k_rows // 2
    cosine, sine = turns[:, 0:1], turns[:, 1:2]
    cos_k, sin_k = cosine[:k_half], sine[:k_half]
    moves = table.shape[1] if lists else normed_ref.shape[0]
    block = moves if lists else math.gcd(moves, 128)
    for start in range(0, moves, block):
        at, to = slice(start, start + block), slice(place + start, place + start + block)
        total = None
        for part in range(count if lists else w_ref.shape[0] if len(w_ref.shape) == 3 else 1):
            w = w_ref[part] if len(w_ref.shape) == 3 else w_ref[...]
            if lists:
                copy(part).wait()
                values = table[part]
            else:
                values = normed_ref[at, part * w.shape[1] : (part + 1) * w.shape[1]]
            term = matmul(w, values, NT)
            total = term if total is None else total + term
        first, second = total[:half], total[half : 2 * half]
        f_first = (first * cosine - second * sine).astype(BF16).astype(F32)
        f_second = (second * cosine + first * sine).astype(BF16).astype(F32)
        first, second = total[plan.q_rows : plan.q_rows + k_half], total[plan.q_rows + k_half : plan.fold_at]
        k_first = (first * cos_k - second * sin_k).astype(BF16).astype(F32)
        k_second = (second * cos_k + first * sin_k).astype(BF16).astype(F32)
        logits, tails = [], []
        for h in range(plan.mine):
            own = slice(h * k_half, (h + 1) * k_half)
            logit = jnp.sum(f_first[own] * k_first + f_second[own] * k_second, axis=0, keepdims=True)
            logits.append(logit.astype(BF16).astype(F32))
            tails.append(logit - logits[-1])
        pad = plan.line_rows - plan.q_rows - 2 * plan.mine
        pieces = [f_first, f_second, *logits, *tails]
        if pad:
            pieces.append(jnp.zeros((pad, block), F32))
        out = jnp.concatenate(pieces, axis=0).astype(BF16)
        if plan.direct:
            q_ref[:, to] = out
        else:
            for line in range(plan.line):
                q_ref[line, :, to] = out
        vo_ref[:, to] = total[plan.fold_at : plan.list_at]


def tied(x, *others):
    return pl.pallas_call(
        lambda *refs: None,
        out_shape=shape(x.shape, x.dtype),
        in_specs=[untouched()] + [pl.BlockSpec(memory_space=pltpu.HBM)] * len(others),
        out_specs=untouched(),
        input_output_aliases={0: 0},
        compiler_params=limits(1),
        cost_estimate=cost(0, 0),
    )(x, *others)


def pack_prefix(plan, prefix_hbm, ws_hbm, after_ref, out_ref, *scratch):
    values, ws_ref, sems = scratch
    boards = values.shape[0]
    heads = plan.heads
    copies = (
        pltpu.make_async_copy(ws_hbm, ws_ref, sems.at[0]),
        pltpu.make_async_copy(prefix_hbm.at[:, :, pl.ds(HD, HD)], values, sems.at[1]),
        pltpu.make_async_copy(prefix_hbm.at[:, :, pl.ds(0, HD)], out_ref.at[pl.ds(0, boards)], sems.at[2]),
    )
    for copy in copies:
        copy.start()
    copies[0].wait()
    span = HD // boards
    ws = jnp.concatenate([ws_ref[...].astype(F32)] * (HD // heads), axis=0)
    row = lax.broadcasted_iota(jnp.int32, (HD, 1), 0)
    copies[1].wait()
    fold = None
    for board in range(boards):
        keep = (row // span == board) & (row % span < 2 * heads)
        term = matmul(values[board], jnp.where(keep, ws, 0.0).astype(BF16), NT)
        fold = term if fold is None else fold + term
    rounded = fold.astype(BF16).astype(F32)
    lane = lax.broadcasted_iota(jnp.int32, fold.shape, 1)
    out_ref[boards] = jnp.where(lane % span < heads, rounded, fold - rounded).astype(BF16)
    copies[2].wait()


def fold_columns(plan, here, block, board, boards, heads):
    lanes = plan.mine * plan.slots
    row = lax.broadcasted_iota(jnp.int32, (HD, lanes), 0) - board * (HD // boards)
    head = here * plan.mine + lax.broadcasted_iota(jnp.int32, (HD, lanes), 1) // plan.slots
    pick = jnp.where((row == head) | (row == head + heads), 1.0, 0.0).astype(BF16)
    return matmul(block, pick)


def prepare(plan, place_ref, board_ref, own_ref, other_ref, *rest):
    *prefix_refs, chosen_ref, fold_ref, slot_ref = rest
    count = board_ref.shape[1]
    board_row = board_ref[...]
    board_col = jnp.broadcast_to(board_row.astype(F32), (8, count)).T[:, 0:1].astype(jnp.int32)
    ahead = lax.broadcasted_iota(jnp.int32, (count, count), 0) < lax.broadcasted_iota(jnp.int32, (count, count), 1)
    rank = jnp.sum(jnp.where((board_col == board_row) & ahead, 1.0, 0.0), axis=0, keepdims=True)
    slot_ref[...] = rank.astype(jnp.int32) + place_ref[PEER] * plan.capacity
    here = place_ref[SLAB]
    boards, moves = chosen_ref.shape[0], chosen_ref.shape[1]
    move_at = lax.broadcasted_iota(jnp.int32, (moves, plan.slots), 0) + 1

    def step(board, carry):
        for j in range(plan.slab):
            place = ((here ^ j) % plan.pair) * boards + board
            row = (own_ref, other_ref)[j // plan.pair][pl.ds(place, 1), :].astype(jnp.int32)
            at = slice(j * plan.slots, (j + 1) * plan.slots)
            chosen_ref[board, :, at] = jnp.where(move_at == row, 1.0, 0.0).astype(BF16)
        for j, prefix_ref in enumerate(prefix_refs):
            fold_ref[j, board] = fold_columns(plan, here, prefix_ref[boards], board, boards, plan.heads)
        return carry

    lax.fori_loop(0, boards, step, 0)


def attend(plan, place_ref, vo_ref, own_ref, other_ref, chosen_ref, fold_ref, *rest):
    prefix_refs, rest = rest[: plan.slab], rest[plan.slab :]
    *q_refs, out_ref, table, extra, scores, taken_even, taken_odd = rest
    here = place_ref[SLAB]
    mine, heads, slots = plan.mine, plan.heads, plan.slots
    moves = vo_ref.shape[1]
    boards = prefix_refs[0].shape[0] - 1
    query_rows = mine * HD

    mixed = None
    for step, q_ref in enumerate(q_refs):
        r = lax.broadcasted_iota(jnp.int32, (query_rows + 8, q_ref.shape[0]), 0)
        c = lax.broadcasted_iota(jnp.int32, (query_rows + 8, q_ref.shape[0]), 1)
        line, at = (place_ref[LINE] ^ step, c) if plan.direct else (c // plan.line_rows, c % plan.line_rows)
        part, head, entry = at // (mine * plan.pairs), (at // plan.pairs) % mine, at % plan.pairs
        goes = jnp.where(at < plan.q_rows, head * HD + part * HALF + line * plan.pairs + entry, -1)
        tail = at - plan.q_rows
        goes = jnp.where((tail >= 0) & (tail < 2 * mine), query_rows + tail % mine, goes)
        term = matmul(jnp.where(r == goes, 1.0, 0.0).astype(BF16), q_ref[...])
        mixed = term if mixed is None else mixed + term
    table[:query_rows] = mixed[:query_rows].astype(BF16)
    extra[...] = jnp.zeros_like(extra)
    for place, value in ((0, mixed[query_rows : query_rows + mine]), (2 * mine, vo_ref[...])):
        rounded = value.astype(BF16).astype(F32)
        extra[place : place + mine] = rounded
        extra[place + mine : place + 2 * mine] = value - rounded
    table[query_rows:] = extra[...].astype(BF16)

    scale = math.log2(math.e) / math.sqrt(HD)
    def per_head(x, base):
        pieces = [x[base + h : base + h + 1] + x[base + mine + h : base + mine + h + 1] for h in range(mine)]
        return jnp.concatenate(pieces, axis=1)

    def moves_of(j, board):
        place = ((here ^ j) % plan.pair) * boards + board
        return (own_ref, other_ref)[j // plan.pair][pl.ds(place, 1), :].astype(jnp.int32)

    def gather(board, taken):
        taken[...] = matmul(table[...], chosen_ref[board])

    def score_board(board, taken):
        for j in range(plan.slab):
            x = taken[:, j * slots : (j + 1) * slots]
            q = jnp.concatenate([x[h * HD : (h + 1) * HD].astype(BF16) for h in range(mine)], axis=1)
            logits = matmul(prefix_refs[j][board], q)
            if j < plan.slab - 1:
                fold = fold_ref[j, board]
            else:
                fold = fold_columns(plan, here, prefix_refs[j][boards], board, boards, heads)
            own_logit = per_head(x, query_rows)
            own_value = per_head(x, query_rows + 2 * mine)
            peak = jnp.maximum(jnp.max(logits, axis=0, keepdims=True), own_logit)
            weight = jnp.exp2((logits - peak) * scale)
            own_weight = jnp.exp2((own_logit - peak) * scale)
            denom = jnp.sum(weight, axis=0, keepdims=True) + own_weight
            value = (jnp.sum(weight * fold, axis=0, keepdims=True) + own_value * own_weight) / denom
            score = sum(value[:, h * slots : (h + 1) * slots] for h in range(mine))
            scores[here ^ j, pl.ds(board, 1), :] = jnp.where(moves_of(j, board) > 0, score, DEAD)

    gather(0, taken_even)

    def step(at, carry):
        board = 2 * at
        gather(jnp.minimum(board + 1, boards - 1), taken_odd)
        score_board(board, taken_even)
        gather(jnp.minimum(board + 2, boards - 1), taken_even)
        score_board(jnp.minimum(board + 1, boards - 1), taken_odd)
        return carry

    lax.fori_loop(0, -(-boards // 2), step, 0)
    live = scores[...] > 0.5 * DEAD
    count = jnp.sum(jnp.where(live, 1.0, 0.0), axis=2, keepdims=True)
    mean = jnp.sum(jnp.where(live, scores[...], 0.0), axis=2, keepdims=True) / jnp.maximum(count, 1.0)
    centered = jnp.where(live, scores[...] - mean, DEAD)
    for g in range(plan.groups):
        both = jnp.concatenate([centered[g * plan.pair + p] for p in range(plan.pair)], axis=0).astype(BF16)
        for copy in range(out_ref.shape[1]):
            out_ref[g, copy] = both


def finish(plan, parts_ref, board_ref, slot_ref, out_ref):
    line = parts_ref.shape[1]
    columns = []
    for at in range(line):
        total = None
        for g in range(parts_ref.shape[0]):
            for p in range(parts_ref.shape[2]):
                term = parts_ref[g, at, p].astype(F32)
                total = term if total is None else total + term
        columns.append(total)
    scores = jnp.concatenate(columns, axis=0)
    live = scores > 0.5 * DEAD
    peak = jnp.max(scores, axis=1, keepdims=True)
    denom = jnp.sum(jnp.where(live, jnp.exp(scores - peak), 0.0), axis=1, keepdims=True)
    logprob = jnp.where(live, scores - peak - jnp.log(denom), 0.0)
    count = board_ref.shape[1]
    member = lax.broadcasted_iota(jnp.int32, (scores.shape[0], count), 0) == board_ref[...]
    member = jnp.where(member, 1.0, 0.0).astype(BF16)
    found = jnp.zeros((plan.slots, count), F32)
    for _ in range(3):
        rounded = logprob.astype(BF16)
        found = found + matmul(rounded, member, TN)
        logprob = logprob - rounded.astype(F32)
    at = lax.broadcasted_iota(jnp.int32, (plan.slots, count), 0) == slot_ref[...]
    out_ref[...] = jnp.sum(jnp.where(at, found, 0.0), axis=0, keepdims=True)


def untouched():
    return pl.BlockSpec(memory_space=pl.ANY)


def local_call(kernel, place, args, outs, scratch=(), mib=40, copied=(), flops=0, nbytes=0, aliases=None, fetched=()):
    vmem, hbm = pl.BlockSpec(memory_space=pltpu.VMEM), pl.BlockSpec(memory_space=pltpu.HBM)
    return pl.pallas_call(
        kernel,
        out_shape=outs,
        in_specs=[pl.BlockSpec(memory_space=pltpu.SMEM)]
        + [hbm if at in fetched else untouched() if at in copied else vmem for at in range(len(args))],
        out_specs=jax.tree.map(lambda x: vmem, outs),
        scratch_shapes=scratch,
        input_output_aliases=aliases or {},
        compiler_params=limits(mib),
        cost_estimate=cost(flops, nbytes),
    )(place, *args)


def cost(flops, nbytes):
    return pl.CostEstimate(flops=int(flops), bytes_accessed=int(nbytes), transcendentals=0)


def swap(x, names, size, step):
    return lax.ppermute(x, names, [(at, at ^ step) for at in range(size)])


def shape(dims, dtype):
    return jax.ShapeDtypeStruct(tuple(dims), dtype)


def turn_table(position):
    frequency = THETA ** (-2.0 * np.arange(HALF, dtype=np.float32) / HD)
    angles = np.float32(position) * frequency.astype(np.float32)
    return np.stack([np.cos(angles), np.sin(angles)], axis=1).astype(np.float32)


def per_device(prefix_kv, move_ids, move_board, move_table, norm_gain, w_query, w_keyval, w_score):
    row_count = move_ids.shape[0]
    boards_here, prefix_len, _ = prefix_kv.shape
    moves, width = move_table.shape
    groups, line, pair = lax.axis_size("groups"), lax.axis_size("line"), lax.axis_size("pair")
    board_total = boards_here * line * pair
    capacity = max(2, (2 * row_count + board_total - 1) // board_total)
    heads = w_query.shape[1] // HD
    plan = Plan(groups, line, pair, heads, capacity, pair * boards_here)
    depth = w_query.shape[0]
    group_at = lax.axis_index("groups").astype(jnp.int32)
    line_at = lax.axis_index("line").astype(jnp.int32)
    pair_at = lax.axis_index("pair").astype(jnp.int32)
    place = jnp.stack([group_at, line_at, line_at * pair + pair_at, group_at * pair + pair_at])
    ws = w_score.reshape(heads, HD)
    slab_axes = ("groups", "pair")
    board_row = move_board.reshape(1, row_count)

    half_cols = w_query.shape[1] // groups
    packed = local_call(
        functools.partial(pack_weights, plan),
        group_at.reshape(1),
        (w_query, w_keyval, ws, board_row, move_ids.reshape(1, row_count)),
        shape((plan.peers, plan.rows, depth), BF16),
        [
            pltpu.VMEM((depth, half_cols), BF16),
            pltpu.VMEM((depth, 2 * HD), BF16),
            pltpu.VMEM((heads, HD), BF16),
            pltpu.VMEM((1, row_count), jnp.int32),
            pltpu.VMEM((1, row_count), jnp.int32),
            pltpu.VMEM((plan.peers * plan.rows, half_cols + 2 * HD), F32),
            pltpu.SemaphoreType.DMA((5,)),
        ],
        62,
        range(5),
    )
    weights = lax.all_to_all(packed, ("line", "pair"), split_axis=0, concat_axis=0, tiled=True)

    payload = pl.pallas_call(
        functools.partial(pack_prefix, plan),
        out_shape=shape((boards_here + 1, prefix_len, HD), BF16),
        in_specs=[untouched()] * 3,
        out_specs=pl.BlockSpec(memory_space=pltpu.VMEM),
        scratch_shapes=[
            pltpu.VMEM((boards_here, prefix_len, HD), BF16),
            pltpu.VMEM((heads, HD), BF16),
            pltpu.SemaphoreType.DMA((3,)),
        ],
        compiler_params=limits(56),
        cost_estimate=cost(0, 0),
    )(prefix_kv, ws, packed)
    beside = swap(payload, slab_axes, plan.slab, 1)
    across = swap(payload, slab_axes, plan.slab, 2)

    block = min(moves, 128)
    blocks = (moves * 3 // 8, moves * 5 // 8)
    vmem = pl.BlockSpec(memory_space=pltpu.VMEM)
    *normed, mark = pl.pallas_call(
        normalize,
        out_shape=[shape((moves, width), BF16), shape((blocks[1], width), BF16), pltpu.HBM((8, width), BF16)],
        in_specs=[untouched(), vmem, untouched()],
        out_specs=[untouched()] * 3,
        scratch_shapes=[
            pltpu.VMEM((1, width), F32),
            pltpu.VMEM((3, block, width), BF16),
            pltpu.VMEM((3, block, width), BF16),
            pltpu.SemaphoreType.DMA((3,)),
            pltpu.SemaphoreType.DMA((3,)),
        ],
        compiler_params=limits(58),
        cost_estimate=cost(moves * width, moves * width // 4),
    )(move_table, norm_gain.reshape(width // HD, HD), packed)
    turns = turn_table(prefix_len).reshape(line, 1, plan.pairs, 2)
    turns = np.tile(turns, (1, plan.mine, 1, 1)).reshape(line, plan.mine * plan.pairs, 2)
    flat = weights.transpose(1, 0, 2).reshape(plan.rows, width) if depth % HD else weights
    sent = (plan.line_rows, moves)
    outs = (shape(sent if plan.direct else (line, *sent), BF16), shape((plan.mine, moves), F32))
    across = tied(across, mark)
    diagonal = swap(across, slab_axes, plan.slab, 1)
    parts = plan.peers if flat.ndim == 3 else 1
    queries, own_values, listed = local_call(
        functools.partial(project, plan, 0, True),
        place,
        (flat, normed[0], jnp.asarray(turns), across),
        (*outs, shape((plan.share, plan.slots), F32)),
        [pltpu.VMEM((parts, blocks[0], width // parts), BF16), pltpu.SemaphoreType.DMA((parts,))],
        53,
        (3,),
        blocks[0] * width * 2048,
        blocks[0] * width,
        fetched=(1,),
    )
    queries, own_values = local_call(
        functools.partial(project, plan, blocks[0], False),
        place,
        (flat, normed[1], jnp.asarray(turns), beside, queries, own_values),
        outs,
        (),
        20,
        (3,),
        blocks[1] * width * 2048,
        blocks[1] * width,
        {5: 0, 6: 1},
    )
    other = swap(listed, slab_axes, plan.slab, pair)
    if plan.direct:
        queries = [queries] + [swap(queries, "line", line, step) for step in range(1, line)]
    else:
        queries = lax.all_to_all(queries, "line", split_axis=0, concat_axis=0, tiled=True)
        queries = [queries.reshape(line * plan.line_rows, moves)]

    query_rows = plan.mine * HD
    back = plan.peers * lax.axis_size("tensor")
    chosen, folds, slot_row = local_call(
        functools.partial(prepare, plan),
        place,
        (board_row, listed, other, payload, beside, across),
        (
            shape((boards_here, moves, plan.slab * plan.slots), BF16),
            shape((plan.slab - 1, boards_here, prefix_len, plan.mine * plan.slots), F32),
            shape((1, row_count), jnp.int32),
        ),
        mib=20,
        flops=10**9,
        nbytes=10**6,
    )
    parts = local_call(
        functools.partial(attend, plan),
        place,
        (own_values, listed, other, chosen, folds, payload, beside, across, diagonal, *queries),
        shape((groups, back, plan.share, plan.slots), BF16),
        [
            pltpu.VMEM((query_rows + 16, moves), BF16),
            pltpu.VMEM((16, moves), F32),
            pltpu.VMEM((plan.slab, boards_here, plan.slots), F32),
            pltpu.VMEM((query_rows + 16, plan.slab * plan.slots), F32),
            pltpu.VMEM((query_rows + 16, plan.slab * plan.slots), F32),
        ],
        24,
    )
    parts = lax.all_to_all(
        parts.reshape(groups * back, plan.share, plan.slots),
        ("groups", "line", "pair", "tensor"),
        split_axis=0,
        concat_axis=0,
        tiled=True,
    )
    parts = parts.reshape(groups, line, back // line, plan.share, plan.slots)
    logprob = pl.pallas_call(
        functools.partial(finish, plan), out_shape=shape((1, row_count), F32), compiler_params=limits(VMEM_MIB)
    )(parts, board_row, slot_row)
    return logprob.reshape(row_count)


def solution(mesh):
    order = ("groups", "dp", "tensor")
    assert mesh.axis_names == order
    pair = 2
    groups, peers, tensor = (mesh.shape[name] for name in order)
    fine = Mesh(mesh.devices.reshape(groups, peers // pair, pair, tensor), ("groups", "line", "pair", "tensor"))
    rows = ("groups", "line", "pair")
    placed = (
        P(rows, None, "tensor"),
        P(rows),
        P(rows, None),
        P(),
        P(),
        P(("line", "pair"), "tensor"),
        P(("line", "pair"), "tensor"),
        P("tensor"),
    )
    return jax.shard_map(per_device, mesh=fine, in_specs=placed, out_specs=P(rows), check_vma=False)
```

```python
import functools
import math

import jax
import jax.numpy as jnp
import numpy as np
from jax import lax
from jax.experimental import pallas as pl
from jax.experimental.pallas import tpu as pltpu
from jax.sharding import Mesh
from jax.sharding import PartitionSpec as P

HD = 128
HALF = HD // 2
EPS = 1e-06
THETA = 5000000.0
DEAD = -1e30
VMEM_MIB = 52
GROUP, LINE, PEER, SLAB = range(4)

F32 = jnp.float32
BF16 = jnp.bfloat16

NN = (((1,), (0,)), ((), ()))
NT = (((1,), (1,)), ((), ()))
TN = (((0,), (0,)), ((), ()))


def matmul(a, b, dims=NN):
    return lax.dot_general(a, b, dims, preferred_element_type=F32)


def limits(mib):
    return pltpu.CompilerParams(vmem_limit_bytes=mib * 1024 * 1024)


class Plan:
    def __init__(self, groups, line, pair, heads, capacity, share):
        self.groups, self.line, self.pair = groups, line, pair
        self.peers = line * pair
        self.slab = groups * pair
        self.heads = heads
        self.mine = heads // self.slab
        self.pairs = HALF // line
        self.q_rows = self.mine * 2 * self.pairs
        self.k_rows = 2 * self.pairs
        self.fold_at = self.q_rows + self.k_rows
        self.list_at = self.fold_at + self.mine
        self.rows = -(-(self.list_at + 1) // 8) * 8
        self.line_rows = -(-(self.q_rows + 2 * self.mine) // 8) * 8
        self.capacity = capacity
        self.share = share
        self.slots = self.peers * capacity
        self.direct = line <= 4


def pack_weights(plan, place_ref, wq_hbm, wkv_hbm, ws_hbm, board_hbm, ids_hbm, *rest):
    out_ref, wq, wkv, ws_ref, board_ref, ids_ref, pick, sems = rest
    group = place_ref[0]
    half_cols = wq.shape[1]
    columns_here = pl.ds(pl.multiple_of(group * half_cols, HD), half_cols)
    copies = (
        pltpu.make_async_copy(ws_hbm, ws_ref, sems.at[0]),
        pltpu.make_async_copy(board_hbm, board_ref, sems.at[1]),
        pltpu.make_async_copy(ids_hbm, ids_ref, sems.at[2]),
        pltpu.make_async_copy(wq_hbm.at[:, columns_here], wq, sems.at[3]),
        pltpu.make_async_copy(wkv_hbm, wkv, sems.at[4]),
    )
    for copy in copies:
        copy.start()
    for copy in copies[:3]:
        copy.wait()
    count, depth = board_ref.shape[1], wq.shape[0]
    board_row = board_ref[...]
    board_col = jnp.broadcast_to(board_row.astype(F32), (8, count)).T[:, 0:1].astype(jnp.int32)
    own = lax.broadcasted_iota(jnp.int32, (count, count), 0)
    other = lax.broadcasted_iota(jnp.int32, (count, count), 1)
    ahead = jnp.where((board_col == board_row) & (other < own), 1.0, 0.0)
    rank = jnp.sum(ahead, axis=1, keepdims=True).astype(jnp.int32)
    move = ids_ref[...] + 1
    boards, span = plan.line * plan.share, plan.share * plan.capacity
    member = lax.broadcasted_iota(jnp.int32, (boards, count), 0) == board_row
    parts = [jnp.where(member, part.astype(F32), 0.0) for part in (move // 64, move % 64)]
    lane = lax.broadcasted_iota(jnp.int32, (count, depth), 1)
    ranked = jnp.where(rank == (lane % span) % plan.capacity, 1.0, 0.0).astype(BF16)
    found = matmul(jnp.concatenate(parts, axis=0).astype(BF16), ranked)
    lane = lax.broadcasted_iota(jnp.int32, (2 * boards, depth), 1)
    row = lax.broadcasted_iota(jnp.int32, (2 * boards, depth), 0)
    keep = (row // boards == lane // span) & (row % plan.share == (lane % span) // plan.capacity)
    found = jnp.where(keep, found, 0.0)
    lists = []
    for line in range(plan.line):
        at = line * plan.share
        both = found[at : at + plan.share] + found[boards + at : boards + at + plan.share]
        lists.append(jnp.sum(both, axis=0, keepdims=True))

    if plan.pairs % 16 == 0:
        turn_weights(plan, group, lists, copies[3:], wq, wkv, ws_ref, out_ref)
    else:
        pick_weights(plan, group, lists, copies[3:], wq, wkv, ws_ref, out_ref, pick)


def turn_weights(plan, group, lists, copies, wq, wkv, ws_ref, out_ref):
    for copy in copies:
        copy.wait()
    q = wq[...].T
    k = wkv[:, :HD].T
    folds = matmul(ws_ref[...], wkv[:, HD:], NT)
    row = lax.broadcasted_iota(jnp.int32, folds.shape, 0)
    pairs = plan.pairs
    zeros = jnp.zeros((plan.rows - plan.list_at - 1, folds.shape[1]), F32)
    for pair in range(plan.pair):
        first = (group * plan.pair + pair) * plan.mine
        mine = [jnp.sum(jnp.where(row == first + h, folds, 0.0), axis=0, keepdims=True) for h in range(plan.mine)]
        for line in range(plan.line):
            peer = line * plan.pair + pair
            for part in range(2):
                entry = part * HALF + line * pairs
                for h in range(plan.mine):
                    at = (part * plan.mine + h) * pairs
                    source = (pair * plan.mine + h) * HD + entry
                    out_ref[peer, at : at + pairs] = q[source : source + pairs]
                at = plan.q_rows + part * pairs
                out_ref[peer, at : at + pairs] = k[entry : entry + pairs]
            last = jnp.concatenate([*mine, lists[line], zeros], axis=0)
            out_ref[peer, plan.fold_at :] = last.astype(BF16)


def pick_weights(plan, group, lists, copies, wq, wkv, ws_ref, out_ref, pick):
    rows, half_cols = plan.rows, wq.shape[1]
    r = lax.broadcasted_iota(jnp.int32, (rows, 1), 0)
    part = r // (plan.mine * plan.pairs)
    head = (r // plan.pairs) % plan.mine
    entry = r % plan.pairs
    is_q = r < plan.q_rows
    k_at = r - plan.q_rows
    is_k = (k_at >= 0) & (k_at < plan.k_rows)
    f_at = r - plan.fold_at
    is_f = (f_at >= 0) & (f_at < plan.mine)
    q_lane = lax.broadcasted_iota(jnp.int32, (rows, half_cols), 1)
    k_lane = lax.broadcasted_iota(jnp.int32, (rows, HD), 1)
    ws = ws_ref[...].astype(F32)

    def fill(peer, carry):
        line, pair = peer // plan.pair, peer % plan.pair
        column = (pair * plan.mine + head) * HD + part * HALF + line * plan.pairs + entry
        column = jnp.where(is_q, column, -1)
        at = pl.ds(pl.multiple_of(peer * rows, 8), rows)
        pick[at, :half_cols] = jnp.where(q_lane == column, 1.0, 0.0)
        k_column = (k_at // plan.pairs) * HALF + line * plan.pairs + k_at % plan.pairs
        k_column = jnp.where(is_k, k_column, -1)
        pick[at, half_cols : half_cols + HD] = jnp.where(k_lane == k_column, 1.0, 0.0)
        fold = jnp.zeros((rows, HD), F32)
        my_head = jnp.where(is_f, (group * plan.pair + pair) * plan.mine + f_at, -1)
        for h in range(plan.heads):
            fold = jnp.where(my_head == h, ws[h : h + 1], fold)
        pick[at, half_cols + HD :] = fold
        return carry

    lax.fori_loop(0, plan.peers, fill, 0, unroll=plan.peers <= 8)

    for copy in copies:
        copy.wait()
    left = pick[...].astype(BF16)
    total = matmul(left[:, :half_cols], wq[...], NT) + matmul(left[:, half_cols:], wkv[...], NT)
    for peer in range(plan.peers):
        mine = total[peer * rows : (peer + 1) * rows]
        out_ref[peer] = jnp.where(r == plan.list_at, lists[peer // plan.pair], mine).astype(BF16)


def normalize(table_hbm, gain_ref, after_ref, *refs):
    *outs, mark_ref, gain, buffers, made, sems, out_sems = refs
    held, block, _ = buffers.shape
    steps = table_hbm.shape[0] // block
    each = outs[0].shape[0] // block

    def copy(step):
        source = table_hbm.at[pl.ds(step * block, block)]
        return pltpu.make_async_copy(source, buffers.at[step % held], sems.at[step % held])

    def store(step):
        target = outs[step // each].at[pl.ds(step % each * block, block)]
        return pltpu.make_async_copy(made.at[step % held], target, out_sems.at[step % held])

    for step in range(min(held, steps)):
        copy(step).start()
    rows = gain_ref[...].astype(F32)
    gain[...] = jnp.concatenate([rows[r : r + 1] for r in range(rows.shape[0])], axis=1)
    for step in range(steps):
        copy(step).wait()
        if step >= held:
            store(step - held).wait()
        raw = buffers[step % held].astype(F32)
        inverse = lax.rsqrt(jnp.mean(raw * raw, axis=-1, keepdims=True) + EPS)
        made[step % held] = (raw * inverse * gain[...]).astype(BF16)
        store(step).start()
        if step + held < steps:
            copy(step + held).start()
    for step in range(max(0, steps - held), steps):
        store(step).wait()
    mark = pltpu.make_async_copy(made.at[0, pl.ds(0, mark_ref.shape[0])], mark_ref, out_sems.at[0])
    mark.start()
    mark.wait()


def read_lists(plan, w_ref, out_ref):
    share, capacity, peers = plan.share, plan.capacity, plan.peers
    span = share * capacity
    if len(w_ref.shape) == 3:
        rows = [w_ref[s].astype(F32)[plan.list_at : plan.list_at + 1] for s in range(peers)]
    else:
        row = w_ref[...].astype(F32)[plan.list_at : plan.list_at + 1]
        rows = [row[:, s * 2 * span : (s + 1) * 2 * span] for s in range(peers)]
    rows = jnp.concatenate(rows, axis=0)
    lane = lax.broadcasted_iota(jnp.int32, (share * peers, 2 * span), 1)
    row = lax.broadcasted_iota(jnp.int32, (share * peers, 2 * span), 0)
    lane = jnp.where(lane < span, lane, lane - span)
    spread = jnp.concatenate([rows] * share, axis=0)
    spread = jnp.where(lane // capacity == row // peers, spread, 0.0).astype(BF16)
    c = lax.broadcasted_iota(jnp.int32, (2 * span, plan.slots), 0)
    slot = lax.broadcasted_iota(jnp.int32, (2 * span, plan.slots), 1)
    scale = jnp.where(c < span, 64.0, 1.0)
    place = jnp.where(c % capacity == slot % capacity, scale, 0.0).astype(BF16)
    listed = matmul(spread, place)
    row = lax.broadcasted_iota(jnp.int32, listed.shape, 0)
    slot = lax.broadcasted_iota(jnp.int32, listed.shape, 1)
    listed = jnp.where(slot // capacity == row % peers, listed, 0.0)
    out_ref[...] = jnp.sum(listed.reshape(share, peers, plan.slots), axis=1)


def project(plan, place, lists, place_ref, w_ref, normed_ref, turn_ref, after_ref, *refs):
    if lists:
        *refs, list_ref = refs
        read_lists(plan, w_ref, list_ref)
    q_ref, vo_ref = refs[-2:]
    turns = turn_ref[place_ref[LINE]]
    half, k_half = plan.q_rows // 2, plan.k_rows // 2
    cosine, sine = turns[:, 0:1], turns[:, 1:2]
    cos_k, sin_k = cosine[:k_half], sine[:k_half]
    moves = normed_ref.shape[0]
    block = min(moves, HD)
    every = []
    for start in range(0, moves, block):
        at, to = slice(start, start + block), slice(place + start, place + start + block)
        if len(w_ref.shape) == 3:
            depth = w_ref.shape[2]
            total = None
            for s in range(w_ref.shape[0]):
                term = matmul(w_ref[s], normed_ref[at, s * depth : (s + 1) * depth], NT)
                total = term if total is None else total + term
        else:
            total = matmul(w_ref[...], normed_ref[at, :], NT)
        first, second = total[:half], total[half : 2 * half]
        f_first = (first * cosine - second * sine).astype(BF16).astype(F32)
        f_second = (second * cosine + first * sine).astype(BF16).astype(F32)
        first, second = total[plan.q_rows : plan.q_rows + k_half], total[plan.q_rows + k_half : plan.fold_at]
        k_first = (first * cos_k - second * sin_k).astype(BF16).astype(F32)
        k_second = (second * cos_k + first * sin_k).astype(BF16).astype(F32)
        logits, tails = [], []
        for h in range(plan.mine):
            own = slice(h * k_half, (h + 1) * k_half)
            logit = jnp.sum(f_first[own] * k_first + f_second[own] * k_second, axis=0, keepdims=True)
            logits.append(logit.astype(BF16).astype(F32))
            tails.append(logit - logits[-1])
        if plan.direct:
            chunk = (place + start) // block * plan.q_rows
            q_ref[chunk : chunk + plan.q_rows] = jnp.concatenate([f_first, f_second], axis=0).astype(BF16)
            every += [*logits, *tails]
        else:
            pad = plan.line_rows - plan.q_rows - 2 * plan.mine
            pieces = [f_first, f_second, *logits, *tails]
            if pad:
                pieces.append(jnp.zeros((pad, block), F32))
            out = jnp.concatenate(pieces, axis=0).astype(BF16)
            for line in range(plan.line):
                q_ref[line, :, to] = out
        vo_ref[:, to] = total[plan.fold_at : plan.list_at]
    if plan.direct:
        first = vo_ref.shape[1] // HD * plan.q_rows + place // block * 2 * plan.mine
        q_ref[first : first + len(every)] = jnp.concatenate(every, axis=0).astype(BF16)


def tied(x, *others):
    return pl.pallas_call(
        lambda *refs: None,
        out_shape=shape(x.shape, x.dtype),
        in_specs=[untouched()] + [pl.BlockSpec(memory_space=pltpu.HBM)] * len(others),
        out_specs=untouched(),
        input_output_aliases={0: 0},
        compiler_params=limits(1),
        cost_estimate=cost(0, 0),
    )(x, *others)


def pack_prefix(plan, prefix_hbm, ws_hbm, after_ref, out_ref, *scratch):
    values, ws_ref, sems = scratch
    boards = values.shape[0]
    heads = plan.heads
    copies = (
        pltpu.make_async_copy(ws_hbm, ws_ref, sems.at[0]),
        pltpu.make_async_copy(prefix_hbm.at[:, :, pl.ds(HD, HD)], values, sems.at[1]),
        pltpu.make_async_copy(prefix_hbm.at[:, :, pl.ds(0, HD)], out_ref.at[pl.ds(0, boards)], sems.at[2]),
    )
    for copy in copies:
        copy.start()
    copies[0].wait()
    span = HD // boards
    ws = jnp.concatenate([ws_ref[...].astype(F32)] * (HD // heads), axis=0)
    row = lax.broadcasted_iota(jnp.int32, (HD, 1), 0)
    copies[1].wait()
    fold = None
    for board in range(boards):
        keep = (row // span == board) & (row % span < 2 * heads)
        term = matmul(values[board], jnp.where(keep, ws, 0.0).astype(BF16), NT)
        fold = term if fold is None else fold + term
    rounded = fold.astype(BF16).astype(F32)
    lane = lax.broadcasted_iota(jnp.int32, fold.shape, 1)
    out_ref[boards] = jnp.where(lane % span < heads, rounded, fold - rounded).astype(BF16)
    copies[2].wait()


def fold_columns(plan, here, block, board, boards, heads):
    lanes = plan.mine * plan.slots
    row = lax.broadcasted_iota(jnp.int32, (HD, lanes), 0) - board * (HD // boards)
    head = here * plan.mine + lax.broadcasted_iota(jnp.int32, (HD, lanes), 1) // plan.slots
    pick = jnp.where((row == head) | (row == head + heads), 1.0, 0.0).astype(BF16)
    return matmul(block, pick)


def prepare(plan, place_ref, board_ref, own_ref, other_ref, *rest):
    *prefix_refs, chosen_ref, fold_ref, slot_ref = rest
    count = board_ref.shape[1]
    board_row = board_ref[...]
    board_col = jnp.broadcast_to(board_row.astype(F32), (8, count)).T[:, 0:1].astype(jnp.int32)
    ahead = lax.broadcasted_iota(jnp.int32, (count, count), 0) < lax.broadcasted_iota(jnp.int32, (count, count), 1)
    rank = jnp.sum(jnp.where((board_col == board_row) & ahead, 1.0, 0.0), axis=0, keepdims=True)
    slot_ref[...] = rank.astype(jnp.int32) + place_ref[PEER] * plan.capacity
    here = place_ref[SLAB]
    boards, moves = chosen_ref.shape[0], chosen_ref.shape[1]
    move_at = lax.broadcasted_iota(jnp.int32, (moves, plan.slots), 0) + 1

    def step(board, carry):
        for j in range(plan.slab):
            place = ((here ^ j) % plan.pair) * boards + board
            row = (own_ref, other_ref)[j // plan.pair][pl.ds(place, 1), :].astype(jnp.int32)
            at = slice(j * plan.slots, (j + 1) * plan.slots)
            chosen_ref[board, :, at] = jnp.where(move_at == row, 1.0, 0.0).astype(BF16)
        for j, prefix_ref in enumerate(prefix_refs):
            fold_ref[j, board] = fold_columns(plan, here, prefix_ref[boards], board, boards, plan.heads)
        return carry

    lax.fori_loop(0, boards, step, 0)


def attend(plan, place_ref, vo_ref, own_ref, other_ref, chosen_ref, fold_ref, *rest):
    prefix_refs, rest = rest[: plan.slab], rest[plan.slab :]
    *q_refs, out_ref, table, extra, scores, taken_even, taken_odd = rest
    here = place_ref[SLAB]
    mine, heads, slots = plan.mine, plan.heads, plan.slots
    moves = vo_ref.shape[1]
    boards = prefix_refs[0].shape[0] - 1
    query_rows = mine * HD

    mixed = own_logits = None
    for step, q_ref in enumerate(q_refs):
        if plan.direct:
            chunks = range(moves // HD)
            values = jnp.concatenate([q_ref[c * plan.q_rows : (c + 1) * plan.q_rows] for c in chunks], axis=1)
            tails = q_ref[moves // HD * plan.q_rows :].astype(F32)
            tails = jnp.concatenate([tails[c * 2 * mine : (c + 1) * 2 * mine] for c in chunks], axis=1)
            tails = tails[:mine] + tails[mine:]
            own_logits = tails if own_logits is None else own_logits + tails
        else:
            values = q_ref[...]
        r = lax.broadcasted_iota(jnp.int32, (query_rows + 8, values.shape[0]), 0)
        c = lax.broadcasted_iota(jnp.int32, (query_rows + 8, values.shape[0]), 1)
        line, at = (place_ref[LINE] ^ step, c) if plan.direct else (c // plan.line_rows, c % plan.line_rows)
        part, head, entry = at // (mine * plan.pairs), (at // plan.pairs) % mine, at % plan.pairs
        goes = jnp.where(at < plan.q_rows, head * HD + part * HALF + line * plan.pairs + entry, -1)
        tail = at - plan.q_rows
        goes = jnp.where((tail >= 0) & (tail < 2 * mine), query_rows + tail % mine, goes)
        term = matmul(jnp.where(r == goes, 1.0, 0.0).astype(BF16), values)
        mixed = term if mixed is None else mixed + term
    if own_logits is None:
        own_logits = mixed[query_rows : query_rows + mine]
    table[:query_rows] = mixed[:query_rows].astype(BF16)
    extra[...] = jnp.zeros_like(extra)
    for place, value in ((0, own_logits), (2 * mine, vo_ref[...])):
        rounded = value.astype(BF16).astype(F32)
        extra[place : place + mine] = rounded
        extra[place + mine : place + 2 * mine] = value - rounded
    table[query_rows:] = extra[...].astype(BF16)

    scale = math.log2(math.e) / math.sqrt(HD)
    def per_head(x, base):
        pieces = [x[base + h : base + h + 1] + x[base + mine + h : base + mine + h + 1] for h in range(mine)]
        return jnp.concatenate(pieces, axis=1)

    def moves_of(j, board):
        place = ((here ^ j) % plan.pair) * boards + board
        return (own_ref, other_ref)[j // plan.pair][pl.ds(place, 1), :].astype(jnp.int32)

    def gather(board, taken):
        taken[...] = matmul(table[...], chosen_ref[board])

    def score_board(board, taken):
        for j in range(plan.slab):
            x = taken[:, j * slots : (j + 1) * slots]
            q = jnp.concatenate([x[h * HD : (h + 1) * HD].astype(BF16) for h in range(mine)], axis=1)
            logits = matmul(prefix_refs[j][board], q)
            if j < plan.slab - 1:
                fold = fold_ref[j, board]
            else:
                fold = fold_columns(plan, here, prefix_refs[j][boards], board, boards, heads)
            own_logit = per_head(x, query_rows)
            own_value = per_head(x, query_rows + 2 * mine)
            peak = jnp.maximum(jnp.max(logits, axis=0, keepdims=True), own_logit)
            weight = jnp.exp2((logits - peak) * scale)
            own_weight = jnp.exp2((own_logit - peak) * scale)
            denom = jnp.sum(weight, axis=0, keepdims=True) + own_weight
            value = (jnp.sum(weight * fold, axis=0, keepdims=True) + own_value * own_weight) / denom
            score = sum(value[:, h * slots : (h + 1) * slots] for h in range(mine))
            scores[here ^ j, pl.ds(board, 1), :] = jnp.where(moves_of(j, board) > 0, score, DEAD)

    gather(0, taken_even)

    def step(at, carry):
        board = 2 * at
        gather(jnp.minimum(board + 1, boards - 1), taken_odd)
        score_board(board, taken_even)
        gather(jnp.minimum(board + 2, boards - 1), taken_even)
        score_board(jnp.minimum(board + 1, boards - 1), taken_odd)
        return carry

    lax.fori_loop(0, -(-boards // 2), step, 0)
    live = scores[...] > 0.5 * DEAD
    count = jnp.sum(jnp.where(live, 1.0, 0.0), axis=2, keepdims=True)
    mean = jnp.sum(jnp.where(live, scores[...], 0.0), axis=2, keepdims=True) / jnp.maximum(count, 1.0)
    centered = jnp.where(live, scores[...] - mean, DEAD)
    for g in range(plan.groups):
        both = jnp.concatenate([centered[g * plan.pair + p] for p in range(plan.pair)], axis=0).astype(BF16)
        for copy in range(out_ref.shape[1]):
            out_ref[g, copy] = both


def finish(plan, parts_ref, board_ref, slot_ref, out_ref):
    line = parts_ref.shape[1]
    columns = []
    for at in range(line):
        total = None
        for g in range(parts_ref.shape[0]):
            for p in range(parts_ref.shape[2]):
                term = parts_ref[g, at, p].astype(F32)
                total = term if total is None else total + term
        columns.append(total)
    scores = jnp.concatenate(columns, axis=0)
    live = scores > 0.5 * DEAD
    peak = jnp.max(scores, axis=1, keepdims=True)
    denom = jnp.sum(jnp.where(live, jnp.exp(scores - peak), 0.0), axis=1, keepdims=True)
    logprob = jnp.where(live, scores - peak - jnp.log(denom), 0.0)
    count = board_ref.shape[1]
    member = lax.broadcasted_iota(jnp.int32, (scores.shape[0], count), 0) == board_ref[...]
    member = jnp.where(member, 1.0, 0.0).astype(BF16)
    found = jnp.zeros((plan.slots, count), F32)
    for _ in range(3):
        rounded = logprob.astype(BF16)
        found = found + matmul(rounded, member, TN)
        logprob = logprob - rounded.astype(F32)
    at = lax.broadcasted_iota(jnp.int32, (plan.slots, count), 0) == slot_ref[...]
    out_ref[...] = jnp.sum(jnp.where(at, found, 0.0), axis=0, keepdims=True)


def untouched():
    return pl.BlockSpec(memory_space=pl.ANY)


def local_call(kernel, place, args, outs, scratch=(), mib=40, copied=(), flops=0, nbytes=0, aliases=None):
    vmem = pl.BlockSpec(memory_space=pltpu.VMEM)
    return pl.pallas_call(
        kernel,
        out_shape=outs,
        in_specs=[pl.BlockSpec(memory_space=pltpu.SMEM)]
        + [untouched() if at in copied else vmem for at in range(len(args))],
        out_specs=jax.tree.map(lambda x: vmem, outs),
        scratch_shapes=scratch,
        input_output_aliases=aliases or {},
        compiler_params=limits(mib),
        cost_estimate=cost(flops, nbytes),
    )(place, *args)


def cost(flops, nbytes):
    return pl.CostEstimate(flops=int(flops), bytes_accessed=int(nbytes), transcendentals=0)


def swap(x, names, size, step):
    return lax.ppermute(x, names, [(at, at ^ step) for at in range(size)])


def shape(dims, dtype):
    return jax.ShapeDtypeStruct(tuple(dims), dtype)


def turn_table(position):
    frequency = THETA ** (-2.0 * np.arange(HALF, dtype=np.float32) / HD)
    angles = np.float32(position) * frequency.astype(np.float32)
    return np.stack([np.cos(angles), np.sin(angles)], axis=1).astype(np.float32)


def per_device(prefix_kv, move_ids, move_board, move_table, norm_gain, w_query, w_keyval, w_score):
    row_count = move_ids.shape[0]
    boards_here, prefix_len, _ = prefix_kv.shape
    moves, width = move_table.shape
    groups, line, pair = lax.axis_size("groups"), lax.axis_size("line"), lax.axis_size("pair")
    board_total = boards_here * line * pair
    capacity = max(2, (2 * row_count + board_total - 1) // board_total)
    heads = w_query.shape[1] // HD
    plan = Plan(groups, line, pair, heads, capacity, pair * boards_here)
    depth = w_query.shape[0]
    group_at = lax.axis_index("groups").astype(jnp.int32)
    line_at = lax.axis_index("line").astype(jnp.int32)
    pair_at = lax.axis_index("pair").astype(jnp.int32)
    place = jnp.stack([group_at, line_at, line_at * pair + pair_at, group_at * pair + pair_at])
    ws = w_score.reshape(heads, HD)
    slab_axes = ("groups", "pair")
    board_row = move_board.reshape(1, row_count)

    half_cols = w_query.shape[1] // groups
    packed = local_call(
        functools.partial(pack_weights, plan),
        group_at.reshape(1),
        (w_query, w_keyval, ws, board_row, move_ids.reshape(1, row_count)),
        shape((plan.peers, plan.rows, depth), BF16),
        [
            pltpu.VMEM((depth, half_cols), BF16),
            pltpu.VMEM((depth, 2 * HD), BF16),
            pltpu.VMEM((heads, HD), BF16),
            pltpu.VMEM((1, row_count), jnp.int32),
            pltpu.VMEM((1, row_count), jnp.int32),
            pltpu.VMEM((plan.peers * plan.rows, half_cols + 2 * HD), F32),
            pltpu.SemaphoreType.DMA((5,)),
        ],
        62,
        range(5),
    )
    weights = lax.all_to_all(packed, ("line", "pair"), split_axis=0, concat_axis=0, tiled=True)

    payload = pl.pallas_call(
        functools.partial(pack_prefix, plan),
        out_shape=shape((boards_here + 1, prefix_len, HD), BF16),
        in_specs=[untouched()] * 3,
        out_specs=pl.BlockSpec(memory_space=pltpu.VMEM),
        scratch_shapes=[
            pltpu.VMEM((boards_here, prefix_len, HD), BF16),
            pltpu.VMEM((heads, HD), BF16),
            pltpu.SemaphoreType.DMA((3,)),
        ],
        compiler_params=limits(56),
        cost_estimate=cost(0, 0),
    )(prefix_kv, ws, packed)
    beside = swap(payload, slab_axes, plan.slab, 1)
    across = swap(payload, slab_axes, plan.slab, 2)

    block = min(moves, 128)
    vmem = pl.BlockSpec(memory_space=pltpu.VMEM)
    *normed, mark = pl.pallas_call(
        normalize,
        out_shape=[*[shape((moves // 2, width), BF16)] * 2, pltpu.HBM((8, width), BF16)],
        in_specs=[untouched(), vmem, untouched()],
        out_specs=[untouched()] * 3,
        scratch_shapes=[
            pltpu.VMEM((1, width), F32),
            pltpu.VMEM((3, block, width), BF16),
            pltpu.VMEM((3, block, width), BF16),
            pltpu.SemaphoreType.DMA((3,)),
            pltpu.SemaphoreType.DMA((3,)),
        ],
        compiler_params=limits(58),
        cost_estimate=cost(moves * width, moves * width // 4),
    )(move_table, norm_gain.reshape(width // HD, HD), packed)
    turns = turn_table(prefix_len).reshape(line, 1, plan.pairs, 2)
    turns = np.tile(turns, (1, plan.mine, 1, 1)).reshape(line, plan.mine * plan.pairs, 2)
    flat = weights.transpose(1, 0, 2).reshape(plan.rows, width) if depth % HD else weights
    sent = (moves // HD * (plan.q_rows + 2 * plan.mine), HD) if plan.direct else (line, plan.line_rows, moves)
    outs = (shape(sent, BF16), shape((plan.mine, moves), F32))
    across = tied(across, mark)
    diagonal = swap(across, slab_axes, plan.slab, 1)
    filled, listed = (), None
    for step, after in enumerate((across, beside)):
        made = local_call(
            functools.partial(project, plan, step * moves // 2, step == 0),
            place,
            (flat, normed[step], jnp.asarray(turns), after, *filled),
            [*outs, *([shape((plan.share, plan.slots), F32)] if step == 0 else [])],
            (),
            20,
            (3,),
            moves * width * 1024,
            moves * width,
            {5: 0, 6: 1} if filled else None,
        )
        filled, listed = made[:2], made[2] if step == 0 else listed
    queries, own_values = filled
    other = swap(listed, slab_axes, plan.slab, pair)
    if plan.direct:
        queries = [queries] + [swap(queries, "line", line, step) for step in range(1, line)]
    else:
        queries = lax.all_to_all(queries, "line", split_axis=0, concat_axis=0, tiled=True)
        queries = [queries.reshape(line * plan.line_rows, moves)]

    query_rows = plan.mine * HD
    back = plan.peers * lax.axis_size("tensor")
    chosen, folds, slot_row = local_call(
        functools.partial(prepare, plan),
        place,
        (board_row, listed, other, payload, beside, across),
        (
            shape((boards_here, moves, plan.slab * plan.slots), BF16),
            shape((plan.slab - 1, boards_here, prefix_len, plan.mine * plan.slots), F32),
            shape((1, row_count), jnp.int32),
        ),
        mib=20,
        flops=10**9,
        nbytes=10**6,
    )
    parts = local_call(
        functools.partial(attend, plan),
        place,
        (own_values, listed, other, chosen, folds, payload, beside, across, diagonal, *queries),
        shape((groups, back, plan.share, plan.slots), BF16),
        [
            pltpu.VMEM((query_rows + 16, moves), BF16),
            pltpu.VMEM((16, moves), F32),
            pltpu.VMEM((plan.slab, boards_here, plan.slots), F32),
            pltpu.VMEM((query_rows + 16, plan.slab * plan.slots), F32),
            pltpu.VMEM((query_rows + 16, plan.slab * plan.slots), F32),
        ],
        24,
    )
    parts = lax.all_to_all(
        parts.reshape(groups * back, plan.share, plan.slots),
        ("groups", "line", "pair", "tensor"),
        split_axis=0,
        concat_axis=0,
        tiled=True,
    )
    parts = parts.reshape(groups, line, back // line, plan.share, plan.slots)
    logprob = pl.pallas_call(
        functools.partial(finish, plan), out_shape=shape((1, row_count), F32), compiler_params=limits(VMEM_MIB)
    )(parts, board_row, slot_row)
    return logprob.reshape(row_count)


def solution(mesh):
    order = ("groups", "dp", "tensor")
    assert mesh.axis_names == order
    pair = 2
    groups, peers, tensor = (mesh.shape[name] for name in order)
    fine = Mesh(mesh.devices.reshape(groups, peers // pair, pair, tensor), ("groups", "line", "pair", "tensor"))
    rows = ("groups", "line", "pair")
    placed = (
        P(rows, None, "tensor"),
        P(rows),
        P(rows, None),
        P(),
        P(),
        P(("line", "pair"), "tensor"),
        P(("line", "pair"), "tensor"),
        P("tensor"),
    )
    return jax.shard_map(per_device, mesh=fine, in_specs=placed, out_specs=P(rows), check_vma=False)
```

```python
import functools
import math

import jax
import jax.numpy as jnp
import numpy as np
from jax import lax
from jax.experimental import pallas as pl
from jax.experimental.pallas import tpu as pltpu
from jax.sharding import Mesh
from jax.sharding import PartitionSpec as P

HD = 128
HALF = HD // 2
EPS = 1e-06
THETA = 5000000.0
DEAD = -1e30
VMEM_MIB = 52
GROUP, LINE, PEER, SLAB = range(4)

F32 = jnp.float32
BF16 = jnp.bfloat16

NN = (((1,), (0,)), ((), ()))
NT = (((1,), (1,)), ((), ()))
TN = (((0,), (0,)), ((), ()))


def matmul(a, b, dims=NN):
    return lax.dot_general(a, b, dims, preferred_element_type=F32)


def limits(mib):
    return pltpu.CompilerParams(vmem_limit_bytes=mib * 1024 * 1024)


class Plan:
    def __init__(self, groups, line, pair, heads, capacity, share):
        self.groups, self.line, self.pair = groups, line, pair
        self.peers = line * pair
        self.slab = groups * pair
        self.heads = heads
        self.mine = heads // self.slab
        self.pairs = HALF // line
        self.q_rows = self.mine * 2 * self.pairs
        self.k_rows = 2 * self.pairs
        self.fold_at = self.q_rows + self.k_rows
        self.list_at = self.fold_at + self.mine
        self.rows = -(-(self.list_at + 1) // 8) * 8
        self.line_rows = -(-(self.q_rows + 2 * self.mine) // 8) * 8
        self.capacity = capacity
        self.share = share
        self.slots = self.peers * capacity
        self.direct = line <= 4


def pack_weights(plan, place_ref, wq_hbm, wkv_hbm, ws_hbm, board_hbm, ids_hbm, *rest):
    out_ref, wq, wkv, ws_ref, board_ref, ids_ref, pick, sems = rest
    group = place_ref[0]
    half_cols = wq.shape[1]
    columns_here = pl.ds(pl.multiple_of(group * half_cols, HD), half_cols)
    copies = (
        pltpu.make_async_copy(ws_hbm, ws_ref, sems.at[0]),
        pltpu.make_async_copy(board_hbm, board_ref, sems.at[1]),
        pltpu.make_async_copy(ids_hbm, ids_ref, sems.at[2]),
        pltpu.make_async_copy(wq_hbm.at[:, columns_here], wq, sems.at[3]),
        pltpu.make_async_copy(wkv_hbm, wkv, sems.at[4]),
    )
    for copy in copies:
        copy.start()
    for copy in copies[:3]:
        copy.wait()
    count, depth = board_ref.shape[1], wq.shape[0]
    board_row = board_ref[...]
    board_col = jnp.broadcast_to(board_row.astype(F32), (8, count)).T[:, 0:1].astype(jnp.int32)
    own = lax.broadcasted_iota(jnp.int32, (count, count), 0)
    other = lax.broadcasted_iota(jnp.int32, (count, count), 1)
    ahead = jnp.where((board_col == board_row) & (other < own), 1.0, 0.0)
    rank = jnp.sum(ahead, axis=1, keepdims=True).astype(jnp.int32)
    move = ids_ref[...] + 1
    boards, span = plan.line * plan.share, plan.share * plan.capacity
    member = lax.broadcasted_iota(jnp.int32, (boards, count), 0) == board_row
    parts = [jnp.where(member, part.astype(F32), 0.0) for part in (move // 64, move % 64)]
    lane = lax.broadcasted_iota(jnp.int32, (count, depth), 1)
    ranked = jnp.where(rank == (lane % span) % plan.capacity, 1.0, 0.0).astype(BF16)
    found = matmul(jnp.concatenate(parts, axis=0).astype(BF16), ranked)
    lane = lax.broadcasted_iota(jnp.int32, (2 * boards, depth), 1)
    row = lax.broadcasted_iota(jnp.int32, (2 * boards, depth), 0)
    keep = (row // boards == lane // span) & (row % plan.share == (lane % span) // plan.capacity)
    found = jnp.where(keep, found, 0.0)
    lists = []
    for line in range(plan.line):
        at = line * plan.share
        both = found[at : at + plan.share] + found[boards + at : boards + at + plan.share]
        lists.append(jnp.sum(both, axis=0, keepdims=True))

    if plan.pairs % 16 == 0:
        turn_weights(plan, group, lists, copies[3:], wq, wkv, ws_ref, out_ref)
    else:
        pick_weights(plan, group, lists, copies[3:], wq, wkv, ws_ref, out_ref, pick)


def turn_weights(plan, group, lists, copies, wq, wkv, ws_ref, out_ref):
    for copy in copies:
        copy.wait()
    q = wq[...].T
    k = wkv[:, :HD].T
    folds = matmul(ws_ref[...], wkv[:, HD:], NT)
    row = lax.broadcasted_iota(jnp.int32, folds.shape, 0)
    pairs = plan.pairs
    zeros = jnp.zeros((plan.rows - plan.list_at - 1, folds.shape[1]), F32)
    for pair in range(plan.pair):
        first = (group * plan.pair + pair) * plan.mine
        mine = [jnp.sum(jnp.where(row == first + h, folds, 0.0), axis=0, keepdims=True) for h in range(plan.mine)]
        for line in range(plan.line):
            peer = line * plan.pair + pair
            for part in range(2):
                entry = part * HALF + line * pairs
                for h in range(plan.mine):
                    at = (part * plan.mine + h) * pairs
                    source = (pair * plan.mine + h) * HD + entry
                    out_ref[peer, at : at + pairs] = q[source : source + pairs]
                at = plan.q_rows + part * pairs
                out_ref[peer, at : at + pairs] = k[entry : entry + pairs]
            last = jnp.concatenate([*mine, lists[line], zeros], axis=0)
            out_ref[peer, plan.fold_at :] = last.astype(BF16)


def pick_weights(plan, group, lists, copies, wq, wkv, ws_ref, out_ref, pick):
    rows, half_cols = plan.rows, wq.shape[1]
    r = lax.broadcasted_iota(jnp.int32, (rows, 1), 0)
    part = r // (plan.mine * plan.pairs)
    head = (r // plan.pairs) % plan.mine
    entry = r % plan.pairs
    is_q = r < plan.q_rows
    k_at = r - plan.q_rows
    is_k = (k_at >= 0) & (k_at < plan.k_rows)
    f_at = r - plan.fold_at
    is_f = (f_at >= 0) & (f_at < plan.mine)
    q_lane = lax.broadcasted_iota(jnp.int32, (rows, half_cols), 1)
    k_lane = lax.broadcasted_iota(jnp.int32, (rows, HD), 1)
    ws = ws_ref[...].astype(F32)

    def fill(peer, carry):
        line, pair = peer // plan.pair, peer % plan.pair
        column = (pair * plan.mine + head) * HD + part * HALF + line * plan.pairs + entry
        column = jnp.where(is_q, column, -1)
        at = pl.ds(pl.multiple_of(peer * rows, 8), rows)
        pick[at, :half_cols] = jnp.where(q_lane == column, 1.0, 0.0)
        k_column = (k_at // plan.pairs) * HALF + line * plan.pairs + k_at % plan.pairs
        k_column = jnp.where(is_k, k_column, -1)
        pick[at, half_cols : half_cols + HD] = jnp.where(k_lane == k_column, 1.0, 0.0)
        fold = jnp.zeros((rows, HD), F32)
        my_head = jnp.where(is_f, (group * plan.pair + pair) * plan.mine + f_at, -1)
        for h in range(plan.heads):
            fold = jnp.where(my_head == h, ws[h : h + 1], fold)
        pick[at, half_cols + HD :] = fold
        return carry

    lax.fori_loop(0, plan.peers, fill, 0, unroll=plan.peers <= 8)

    for copy in copies:
        copy.wait()
    left = pick[...].astype(BF16)
    total = matmul(left[:, :half_cols], wq[...], NT) + matmul(left[:, half_cols:], wkv[...], NT)
    for peer in range(plan.peers):
        mine = total[peer * rows : (peer + 1) * rows]
        out_ref[peer] = jnp.where(r == plan.list_at, lists[peer // plan.pair], mine).astype(BF16)


def normalize(table_hbm, gain_ref, after_ref, *refs):
    *outs, mark_ref, gain, buffers, made, sems, out_sems = refs
    held, block, _ = buffers.shape
    steps = table_hbm.shape[0] // block
    places = [(out, at) for out in outs for at in range(0, out.shape[0], block)]

    def copy(step):
        source = table_hbm.at[pl.ds(step * block, block)]
        return pltpu.make_async_copy(source, buffers.at[step % held], sems.at[step % held])

    def store(step):
        out, at = places[step]
        return pltpu.make_async_copy(made.at[step % held], out.at[pl.ds(at, block)], out_sems.at[step % held])

    for step in range(min(held, steps)):
        copy(step).start()
    rows = gain_ref[...].astype(F32)
    gain[...] = jnp.concatenate([rows[r : r + 1] for r in range(rows.shape[0])], axis=1)
    for step in range(steps):
        copy(step).wait()
        if step >= held:
            store(step - held).wait()
        raw = buffers[step % held].astype(F32)
        inverse = lax.rsqrt(jnp.mean(raw * raw, axis=-1, keepdims=True) + EPS)
        made[step % held] = (raw * inverse * gain[...]).astype(BF16)
        store(step).start()
        if step + held < steps:
            copy(step + held).start()
    for step in range(max(0, steps - held), steps):
        store(step).wait()
    mark = pltpu.make_async_copy(made.at[0, pl.ds(0, mark_ref.shape[0])], mark_ref, out_sems.at[0])
    mark.start()
    mark.wait()


def read_lists(plan, w_ref, out_ref):
    share, capacity, peers = plan.share, plan.capacity, plan.peers
    span = share * capacity
    if len(w_ref.shape) == 3:
        rows = [w_ref[s].astype(F32)[plan.list_at : plan.list_at + 1] for s in range(peers)]
    else:
        row = w_ref[...].astype(F32)[plan.list_at : plan.list_at + 1]
        rows = [row[:, s * 2 * span : (s + 1) * 2 * span] for s in range(peers)]
    rows = jnp.concatenate(rows, axis=0)
    lane = lax.broadcasted_iota(jnp.int32, (share * peers, 2 * span), 1)
    row = lax.broadcasted_iota(jnp.int32, (share * peers, 2 * span), 0)
    lane = jnp.where(lane < span, lane, lane - span)
    spread = jnp.concatenate([rows] * share, axis=0)
    spread = jnp.where(lane // capacity == row // peers, spread, 0.0).astype(BF16)
    c = lax.broadcasted_iota(jnp.int32, (2 * span, plan.slots), 0)
    slot = lax.broadcasted_iota(jnp.int32, (2 * span, plan.slots), 1)
    scale = jnp.where(c < span, 64.0, 1.0)
    place = jnp.where(c % capacity == slot % capacity, scale, 0.0).astype(BF16)
    listed = matmul(spread, place)
    row = lax.broadcasted_iota(jnp.int32, listed.shape, 0)
    slot = lax.broadcasted_iota(jnp.int32, listed.shape, 1)
    listed = jnp.where(slot // capacity == row % peers, listed, 0.0)
    out_ref[...] = jnp.sum(listed.reshape(share, peers, plan.slots), axis=1)


def project(plan, place, lists, place_ref, w_ref, normed_ref, turn_ref, after_ref, *refs):
    if lists:
        q_ref, vo_ref, tail_ref, list_ref = refs
        read_lists(plan, w_ref, list_ref)
    else:
        tail_ref, q_ref, vo_ref = refs[0], *refs[-2:]
    turns = turn_ref[place_ref[LINE]]
    half, k_half = plan.q_rows // 2, plan.k_rows // 2
    cosine, sine = turns[:, 0:1], turns[:, 1:2]
    cos_k, sin_k = cosine[:k_half], sine[:k_half]
    moves = normed_ref.shape[0]
    block = min(moves, HD)
    every = []
    for start in range(0, moves, block):
        at, to = slice(start, start + block), slice(place + start, place + start + block)
        if len(w_ref.shape) == 3:
            depth = w_ref.shape[2]
            total = None
            for s in range(w_ref.shape[0]):
                term = matmul(w_ref[s], normed_ref[at, s * depth : (s + 1) * depth], NT)
                total = term if total is None else total + term
        else:
            total = matmul(w_ref[...], normed_ref[at, :], NT)
        first, second = total[:half], total[half : 2 * half]
        f_first = (first * cosine - second * sine).astype(BF16).astype(F32)
        f_second = (second * cosine + first * sine).astype(BF16).astype(F32)
        first, second = total[plan.q_rows : plan.q_rows + k_half], total[plan.q_rows + k_half : plan.fold_at]
        k_first = (first * cos_k - second * sin_k).astype(BF16).astype(F32)
        k_second = (second * cos_k + first * sin_k).astype(BF16).astype(F32)
        logits, tails = [], []
        for h in range(plan.mine):
            own = slice(h * k_half, (h + 1) * k_half)
            logit = jnp.sum(f_first[own] * k_first + f_second[own] * k_second, axis=0, keepdims=True)
            logits.append(logit.astype(BF16).astype(F32))
            tails.append(logit - logits[-1])
        if plan.direct:
            chunk = (place + start) // block * plan.q_rows
            q_ref[chunk : chunk + plan.q_rows] = jnp.concatenate([f_first, f_second], axis=0).astype(BF16)
            every += [*logits, *tails]
        else:
            pad = plan.line_rows - plan.q_rows - 2 * plan.mine
            pieces = [f_first, f_second, *logits, *tails]
            if pad:
                pieces.append(jnp.zeros((pad, block), F32))
            out = jnp.concatenate(pieces, axis=0).astype(BF16)
            for line in range(plan.line):
                q_ref[line, :, to] = out
        vo_ref[:, to] = total[plan.fold_at : plan.list_at]
    if plan.direct and lists:
        tail_ref[: len(every)] = jnp.concatenate(every, axis=0)
    elif plan.direct:
        before = place // block * 2 * plan.mine
        last = q_ref.shape[0] - before - len(every)
        q_ref[last:] = jnp.concatenate([tail_ref[:before], *every], axis=0).astype(BF16)


def tied(x, *others):
    return pl.pallas_call(
        lambda *refs: None,
        out_shape=shape(x.shape, x.dtype),
        in_specs=[untouched()] + [pl.BlockSpec(memory_space=pltpu.HBM)] * len(others),
        out_specs=untouched(),
        input_output_aliases={0: 0},
        compiler_params=limits(1),
        cost_estimate=cost(0, 0),
    )(x, *others)


def pack_prefix(plan, prefix_hbm, ws_hbm, after_ref, out_ref, *scratch):
    values, ws_ref, sems = scratch
    boards = values.shape[0]
    heads = plan.heads
    copies = (
        pltpu.make_async_copy(ws_hbm, ws_ref, sems.at[0]),
        pltpu.make_async_copy(prefix_hbm.at[:, :, pl.ds(HD, HD)], values, sems.at[1]),
        pltpu.make_async_copy(prefix_hbm.at[:, :, pl.ds(0, HD)], out_ref.at[pl.ds(0, boards)], sems.at[2]),
    )
    for copy in copies:
        copy.start()
    copies[0].wait()
    span = HD // boards
    ws = jnp.concatenate([ws_ref[...].astype(F32)] * (HD // heads), axis=0)
    row = lax.broadcasted_iota(jnp.int32, (HD, 1), 0)
    copies[1].wait()
    fold = None
    for board in range(boards):
        keep = (row // span == board) & (row % span < 2 * heads)
        term = matmul(values[board], jnp.where(keep, ws, 0.0).astype(BF16), NT)
        fold = term if fold is None else fold + term
    rounded = fold.astype(BF16).astype(F32)
    lane = lax.broadcasted_iota(jnp.int32, fold.shape, 1)
    out_ref[boards] = jnp.where(lane % span < heads, rounded, fold - rounded).astype(BF16)
    copies[2].wait()


def fold_columns(plan, here, block, board, boards, heads):
    lanes = plan.mine * plan.slots
    row = lax.broadcasted_iota(jnp.int32, (HD, lanes), 0) - board * (HD // boards)
    head = here * plan.mine + lax.broadcasted_iota(jnp.int32, (HD, lanes), 1) // plan.slots
    pick = jnp.where((row == head) | (row == head + heads), 1.0, 0.0).astype(BF16)
    return matmul(block, pick)


def choose(plan, here, list_ref, chosen_ref):
    boards, moves = chosen_ref.shape[0], chosen_ref.shape[1]
    move_at = lax.broadcasted_iota(jnp.int32, (moves, plan.slots), 0) + 1

    def step(board, carry):
        for j in range(plan.pair):
            place = ((here ^ j) % plan.pair) * boards + board
            row = list_ref[pl.ds(place, 1), :].astype(jnp.int32)
            at = slice(j * plan.slots, (j + 1) * plan.slots)
            chosen_ref[board, :, at] = jnp.where(move_at == row, 1.0, 0.0).astype(BF16)
        return carry

    lax.fori_loop(0, boards, step, 0)


def prepare(plan, place_ref, board_ref, own_ref, *rest):
    *prefix_refs, chosen_ref, fold_ref, slot_ref = rest
    count = board_ref.shape[1]
    board_row = board_ref[...]
    board_col = jnp.broadcast_to(board_row.astype(F32), (8, count)).T[:, 0:1].astype(jnp.int32)
    ahead = lax.broadcasted_iota(jnp.int32, (count, count), 0) < lax.broadcasted_iota(jnp.int32, (count, count), 1)
    rank = jnp.sum(jnp.where((board_col == board_row) & ahead, 1.0, 0.0), axis=0, keepdims=True)
    slot_ref[...] = rank.astype(jnp.int32) + place_ref[PEER] * plan.capacity
    here = place_ref[SLAB]
    boards = fold_ref.shape[1]
    choose(plan, here, own_ref, chosen_ref)

    def step(board, carry):
        for j, prefix_ref in enumerate(prefix_refs):
            fold_ref[j, board] = fold_columns(plan, here, prefix_ref[boards], board, boards, plan.heads)
        return carry

    lax.fori_loop(0, boards, step, 0)


def prepare_other(plan, place_ref, other_ref, chosen_ref):
    choose(plan, place_ref[SLAB], other_ref, chosen_ref)


def attend(plan, place_ref, vo_ref, own_ref, other_ref, own_choice, other_choice, fold_ref, *rest):
    prefix_refs, rest = rest[: plan.slab], rest[plan.slab :]
    *q_refs, out_ref, table, extra, scores, taken_even, taken_odd = rest
    here = place_ref[SLAB]
    mine, heads, slots = plan.mine, plan.heads, plan.slots
    moves = vo_ref.shape[1]
    boards = prefix_refs[0].shape[0] - 1
    query_rows = mine * HD

    mixed = own_logits = None
    for step, q_ref in enumerate(q_refs):
        if plan.direct:
            chunks = range(moves // HD)
            values = jnp.concatenate([q_ref[c * plan.q_rows : (c + 1) * plan.q_rows] for c in chunks], axis=1)
            tails = q_ref[moves // HD * plan.q_rows :].astype(F32)
            tails = jnp.concatenate([tails[c * 2 * mine : (c + 1) * 2 * mine] for c in chunks], axis=1)
            tails = tails[:mine] + tails[mine:]
            own_logits = tails if own_logits is None else own_logits + tails
        else:
            values = q_ref[...]
        r = lax.broadcasted_iota(jnp.int32, (query_rows + 8, values.shape[0]), 0)
        c = lax.broadcasted_iota(jnp.int32, (query_rows + 8, values.shape[0]), 1)
        line, at = (place_ref[LINE] ^ step, c) if plan.direct else (c // plan.line_rows, c % plan.line_rows)
        part, head, entry = at // (mine * plan.pairs), (at // plan.pairs) % mine, at % plan.pairs
        goes = jnp.where(at < plan.q_rows, head * HD + part * HALF + line * plan.pairs + entry, -1)
        tail = at - plan.q_rows
        goes = jnp.where((tail >= 0) & (tail < 2 * mine), query_rows + tail % mine, goes)
        term = matmul(jnp.where(r == goes, 1.0, 0.0).astype(BF16), values)
        mixed = term if mixed is None else mixed + term
    if own_logits is None:
        own_logits = mixed[query_rows : query_rows + mine]
    table[:query_rows] = mixed[:query_rows].astype(BF16)
    extra[...] = jnp.zeros_like(extra)
    for place, value in ((0, own_logits), (2 * mine, vo_ref[...])):
        rounded = value.astype(BF16).astype(F32)
        extra[place : place + mine] = rounded
        extra[place + mine : place + 2 * mine] = value - rounded
    table[query_rows:] = extra[...].astype(BF16)

    scale = math.log2(math.e) / math.sqrt(HD)
    def per_head(x, base):
        pieces = [x[base + h : base + h + 1] + x[base + mine + h : base + mine + h + 1] for h in range(mine)]
        return jnp.concatenate(pieces, axis=1)

    def moves_of(j, board):
        place = ((here ^ j) % plan.pair) * boards + board
        return (own_ref, other_ref)[j // plan.pair][pl.ds(place, 1), :].astype(jnp.int32)

    def gather(board, taken):
        taken[...] = matmul(table[...], jnp.concatenate([own_choice[board], other_choice[board]], axis=1))

    def score_board(board, taken):
        for j in range(plan.slab):
            x = taken[:, j * slots : (j + 1) * slots]
            q = jnp.concatenate([x[h * HD : (h + 1) * HD].astype(BF16) for h in range(mine)], axis=1)
            logits = matmul(prefix_refs[j][board], q)
            if j < plan.slab - 1:
                fold = fold_ref[j, board]
            else:
                fold = fold_columns(plan, here, prefix_refs[j][boards], board, boards, heads)
            own_logit = per_head(x, query_rows)
            own_value = per_head(x, query_rows + 2 * mine)
            peak = jnp.maximum(jnp.max(logits, axis=0, keepdims=True), own_logit)
            weight = jnp.exp2((logits - peak) * scale)
            own_weight = jnp.exp2((own_logit - peak) * scale)
            denom = jnp.sum(weight, axis=0, keepdims=True) + own_weight
            value = (jnp.sum(weight * fold, axis=0, keepdims=True) + own_value * own_weight) / denom
            score = sum(value[:, h * slots : (h + 1) * slots] for h in range(mine))
            scores[here ^ j, pl.ds(board, 1), :] = jnp.where(moves_of(j, board) > 0, score, DEAD)

    gather(0, taken_even)

    def step(at, carry):
        board = 2 * at
        gather(jnp.minimum(board + 1, boards - 1), taken_odd)
        score_board(board, taken_even)
        gather(jnp.minimum(board + 2, boards - 1), taken_even)
        score_board(jnp.minimum(board + 1, boards - 1), taken_odd)
        return carry

    lax.fori_loop(0, -(-boards // 2), step, 0)
    live = scores[...] > 0.5 * DEAD
    count = jnp.sum(jnp.where(live, 1.0, 0.0), axis=2, keepdims=True)
    mean = jnp.sum(jnp.where(live, scores[...], 0.0), axis=2, keepdims=True) / jnp.maximum(count, 1.0)
    centered = jnp.where(live, scores[...] - mean, DEAD)
    for g in range(plan.groups):
        both = jnp.concatenate([centered[g * plan.pair + p] for p in range(plan.pair)], axis=0).astype(BF16)
        for copy in range(out_ref.shape[1]):
            out_ref[g, copy] = both


def finish(plan, parts_ref, board_ref, slot_ref, out_ref):
    line = parts_ref.shape[1]
    columns = []
    for at in range(line):
        total = None
        for g in range(parts_ref.shape[0]):
            for p in range(parts_ref.shape[2]):
                term = parts_ref[g, at, p].astype(F32)
                total = term if total is None else total + term
        columns.append(total)
    scores = jnp.concatenate(columns, axis=0)
    live = scores > 0.5 * DEAD
    peak = jnp.max(scores, axis=1, keepdims=True)
    denom = jnp.sum(jnp.where(live, jnp.exp(scores - peak), 0.0), axis=1, keepdims=True)
    logprob = jnp.where(live, scores - peak - jnp.log(denom), 0.0)
    count = board_ref.shape[1]
    member = lax.broadcasted_iota(jnp.int32, (scores.shape[0], count), 0) == board_ref[...]
    member = jnp.where(member, 1.0, 0.0).astype(BF16)
    found = jnp.zeros((plan.slots, count), F32)
    for _ in range(3):
        rounded = logprob.astype(BF16)
        found = found + matmul(rounded, member, TN)
        logprob = logprob - rounded.astype(F32)
    at = lax.broadcasted_iota(jnp.int32, (plan.slots, count), 0) == slot_ref[...]
    out_ref[...] = jnp.sum(jnp.where(at, found, 0.0), axis=0, keepdims=True)


def untouched():
    return pl.BlockSpec(memory_space=pl.ANY)


def local_call(kernel, place, args, outs, scratch=(), mib=40, copied=(), flops=0, nbytes=0, aliases=None):
    vmem = pl.BlockSpec(memory_space=pltpu.VMEM)
    return pl.pallas_call(
        kernel,
        out_shape=outs,
        in_specs=[pl.BlockSpec(memory_space=pltpu.SMEM)]
        + [untouched() if at in copied else vmem for at in range(len(args))],
        out_specs=jax.tree.map(lambda x: vmem, outs),
        scratch_shapes=scratch,
        input_output_aliases=aliases or {},
        compiler_params=limits(mib),
        cost_estimate=cost(flops, nbytes),
    )(place, *args)


def cost(flops, nbytes):
    return pl.CostEstimate(flops=int(flops), bytes_accessed=int(nbytes), transcendentals=0)


def swap(x, names, size, step):
    return lax.ppermute(x, names, [(at, at ^ step) for at in range(size)])


def shape(dims, dtype):
    return jax.ShapeDtypeStruct(tuple(dims), dtype)


def turn_table(position):
    frequency = THETA ** (-2.0 * np.arange(HALF, dtype=np.float32) / HD)
    angles = np.float32(position) * frequency.astype(np.float32)
    return np.stack([np.cos(angles), np.sin(angles)], axis=1).astype(np.float32)


def per_device(prefix_kv, move_ids, move_board, move_table, norm_gain, w_query, w_keyval, w_score):
    row_count = move_ids.shape[0]
    boards_here, prefix_len, _ = prefix_kv.shape
    moves, width = move_table.shape
    groups, line, pair = lax.axis_size("groups"), lax.axis_size("line"), lax.axis_size("pair")
    board_total = boards_here * line * pair
    capacity = max(2, (2 * row_count + board_total - 1) // board_total)
    heads = w_query.shape[1] // HD
    plan = Plan(groups, line, pair, heads, capacity, pair * boards_here)
    depth = w_query.shape[0]
    group_at = lax.axis_index("groups").astype(jnp.int32)
    line_at = lax.axis_index("line").astype(jnp.int32)
    pair_at = lax.axis_index("pair").astype(jnp.int32)
    place = jnp.stack([group_at, line_at, line_at * pair + pair_at, group_at * pair + pair_at])
    ws = w_score.reshape(heads, HD)
    slab_axes = ("groups", "pair")
    board_row = move_board.reshape(1, row_count)

    half_cols = w_query.shape[1] // groups
    packed = local_call(
        functools.partial(pack_weights, plan),
        group_at.reshape(1),
        (w_query, w_keyval, ws, board_row, move_ids.reshape(1, row_count)),
        shape((plan.peers, plan.rows, depth), BF16),
        [
            pltpu.VMEM((depth, half_cols), BF16),
            pltpu.VMEM((depth, 2 * HD), BF16),
            pltpu.VMEM((heads, HD), BF16),
            pltpu.VMEM((1, row_count), jnp.int32),
            pltpu.VMEM((1, row_count), jnp.int32),
            pltpu.VMEM((plan.peers * plan.rows, half_cols + 2 * HD), F32),
            pltpu.SemaphoreType.DMA((5,)),
        ],
        62,
        range(5),
    )
    weights = lax.all_to_all(packed, ("line", "pair"), split_axis=0, concat_axis=0, tiled=True)

    payload = pl.pallas_call(
        functools.partial(pack_prefix, plan),
        out_shape=shape((boards_here + 1, prefix_len, HD), BF16),
        in_specs=[untouched()] * 3,
        out_specs=pl.BlockSpec(memory_space=pltpu.VMEM),
        scratch_shapes=[
            pltpu.VMEM((boards_here, prefix_len, HD), BF16),
            pltpu.VMEM((heads, HD), BF16),
            pltpu.SemaphoreType.DMA((3,)),
        ],
        compiler_params=limits(56),
        cost_estimate=cost(0, 0),
    )(prefix_kv, ws, packed)
    beside = swap(payload, slab_axes, plan.slab, 1)
    across = swap(payload, slab_axes, plan.slab, 2)

    block = min(moves, 128)
    blocks = (moves * 3 // 8, moves * 5 // 8)
    vmem = pl.BlockSpec(memory_space=pltpu.VMEM)
    *normed, mark = pl.pallas_call(
        normalize,
        out_shape=[*[shape((size, width), BF16) for size in blocks], pltpu.HBM((8, width), BF16)],
        in_specs=[untouched(), vmem, untouched()],
        out_specs=[untouched()] * 3,
        scratch_shapes=[
            pltpu.VMEM((1, width), F32),
            pltpu.VMEM((3, block, width), BF16),
            pltpu.VMEM((3, block, width), BF16),
            pltpu.SemaphoreType.DMA((3,)),
            pltpu.SemaphoreType.DMA((3,)),
        ],
        compiler_params=limits(58),
        cost_estimate=cost(moves * width, moves * width // 4),
    )(move_table, norm_gain.reshape(width // HD, HD), packed)
    turns = turn_table(prefix_len).reshape(line, 1, plan.pairs, 2)
    turns = np.tile(turns, (1, plan.mine, 1, 1)).reshape(line, plan.mine * plan.pairs, 2)
    flat = weights.transpose(1, 0, 2).reshape(plan.rows, width) if depth % HD else weights
    sent = (moves // HD * (plan.q_rows + 2 * plan.mine), HD) if plan.direct else (line, plan.line_rows, moves)
    outs = (shape(sent, BF16), shape((plan.mine, moves), F32))
    across = tied(across, mark)
    diagonal = swap(across, slab_axes, plan.slab, 1)
    queries, own_values, tails, listed = local_call(
        functools.partial(project, plan, 0, True),
        place,
        (flat, normed[0], jnp.asarray(turns), across),
        (*outs, shape((-(-blocks[0] // HD * 2 * plan.mine // 8) * 8, HD), F32), shape((plan.share, plan.slots), F32)),
        (),
        20,
        (3,),
        blocks[0] * width * 2048,
        blocks[0] * width,
    )
    queries, own_values = local_call(
        functools.partial(project, plan, blocks[0], False),
        place,
        (flat, normed[1], jnp.asarray(turns), beside, tails, queries, own_values),
        outs,
        (),
        20,
        (3,),
        blocks[1] * width * 2048,
        blocks[1] * width,
        {6: 0, 7: 1},
    )
    other = swap(listed, slab_axes, plan.slab, pair)
    if plan.direct:
        queries = [queries] + [swap(queries, "line", line, step) for step in range(1, line)]
    else:
        queries = lax.all_to_all(queries, "line", split_axis=0, concat_axis=0, tiled=True)
        queries = [queries.reshape(line * plan.line_rows, moves)]

    query_rows = plan.mine * HD
    back = plan.peers * lax.axis_size("tensor")
    choice = shape((boards_here, moves, pair * plan.slots), BF16)
    own_choice, folds, slot_row = local_call(
        functools.partial(prepare, plan),
        place,
        (board_row, listed, payload, beside, across),
        (
            choice,
            shape((plan.slab - 1, boards_here, prefix_len, plan.mine * plan.slots), F32),
            shape((1, row_count), jnp.int32),
        ),
        mib=20,
        flops=10**9,
        nbytes=10**6,
    )
    other_choice = local_call(
        functools.partial(prepare_other, plan), place, (other,), choice, mib=20, flops=10**9, nbytes=10**6
    )
    parts = local_call(
        functools.partial(attend, plan),
        place,
        (own_values, listed, other, own_choice, other_choice, folds, payload, beside, across, diagonal, *queries),
        shape((groups, back, plan.share, plan.slots), BF16),
        [
            pltpu.VMEM((query_rows + 16, moves), BF16),
            pltpu.VMEM((16, moves), F32),
            pltpu.VMEM((plan.slab, boards_here, plan.slots), F32),
            pltpu.VMEM((query_rows + 16, plan.slab * plan.slots), F32),
            pltpu.VMEM((query_rows + 16, plan.slab * plan.slots), F32),
        ],
        24,
    )
    parts = lax.all_to_all(
        parts.reshape(groups * back, plan.share, plan.slots),
        ("groups", "line", "pair", "tensor"),
        split_axis=0,
        concat_axis=0,
        tiled=True,
    )
    parts = parts.reshape(groups, line, back // line, plan.share, plan.slots)
    logprob = pl.pallas_call(
        functools.partial(finish, plan), out_shape=shape((1, row_count), F32), compiler_params=limits(VMEM_MIB)
    )(parts, board_row, slot_row)
    return logprob.reshape(row_count)


def solution(mesh):
    order = ("groups", "dp", "tensor")
    assert mesh.axis_names == order
    pair = 2
    groups, peers, tensor = (mesh.shape[name] for name in order)
    fine = Mesh(mesh.devices.reshape(groups, peers // pair, pair, tensor), ("groups", "line", "pair", "tensor"))
    rows = ("groups", "line", "pair")
    placed = (
        P(rows, None, "tensor"),
        P(rows),
        P(rows, None),
        P(),
        P(),
        P(("line", "pair"), "tensor"),
        P(("line", "pair"), "tensor"),
        P("tensor"),
    )
    return jax.shard_map(per_device, mesh=fine, in_specs=placed, out_specs=P(rows), check_vma=False)
```

```python
import functools
import math

import jax
import jax.numpy as jnp
import numpy as np
from jax import lax
from jax.experimental import pallas as pl
from jax.experimental.pallas import tpu as pltpu
from jax.sharding import Mesh
from jax.sharding import PartitionSpec as P

HD = 128
HALF = HD // 2
EPS = 1e-06
THETA = 5000000.0
DEAD = -1e30
VMEM_MIB = 52
GROUP, LINE, PEER, SLAB = range(4)

F32 = jnp.float32
BF16 = jnp.bfloat16

NN = (((1,), (0,)), ((), ()))
NT = (((1,), (1,)), ((), ()))
TN = (((0,), (0,)), ((), ()))


def matmul(a, b, dims=NN):
    return lax.dot_general(a, b, dims, preferred_element_type=F32)


def limits(mib):
    return pltpu.CompilerParams(vmem_limit_bytes=mib * 1024 * 1024)


class Plan:
    def __init__(self, groups, line, pair, heads, capacity, share, depth):
        self.groups, self.line, self.pair = groups, line, pair
        self.peers = line * pair
        self.slab = groups * pair
        self.heads = heads
        self.mine = heads // self.slab
        self.pairs = HALF // line
        self.q_rows = self.mine * 2 * self.pairs
        self.k_rows = 2 * self.pairs
        self.fold_at = self.q_rows + self.k_rows
        self.list_at = self.fold_at + self.mine
        self.rows = -(-(self.list_at + 1) // 8) * 8
        self.line_rows = -(-(self.q_rows + 2 * self.mine) // 8) * 8
        self.capacity = capacity
        self.share = share
        self.slots = self.peers * capacity
        self.direct = line <= 4
        self.tight = self.pairs % 16 == 0 and depth % HD == 0
        self.chunks = depth // HD
        last = -(-(self.mine + 1) * self.chunks // 16) * 16
        self.sent = (self.fold_at * self.chunks + last, HD) if self.tight else (self.rows, depth)


def pack_weights(plan, place_ref, wq_hbm, wkv_hbm, ws_hbm, board_hbm, ids_hbm, *rest):
    out_ref, wq, wkv, ws_ref, board_ref, ids_ref, pick, sems = rest
    group = place_ref[0]
    half_cols = wq.shape[1]
    columns_here = pl.ds(pl.multiple_of(group * half_cols, HD), half_cols)
    copies = (
        pltpu.make_async_copy(ws_hbm, ws_ref, sems.at[0]),
        pltpu.make_async_copy(board_hbm, board_ref, sems.at[1]),
        pltpu.make_async_copy(ids_hbm, ids_ref, sems.at[2]),
        pltpu.make_async_copy(wq_hbm.at[:, columns_here], wq, sems.at[3]),
        pltpu.make_async_copy(wkv_hbm, wkv, sems.at[4]),
    )
    for copy in copies:
        copy.start()
    for copy in copies[:3]:
        copy.wait()
    count, depth = board_ref.shape[1], wq.shape[0]
    board_row = board_ref[...]
    board_col = jnp.broadcast_to(board_row.astype(F32), (8, count)).T[:, 0:1].astype(jnp.int32)
    own = lax.broadcasted_iota(jnp.int32, (count, count), 0)
    other = lax.broadcasted_iota(jnp.int32, (count, count), 1)
    ahead = jnp.where((board_col == board_row) & (other < own), 1.0, 0.0)
    rank = jnp.sum(ahead, axis=1, keepdims=True).astype(jnp.int32)
    move = ids_ref[...] + 1
    boards, span = plan.line * plan.share, plan.share * plan.capacity
    member = lax.broadcasted_iota(jnp.int32, (boards, count), 0) == board_row
    parts = [jnp.where(member, part.astype(F32), 0.0) for part in (move // 64, move % 64)]
    lane = lax.broadcasted_iota(jnp.int32, (count, depth), 1)
    ranked = jnp.where(rank == (lane % span) % plan.capacity, 1.0, 0.0).astype(BF16)
    found = matmul(jnp.concatenate(parts, axis=0).astype(BF16), ranked)
    lane = lax.broadcasted_iota(jnp.int32, (2 * boards, depth), 1)
    row = lax.broadcasted_iota(jnp.int32, (2 * boards, depth), 0)
    keep = (row // boards == lane // span) & (row % plan.share == (lane % span) // plan.capacity)
    found = jnp.where(keep, found, 0.0)
    lists = []
    for line in range(plan.line):
        at = line * plan.share
        both = found[at : at + plan.share] + found[boards + at : boards + at + plan.share]
        lists.append(jnp.sum(both, axis=0, keepdims=True))

    if plan.tight:
        turn_weights(plan, group, lists, copies[3:], wq, wkv, ws_ref, out_ref)
    else:
        pick_weights(plan, group, lists, copies[3:], wq, wkv, ws_ref, out_ref, pick)


def turn_weights(plan, group, lists, copies, wq, wkv, ws_ref, out_ref):
    for copy in copies:
        copy.wait()
    q = wq[...].T
    k = wkv[:, :HD].T
    folds = matmul(ws_ref[...], wkv[:, HD:], NT)
    row = lax.broadcasted_iota(jnp.int32, folds.shape, 0)
    pairs = plan.pairs
    lanes = [slice(c * HD, (c + 1) * HD) for c in range(plan.chunks)]
    first_last = plan.fold_at * plan.chunks
    zeros = jnp.zeros((plan.sent[0] - first_last - (plan.mine + 1) * plan.chunks, HD), F32)
    for pair in range(plan.pair):
        first = (group * plan.pair + pair) * plan.mine
        mine = [jnp.sum(jnp.where(row == first + h, folds, 0.0), axis=0, keepdims=True) for h in range(plan.mine)]
        for line in range(plan.line):
            peer = line * plan.pair + pair
            for c, lane in enumerate(lanes):
                for part in range(2):
                    entry = part * HALF + line * pairs
                    for h in range(plan.mine):
                        at = c * plan.fold_at + (part * plan.mine + h) * pairs
                        source = (pair * plan.mine + h) * HD + entry
                        out_ref[peer, at : at + pairs] = q[source : source + pairs, lane]
                    at = c * plan.fold_at + plan.q_rows + part * pairs
                    out_ref[peer, at : at + pairs] = k[entry : entry + pairs, lane]
            last = [values[:, lane] for values in (*mine, lists[line]) for lane in lanes]
            out_ref[peer, first_last:] = jnp.concatenate([*last, zeros], axis=0).astype(BF16)


def pick_weights(plan, group, lists, copies, wq, wkv, ws_ref, out_ref, pick):
    rows, half_cols = plan.rows, wq.shape[1]
    r = lax.broadcasted_iota(jnp.int32, (rows, 1), 0)
    part = r // (plan.mine * plan.pairs)
    head = (r // plan.pairs) % plan.mine
    entry = r % plan.pairs
    is_q = r < plan.q_rows
    k_at = r - plan.q_rows
    is_k = (k_at >= 0) & (k_at < plan.k_rows)
    f_at = r - plan.fold_at
    is_f = (f_at >= 0) & (f_at < plan.mine)
    q_lane = lax.broadcasted_iota(jnp.int32, (rows, half_cols), 1)
    k_lane = lax.broadcasted_iota(jnp.int32, (rows, HD), 1)
    ws = ws_ref[...].astype(F32)

    def fill(peer, carry):
        line, pair = peer // plan.pair, peer % plan.pair
        column = (pair * plan.mine + head) * HD + part * HALF + line * plan.pairs + entry
        column = jnp.where(is_q, column, -1)
        at = pl.ds(pl.multiple_of(peer * rows, 8), rows)
        pick[at, :half_cols] = jnp.where(q_lane == column, 1.0, 0.0)
        k_column = (k_at // plan.pairs) * HALF + line * plan.pairs + k_at % plan.pairs
        k_column = jnp.where(is_k, k_column, -1)
        pick[at, half_cols : half_cols + HD] = jnp.where(k_lane == k_column, 1.0, 0.0)
        fold = jnp.zeros((rows, HD), F32)
        my_head = jnp.where(is_f, (group * plan.pair + pair) * plan.mine + f_at, -1)
        for h in range(plan.heads):
            fold = jnp.where(my_head == h, ws[h : h + 1], fold)
        pick[at, half_cols + HD :] = fold
        return carry

    lax.fori_loop(0, plan.peers, fill, 0, unroll=plan.peers <= 8)

    for copy in copies:
        copy.wait()
    left = pick[...].astype(BF16)
    total = matmul(left[:, :half_cols], wq[...], NT) + matmul(left[:, half_cols:], wkv[...], NT)
    for peer in range(plan.peers):
        mine = total[peer * rows : (peer + 1) * rows]
        out_ref[peer] = jnp.where(r == plan.list_at, lists[peer // plan.pair], mine).astype(BF16)


def normalize(table_hbm, gain_ref, after_ref, *refs):
    *outs, mark_ref, gain, buffers, made, sems, out_sems = refs
    held, block, _ = buffers.shape
    steps = table_hbm.shape[0] // block
    each = outs[0].shape[0] // block

    def copy(step):
        source = table_hbm.at[pl.ds(step * block, block)]
        return pltpu.make_async_copy(source, buffers.at[step % held], sems.at[step % held])

    def store(step):
        target = outs[step // each].at[pl.ds(step % each * block, block)]
        return pltpu.make_async_copy(made.at[step % held], target, out_sems.at[step % held])

    for step in range(min(held, steps)):
        copy(step).start()
    rows = gain_ref[...].astype(F32)
    gain[...] = jnp.concatenate([rows[r : r + 1] for r in range(rows.shape[0])], axis=1)
    for step in range(steps):
        copy(step).wait()
        if step >= held:
            store(step - held).wait()
        raw = buffers[step % held].astype(F32)
        inverse = lax.rsqrt(jnp.mean(raw * raw, axis=-1, keepdims=True) + EPS)
        made[step % held] = (raw * inverse * gain[...]).astype(BF16)
        store(step).start()
        if step + held < steps:
            copy(step + held).start()
    for step in range(max(0, steps - held), steps):
        store(step).wait()
    mark = pltpu.make_async_copy(made.at[0, pl.ds(0, mark_ref.shape[0])], mark_ref, out_sems.at[0])
    mark.start()
    mark.wait()


def spread_weights(plan, w_ref, full_ref):
    lists = []
    for s in range(plan.peers):
        for c in range(plan.chunks):
            rows = w_ref[s, c * plan.fold_at : (c + 1) * plan.fold_at]
            full_ref[s, : plan.fold_at, c * HD : (c + 1) * HD] = rows
        last = w_ref[s, plan.fold_at * plan.chunks :].astype(F32)
        last = [
            jnp.concatenate([last[i * plan.chunks + c : i * plan.chunks + c + 1] for c in range(plan.chunks)], axis=1)
            for i in range(plan.mine + 1)
        ]
        zeros = jnp.zeros((plan.rows - plan.list_at, last[0].shape[1]), F32)
        full_ref[s, plan.fold_at :] = jnp.concatenate([*last[: plan.mine], zeros], axis=0).astype(BF16)
        lists.append(last[plan.mine])
    return jnp.concatenate(lists, axis=0)


def list_rows(plan, w_ref):
    if len(w_ref.shape) == 3:
        rows = [w_ref[s].astype(F32)[plan.list_at : plan.list_at + 1] for s in range(plan.peers)]
    else:
        row = w_ref[...].astype(F32)[plan.list_at : plan.list_at + 1]
        span = plan.share * plan.capacity
        rows = [row[:, s * 2 * span : (s + 1) * 2 * span] for s in range(plan.peers)]
    return jnp.concatenate(rows, axis=0)


def read_lists(plan, rows, out_ref):
    share, capacity, peers = plan.share, plan.capacity, plan.peers
    span = share * capacity
    lane = lax.broadcasted_iota(jnp.int32, (share * peers, 2 * span), 1)
    row = lax.broadcasted_iota(jnp.int32, (share * peers, 2 * span), 0)
    lane = jnp.where(lane < span, lane, lane - span)
    spread = jnp.concatenate([rows] * share, axis=0)
    spread = jnp.where(lane // capacity == row // peers, spread, 0.0).astype(BF16)
    c = lax.broadcasted_iota(jnp.int32, (2 * span, plan.slots), 0)
    slot = lax.broadcasted_iota(jnp.int32, (2 * span, plan.slots), 1)
    scale = jnp.where(c < span, 64.0, 1.0)
    place = jnp.where(c % capacity == slot % capacity, scale, 0.0).astype(BF16)
    listed = matmul(spread, place)
    row = lax.broadcasted_iota(jnp.int32, listed.shape, 0)
    slot = lax.broadcasted_iota(jnp.int32, listed.shape, 1)
    listed = jnp.where(slot // capacity == row % peers, listed, 0.0)
    out_ref[...] = jnp.sum(listed.reshape(share, peers, plan.slots), axis=1)


def project(plan, place, lists, place_ref, w_ref, normed_ref, turn_ref, after_ref, *refs):
    if lists:
        *refs, list_ref, full_ref = refs
        if plan.tight:
            rows = spread_weights(plan, w_ref, full_ref)
            w_ref = full_ref
        else:
            rows = list_rows(plan, w_ref)
            full_ref[...] = w_ref[...]
        read_lists(plan, rows, list_ref)
    q_ref, vo_ref = refs[-2:]
    turns = turn_ref[place_ref[LINE]]
    half, k_half = plan.q_rows // 2, plan.k_rows // 2
    cosine, sine = turns[:, 0:1], turns[:, 1:2]
    cos_k, sin_k = cosine[:k_half], sine[:k_half]
    moves = normed_ref.shape[0]
    block = min(moves, HD)
    every = []
    for start in range(0, moves, block):
        at, to = slice(start, start + block), slice(place + start, place + start + block)
        if len(w_ref.shape) == 3:
            depth = w_ref.shape[2]
            total = None
            for s in range(w_ref.shape[0]):
                term = matmul(w_ref[s], normed_ref[at, s * depth : (s + 1) * depth], NT)
                total = term if total is None else total + term
        else:
            total = matmul(w_ref[...], normed_ref[at, :], NT)
        first, second = total[:half], total[half : 2 * half]
        f_first = (first * cosine - second * sine).astype(BF16).astype(F32)
        f_second = (second * cosine + first * sine).astype(BF16).astype(F32)
        first, second = total[plan.q_rows : plan.q_rows + k_half], total[plan.q_rows + k_half : plan.fold_at]
        k_first = (first * cos_k - second * sin_k).astype(BF16).astype(F32)
        k_second = (second * cos_k + first * sin_k).astype(BF16).astype(F32)
        logits, tails = [], []
        for h in range(plan.mine):
            own = slice(h * k_half, (h + 1) * k_half)
            logit = jnp.sum(f_first[own] * k_first + f_second[own] * k_second, axis=0, keepdims=True)
            logits.append(logit.astype(BF16).astype(F32))
            tails.append(logit - logits[-1])
        if plan.direct:
            chunk = (place + start) // block * plan.q_rows
            q_ref[chunk : chunk + plan.q_rows] = jnp.concatenate([f_first, f_second], axis=0).astype(BF16)
            every += [*logits, *tails]
        else:
            pad = plan.line_rows - plan.q_rows - 2 * plan.mine
            pieces = [f_first, f_second, *logits, *tails]
            if pad:
                pieces.append(jnp.zeros((pad, block), F32))
            out = jnp.concatenate(pieces, axis=0).astype(BF16)
            for line in range(plan.line):
                q_ref[line, :, to] = out
        vo_ref[:, to] = total[plan.fold_at : plan.list_at]
    if plan.direct:
        first = vo_ref.shape[1] // HD * plan.q_rows + place // block * 2 * plan.mine
        q_ref[first : first + len(every)] = jnp.concatenate(every, axis=0).astype(BF16)


def tied(x, *others):
    return pl.pallas_call(
        lambda *refs: None,
        out_shape=shape(x.shape, x.dtype),
        in_specs=[untouched()] + [pl.BlockSpec(memory_space=pltpu.HBM)] * len(others),
        out_specs=untouched(),
        input_output_aliases={0: 0},
        compiler_params=limits(1),
        cost_estimate=cost(0, 0),
    )(x, *others)


def pack_prefix(plan, prefix_hbm, ws_hbm, after_ref, out_ref, *scratch):
    values, ws_ref, sems = scratch
    boards = values.shape[0]
    heads = plan.heads
    copies = (
        pltpu.make_async_copy(ws_hbm, ws_ref, sems.at[0]),
        pltpu.make_async_copy(prefix_hbm.at[:, :, pl.ds(HD, HD)], values, sems.at[1]),
        pltpu.make_async_copy(prefix_hbm.at[:, :, pl.ds(0, HD)], out_ref.at[pl.ds(0, boards)], sems.at[2]),
    )
    for copy in copies:
        copy.start()
    copies[0].wait()
    span = HD // boards
    ws = jnp.concatenate([ws_ref[...].astype(F32)] * (HD // heads), axis=0)
    row = lax.broadcasted_iota(jnp.int32, (HD, 1), 0)
    copies[1].wait()
    fold = None
    for board in range(boards):
        keep = (row // span == board) & (row % span < 2 * heads)
        term = matmul(values[board], jnp.where(keep, ws, 0.0).astype(BF16), NT)
        fold = term if fold is None else fold + term
    rounded = fold.astype(BF16).astype(F32)
    lane = lax.broadcasted_iota(jnp.int32, fold.shape, 1)
    out_ref[boards] = jnp.where(lane % span < heads, rounded, fold - rounded).astype(BF16)
    copies[2].wait()


def fold_columns(plan, here, block, board, boards, heads):
    lanes = plan.mine * plan.slots
    row = lax.broadcasted_iota(jnp.int32, (HD, lanes), 0) - board * (HD // boards)
    head = here * plan.mine + lax.broadcasted_iota(jnp.int32, (HD, lanes), 1) // plan.slots
    pick = jnp.where((row == head) | (row == head + heads), 1.0, 0.0).astype(BF16)
    return matmul(block, pick)


def prepare(plan, place_ref, board_ref, own_ref, other_ref, *rest):
    *prefix_refs, chosen_ref, fold_ref, slot_ref = rest
    count = board_ref.shape[1]
    board_row = board_ref[...]
    board_col = jnp.broadcast_to(board_row.astype(F32), (8, count)).T[:, 0:1].astype(jnp.int32)
    ahead = lax.broadcasted_iota(jnp.int32, (count, count), 0) < lax.broadcasted_iota(jnp.int32, (count, count), 1)
    rank = jnp.sum(jnp.where((board_col == board_row) & ahead, 1.0, 0.0), axis=0, keepdims=True)
    slot_ref[...] = rank.astype(jnp.int32) + place_ref[PEER] * plan.capacity
    here = place_ref[SLAB]
    boards, moves = chosen_ref.shape[0], chosen_ref.shape[1]
    move_at = lax.broadcasted_iota(jnp.int32, (moves, plan.slots), 0) + 1

    def step(board, carry):
        for j in range(plan.slab):
            place = ((here ^ j) % plan.pair) * boards + board
            row = (own_ref, other_ref)[j // plan.pair][pl.ds(place, 1), :].astype(jnp.int32)
            at = slice(j * plan.slots, (j + 1) * plan.slots)
            chosen_ref[board, :, at] = jnp.where(move_at == row, 1.0, 0.0).astype(BF16)
        for j, prefix_ref in enumerate(prefix_refs):
            fold_ref[j, board] = fold_columns(plan, here, prefix_ref[boards], board, boards, plan.heads)
        return carry

    lax.fori_loop(0, boards, step, 0)


def attend(plan, place_ref, vo_ref, own_ref, other_ref, chosen_ref, fold_ref, *rest):
    prefix_refs, rest = rest[: plan.slab], rest[plan.slab :]
    *q_refs, out_ref, table, extra, scores, taken_even, taken_odd = rest
    here = place_ref[SLAB]
    mine, heads, slots = plan.mine, plan.heads, plan.slots
    moves = vo_ref.shape[1]
    boards = prefix_refs[0].shape[0] - 1
    query_rows = mine * HD

    mixed = own_logits = None
    for step, q_ref in enumerate(q_refs):
        if plan.direct:
            chunks = range(moves // HD)
            values = jnp.concatenate([q_ref[c * plan.q_rows : (c + 1) * plan.q_rows] for c in chunks], axis=1)
            tails = q_ref[moves // HD * plan.q_rows :].astype(F32)
            tails = jnp.concatenate([tails[c * 2 * mine : (c + 1) * 2 * mine] for c in chunks], axis=1)
            tails = tails[:mine] + tails[mine:]
            own_logits = tails if own_logits is None else own_logits + tails
        else:
            values = q_ref[...]
        r = lax.broadcasted_iota(jnp.int32, (query_rows + 8, values.shape[0]), 0)
        c = lax.broadcasted_iota(jnp.int32, (query_rows + 8, values.shape[0]), 1)
        line, at = (place_ref[LINE] ^ step, c) if plan.direct else (c // plan.line_rows, c % plan.line_rows)
        part, head, entry = at // (mine * plan.pairs), (at // plan.pairs) % mine, at % plan.pairs
        goes = jnp.where(at < plan.q_rows, head * HD + part * HALF + line * plan.pairs + entry, -1)
        tail = at - plan.q_rows
        goes = jnp.where((tail >= 0) & (tail < 2 * mine), query_rows + tail % mine, goes)
        term = matmul(jnp.where(r == goes, 1.0, 0.0).astype(BF16), values)
        mixed = term if mixed is None else mixed + term
    if own_logits is None:
        own_logits = mixed[query_rows : query_rows + mine]
    table[:query_rows] = mixed[:query_rows].astype(BF16)
    extra[...] = jnp.zeros_like(extra)
    for place, value in ((0, own_logits), (2 * mine, vo_ref[...])):
        rounded = value.astype(BF16).astype(F32)
        extra[place : place + mine] = rounded
        extra[place + mine : place + 2 * mine] = value - rounded
    table[query_rows:] = extra[...].astype(BF16)

    scale = math.log2(math.e) / math.sqrt(HD)
    def per_head(x, base):
        pieces = [x[base + h : base + h + 1] + x[base + mine + h : base + mine + h + 1] for h in range(mine)]
        return jnp.concatenate(pieces, axis=1)

    def moves_of(j, board):
        place = ((here ^ j) % plan.pair) * boards + board
        return (own_ref, other_ref)[j // plan.pair][pl.ds(place, 1), :].astype(jnp.int32)

    def gather(board, taken):
        taken[...] = matmul(table[...], chosen_ref[board])

    def score_board(board, taken):
        for j in range(plan.slab):
            x = taken[:, j * slots : (j + 1) * slots]
            q = jnp.concatenate([x[h * HD : (h + 1) * HD].astype(BF16) for h in range(mine)], axis=1)
            logits = matmul(prefix_refs[j][board], q)
            if j < plan.slab - 1:
                fold = fold_ref[j, board]
            else:
                fold = fold_columns(plan, here, prefix_refs[j][boards], board, boards, heads)
            own_logit = per_head(x, query_rows)
            own_value = per_head(x, query_rows + 2 * mine)
            peak = jnp.maximum(jnp.max(logits, axis=0, keepdims=True), own_logit)
            weight = jnp.exp2((logits - peak) * scale)
            own_weight = jnp.exp2((own_logit - peak) * scale)
            denom = jnp.sum(weight, axis=0, keepdims=True) + own_weight
            value = (jnp.sum(weight * fold, axis=0, keepdims=True) + own_value * own_weight) / denom
            score = sum(value[:, h * slots : (h + 1) * slots] for h in range(mine))
            scores[here ^ j, pl.ds(board, 1), :] = jnp.where(moves_of(j, board) > 0, score, DEAD)

    gather(0, taken_even)

    def step(at, carry):
        board = 2 * at
        gather(jnp.minimum(board + 1, boards - 1), taken_odd)
        score_board(board, taken_even)
        gather(jnp.minimum(board + 2, boards - 1), taken_even)
        score_board(jnp.minimum(board + 1, boards - 1), taken_odd)
        return carry

    lax.fori_loop(0, -(-boards // 2), step, 0)
    live = scores[...] > 0.5 * DEAD
    count = jnp.sum(jnp.where(live, 1.0, 0.0), axis=2, keepdims=True)
    mean = jnp.sum(jnp.where(live, scores[...], 0.0), axis=2, keepdims=True) / jnp.maximum(count, 1.0)
    centered = jnp.where(live, scores[...] - mean, DEAD)
    for g in range(plan.groups):
        both = jnp.concatenate([centered[g * plan.pair + p] for p in range(plan.pair)], axis=0).astype(BF16)
        for copy in range(out_ref.shape[1]):
            out_ref[g, copy] = both


def finish(plan, parts_ref, board_ref, slot_ref, out_ref):
    line = parts_ref.shape[1]
    columns = []
    for at in range(line):
        total = None
        for g in range(parts_ref.shape[0]):
            for p in range(parts_ref.shape[2]):
                term = parts_ref[g, at, p].astype(F32)
                total = term if total is None else total + term
        columns.append(total)
    scores = jnp.concatenate(columns, axis=0)
    live = scores > 0.5 * DEAD
    peak = jnp.max(scores, axis=1, keepdims=True)
    denom = jnp.sum(jnp.where(live, jnp.exp(scores - peak), 0.0), axis=1, keepdims=True)
    logprob = jnp.where(live, scores - peak - jnp.log(denom), 0.0)
    count = board_ref.shape[1]
    member = lax.broadcasted_iota(jnp.int32, (scores.shape[0], count), 0) == board_ref[...]
    member = jnp.where(member, 1.0, 0.0).astype(BF16)
    found = jnp.zeros((plan.slots, count), F32)
    for _ in range(3):
        rounded = logprob.astype(BF16)
        found = found + matmul(rounded, member, TN)
        logprob = logprob - rounded.astype(F32)
    at = lax.broadcasted_iota(jnp.int32, (plan.slots, count), 0) == slot_ref[...]
    out_ref[...] = jnp.sum(jnp.where(at, found, 0.0), axis=0, keepdims=True)


def untouched():
    return pl.BlockSpec(memory_space=pl.ANY)


def local_call(kernel, place, args, outs, scratch=(), mib=40, copied=(), flops=0, nbytes=0, aliases=None):
    vmem = pl.BlockSpec(memory_space=pltpu.VMEM)
    return pl.pallas_call(
        kernel,
        out_shape=outs,
        in_specs=[pl.BlockSpec(memory_space=pltpu.SMEM)]
        + [untouched() if at in copied else vmem for at in range(len(args))],
        out_specs=jax.tree.map(lambda x: vmem, outs),
        scratch_shapes=scratch,
        input_output_aliases=aliases or {},
        compiler_params=limits(mib),
        cost_estimate=cost(flops, nbytes),
    )(place, *args)


def cost(flops, nbytes):
    return pl.CostEstimate(flops=int(flops), bytes_accessed=int(nbytes), transcendentals=0)


def swap(x, names, size, step):
    return lax.ppermute(x, names, [(at, at ^ step) for at in range(size)])


def shape(dims, dtype):
    return jax.ShapeDtypeStruct(tuple(dims), dtype)


def turn_table(position):
    frequency = THETA ** (-2.0 * np.arange(HALF, dtype=np.float32) / HD)
    angles = np.float32(position) * frequency.astype(np.float32)
    return np.stack([np.cos(angles), np.sin(angles)], axis=1).astype(np.float32)


def per_device(prefix_kv, move_ids, move_board, move_table, norm_gain, w_query, w_keyval, w_score):
    row_count = move_ids.shape[0]
    boards_here, prefix_len, _ = prefix_kv.shape
    moves, width = move_table.shape
    groups, line, pair = lax.axis_size("groups"), lax.axis_size("line"), lax.axis_size("pair")
    board_total = boards_here * line * pair
    capacity = max(2, (2 * row_count + board_total - 1) // board_total)
    heads = w_query.shape[1] // HD
    depth = w_query.shape[0]
    plan = Plan(groups, line, pair, heads, capacity, pair * boards_here, depth)
    group_at = lax.axis_index("groups").astype(jnp.int32)
    line_at = lax.axis_index("line").astype(jnp.int32)
    pair_at = lax.axis_index("pair").astype(jnp.int32)
    place = jnp.stack([group_at, line_at, line_at * pair + pair_at, group_at * pair + pair_at])
    ws = w_score.reshape(heads, HD)
    slab_axes = ("groups", "pair")
    board_row = move_board.reshape(1, row_count)

    half_cols = w_query.shape[1] // groups
    packed = local_call(
        functools.partial(pack_weights, plan),
        group_at.reshape(1),
        (w_query, w_keyval, ws, board_row, move_ids.reshape(1, row_count)),
        shape((plan.peers, *plan.sent), BF16),
        [
            pltpu.VMEM((depth, half_cols), BF16),
            pltpu.VMEM((depth, 2 * HD), BF16),
            pltpu.VMEM((heads, HD), BF16),
            pltpu.VMEM((1, row_count), jnp.int32),
            pltpu.VMEM((1, row_count), jnp.int32),
            pltpu.VMEM((plan.peers * plan.rows, half_cols + 2 * HD), F32),
            pltpu.SemaphoreType.DMA((5,)),
        ],
        62,
        range(5),
    )
    weights = lax.all_to_all(packed, ("line", "pair"), split_axis=0, concat_axis=0, tiled=True)

    payload = pl.pallas_call(
        functools.partial(pack_prefix, plan),
        out_shape=shape((boards_here + 1, prefix_len, HD), BF16),
        in_specs=[untouched()] * 3,
        out_specs=pl.BlockSpec(memory_space=pltpu.VMEM),
        scratch_shapes=[
            pltpu.VMEM((boards_here, prefix_len, HD), BF16),
            pltpu.VMEM((heads, HD), BF16),
            pltpu.SemaphoreType.DMA((3,)),
        ],
        compiler_params=limits(56),
        cost_estimate=cost(0, 0),
    )(prefix_kv, ws, packed)
    beside = swap(payload, slab_axes, plan.slab, 1)
    across = swap(payload, slab_axes, plan.slab, 2)

    block = min(moves, 128)
    vmem = pl.BlockSpec(memory_space=pltpu.VMEM)
    *normed, mark = pl.pallas_call(
        normalize,
        out_shape=[*[shape((moves // 2, width), BF16)] * 2, pltpu.HBM((8, width), BF16)],
        in_specs=[untouched(), vmem, untouched()],
        out_specs=[untouched()] * 3,
        scratch_shapes=[
            pltpu.VMEM((1, width), F32),
            pltpu.VMEM((3, block, width), BF16),
            pltpu.VMEM((3, block, width), BF16),
            pltpu.SemaphoreType.DMA((3,)),
            pltpu.SemaphoreType.DMA((3,)),
        ],
        compiler_params=limits(58),
        cost_estimate=cost(moves * width, moves * width // 4),
    )(move_table, norm_gain.reshape(width // HD, HD), packed)
    turns = turn_table(prefix_len).reshape(line, 1, plan.pairs, 2)
    turns = np.tile(turns, (1, plan.mine, 1, 1)).reshape(line, plan.mine * plan.pairs, 2)
    flat = weights.transpose(1, 0, 2).reshape(plan.rows, width) if depth % HD else weights
    sent = (moves // HD * (plan.q_rows + 2 * plan.mine), HD) if plan.direct else (line, plan.line_rows, moves)
    outs = (shape(sent, BF16), shape((plan.mine, moves), F32))
    across = tied(across, mark)
    diagonal = swap(across, slab_axes, plan.slab, 1)
    full = shape((plan.peers, plan.rows, depth), BF16) if plan.tight else shape(flat.shape, BF16)
    filled, listed = (), None
    for step, after in enumerate((across, beside)):
        made = local_call(
            functools.partial(project, plan, step * moves // 2, step == 0),
            place,
            (flat, normed[step], jnp.asarray(turns), after, *filled),
            [*outs, *([shape((plan.share, plan.slots), F32), full] if step == 0 else [])],
            (),
            20,
            (3,),
            moves * width * 1024,
            moves * width,
            {5: 0, 6: 1} if filled else None,
        )
        filled = made[:2]
        if step == 0:
            listed, flat = made[2:]
    queries, own_values = filled
    other = swap(listed, slab_axes, plan.slab, pair)
    if plan.direct:
        queries = [queries] + [swap(queries, "line", line, step) for step in range(1, line)]
    else:
        queries = lax.all_to_all(queries, "line", split_axis=0, concat_axis=0, tiled=True)
        queries = [queries.reshape(line * plan.line_rows, moves)]

    query_rows = plan.mine * HD
    back = plan.peers * lax.axis_size("tensor")
    chosen, folds, slot_row = local_call(
        functools.partial(prepare, plan),
        place,
        (board_row, listed, other, payload, beside, across),
        (
            shape((boards_here, moves, plan.slab * plan.slots), BF16),
            shape((plan.slab - 1, boards_here, prefix_len, plan.mine * plan.slots), F32),
            shape((1, row_count), jnp.int32),
        ),
        mib=20,
        flops=10**9,
        nbytes=10**6,
    )
    parts = local_call(
        functools.partial(attend, plan),
        place,
        (own_values, listed, other, chosen, folds, payload, beside, across, diagonal, *queries),
        shape((groups, back, plan.share, plan.slots), BF16),
        [
            pltpu.VMEM((query_rows + 16, moves), BF16),
            pltpu.VMEM((16, moves), F32),
            pltpu.VMEM((plan.slab, boards_here, plan.slots), F32),
            pltpu.VMEM((query_rows + 16, plan.slab * plan.slots), F32),
            pltpu.VMEM((query_rows + 16, plan.slab * plan.slots), F32),
        ],
        24,
    )
    parts = lax.all_to_all(
        parts.reshape(groups * back, plan.share, plan.slots),
        ("groups", "line", "pair", "tensor"),
        split_axis=0,
        concat_axis=0,
        tiled=True,
    )
    parts = parts.reshape(groups, line, back // line, plan.share, plan.slots)
    logprob = pl.pallas_call(
        functools.partial(finish, plan), out_shape=shape((1, row_count), F32), compiler_params=limits(VMEM_MIB)
    )(parts, board_row, slot_row)
    return logprob.reshape(row_count)


def solution(mesh):
    order = ("groups", "dp", "tensor")
    assert mesh.axis_names == order
    pair = 2
    groups, peers, tensor = (mesh.shape[name] for name in order)
    fine = Mesh(mesh.devices.reshape(groups, peers // pair, pair, tensor), ("groups", "line", "pair", "tensor"))
    rows = ("groups", "line", "pair")
    placed = (
        P(rows, None, "tensor"),
        P(rows),
        P(rows, None),
        P(),
        P(),
        P(("line", "pair"), "tensor"),
        P(("line", "pair"), "tensor"),
        P("tensor"),
    )
    return jax.shard_map(per_device, mesh=fine, in_specs=placed, out_specs=P(rows), check_vma=False)
```

```python
import functools
import math

import jax
import jax.numpy as jnp
import numpy as np
from jax import lax
from jax.experimental import pallas as pl
from jax.experimental.pallas import tpu as pltpu
from jax.sharding import Mesh
from jax.sharding import PartitionSpec as P

HD = 128
HALF = HD // 2
EPS = 1e-06
THETA = 5000000.0
DEAD = -1e30
VMEM_MIB = 52
GROUP, LINE, PEER, SLAB = range(4)

F32 = jnp.float32
BF16 = jnp.bfloat16

NN = (((1,), (0,)), ((), ()))
NT = (((1,), (1,)), ((), ()))
TN = (((0,), (0,)), ((), ()))


def matmul(a, b, dims=NN):
    return lax.dot_general(a, b, dims, preferred_element_type=F32)


def limits(mib):
    return pltpu.CompilerParams(vmem_limit_bytes=mib * 1024 * 1024)


class Plan:
    def __init__(self, groups, line, pair, heads, capacity, share, depth):
        self.groups, self.line, self.pair = groups, line, pair
        self.peers = line * pair
        self.slab = groups * pair
        self.heads = heads
        self.mine = heads // self.slab
        self.pairs = HALF // line
        self.q_rows = self.mine * 2 * self.pairs
        self.k_rows = 2 * self.pairs
        self.fold_at = self.q_rows + self.k_rows
        self.list_at = self.fold_at + self.mine
        self.rows = -(-(self.list_at + 1) // 8) * 8
        self.line_rows = -(-(self.q_rows + 2 * self.mine) // 8) * 8
        self.capacity = capacity
        self.share = share
        self.slots = self.peers * capacity
        self.direct = line <= 4
        self.tight = self.pairs % 16 == 0 and depth % HD == 0
        self.chunks = depth // HD
        last = -(-(self.mine + 1) * self.chunks // 16) * 16
        self.sent = (self.fold_at * self.chunks + last, HD) if self.tight else (self.rows, depth)


def pack_weights(plan, place_ref, wq_hbm, wkv_hbm, ws_hbm, board_hbm, ids_hbm, *rest):
    out_ref, wq, wkv, ws_ref, board_ref, ids_ref, pick, sems = rest
    group = place_ref[0]
    half_cols = wq.shape[1]
    columns_here = pl.ds(pl.multiple_of(group * half_cols, HD), half_cols)
    copies = (
        pltpu.make_async_copy(ws_hbm, ws_ref, sems.at[0]),
        pltpu.make_async_copy(board_hbm, board_ref, sems.at[1]),
        pltpu.make_async_copy(ids_hbm, ids_ref, sems.at[2]),
        pltpu.make_async_copy(wq_hbm.at[:, columns_here], wq, sems.at[3]),
        pltpu.make_async_copy(wkv_hbm, wkv, sems.at[4]),
    )
    for copy in copies[::-1]:
        copy.start()
    for copy in copies[:3]:
        copy.wait()
    count, depth = board_ref.shape[1], wq.shape[0]
    board_row = board_ref[...]
    board_col = jnp.broadcast_to(board_row.astype(F32), (8, count)).T[:, 0:1].astype(jnp.int32)
    own = lax.broadcasted_iota(jnp.int32, (count, count), 0)
    other = lax.broadcasted_iota(jnp.int32, (count, count), 1)
    ahead = jnp.where((board_col == board_row) & (other < own), 1.0, 0.0)
    rank = jnp.sum(ahead, axis=1, keepdims=True).astype(jnp.int32)
    move = ids_ref[...] + 1
    boards, span = plan.line * plan.share, plan.share * plan.capacity
    member = lax.broadcasted_iota(jnp.int32, (boards, count), 0) == board_row
    parts = [jnp.where(member, part.astype(F32), 0.0) for part in (move // 64, move % 64)]
    lane = lax.broadcasted_iota(jnp.int32, (count, depth), 1)
    ranked = jnp.where(rank == (lane % span) % plan.capacity, 1.0, 0.0).astype(BF16)
    found = matmul(jnp.concatenate(parts, axis=0).astype(BF16), ranked)
    lane = lax.broadcasted_iota(jnp.int32, (2 * boards, depth), 1)
    row = lax.broadcasted_iota(jnp.int32, (2 * boards, depth), 0)
    keep = (row // boards == lane // span) & (row % plan.share == (lane % span) // plan.capacity)
    found = jnp.where(keep, found, 0.0)
    lists = []
    for line in range(plan.line):
        at = line * plan.share
        both = found[at : at + plan.share] + found[boards + at : boards + at + plan.share]
        lists.append(jnp.sum(both, axis=0, keepdims=True))

    if plan.tight:
        turn_weights(plan, group, lists, copies[3:], wq, wkv, ws_ref, out_ref)
    else:
        pick_weights(plan, group, lists, copies[3:], wq, wkv, ws_ref, out_ref, pick)


def turn_weights(plan, group, lists, copies, wq, wkv, ws_ref, out_ref):
    for copy in copies:
        copy.wait()
    q = wq[...].T
    k = wkv[:, :HD].T
    folds = matmul(ws_ref[...], wkv[:, HD:], NT)
    row = lax.broadcasted_iota(jnp.int32, folds.shape, 0)
    pairs = plan.pairs
    lanes = [slice(c * HD, (c + 1) * HD) for c in range(plan.chunks)]
    first_last = plan.fold_at * plan.chunks
    zeros = jnp.zeros((plan.sent[0] - first_last - (plan.mine + 1) * plan.chunks, HD), F32)
    for pair in range(plan.pair):
        first = (group * plan.pair + pair) * plan.mine
        mine = [jnp.sum(jnp.where(row == first + h, folds, 0.0), axis=0, keepdims=True) for h in range(plan.mine)]
        for line in range(plan.line):
            peer = line * plan.pair + pair
            for c, lane in enumerate(lanes):
                for part in range(2):
                    entry = part * HALF + line * pairs
                    for h in range(plan.mine):
                        at = c * plan.fold_at + (part * plan.mine + h) * pairs
                        source = (pair * plan.mine + h) * HD + entry
                        out_ref[peer, at : at + pairs] = q[source : source + pairs, lane]
                    at = c * plan.fold_at + plan.q_rows + part * pairs
                    out_ref[peer, at : at + pairs] = k[entry : entry + pairs, lane]
            last = [values[:, lane] for values in (*mine, lists[line]) for lane in lanes]
            out_ref[peer, first_last:] = jnp.concatenate([*last, zeros], axis=0).astype(BF16)


def pick_weights(plan, group, lists, copies, wq, wkv, ws_ref, out_ref, pick):
    rows, half_cols = plan.rows, wq.shape[1]
    r = lax.broadcasted_iota(jnp.int32, (rows, 1), 0)
    part = r // (plan.mine * plan.pairs)
    head = (r // plan.pairs) % plan.mine
    entry = r % plan.pairs
    is_q = r < plan.q_rows
    k_at = r - plan.q_rows
    is_k = (k_at >= 0) & (k_at < plan.k_rows)
    f_at = r - plan.fold_at
    is_f = (f_at >= 0) & (f_at < plan.mine)
    q_lane = lax.broadcasted_iota(jnp.int32, (rows, half_cols), 1)
    k_lane = lax.broadcasted_iota(jnp.int32, (rows, HD), 1)
    ws = ws_ref[...].astype(F32)

    def fill(peer, carry):
        line, pair = peer // plan.pair, peer % plan.pair
        column = (pair * plan.mine + head) * HD + part * HALF + line * plan.pairs + entry
        column = jnp.where(is_q, column, -1)
        at = pl.ds(pl.multiple_of(peer * rows, 8), rows)
        pick[at, :half_cols] = jnp.where(q_lane == column, 1.0, 0.0)
        k_column = (k_at // plan.pairs) * HALF + line * plan.pairs + k_at % plan.pairs
        k_column = jnp.where(is_k, k_column, -1)
        pick[at, half_cols : half_cols + HD] = jnp.where(k_lane == k_column, 1.0, 0.0)
        fold = jnp.zeros((rows, HD), F32)
        my_head = jnp.where(is_f, (group * plan.pair + pair) * plan.mine + f_at, -1)
        for h in range(plan.heads):
            fold = jnp.where(my_head == h, ws[h : h + 1], fold)
        pick[at, half_cols + HD :] = fold
        return carry

    lax.fori_loop(0, plan.peers, fill, 0, unroll=plan.peers <= 8)

    for copy in copies:
        copy.wait()
    left = pick[...].astype(BF16)
    total = matmul(left[:, :half_cols], wq[...], NT) + matmul(left[:, half_cols:], wkv[...], NT)
    for peer in range(plan.peers):
        mine = total[peer * rows : (peer + 1) * rows]
        out_ref[peer] = jnp.where(r == plan.list_at, lists[peer // plan.pair], mine).astype(BF16)


def normalize(table_hbm, gain_ref, after_ref, *refs):
    *outs, mark_ref, gain, buffers, made, sems, out_sems = refs
    held, block, _ = buffers.shape
    steps = table_hbm.shape[0] // block
    each = outs[0].shape[0] // block

    def copy(step):
        source = table_hbm.at[pl.ds(step * block, block)]
        return pltpu.make_async_copy(source, buffers.at[step % held], sems.at[step % held])

    def store(step):
        target = outs[step // each].at[pl.ds(step % each * block, block)]
        return pltpu.make_async_copy(made.at[step % held], target, out_sems.at[step % held])

    for step in range(min(held, steps)):
        copy(step).start()
    rows = gain_ref[...].astype(F32)
    gain[...] = jnp.concatenate([rows[r : r + 1] for r in range(rows.shape[0])], axis=1)
    for step in range(steps):
        copy(step).wait()
        if step >= held:
            store(step - held).wait()
        raw = buffers[step % held].astype(F32)
        inverse = lax.rsqrt(jnp.mean(raw * raw, axis=-1, keepdims=True) + EPS)
        made[step % held] = (raw * inverse * gain[...]).astype(BF16)
        store(step).start()
        if step + held < steps:
            copy(step + held).start()
    for step in range(max(0, steps - held), steps):
        store(step).wait()
    mark_ref[...] = jnp.zeros_like(mark_ref)


def spread_weights(plan, w_ref, full_ref):
    lists = []
    for s in range(plan.peers):
        for c in range(plan.chunks):
            rows = w_ref[s, c * plan.fold_at : (c + 1) * plan.fold_at]
            full_ref[s, : plan.fold_at, c * HD : (c + 1) * HD] = rows
        last = w_ref[s, plan.fold_at * plan.chunks :].astype(F32)
        last = [
            jnp.concatenate([last[i * plan.chunks + c : i * plan.chunks + c + 1] for c in range(plan.chunks)], axis=1)
            for i in range(plan.mine + 1)
        ]
        zeros = jnp.zeros((plan.rows - plan.list_at, last[0].shape[1]), F32)
        full_ref[s, plan.fold_at :] = jnp.concatenate([*last[: plan.mine], zeros], axis=0).astype(BF16)
        lists.append(last[plan.mine])
    return jnp.concatenate(lists, axis=0)


def list_rows(plan, w_ref):
    if len(w_ref.shape) == 3:
        rows = [w_ref[s].astype(F32)[plan.list_at : plan.list_at + 1] for s in range(plan.peers)]
    else:
        row = w_ref[...].astype(F32)[plan.list_at : plan.list_at + 1]
        span = plan.share * plan.capacity
        rows = [row[:, s * 2 * span : (s + 1) * 2 * span] for s in range(plan.peers)]
    return jnp.concatenate(rows, axis=0)


def read_lists(plan, rows, out_ref):
    share, capacity, peers = plan.share, plan.capacity, plan.peers
    span = share * capacity
    lane = lax.broadcasted_iota(jnp.int32, (share * peers, 2 * span), 1)
    row = lax.broadcasted_iota(jnp.int32, (share * peers, 2 * span), 0)
    lane = jnp.where(lane < span, lane, lane - span)
    spread = jnp.concatenate([rows] * share, axis=0)
    spread = jnp.where(lane // capacity == row // peers, spread, 0.0).astype(BF16)
    c = lax.broadcasted_iota(jnp.int32, (2 * span, plan.slots), 0)
    slot = lax.broadcasted_iota(jnp.int32, (2 * span, plan.slots), 1)
    scale = jnp.where(c < span, 64.0, 1.0)
    place = jnp.where(c % capacity == slot % capacity, scale, 0.0).astype(BF16)
    listed = matmul(spread, place)
    row = lax.broadcasted_iota(jnp.int32, listed.shape, 0)
    slot = lax.broadcasted_iota(jnp.int32, listed.shape, 1)
    listed = jnp.where(slot // capacity == row % peers, listed, 0.0)
    out_ref[...] = jnp.sum(listed.reshape(share, peers, plan.slots), axis=1)


def project(plan, place, lists, place_ref, w_ref, normed_ref, turn_ref, after_ref, *refs):
    if lists:
        *refs, list_ref, full_ref = refs
        if plan.tight:
            rows = spread_weights(plan, w_ref, full_ref)
            w_ref = full_ref
        else:
            rows = list_rows(plan, w_ref)
            full_ref[...] = w_ref[...]
        read_lists(plan, rows, list_ref)
    q_ref, vo_ref = refs[-2:]
    turns = turn_ref[place_ref[LINE]]
    half, k_half = plan.q_rows // 2, plan.k_rows // 2
    cosine, sine = turns[:, 0:1], turns[:, 1:2]
    cos_k, sin_k = cosine[:k_half], sine[:k_half]
    moves = normed_ref.shape[0]
    block = min(moves, HD)
    every = []
    for start in range(0, moves, block):
        at, to = slice(start, start + block), slice(place + start, place + start + block)
        if len(w_ref.shape) == 3:
            depth = w_ref.shape[2]
            total = None
            for s in range(w_ref.shape[0]):
                term = matmul(w_ref[s], normed_ref[at, s * depth : (s + 1) * depth], NT)
                total = term if total is None else total + term
        else:
            total = matmul(w_ref[...], normed_ref[at, :], NT)
        first, second = total[:half], total[half : 2 * half]
        f_first = (first * cosine - second * sine).astype(BF16).astype(F32)
        f_second = (second * cosine + first * sine).astype(BF16).astype(F32)
        first, second = total[plan.q_rows : plan.q_rows + k_half], total[plan.q_rows + k_half : plan.fold_at]
        k_first = (first * cos_k - second * sin_k).astype(BF16).astype(F32)
        k_second = (second * cos_k + first * sin_k).astype(BF16).astype(F32)
        logits, tails = [], []
        for h in range(plan.mine):
            own = slice(h * k_half, (h + 1) * k_half)
            logit = jnp.sum(f_first[own] * k_first + f_second[own] * k_second, axis=0, keepdims=True)
            logits.append(logit.astype(BF16).astype(F32))
            tails.append(logit - logits[-1])
        if plan.direct:
            chunk = (place + start) // block * plan.q_rows
            q_ref[chunk : chunk + plan.q_rows] = jnp.concatenate([f_first, f_second], axis=0).astype(BF16)
            every += [*logits, *tails]
        else:
            pad = plan.line_rows - plan.q_rows - 2 * plan.mine
            pieces = [f_first, f_second, *logits, *tails]
            if pad:
                pieces.append(jnp.zeros((pad, block), F32))
            out = jnp.concatenate(pieces, axis=0).astype(BF16)
            for line in range(plan.line):
                q_ref[line, :, to] = out
        vo_ref[:, to] = total[plan.fold_at : plan.list_at]
    if plan.direct:
        first = vo_ref.shape[1] // HD * plan.q_rows + place // block * 2 * plan.mine
        q_ref[first : first + len(every)] = jnp.concatenate(every, axis=0).astype(BF16)


def tied(x, *others):
    return pl.pallas_call(
        lambda *refs: None,
        out_shape=shape(x.shape, x.dtype),
        in_specs=[untouched()] + [pl.BlockSpec(memory_space=pltpu.VMEM)] * len(others),
        out_specs=untouched(),
        input_output_aliases={0: 0},
        compiler_params=limits(1),
        cost_estimate=cost(0, 0),
    )(x, *others)


def pack_prefix(plan, prefix_hbm, ws_hbm, after_ref, out_ref, *scratch):
    values, ws_ref, sems = scratch
    boards = values.shape[0]
    heads = plan.heads
    copies = (
        pltpu.make_async_copy(ws_hbm, ws_ref, sems.at[0]),
        pltpu.make_async_copy(prefix_hbm.at[:, :, pl.ds(HD, HD)], values, sems.at[1]),
        pltpu.make_async_copy(prefix_hbm.at[:, :, pl.ds(0, HD)], out_ref.at[pl.ds(0, boards)], sems.at[2]),
    )
    for copy in copies:
        copy.start()
    copies[0].wait()
    span = HD // boards
    ws = jnp.concatenate([ws_ref[...].astype(F32)] * (HD // heads), axis=0)
    row = lax.broadcasted_iota(jnp.int32, (HD, 1), 0)
    copies[1].wait()
    fold = None
    for board in range(boards):
        keep = (row // span == board) & (row % span < 2 * heads)
        term = matmul(values[board], jnp.where(keep, ws, 0.0).astype(BF16), NT)
        fold = term if fold is None else fold + term
    rounded = fold.astype(BF16).astype(F32)
    lane = lax.broadcasted_iota(jnp.int32, fold.shape, 1)
    out_ref[boards] = jnp.where(lane % span < heads, rounded, fold - rounded).astype(BF16)
    copies[2].wait()


def fold_columns(plan, here, block, board, boards, heads):
    lanes = plan.mine * plan.slots
    row = lax.broadcasted_iota(jnp.int32, (HD, lanes), 0) - board * (HD // boards)
    head = here * plan.mine + lax.broadcasted_iota(jnp.int32, (HD, lanes), 1) // plan.slots
    pick = jnp.where((row == head) | (row == head + heads), 1.0, 0.0).astype(BF16)
    return matmul(block, pick)


def prepare(plan, place_ref, board_ref, own_ref, other_ref, *rest):
    *prefix_refs, chosen_ref, fold_ref, slot_ref = rest
    count = board_ref.shape[1]
    board_row = board_ref[...]
    board_col = jnp.broadcast_to(board_row.astype(F32), (8, count)).T[:, 0:1].astype(jnp.int32)
    ahead = lax.broadcasted_iota(jnp.int32, (count, count), 0) < lax.broadcasted_iota(jnp.int32, (count, count), 1)
    rank = jnp.sum(jnp.where((board_col == board_row) & ahead, 1.0, 0.0), axis=0, keepdims=True)
    slot_ref[...] = rank.astype(jnp.int32) + place_ref[PEER] * plan.capacity
    here = place_ref[SLAB]
    boards, moves = chosen_ref.shape[0], chosen_ref.shape[1]
    move_at = lax.broadcasted_iota(jnp.int32, (moves, plan.slots), 0) + 1

    def step(board, carry):
        for j in range(plan.slab):
            place = ((here ^ j) % plan.pair) * boards + board
            row = (own_ref, other_ref)[j // plan.pair][pl.ds(place, 1), :].astype(jnp.int32)
            at = slice(j * plan.slots, (j + 1) * plan.slots)
            chosen_ref[board, :, at] = jnp.where(move_at == row, 1.0, 0.0).astype(BF16)
        for j, prefix_ref in enumerate(prefix_refs):
            fold_ref[j, board] = fold_columns(plan, here, prefix_ref[boards], board, boards, plan.heads)
        return carry

    lax.fori_loop(0, boards, step, 0)


def attend(plan, place_ref, vo_ref, own_ref, other_ref, chosen_ref, fold_ref, *rest):
    prefix_refs, rest = rest[: plan.slab], rest[plan.slab :]
    *q_refs, out_ref, table, extra, scores, taken_even, taken_odd = rest
    here = place_ref[SLAB]
    mine, heads, slots = plan.mine, plan.heads, plan.slots
    moves = vo_ref.shape[1]
    boards = prefix_refs[0].shape[0] - 1
    query_rows = mine * HD

    mixed = own_logits = None
    for step, q_ref in enumerate(q_refs):
        if plan.direct:
            chunks = range(moves // HD)
            values = jnp.concatenate([q_ref[c * plan.q_rows : (c + 1) * plan.q_rows] for c in chunks], axis=1)
            tails = q_ref[moves // HD * plan.q_rows :].astype(F32)
            tails = jnp.concatenate([tails[c * 2 * mine : (c + 1) * 2 * mine] for c in chunks], axis=1)
            tails = tails[:mine] + tails[mine:]
            own_logits = tails if own_logits is None else own_logits + tails
        else:
            values = q_ref[...]
        r = lax.broadcasted_iota(jnp.int32, (query_rows + 8, values.shape[0]), 0)
        c = lax.broadcasted_iota(jnp.int32, (query_rows + 8, values.shape[0]), 1)
        line, at = (place_ref[LINE] ^ step, c) if plan.direct else (c // plan.line_rows, c % plan.line_rows)
        part, head, entry = at // (mine * plan.pairs), (at // plan.pairs) % mine, at % plan.pairs
        goes = jnp.where(at < plan.q_rows, head * HD + part * HALF + line * plan.pairs + entry, -1)
        tail = at - plan.q_rows
        goes = jnp.where((tail >= 0) & (tail < 2 * mine), query_rows + tail % mine, goes)
        term = matmul(jnp.where(r == goes, 1.0, 0.0).astype(BF16), values)
        mixed = term if mixed is None else mixed + term
    if own_logits is None:
        own_logits = mixed[query_rows : query_rows + mine]
    table[:query_rows] = mixed[:query_rows].astype(BF16)
    extra[...] = jnp.zeros_like(extra)
    for place, value in ((0, own_logits), (2 * mine, vo_ref[...])):
        rounded = value.astype(BF16).astype(F32)
        extra[place : place + mine] = rounded
        extra[place + mine : place + 2 * mine] = value - rounded
    table[query_rows:] = extra[...].astype(BF16)

    scale = math.log2(math.e) / math.sqrt(HD)
    def per_head(x, base):
        pieces = [x[base + h : base + h + 1] + x[base + mine + h : base + mine + h + 1] for h in range(mine)]
        return jnp.concatenate(pieces, axis=1)

    def moves_of(j, board):
        place = ((here ^ j) % plan.pair) * boards + board
        return (own_ref, other_ref)[j // plan.pair][pl.ds(place, 1), :].astype(jnp.int32)

    def gather(board, taken):
        taken[...] = matmul(table[...], chosen_ref[board])

    def score_board(board, taken):
        for j in range(plan.slab):
            x = taken[:, j * slots : (j + 1) * slots]
            q = jnp.concatenate([x[h * HD : (h + 1) * HD].astype(BF16) for h in range(mine)], axis=1)
            logits = matmul(prefix_refs[j][board], q)
            if j < plan.slab - 1:
                fold = fold_ref[j, board]
            else:
                fold = fold_columns(plan, here, prefix_refs[j][boards], board, boards, heads)
            own_logit = per_head(x, query_rows)
            own_value = per_head(x, query_rows + 2 * mine)
            peak = jnp.maximum(jnp.max(logits, axis=0, keepdims=True), own_logit)
            weight = jnp.exp2((logits - peak) * scale)
            own_weight = jnp.exp2((own_logit - peak) * scale)
            denom = jnp.sum(weight, axis=0, keepdims=True) + own_weight
            value = (jnp.sum(weight * fold, axis=0, keepdims=True) + own_value * own_weight) / denom
            score = sum(value[:, h * slots : (h + 1) * slots] for h in range(mine))
            scores[here ^ j, pl.ds(board, 1), :] = jnp.where(moves_of(j, board) > 0, score, DEAD)

    gather(0, taken_even)

    def step(at, carry):
        board = 2 * at
        gather(jnp.minimum(board + 1, boards - 1), taken_odd)
        score_board(board, taken_even)
        gather(jnp.minimum(board + 2, boards - 1), taken_even)
        score_board(jnp.minimum(board + 1, boards - 1), taken_odd)
        return carry

    lax.fori_loop(0, -(-boards // 2), step, 0)
    live = scores[...] > 0.5 * DEAD
    count = jnp.sum(jnp.where(live, 1.0, 0.0), axis=2, keepdims=True)
    mean = jnp.sum(jnp.where(live, scores[...], 0.0), axis=2, keepdims=True) / jnp.maximum(count, 1.0)
    centered = jnp.where(live, scores[...] - mean, DEAD)
    for g in range(plan.groups):
        both = jnp.concatenate([centered[g * plan.pair + p] for p in range(plan.pair)], axis=0).astype(BF16)
        for copy in range(out_ref.shape[1]):
            out_ref[g, copy] = both


def finish(plan, parts_ref, board_ref, slot_ref, out_ref):
    line = parts_ref.shape[1]
    columns = []
    for at in range(line):
        total = None
        for g in range(parts_ref.shape[0]):
            for p in range(parts_ref.shape[2]):
                term = parts_ref[g, at, p].astype(F32)
                total = term if total is None else total + term
        columns.append(total)
    scores = jnp.concatenate(columns, axis=0)
    live = scores > 0.5 * DEAD
    peak = jnp.max(scores, axis=1, keepdims=True)
    denom = jnp.sum(jnp.where(live, jnp.exp(scores - peak), 0.0), axis=1, keepdims=True)
    logprob = jnp.where(live, scores - peak - jnp.log(denom), 0.0)
    count = board_ref.shape[1]
    member = lax.broadcasted_iota(jnp.int32, (scores.shape[0], count), 0) == board_ref[...]
    member = jnp.where(member, 1.0, 0.0).astype(BF16)
    found = jnp.zeros((plan.slots, count), F32)
    for _ in range(3):
        rounded = logprob.astype(BF16)
        found = found + matmul(rounded, member, TN)
        logprob = logprob - rounded.astype(F32)
    at = lax.broadcasted_iota(jnp.int32, (plan.slots, count), 0) == slot_ref[...]
    out_ref[...] = jnp.sum(jnp.where(at, found, 0.0), axis=0, keepdims=True)


def untouched():
    return pl.BlockSpec(memory_space=pl.ANY)


def local_call(kernel, place, args, outs, scratch=(), mib=40, copied=(), flops=0, nbytes=0, aliases=None):
    vmem = pl.BlockSpec(memory_space=pltpu.VMEM)
    return pl.pallas_call(
        kernel,
        out_shape=outs,
        in_specs=[pl.BlockSpec(memory_space=pltpu.SMEM)]
        + [untouched() if at in copied else vmem for at in range(len(args))],
        out_specs=jax.tree.map(lambda x: vmem, outs),
        scratch_shapes=scratch,
        input_output_aliases=aliases or {},
        compiler_params=limits(mib),
        cost_estimate=cost(flops, nbytes),
    )(place, *args)


def cost(flops, nbytes):
    return pl.CostEstimate(flops=int(flops), bytes_accessed=int(nbytes), transcendentals=0)


def swap(x, names, size, step):
    return lax.ppermute(x, names, [(at, at ^ step) for at in range(size)])


def shape(dims, dtype):
    return jax.ShapeDtypeStruct(tuple(dims), dtype)


def turn_table(position):
    frequency = THETA ** (-2.0 * np.arange(HALF, dtype=np.float32) / HD)
    angles = np.float32(position) * frequency.astype(np.float32)
    return np.stack([np.cos(angles), np.sin(angles)], axis=1).astype(np.float32)


def per_device(prefix_kv, move_ids, move_board, move_table, norm_gain, w_query, w_keyval, w_score):
    row_count = move_ids.shape[0]
    boards_here, prefix_len, _ = prefix_kv.shape
    moves, width = move_table.shape
    groups, line, pair = lax.axis_size("groups"), lax.axis_size("line"), lax.axis_size("pair")
    board_total = boards_here * line * pair
    capacity = max(2, (2 * row_count + board_total - 1) // board_total)
    heads = w_query.shape[1] // HD
    depth = w_query.shape[0]
    plan = Plan(groups, line, pair, heads, capacity, pair * boards_here, depth)
    group_at = lax.axis_index("groups").astype(jnp.int32)
    line_at = lax.axis_index("line").astype(jnp.int32)
    pair_at = lax.axis_index("pair").astype(jnp.int32)
    place = jnp.stack([group_at, line_at, line_at * pair + pair_at, group_at * pair + pair_at])
    ws = w_score.reshape(heads, HD)
    slab_axes = ("groups", "pair")
    board_row = move_board.reshape(1, row_count)

    half_cols = w_query.shape[1] // groups
    packed = local_call(
        functools.partial(pack_weights, plan),
        group_at.reshape(1),
        (w_query, w_keyval, ws, board_row, move_ids.reshape(1, row_count)),
        shape((plan.peers, *plan.sent), BF16),
        [
            pltpu.VMEM((depth, half_cols), BF16),
            pltpu.VMEM((depth, 2 * HD), BF16),
            pltpu.VMEM((heads, HD), BF16),
            pltpu.VMEM((1, row_count), jnp.int32),
            pltpu.VMEM((1, row_count), jnp.int32),
            pltpu.VMEM((plan.peers * plan.rows, half_cols + 2 * HD), F32),
            pltpu.SemaphoreType.DMA((5,)),
        ],
        62,
        range(5),
    )
    weights = lax.all_to_all(packed, ("line", "pair"), split_axis=0, concat_axis=0, tiled=True)

    payload = pl.pallas_call(
        functools.partial(pack_prefix, plan),
        out_shape=shape((boards_here + 1, prefix_len, HD), BF16),
        in_specs=[untouched()] * 3,
        out_specs=pl.BlockSpec(memory_space=pltpu.VMEM),
        scratch_shapes=[
            pltpu.VMEM((boards_here, prefix_len, HD), BF16),
            pltpu.VMEM((heads, HD), BF16),
            pltpu.SemaphoreType.DMA((3,)),
        ],
        compiler_params=limits(56),
        cost_estimate=cost(0, 0),
    )(prefix_kv, ws, packed)
    beside = swap(payload, slab_axes, plan.slab, 1)
    across = swap(payload, slab_axes, plan.slab, 2)

    block = min(moves, 128)
    vmem = pl.BlockSpec(memory_space=pltpu.VMEM)
    *normed, mark = pl.pallas_call(
        normalize,
        out_shape=[*[shape((moves // 2, width), BF16)] * 2, pltpu.VMEM((8, HD), F32)],
        in_specs=[untouched(), vmem, untouched()],
        out_specs=[untouched(), untouched(), vmem],
        scratch_shapes=[
            pltpu.VMEM((1, width), F32),
            pltpu.VMEM((3, block, width), BF16),
            pltpu.VMEM((3, block, width), BF16),
            pltpu.SemaphoreType.DMA((3,)),
            pltpu.SemaphoreType.DMA((3,)),
        ],
        compiler_params=limits(58),
        cost_estimate=cost(moves * width, moves * width // 4),
    )(move_table, norm_gain.reshape(width // HD, HD), packed)
    turns = turn_table(prefix_len).reshape(line, 1, plan.pairs, 2)
    turns = np.tile(turns, (1, plan.mine, 1, 1)).reshape(line, plan.mine * plan.pairs, 2)
    flat = weights.transpose(1, 0, 2).reshape(plan.rows, width) if depth % HD else weights
    sent = (moves // HD * (plan.q_rows + 2 * plan.mine), HD) if plan.direct else (line, plan.line_rows, moves)
    outs = (shape(sent, BF16), shape((plan.mine, moves), F32))
    across = tied(across, mark)
    diagonal = swap(across, slab_axes, plan.slab, 1)
    full = shape((plan.peers, plan.rows, depth), BF16) if plan.tight else shape(flat.shape, BF16)
    filled, listed = (), None
    for step, after in enumerate((across, beside)):
        made = local_call(
            functools.partial(project, plan, step * moves // 2, step == 0),
            place,
            (flat, normed[step], jnp.asarray(turns), after, *filled),
            [*outs, *([shape((plan.share, plan.slots), F32), full] if step == 0 else [])],
            (),
            20,
            (3,),
            moves * width * 1024,
            moves * width,
            {5: 0, 6: 1} if filled else None,
        )
        filled = made[:2]
        if step == 0:
            listed, flat = made[2:]
    queries, own_values = filled
    other = swap(listed, slab_axes, plan.slab, pair)
    if plan.direct:
        queries = [queries] + [swap(queries, "line", line, step) for step in range(1, line)]
    else:
        queries = lax.all_to_all(queries, "line", split_axis=0, concat_axis=0, tiled=True)
        queries = [queries.reshape(line * plan.line_rows, moves)]

    query_rows = plan.mine * HD
    back = plan.peers * lax.axis_size("tensor")
    chosen, folds, slot_row = local_call(
        functools.partial(prepare, plan),
        place,
        (board_row, listed, other, payload, beside, across),
        (
            shape((boards_here, moves, plan.slab * plan.slots), BF16),
            shape((plan.slab - 1, boards_here, prefix_len, plan.mine * plan.slots), F32),
            shape((1, row_count), jnp.int32),
        ),
        mib=20,
        flops=10**9,
        nbytes=10**6,
    )
    parts = local_call(
        functools.partial(attend, plan),
        place,
        (own_values, listed, other, chosen, folds, payload, beside, across, diagonal, *queries),
        shape((groups, back, plan.share, plan.slots), BF16),
        [
            pltpu.VMEM((query_rows + 16, moves), BF16),
            pltpu.VMEM((16, moves), F32),
            pltpu.VMEM((plan.slab, boards_here, plan.slots), F32),
            pltpu.VMEM((query_rows + 16, plan.slab * plan.slots), F32),
            pltpu.VMEM((query_rows + 16, plan.slab * plan.slots), F32),
        ],
        24,
    )
    parts = lax.all_to_all(
        parts.reshape(groups * back, plan.share, plan.slots),
        ("groups", "line", "pair", "tensor"),
        split_axis=0,
        concat_axis=0,
        tiled=True,
    )
    parts = parts.reshape(groups, line, back // line, plan.share, plan.slots)
    logprob = pl.pallas_call(
        functools.partial(finish, plan), out_shape=shape((1, row_count), F32), compiler_params=limits(VMEM_MIB)
    )(parts, board_row, slot_row)
    return logprob.reshape(row_count)


def solution(mesh):
    order = ("groups", "dp", "tensor")
    assert mesh.axis_names == order
    pair = 2
    groups, peers, tensor = (mesh.shape[name] for name in order)
    fine = Mesh(mesh.devices.reshape(groups, peers // pair, pair, tensor), ("groups", "line", "pair", "tensor"))
    rows = ("groups", "line", "pair")
    placed = (
        P(rows, None, "tensor"),
        P(rows),
        P(rows, None),
        P(),
        P(),
        P(("line", "pair"), "tensor"),
        P(("line", "pair"), "tensor"),
        P("tensor"),
    )
    return jax.shard_map(per_device, mesh=fine, in_specs=placed, out_specs=P(rows), check_vma=False)
```

```python
import functools
import math

import jax
import jax.numpy as jnp
import numpy as np
from jax import lax
from jax.experimental import pallas as pl
from jax.experimental.pallas import tpu as pltpu
from jax.sharding import Mesh
from jax.sharding import PartitionSpec as P

HD = 128
HALF = HD // 2
EPS = 1e-06
THETA = 5000000.0
DEAD = -1e30
VMEM_MIB = 52
GROUP, LINE, PEER, SLAB = range(4)

F32 = jnp.float32
BF16 = jnp.bfloat16

NN = (((1,), (0,)), ((), ()))
NT = (((1,), (1,)), ((), ()))
TN = (((0,), (0,)), ((), ()))


def matmul(a, b, dims=NN):
    return lax.dot_general(a, b, dims, preferred_element_type=F32)


def limits(mib):
    return pltpu.CompilerParams(vmem_limit_bytes=mib * 1024 * 1024)


class Plan:
    def __init__(self, groups, line, pair, heads, capacity, share, depth):
        self.groups, self.line, self.pair = groups, line, pair
        self.peers = line * pair
        self.slab = groups * pair
        self.heads = heads
        self.mine = heads // self.slab
        self.pairs = HALF // line
        self.q_rows = self.mine * 2 * self.pairs
        self.k_rows = 2 * self.pairs
        self.fold_at = self.q_rows + self.k_rows
        self.list_at = self.fold_at + self.mine
        self.rows = -(-(self.list_at + 1) // 8) * 8
        self.line_rows = -(-(self.q_rows + 2 * self.mine) // 8) * 8
        self.capacity = capacity
        self.share = share
        self.slots = self.peers * capacity
        self.direct = line <= 4
        self.tight = self.pairs % 16 == 0 and depth % HD == 0
        self.chunks = depth // HD
        last = -(-(self.mine + 1) * self.chunks // 16) * 16
        self.sent = (self.fold_at * self.chunks + last, HD) if self.tight else (self.rows, depth)


def pack_weights(plan, place_ref, wq_hbm, wkv_hbm, ws_hbm, board_hbm, ids_hbm, *rest):
    out_hbm, wq, wkv, ws_ref, board_ref, ids_ref, pick, made, ends, sems, out_sems = rest
    group = place_ref[0]
    half_cols = wq.shape[1]
    columns_here = pl.ds(pl.multiple_of(group * half_cols, HD), half_cols)
    copies = (
        pltpu.make_async_copy(ws_hbm, ws_ref, sems.at[0]),
        pltpu.make_async_copy(board_hbm, board_ref, sems.at[1]),
        pltpu.make_async_copy(ids_hbm, ids_ref, sems.at[2]),
        pltpu.make_async_copy(wq_hbm.at[:, columns_here], wq, sems.at[3]),
        pltpu.make_async_copy(wkv_hbm, wkv, sems.at[4]),
    )
    for copy in copies:
        copy.start()

    def send(part):
        source, first = ((made, 0), (ends, made.shape[1]))[part]
        return pltpu.make_async_copy(source, out_hbm.at[:, pl.ds(first, source.shape[1])], out_sems.at[part])

    if plan.tight:
        for copy in copies[3:]:
            copy.wait()
        turn_weights(plan, wq, wkv, made)
        send(0).start()
    for copy in copies[:3]:
        copy.wait()
    count, depth = board_ref.shape[1], wq.shape[0]
    board_row = board_ref[...]
    board_col = jnp.broadcast_to(board_row.astype(F32), (8, count)).T[:, 0:1].astype(jnp.int32)
    own = lax.broadcasted_iota(jnp.int32, (count, count), 0)
    other = lax.broadcasted_iota(jnp.int32, (count, count), 1)
    ahead = jnp.where((board_col == board_row) & (other < own), 1.0, 0.0)
    rank = jnp.sum(ahead, axis=1, keepdims=True).astype(jnp.int32)
    move = ids_ref[...] + 1
    boards, span = plan.line * plan.share, plan.share * plan.capacity
    member = lax.broadcasted_iota(jnp.int32, (boards, count), 0) == board_row
    parts = [jnp.where(member, part.astype(F32), 0.0) for part in (move // 64, move % 64)]
    lane = lax.broadcasted_iota(jnp.int32, (count, depth), 1)
    ranked = jnp.where(rank == (lane % span) % plan.capacity, 1.0, 0.0).astype(BF16)
    found = matmul(jnp.concatenate(parts, axis=0).astype(BF16), ranked)
    lane = lax.broadcasted_iota(jnp.int32, (2 * boards, depth), 1)
    row = lax.broadcasted_iota(jnp.int32, (2 * boards, depth), 0)
    keep = (row // boards == lane // span) & (row % plan.share == (lane % span) // plan.capacity)
    found = jnp.where(keep, found, 0.0)
    lists = []
    for line in range(plan.line):
        at = line * plan.share
        both = found[at : at + plan.share] + found[boards + at : boards + at + plan.share]
        lists.append(jnp.sum(both, axis=0, keepdims=True))

    if plan.tight:
        last_rows(plan, group, lists, wkv, ws_ref, ends)
        send(1).start()
        send(0).wait()
        send(1).wait()
    else:
        pick_weights(plan, group, lists, copies[3:], wq, wkv, ws_ref, made, pick)
        copy = pltpu.make_async_copy(made, out_hbm, out_sems.at[0])
        copy.start()
        copy.wait()


def turn_weights(plan, wq, wkv, out_ref):
    q = wq[...].T
    k = wkv[:, :HD].T
    pairs = plan.pairs
    for pair in range(plan.pair):
        for line in range(plan.line):
            peer = line * plan.pair + pair
            for c in range(plan.chunks):
                lane = slice(c * HD, (c + 1) * HD)
                for part in range(2):
                    entry = part * HALF + line * pairs
                    for h in range(plan.mine):
                        at = c * plan.fold_at + (part * plan.mine + h) * pairs
                        source = (pair * plan.mine + h) * HD + entry
                        out_ref[peer, at : at + pairs] = q[source : source + pairs, lane]
                    at = c * plan.fold_at + plan.q_rows + part * pairs
                    out_ref[peer, at : at + pairs] = k[entry : entry + pairs, lane]


def last_rows(plan, group, lists, wkv, ws_ref, out_ref):
    folds = matmul(ws_ref[...], wkv[:, HD:], NT)
    row = lax.broadcasted_iota(jnp.int32, folds.shape, 0)
    lanes = [slice(c * HD, (c + 1) * HD) for c in range(plan.chunks)]
    zeros = jnp.zeros((out_ref.shape[1] - (plan.mine + 1) * plan.chunks, HD), F32)
    for pair in range(plan.pair):
        first = (group * plan.pair + pair) * plan.mine
        mine = [jnp.sum(jnp.where(row == first + h, folds, 0.0), axis=0, keepdims=True) for h in range(plan.mine)]
        for line in range(plan.line):
            last = [values[:, lane] for values in (*mine, lists[line]) for lane in lanes]
            out_ref[line * plan.pair + pair] = jnp.concatenate([*last, zeros], axis=0).astype(BF16)


def pick_weights(plan, group, lists, copies, wq, wkv, ws_ref, out_ref, pick):
    rows, half_cols = plan.rows, wq.shape[1]
    r = lax.broadcasted_iota(jnp.int32, (rows, 1), 0)
    part = r // (plan.mine * plan.pairs)
    head = (r // plan.pairs) % plan.mine
    entry = r % plan.pairs
    is_q = r < plan.q_rows
    k_at = r - plan.q_rows
    is_k = (k_at >= 0) & (k_at < plan.k_rows)
    f_at = r - plan.fold_at
    is_f = (f_at >= 0) & (f_at < plan.mine)
    q_lane = lax.broadcasted_iota(jnp.int32, (rows, half_cols), 1)
    k_lane = lax.broadcasted_iota(jnp.int32, (rows, HD), 1)
    ws = ws_ref[...].astype(F32)

    def fill(peer, carry):
        line, pair = peer // plan.pair, peer % plan.pair
        column = (pair * plan.mine + head) * HD + part * HALF + line * plan.pairs + entry
        column = jnp.where(is_q, column, -1)
        at = pl.ds(pl.multiple_of(peer * rows, 8), rows)
        pick[at, :half_cols] = jnp.where(q_lane == column, 1.0, 0.0)
        k_column = (k_at // plan.pairs) * HALF + line * plan.pairs + k_at % plan.pairs
        k_column = jnp.where(is_k, k_column, -1)
        pick[at, half_cols : half_cols + HD] = jnp.where(k_lane == k_column, 1.0, 0.0)
        fold = jnp.zeros((rows, HD), F32)
        my_head = jnp.where(is_f, (group * plan.pair + pair) * plan.mine + f_at, -1)
        for h in range(plan.heads):
            fold = jnp.where(my_head == h, ws[h : h + 1], fold)
        pick[at, half_cols + HD :] = fold
        return carry

    lax.fori_loop(0, plan.peers, fill, 0, unroll=plan.peers <= 8)

    for copy in copies:
        copy.wait()
    left = pick[...].astype(BF16)
    total = matmul(left[:, :half_cols], wq[...], NT) + matmul(left[:, half_cols:], wkv[...], NT)
    for peer in range(plan.peers):
        mine = total[peer * rows : (peer + 1) * rows]
        out_ref[peer] = jnp.where(r == plan.list_at, lists[peer // plan.pair], mine).astype(BF16)


def normalize(table_hbm, gain_ref, after_ref, *refs):
    *outs, mark_ref, gain, buffers, made, sems, out_sems = refs
    held, block, _ = buffers.shape
    steps = table_hbm.shape[0] // block
    each = outs[0].shape[0] // block

    def copy(step):
        source = table_hbm.at[pl.ds(step * block, block)]
        return pltpu.make_async_copy(source, buffers.at[step % held], sems.at[step % held])

    def store(step):
        target = outs[step // each].at[pl.ds(step % each * block, block)]
        return pltpu.make_async_copy(made.at[step % held], target, out_sems.at[step % held])

    for step in range(min(held, steps)):
        copy(step).start()
    rows = gain_ref[...].astype(F32)
    gain[...] = jnp.concatenate([rows[r : r + 1] for r in range(rows.shape[0])], axis=1)
    for step in range(steps):
        copy(step).wait()
        if step >= held:
            store(step - held).wait()
        raw = buffers[step % held].astype(F32)
        inverse = lax.rsqrt(jnp.mean(raw * raw, axis=-1, keepdims=True) + EPS)
        made[step % held] = (raw * inverse * gain[...]).astype(BF16)
        store(step).start()
        if step + held < steps:
            copy(step + held).start()
    for step in range(max(0, steps - held), steps):
        store(step).wait()
    mark_ref[...] = jnp.zeros_like(mark_ref)


def spread_weights(plan, w_ref, full_ref):
    lists = []
    for s in range(plan.peers):
        for c in range(plan.chunks):
            rows = w_ref[s, c * plan.fold_at : (c + 1) * plan.fold_at]
            full_ref[s, : plan.fold_at, c * HD : (c + 1) * HD] = rows
        last = w_ref[s, plan.fold_at * plan.chunks :].astype(F32)
        last = [
            jnp.concatenate([last[i * plan.chunks + c : i * plan.chunks + c + 1] for c in range(plan.chunks)], axis=1)
            for i in range(plan.mine + 1)
        ]
        zeros = jnp.zeros((plan.rows - plan.list_at, last[0].shape[1]), F32)
        full_ref[s, plan.fold_at :] = jnp.concatenate([*last[: plan.mine], zeros], axis=0).astype(BF16)
        lists.append(last[plan.mine])
    return jnp.concatenate(lists, axis=0)


def list_rows(plan, w_ref):
    if len(w_ref.shape) == 3:
        rows = [w_ref[s].astype(F32)[plan.list_at : plan.list_at + 1] for s in range(plan.peers)]
    else:
        row = w_ref[...].astype(F32)[plan.list_at : plan.list_at + 1]
        span = plan.share * plan.capacity
        rows = [row[:, s * 2 * span : (s + 1) * 2 * span] for s in range(plan.peers)]
    return jnp.concatenate(rows, axis=0)


def read_lists(plan, rows, out_ref):
    share, capacity, peers = plan.share, plan.capacity, plan.peers
    span = share * capacity
    lane = lax.broadcasted_iota(jnp.int32, (share * peers, 2 * span), 1)
    row = lax.broadcasted_iota(jnp.int32, (share * peers, 2 * span), 0)
    lane = jnp.where(lane < span, lane, lane - span)
    spread = jnp.concatenate([rows] * share, axis=0)
    spread = jnp.where(lane // capacity == row // peers, spread, 0.0).astype(BF16)
    c = lax.broadcasted_iota(jnp.int32, (2 * span, plan.slots), 0)
    slot = lax.broadcasted_iota(jnp.int32, (2 * span, plan.slots), 1)
    scale = jnp.where(c < span, 64.0, 1.0)
    place = jnp.where(c % capacity == slot % capacity, scale, 0.0).astype(BF16)
    listed = matmul(spread, place)
    row = lax.broadcasted_iota(jnp.int32, listed.shape, 0)
    slot = lax.broadcasted_iota(jnp.int32, listed.shape, 1)
    listed = jnp.where(slot // capacity == row % peers, listed, 0.0)
    out_ref[...] = jnp.sum(listed.reshape(share, peers, plan.slots), axis=1)


def project(plan, place, lists, place_ref, w_ref, normed_ref, turn_ref, after_ref, *refs):
    if lists:
        *refs, list_ref, full_ref = refs
        if plan.tight:
            rows = spread_weights(plan, w_ref, full_ref)
            w_ref = full_ref
        else:
            rows = list_rows(plan, w_ref)
            full_ref[...] = w_ref[...]
        read_lists(plan, rows, list_ref)
    q_ref, vo_ref = refs[-2:]
    turns = turn_ref[place_ref[LINE]]
    half, k_half = plan.q_rows // 2, plan.k_rows // 2
    cosine, sine = turns[:, 0:1], turns[:, 1:2]
    cos_k, sin_k = cosine[:k_half], sine[:k_half]
    moves = normed_ref.shape[0]
    block = min(moves, HD)
    every = []
    for start in range(0, moves, block):
        at, to = slice(start, start + block), slice(place + start, place + start + block)
        if len(w_ref.shape) == 3:
            depth = w_ref.shape[2]
            total = None
            for s in range(w_ref.shape[0]):
                term = matmul(w_ref[s], normed_ref[at, s * depth : (s + 1) * depth], NT)
                total = term if total is None else total + term
        else:
            total = matmul(w_ref[...], normed_ref[at, :], NT)
        first, second = total[:half], total[half : 2 * half]
        f_first = (first * cosine - second * sine).astype(BF16).astype(F32)
        f_second = (second * cosine + first * sine).astype(BF16).astype(F32)
        first, second = total[plan.q_rows : plan.q_rows + k_half], total[plan.q_rows + k_half : plan.fold_at]
        k_first = (first * cos_k - second * sin_k).astype(BF16).astype(F32)
        k_second = (second * cos_k + first * sin_k).astype(BF16).astype(F32)
        logits, tails = [], []
        for h in range(plan.mine):
            own = slice(h * k_half, (h + 1) * k_half)
            logit = jnp.sum(f_first[own] * k_first + f_second[own] * k_second, axis=0, keepdims=True)
            logits.append(logit.astype(BF16).astype(F32))
            tails.append(logit - logits[-1])
        if plan.direct:
            chunk = (place + start) // block * plan.q_rows
            q_ref[chunk : chunk + plan.q_rows] = jnp.concatenate([f_first, f_second], axis=0).astype(BF16)
            every += [*logits, *tails]
        else:
            pad = plan.line_rows - plan.q_rows - 2 * plan.mine
            pieces = [f_first, f_second, *logits, *tails]
            if pad:
                pieces.append(jnp.zeros((pad, block), F32))
            out = jnp.concatenate(pieces, axis=0).astype(BF16)
            for line in range(plan.line):
                q_ref[line, :, to] = out
        vo_ref[:, to] = total[plan.fold_at : plan.list_at]
    if plan.direct:
        first = vo_ref.shape[1] // HD * plan.q_rows + place // block * 2 * plan.mine
        q_ref[first : first + len(every)] = jnp.concatenate(every, axis=0).astype(BF16)


def tied(x, *others):
    return pl.pallas_call(
        lambda *refs: None,
        out_shape=shape(x.shape, x.dtype),
        in_specs=[untouched()] + [pl.BlockSpec(memory_space=pltpu.VMEM)] * len(others),
        out_specs=untouched(),
        input_output_aliases={0: 0},
        compiler_params=limits(1),
        cost_estimate=cost(0, 0),
    )(x, *others)


def pack_prefix(plan, prefix_hbm, ws_hbm, after_ref, out_ref, *scratch):
    values, ws_ref, sems = scratch
    boards = values.shape[0]
    heads = plan.heads
    copies = (
        pltpu.make_async_copy(ws_hbm, ws_ref, sems.at[0]),
        pltpu.make_async_copy(prefix_hbm.at[:, :, pl.ds(HD, HD)], values, sems.at[1]),
        pltpu.make_async_copy(prefix_hbm.at[:, :, pl.ds(0, HD)], out_ref.at[pl.ds(0, boards)], sems.at[2]),
    )
    for copy in copies:
        copy.start()
    copies[0].wait()
    span = HD // boards
    ws = jnp.concatenate([ws_ref[...].astype(F32)] * (HD // heads), axis=0)
    row = lax.broadcasted_iota(jnp.int32, (HD, 1), 0)
    copies[1].wait()
    fold = None
    for board in range(boards):
        keep = (row // span == board) & (row % span < 2 * heads)
        term = matmul(values[board], jnp.where(keep, ws, 0.0).astype(BF16), NT)
        fold = term if fold is None else fold + term
    rounded = fold.astype(BF16).astype(F32)
    lane = lax.broadcasted_iota(jnp.int32, fold.shape, 1)
    out_ref[boards] = jnp.where(lane % span < heads, rounded, fold - rounded).astype(BF16)
    copies[2].wait()


def fold_columns(plan, here, block, board, boards, heads):
    lanes = plan.mine * plan.slots
    row = lax.broadcasted_iota(jnp.int32, (HD, lanes), 0) - board * (HD // boards)
    head = here * plan.mine + lax.broadcasted_iota(jnp.int32, (HD, lanes), 1) // plan.slots
    pick = jnp.where((row == head) | (row == head + heads), 1.0, 0.0).astype(BF16)
    return matmul(block, pick)


def prepare(plan, place_ref, board_ref, own_ref, other_ref, *rest):
    *prefix_refs, chosen_ref, fold_ref, slot_ref = rest
    count = board_ref.shape[1]
    board_row = board_ref[...]
    board_col = jnp.broadcast_to(board_row.astype(F32), (8, count)).T[:, 0:1].astype(jnp.int32)
    ahead = lax.broadcasted_iota(jnp.int32, (count, count), 0) < lax.broadcasted_iota(jnp.int32, (count, count), 1)
    rank = jnp.sum(jnp.where((board_col == board_row) & ahead, 1.0, 0.0), axis=0, keepdims=True)
    slot_ref[...] = rank.astype(jnp.int32) + place_ref[PEER] * plan.capacity
    here = place_ref[SLAB]
    boards, moves = chosen_ref.shape[0], chosen_ref.shape[1]
    move_at = lax.broadcasted_iota(jnp.int32, (moves, plan.slots), 0) + 1

    def step(board, carry):
        for j in range(plan.slab):
            place = ((here ^ j) % plan.pair) * boards + board
            row = (own_ref, other_ref)[j // plan.pair][pl.ds(place, 1), :].astype(jnp.int32)
            at = slice(j * plan.slots, (j + 1) * plan.slots)
            chosen_ref[board, :, at] = jnp.where(move_at == row, 1.0, 0.0).astype(BF16)
        for j, prefix_ref in enumerate(prefix_refs):
            fold_ref[j, board] = fold_columns(plan, here, prefix_ref[boards], board, boards, plan.heads)
        return carry

    lax.fori_loop(0, boards, step, 0)


def attend(plan, place_ref, vo_ref, own_ref, other_ref, chosen_ref, fold_ref, *rest):
    prefix_refs, rest = rest[: plan.slab], rest[plan.slab :]
    *q_refs, out_ref, table, extra, scores, taken_even, taken_odd = rest
    here = place_ref[SLAB]
    mine, heads, slots = plan.mine, plan.heads, plan.slots
    moves = vo_ref.shape[1]
    boards = prefix_refs[0].shape[0] - 1
    query_rows = mine * HD

    mixed = own_logits = None
    for step, q_ref in enumerate(q_refs):
        if plan.direct:
            chunks = range(moves // HD)
            values = jnp.concatenate([q_ref[c * plan.q_rows : (c + 1) * plan.q_rows] for c in chunks], axis=1)
            tails = q_ref[moves // HD * plan.q_rows :].astype(F32)
            tails = jnp.concatenate([tails[c * 2 * mine : (c + 1) * 2 * mine] for c in chunks], axis=1)
            tails = tails[:mine] + tails[mine:]
            own_logits = tails if own_logits is None else own_logits + tails
        else:
            values = q_ref[...]
        r = lax.broadcasted_iota(jnp.int32, (query_rows + 8, values.shape[0]), 0)
        c = lax.broadcasted_iota(jnp.int32, (query_rows + 8, values.shape[0]), 1)
        line, at = (place_ref[LINE] ^ step, c) if plan.direct else (c // plan.line_rows, c % plan.line_rows)
        part, head, entry = at // (mine * plan.pairs), (at // plan.pairs) % mine, at % plan.pairs
        goes = jnp.where(at < plan.q_rows, head * HD + part * HALF + line * plan.pairs + entry, -1)
        tail = at - plan.q_rows
        goes = jnp.where((tail >= 0) & (tail < 2 * mine), query_rows + tail % mine, goes)
        term = matmul(jnp.where(r == goes, 1.0, 0.0).astype(BF16), values)
        mixed = term if mixed is None else mixed + term
    if own_logits is None:
        own_logits = mixed[query_rows : query_rows + mine]
    table[:query_rows] = mixed[:query_rows].astype(BF16)
    extra[...] = jnp.zeros_like(extra)
    for place, value in ((0, own_logits), (2 * mine, vo_ref[...])):
        rounded = value.astype(BF16).astype(F32)
        extra[place : place + mine] = rounded
        extra[place + mine : place + 2 * mine] = value - rounded
    table[query_rows:] = extra[...].astype(BF16)

    scale = math.log2(math.e) / math.sqrt(HD)
    def per_head(x, base):
        pieces = [x[base + h : base + h + 1] + x[base + mine + h : base + mine + h + 1] for h in range(mine)]
        return jnp.concatenate(pieces, axis=1)

    def moves_of(j, board):
        place = ((here ^ j) % plan.pair) * boards + board
        return (own_ref, other_ref)[j // plan.pair][pl.ds(place, 1), :].astype(jnp.int32)

    def gather(board, taken):
        taken[...] = matmul(table[...], chosen_ref[board])

    def score_board(board, taken):
        for j in range(plan.slab):
            x = taken[:, j * slots : (j + 1) * slots]
            q = jnp.concatenate([x[h * HD : (h + 1) * HD].astype(BF16) for h in range(mine)], axis=1)
            logits = matmul(prefix_refs[j][board], q)
            if j < plan.slab - 1:
                fold = fold_ref[j, board]
            else:
                fold = fold_columns(plan, here, prefix_refs[j][boards], board, boards, heads)
            own_logit = per_head(x, query_rows)
            own_value = per_head(x, query_rows + 2 * mine)
            peak = jnp.maximum(jnp.max(logits, axis=0, keepdims=True), own_logit)
            weight = jnp.exp2((logits - peak) * scale)
            own_weight = jnp.exp2((own_logit - peak) * scale)
            denom = jnp.sum(weight, axis=0, keepdims=True) + own_weight
            value = (jnp.sum(weight * fold, axis=0, keepdims=True) + own_value * own_weight) / denom
            score = sum(value[:, h * slots : (h + 1) * slots] for h in range(mine))
            scores[here ^ j, pl.ds(board, 1), :] = jnp.where(moves_of(j, board) > 0, score, DEAD)

    gather(0, taken_even)

    def step(at, carry):
        board = 2 * at
        gather(jnp.minimum(board + 1, boards - 1), taken_odd)
        score_board(board, taken_even)
        gather(jnp.minimum(board + 2, boards - 1), taken_even)
        score_board(jnp.minimum(board + 1, boards - 1), taken_odd)
        return carry

    lax.fori_loop(0, -(-boards // 2), step, 0)
    live = scores[...] > 0.5 * DEAD
    count = jnp.sum(jnp.where(live, 1.0, 0.0), axis=2, keepdims=True)
    mean = jnp.sum(jnp.where(live, scores[...], 0.0), axis=2, keepdims=True) / jnp.maximum(count, 1.0)
    centered = jnp.where(live, scores[...] - mean, DEAD)
    for g in range(plan.groups):
        both = jnp.concatenate([centered[g * plan.pair + p] for p in range(plan.pair)], axis=0).astype(BF16)
        for copy in range(out_ref.shape[1]):
            out_ref[g, copy] = both


def finish(plan, parts_ref, board_ref, slot_ref, out_ref):
    line = parts_ref.shape[1]
    columns = []
    for at in range(line):
        total = None
        for g in range(parts_ref.shape[0]):
            for p in range(parts_ref.shape[2]):
                term = parts_ref[g, at, p].astype(F32)
                total = term if total is None else total + term
        columns.append(total)
    scores = jnp.concatenate(columns, axis=0)
    live = scores > 0.5 * DEAD
    peak = jnp.max(scores, axis=1, keepdims=True)
    denom = jnp.sum(jnp.where(live, jnp.exp(scores - peak), 0.0), axis=1, keepdims=True)
    logprob = jnp.where(live, scores - peak - jnp.log(denom), 0.0)
    count = board_ref.shape[1]
    member = lax.broadcasted_iota(jnp.int32, (scores.shape[0], count), 0) == board_ref[...]
    member = jnp.where(member, 1.0, 0.0).astype(BF16)
    found = jnp.zeros((plan.slots, count), F32)
    for _ in range(3):
        rounded = logprob.astype(BF16)
        found = found + matmul(rounded, member, TN)
        logprob = logprob - rounded.astype(F32)
    at = lax.broadcasted_iota(jnp.int32, (plan.slots, count), 0) == slot_ref[...]
    out_ref[...] = jnp.sum(jnp.where(at, found, 0.0), axis=0, keepdims=True)


def untouched():
    return pl.BlockSpec(memory_space=pl.ANY)


def local_call(kernel, place, args, outs, scratch=(), mib=40, copied=(), flops=0, nbytes=0, aliases=None):
    vmem = pl.BlockSpec(memory_space=pltpu.VMEM)
    return pl.pallas_call(
        kernel,
        out_shape=outs,
        in_specs=[pl.BlockSpec(memory_space=pltpu.SMEM)]
        + [untouched() if at in copied else vmem for at in range(len(args))],
        out_specs=jax.tree.map(lambda x: vmem, outs),
        scratch_shapes=scratch,
        input_output_aliases=aliases or {},
        compiler_params=limits(mib),
        cost_estimate=cost(flops, nbytes),
    )(place, *args)


def cost(flops, nbytes):
    return pl.CostEstimate(flops=int(flops), bytes_accessed=int(nbytes), transcendentals=0)


def swap(x, names, size, step):
    return lax.ppermute(x, names, [(at, at ^ step) for at in range(size)])


def shape(dims, dtype):
    return jax.ShapeDtypeStruct(tuple(dims), dtype)


def turn_table(position):
    frequency = THETA ** (-2.0 * np.arange(HALF, dtype=np.float32) / HD)
    angles = np.float32(position) * frequency.astype(np.float32)
    return np.stack([np.cos(angles), np.sin(angles)], axis=1).astype(np.float32)


def per_device(prefix_kv, move_ids, move_board, move_table, norm_gain, w_query, w_keyval, w_score):
    row_count = move_ids.shape[0]
    boards_here, prefix_len, _ = prefix_kv.shape
    moves, width = move_table.shape
    groups, line, pair = lax.axis_size("groups"), lax.axis_size("line"), lax.axis_size("pair")
    board_total = boards_here * line * pair
    capacity = max(2, (2 * row_count + board_total - 1) // board_total)
    heads = w_query.shape[1] // HD
    depth = w_query.shape[0]
    plan = Plan(groups, line, pair, heads, capacity, pair * boards_here, depth)
    group_at = lax.axis_index("groups").astype(jnp.int32)
    line_at = lax.axis_index("line").astype(jnp.int32)
    pair_at = lax.axis_index("pair").astype(jnp.int32)
    place = jnp.stack([group_at, line_at, line_at * pair + pair_at, group_at * pair + pair_at])
    ws = w_score.reshape(heads, HD)
    slab_axes = ("groups", "pair")
    board_row = move_board.reshape(1, row_count)

    half_cols = w_query.shape[1] // groups
    turned = plan.fold_at * plan.chunks if plan.tight else plan.sent[0]
    made = [pltpu.VMEM((plan.peers, size, plan.sent[1]), BF16) for size in (turned, max(16, plan.sent[0] - turned))]
    packed = pl.pallas_call(
        functools.partial(pack_weights, plan),
        out_shape=shape((plan.peers, *plan.sent), BF16),
        in_specs=[pl.BlockSpec(memory_space=pltpu.SMEM)] + [untouched()] * 5,
        out_specs=untouched(),
        scratch_shapes=[
            pltpu.VMEM((depth, half_cols), BF16),
            pltpu.VMEM((depth, 2 * HD), BF16),
            pltpu.VMEM((heads, HD), BF16),
            pltpu.VMEM((1, row_count), jnp.int32),
            pltpu.VMEM((1, row_count), jnp.int32),
            pltpu.VMEM((plan.peers * plan.rows, half_cols + 2 * HD), F32),
            *made,
            pltpu.SemaphoreType.DMA((5,)),
            pltpu.SemaphoreType.DMA((2,)),
        ],
        compiler_params=limits(62),
        cost_estimate=cost(0, 0),
    )(group_at.reshape(1), w_query, w_keyval, ws, board_row, move_ids.reshape(1, row_count))
    weights = lax.all_to_all(packed, ("line", "pair"), split_axis=0, concat_axis=0, tiled=True)

    payload = pl.pallas_call(
        functools.partial(pack_prefix, plan),
        out_shape=shape((boards_here + 1, prefix_len, HD), BF16),
        in_specs=[untouched()] * 3,
        out_specs=pl.BlockSpec(memory_space=pltpu.VMEM),
        scratch_shapes=[
            pltpu.VMEM((boards_here, prefix_len, HD), BF16),
            pltpu.VMEM((heads, HD), BF16),
            pltpu.SemaphoreType.DMA((3,)),
        ],
        compiler_params=limits(56),
        cost_estimate=cost(0, 0),
    )(prefix_kv, ws, packed)
    beside = swap(payload, slab_axes, plan.slab, 1)
    across = swap(payload, slab_axes, plan.slab, 2)

    block = min(moves, 128)
    vmem = pl.BlockSpec(memory_space=pltpu.VMEM)
    *normed, mark = pl.pallas_call(
        normalize,
        out_shape=[*[shape((moves // 2, width), BF16)] * 2, pltpu.VMEM((8, HD), F32)],
        in_specs=[untouched(), vmem, untouched()],
        out_specs=[untouched(), untouched(), vmem],
        scratch_shapes=[
            pltpu.VMEM((1, width), F32),
            pltpu.VMEM((3, block, width), BF16),
            pltpu.VMEM((3, block, width), BF16),
            pltpu.SemaphoreType.DMA((3,)),
            pltpu.SemaphoreType.DMA((3,)),
        ],
        compiler_params=limits(58),
        cost_estimate=cost(moves * width, moves * width // 4),
    )(move_table, norm_gain.reshape(width // HD, HD), packed)
    turns = turn_table(prefix_len).reshape(line, 1, plan.pairs, 2)
    turns = np.tile(turns, (1, plan.mine, 1, 1)).reshape(line, plan.mine * plan.pairs, 2)
    flat = weights.transpose(1, 0, 2).reshape(plan.rows, width) if depth % HD else weights
    sent = (moves // HD * (plan.q_rows + 2 * plan.mine), HD) if plan.direct else (line, plan.line_rows, moves)
    outs = (shape(sent, BF16), shape((plan.mine, moves), F32))
    across = tied(across, mark)
    diagonal = swap(across, slab_axes, plan.slab, 1)
    full = shape((plan.peers, plan.rows, depth), BF16) if plan.tight else shape(flat.shape, BF16)
    filled, listed = (), None
    for step, after in enumerate((across, beside)):
        made = local_call(
            functools.partial(project, plan, step * moves // 2, step == 0),
            place,
            (flat, normed[step], jnp.asarray(turns), after, *filled),
            [*outs, *([shape((plan.share, plan.slots), F32), full] if step == 0 else [])],
            (),
            20,
            (3,),
            moves * width * 1024,
            moves * width,
            {5: 0, 6: 1} if filled else None,
        )
        filled = made[:2]
        if step == 0:
            listed, flat = made[2:]
    queries, own_values = filled
    other = swap(listed, slab_axes, plan.slab, pair)
    if plan.direct:
        queries = [queries] + [swap(queries, "line", line, step) for step in range(1, line)]
    else:
        queries = lax.all_to_all(queries, "line", split_axis=0, concat_axis=0, tiled=True)
        queries = [queries.reshape(line * plan.line_rows, moves)]

    query_rows = plan.mine * HD
    back = plan.peers * lax.axis_size("tensor")
    chosen, folds, slot_row = local_call(
        functools.partial(prepare, plan),
        place,
        (board_row, listed, other, payload, beside, across),
        (
            shape((boards_here, moves, plan.slab * plan.slots), BF16),
            shape((plan.slab - 1, boards_here, prefix_len, plan.mine * plan.slots), F32),
            shape((1, row_count), jnp.int32),
        ),
        mib=20,
        flops=10**9,
        nbytes=10**6,
    )
    parts = local_call(
        functools.partial(attend, plan),
        place,
        (own_values, listed, other, chosen, folds, payload, beside, across, diagonal, *queries),
        shape((groups, back, plan.share, plan.slots), BF16),
        [
            pltpu.VMEM((query_rows + 16, moves), BF16),
            pltpu.VMEM((16, moves), F32),
            pltpu.VMEM((plan.slab, boards_here, plan.slots), F32),
            pltpu.VMEM((query_rows + 16, plan.slab * plan.slots), F32),
            pltpu.VMEM((query_rows + 16, plan.slab * plan.slots), F32),
        ],
        24,
    )
    parts = lax.all_to_all(
        parts.reshape(groups * back, plan.share, plan.slots),
        ("groups", "line", "pair", "tensor"),
        split_axis=0,
        concat_axis=0,
        tiled=True,
    )
    parts = parts.reshape(groups, line, back // line, plan.share, plan.slots)
    logprob = pl.pallas_call(
        functools.partial(finish, plan), out_shape=shape((1, row_count), F32), compiler_params=limits(VMEM_MIB)
    )(parts, board_row, slot_row)
    return logprob.reshape(row_count)


def solution(mesh):
    order = ("groups", "dp", "tensor")
    assert mesh.axis_names == order
    pair = 2
    groups, peers, tensor = (mesh.shape[name] for name in order)
    fine = Mesh(mesh.devices.reshape(groups, peers // pair, pair, tensor), ("groups", "line", "pair", "tensor"))
    rows = ("groups", "line", "pair")
    placed = (
        P(rows, None, "tensor"),
        P(rows),
        P(rows, None),
        P(),
        P(),
        P(("line", "pair"), "tensor"),
        P(("line", "pair"), "tensor"),
        P("tensor"),
    )
    return jax.shard_map(per_device, mesh=fine, in_specs=placed, out_specs=P(rows), check_vma=False)
```

```python
import functools
import math

import jax
import jax.numpy as jnp
import numpy as np
from jax import lax
from jax.experimental import pallas as pl
from jax.experimental.pallas import tpu as pltpu
from jax.sharding import Mesh
from jax.sharding import PartitionSpec as P

HD = 128
HALF = HD // 2
EPS = 1e-06
THETA = 5000000.0
DEAD = -1e30
VMEM_MIB = 52
GROUP, LINE, PEER, SLAB = range(4)

F32 = jnp.float32
BF16 = jnp.bfloat16

NN = (((1,), (0,)), ((), ()))
NT = (((1,), (1,)), ((), ()))
TN = (((0,), (0,)), ((), ()))


def matmul(a, b, dims=NN):
    return lax.dot_general(a, b, dims, preferred_element_type=F32)


def limits(mib):
    return pltpu.CompilerParams(vmem_limit_bytes=mib * 1024 * 1024)


class Plan:
    def __init__(self, groups, line, pair, heads, capacity, share, depth):
        self.groups, self.line, self.pair = groups, line, pair
        self.peers = line * pair
        self.slab = groups * pair
        self.heads = heads
        self.mine = heads // self.slab
        self.pairs = HALF // line
        self.q_rows = self.mine * 2 * self.pairs
        self.k_rows = 2 * self.pairs
        self.fold_at = self.q_rows + self.k_rows
        self.list_at = self.fold_at + self.mine
        self.rows = -(-(self.list_at + 1) // 8) * 8
        self.line_rows = -(-(self.q_rows + 2 * self.mine) // 8) * 8
        self.capacity = capacity
        self.share = share
        self.slots = self.peers * capacity
        self.direct = line <= 4
        self.tight = self.pairs % 16 == 0 and depth % HD == 0
        self.chunks = depth // HD
        last = -(-(self.mine + 1) * self.chunks // 16) * 16
        self.sent = (self.fold_at * self.chunks + last, HD) if self.tight else (self.rows, depth)


def pack_weights(plan, place_ref, wq_hbm, wkv_hbm, ws_hbm, board_hbm, ids_hbm, *rest):
    out_ref, wq, wkv, ws_ref, board_ref, ids_ref, pick, sems = rest
    group = place_ref[0]
    half_cols = wq.shape[1]
    columns_here = pl.ds(pl.multiple_of(group * half_cols, HD), half_cols)
    copies = (
        pltpu.make_async_copy(ws_hbm, ws_ref, sems.at[0]),
        pltpu.make_async_copy(board_hbm, board_ref, sems.at[1]),
        pltpu.make_async_copy(ids_hbm, ids_ref, sems.at[2]),
        pltpu.make_async_copy(wq_hbm.at[:, columns_here], wq, sems.at[3]),
        pltpu.make_async_copy(wkv_hbm, wkv, sems.at[4]),
    )
    for copy in copies:
        copy.start()
    for copy in copies[:3]:
        copy.wait()
    count, depth = board_ref.shape[1], wq.shape[0]
    board_row = board_ref[...]
    board_col = jnp.broadcast_to(board_row.astype(F32), (8, count)).T[:, 0:1].astype(jnp.int32)
    own = lax.broadcasted_iota(jnp.int32, (count, count), 0)
    other = lax.broadcasted_iota(jnp.int32, (count, count), 1)
    ahead = jnp.where((board_col == board_row) & (other < own), 1.0, 0.0)
    rank = jnp.sum(ahead, axis=1, keepdims=True).astype(jnp.int32)
    move = ids_ref[...] + 1
    boards, span = plan.line * plan.share, plan.share * plan.capacity
    member = lax.broadcasted_iota(jnp.int32, (boards, count), 0) == board_row
    parts = [jnp.where(member, part.astype(F32), 0.0) for part in (move // 64, move % 64)]
    lane = lax.broadcasted_iota(jnp.int32, (count, depth), 1)
    ranked = jnp.where(rank == (lane % span) % plan.capacity, 1.0, 0.0).astype(BF16)
    found = matmul(jnp.concatenate(parts, axis=0).astype(BF16), ranked)
    lane = lax.broadcasted_iota(jnp.int32, (2 * boards, depth), 1)
    row = lax.broadcasted_iota(jnp.int32, (2 * boards, depth), 0)
    keep = (row // boards == lane // span) & (row % plan.share == (lane % span) // plan.capacity)
    found = jnp.where(keep, found, 0.0)
    lists = []
    for line in range(plan.line):
        at = line * plan.share
        both = found[at : at + plan.share] + found[boards + at : boards + at + plan.share]
        lists.append(jnp.sum(both, axis=0, keepdims=True))

    if plan.tight:
        turn_weights(plan, group, lists, copies[3:], wq, wkv, ws_ref, out_ref)
    else:
        pick_weights(plan, group, lists, copies[3:], wq, wkv, ws_ref, out_ref, pick)


def turn_weights(plan, group, lists, copies, wq, wkv, ws_ref, out_ref):
    for copy in copies:
        copy.wait()
    q = wq[...].T
    k = wkv[:, :HD].T
    folds = matmul(ws_ref[...], wkv[:, HD:], NT)
    row = lax.broadcasted_iota(jnp.int32, folds.shape, 0)
    pairs = plan.pairs
    lanes = [slice(c * HD, (c + 1) * HD) for c in range(plan.chunks)]
    first_last = plan.fold_at * plan.chunks
    zeros = jnp.zeros((plan.sent[0] - first_last - (plan.mine + 1) * plan.chunks, HD), F32)
    for pair in range(plan.pair):
        first = (group * plan.pair + pair) * plan.mine
        mine = [jnp.sum(jnp.where(row == first + h, folds, 0.0), axis=0, keepdims=True) for h in range(plan.mine)]
        for line in range(plan.line):
            peer = line * plan.pair + pair
            for c, lane in enumerate(lanes):
                for part in range(2):
                    entry = part * HALF + line * pairs
                    for h in range(plan.mine):
                        at = c * plan.fold_at + (part * plan.mine + h) * pairs
                        source = (pair * plan.mine + h) * HD + entry
                        out_ref[peer, at : at + pairs] = q[source : source + pairs, lane]
                    at = c * plan.fold_at + plan.q_rows + part * pairs
                    out_ref[peer, at : at + pairs] = k[entry : entry + pairs, lane]
            last = [values[:, lane] for values in (*mine, lists[line]) for lane in lanes]
            out_ref[peer, first_last:] = jnp.concatenate([*last, zeros], axis=0).astype(BF16)


def pick_weights(plan, group, lists, copies, wq, wkv, ws_ref, out_ref, pick):
    rows, half_cols = plan.rows, wq.shape[1]
    r = lax.broadcasted_iota(jnp.int32, (rows, 1), 0)
    part = r // (plan.mine * plan.pairs)
    head = (r // plan.pairs) % plan.mine
    entry = r % plan.pairs
    is_q = r < plan.q_rows
    k_at = r - plan.q_rows
    is_k = (k_at >= 0) & (k_at < plan.k_rows)
    f_at = r - plan.fold_at
    is_f = (f_at >= 0) & (f_at < plan.mine)
    q_lane = lax.broadcasted_iota(jnp.int32, (rows, half_cols), 1)
    k_lane = lax.broadcasted_iota(jnp.int32, (rows, HD), 1)
    ws = ws_ref[...].astype(F32)

    def fill(peer, carry):
        line, pair = peer // plan.pair, peer % plan.pair
        column = (pair * plan.mine + head) * HD + part * HALF + line * plan.pairs + entry
        column = jnp.where(is_q, column, -1)
        at = pl.ds(pl.multiple_of(peer * rows, 8), rows)
        pick[at, :half_cols] = jnp.where(q_lane == column, 1.0, 0.0)
        k_column = (k_at // plan.pairs) * HALF + line * plan.pairs + k_at % plan.pairs
        k_column = jnp.where(is_k, k_column, -1)
        pick[at, half_cols : half_cols + HD] = jnp.where(k_lane == k_column, 1.0, 0.0)
        fold = jnp.zeros((rows, HD), F32)
        my_head = jnp.where(is_f, (group * plan.pair + pair) * plan.mine + f_at, -1)
        for h in range(plan.heads):
            fold = jnp.where(my_head == h, ws[h : h + 1], fold)
        pick[at, half_cols + HD :] = fold
        return carry

    lax.fori_loop(0, plan.peers, fill, 0, unroll=plan.peers <= 8)

    for copy in copies:
        copy.wait()
    left = pick[...].astype(BF16)
    total = matmul(left[:, :half_cols], wq[...], NT) + matmul(left[:, half_cols:], wkv[...], NT)
    for peer in range(plan.peers):
        mine = total[peer * rows : (peer + 1) * rows]
        out_ref[peer] = jnp.where(r == plan.list_at, lists[peer // plan.pair], mine).astype(BF16)


def normalize(table_hbm, gain_ref, after_ref, *refs):
    *outs, mark_ref, gain, buffers, made, sems, out_sems = refs
    held, block, _ = buffers.shape
    steps = table_hbm.shape[0] // block
    each = outs[0].shape[0] // block

    def copy(step):
        source = table_hbm.at[pl.ds(step * block, block)]
        return pltpu.make_async_copy(source, buffers.at[step % held], sems.at[step % held])

    def store(step):
        target = outs[step // each].at[pl.ds(step % each * block, block)]
        return pltpu.make_async_copy(made.at[step % held], target, out_sems.at[step % held])

    for step in range(min(held, steps)):
        copy(step).start()
    rows = gain_ref[...].astype(F32)
    gain[...] = jnp.concatenate([rows[r : r + 1] for r in range(rows.shape[0])], axis=1)
    for step in range(steps):
        copy(step).wait()
        if step >= held:
            store(step - held).wait()
        raw = buffers[step % held].astype(F32)
        inverse = lax.rsqrt(jnp.mean(raw * raw, axis=-1, keepdims=True) + EPS)
        made[step % held] = (raw * inverse * gain[...]).astype(BF16)
        store(step).start()
        if step + held < steps:
            copy(step + held).start()
    for step in range(max(0, steps - held), steps):
        store(step).wait()
    mark_ref[...] = jnp.zeros_like(mark_ref)


def spread_weights(plan, w_ref, full_ref):
    lists = []
    for s in range(plan.peers):
        for c in range(plan.chunks):
            rows = w_ref[s, c * plan.fold_at : (c + 1) * plan.fold_at]
            full_ref[s, : plan.fold_at, c * HD : (c + 1) * HD] = rows
        last = w_ref[s, plan.fold_at * plan.chunks :].astype(F32)
        last = [
            jnp.concatenate([last[i * plan.chunks + c : i * plan.chunks + c + 1] for c in range(plan.chunks)], axis=1)
            for i in range(plan.mine + 1)
        ]
        zeros = jnp.zeros((plan.rows - plan.list_at, last[0].shape[1]), F32)
        full_ref[s, plan.fold_at :] = jnp.concatenate([*last[: plan.mine], zeros], axis=0).astype(BF16)
        lists.append(last[plan.mine])
    return jnp.concatenate(lists, axis=0)


def list_rows(plan, w_ref):
    if len(w_ref.shape) == 3:
        rows = [w_ref[s].astype(F32)[plan.list_at : plan.list_at + 1] for s in range(plan.peers)]
    else:
        row = w_ref[...].astype(F32)[plan.list_at : plan.list_at + 1]
        span = plan.share * plan.capacity
        rows = [row[:, s * 2 * span : (s + 1) * 2 * span] for s in range(plan.peers)]
    return jnp.concatenate(rows, axis=0)


def read_lists(plan, rows, out_ref):
    share, capacity, peers = plan.share, plan.capacity, plan.peers
    span = share * capacity
    lane = lax.broadcasted_iota(jnp.int32, (share * peers, 2 * span), 1)
    row = lax.broadcasted_iota(jnp.int32, (share * peers, 2 * span), 0)
    lane = jnp.where(lane < span, lane, lane - span)
    spread = jnp.concatenate([rows] * share, axis=0)
    spread = jnp.where(lane // capacity == row // peers, spread, 0.0).astype(BF16)
    c = lax.broadcasted_iota(jnp.int32, (2 * span, plan.slots), 0)
    slot = lax.broadcasted_iota(jnp.int32, (2 * span, plan.slots), 1)
    scale = jnp.where(c < span, 64.0, 1.0)
    place = jnp.where(c % capacity == slot % capacity, scale, 0.0).astype(BF16)
    listed = matmul(spread, place)
    row = lax.broadcasted_iota(jnp.int32, listed.shape, 0)
    slot = lax.broadcasted_iota(jnp.int32, listed.shape, 1)
    listed = jnp.where(slot // capacity == row % peers, listed, 0.0)
    out_ref[...] = jnp.sum(listed.reshape(share, peers, plan.slots), axis=1)


def project(plan, place, lists, place_ref, w_ref, normed_ref, turn_ref, after_ref, *refs):
    if lists:
        *refs, list_ref, full_ref = refs
        if plan.tight:
            rows = spread_weights(plan, w_ref, full_ref)
            w_ref = full_ref
        else:
            rows = list_rows(plan, w_ref)
            full_ref[...] = w_ref[...]
        read_lists(plan, rows, list_ref)
    q_ref, vo_ref = refs[-2:]
    turns = turn_ref[place_ref[LINE]]
    half, k_half = plan.q_rows // 2, plan.k_rows // 2
    cosine, sine = turns[:, 0:1], turns[:, 1:2]
    cos_k, sin_k = cosine[:k_half], sine[:k_half]
    moves = normed_ref.shape[0]
    block = min(moves, HD)
    every = []
    for start in range(0, moves, block):
        at, to = slice(start, start + block), slice(place + start, place + start + block)
        if len(w_ref.shape) == 3:
            depth = w_ref.shape[2]
            total = None
            for s in range(w_ref.shape[0]):
                term = matmul(w_ref[s], normed_ref[at, s * depth : (s + 1) * depth], NT)
                total = term if total is None else total + term
        else:
            total = matmul(w_ref[...], normed_ref[at, :], NT)
        first, second = total[:half], total[half : 2 * half]
        f_first = (first * cosine - second * sine).astype(BF16).astype(F32)
        f_second = (second * cosine + first * sine).astype(BF16).astype(F32)
        first, second = total[plan.q_rows : plan.q_rows + k_half], total[plan.q_rows + k_half : plan.fold_at]
        k_first = (first * cos_k - second * sin_k).astype(BF16).astype(F32)
        k_second = (second * cos_k + first * sin_k).astype(BF16).astype(F32)
        logits, tails = [], []
        for h in range(plan.mine):
            own = slice(h * k_half, (h + 1) * k_half)
            logit = jnp.sum(f_first[own] * k_first + f_second[own] * k_second, axis=0, keepdims=True)
            logits.append(logit.astype(BF16).astype(F32))
            tails.append(logit - logits[-1])
        if plan.direct:
            chunk = (place + start) // block * plan.q_rows
            q_ref[chunk : chunk + plan.q_rows] = jnp.concatenate([f_first, f_second], axis=0).astype(BF16)
            every += [*logits, *tails]
        else:
            pad = plan.line_rows - plan.q_rows - 2 * plan.mine
            pieces = [f_first, f_second, *logits, *tails]
            if pad:
                pieces.append(jnp.zeros((pad, block), F32))
            out = jnp.concatenate(pieces, axis=0).astype(BF16)
            for line in range(plan.line):
                q_ref[line, :, to] = out
        vo_ref[:, to] = total[plan.fold_at : plan.list_at]
    if plan.direct:
        first = vo_ref.shape[1] // HD * plan.q_rows + place // block * 2 * plan.mine
        q_ref[first : first + len(every)] = jnp.concatenate(every, axis=0).astype(BF16)


def tied(x, *others):
    return pl.pallas_call(
        lambda *refs: None,
        out_shape=shape(x.shape, x.dtype),
        in_specs=[untouched()] * (1 + len(others)),
        out_specs=untouched(),
        input_output_aliases={0: 0},
        compiler_params=limits(1),
        cost_estimate=cost(0, 0),
    )(x, *others)


def pack_prefix(plan, prefix_hbm, ws_hbm, after_ref, out_ref, *scratch):
    values, ws_ref, sems = scratch
    boards = values.shape[0]
    heads = plan.heads
    copies = (
        pltpu.make_async_copy(ws_hbm, ws_ref, sems.at[0]),
        pltpu.make_async_copy(prefix_hbm.at[:, :, pl.ds(HD, HD)], values, sems.at[1]),
        pltpu.make_async_copy(prefix_hbm.at[:, :, pl.ds(0, HD)], out_ref.at[pl.ds(0, boards)], sems.at[2]),
    )
    for copy in copies:
        copy.start()
    copies[0].wait()
    span = HD // boards
    ws = jnp.concatenate([ws_ref[...].astype(F32)] * (HD // heads), axis=0)
    row = lax.broadcasted_iota(jnp.int32, (HD, 1), 0)
    copies[1].wait()
    fold = None
    for board in range(boards):
        keep = (row // span == board) & (row % span < 2 * heads)
        term = matmul(values[board], jnp.where(keep, ws, 0.0).astype(BF16), NT)
        fold = term if fold is None else fold + term
    rounded = fold.astype(BF16).astype(F32)
    lane = lax.broadcasted_iota(jnp.int32, fold.shape, 1)
    out_ref[boards] = jnp.where(lane % span < heads, rounded, fold - rounded).astype(BF16)
    copies[2].wait()


def fold_columns(plan, here, block, board, boards, heads):
    lanes = plan.mine * plan.slots
    row = lax.broadcasted_iota(jnp.int32, (HD, lanes), 0) - board * (HD // boards)
    head = here * plan.mine + lax.broadcasted_iota(jnp.int32, (HD, lanes), 1) // plan.slots
    pick = jnp.where((row == head) | (row == head + heads), 1.0, 0.0).astype(BF16)
    return matmul(block, pick)


def prepare(plan, place_ref, board_ref, own_ref, other_ref, *rest):
    *prefix_refs, chosen_ref, fold_ref, slot_ref = rest
    count = board_ref.shape[1]
    board_row = board_ref[...]
    board_col = jnp.broadcast_to(board_row.astype(F32), (8, count)).T[:, 0:1].astype(jnp.int32)
    ahead = lax.broadcasted_iota(jnp.int32, (count, count), 0) < lax.broadcasted_iota(jnp.int32, (count, count), 1)
    rank = jnp.sum(jnp.where((board_col == board_row) & ahead, 1.0, 0.0), axis=0, keepdims=True)
    slot_ref[...] = rank.astype(jnp.int32) + place_ref[PEER] * plan.capacity
    here = place_ref[SLAB]
    boards, moves = chosen_ref.shape[0], chosen_ref.shape[1]
    move_at = lax.broadcasted_iota(jnp.int32, (moves, plan.slots), 0) + 1

    def step(board, carry):
        for j in range(plan.slab):
            place = ((here ^ j) % plan.pair) * boards + board
            row = (own_ref, other_ref)[j // plan.pair][pl.ds(place, 1), :].astype(jnp.int32)
            at = slice(j * plan.slots, (j + 1) * plan.slots)
            chosen_ref[board, :, at] = jnp.where(move_at == row, 1.0, 0.0).astype(BF16)
        for j, prefix_ref in enumerate(prefix_refs):
            fold_ref[j, board] = fold_columns(plan, here, prefix_ref[boards], board, boards, plan.heads)
        return carry

    lax.fori_loop(0, boards, step, 0)


def attend(plan, place_ref, vo_ref, own_ref, other_ref, chosen_ref, fold_ref, *rest):
    prefix_refs, rest = rest[: plan.slab], rest[plan.slab :]
    *q_refs, out_ref, table, extra, scores, taken_even, taken_odd = rest
    here = place_ref[SLAB]
    mine, heads, slots = plan.mine, plan.heads, plan.slots
    moves = vo_ref.shape[1]
    boards = prefix_refs[0].shape[0] - 1
    query_rows = mine * HD

    mixed = own_logits = None
    for step, q_ref in enumerate(q_refs):
        if plan.direct:
            chunks = range(moves // HD)
            values = jnp.concatenate([q_ref[c * plan.q_rows : (c + 1) * plan.q_rows] for c in chunks], axis=1)
            tails = q_ref[moves // HD * plan.q_rows :].astype(F32)
            tails = jnp.concatenate([tails[c * 2 * mine : (c + 1) * 2 * mine] for c in chunks], axis=1)
            tails = tails[:mine] + tails[mine:]
            own_logits = tails if own_logits is None else own_logits + tails
        else:
            values = q_ref[...]
        r = lax.broadcasted_iota(jnp.int32, (query_rows + 8, values.shape[0]), 0)
        c = lax.broadcasted_iota(jnp.int32, (query_rows + 8, values.shape[0]), 1)
        line, at = (place_ref[LINE] ^ step, c) if plan.direct else (c // plan.line_rows, c % plan.line_rows)
        part, head, entry = at // (mine * plan.pairs), (at // plan.pairs) % mine, at % plan.pairs
        goes = jnp.where(at < plan.q_rows, head * HD + part * HALF + line * plan.pairs + entry, -1)
        tail = at - plan.q_rows
        goes = jnp.where((tail >= 0) & (tail < 2 * mine), query_rows + tail % mine, goes)
        term = matmul(jnp.where(r == goes, 1.0, 0.0).astype(BF16), values)
        mixed = term if mixed is None else mixed + term
    if own_logits is None:
        own_logits = mixed[query_rows : query_rows + mine]
    table[:query_rows] = mixed[:query_rows].astype(BF16)
    extra[...] = jnp.zeros_like(extra)
    for place, value in ((0, own_logits), (2 * mine, vo_ref[...])):
        rounded = value.astype(BF16).astype(F32)
        extra[place : place + mine] = rounded
        extra[place + mine : place + 2 * mine] = value - rounded
    table[query_rows:] = extra[...].astype(BF16)

    scale = math.log2(math.e) / math.sqrt(HD)
    def per_head(x, base):
        pieces = [x[base + h : base + h + 1] + x[base + mine + h : base + mine + h + 1] for h in range(mine)]
        return jnp.concatenate(pieces, axis=1)

    def moves_of(j, board):
        place = ((here ^ j) % plan.pair) * boards + board
        return (own_ref, other_ref)[j // plan.pair][pl.ds(place, 1), :].astype(jnp.int32)

    def gather(board, taken):
        taken[...] = matmul(table[...], chosen_ref[board])

    def score_board(board, taken):
        for j in range(plan.slab):
            x = taken[:, j * slots : (j + 1) * slots]
            q = jnp.concatenate([x[h * HD : (h + 1) * HD].astype(BF16) for h in range(mine)], axis=1)
            logits = matmul(prefix_refs[j][board], q)
            if j < plan.slab - 1:
                fold = fold_ref[j, board]
            else:
                fold = fold_columns(plan, here, prefix_refs[j][boards], board, boards, heads)
            own_logit = per_head(x, query_rows)
            own_value = per_head(x, query_rows + 2 * mine)
            peak = jnp.maximum(jnp.max(logits, axis=0, keepdims=True), own_logit)
            weight = jnp.exp2((logits - peak) * scale)
            own_weight = jnp.exp2((own_logit - peak) * scale)
            denom = jnp.sum(weight, axis=0, keepdims=True) + own_weight
            value = (jnp.sum(weight * fold, axis=0, keepdims=True) + own_value * own_weight) / denom
            score = sum(value[:, h * slots : (h + 1) * slots] for h in range(mine))
            scores[here ^ j, pl.ds(board, 1), :] = jnp.where(moves_of(j, board) > 0, score, DEAD)

    gather(0, taken_even)

    def step(at, carry):
        board = 2 * at
        gather(jnp.minimum(board + 1, boards - 1), taken_odd)
        score_board(board, taken_even)
        gather(jnp.minimum(board + 2, boards - 1), taken_even)
        score_board(jnp.minimum(board + 1, boards - 1), taken_odd)
        return carry

    lax.fori_loop(0, -(-boards // 2), step, 0)
    live = scores[...] > 0.5 * DEAD
    count = jnp.sum(jnp.where(live, 1.0, 0.0), axis=2, keepdims=True)
    mean = jnp.sum(jnp.where(live, scores[...], 0.0), axis=2, keepdims=True) / jnp.maximum(count, 1.0)
    centered = jnp.where(live, scores[...] - mean, DEAD)
    for g in range(plan.groups):
        both = jnp.concatenate([centered[g * plan.pair + p] for p in range(plan.pair)], axis=0).astype(BF16)
        for copy in range(out_ref.shape[1]):
            out_ref[g, copy] = both


def finish(plan, parts_ref, board_ref, slot_ref, out_ref):
    line = parts_ref.shape[1]
    columns = []
    for at in range(line):
        total = None
        for g in range(parts_ref.shape[0]):
            for p in range(parts_ref.shape[2]):
                term = parts_ref[g, at, p].astype(F32)
                total = term if total is None else total + term
        columns.append(total)
    scores = jnp.concatenate(columns, axis=0)
    live = scores > 0.5 * DEAD
    peak = jnp.max(scores, axis=1, keepdims=True)
    denom = jnp.sum(jnp.where(live, jnp.exp(scores - peak), 0.0), axis=1, keepdims=True)
    logprob = jnp.where(live, scores - peak - jnp.log(denom), 0.0)
    count = board_ref.shape[1]
    member = lax.broadcasted_iota(jnp.int32, (scores.shape[0], count), 0) == board_ref[...]
    member = jnp.where(member, 1.0, 0.0).astype(BF16)
    found = jnp.zeros((plan.slots, count), F32)
    for _ in range(3):
        rounded = logprob.astype(BF16)
        found = found + matmul(rounded, member, TN)
        logprob = logprob - rounded.astype(F32)
    at = lax.broadcasted_iota(jnp.int32, (plan.slots, count), 0) == slot_ref[...]
    out_ref[...] = jnp.sum(jnp.where(at, found, 0.0), axis=0, keepdims=True)


def untouched():
    return pl.BlockSpec(memory_space=pl.ANY)


def local_call(kernel, place, args, outs, scratch=(), mib=40, copied=(), flops=0, nbytes=0, aliases=None):
    vmem = pl.BlockSpec(memory_space=pltpu.VMEM)
    return pl.pallas_call(
        kernel,
        out_shape=outs,
        in_specs=[pl.BlockSpec(memory_space=pltpu.SMEM)]
        + [untouched() if at in copied else vmem for at in range(len(args))],
        out_specs=jax.tree.map(lambda x: vmem, outs),
        scratch_shapes=scratch,
        input_output_aliases=aliases or {},
        compiler_params=limits(mib),
        cost_estimate=cost(flops, nbytes),
    )(place, *args)


def cost(flops, nbytes):
    return pl.CostEstimate(flops=int(flops), bytes_accessed=int(nbytes), transcendentals=0)


def swap(x, names, size, step):
    return lax.ppermute(x, names, [(at, at ^ step) for at in range(size)])


def shape(dims, dtype):
    return jax.ShapeDtypeStruct(tuple(dims), dtype)


def turn_table(position):
    frequency = THETA ** (-2.0 * np.arange(HALF, dtype=np.float32) / HD)
    angles = np.float32(position) * frequency.astype(np.float32)
    return np.stack([np.cos(angles), np.sin(angles)], axis=1).astype(np.float32)


def per_device(prefix_kv, move_ids, move_board, move_table, norm_gain, w_query, w_keyval, w_score):
    row_count = move_ids.shape[0]
    boards_here, prefix_len, _ = prefix_kv.shape
    moves, width = move_table.shape
    groups, line, pair = lax.axis_size("groups"), lax.axis_size("line"), lax.axis_size("pair")
    board_total = boards_here * line * pair
    capacity = max(2, (2 * row_count + board_total - 1) // board_total)
    heads = w_query.shape[1] // HD
    depth = w_query.shape[0]
    plan = Plan(groups, line, pair, heads, capacity, pair * boards_here, depth)
    group_at = lax.axis_index("groups").astype(jnp.int32)
    line_at = lax.axis_index("line").astype(jnp.int32)
    pair_at = lax.axis_index("pair").astype(jnp.int32)
    place = jnp.stack([group_at, line_at, line_at * pair + pair_at, group_at * pair + pair_at])
    ws = w_score.reshape(heads, HD)
    slab_axes = ("groups", "pair")
    board_row = move_board.reshape(1, row_count)

    half_cols = w_query.shape[1] // groups
    packed = local_call(
        functools.partial(pack_weights, plan),
        group_at.reshape(1),
        (w_query, w_keyval, ws, board_row, move_ids.reshape(1, row_count)),
        shape((plan.peers, *plan.sent), BF16),
        [
            pltpu.VMEM((depth, half_cols), BF16),
            pltpu.VMEM((depth, 2 * HD), BF16),
            pltpu.VMEM((heads, HD), BF16),
            pltpu.VMEM((1, row_count), jnp.int32),
            pltpu.VMEM((1, row_count), jnp.int32),
            pltpu.VMEM((plan.peers * plan.rows, half_cols + 2 * HD), F32),
            pltpu.SemaphoreType.DMA((5,)),
        ],
        62,
        range(5),
    )
    weights = lax.all_to_all(packed, ("line", "pair"), split_axis=0, concat_axis=0, tiled=True)

    payload = pl.pallas_call(
        functools.partial(pack_prefix, plan),
        out_shape=shape((boards_here + 1, prefix_len, HD), BF16),
        in_specs=[untouched()] * 3,
        out_specs=pl.BlockSpec(memory_space=pltpu.VMEM),
        scratch_shapes=[
            pltpu.VMEM((boards_here, prefix_len, HD), BF16),
            pltpu.VMEM((heads, HD), BF16),
            pltpu.SemaphoreType.DMA((3,)),
        ],
        compiler_params=limits(56),
        cost_estimate=cost(0, 0),
    )(prefix_kv, ws, packed)
    beside = swap(payload, slab_axes, plan.slab, 1)
    across = swap(payload, slab_axes, plan.slab, 2)

    block = min(moves, 128)
    vmem = pl.BlockSpec(memory_space=pltpu.VMEM)
    *normed, mark = pl.pallas_call(
        normalize,
        out_shape=[*[shape((moves // 2, width), BF16)] * 2, pltpu.VMEM((8, HD), F32)],
        in_specs=[untouched(), vmem, untouched()],
        out_specs=[untouched(), untouched(), vmem],
        scratch_shapes=[
            pltpu.VMEM((1, width), F32),
            pltpu.VMEM((3, block, width), BF16),
            pltpu.VMEM((3, block, width), BF16),
            pltpu.SemaphoreType.DMA((3,)),
            pltpu.SemaphoreType.DMA((3,)),
        ],
        compiler_params=limits(58),
        cost_estimate=cost(moves * width, moves * width // 4),
    )(move_table, norm_gain.reshape(width // HD, HD), packed)
    turns = turn_table(prefix_len).reshape(line, 1, plan.pairs, 2)
    turns = np.tile(turns, (1, plan.mine, 1, 1)).reshape(line, plan.mine * plan.pairs, 2)
    flat = weights.transpose(1, 0, 2).reshape(plan.rows, width) if depth % HD else weights
    sent = (moves // HD * (plan.q_rows + 2 * plan.mine), HD) if plan.direct else (line, plan.line_rows, moves)
    outs = (shape(sent, BF16), shape((plan.mine, moves), F32))
    across = tied(across, mark)
    diagonal = swap(across, slab_axes, plan.slab, 1)
    full = shape((plan.peers, plan.rows, depth), BF16) if plan.tight else shape(flat.shape, BF16)
    filled, listed = (), None
    for step, after in enumerate((across, across)):
        made = local_call(
            functools.partial(project, plan, step * moves // 2, step == 0),
            place,
            (flat, normed[step], jnp.asarray(turns), after, *filled),
            [*outs, *([shape((plan.share, plan.slots), F32), full] if step == 0 else [])],
            (),
            20,
            (3,),
            moves * width * 1024,
            moves * width,
            {5: 0, 6: 1} if filled else None,
        )
        filled = made[:2]
        if step == 0:
            listed, flat = made[2:]
    queries, own_values = filled
    queries = tied(queries, beside)
    other = swap(listed, slab_axes, plan.slab, pair)
    if plan.direct:
        queries = [queries] + [swap(queries, "line", line, step) for step in range(1, line)]
    else:
        queries = lax.all_to_all(queries, "line", split_axis=0, concat_axis=0, tiled=True)
        queries = [queries.reshape(line * plan.line_rows, moves)]

    query_rows = plan.mine * HD
    back = plan.peers * lax.axis_size("tensor")
    chosen, folds, slot_row = local_call(
        functools.partial(prepare, plan),
        place,
        (board_row, listed, other, payload, beside, across),
        (
            shape((boards_here, moves, plan.slab * plan.slots), BF16),
            shape((plan.slab - 1, boards_here, prefix_len, plan.mine * plan.slots), F32),
            shape((1, row_count), jnp.int32),
        ),
        mib=20,
        flops=10**9,
        nbytes=10**6,
    )
    parts = local_call(
        functools.partial(attend, plan),
        place,
        (own_values, listed, other, chosen, folds, payload, beside, across, diagonal, *queries),
        shape((groups, back, plan.share, plan.slots), BF16),
        [
            pltpu.VMEM((query_rows + 16, moves), BF16),
            pltpu.VMEM((16, moves), F32),
            pltpu.VMEM((plan.slab, boards_here, plan.slots), F32),
            pltpu.VMEM((query_rows + 16, plan.slab * plan.slots), F32),
            pltpu.VMEM((query_rows + 16, plan.slab * plan.slots), F32),
        ],
        24,
    )
    parts = lax.all_to_all(
        parts.reshape(groups * back, plan.share, plan.slots),
        ("groups", "line", "pair", "tensor"),
        split_axis=0,
        concat_axis=0,
        tiled=True,
    )
    parts = parts.reshape(groups, line, back // line, plan.share, plan.slots)
    logprob = pl.pallas_call(
        functools.partial(finish, plan), out_shape=shape((1, row_count), F32), compiler_params=limits(VMEM_MIB)
    )(parts, board_row, slot_row)
    return logprob.reshape(row_count)


def solution(mesh):
    order = ("groups", "dp", "tensor")
    assert mesh.axis_names == order
    pair = 2
    groups, peers, tensor = (mesh.shape[name] for name in order)
    fine = Mesh(mesh.devices.reshape(groups, peers // pair, pair, tensor), ("groups", "line", "pair", "tensor"))
    rows = ("groups", "line", "pair")
    placed = (
        P(rows, None, "tensor"),
        P(rows),
        P(rows, None),
        P(),
        P(),
        P(("line", "pair"), "tensor"),
        P(("line", "pair"), "tensor"),
        P("tensor"),
    )
    return jax.shard_map(per_device, mesh=fine, in_specs=placed, out_specs=P(rows), check_vma=False)
```

```python
import functools
import math

import jax
import jax.numpy as jnp
import numpy as np
from jax import lax
from jax.experimental import pallas as pl
from jax.experimental.pallas import tpu as pltpu
from jax.sharding import Mesh
from jax.sharding import PartitionSpec as P

HD = 128
HALF = HD // 2
EPS = 1e-06
THETA = 5000000.0
DEAD = -1e30
VMEM_MIB = 52
GROUP, LINE, PEER, SLAB = range(4)

F32 = jnp.float32
BF16 = jnp.bfloat16

NN = (((1,), (0,)), ((), ()))
NT = (((1,), (1,)), ((), ()))
TN = (((0,), (0,)), ((), ()))


def matmul(a, b, dims=NN):
    return lax.dot_general(a, b, dims, preferred_element_type=F32)


def limits(mib):
    return pltpu.CompilerParams(vmem_limit_bytes=mib * 1024 * 1024)


class Plan:
    def __init__(self, groups, line, pair, heads, capacity, share, depth):
        self.groups, self.line, self.pair = groups, line, pair
        self.peers = line * pair
        self.slab = groups * pair
        self.heads = heads
        self.mine = heads // self.slab
        self.pairs = HALF // line
        self.q_rows = self.mine * 2 * self.pairs
        self.k_rows = 2 * self.pairs
        self.fold_at = self.q_rows + self.k_rows
        self.list_at = self.fold_at + self.mine
        self.rows = -(-(self.list_at + 1) // 8) * 8
        self.line_rows = -(-(self.q_rows + 2 * self.mine) // 8) * 8
        self.capacity = capacity
        self.share = share
        self.slots = self.peers * capacity
        self.direct = line <= 4
        self.tight = self.pairs % 16 == 0 and depth % HD == 0
        self.chunks = depth // HD
        last = -(-(self.mine + 1) * self.chunks // 16) * 16
        self.sent = (self.fold_at * self.chunks + last, HD) if self.tight else (self.rows, depth)


def pack_weights(plan, place_ref, wq_hbm, wkv_hbm, ws_hbm, board_hbm, ids_hbm, *rest):
    out_ref, wq, wkv, ws_ref, board_ref, ids_ref, pick, sems = rest
    group = place_ref[0]
    half_cols = wq.shape[1]
    columns_here = pl.ds(pl.multiple_of(group * half_cols, HD), half_cols)
    copies = (
        pltpu.make_async_copy(ws_hbm, ws_ref, sems.at[0]),
        pltpu.make_async_copy(board_hbm, board_ref, sems.at[1]),
        pltpu.make_async_copy(ids_hbm, ids_ref, sems.at[2]),
        pltpu.make_async_copy(wq_hbm.at[:, columns_here], wq, sems.at[3]),
        pltpu.make_async_copy(wkv_hbm, wkv, sems.at[4]),
    )
    for copy in copies:
        copy.start()
    for copy in copies[:3]:
        copy.wait()
    count, depth = board_ref.shape[1], wq.shape[0]
    board_row = board_ref[...]
    board_col = jnp.broadcast_to(board_row.astype(F32), (8, count)).T[:, 0:1].astype(jnp.int32)
    own = lax.broadcasted_iota(jnp.int32, (count, count), 0)
    other = lax.broadcasted_iota(jnp.int32, (count, count), 1)
    ahead = jnp.where((board_col == board_row) & (other < own), 1.0, 0.0)
    rank = jnp.sum(ahead, axis=1, keepdims=True).astype(jnp.int32)
    move = ids_ref[...] + 1
    boards, span = plan.line * plan.share, plan.share * plan.capacity
    member = lax.broadcasted_iota(jnp.int32, (boards, count), 0) == board_row
    parts = [jnp.where(member, part.astype(F32), 0.0) for part in (move // 64, move % 64)]
    lane = lax.broadcasted_iota(jnp.int32, (count, depth), 1)
    ranked = jnp.where(rank == (lane % span) % plan.capacity, 1.0, 0.0).astype(BF16)
    found = matmul(jnp.concatenate(parts, axis=0).astype(BF16), ranked)
    lane = lax.broadcasted_iota(jnp.int32, (2 * boards, depth), 1)
    row = lax.broadcasted_iota(jnp.int32, (2 * boards, depth), 0)
    keep = (row // boards == lane // span) & (row % plan.share == (lane % span) // plan.capacity)
    found = jnp.where(keep, found, 0.0)
    lists = []
    for line in range(plan.line):
        at = line * plan.share
        both = found[at : at + plan.share] + found[boards + at : boards + at + plan.share]
        lists.append(jnp.sum(both, axis=0, keepdims=True))

    if plan.tight:
        turn_weights(plan, group, lists, copies[3:], wq, wkv, ws_ref, out_ref)
    else:
        pick_weights(plan, group, lists, copies[3:], wq, wkv, ws_ref, out_ref, pick)


def turn_weights(plan, group, lists, copies, wq, wkv, ws_ref, out_ref):
    for copy in copies:
        copy.wait()
    q = wq[...].T
    k = wkv[:, :HD].T
    folds = matmul(ws_ref[...], wkv[:, HD:], NT)
    row = lax.broadcasted_iota(jnp.int32, folds.shape, 0)
    pairs = plan.pairs
    lanes = [slice(c * HD, (c + 1) * HD) for c in range(plan.chunks)]
    first_last = plan.fold_at * plan.chunks
    zeros = jnp.zeros((plan.sent[0] - first_last - (plan.mine + 1) * plan.chunks, HD), F32)
    for pair in range(plan.pair):
        first = (group * plan.pair + pair) * plan.mine
        mine = [jnp.sum(jnp.where(row == first + h, folds, 0.0), axis=0, keepdims=True) for h in range(plan.mine)]
        for line in range(plan.line):
            peer = line * plan.pair + pair
            for c, lane in enumerate(lanes):
                for part in range(2):
                    entry = part * HALF + line * pairs
                    for h in range(plan.mine):
                        at = c * plan.fold_at + (part * plan.mine + h) * pairs
                        source = (pair * plan.mine + h) * HD + entry
                        out_ref[peer, at : at + pairs] = q[source : source + pairs, lane]
                    at = c * plan.fold_at + plan.q_rows + part * pairs
                    out_ref[peer, at : at + pairs] = k[entry : entry + pairs, lane]
            last = [values[:, lane] for values in (*mine, lists[line]) for lane in lanes]
            out_ref[peer, first_last:] = jnp.concatenate([*last, zeros], axis=0).astype(BF16)


def pick_weights(plan, group, lists, copies, wq, wkv, ws_ref, out_ref, pick):
    rows, half_cols = plan.rows, wq.shape[1]
    r = lax.broadcasted_iota(jnp.int32, (rows, 1), 0)
    part = r // (plan.mine * plan.pairs)
    head = (r // plan.pairs) % plan.mine
    entry = r % plan.pairs
    is_q = r < plan.q_rows
    k_at = r - plan.q_rows
    is_k = (k_at >= 0) & (k_at < plan.k_rows)
    f_at = r - plan.fold_at
    is_f = (f_at >= 0) & (f_at < plan.mine)
    q_lane = lax.broadcasted_iota(jnp.int32, (rows, half_cols), 1)
    k_lane = lax.broadcasted_iota(jnp.int32, (rows, HD), 1)
    ws = ws_ref[...].astype(F32)

    def fill(peer, carry):
        line, pair = peer // plan.pair, peer % plan.pair
        column = (pair * plan.mine + head) * HD + part * HALF + line * plan.pairs + entry
        column = jnp.where(is_q, column, -1)
        at = pl.ds(pl.multiple_of(peer * rows, 8), rows)
        pick[at, :half_cols] = jnp.where(q_lane == column, 1.0, 0.0)
        k_column = (k_at // plan.pairs) * HALF + line * plan.pairs + k_at % plan.pairs
        k_column = jnp.where(is_k, k_column, -1)
        pick[at, half_cols : half_cols + HD] = jnp.where(k_lane == k_column, 1.0, 0.0)
        fold = jnp.zeros((rows, HD), F32)
        my_head = jnp.where(is_f, (group * plan.pair + pair) * plan.mine + f_at, -1)
        for h in range(plan.heads):
            fold = jnp.where(my_head == h, ws[h : h + 1], fold)
        pick[at, half_cols + HD :] = fold
        return carry

    lax.fori_loop(0, plan.peers, fill, 0, unroll=plan.peers <= 8)

    for copy in copies:
        copy.wait()
    left = pick[...].astype(BF16)
    total = matmul(left[:, :half_cols], wq[...], NT) + matmul(left[:, half_cols:], wkv[...], NT)
    for peer in range(plan.peers):
        mine = total[peer * rows : (peer + 1) * rows]
        out_ref[peer] = jnp.where(r == plan.list_at, lists[peer // plan.pair], mine).astype(BF16)


def normalize(table_hbm, gain_ref, after_ref, *refs):
    *outs, mark_ref, gain, buffers, made, sems, out_sems = refs
    held, block, _ = buffers.shape
    steps = table_hbm.shape[0] // block
    each = outs[0].shape[0] // block

    def copy(step):
        source = table_hbm.at[pl.ds(step * block, block)]
        return pltpu.make_async_copy(source, buffers.at[step % held], sems.at[step % held])

    def store(step):
        target = outs[step // each].at[pl.ds(step % each * block, block)]
        return pltpu.make_async_copy(made.at[step % held], target, out_sems.at[step % held])

    for step in range(min(held, steps)):
        copy(step).start()
    rows = gain_ref[...].astype(F32)
    gain[...] = jnp.concatenate([rows[r : r + 1] for r in range(rows.shape[0])], axis=1)
    for step in range(steps):
        copy(step).wait()
        if step >= held:
            store(step - held).wait()
        raw = buffers[step % held].astype(F32)
        inverse = lax.rsqrt(jnp.mean(raw * raw, axis=-1, keepdims=True) + EPS)
        made[step % held] = (raw * inverse * gain[...]).astype(BF16)
        store(step).start()
        if step + held < steps:
            copy(step + held).start()
    for step in range(max(0, steps - held), steps):
        store(step).wait()
    mark_ref[...] = jnp.zeros_like(mark_ref)


def spread_weights(plan, w_ref, full_ref):
    lists = []
    for s in range(plan.peers):
        for c in range(plan.chunks):
            rows = w_ref[s, c * plan.fold_at : (c + 1) * plan.fold_at]
            full_ref[s, : plan.fold_at, c * HD : (c + 1) * HD] = rows
        last = w_ref[s, plan.fold_at * plan.chunks :].astype(F32)
        last = [
            jnp.concatenate([last[i * plan.chunks + c : i * plan.chunks + c + 1] for c in range(plan.chunks)], axis=1)
            for i in range(plan.mine + 1)
        ]
        zeros = jnp.zeros((plan.rows - plan.list_at, last[0].shape[1]), F32)
        full_ref[s, plan.fold_at :] = jnp.concatenate([*last[: plan.mine], zeros], axis=0).astype(BF16)
        lists.append(last[plan.mine])
    return jnp.concatenate(lists, axis=0)


def list_rows(plan, w_ref):
    if len(w_ref.shape) == 3:
        rows = [w_ref[s].astype(F32)[plan.list_at : plan.list_at + 1] for s in range(plan.peers)]
    else:
        row = w_ref[...].astype(F32)[plan.list_at : plan.list_at + 1]
        span = plan.share * plan.capacity
        rows = [row[:, s * 2 * span : (s + 1) * 2 * span] for s in range(plan.peers)]
    return jnp.concatenate(rows, axis=0)


def read_lists(plan, rows, out_ref):
    share, capacity, peers = plan.share, plan.capacity, plan.peers
    span = share * capacity
    lane = lax.broadcasted_iota(jnp.int32, (share * peers, 2 * span), 1)
    row = lax.broadcasted_iota(jnp.int32, (share * peers, 2 * span), 0)
    lane = jnp.where(lane < span, lane, lane - span)
    spread = jnp.concatenate([rows] * share, axis=0)
    spread = jnp.where(lane // capacity == row // peers, spread, 0.0).astype(BF16)
    c = lax.broadcasted_iota(jnp.int32, (2 * span, plan.slots), 0)
    slot = lax.broadcasted_iota(jnp.int32, (2 * span, plan.slots), 1)
    scale = jnp.where(c < span, 64.0, 1.0)
    place = jnp.where(c % capacity == slot % capacity, scale, 0.0).astype(BF16)
    listed = matmul(spread, place)
    row = lax.broadcasted_iota(jnp.int32, listed.shape, 0)
    slot = lax.broadcasted_iota(jnp.int32, listed.shape, 1)
    listed = jnp.where(slot // capacity == row % peers, listed, 0.0)
    out_ref[...] = jnp.sum(listed.reshape(share, peers, plan.slots), axis=1)


def project(plan, place, lists, place_ref, w_ref, normed_ref, turn_ref, after_ref, *refs):
    if lists:
        *refs, list_ref, full_ref = refs
        if plan.tight:
            rows = spread_weights(plan, w_ref, full_ref)
            w_ref = full_ref
        else:
            rows = list_rows(plan, w_ref)
            full_ref[...] = w_ref[...]
        read_lists(plan, rows, list_ref)
    q_ref, vo_ref = refs[-2:]
    turns = turn_ref[place_ref[LINE]]
    half, k_half = plan.q_rows // 2, plan.k_rows // 2
    cosine, sine = turns[:, 0:1], turns[:, 1:2]
    cos_k, sin_k = cosine[:k_half], sine[:k_half]
    moves = normed_ref.shape[0]
    block = min(moves, HD)
    every = []
    for start in range(0, moves, block):
        at, to = slice(start, start + block), slice(place + start, place + start + block)
        if len(w_ref.shape) == 3:
            depth = w_ref.shape[2]
            total = None
            for s in range(w_ref.shape[0]):
                term = matmul(w_ref[s], normed_ref[at, s * depth : (s + 1) * depth], NT)
                total = term if total is None else total + term
        else:
            total = matmul(w_ref[...], normed_ref[at, :], NT)
        first, second = total[:half], total[half : 2 * half]
        f_first = (first * cosine - second * sine).astype(BF16).astype(F32)
        f_second = (second * cosine + first * sine).astype(BF16).astype(F32)
        first, second = total[plan.q_rows : plan.q_rows + k_half], total[plan.q_rows + k_half : plan.fold_at]
        k_first = (first * cos_k - second * sin_k).astype(BF16).astype(F32)
        k_second = (second * cos_k + first * sin_k).astype(BF16).astype(F32)
        logits, tails = [], []
        for h in range(plan.mine):
            own = slice(h * k_half, (h + 1) * k_half)
            logit = jnp.sum(f_first[own] * k_first + f_second[own] * k_second, axis=0, keepdims=True)
            logits.append(logit.astype(BF16).astype(F32))
            tails.append(logit - logits[-1])
        if plan.direct:
            chunk = (place + start) // block * plan.q_rows
            q_ref[chunk : chunk + plan.q_rows] = jnp.concatenate([f_first, f_second], axis=0).astype(BF16)
            every += [*logits, *tails]
        else:
            pad = plan.line_rows - plan.q_rows - 2 * plan.mine
            pieces = [f_first, f_second, *logits, *tails]
            if pad:
                pieces.append(jnp.zeros((pad, block), F32))
            out = jnp.concatenate(pieces, axis=0).astype(BF16)
            for line in range(plan.line):
                q_ref[line, :, to] = out
        vo_ref[:, to] = total[plan.fold_at : plan.list_at]
    if plan.direct:
        first = vo_ref.shape[1] // HD * plan.q_rows + place // block * 2 * plan.mine
        q_ref[first : first + len(every)] = jnp.concatenate(every, axis=0).astype(BF16)


def tied(x, *others):
    return pl.pallas_call(
        lambda *refs: None,
        out_shape=shape(x.shape, x.dtype),
        in_specs=[untouched()] * (1 + len(others)),
        out_specs=untouched(),
        input_output_aliases={0: 0},
        compiler_params=limits(1),
        cost_estimate=cost(0, 0),
    )(x, *others)


def pack_prefix(plan, prefix_hbm, ws_hbm, after_ref, out_ref, *scratch):
    values, ws_ref, sems = scratch
    boards = values.shape[0]
    heads = plan.heads
    copies = (
        pltpu.make_async_copy(ws_hbm, ws_ref, sems.at[0]),
        pltpu.make_async_copy(prefix_hbm.at[:, :, pl.ds(HD, HD)], values, sems.at[1]),
        pltpu.make_async_copy(prefix_hbm.at[:, :, pl.ds(0, HD)], out_ref.at[pl.ds(0, boards)], sems.at[2]),
    )
    for copy in copies:
        copy.start()
    copies[0].wait()
    span = HD // boards
    ws = jnp.concatenate([ws_ref[...].astype(F32)] * (HD // heads), axis=0)
    row = lax.broadcasted_iota(jnp.int32, (HD, 1), 0)
    copies[1].wait()
    fold = None
    for board in range(boards):
        keep = (row // span == board) & (row % span < 2 * heads)
        term = matmul(values[board], jnp.where(keep, ws, 0.0).astype(BF16), NT)
        fold = term if fold is None else fold + term
    rounded = fold.astype(BF16).astype(F32)
    lane = lax.broadcasted_iota(jnp.int32, fold.shape, 1)
    out_ref[boards] = jnp.where(lane % span < heads, rounded, fold - rounded).astype(BF16)
    copies[2].wait()


def fold_columns(plan, here, block, board, boards, heads):
    lanes = plan.mine * plan.slots
    row = lax.broadcasted_iota(jnp.int32, (HD, lanes), 0) - board * (HD // boards)
    head = here * plan.mine + lax.broadcasted_iota(jnp.int32, (HD, lanes), 1) // plan.slots
    pick = jnp.where((row == head) | (row == head + heads), 1.0, 0.0).astype(BF16)
    return matmul(block, pick)


def prepare(plan, place_ref, board_ref, own_ref, other_ref, *rest):
    chosen_ref, slot_ref = rest
    count = board_ref.shape[1]
    board_row = board_ref[...]
    board_col = jnp.broadcast_to(board_row.astype(F32), (8, count)).T[:, 0:1].astype(jnp.int32)
    ahead = lax.broadcasted_iota(jnp.int32, (count, count), 0) < lax.broadcasted_iota(jnp.int32, (count, count), 1)
    rank = jnp.sum(jnp.where((board_col == board_row) & ahead, 1.0, 0.0), axis=0, keepdims=True)
    slot_ref[...] = rank.astype(jnp.int32) + place_ref[PEER] * plan.capacity
    here = place_ref[SLAB]
    boards, moves = chosen_ref.shape[0], chosen_ref.shape[1]
    move_at = lax.broadcasted_iota(jnp.int32, (moves, plan.slots), 0) + 1

    def step(board, carry):
        for j in range(plan.slab):
            place = ((here ^ j) % plan.pair) * boards + board
            row = (own_ref, other_ref)[j // plan.pair][pl.ds(place, 1), :].astype(jnp.int32)
            at = slice(j * plan.slots, (j + 1) * plan.slots)
            chosen_ref[board, :, at] = jnp.where(move_at == row, 1.0, 0.0).astype(BF16)
        return carry

    lax.fori_loop(0, boards, step, 0)


def attend(plan, place_ref, vo_ref, own_ref, other_ref, chosen_ref, *rest):
    prefix_refs, rest = rest[: plan.slab], rest[plan.slab :]
    *q_refs, out_ref, table, extra, scores, taken_even, taken_odd = rest
    here = place_ref[SLAB]
    mine, heads, slots = plan.mine, plan.heads, plan.slots
    moves = vo_ref.shape[1]
    boards = prefix_refs[0].shape[0] - 1
    query_rows = mine * HD

    mixed = own_logits = None
    for step, q_ref in enumerate(q_refs):
        if plan.direct:
            chunks = range(moves // HD)
            values = jnp.concatenate([q_ref[c * plan.q_rows : (c + 1) * plan.q_rows] for c in chunks], axis=1)
            tails = q_ref[moves // HD * plan.q_rows :].astype(F32)
            tails = jnp.concatenate([tails[c * 2 * mine : (c + 1) * 2 * mine] for c in chunks], axis=1)
            tails = tails[:mine] + tails[mine:]
            own_logits = tails if own_logits is None else own_logits + tails
        else:
            values = q_ref[...]
        r = lax.broadcasted_iota(jnp.int32, (query_rows + 8, values.shape[0]), 0)
        c = lax.broadcasted_iota(jnp.int32, (query_rows + 8, values.shape[0]), 1)
        line, at = (place_ref[LINE] ^ step, c) if plan.direct else (c // plan.line_rows, c % plan.line_rows)
        part, head, entry = at // (mine * plan.pairs), (at // plan.pairs) % mine, at % plan.pairs
        goes = jnp.where(at < plan.q_rows, head * HD + part * HALF + line * plan.pairs + entry, -1)
        tail = at - plan.q_rows
        goes = jnp.where((tail >= 0) & (tail < 2 * mine), query_rows + tail % mine, goes)
        term = matmul(jnp.where(r == goes, 1.0, 0.0).astype(BF16), values)
        mixed = term if mixed is None else mixed + term
    if own_logits is None:
        own_logits = mixed[query_rows : query_rows + mine]
    table[:query_rows] = mixed[:query_rows].astype(BF16)
    extra[...] = jnp.zeros_like(extra)
    for place, value in ((0, own_logits), (2 * mine, vo_ref[...])):
        rounded = value.astype(BF16).astype(F32)
        extra[place : place + mine] = rounded
        extra[place + mine : place + 2 * mine] = value - rounded
    table[query_rows:] = extra[...].astype(BF16)

    scale = math.log2(math.e) / math.sqrt(HD)
    def per_head(x, base):
        pieces = [x[base + h : base + h + 1] + x[base + mine + h : base + mine + h + 1] for h in range(mine)]
        return jnp.concatenate(pieces, axis=1)

    def moves_of(j, board):
        place = ((here ^ j) % plan.pair) * boards + board
        return (own_ref, other_ref)[j // plan.pair][pl.ds(place, 1), :].astype(jnp.int32)

    def gather(board, taken):
        taken[...] = matmul(table[...], chosen_ref[board])

    def score_board(board, taken):
        for j in range(plan.slab):
            x = taken[:, j * slots : (j + 1) * slots]
            q = jnp.concatenate([x[h * HD : (h + 1) * HD].astype(BF16) for h in range(mine)], axis=1)
            logits = matmul(prefix_refs[j][board], q)
            fold = fold_columns(plan, here, prefix_refs[j][boards], board, boards, heads)
            own_logit = per_head(x, query_rows)
            own_value = per_head(x, query_rows + 2 * mine)
            peak = jnp.maximum(jnp.max(logits, axis=0, keepdims=True), own_logit)
            weight = jnp.exp2((logits - peak) * scale)
            own_weight = jnp.exp2((own_logit - peak) * scale)
            denom = jnp.sum(weight, axis=0, keepdims=True) + own_weight
            value = (jnp.sum(weight * fold, axis=0, keepdims=True) + own_value * own_weight) / denom
            score = sum(value[:, h * slots : (h + 1) * slots] for h in range(mine))
            scores[here ^ j, pl.ds(board, 1), :] = jnp.where(moves_of(j, board) > 0, score, DEAD)

    gather(0, taken_even)

    def step(at, carry):
        board = 2 * at
        gather(jnp.minimum(board + 1, boards - 1), taken_odd)
        score_board(board, taken_even)
        gather(jnp.minimum(board + 2, boards - 1), taken_even)
        score_board(jnp.minimum(board + 1, boards - 1), taken_odd)
        return carry

    lax.fori_loop(0, -(-boards // 2), step, 0)
    live = scores[...] > 0.5 * DEAD
    count = jnp.sum(jnp.where(live, 1.0, 0.0), axis=2, keepdims=True)
    mean = jnp.sum(jnp.where(live, scores[...], 0.0), axis=2, keepdims=True) / jnp.maximum(count, 1.0)
    centered = jnp.where(live, scores[...] - mean, DEAD)
    for g in range(plan.groups):
        both = jnp.concatenate([centered[g * plan.pair + p] for p in range(plan.pair)], axis=0).astype(BF16)
        for copy in range(out_ref.shape[1]):
            out_ref[g, copy] = both


def finish(plan, parts_ref, board_ref, slot_ref, out_ref):
    line = parts_ref.shape[1]
    columns = []
    for at in range(line):
        total = None
        for g in range(parts_ref.shape[0]):
            for p in range(parts_ref.shape[2]):
                term = parts_ref[g, at, p].astype(F32)
                total = term if total is None else total + term
        columns.append(total)
    scores = jnp.concatenate(columns, axis=0)
    live = scores > 0.5 * DEAD
    peak = jnp.max(scores, axis=1, keepdims=True)
    denom = jnp.sum(jnp.where(live, jnp.exp(scores - peak), 0.0), axis=1, keepdims=True)
    logprob = jnp.where(live, scores - peak - jnp.log(denom), 0.0)
    count = board_ref.shape[1]
    member = lax.broadcasted_iota(jnp.int32, (scores.shape[0], count), 0) == board_ref[...]
    member = jnp.where(member, 1.0, 0.0).astype(BF16)
    found = jnp.zeros((plan.slots, count), F32)
    for _ in range(3):
        rounded = logprob.astype(BF16)
        found = found + matmul(rounded, member, TN)
        logprob = logprob - rounded.astype(F32)
    at = lax.broadcasted_iota(jnp.int32, (plan.slots, count), 0) == slot_ref[...]
    out_ref[...] = jnp.sum(jnp.where(at, found, 0.0), axis=0, keepdims=True)


def untouched():
    return pl.BlockSpec(memory_space=pl.ANY)


def local_call(kernel, place, args, outs, scratch=(), mib=40, copied=(), flops=0, nbytes=0, aliases=None):
    vmem = pl.BlockSpec(memory_space=pltpu.VMEM)
    return pl.pallas_call(
        kernel,
        out_shape=outs,
        in_specs=[pl.BlockSpec(memory_space=pltpu.SMEM)]
        + [untouched() if at in copied else vmem for at in range(len(args))],
        out_specs=jax.tree.map(lambda x: vmem, outs),
        scratch_shapes=scratch,
        input_output_aliases=aliases or {},
        compiler_params=limits(mib),
        cost_estimate=cost(flops, nbytes),
    )(place, *args)


def cost(flops, nbytes):
    return pl.CostEstimate(flops=int(flops), bytes_accessed=int(nbytes), transcendentals=0)


def swap(x, names, size, step):
    return lax.ppermute(x, names, [(at, at ^ step) for at in range(size)])


def shape(dims, dtype):
    return jax.ShapeDtypeStruct(tuple(dims), dtype)


def turn_table(position):
    frequency = THETA ** (-2.0 * np.arange(HALF, dtype=np.float32) / HD)
    angles = np.float32(position) * frequency.astype(np.float32)
    return np.stack([np.cos(angles), np.sin(angles)], axis=1).astype(np.float32)


def per_device(prefix_kv, move_ids, move_board, move_table, norm_gain, w_query, w_keyval, w_score):
    row_count = move_ids.shape[0]
    boards_here, prefix_len, _ = prefix_kv.shape
    moves, width = move_table.shape
    groups, line, pair = lax.axis_size("groups"), lax.axis_size("line"), lax.axis_size("pair")
    board_total = boards_here * line * pair
    capacity = max(2, (2 * row_count + board_total - 1) // board_total)
    heads = w_query.shape[1] // HD
    depth = w_query.shape[0]
    plan = Plan(groups, line, pair, heads, capacity, pair * boards_here, depth)
    group_at = lax.axis_index("groups").astype(jnp.int32)
    line_at = lax.axis_index("line").astype(jnp.int32)
    pair_at = lax.axis_index("pair").astype(jnp.int32)
    place = jnp.stack([group_at, line_at, line_at * pair + pair_at, group_at * pair + pair_at])
    ws = w_score.reshape(heads, HD)
    slab_axes = ("groups", "pair")
    board_row = move_board.reshape(1, row_count)

    half_cols = w_query.shape[1] // groups
    packed = local_call(
        functools.partial(pack_weights, plan),
        group_at.reshape(1),
        (w_query, w_keyval, ws, board_row, move_ids.reshape(1, row_count)),
        shape((plan.peers, *plan.sent), BF16),
        [
            pltpu.VMEM((depth, half_cols), BF16),
            pltpu.VMEM((depth, 2 * HD), BF16),
            pltpu.VMEM((heads, HD), BF16),
            pltpu.VMEM((1, row_count), jnp.int32),
            pltpu.VMEM((1, row_count), jnp.int32),
            pltpu.VMEM((plan.peers * plan.rows, half_cols + 2 * HD), F32),
            pltpu.SemaphoreType.DMA((5,)),
        ],
        62,
        range(5),
    )
    weights = lax.all_to_all(packed, ("line", "pair"), split_axis=0, concat_axis=0, tiled=True)

    payload = pl.pallas_call(
        functools.partial(pack_prefix, plan),
        out_shape=shape((boards_here + 1, prefix_len, HD), BF16),
        in_specs=[untouched()] * 3,
        out_specs=pl.BlockSpec(memory_space=pltpu.VMEM),
        scratch_shapes=[
            pltpu.VMEM((boards_here, prefix_len, HD), BF16),
            pltpu.VMEM((heads, HD), BF16),
            pltpu.SemaphoreType.DMA((3,)),
        ],
        compiler_params=limits(56),
        cost_estimate=cost(0, 0),
    )(prefix_kv, ws, packed)
    beside = swap(payload, slab_axes, plan.slab, 1)
    across = swap(payload, slab_axes, plan.slab, 2)

    block = min(moves, 128)
    vmem = pl.BlockSpec(memory_space=pltpu.VMEM)
    *normed, mark = pl.pallas_call(
        normalize,
        out_shape=[*[shape((moves // 2, width), BF16)] * 2, pltpu.VMEM((8, HD), F32)],
        in_specs=[untouched(), vmem, untouched()],
        out_specs=[untouched(), untouched(), vmem],
        scratch_shapes=[
            pltpu.VMEM((1, width), F32),
            pltpu.VMEM((3, block, width), BF16),
            pltpu.VMEM((3, block, width), BF16),
            pltpu.SemaphoreType.DMA((3,)),
            pltpu.SemaphoreType.DMA((3,)),
        ],
        compiler_params=limits(58),
        cost_estimate=cost(moves * width, moves * width // 4),
    )(move_table, norm_gain.reshape(width // HD, HD), packed)
    turns = turn_table(prefix_len).reshape(line, 1, plan.pairs, 2)
    turns = np.tile(turns, (1, plan.mine, 1, 1)).reshape(line, plan.mine * plan.pairs, 2)
    flat = weights.transpose(1, 0, 2).reshape(plan.rows, width) if depth % HD else weights
    sent = (moves // HD * (plan.q_rows + 2 * plan.mine), HD) if plan.direct else (line, plan.line_rows, moves)
    outs = (shape(sent, BF16), shape((plan.mine, moves), F32))
    across = tied(across, mark)
    diagonal = swap(across, slab_axes, plan.slab, 1)
    full = shape((plan.peers, plan.rows, depth), BF16) if plan.tight else shape(flat.shape, BF16)
    filled, listed = (), None
    for step, after in enumerate((across, across)):
        made = local_call(
            functools.partial(project, plan, step * moves // 2, step == 0),
            place,
            (flat, normed[step], jnp.asarray(turns), after, *filled),
            [*outs, *([shape((plan.share, plan.slots), F32), full] if step == 0 else [])],
            (),
            20,
            (3,),
            moves * width * 1024,
            moves * width,
            {5: 0, 6: 1} if filled else None,
        )
        filled = made[:2]
        if step == 0:
            listed, flat = made[2:]
    queries, own_values = filled
    queries = tied(queries, beside)
    other = swap(listed, slab_axes, plan.slab, pair)
    if plan.direct:
        queries = [queries] + [swap(queries, "line", line, step) for step in range(1, line)]
    else:
        queries = lax.all_to_all(queries, "line", split_axis=0, concat_axis=0, tiled=True)
        queries = [queries.reshape(line * plan.line_rows, moves)]

    query_rows = plan.mine * HD
    back = plan.peers * lax.axis_size("tensor")
    chosen, slot_row = local_call(
        functools.partial(prepare, plan),
        place,
        (board_row, listed, other),
        (
            shape((boards_here, moves, plan.slab * plan.slots), BF16),
            shape((1, row_count), jnp.int32),
        ),
        mib=20,
        flops=10**9,
        nbytes=10**6,
    )
    parts = local_call(
        functools.partial(attend, plan),
        place,
        (own_values, listed, other, chosen, payload, beside, across, diagonal, *queries),
        shape((groups, back, plan.share, plan.slots), BF16),
        [
            pltpu.VMEM((query_rows + 16, moves), BF16),
            pltpu.VMEM((16, moves), F32),
            pltpu.VMEM((plan.slab, boards_here, plan.slots), F32),
            pltpu.VMEM((query_rows + 16, plan.slab * plan.slots), F32),
            pltpu.VMEM((query_rows + 16, plan.slab * plan.slots), F32),
        ],
        24,
    )
    parts = lax.all_to_all(
        parts.reshape(groups * back, plan.share, plan.slots),
        ("groups", "line", "pair", "tensor"),
        split_axis=0,
        concat_axis=0,
        tiled=True,
    )
    parts = parts.reshape(groups, line, back // line, plan.share, plan.slots)
    logprob = pl.pallas_call(
        functools.partial(finish, plan), out_shape=shape((1, row_count), F32), compiler_params=limits(VMEM_MIB)
    )(parts, board_row, slot_row)
    return logprob.reshape(row_count)


def solution(mesh):
    order = ("groups", "dp", "tensor")
    assert mesh.axis_names == order
    pair = 2
    groups, peers, tensor = (mesh.shape[name] for name in order)
    fine = Mesh(mesh.devices.reshape(groups, peers // pair, pair, tensor), ("groups", "line", "pair", "tensor"))
    rows = ("groups", "line", "pair")
    placed = (
        P(rows, None, "tensor"),
        P(rows),
        P(rows, None),
        P(),
        P(),
        P(("line", "pair"), "tensor"),
        P(("line", "pair"), "tensor"),
        P("tensor"),
    )
    return jax.shard_map(per_device, mesh=fine, in_specs=placed, out_specs=P(rows), check_vma=False)
```

```python
import functools
import math

import jax
import jax.numpy as jnp
import numpy as np
from jax import lax
from jax.experimental import pallas as pl
from jax.experimental.pallas import tpu as pltpu
from jax.sharding import Mesh
from jax.sharding import PartitionSpec as P

HD = 128
HALF = HD // 2
EPS = 1e-06
THETA = 5000000.0
DEAD = -1e30
VMEM_MIB = 52
GROUP, LINE, PEER, SLAB = range(4)

F32 = jnp.float32
BF16 = jnp.bfloat16

NN = (((1,), (0,)), ((), ()))
NT = (((1,), (1,)), ((), ()))
TN = (((0,), (0,)), ((), ()))


def matmul(a, b, dims=NN):
    return lax.dot_general(a, b, dims, preferred_element_type=F32)


def limits(mib):
    return pltpu.CompilerParams(vmem_limit_bytes=mib * 1024 * 1024)


class Plan:
    def __init__(self, groups, line, pair, heads, capacity, share, depth):
        self.groups, self.line, self.pair = groups, line, pair
        self.peers = line * pair
        self.slab = groups * pair
        self.heads = heads
        self.mine = heads // self.slab
        self.pairs = HALF // line
        self.q_rows = self.mine * 2 * self.pairs
        self.k_rows = 2 * self.pairs
        self.fold_at = self.q_rows + self.k_rows
        self.list_at = self.fold_at + self.mine
        self.rows = -(-(self.list_at + 1) // 8) * 8
        self.line_rows = -(-(self.q_rows + 2 * self.mine) // 8) * 8
        self.capacity = capacity
        self.share = share
        self.slots = self.peers * capacity
        self.direct = line <= 4
        self.tight = self.pairs % 16 == 0 and depth % HD == 0
        self.chunks = depth // HD
        last = -(-(self.mine + 1) * self.chunks // 16) * 16
        self.sent = (self.fold_at * self.chunks + last, HD) if self.tight else (self.rows, depth)


def pack_weights(plan, place_ref, wq_hbm, wkv_hbm, ws_hbm, board_hbm, ids_hbm, *rest):
    out_ref, wq, wkv, ws_ref, board_ref, ids_ref, pick, sems = rest
    group = place_ref[0]
    half_cols = wq.shape[1]
    columns_here = pl.ds(pl.multiple_of(group * half_cols, HD), half_cols)
    copies = (
        pltpu.make_async_copy(ws_hbm, ws_ref, sems.at[0]),
        pltpu.make_async_copy(board_hbm, board_ref, sems.at[1]),
        pltpu.make_async_copy(ids_hbm, ids_ref, sems.at[2]),
        pltpu.make_async_copy(wq_hbm.at[:, columns_here], wq, sems.at[3]),
        pltpu.make_async_copy(wkv_hbm, wkv, sems.at[4]),
    )
    for copy in copies:
        copy.start()
    for copy in copies[:3]:
        copy.wait()
    count, depth = board_ref.shape[1], wq.shape[0]
    board_row = board_ref[...]
    board_col = jnp.broadcast_to(board_row.astype(F32), (8, count)).T[:, 0:1].astype(jnp.int32)
    own = lax.broadcasted_iota(jnp.int32, (count, count), 0)
    other = lax.broadcasted_iota(jnp.int32, (count, count), 1)
    ahead = jnp.where((board_col == board_row) & (other < own), 1.0, 0.0)
    rank = jnp.sum(ahead, axis=1, keepdims=True).astype(jnp.int32)
    move = ids_ref[...] + 1
    boards, span = plan.line * plan.share, plan.share * plan.capacity
    member = lax.broadcasted_iota(jnp.int32, (boards, count), 0) == board_row
    parts = [jnp.where(member, part.astype(F32), 0.0) for part in (move // 64, move % 64)]
    lane = lax.broadcasted_iota(jnp.int32, (count, depth), 1)
    ranked = jnp.where(rank == (lane % span) % plan.capacity, 1.0, 0.0).astype(BF16)
    found = matmul(jnp.concatenate(parts, axis=0).astype(BF16), ranked)
    lane = lax.broadcasted_iota(jnp.int32, (2 * boards, depth), 1)
    row = lax.broadcasted_iota(jnp.int32, (2 * boards, depth), 0)
    keep = (row // boards == lane // span) & (row % plan.share == (lane % span) // plan.capacity)
    found = jnp.where(keep, found, 0.0)
    lists = []
    for line in range(plan.line):
        at = line * plan.share
        both = found[at : at + plan.share] + found[boards + at : boards + at + plan.share]
        lists.append(jnp.sum(both, axis=0, keepdims=True))

    if plan.tight:
        turn_weights(plan, group, lists, copies[3:], wq, wkv, ws_ref, out_ref)
    else:
        pick_weights(plan, group, lists, copies[3:], wq, wkv, ws_ref, out_ref, pick)


def turn_weights(plan, group, lists, copies, wq, wkv, ws_ref, out_ref):
    for copy in copies:
        copy.wait()
    q = wq[...].T
    k = wkv[:, :HD].T
    folds = matmul(ws_ref[...], wkv[:, HD:], NT)
    row = lax.broadcasted_iota(jnp.int32, folds.shape, 0)
    pairs = plan.pairs
    lanes = [slice(c * HD, (c + 1) * HD) for c in range(plan.chunks)]
    first_last = plan.fold_at * plan.chunks
    zeros = jnp.zeros((plan.sent[0] - first_last - (plan.mine + 1) * plan.chunks, HD), F32)
    for pair in range(plan.pair):
        first = (group * plan.pair + pair) * plan.mine
        mine = [jnp.sum(jnp.where(row == first + h, folds, 0.0), axis=0, keepdims=True) for h in range(plan.mine)]
        for line in range(plan.line):
            peer = line * plan.pair + pair
            for c, lane in enumerate(lanes):
                for part in range(2):
                    entry = part * HALF + line * pairs
                    for h in range(plan.mine):
                        at = c * plan.fold_at + (part * plan.mine + h) * pairs
                        source = (pair * plan.mine + h) * HD + entry
                        out_ref[peer, at : at + pairs] = q[source : source + pairs, lane]
                    at = c * plan.fold_at + plan.q_rows + part * pairs
                    out_ref[peer, at : at + pairs] = k[entry : entry + pairs, lane]
            last = [values[:, lane] for values in (*mine, lists[line]) for lane in lanes]
            out_ref[peer, first_last:] = jnp.concatenate([*last, zeros], axis=0).astype(BF16)


def pick_weights(plan, group, lists, copies, wq, wkv, ws_ref, out_ref, pick):
    rows, half_cols = plan.rows, wq.shape[1]
    r = lax.broadcasted_iota(jnp.int32, (rows, 1), 0)
    part = r // (plan.mine * plan.pairs)
    head = (r // plan.pairs) % plan.mine
    entry = r % plan.pairs
    is_q = r < plan.q_rows
    k_at = r - plan.q_rows
    is_k = (k_at >= 0) & (k_at < plan.k_rows)
    f_at = r - plan.fold_at
    is_f = (f_at >= 0) & (f_at < plan.mine)
    q_lane = lax.broadcasted_iota(jnp.int32, (rows, half_cols), 1)
    k_lane = lax.broadcasted_iota(jnp.int32, (rows, HD), 1)
    ws = ws_ref[...].astype(F32)

    def fill(peer, carry):
        line, pair = peer // plan.pair, peer % plan.pair
        column = (pair * plan.mine + head) * HD + part * HALF + line * plan.pairs + entry
        column = jnp.where(is_q, column, -1)
        at = pl.ds(pl.multiple_of(peer * rows, 8), rows)
        pick[at, :half_cols] = jnp.where(q_lane == column, 1.0, 0.0)
        k_column = (k_at // plan.pairs) * HALF + line * plan.pairs + k_at % plan.pairs
        k_column = jnp.where(is_k, k_column, -1)
        pick[at, half_cols : half_cols + HD] = jnp.where(k_lane == k_column, 1.0, 0.0)
        fold = jnp.zeros((rows, HD), F32)
        my_head = jnp.where(is_f, (group * plan.pair + pair) * plan.mine + f_at, -1)
        for h in range(plan.heads):
            fold = jnp.where(my_head == h, ws[h : h + 1], fold)
        pick[at, half_cols + HD :] = fold
        return carry

    lax.fori_loop(0, plan.peers, fill, 0, unroll=plan.peers <= 8)

    for copy in copies:
        copy.wait()
    left = pick[...].astype(BF16)
    total = matmul(left[:, :half_cols], wq[...], NT) + matmul(left[:, half_cols:], wkv[...], NT)
    for peer in range(plan.peers):
        mine = total[peer * rows : (peer + 1) * rows]
        out_ref[peer] = jnp.where(r == plan.list_at, lists[peer // plan.pair], mine).astype(BF16)


def normalize(plan, place_ref, table_hbm, gain_ref, board_ref, after_ref, *refs):
    *outs, mark_ref, slot_ref, gain, buffers, made, sems, out_sems = refs
    held, block, _ = buffers.shape
    steps = table_hbm.shape[0] // block
    each = outs[0].shape[0] // block

    def copy(step):
        source = table_hbm.at[pl.ds(step * block, block)]
        return pltpu.make_async_copy(source, buffers.at[step % held], sems.at[step % held])

    def store(step):
        target = outs[step // each].at[pl.ds(step % each * block, block)]
        return pltpu.make_async_copy(made.at[step % held], target, out_sems.at[step % held])

    for step in range(min(held, steps)):
        copy(step).start()
    rows = gain_ref[...].astype(F32)
    gain[...] = jnp.concatenate([rows[r : r + 1] for r in range(rows.shape[0])], axis=1)
    for step in range(steps):
        copy(step).wait()
        if step >= held:
            store(step - held).wait()
        raw = buffers[step % held].astype(F32)
        inverse = lax.rsqrt(jnp.mean(raw * raw, axis=-1, keepdims=True) + EPS)
        made[step % held] = (raw * inverse * gain[...]).astype(BF16)
        store(step).start()
        if step + held < steps:
            copy(step + held).start()
    for step in range(max(0, steps - held), steps):
        store(step).wait()
    count = board_ref.shape[1]
    board_row = board_ref[...]
    board_col = jnp.broadcast_to(board_row.astype(F32), (8, count)).T[:, 0:1].astype(jnp.int32)
    ahead = lax.broadcasted_iota(jnp.int32, (count, count), 0) < lax.broadcasted_iota(jnp.int32, (count, count), 1)
    rank = jnp.sum(jnp.where((board_col == board_row) & ahead, 1.0, 0.0), axis=0, keepdims=True)
    slot_ref[...] = rank.astype(jnp.int32) + place_ref[PEER] * plan.capacity
    mark_ref[...] = jnp.zeros_like(mark_ref)


def spread_weights(plan, w_ref, full_ref):
    lists = []
    for s in range(plan.peers):
        for c in range(plan.chunks):
            rows = w_ref[s, c * plan.fold_at : (c + 1) * plan.fold_at]
            full_ref[s, : plan.fold_at, c * HD : (c + 1) * HD] = rows
        last = w_ref[s, plan.fold_at * plan.chunks :].astype(F32)
        last = [
            jnp.concatenate([last[i * plan.chunks + c : i * plan.chunks + c + 1] for c in range(plan.chunks)], axis=1)
            for i in range(plan.mine + 1)
        ]
        zeros = jnp.zeros((plan.rows - plan.list_at, last[0].shape[1]), F32)
        full_ref[s, plan.fold_at :] = jnp.concatenate([*last[: plan.mine], zeros], axis=0).astype(BF16)
        lists.append(last[plan.mine])
    return jnp.concatenate(lists, axis=0)


def list_rows(plan, w_ref):
    if len(w_ref.shape) == 3:
        rows = [w_ref[s].astype(F32)[plan.list_at : plan.list_at + 1] for s in range(plan.peers)]
    else:
        row = w_ref[...].astype(F32)[plan.list_at : plan.list_at + 1]
        span = plan.share * plan.capacity
        rows = [row[:, s * 2 * span : (s + 1) * 2 * span] for s in range(plan.peers)]
    return jnp.concatenate(rows, axis=0)


def read_lists(plan, rows, out_ref):
    share, capacity, peers = plan.share, plan.capacity, plan.peers
    span = share * capacity
    lane = lax.broadcasted_iota(jnp.int32, (share * peers, 2 * span), 1)
    row = lax.broadcasted_iota(jnp.int32, (share * peers, 2 * span), 0)
    lane = jnp.where(lane < span, lane, lane - span)
    spread = jnp.concatenate([rows] * share, axis=0)
    spread = jnp.where(lane // capacity == row // peers, spread, 0.0).astype(BF16)
    c = lax.broadcasted_iota(jnp.int32, (2 * span, plan.slots), 0)
    slot = lax.broadcasted_iota(jnp.int32, (2 * span, plan.slots), 1)
    scale = jnp.where(c < span, 64.0, 1.0)
    place = jnp.where(c % capacity == slot % capacity, scale, 0.0).astype(BF16)
    listed = matmul(spread, place)
    row = lax.broadcasted_iota(jnp.int32, listed.shape, 0)
    slot = lax.broadcasted_iota(jnp.int32, listed.shape, 1)
    listed = jnp.where(slot // capacity == row % peers, listed, 0.0)
    out_ref[...] = jnp.sum(listed.reshape(share, peers, plan.slots), axis=1)


def project(plan, place, lists, place_ref, w_ref, normed_ref, turn_ref, after_ref, *refs):
    if lists:
        *refs, list_ref, full_ref = refs
        if plan.tight:
            rows = spread_weights(plan, w_ref, full_ref)
            w_ref = full_ref
        else:
            rows = list_rows(plan, w_ref)
            full_ref[...] = w_ref[...]
        read_lists(plan, rows, list_ref)
    q_ref, vo_ref = refs[-2:]
    turns = turn_ref[place_ref[LINE]]
    half, k_half = plan.q_rows // 2, plan.k_rows // 2
    cosine, sine = turns[:, 0:1], turns[:, 1:2]
    cos_k, sin_k = cosine[:k_half], sine[:k_half]
    moves = normed_ref.shape[0]
    block = min(moves, HD)
    every = []
    for start in range(0, moves, block):
        at, to = slice(start, start + block), slice(place + start, place + start + block)
        if len(w_ref.shape) == 3:
            depth = w_ref.shape[2]
            total = None
            for s in range(w_ref.shape[0]):
                term = matmul(w_ref[s], normed_ref[at, s * depth : (s + 1) * depth], NT)
                total = term if total is None else total + term
        else:
            total = matmul(w_ref[...], normed_ref[at, :], NT)
        first, second = total[:half], total[half : 2 * half]
        f_first = (first * cosine - second * sine).astype(BF16).astype(F32)
        f_second = (second * cosine + first * sine).astype(BF16).astype(F32)
        first, second = total[plan.q_rows : plan.q_rows + k_half], total[plan.q_rows + k_half : plan.fold_at]
        k_first = (first * cos_k - second * sin_k).astype(BF16).astype(F32)
        k_second = (second * cos_k + first * sin_k).astype(BF16).astype(F32)
        logits, tails = [], []
        for h in range(plan.mine):
            own = slice(h * k_half, (h + 1) * k_half)
            logit = jnp.sum(f_first[own] * k_first + f_second[own] * k_second, axis=0, keepdims=True)
            logits.append(logit.astype(BF16).astype(F32))
            tails.append(logit - logits[-1])
        if plan.direct:
            chunk = (place + start) // block * plan.q_rows
            q_ref[chunk : chunk + plan.q_rows] = jnp.concatenate([f_first, f_second], axis=0).astype(BF16)
            every += [*logits, *tails]
        else:
            pad = plan.line_rows - plan.q_rows - 2 * plan.mine
            pieces = [f_first, f_second, *logits, *tails]
            if pad:
                pieces.append(jnp.zeros((pad, block), F32))
            out = jnp.concatenate(pieces, axis=0).astype(BF16)
            for line in range(plan.line):
                q_ref[line, :, to] = out
        vo_ref[:, to] = total[plan.fold_at : plan.list_at]
    if plan.direct:
        first = vo_ref.shape[1] // HD * plan.q_rows + place // block * 2 * plan.mine
        q_ref[first : first + len(every)] = jnp.concatenate(every, axis=0).astype(BF16)


def tied(x, *others):
    return pl.pallas_call(
        lambda *refs: None,
        out_shape=shape(x.shape, x.dtype),
        in_specs=[untouched()] * (1 + len(others)),
        out_specs=untouched(),
        input_output_aliases={0: 0},
        compiler_params=limits(1),
        cost_estimate=cost(0, 0),
    )(x, *others)


def pack_prefix(plan, prefix_hbm, ws_hbm, after_ref, out_ref, *scratch):
    values, ws_ref, sems = scratch
    boards = values.shape[0]
    heads = plan.heads
    copies = (
        pltpu.make_async_copy(ws_hbm, ws_ref, sems.at[0]),
        pltpu.make_async_copy(prefix_hbm.at[:, :, pl.ds(HD, HD)], values, sems.at[1]),
        pltpu.make_async_copy(prefix_hbm.at[:, :, pl.ds(0, HD)], out_ref.at[pl.ds(0, boards)], sems.at[2]),
    )
    for copy in copies:
        copy.start()
    copies[0].wait()
    span = HD // boards
    ws = jnp.concatenate([ws_ref[...].astype(F32)] * (HD // heads), axis=0)
    row = lax.broadcasted_iota(jnp.int32, (HD, 1), 0)
    copies[1].wait()
    fold = None
    for board in range(boards):
        keep = (row // span == board) & (row % span < 2 * heads)
        term = matmul(values[board], jnp.where(keep, ws, 0.0).astype(BF16), NT)
        fold = term if fold is None else fold + term
    rounded = fold.astype(BF16).astype(F32)
    lane = lax.broadcasted_iota(jnp.int32, fold.shape, 1)
    out_ref[boards] = jnp.where(lane % span < heads, rounded, fold - rounded).astype(BF16)
    copies[2].wait()


def fold_columns(plan, here, block, board, boards, heads):
    lanes = plan.mine * plan.slots
    row = lax.broadcasted_iota(jnp.int32, (HD, lanes), 0) - board * (HD // boards)
    head = here * plan.mine + lax.broadcasted_iota(jnp.int32, (HD, lanes), 1) // plan.slots
    pick = jnp.where((row == head) | (row == head + heads), 1.0, 0.0).astype(BF16)
    return matmul(block, pick)


def prepare(plan, place_ref, own_ref, other_ref, *rest):
    *prefix_refs, chosen_ref, fold_ref = rest
    here = place_ref[SLAB]
    boards, moves = chosen_ref.shape[0], chosen_ref.shape[1]
    move_at = lax.broadcasted_iota(jnp.int32, (moves, plan.slots), 0) + 1

    def step(board, carry):
        for j in range(plan.slab):
            place = ((here ^ j) % plan.pair) * boards + board
            row = (own_ref, other_ref)[j // plan.pair][pl.ds(place, 1), :].astype(jnp.int32)
            at = slice(j * plan.slots, (j + 1) * plan.slots)
            chosen_ref[board, :, at] = jnp.where(move_at == row, 1.0, 0.0).astype(BF16)
        for j, prefix_ref in enumerate(prefix_refs):
            fold_ref[j, board] = fold_columns(plan, here, prefix_ref[boards], board, boards, plan.heads)
        return carry

    lax.fori_loop(0, boards, step, 0)


def spread_fold(plan, place_ref, prefix_ref, fold_ref):
    boards = fold_ref.shape[0]

    def step(board, carry):
        fold_ref[board] = fold_columns(plan, place_ref[SLAB], prefix_ref[boards], board, boards, plan.heads)
        return carry

    lax.fori_loop(0, boards, step, 0)


def attend(plan, place_ref, vo_ref, own_ref, other_ref, chosen_ref, fold_ref, far_ref, *rest):
    prefix_refs, rest = rest[: plan.slab], rest[plan.slab :]
    *q_refs, out_ref, table, extra, scores, taken_even, taken_odd = rest
    here = place_ref[SLAB]
    mine, heads, slots = plan.mine, plan.heads, plan.slots
    moves = vo_ref.shape[1]
    boards = prefix_refs[0].shape[0] - 1
    query_rows = mine * HD

    mixed = own_logits = None
    for step, q_ref in enumerate(q_refs):
        if plan.direct:
            chunks = range(moves // HD)
            values = jnp.concatenate([q_ref[c * plan.q_rows : (c + 1) * plan.q_rows] for c in chunks], axis=1)
            tails = q_ref[moves // HD * plan.q_rows :].astype(F32)
            tails = jnp.concatenate([tails[c * 2 * mine : (c + 1) * 2 * mine] for c in chunks], axis=1)
            tails = tails[:mine] + tails[mine:]
            own_logits = tails if own_logits is None else own_logits + tails
        else:
            values = q_ref[...]
        r = lax.broadcasted_iota(jnp.int32, (query_rows + 8, values.shape[0]), 0)
        c = lax.broadcasted_iota(jnp.int32, (query_rows + 8, values.shape[0]), 1)
        line, at = (place_ref[LINE] ^ step, c) if plan.direct else (c // plan.line_rows, c % plan.line_rows)
        part, head, entry = at // (mine * plan.pairs), (at // plan.pairs) % mine, at % plan.pairs
        goes = jnp.where(at < plan.q_rows, head * HD + part * HALF + line * plan.pairs + entry, -1)
        tail = at - plan.q_rows
        goes = jnp.where((tail >= 0) & (tail < 2 * mine), query_rows + tail % mine, goes)
        term = matmul(jnp.where(r == goes, 1.0, 0.0).astype(BF16), values)
        mixed = term if mixed is None else mixed + term
    if own_logits is None:
        own_logits = mixed[query_rows : query_rows + mine]
    table[:query_rows] = mixed[:query_rows].astype(BF16)
    extra[...] = jnp.zeros_like(extra)
    for place, value in ((0, own_logits), (2 * mine, vo_ref[...])):
        rounded = value.astype(BF16).astype(F32)
        extra[place : place + mine] = rounded
        extra[place + mine : place + 2 * mine] = value - rounded
    table[query_rows:] = extra[...].astype(BF16)

    scale = math.log2(math.e) / math.sqrt(HD)
    def per_head(x, base):
        pieces = [x[base + h : base + h + 1] + x[base + mine + h : base + mine + h + 1] for h in range(mine)]
        return jnp.concatenate(pieces, axis=1)

    def moves_of(j, board):
        place = ((here ^ j) % plan.pair) * boards + board
        return (own_ref, other_ref)[j // plan.pair][pl.ds(place, 1), :].astype(jnp.int32)

    def gather(board, taken):
        taken[...] = matmul(table[...], chosen_ref[board])

    def score_board(board, taken):
        for j in range(plan.slab):
            x = taken[:, j * slots : (j + 1) * slots]
            q = jnp.concatenate([x[h * HD : (h + 1) * HD].astype(BF16) for h in range(mine)], axis=1)
            logits = matmul(prefix_refs[j][board], q)
            fold = fold_ref[j, board] if j < plan.slab - 1 else far_ref[board]
            own_logit = per_head(x, query_rows)
            own_value = per_head(x, query_rows + 2 * mine)
            peak = jnp.maximum(jnp.max(logits, axis=0, keepdims=True), own_logit)
            weight = jnp.exp2((logits - peak) * scale)
            own_weight = jnp.exp2((own_logit - peak) * scale)
            denom = jnp.sum(weight, axis=0, keepdims=True) + own_weight
            value = (jnp.sum(weight * fold, axis=0, keepdims=True) + own_value * own_weight) / denom
            score = sum(value[:, h * slots : (h + 1) * slots] for h in range(mine))
            scores[here ^ j, pl.ds(board, 1), :] = jnp.where(moves_of(j, board) > 0, score, DEAD)

    gather(0, taken_even)

    def step(at, carry):
        board = 2 * at
        gather(jnp.minimum(board + 1, boards - 1), taken_odd)
        score_board(board, taken_even)
        gather(jnp.minimum(board + 2, boards - 1), taken_even)
        score_board(jnp.minimum(board + 1, boards - 1), taken_odd)
        return carry

    lax.fori_loop(0, -(-boards // 2), step, 0)
    live = scores[...] > 0.5 * DEAD
    count = jnp.sum(jnp.where(live, 1.0, 0.0), axis=2, keepdims=True)
    mean = jnp.sum(jnp.where(live, scores[...], 0.0), axis=2, keepdims=True) / jnp.maximum(count, 1.0)
    centered = jnp.where(live, scores[...] - mean, DEAD)
    for g in range(plan.groups):
        both = jnp.concatenate([centered[g * plan.pair + p] for p in range(plan.pair)], axis=0).astype(BF16)
        for copy in range(out_ref.shape[1]):
            out_ref[g, copy] = both


def finish(plan, parts_ref, board_ref, slot_ref, out_ref):
    line = parts_ref.shape[1]
    columns = []
    for at in range(line):
        total = None
        for g in range(parts_ref.shape[0]):
            for p in range(parts_ref.shape[2]):
                term = parts_ref[g, at, p].astype(F32)
                total = term if total is None else total + term
        columns.append(total)
    scores = jnp.concatenate(columns, axis=0)
    live = scores > 0.5 * DEAD
    peak = jnp.max(scores, axis=1, keepdims=True)
    denom = jnp.sum(jnp.where(live, jnp.exp(scores - peak), 0.0), axis=1, keepdims=True)
    logprob = jnp.where(live, scores - peak - jnp.log(denom), 0.0)
    count = board_ref.shape[1]
    member = lax.broadcasted_iota(jnp.int32, (scores.shape[0], count), 0) == board_ref[...]
    member = jnp.where(member, 1.0, 0.0).astype(BF16)
    found = jnp.zeros((plan.slots, count), F32)
    for _ in range(3):
        rounded = logprob.astype(BF16)
        found = found + matmul(rounded, member, TN)
        logprob = logprob - rounded.astype(F32)
    at = lax.broadcasted_iota(jnp.int32, (plan.slots, count), 0) == slot_ref[...]
    out_ref[...] = jnp.sum(jnp.where(at, found, 0.0), axis=0, keepdims=True)


def untouched():
    return pl.BlockSpec(memory_space=pl.ANY)


def local_call(kernel, place, args, outs, scratch=(), mib=40, copied=(), flops=0, nbytes=0, aliases=None):
    vmem = pl.BlockSpec(memory_space=pltpu.VMEM)
    return pl.pallas_call(
        kernel,
        out_shape=outs,
        in_specs=[pl.BlockSpec(memory_space=pltpu.SMEM)]
        + [untouched() if at in copied else vmem for at in range(len(args))],
        out_specs=jax.tree.map(lambda x: vmem, outs),
        scratch_shapes=scratch,
        input_output_aliases=aliases or {},
        compiler_params=limits(mib),
        cost_estimate=cost(flops, nbytes),
    )(place, *args)


def cost(flops, nbytes):
    return pl.CostEstimate(flops=int(flops), bytes_accessed=int(nbytes), transcendentals=0)


def swap(x, names, size, step):
    return lax.ppermute(x, names, [(at, at ^ step) for at in range(size)])


def shape(dims, dtype):
    return jax.ShapeDtypeStruct(tuple(dims), dtype)


def turn_table(position):
    frequency = THETA ** (-2.0 * np.arange(HALF, dtype=np.float32) / HD)
    angles = np.float32(position) * frequency.astype(np.float32)
    return np.stack([np.cos(angles), np.sin(angles)], axis=1).astype(np.float32)


def per_device(prefix_kv, move_ids, move_board, move_table, norm_gain, w_query, w_keyval, w_score):
    row_count = move_ids.shape[0]
    boards_here, prefix_len, _ = prefix_kv.shape
    moves, width = move_table.shape
    groups, line, pair = lax.axis_size("groups"), lax.axis_size("line"), lax.axis_size("pair")
    board_total = boards_here * line * pair
    capacity = max(2, (2 * row_count + board_total - 1) // board_total)
    heads = w_query.shape[1] // HD
    depth = w_query.shape[0]
    plan = Plan(groups, line, pair, heads, capacity, pair * boards_here, depth)
    group_at = lax.axis_index("groups").astype(jnp.int32)
    line_at = lax.axis_index("line").astype(jnp.int32)
    pair_at = lax.axis_index("pair").astype(jnp.int32)
    place = jnp.stack([group_at, line_at, line_at * pair + pair_at, group_at * pair + pair_at])
    ws = w_score.reshape(heads, HD)
    slab_axes = ("groups", "pair")
    board_row = move_board.reshape(1, row_count)

    half_cols = w_query.shape[1] // groups
    packed = local_call(
        functools.partial(pack_weights, plan),
        group_at.reshape(1),
        (w_query, w_keyval, ws, board_row, move_ids.reshape(1, row_count)),
        shape((plan.peers, *plan.sent), BF16),
        [
            pltpu.VMEM((depth, half_cols), BF16),
            pltpu.VMEM((depth, 2 * HD), BF16),
            pltpu.VMEM((heads, HD), BF16),
            pltpu.VMEM((1, row_count), jnp.int32),
            pltpu.VMEM((1, row_count), jnp.int32),
            pltpu.VMEM((plan.peers * plan.rows, half_cols + 2 * HD), F32),
            pltpu.SemaphoreType.DMA((5,)),
        ],
        62,
        range(5),
    )
    weights = lax.all_to_all(packed, ("line", "pair"), split_axis=0, concat_axis=0, tiled=True)

    payload = pl.pallas_call(
        functools.partial(pack_prefix, plan),
        out_shape=shape((boards_here + 1, prefix_len, HD), BF16),
        in_specs=[untouched()] * 3,
        out_specs=pl.BlockSpec(memory_space=pltpu.VMEM),
        scratch_shapes=[
            pltpu.VMEM((boards_here, prefix_len, HD), BF16),
            pltpu.VMEM((heads, HD), BF16),
            pltpu.SemaphoreType.DMA((3,)),
        ],
        compiler_params=limits(56),
        cost_estimate=cost(0, 0),
    )(prefix_kv, ws, packed)
    beside = swap(payload, slab_axes, plan.slab, 1)
    across = swap(payload, slab_axes, plan.slab, 2)

    block = min(moves, 128)
    vmem = pl.BlockSpec(memory_space=pltpu.VMEM)
    *normed, mark, slot_row = pl.pallas_call(
        functools.partial(normalize, plan),
        out_shape=[*[shape((moves // 2, width), BF16)] * 2, pltpu.VMEM((8, HD), F32), shape((1, row_count), jnp.int32)],
        in_specs=[pl.BlockSpec(memory_space=pltpu.SMEM), untouched(), vmem, vmem, untouched()],
        out_specs=[untouched(), untouched(), vmem, vmem],
        scratch_shapes=[
            pltpu.VMEM((1, width), F32),
            pltpu.VMEM((3, block, width), BF16),
            pltpu.VMEM((3, block, width), BF16),
            pltpu.SemaphoreType.DMA((3,)),
            pltpu.SemaphoreType.DMA((3,)),
        ],
        compiler_params=limits(58),
        cost_estimate=cost(moves * width, moves * width // 4),
    )(place, move_table, norm_gain.reshape(width // HD, HD), board_row, packed)
    turns = turn_table(prefix_len).reshape(line, 1, plan.pairs, 2)
    turns = np.tile(turns, (1, plan.mine, 1, 1)).reshape(line, plan.mine * plan.pairs, 2)
    flat = weights.transpose(1, 0, 2).reshape(plan.rows, width) if depth % HD else weights
    sent = (moves // HD * (plan.q_rows + 2 * plan.mine), HD) if plan.direct else (line, plan.line_rows, moves)
    outs = (shape(sent, BF16), shape((plan.mine, moves), F32))
    across = tied(across, mark)
    diagonal = swap(across, slab_axes, plan.slab, 1)
    full = shape((plan.peers, plan.rows, depth), BF16) if plan.tight else shape(flat.shape, BF16)
    filled, listed = (), None
    for step, after in enumerate((across, across)):
        made = local_call(
            functools.partial(project, plan, step * moves // 2, step == 0),
            place,
            (flat, normed[step], jnp.asarray(turns), after, *filled),
            [*outs, *([shape((plan.share, plan.slots), F32), full] if step == 0 else [])],
            (),
            20,
            (3,),
            moves * width * 1024,
            moves * width,
            {5: 0, 6: 1} if filled else None,
        )
        filled = made[:2]
        if step == 0:
            listed, flat = made[2:]
    queries, own_values = filled
    queries = tied(queries, beside)
    other = swap(listed, slab_axes, plan.slab, pair)
    if plan.direct:
        queries = [queries] + [swap(queries, "line", line, step) for step in range(1, line)]
    else:
        queries = lax.all_to_all(queries, "line", split_axis=0, concat_axis=0, tiled=True)
        queries = [queries.reshape(line * plan.line_rows, moves)]

    query_rows = plan.mine * HD
    back = plan.peers * lax.axis_size("tensor")
    chosen, folds = local_call(
        functools.partial(prepare, plan),
        place,
        (listed, other, payload, beside, across),
        (
            shape((boards_here, moves, plan.slab * plan.slots), BF16),
            shape((plan.slab - 1, boards_here, prefix_len, plan.mine * plan.slots), F32),
        ),
        mib=20,
        flops=10**9,
        nbytes=10**6,
    )
    far = local_call(
        functools.partial(spread_fold, plan),
        place,
        (diagonal,),
        shape((boards_here, prefix_len, plan.mine * plan.slots), F32),
        mib=20,
    )
    parts = local_call(
        functools.partial(attend, plan),
        place,
        (own_values, listed, other, chosen, folds, far, payload, beside, across, diagonal, *queries),
        shape((groups, back, plan.share, plan.slots), BF16),
        [
            pltpu.VMEM((query_rows + 8, moves), BF16),
            pltpu.VMEM((8, moves), F32),
            pltpu.VMEM((plan.slab, boards_here, plan.slots), F32),
            pltpu.VMEM((query_rows + 8, plan.slab * plan.slots), F32),
            pltpu.VMEM((query_rows + 8, plan.slab * plan.slots), F32),
        ],
        24,
    )
    parts = lax.all_to_all(
        parts.reshape(groups * back, plan.share, plan.slots),
        ("groups", "line", "pair", "tensor"),
        split_axis=0,
        concat_axis=0,
        tiled=True,
    )
    parts = parts.reshape(groups, line, back // line, plan.share, plan.slots)
    logprob = pl.pallas_call(
        functools.partial(finish, plan), out_shape=shape((1, row_count), F32), compiler_params=limits(VMEM_MIB)
    )(parts, board_row, slot_row)
    return logprob.reshape(row_count)


def solution(mesh):
    order = ("groups", "dp", "tensor")
    assert mesh.axis_names == order
    pair = 2
    groups, peers, tensor = (mesh.shape[name] for name in order)
    fine = Mesh(mesh.devices.reshape(groups, peers // pair, pair, tensor), ("groups", "line", "pair", "tensor"))
    rows = ("groups", "line", "pair")
    placed = (
        P(rows, None, "tensor"),
        P(rows),
        P(rows, None),
        P(),
        P(),
        P(("line", "pair"), "tensor"),
        P(("line", "pair"), "tensor"),
        P("tensor"),
    )
    return jax.shard_map(per_device, mesh=fine, in_specs=placed, out_specs=P(rows), check_vma=False)
```

```python
import functools
import math

import jax
import jax.numpy as jnp
import numpy as np
from jax import lax
from jax.experimental import pallas as pl
from jax.experimental.pallas import tpu as pltpu
from jax.sharding import Mesh
from jax.sharding import PartitionSpec as P

HD = 128
HALF = HD // 2
EPS = 1e-06
THETA = 5000000.0
DEAD = -1e30
VMEM_MIB = 52
GROUP, LINE, PEER, SLAB = range(4)

F32 = jnp.float32
BF16 = jnp.bfloat16

NN = (((1,), (0,)), ((), ()))
NT = (((1,), (1,)), ((), ()))
TN = (((0,), (0,)), ((), ()))


def matmul(a, b, dims=NN):
    return lax.dot_general(a, b, dims, preferred_element_type=F32)


def limits(mib):
    return pltpu.CompilerParams(vmem_limit_bytes=mib * 1024 * 1024)


class Plan:
    def __init__(self, groups, line, pair, heads, capacity, share, depth):
        self.groups, self.line, self.pair = groups, line, pair
        self.peers = line * pair
        self.slab = groups * pair
        self.heads = heads
        self.mine = heads // self.slab
        self.pairs = HALF // line
        self.q_rows = self.mine * 2 * self.pairs
        self.k_rows = 2 * self.pairs
        self.fold_at = self.q_rows + self.k_rows
        self.list_at = self.fold_at + self.mine
        self.rows = -(-(self.list_at + 1) // 8) * 8
        self.line_rows = -(-(self.q_rows + 2 * self.mine) // 8) * 8
        self.capacity = capacity
        self.share = share
        self.slots = self.peers * capacity
        self.direct = line <= 4
        self.tight = self.pairs % 16 == 0 and depth % HD == 0
        self.chunks = depth // HD
        last = -(-(self.mine + 1) * self.chunks // 16) * 16
        self.sent = (self.fold_at * self.chunks + last, HD) if self.tight else (self.rows, depth)


def pack_weights(plan, place_ref, wq_hbm, wkv_hbm, ws_hbm, board_hbm, ids_hbm, *rest):
    out_ref, wq, wkv, ws_ref, board_ref, ids_ref, pick, sems = rest
    group = place_ref[0]
    half_cols = wq.shape[1]
    columns_here = pl.ds(pl.multiple_of(group * half_cols, HD), half_cols)
    copies = (
        pltpu.make_async_copy(ws_hbm, ws_ref, sems.at[0]),
        pltpu.make_async_copy(board_hbm, board_ref, sems.at[1]),
        pltpu.make_async_copy(ids_hbm, ids_ref, sems.at[2]),
        pltpu.make_async_copy(wq_hbm.at[:, columns_here], wq, sems.at[3]),
        pltpu.make_async_copy(wkv_hbm, wkv, sems.at[4]),
    )
    for copy in copies:
        copy.start()
    for copy in copies[:3]:
        copy.wait()
    count, depth = board_ref.shape[1], wq.shape[0]
    board_row = board_ref[...]
    board_col = jnp.broadcast_to(board_row.astype(F32), (8, count)).T[:, 0:1].astype(jnp.int32)
    own = lax.broadcasted_iota(jnp.int32, (count, count), 0)
    other = lax.broadcasted_iota(jnp.int32, (count, count), 1)
    ahead = jnp.where((board_col == board_row) & (other < own), 1.0, 0.0)
    rank = jnp.sum(ahead, axis=1, keepdims=True).astype(jnp.int32)
    move = ids_ref[...] + 1
    boards, span = plan.line * plan.share, plan.share * plan.capacity
    member = lax.broadcasted_iota(jnp.int32, (boards, count), 0) == board_row
    parts = [jnp.where(member, part.astype(F32), 0.0) for part in (move // 64, move % 64)]
    lane = lax.broadcasted_iota(jnp.int32, (count, depth), 1)
    ranked = jnp.where(rank == (lane % span) % plan.capacity, 1.0, 0.0).astype(BF16)
    found = matmul(jnp.concatenate(parts, axis=0).astype(BF16), ranked)
    lane = lax.broadcasted_iota(jnp.int32, (2 * boards, depth), 1)
    row = lax.broadcasted_iota(jnp.int32, (2 * boards, depth), 0)
    keep = (row // boards == lane // span) & (row % plan.share == (lane % span) // plan.capacity)
    found = jnp.where(keep, found, 0.0)
    lists = []
    for line in range(plan.line):
        at = line * plan.share
        both = found[at : at + plan.share] + found[boards + at : boards + at + plan.share]
        lists.append(jnp.sum(both, axis=0, keepdims=True))

    if plan.tight:
        turn_weights(plan, group, lists, copies[3:], wq, wkv, ws_ref, out_ref)
    else:
        pick_weights(plan, group, lists, copies[3:], wq, wkv, ws_ref, out_ref, pick)


def turn_weights(plan, group, lists, copies, wq, wkv, ws_ref, out_ref):
    for copy in copies:
        copy.wait()
    q = wq[...].T
    k = wkv[:, :HD].T
    folds = matmul(ws_ref[...], wkv[:, HD:], NT)
    row = lax.broadcasted_iota(jnp.int32, folds.shape, 0)
    pairs = plan.pairs
    lanes = [slice(c * HD, (c + 1) * HD) for c in range(plan.chunks)]
    first_last = plan.fold_at * plan.chunks
    zeros = jnp.zeros((plan.sent[0] - first_last - (plan.mine + 1) * plan.chunks, HD), F32)
    for pair in range(plan.pair):
        first = (group * plan.pair + pair) * plan.mine
        mine = [jnp.sum(jnp.where(row == first + h, folds, 0.0), axis=0, keepdims=True) for h in range(plan.mine)]
        for line in range(plan.line):
            peer = line * plan.pair + pair
            for c, lane in enumerate(lanes):
                for part in range(2):
                    entry = part * HALF + line * pairs
                    for h in range(plan.mine):
                        at = c * plan.fold_at + (part * plan.mine + h) * pairs
                        source = (pair * plan.mine + h) * HD + entry
                        out_ref[peer, at : at + pairs] = q[source : source + pairs, lane]
                    at = c * plan.fold_at + plan.q_rows + part * pairs
                    out_ref[peer, at : at + pairs] = k[entry : entry + pairs, lane]
            last = [values[:, lane] for values in (*mine, lists[line]) for lane in lanes]
            out_ref[peer, first_last:] = jnp.concatenate([*last, zeros], axis=0).astype(BF16)


def pick_weights(plan, group, lists, copies, wq, wkv, ws_ref, out_ref, pick):
    rows, half_cols = plan.rows, wq.shape[1]
    r = lax.broadcasted_iota(jnp.int32, (rows, 1), 0)
    part = r // (plan.mine * plan.pairs)
    head = (r // plan.pairs) % plan.mine
    entry = r % plan.pairs
    is_q = r < plan.q_rows
    k_at = r - plan.q_rows
    is_k = (k_at >= 0) & (k_at < plan.k_rows)
    f_at = r - plan.fold_at
    is_f = (f_at >= 0) & (f_at < plan.mine)
    q_lane = lax.broadcasted_iota(jnp.int32, (rows, half_cols), 1)
    k_lane = lax.broadcasted_iota(jnp.int32, (rows, HD), 1)
    ws = ws_ref[...].astype(F32)

    def fill(peer, carry):
        line, pair = peer // plan.pair, peer % plan.pair
        column = (pair * plan.mine + head) * HD + part * HALF + line * plan.pairs + entry
        column = jnp.where(is_q, column, -1)
        at = pl.ds(pl.multiple_of(peer * rows, 8), rows)
        pick[at, :half_cols] = jnp.where(q_lane == column, 1.0, 0.0)
        k_column = (k_at // plan.pairs) * HALF + line * plan.pairs + k_at % plan.pairs
        k_column = jnp.where(is_k, k_column, -1)
        pick[at, half_cols : half_cols + HD] = jnp.where(k_lane == k_column, 1.0, 0.0)
        fold = jnp.zeros((rows, HD), F32)
        my_head = jnp.where(is_f, (group * plan.pair + pair) * plan.mine + f_at, -1)
        for h in range(plan.heads):
            fold = jnp.where(my_head == h, ws[h : h + 1], fold)
        pick[at, half_cols + HD :] = fold
        return carry

    lax.fori_loop(0, plan.peers, fill, 0, unroll=plan.peers <= 8)

    for copy in copies:
        copy.wait()
    left = pick[...].astype(BF16)
    total = matmul(left[:, :half_cols], wq[...], NT) + matmul(left[:, half_cols:], wkv[...], NT)
    for peer in range(plan.peers):
        mine = total[peer * rows : (peer + 1) * rows]
        out_ref[peer] = jnp.where(r == plan.list_at, lists[peer // plan.pair], mine).astype(BF16)


def normalize(plan, place_ref, table_hbm, gain_ref, board_ref, after_ref, *refs):
    *outs, mark_ref, slot_ref, gain, buffers, made, sems, out_sems = refs
    held, block, _ = buffers.shape
    steps = table_hbm.shape[0] // block
    each = outs[0].shape[0] // block

    def copy(step):
        source = table_hbm.at[pl.ds(step * block, block)]
        return pltpu.make_async_copy(source, buffers.at[step % held], sems.at[step % held])

    def store(step):
        target = outs[step // each].at[pl.ds(step % each * block, block)]
        return pltpu.make_async_copy(made.at[step % held], target, out_sems.at[step % held])

    for step in range(min(held, steps)):
        copy(step).start()
    rows = gain_ref[...].astype(F32)
    gain[...] = jnp.concatenate([rows[r : r + 1] for r in range(rows.shape[0])], axis=1)
    for step in range(steps):
        copy(step).wait()
        if step >= held:
            store(step - held).wait()
        raw = buffers[step % held].astype(F32)
        inverse = lax.rsqrt(jnp.mean(raw * raw, axis=-1, keepdims=True) + EPS)
        made[step % held] = (raw * inverse * gain[...]).astype(BF16)
        store(step).start()
        if step + held < steps:
            copy(step + held).start()
    for step in range(max(0, steps - held), steps):
        store(step).wait()
    count = board_ref.shape[1]
    board_row = board_ref[...]
    board_col = jnp.broadcast_to(board_row.astype(F32), (8, count)).T[:, 0:1].astype(jnp.int32)
    ahead = lax.broadcasted_iota(jnp.int32, (count, count), 0) < lax.broadcasted_iota(jnp.int32, (count, count), 1)
    rank = jnp.sum(jnp.where((board_col == board_row) & ahead, 1.0, 0.0), axis=0, keepdims=True)
    slot_ref[...] = rank.astype(jnp.int32) + place_ref[PEER] * plan.capacity
    mark_ref[...] = jnp.zeros_like(mark_ref)


def spread_weights(plan, w_ref, full_ref):
    lists = []
    for s in range(plan.peers):
        for c in range(plan.chunks):
            rows = w_ref[s, c * plan.fold_at : (c + 1) * plan.fold_at]
            full_ref[s, : plan.fold_at, c * HD : (c + 1) * HD] = rows
        last = w_ref[s, plan.fold_at * plan.chunks :].astype(F32)
        last = [
            jnp.concatenate([last[i * plan.chunks + c : i * plan.chunks + c + 1] for c in range(plan.chunks)], axis=1)
            for i in range(plan.mine + 1)
        ]
        zeros = jnp.zeros((plan.rows - plan.list_at, last[0].shape[1]), F32)
        full_ref[s, plan.fold_at :] = jnp.concatenate([*last[: plan.mine], zeros], axis=0).astype(BF16)
        lists.append(last[plan.mine])
    return jnp.concatenate(lists, axis=0)


def list_rows(plan, w_ref):
    if len(w_ref.shape) == 3:
        rows = [w_ref[s].astype(F32)[plan.list_at : plan.list_at + 1] for s in range(plan.peers)]
    else:
        row = w_ref[...].astype(F32)[plan.list_at : plan.list_at + 1]
        span = plan.share * plan.capacity
        rows = [row[:, s * 2 * span : (s + 1) * 2 * span] for s in range(plan.peers)]
    return jnp.concatenate(rows, axis=0)


def read_lists(plan, rows, out_ref):
    share, capacity, peers = plan.share, plan.capacity, plan.peers
    span = share * capacity
    lane = lax.broadcasted_iota(jnp.int32, (share * peers, 2 * span), 1)
    row = lax.broadcasted_iota(jnp.int32, (share * peers, 2 * span), 0)
    lane = jnp.where(lane < span, lane, lane - span)
    spread = jnp.concatenate([rows] * share, axis=0)
    spread = jnp.where(lane // capacity == row // peers, spread, 0.0).astype(BF16)
    c = lax.broadcasted_iota(jnp.int32, (2 * span, plan.slots), 0)
    slot = lax.broadcasted_iota(jnp.int32, (2 * span, plan.slots), 1)
    scale = jnp.where(c < span, 64.0, 1.0)
    place = jnp.where(c % capacity == slot % capacity, scale, 0.0).astype(BF16)
    listed = matmul(spread, place)
    row = lax.broadcasted_iota(jnp.int32, listed.shape, 0)
    slot = lax.broadcasted_iota(jnp.int32, listed.shape, 1)
    listed = jnp.where(slot // capacity == row % peers, listed, 0.0)
    out_ref[...] = jnp.sum(listed.reshape(share, peers, plan.slots), axis=1)


def project(plan, place, lists, place_ref, w_ref, normed_ref, turn_ref, after_ref, *refs):
    if lists:
        *refs, list_ref, full_ref = refs
        if plan.tight:
            rows = spread_weights(plan, w_ref, full_ref)
            w_ref = full_ref
        else:
            rows = list_rows(plan, w_ref)
            full_ref[...] = w_ref[...]
        read_lists(plan, rows, list_ref)
    q_ref, vo_ref = refs[-2:]
    turns = turn_ref[place_ref[LINE]]
    half, k_half = plan.q_rows // 2, plan.k_rows // 2
    cosine, sine = turns[:, 0:1], turns[:, 1:2]
    cos_k, sin_k = cosine[:k_half], sine[:k_half]
    moves = normed_ref.shape[0]
    block = min(moves, HD)
    every = []
    for start in range(0, moves, block):
        at, to = slice(start, start + block), slice(place + start, place + start + block)
        if len(w_ref.shape) == 3:
            depth = w_ref.shape[2]
            total = None
            for s in range(w_ref.shape[0]):
                term = matmul(w_ref[s], normed_ref[at, s * depth : (s + 1) * depth], NT)
                total = term if total is None else total + term
        else:
            total = matmul(w_ref[...], normed_ref[at, :], NT)
        first, second = total[:half], total[half : 2 * half]
        f_first = (first * cosine - second * sine).astype(BF16).astype(F32)
        f_second = (second * cosine + first * sine).astype(BF16).astype(F32)
        first, second = total[plan.q_rows : plan.q_rows + k_half], total[plan.q_rows + k_half : plan.fold_at]
        k_first = (first * cos_k - second * sin_k).astype(BF16).astype(F32)
        k_second = (second * cos_k + first * sin_k).astype(BF16).astype(F32)
        logits, tails = [], []
        for h in range(plan.mine):
            own = slice(h * k_half, (h + 1) * k_half)
            logit = jnp.sum(f_first[own] * k_first + f_second[own] * k_second, axis=0, keepdims=True)
            logits.append(logit.astype(BF16).astype(F32))
            tails.append(logit - logits[-1])
        if plan.direct:
            chunk = (place + start) // block * plan.q_rows
            q_ref[chunk : chunk + plan.q_rows] = jnp.concatenate([f_first, f_second], axis=0).astype(BF16)
            every += [*logits, *tails]
        else:
            pad = plan.line_rows - plan.q_rows - 2 * plan.mine
            pieces = [f_first, f_second, *logits, *tails]
            if pad:
                pieces.append(jnp.zeros((pad, block), F32))
            out = jnp.concatenate(pieces, axis=0).astype(BF16)
            for line in range(plan.line):
                q_ref[line, :, to] = out
        vo_ref[:, to] = total[plan.fold_at : plan.list_at]
    if plan.direct:
        first = vo_ref.shape[1] // HD * plan.q_rows + place // block * 2 * plan.mine
        q_ref[first : first + len(every)] = jnp.concatenate(every, axis=0).astype(BF16)


def tied(x, *others):
    return pl.pallas_call(
        lambda *refs: None,
        out_shape=shape(x.shape, x.dtype),
        in_specs=[untouched()] * (1 + len(others)),
        out_specs=untouched(),
        input_output_aliases={0: 0},
        compiler_params=limits(1),
        cost_estimate=cost(0, 0),
    )(x, *others)


def pack_prefix(plan, prefix_hbm, ws_hbm, after_ref, out_ref, *scratch):
    values, ws_ref, sems = scratch
    boards = values.shape[0]
    heads = plan.heads
    copies = (
        pltpu.make_async_copy(ws_hbm, ws_ref, sems.at[0]),
        pltpu.make_async_copy(prefix_hbm.at[:, :, pl.ds(HD, HD)], values, sems.at[1]),
        pltpu.make_async_copy(prefix_hbm.at[:, :, pl.ds(0, HD)], out_ref.at[pl.ds(0, boards)], sems.at[2]),
    )
    for copy in copies:
        copy.start()
    copies[0].wait()
    span = HD // boards
    ws = jnp.concatenate([ws_ref[...].astype(F32)] * (HD // heads), axis=0)
    row = lax.broadcasted_iota(jnp.int32, (HD, 1), 0)
    copies[1].wait()
    fold = None
    for board in range(boards):
        keep = (row // span == board) & (row % span < 2 * heads)
        term = matmul(values[board], jnp.where(keep, ws, 0.0).astype(BF16), NT)
        fold = term if fold is None else fold + term
    rounded = fold.astype(BF16).astype(F32)
    lane = lax.broadcasted_iota(jnp.int32, fold.shape, 1)
    out_ref[boards] = jnp.where(lane % span < heads, rounded, fold - rounded).astype(BF16)
    copies[2].wait()


def fold_columns(plan, here, block, board, boards, heads):
    lanes = plan.mine * plan.slots
    row = lax.broadcasted_iota(jnp.int32, (HD, lanes), 0) - board * (HD // boards)
    head = here * plan.mine + lax.broadcasted_iota(jnp.int32, (HD, lanes), 1) // plan.slots
    pick = jnp.where((row == head) | (row == head + heads), 1.0, 0.0).astype(BF16)
    return matmul(block, pick)


def prepare(plan, place_ref, own_ref, other_ref, *rest):
    *prefix_refs, chosen_ref, fold_ref = rest
    here = place_ref[SLAB]
    boards, moves = chosen_ref.shape[0], chosen_ref.shape[1]
    move_at = lax.broadcasted_iota(jnp.int32, (moves, plan.slots), 0) + 1

    def step(board, carry):
        for j in range(plan.slab):
            place = ((here ^ j) % plan.pair) * boards + board
            row = (own_ref, other_ref)[j // plan.pair][pl.ds(place, 1), :].astype(jnp.int32)
            at = slice(j * plan.slots, (j + 1) * plan.slots)
            chosen_ref[board, :, at] = jnp.where(move_at == row, 1.0, 0.0).astype(BF16)
        for j, prefix_ref in enumerate(prefix_refs):
            fold_ref[j, board] = fold_columns(plan, here, prefix_ref[boards], board, boards, plan.heads)
        return carry

    lax.fori_loop(0, boards, step, 0)


def attend(plan, place_ref, vo_ref, own_ref, other_ref, chosen_ref, fold_ref, *rest):
    prefix_refs, rest = rest[: plan.slab], rest[plan.slab :]
    *q_refs, out_ref, table, extra, scores, taken_even, taken_odd = rest
    here = place_ref[SLAB]
    mine, heads, slots = plan.mine, plan.heads, plan.slots
    moves = vo_ref.shape[1]
    boards = prefix_refs[0].shape[0] - 1
    query_rows = mine * HD

    mixed = own_logits = None
    for step, q_ref in enumerate(q_refs):
        if plan.direct:
            chunks = range(moves // HD)
            values = jnp.concatenate([q_ref[c * plan.q_rows : (c + 1) * plan.q_rows] for c in chunks], axis=1)
            tails = q_ref[moves // HD * plan.q_rows :].astype(F32)
            tails = jnp.concatenate([tails[c * 2 * mine : (c + 1) * 2 * mine] for c in chunks], axis=1)
            tails = tails[:mine] + tails[mine:]
            own_logits = tails if own_logits is None else own_logits + tails
        else:
            values = q_ref[...]
        r = lax.broadcasted_iota(jnp.int32, (query_rows + 8, values.shape[0]), 0)
        c = lax.broadcasted_iota(jnp.int32, (query_rows + 8, values.shape[0]), 1)
        line, at = (place_ref[LINE] ^ step, c) if plan.direct else (c // plan.line_rows, c % plan.line_rows)
        part, head, entry = at // (mine * plan.pairs), (at // plan.pairs) % mine, at % plan.pairs
        goes = jnp.where(at < plan.q_rows, head * HD + part * HALF + line * plan.pairs + entry, -1)
        tail = at - plan.q_rows
        goes = jnp.where((tail >= 0) & (tail < 2 * mine), query_rows + tail % mine, goes)
        term = matmul(jnp.where(r == goes, 1.0, 0.0).astype(BF16), values)
        mixed = term if mixed is None else mixed + term
    if own_logits is None:
        own_logits = mixed[query_rows : query_rows + mine]
    table[:query_rows] = mixed[:query_rows].astype(BF16)
    extra[...] = jnp.zeros_like(extra)
    for place, value in ((0, own_logits), (2 * mine, vo_ref[...])):
        rounded = value.astype(BF16).astype(F32)
        extra[place : place + mine] = rounded
        extra[place + mine : place + 2 * mine] = value - rounded
    table[query_rows:] = extra[...].astype(BF16)

    scale = math.log2(math.e) / math.sqrt(HD)
    def per_head(x, base):
        pieces = [x[base + h : base + h + 1] + x[base + mine + h : base + mine + h + 1] for h in range(mine)]
        return jnp.concatenate(pieces, axis=1)

    def moves_of(j, board):
        place = ((here ^ j) % plan.pair) * boards + board
        return (own_ref, other_ref)[j // plan.pair][pl.ds(place, 1), :].astype(jnp.int32)

    def gather(board, taken):
        taken[...] = matmul(table[...], chosen_ref[board])

    def score_board(board, taken):
        for j in range(plan.slab):
            x = taken[:, j * slots : (j + 1) * slots]
            q = jnp.concatenate([x[h * HD : (h + 1) * HD].astype(BF16) for h in range(mine)], axis=1)
            logits = matmul(prefix_refs[j][board], q)
            if j < plan.slab - 1:
                fold = fold_ref[j, board]
            else:
                fold = fold_columns(plan, here, prefix_refs[j][boards], board, boards, heads)
            own_logit = per_head(x, query_rows)
            own_value = per_head(x, query_rows + 2 * mine)
            peak = jnp.maximum(jnp.max(logits, axis=0, keepdims=True), own_logit)
            weight = jnp.exp2((logits - peak) * scale)
            own_weight = jnp.exp2((own_logit - peak) * scale)
            denom = jnp.sum(weight, axis=0, keepdims=True) + own_weight
            value = (jnp.sum(weight * fold, axis=0, keepdims=True) + own_value * own_weight) / denom
            score = sum(value[:, h * slots : (h + 1) * slots] for h in range(mine))
            scores[here ^ j, pl.ds(board, 1), :] = jnp.where(moves_of(j, board) > 0, score, DEAD)

    gather(0, taken_even)

    def step(at, carry):
        board = 2 * at
        gather(jnp.minimum(board + 1, boards - 1), taken_odd)
        score_board(board, taken_even)
        gather(jnp.minimum(board + 2, boards - 1), taken_even)
        score_board(jnp.minimum(board + 1, boards - 1), taken_odd)
        return carry

    lax.fori_loop(0, -(-boards // 2), step, 0)
    live = scores[...] > 0.5 * DEAD
    count = jnp.sum(jnp.where(live, 1.0, 0.0), axis=2, keepdims=True)
    mean = jnp.sum(jnp.where(live, scores[...], 0.0), axis=2, keepdims=True) / jnp.maximum(count, 1.0)
    centered = jnp.where(live, scores[...] - mean, DEAD)
    for g in range(plan.groups):
        both = jnp.concatenate([centered[g * plan.pair + p] for p in range(plan.pair)], axis=0).astype(BF16)
        for copy in range(out_ref.shape[1]):
            out_ref[g, copy] = both


def finish(plan, parts_ref, board_ref, slot_ref, out_ref):
    line = parts_ref.shape[1]
    columns = []
    for at in range(line):
        total = None
        for g in range(parts_ref.shape[0]):
            for p in range(parts_ref.shape[2]):
                term = parts_ref[g, at, p].astype(F32)
                total = term if total is None else total + term
        columns.append(total)
    scores = jnp.concatenate(columns, axis=0)
    live = scores > 0.5 * DEAD
    peak = jnp.max(scores, axis=1, keepdims=True)
    denom = jnp.sum(jnp.where(live, jnp.exp(scores - peak), 0.0), axis=1, keepdims=True)
    logprob = jnp.where(live, scores - peak - jnp.log(denom), 0.0)
    count = board_ref.shape[1]
    member = lax.broadcasted_iota(jnp.int32, (scores.shape[0], count), 0) == board_ref[...]
    member = jnp.where(member, 1.0, 0.0).astype(BF16)
    rounded = logprob.astype(BF16)
    pieces = jnp.concatenate([rounded, (logprob - rounded.astype(F32)).astype(BF16)], axis=1)
    found = matmul(pieces, member, TN)
    found = found[: plan.slots] + found[plan.slots :]
    at = lax.broadcasted_iota(jnp.int32, (plan.slots, count), 0) == slot_ref[...]
    out_ref[...] = jnp.sum(jnp.where(at, found, 0.0), axis=0, keepdims=True)


def untouched():
    return pl.BlockSpec(memory_space=pl.ANY)


def local_call(kernel, place, args, outs, scratch=(), mib=40, copied=(), flops=0, nbytes=0, aliases=None):
    vmem = pl.BlockSpec(memory_space=pltpu.VMEM)
    return pl.pallas_call(
        kernel,
        out_shape=outs,
        in_specs=[pl.BlockSpec(memory_space=pltpu.SMEM)]
        + [untouched() if at in copied else vmem for at in range(len(args))],
        out_specs=jax.tree.map(lambda x: vmem, outs),
        scratch_shapes=scratch,
        input_output_aliases=aliases or {},
        compiler_params=limits(mib),
        cost_estimate=cost(flops, nbytes),
    )(place, *args)


def cost(flops, nbytes):
    return pl.CostEstimate(flops=int(flops), bytes_accessed=int(nbytes), transcendentals=0)


def swap(x, names, size, step):
    return lax.ppermute(x, names, [(at, at ^ step) for at in range(size)])


def shape(dims, dtype):
    return jax.ShapeDtypeStruct(tuple(dims), dtype)


def turn_table(position):
    frequency = THETA ** (-2.0 * np.arange(HALF, dtype=np.float32) / HD)
    angles = np.float32(position) * frequency.astype(np.float32)
    return np.stack([np.cos(angles), np.sin(angles)], axis=1).astype(np.float32)


def per_device(prefix_kv, move_ids, move_board, move_table, norm_gain, w_query, w_keyval, w_score):
    row_count = move_ids.shape[0]
    boards_here, prefix_len, _ = prefix_kv.shape
    moves, width = move_table.shape
    groups, line, pair = lax.axis_size("groups"), lax.axis_size("line"), lax.axis_size("pair")
    board_total = boards_here * line * pair
    capacity = max(2, (2 * row_count + board_total - 1) // board_total)
    heads = w_query.shape[1] // HD
    depth = w_query.shape[0]
    plan = Plan(groups, line, pair, heads, capacity, pair * boards_here, depth)
    group_at = lax.axis_index("groups").astype(jnp.int32)
    line_at = lax.axis_index("line").astype(jnp.int32)
    pair_at = lax.axis_index("pair").astype(jnp.int32)
    place = jnp.stack([group_at, line_at, line_at * pair + pair_at, group_at * pair + pair_at])
    ws = w_score.reshape(heads, HD)
    slab_axes = ("groups", "pair")
    board_row = move_board.reshape(1, row_count)

    half_cols = w_query.shape[1] // groups
    packed = local_call(
        functools.partial(pack_weights, plan),
        group_at.reshape(1),
        (w_query, w_keyval, ws, board_row, move_ids.reshape(1, row_count)),
        shape((plan.peers, *plan.sent), BF16),
        [
            pltpu.VMEM((depth, half_cols), BF16),
            pltpu.VMEM((depth, 2 * HD), BF16),
            pltpu.VMEM((heads, HD), BF16),
            pltpu.VMEM((1, row_count), jnp.int32),
            pltpu.VMEM((1, row_count), jnp.int32),
            pltpu.VMEM((plan.peers * plan.rows, half_cols + 2 * HD), F32),
            pltpu.SemaphoreType.DMA((5,)),
        ],
        62,
        range(5),
    )
    weights = lax.all_to_all(packed, ("line", "pair"), split_axis=0, concat_axis=0, tiled=True)

    payload = pl.pallas_call(
        functools.partial(pack_prefix, plan),
        out_shape=shape((boards_here + 1, prefix_len, HD), BF16),
        in_specs=[untouched()] * 3,
        out_specs=pl.BlockSpec(memory_space=pltpu.VMEM),
        scratch_shapes=[
            pltpu.VMEM((boards_here, prefix_len, HD), BF16),
            pltpu.VMEM((heads, HD), BF16),
            pltpu.SemaphoreType.DMA((3,)),
        ],
        compiler_params=limits(56),
        cost_estimate=cost(0, 0),
    )(prefix_kv, ws, packed)
    beside = swap(payload, slab_axes, plan.slab, 1)
    across = swap(payload, slab_axes, plan.slab, 2)

    block = min(moves, 128)
    vmem = pl.BlockSpec(memory_space=pltpu.VMEM)
    *normed, mark, slot_row = pl.pallas_call(
        functools.partial(normalize, plan),
        out_shape=[*[shape((moves // 2, width), BF16)] * 2, pltpu.VMEM((8, HD), F32), shape((1, row_count), jnp.int32)],
        in_specs=[pl.BlockSpec(memory_space=pltpu.SMEM), untouched(), vmem, vmem, untouched()],
        out_specs=[untouched(), untouched(), vmem, vmem],
        scratch_shapes=[
            pltpu.VMEM((1, width), F32),
            pltpu.VMEM((3, block, width), BF16),
            pltpu.VMEM((3, block, width), BF16),
            pltpu.SemaphoreType.DMA((3,)),
            pltpu.SemaphoreType.DMA((3,)),
        ],
        compiler_params=limits(58),
        cost_estimate=cost(moves * width, moves * width // 4),
    )(place, move_table, norm_gain.reshape(width // HD, HD), board_row, packed)
    turns = turn_table(prefix_len).reshape(line, 1, plan.pairs, 2)
    turns = np.tile(turns, (1, plan.mine, 1, 1)).reshape(line, plan.mine * plan.pairs, 2)
    flat = weights.transpose(1, 0, 2).reshape(plan.rows, width) if depth % HD else weights
    sent = (moves // HD * (plan.q_rows + 2 * plan.mine), HD) if plan.direct else (line, plan.line_rows, moves)
    outs = (shape(sent, BF16), shape((plan.mine, moves), F32))
    across = tied(across, mark)
    diagonal = swap(across, slab_axes, plan.slab, 1)
    full = shape((plan.peers, plan.rows, depth), BF16) if plan.tight else shape(flat.shape, BF16)
    filled, listed = (), None
    for step, after in enumerate((across, across)):
        made = local_call(
            functools.partial(project, plan, step * moves // 2, step == 0),
            place,
            (flat, normed[step], jnp.asarray(turns), after, *filled),
            [*outs, *([shape((plan.share, plan.slots), F32), full] if step == 0 else [])],
            (),
            20,
            (3,),
            moves * width * 1024,
            moves * width,
            {5: 0, 6: 1} if filled else None,
        )
        filled = made[:2]
        if step == 0:
            listed, flat = made[2:]
    queries, own_values = filled
    queries = tied(queries, beside)
    other = swap(listed, slab_axes, plan.slab, pair)
    if plan.direct:
        queries = [queries] + [swap(queries, "line", line, step) for step in range(1, line)]
    else:
        queries = lax.all_to_all(queries, "line", split_axis=0, concat_axis=0, tiled=True)
        queries = [queries.reshape(line * plan.line_rows, moves)]

    query_rows = plan.mine * HD
    back = plan.peers * lax.axis_size("tensor")
    chosen, folds = local_call(
        functools.partial(prepare, plan),
        place,
        (listed, other, payload, beside, across),
        (
            shape((boards_here, moves, plan.slab * plan.slots), BF16),
            shape((plan.slab - 1, boards_here, prefix_len, plan.mine * plan.slots), F32),
        ),
        mib=20,
        flops=10**9,
        nbytes=10**6,
    )
    parts = local_call(
        functools.partial(attend, plan),
        place,
        (own_values, listed, other, chosen, folds, payload, beside, across, diagonal, *queries),
        shape((groups, back, plan.share, plan.slots), BF16),
        [
            pltpu.VMEM((query_rows + 16, moves), BF16),
            pltpu.VMEM((16, moves), F32),
            pltpu.VMEM((plan.slab, boards_here, plan.slots), F32),
            pltpu.VMEM((query_rows + 16, plan.slab * plan.slots), F32),
            pltpu.VMEM((query_rows + 16, plan.slab * plan.slots), F32),
        ],
        24,
    )
    parts = lax.all_to_all(
        parts.reshape(groups * back, plan.share, plan.slots),
        ("groups", "line", "pair", "tensor"),
        split_axis=0,
        concat_axis=0,
        tiled=True,
    )
    parts = parts.reshape(groups, line, back // line, plan.share, plan.slots)
    logprob = pl.pallas_call(
        functools.partial(finish, plan), out_shape=shape((1, row_count), F32), compiler_params=limits(VMEM_MIB)
    )(parts, board_row, slot_row)
    return logprob.reshape(row_count)


def solution(mesh):
    order = ("groups", "dp", "tensor")
    assert mesh.axis_names == order
    pair = 2
    groups, peers, tensor = (mesh.shape[name] for name in order)
    fine = Mesh(mesh.devices.reshape(groups, peers // pair, pair, tensor), ("groups", "line", "pair", "tensor"))
    rows = ("groups", "line", "pair")
    placed = (
        P(rows, None, "tensor"),
        P(rows),
        P(rows, None),
        P(),
        P(),
        P(("line", "pair"), "tensor"),
        P(("line", "pair"), "tensor"),
        P("tensor"),
    )
    return jax.shard_map(per_device, mesh=fine, in_specs=placed, out_specs=P(rows), check_vma=False)
```

```python
import functools
import math

import jax
import jax.numpy as jnp
import numpy as np
from jax import lax
from jax.experimental import pallas as pl
from jax.experimental.pallas import tpu as pltpu
from jax.sharding import Mesh
from jax.sharding import PartitionSpec as P

HD = 128
HALF = HD // 2
EPS = 1e-06
THETA = 5000000.0
DEAD = -1e30
VMEM_MIB = 52
GROUP, LINE, PEER, SLAB = range(4)

F32 = jnp.float32
BF16 = jnp.bfloat16

NN = (((1,), (0,)), ((), ()))
NT = (((1,), (1,)), ((), ()))
TN = (((0,), (0,)), ((), ()))


def matmul(a, b, dims=NN):
    return lax.dot_general(a, b, dims, preferred_element_type=F32)


def limits(mib):
    return pltpu.CompilerParams(vmem_limit_bytes=mib * 1024 * 1024)


class Plan:
    def __init__(self, groups, line, pair, heads, capacity, share, depth):
        self.groups, self.line, self.pair = groups, line, pair
        self.peers = line * pair
        self.slab = groups * pair
        self.heads = heads
        self.mine = heads // self.slab
        self.pairs = HALF // line
        self.q_rows = self.mine * 2 * self.pairs
        self.k_rows = 2 * self.pairs
        self.fold_at = self.q_rows + self.k_rows
        self.list_at = self.fold_at + self.mine
        self.rows = -(-(self.list_at + 1) // 8) * 8
        self.line_rows = -(-(self.q_rows + 2 * self.mine) // 8) * 8
        self.capacity = capacity
        self.share = share
        self.slots = self.peers * capacity
        self.direct = line <= 4
        self.tight = self.pairs % 16 == 0 and depth % HD == 0
        self.chunks = depth // HD
        last = -(-(self.mine + 1) * self.chunks // 16) * 16
        self.sent = (self.fold_at * self.chunks + last, HD) if self.tight else (self.rows, depth)


def pack_weights(plan, place_ref, wq_hbm, wkv_hbm, ws_hbm, board_hbm, ids_hbm, *rest):
    out_ref, wq, wkv, ws_ref, board_ref, ids_ref, pick, sems = rest
    group = place_ref[0]
    half_cols = wq.shape[1]
    columns_here = pl.ds(pl.multiple_of(group * half_cols, HD), half_cols)
    copies = (
        pltpu.make_async_copy(ws_hbm, ws_ref, sems.at[0]),
        pltpu.make_async_copy(board_hbm, board_ref, sems.at[1]),
        pltpu.make_async_copy(ids_hbm, ids_ref, sems.at[2]),
        pltpu.make_async_copy(wq_hbm.at[:, columns_here], wq, sems.at[3]),
        pltpu.make_async_copy(wkv_hbm, wkv, sems.at[4]),
    )
    for copy in copies:
        copy.start()
    for copy in copies[:3]:
        copy.wait()
    count, depth = board_ref.shape[1], wq.shape[0]
    board_row = board_ref[...]
    board_col = jnp.broadcast_to(board_row.astype(F32), (8, count)).T[:, 0:1].astype(jnp.int32)
    own = lax.broadcasted_iota(jnp.int32, (count, count), 0)
    other = lax.broadcasted_iota(jnp.int32, (count, count), 1)
    ahead = jnp.where((board_col == board_row) & (other < own), 1.0, 0.0)
    rank = jnp.sum(ahead, axis=1, keepdims=True).astype(jnp.int32)
    move = ids_ref[...] + 1
    boards, span = plan.line * plan.share, plan.share * plan.capacity
    member = lax.broadcasted_iota(jnp.int32, (boards, count), 0) == board_row
    parts = [jnp.where(member, part.astype(F32), 0.0) for part in (move // 64, move % 64)]
    lane = lax.broadcasted_iota(jnp.int32, (count, depth), 1)
    ranked = jnp.where(rank == (lane % span) % plan.capacity, 1.0, 0.0).astype(BF16)
    found = matmul(jnp.concatenate(parts, axis=0).astype(BF16), ranked)
    lane = lax.broadcasted_iota(jnp.int32, (2 * boards, depth), 1)
    row = lax.broadcasted_iota(jnp.int32, (2 * boards, depth), 0)
    keep = (row // boards == lane // span) & (row % plan.share == (lane % span) // plan.capacity)
    found = jnp.where(keep, found, 0.0)
    lists = []
    for line in range(plan.line):
        at = line * plan.share
        both = found[at : at + plan.share] + found[boards + at : boards + at + plan.share]
        lists.append(jnp.sum(both, axis=0, keepdims=True))

    if plan.tight:
        turn_weights(plan, group, lists, copies[3:], wq, wkv, ws_ref, out_ref)
    else:
        pick_weights(plan, group, lists, copies[3:], wq, wkv, ws_ref, out_ref, pick)


def turn_weights(plan, group, lists, copies, wq, wkv, ws_ref, out_ref):
    for copy in copies:
        copy.wait()
    q = wq[...].T
    k = wkv[:, :HD].T
    folds = matmul(ws_ref[...], wkv[:, HD:], NT)
    row = lax.broadcasted_iota(jnp.int32, folds.shape, 0)
    pairs = plan.pairs
    lanes = [slice(c * HD, (c + 1) * HD) for c in range(plan.chunks)]
    first_last = plan.fold_at * plan.chunks
    zeros = jnp.zeros((plan.sent[0] - first_last - (plan.mine + 1) * plan.chunks, HD), F32)
    for pair in range(plan.pair):
        first = (group * plan.pair + pair) * plan.mine
        mine = [jnp.sum(jnp.where(row == first + h, folds, 0.0), axis=0, keepdims=True) for h in range(plan.mine)]
        for line in range(plan.line):
            peer = line * plan.pair + pair
            for c, lane in enumerate(lanes):
                for part in range(2):
                    entry = part * HALF + line * pairs
                    for h in range(plan.mine):
                        at = c * plan.fold_at + (part * plan.mine + h) * pairs
                        source = (pair * plan.mine + h) * HD + entry
                        out_ref[peer, at : at + pairs] = q[source : source + pairs, lane]
                    at = c * plan.fold_at + plan.q_rows + part * pairs
                    out_ref[peer, at : at + pairs] = k[entry : entry + pairs, lane]
            last = [values[:, lane] for values in (*mine, lists[line]) for lane in lanes]
            out_ref[peer, first_last:] = jnp.concatenate([*last, zeros], axis=0).astype(BF16)


def pick_weights(plan, group, lists, copies, wq, wkv, ws_ref, out_ref, pick):
    rows, half_cols = plan.rows, wq.shape[1]
    r = lax.broadcasted_iota(jnp.int32, (rows, 1), 0)
    part = r // (plan.mine * plan.pairs)
    head = (r // plan.pairs) % plan.mine
    entry = r % plan.pairs
    is_q = r < plan.q_rows
    k_at = r - plan.q_rows
    is_k = (k_at >= 0) & (k_at < plan.k_rows)
    f_at = r - plan.fold_at
    is_f = (f_at >= 0) & (f_at < plan.mine)
    q_lane = lax.broadcasted_iota(jnp.int32, (rows, half_cols), 1)
    k_lane = lax.broadcasted_iota(jnp.int32, (rows, HD), 1)
    ws = ws_ref[...].astype(F32)

    def fill(peer, carry):
        line, pair = peer // plan.pair, peer % plan.pair
        column = (pair * plan.mine + head) * HD + part * HALF + line * plan.pairs + entry
        column = jnp.where(is_q, column, -1)
        at = pl.ds(pl.multiple_of(peer * rows, 8), rows)
        pick[at, :half_cols] = jnp.where(q_lane == column, 1.0, 0.0)
        k_column = (k_at // plan.pairs) * HALF + line * plan.pairs + k_at % plan.pairs
        k_column = jnp.where(is_k, k_column, -1)
        pick[at, half_cols : half_cols + HD] = jnp.where(k_lane == k_column, 1.0, 0.0)
        fold = jnp.zeros((rows, HD), F32)
        my_head = jnp.where(is_f, (group * plan.pair + pair) * plan.mine + f_at, -1)
        for h in range(plan.heads):
            fold = jnp.where(my_head == h, ws[h : h + 1], fold)
        pick[at, half_cols + HD :] = fold
        return carry

    lax.fori_loop(0, plan.peers, fill, 0, unroll=plan.peers <= 8)

    for copy in copies:
        copy.wait()
    left = pick[...].astype(BF16)
    total = matmul(left[:, :half_cols], wq[...], NT) + matmul(left[:, half_cols:], wkv[...], NT)
    for peer in range(plan.peers):
        mine = total[peer * rows : (peer + 1) * rows]
        out_ref[peer] = jnp.where(r == plan.list_at, lists[peer // plan.pair], mine).astype(BF16)


def normalize(plan, place_ref, table_hbm, gain_ref, board_ref, after_ref, *refs):
    *outs, mark_ref, slot_ref, gain, buffers, made, sems, out_sems = refs
    held, block, _ = buffers.shape
    steps = table_hbm.shape[0] // block
    each = outs[0].shape[0] // block

    def copy(step):
        source = table_hbm.at[pl.ds(step * block, block)]
        return pltpu.make_async_copy(source, buffers.at[step % held], sems.at[step % held])

    def store(step):
        target = outs[step // each].at[pl.ds(step % each * block, block)]
        return pltpu.make_async_copy(made.at[step % held], target, out_sems.at[step % held])

    for step in range(min(held, steps)):
        copy(step).start()
    rows = gain_ref[...].astype(F32)
    gain[...] = jnp.concatenate([rows[r : r + 1] for r in range(rows.shape[0])], axis=1)
    for step in range(steps):
        copy(step).wait()
        if step >= held:
            store(step - held).wait()
        raw = buffers[step % held].astype(F32)
        inverse = lax.rsqrt(jnp.mean(raw * raw, axis=-1, keepdims=True) + EPS)
        made[step % held] = (raw * inverse * gain[...]).astype(BF16)
        store(step).start()
        if step + held < steps:
            copy(step + held).start()
    for step in range(max(0, steps - held), steps):
        store(step).wait()
    count = board_ref.shape[1]
    board_row = board_ref[...]
    board_col = jnp.broadcast_to(board_row.astype(F32), (8, count)).T[:, 0:1].astype(jnp.int32)
    ahead = lax.broadcasted_iota(jnp.int32, (count, count), 0) < lax.broadcasted_iota(jnp.int32, (count, count), 1)
    rank = jnp.sum(jnp.where((board_col == board_row) & ahead, 1.0, 0.0), axis=0, keepdims=True)
    slot_ref[...] = rank.astype(jnp.int32) + place_ref[PEER] * plan.capacity
    mark_ref[...] = jnp.zeros_like(mark_ref)


def spread_weights(plan, w_ref, full_ref):
    lists = []
    for s in range(plan.peers):
        for c in range(plan.chunks):
            rows = w_ref[s, c * plan.fold_at : (c + 1) * plan.fold_at]
            full_ref[s, : plan.fold_at, c * HD : (c + 1) * HD] = rows
        last = w_ref[s, plan.fold_at * plan.chunks :].astype(F32)
        last = [
            jnp.concatenate([last[i * plan.chunks + c : i * plan.chunks + c + 1] for c in range(plan.chunks)], axis=1)
            for i in range(plan.mine + 1)
        ]
        zeros = jnp.zeros((plan.rows - plan.list_at, last[0].shape[1]), F32)
        full_ref[s, plan.fold_at :] = jnp.concatenate([*last[: plan.mine], zeros], axis=0).astype(BF16)
        lists.append(last[plan.mine])
    return jnp.concatenate(lists, axis=0)


def list_rows(plan, w_ref):
    if len(w_ref.shape) == 3:
        rows = [w_ref[s].astype(F32)[plan.list_at : plan.list_at + 1] for s in range(plan.peers)]
    else:
        row = w_ref[...].astype(F32)[plan.list_at : plan.list_at + 1]
        span = plan.share * plan.capacity
        rows = [row[:, s * 2 * span : (s + 1) * 2 * span] for s in range(plan.peers)]
    return jnp.concatenate(rows, axis=0)


def read_lists(plan, rows, out_ref):
    share, capacity, peers = plan.share, plan.capacity, plan.peers
    span = share * capacity
    lane = lax.broadcasted_iota(jnp.int32, (share * peers, 2 * span), 1)
    row = lax.broadcasted_iota(jnp.int32, (share * peers, 2 * span), 0)
    lane = jnp.where(lane < span, lane, lane - span)
    spread = jnp.concatenate([rows] * share, axis=0)
    spread = jnp.where(lane // capacity == row // peers, spread, 0.0).astype(BF16)
    c = lax.broadcasted_iota(jnp.int32, (2 * span, plan.slots), 0)
    slot = lax.broadcasted_iota(jnp.int32, (2 * span, plan.slots), 1)
    scale = jnp.where(c < span, 64.0, 1.0)
    place = jnp.where(c % capacity == slot % capacity, scale, 0.0).astype(BF16)
    listed = matmul(spread, place)
    row = lax.broadcasted_iota(jnp.int32, listed.shape, 0)
    slot = lax.broadcasted_iota(jnp.int32, listed.shape, 1)
    listed = jnp.where(slot // capacity == row % peers, listed, 0.0)
    out_ref[...] = jnp.sum(listed.reshape(share, peers, plan.slots), axis=1)


def project(plan, place, lists, place_ref, w_ref, normed_ref, turn_ref, after_ref, *refs):
    if lists:
        *refs, list_ref, full_ref = refs
        if plan.tight:
            rows = spread_weights(plan, w_ref, full_ref)
            w_ref = full_ref
        else:
            rows = list_rows(plan, w_ref)
            full_ref[...] = w_ref[...]
        read_lists(plan, rows, list_ref)
    q_ref, vo_ref = refs[-2:]
    turns = turn_ref[place_ref[LINE]]
    half, k_half = plan.q_rows // 2, plan.k_rows // 2
    cosine, sine = turns[:, 0:1], turns[:, 1:2]
    cos_k, sin_k = cosine[:k_half], sine[:k_half]
    moves = normed_ref.shape[0]
    block = min(moves, HD)
    every = []
    for start in range(0, moves, block):
        at, to = slice(start, start + block), slice(place + start, place + start + block)
        if len(w_ref.shape) == 3:
            depth = w_ref.shape[2]
            total = None
            for s in range(w_ref.shape[0]):
                term = matmul(w_ref[s], normed_ref[at, s * depth : (s + 1) * depth], NT)
                total = term if total is None else total + term
        else:
            total = matmul(w_ref[...], normed_ref[at, :], NT)
        first, second = total[:half], total[half : 2 * half]
        f_first = (first * cosine - second * sine).astype(BF16).astype(F32)
        f_second = (second * cosine + first * sine).astype(BF16).astype(F32)
        first, second = total[plan.q_rows : plan.q_rows + k_half], total[plan.q_rows + k_half : plan.fold_at]
        k_first = (first * cos_k - second * sin_k).astype(BF16).astype(F32)
        k_second = (second * cos_k + first * sin_k).astype(BF16).astype(F32)
        logits, tails = [], []
        for h in range(plan.mine):
            own = slice(h * k_half, (h + 1) * k_half)
            logit = jnp.sum(f_first[own] * k_first + f_second[own] * k_second, axis=0, keepdims=True)
            logits.append(logit.astype(BF16).astype(F32))
            tails.append(logit - logits[-1])
        if plan.direct:
            chunk = (place + start) // block * plan.q_rows
            q_ref[chunk : chunk + plan.q_rows] = jnp.concatenate([f_first, f_second], axis=0).astype(BF16)
            every += [*logits, *tails]
        else:
            pad = plan.line_rows - plan.q_rows - 2 * plan.mine
            pieces = [f_first, f_second, *logits, *tails]
            if pad:
                pieces.append(jnp.zeros((pad, block), F32))
            out = jnp.concatenate(pieces, axis=0).astype(BF16)
            for line in range(plan.line):
                q_ref[line, :, to] = out
        vo_ref[:, to] = total[plan.fold_at : plan.list_at]
    if plan.direct:
        first = vo_ref.shape[1] // HD * plan.q_rows + place // block * 2 * plan.mine
        q_ref[first : first + len(every)] = jnp.concatenate(every, axis=0).astype(BF16)


def tied(x, *others):
    return pl.pallas_call(
        lambda *refs: None,
        out_shape=shape(x.shape, x.dtype),
        in_specs=[untouched()] * (1 + len(others)),
        out_specs=untouched(),
        input_output_aliases={0: 0},
        compiler_params=limits(1),
        cost_estimate=cost(0, 0),
    )(x, *others)


def pack_prefix(plan, prefix_hbm, ws_hbm, after_ref, out_ref, *scratch):
    values, ws_ref, sems = scratch
    boards = values.shape[0]
    heads = plan.heads
    copies = (
        pltpu.make_async_copy(ws_hbm, ws_ref, sems.at[0]),
        pltpu.make_async_copy(prefix_hbm.at[:, :, pl.ds(HD, HD)], values, sems.at[1]),
        pltpu.make_async_copy(prefix_hbm.at[:, :, pl.ds(0, HD)], out_ref.at[pl.ds(0, boards)], sems.at[2]),
    )
    for copy in copies:
        copy.start()
    copies[0].wait()
    span = HD // boards
    ws = jnp.concatenate([ws_ref[...].astype(F32)] * (HD // heads), axis=0)
    row = lax.broadcasted_iota(jnp.int32, (HD, 1), 0)
    copies[1].wait()
    fold = None
    for board in range(boards):
        keep = (row // span == board) & (row % span < 2 * heads)
        term = matmul(values[board], jnp.where(keep, ws, 0.0).astype(BF16), NT)
        fold = term if fold is None else fold + term
    rounded = fold.astype(BF16).astype(F32)
    lane = lax.broadcasted_iota(jnp.int32, fold.shape, 1)
    out_ref[boards] = jnp.where(lane % span < heads, rounded, fold - rounded).astype(BF16)
    copies[2].wait()


def fold_columns(plan, here, block, board, boards, heads):
    lanes = plan.mine * plan.slots
    row = lax.broadcasted_iota(jnp.int32, (HD, lanes), 0) - board * (HD // boards)
    head = here * plan.mine + lax.broadcasted_iota(jnp.int32, (HD, lanes), 1) // plan.slots
    pick = jnp.where((row == head) | (row == head + heads), 1.0, 0.0).astype(BF16)
    return matmul(block, pick)


def prepare(plan, place_ref, own_ref, other_ref, *rest):
    *prefix_refs, chosen_ref, fold_ref = rest
    here = place_ref[SLAB]
    boards, moves = chosen_ref.shape[0], chosen_ref.shape[1]
    move_at = lax.broadcasted_iota(jnp.int32, (moves, plan.slots), 0) + 1

    def step(board, carry):
        for j in range(plan.slab):
            place = ((here ^ j) % plan.pair) * boards + board
            row = (own_ref, other_ref)[j // plan.pair][pl.ds(place, 1), :].astype(jnp.int32)
            at = slice(j * plan.slots, (j + 1) * plan.slots)
            chosen_ref[board, :, at] = jnp.where(move_at == row, 1.0, 0.0).astype(BF16)
        for j, prefix_ref in enumerate(prefix_refs):
            fold_ref[j, board] = fold_columns(plan, here, prefix_ref[boards], board, boards, plan.heads)
        return carry

    lax.fori_loop(0, boards, step, 0)


def attend(plan, place_ref, vo_ref, own_ref, other_ref, chosen_ref, fold_ref, *rest):
    prefix_refs, rest = rest[: plan.slab], rest[plan.slab :]
    *q_refs, out_ref, table, extra, scores, taken_even, taken_odd = rest
    here = place_ref[SLAB]
    mine, heads, slots = plan.mine, plan.heads, plan.slots
    moves = vo_ref.shape[1]
    boards = prefix_refs[0].shape[0] - 1
    query_rows = mine * HD

    mixed = own_logits = None
    for step, q_ref in enumerate(q_refs):
        if plan.direct:
            chunks = range(moves // HD)
            values = jnp.concatenate([q_ref[c * plan.q_rows : (c + 1) * plan.q_rows] for c in chunks], axis=1)
            tails = q_ref[moves // HD * plan.q_rows :].astype(F32)
            tails = jnp.concatenate([tails[c * 2 * mine : (c + 1) * 2 * mine] for c in chunks], axis=1)
            tails = tails[:mine] + tails[mine:]
            own_logits = tails if own_logits is None else own_logits + tails
        else:
            values = q_ref[...]
        r = lax.broadcasted_iota(jnp.int32, (query_rows + 8, values.shape[0]), 0)
        c = lax.broadcasted_iota(jnp.int32, (query_rows + 8, values.shape[0]), 1)
        line, at = (place_ref[LINE] ^ step, c) if plan.direct else (c // plan.line_rows, c % plan.line_rows)
        part, head, entry = at // (mine * plan.pairs), (at // plan.pairs) % mine, at % plan.pairs
        goes = jnp.where(at < plan.q_rows, head * HD + part * HALF + line * plan.pairs + entry, -1)
        tail = at - plan.q_rows
        goes = jnp.where((tail >= 0) & (tail < 2 * mine), query_rows + tail % mine, goes)
        term = matmul(jnp.where(r == goes, 1.0, 0.0).astype(BF16), values)
        mixed = term if mixed is None else mixed + term
    if own_logits is None:
        own_logits = mixed[query_rows : query_rows + mine]
    table[:query_rows] = mixed[:query_rows].astype(BF16)
    extra[...] = jnp.zeros_like(extra)
    for place, value in ((0, own_logits), (2 * mine, vo_ref[...])):
        rounded = value.astype(BF16).astype(F32)
        extra[place : place + mine] = rounded
        extra[place + mine : place + 2 * mine] = value - rounded
    table[query_rows:] = extra[...].astype(BF16)

    scale = math.log2(math.e) / math.sqrt(HD)
    def per_head(x, base):
        pieces = [x[base + h : base + h + 1] + x[base + mine + h : base + mine + h + 1] for h in range(mine)]
        return jnp.concatenate(pieces, axis=1)

    def moves_of(j, board):
        place = ((here ^ j) % plan.pair) * boards + board
        return (own_ref, other_ref)[j // plan.pair][pl.ds(place, 1), :].astype(jnp.int32)

    def gather(board, taken):
        taken[...] = matmul(table[...], chosen_ref[board])

    def score_board(board, taken):
        for j in range(plan.slab):
            x = taken[:, j * slots : (j + 1) * slots]
            q = jnp.concatenate([x[h * HD : (h + 1) * HD].astype(BF16) for h in range(mine)], axis=1)
            logits = matmul(prefix_refs[j][board], q)
            if j < plan.slab - 1:
                fold = fold_ref[j, board]
            else:
                fold = fold_columns(plan, here, prefix_refs[j][boards], board, boards, heads)
            own_logit = per_head(x, query_rows)
            own_value = per_head(x, query_rows + 2 * mine)
            peak = jnp.maximum(jnp.max(logits, axis=0, keepdims=True), own_logit)
            weight = jnp.exp2((logits - peak) * scale)
            own_weight = jnp.exp2((own_logit - peak) * scale)
            denom = jnp.sum(weight, axis=0, keepdims=True) + own_weight
            value = (jnp.sum(weight * fold, axis=0, keepdims=True) + own_value * own_weight) / denom
            score = sum(value[:, h * slots : (h + 1) * slots] for h in range(mine))
            scores[here ^ j, pl.ds(board, 1), :] = jnp.where(moves_of(j, board) > 0, score, DEAD)

    gather(0, taken_even)

    def step(at, carry):
        board = 2 * at
        gather(jnp.minimum(board + 1, boards - 1), taken_odd)
        score_board(board, taken_even)
        gather(jnp.minimum(board + 2, boards - 1), taken_even)
        score_board(jnp.minimum(board + 1, boards - 1), taken_odd)
        return carry

    lax.fori_loop(0, -(-boards // 2), step, 0)
    live = scores[...] > 0.5 * DEAD
    count = jnp.sum(jnp.where(live, 1.0, 0.0), axis=2, keepdims=True)
    mean = jnp.sum(jnp.where(live, scores[...], 0.0), axis=2, keepdims=True) / jnp.maximum(count, 1.0)
    centered = jnp.where(live, scores[...] - mean, DEAD)
    for g in range(plan.groups):
        both = jnp.concatenate([centered[g * plan.pair + p] for p in range(plan.pair)], axis=0).astype(BF16)
        for copy in range(out_ref.shape[1]):
            out_ref[g, copy] = both


def finish(plan, parts_ref, board_ref, slot_ref, out_ref):
    line = parts_ref.shape[1]
    columns = []
    for at in range(line):
        total = None
        for g in range(parts_ref.shape[0]):
            for p in range(parts_ref.shape[2]):
                term = parts_ref[g, at, p].astype(F32)
                total = term if total is None else total + term
        columns.append(total)
    scores = jnp.concatenate(columns, axis=0)
    live = scores > 0.5 * DEAD
    peak = jnp.max(scores, axis=1, keepdims=True)
    denom = jnp.sum(jnp.where(live, jnp.exp(scores - peak), 0.0), axis=1, keepdims=True)
    logprob = jnp.where(live, scores - peak - jnp.log(denom), 0.0)
    count = board_ref.shape[1]
    member = lax.broadcasted_iota(jnp.int32, (scores.shape[0], count), 0) == board_ref[...]
    member = jnp.where(member, 1.0, 0.0).astype(BF16)
    rounded = logprob.astype(BF16)
    pieces = jnp.concatenate([rounded, (logprob - rounded.astype(F32)).astype(BF16)], axis=1)
    found = matmul(pieces, member, TN)
    found = found[: plan.slots] + found[plan.slots :]
    at = lax.broadcasted_iota(jnp.int32, (plan.slots, count), 0) == slot_ref[...]
    out_ref[...] = jnp.sum(jnp.where(at, found, 0.0), axis=0, keepdims=True)


def untouched():
    return pl.BlockSpec(memory_space=pl.ANY)


def local_call(kernel, place, args, outs, scratch=(), mib=40, copied=(), flops=0, nbytes=0, aliases=None):
    vmem = pl.BlockSpec(memory_space=pltpu.VMEM)
    return pl.pallas_call(
        kernel,
        out_shape=outs,
        in_specs=[pl.BlockSpec(memory_space=pltpu.SMEM)]
        + [untouched() if at in copied else vmem for at in range(len(args))],
        out_specs=jax.tree.map(lambda x: vmem, outs),
        scratch_shapes=scratch,
        input_output_aliases=aliases or {},
        compiler_params=limits(mib),
        cost_estimate=cost(flops, nbytes),
    )(place, *args)


def cost(flops, nbytes):
    return pl.CostEstimate(flops=int(flops), bytes_accessed=int(nbytes), transcendentals=0)


def swap(x, names, size, step):
    return lax.ppermute(x, names, [(at, at ^ step) for at in range(size)])


def shape(dims, dtype):
    return jax.ShapeDtypeStruct(tuple(dims), dtype)


def turn_table(position):
    frequency = THETA ** (-2.0 * np.arange(HALF, dtype=np.float32) / HD)
    angles = np.float32(position) * frequency.astype(np.float32)
    return np.stack([np.cos(angles), np.sin(angles)], axis=1).astype(np.float32)


def per_device(prefix_kv, move_ids, move_board, move_table, norm_gain, w_query, w_keyval, w_score):
    row_count = move_ids.shape[0]
    boards_here, prefix_len, _ = prefix_kv.shape
    moves, width = move_table.shape
    groups, line, pair = lax.axis_size("groups"), lax.axis_size("line"), lax.axis_size("pair")
    board_total = boards_here * line * pair
    capacity = max(2, (2 * row_count + board_total - 1) // board_total)
    heads = w_query.shape[1] // HD
    depth = w_query.shape[0]
    plan = Plan(groups, line, pair, heads, capacity, pair * boards_here, depth)
    group_at = lax.axis_index("groups").astype(jnp.int32)
    line_at = lax.axis_index("line").astype(jnp.int32)
    pair_at = lax.axis_index("pair").astype(jnp.int32)
    place = jnp.stack([group_at, line_at, line_at * pair + pair_at, group_at * pair + pair_at])
    ws = w_score.reshape(heads, HD)
    slab_axes = ("groups", "pair")
    board_row = move_board.reshape(1, row_count)

    half_cols = w_query.shape[1] // groups
    packed = local_call(
        functools.partial(pack_weights, plan),
        group_at.reshape(1),
        (w_query, w_keyval, ws, board_row, move_ids.reshape(1, row_count)),
        shape((plan.peers, *plan.sent), BF16),
        [
            pltpu.VMEM((depth, half_cols), BF16),
            pltpu.VMEM((depth, 2 * HD), BF16),
            pltpu.VMEM((heads, HD), BF16),
            pltpu.VMEM((1, row_count), jnp.int32),
            pltpu.VMEM((1, row_count), jnp.int32),
            pltpu.VMEM((plan.peers * plan.rows, half_cols + 2 * HD), F32),
            pltpu.SemaphoreType.DMA((5,)),
        ],
        62,
        range(5),
    )
    weights = lax.all_to_all(packed, ("line", "pair"), split_axis=0, concat_axis=0, tiled=True)

    payload = pl.pallas_call(
        functools.partial(pack_prefix, plan),
        out_shape=shape((boards_here + 1, prefix_len, HD), BF16),
        in_specs=[untouched()] * 3,
        out_specs=pl.BlockSpec(memory_space=pltpu.VMEM),
        scratch_shapes=[
            pltpu.VMEM((boards_here, prefix_len, HD), BF16),
            pltpu.VMEM((heads, HD), BF16),
            pltpu.SemaphoreType.DMA((3,)),
        ],
        compiler_params=limits(56),
        cost_estimate=cost(0, 0),
    )(prefix_kv, ws, packed)
    beside = swap(payload, slab_axes, plan.slab, 1)
    across = swap(payload, slab_axes, plan.slab, 2)

    block = min(moves, 128)
    vmem = pl.BlockSpec(memory_space=pltpu.VMEM)
    *normed, mark, slot_row = pl.pallas_call(
        functools.partial(normalize, plan),
        out_shape=[*[shape((moves // 2, width), BF16)] * 2, pltpu.VMEM((8, HD), F32), shape((1, row_count), jnp.int32)],
        in_specs=[pl.BlockSpec(memory_space=pltpu.SMEM), untouched(), vmem, vmem, untouched()],
        out_specs=[untouched(), untouched(), vmem, vmem],
        scratch_shapes=[
            pltpu.VMEM((1, width), F32),
            pltpu.VMEM((3, block, width), BF16),
            pltpu.VMEM((3, block, width), BF16),
            pltpu.SemaphoreType.DMA((3,)),
            pltpu.SemaphoreType.DMA((3,)),
        ],
        compiler_params=limits(58),
        cost_estimate=cost(moves * width, moves * width // 4),
    )(place, move_table, norm_gain.reshape(width // HD, HD), board_row, packed)
    turns = turn_table(prefix_len).reshape(line, 1, plan.pairs, 2)
    turns = np.tile(turns, (1, plan.mine, 1, 1)).reshape(line, plan.mine * plan.pairs, 2)
    flat = weights.transpose(1, 0, 2).reshape(plan.rows, width) if depth % HD else weights
    sent = (moves // HD * (plan.q_rows + 2 * plan.mine), HD) if plan.direct else (line, plan.line_rows, moves)
    outs = (shape(sent, BF16), shape((plan.mine, moves), F32))
    across = tied(across, mark)
    diagonal = swap(across, slab_axes, plan.slab, 1)
    full = shape((plan.peers, plan.rows, depth), BF16) if plan.tight else shape(flat.shape, BF16)
    filled, listed = (), None
    for step, after in enumerate((across, across)):
        made = local_call(
            functools.partial(project, plan, step * moves // 2, step == 0),
            place,
            (flat, normed[step], jnp.asarray(turns), after, *filled),
            [*outs, *([shape((plan.share, plan.slots), F32), full] if step == 0 else [])],
            (),
            20,
            (3,),
            moves * width * 1024,
            moves * width,
            {5: 0, 6: 1} if filled else None,
        )
        filled = made[:2]
        if step == 0:
            listed, flat = made[2:]
    queries, own_values = filled
    queries = tied(queries, beside)
    other = swap(listed, slab_axes, plan.slab, pair)
    if plan.direct:
        queries = [queries] + [swap(queries, "line", line, step) for step in range(1, line)]
    else:
        queries = lax.all_to_all(queries, "line", split_axis=0, concat_axis=0, tiled=True)
        queries = [queries.reshape(line * plan.line_rows, moves)]

    query_rows = plan.mine * HD
    back = plan.peers * lax.axis_size("tensor")
    chosen, folds = local_call(
        functools.partial(prepare, plan),
        place,
        (listed, other, payload, beside, across),
        (
            shape((boards_here, moves, plan.slab * plan.slots), BF16),
            shape((plan.slab - 1, boards_here, prefix_len, plan.mine * plan.slots), F32),
        ),
        mib=20,
        flops=10**9,
        nbytes=10**6,
    )
    parts = local_call(
        functools.partial(attend, plan),
        place,
        (own_values, listed, other, chosen, folds, payload, beside, across, diagonal, *queries),
        shape((groups, back, plan.share, plan.slots), BF16),
        [
            pltpu.VMEM((query_rows + 8, moves), BF16),
            pltpu.VMEM((8, moves), F32),
            pltpu.VMEM((plan.slab, boards_here, plan.slots), F32),
            pltpu.VMEM((query_rows + 8, plan.slab * plan.slots), F32),
            pltpu.VMEM((query_rows + 8, plan.slab * plan.slots), F32),
        ],
        24,
    )
    parts = lax.all_to_all(
        parts.reshape(groups * back, plan.share, plan.slots),
        ("groups", "line", "pair", "tensor"),
        split_axis=0,
        concat_axis=0,
        tiled=True,
    )
    parts = parts.reshape(groups, line, back // line, plan.share, plan.slots)
    logprob = pl.pallas_call(
        functools.partial(finish, plan), out_shape=shape((1, row_count), F32), compiler_params=limits(VMEM_MIB)
    )(parts, board_row, slot_row)
    return logprob.reshape(row_count)


def solution(mesh):
    order = ("groups", "dp", "tensor")
    assert mesh.axis_names == order
    pair = 2
    groups, peers, tensor = (mesh.shape[name] for name in order)
    fine = Mesh(mesh.devices.reshape(groups, peers // pair, pair, tensor), ("groups", "line", "pair", "tensor"))
    rows = ("groups", "line", "pair")
    placed = (
        P(rows, None, "tensor"),
        P(rows),
        P(rows, None),
        P(),
        P(),
        P(("line", "pair"), "tensor"),
        P(("line", "pair"), "tensor"),
        P("tensor"),
    )
    return jax.shard_map(per_device, mesh=fine, in_specs=placed, out_specs=P(rows), check_vma=False)
```
